32 devices in a mesh: groups: 2 (over y), leaf: 2 (over x), sub: 4 (over z), rep: 2 (over core).
Axes of the slice: x: 2, y: 2, z: 4, core: 2. Of those that a mesh axis runs over, the one named last changes fastest.
Arguments:
- points: float32 [16384, 64], P(('groups', 'leaf', 'sub')), parts along dimension 0, may hold values from -12 to 12
- weights: float32 [16384, 256], P(('groups', 'leaf', 'sub'), 'rep'), parts along dimension 0, may hold values from -6 to 6
- tree_slot: int32 [16384], P(('groups', 'leaf', 'sub')), parts along dimension 0, may hold values from 0 to 8191, as said below
- near_count: int32 [4, 8], P(('groups', 'leaf')), parts along dimension 0, may hold values from 1 to 16, 32 in all within a row
- near_list: int32 [4, 8, 16], P(('groups', 'leaf')), parts along dimension 0, may hold values from 0 to 7
- skeleton_base: int32 [16, 128], P(('groups', 'leaf', 'sub')), parts along dimension 0, may hold values from 0 to 1023, as said below
- skeleton_upper: int32 [12, 128], P('groups'), parts along dimension 0, may hold values from 0 to 255, as said below
- far_use: int32 [32, 3], P(('groups', 'leaf', 'sub')), parts along dimension 0, may hold values 0 or 1
Outputs:
- result: float32 [16384, 256], P(('groups', 'leaf', 'sub'), 'rep'), parts along dimension 0
The draws below stay inside these ranges and needn't reach their ends.
There are 2 independent parts, one for each index of `groups`. The reference program is written for one: setup_inputs(seed, part) draws one part's arguments, and reference() takes and returns one part's arrays. A program takes and returns all parts, laid end to end along the dimension named above; each array names one. Nothing has to cross between parts.
Inputs may be any that keep to these rules, and one draw needn't show every extreme that they name: `tree_slot`: A permutation; each device block's input rows hold exactly 128 points of every device block of the tree. `near_count`: the counts of one subtree sum to 32. `near_list`: only the first near_count slots of a leaf are read; entries may repeat. `skeleton_base`: entries of a row are distinct. `skeleton_upper`: entries of a row are distinct; node j of level l is row 8 - (8 >> (l - 1)) + j.
All inputs are finite; a program needn't handle non-finite values. No bound on the sum of `far_use` on one device may be relied on, other than what follows from the above.
Results may differ from the reference program's by a relative error of at most 0.0028.
Values sent between devices are 32-bit elements; how exact they have to be, the bound alone decides.
No kernel may reach another device: no remote copies, remote signals or barrier semaphores. Data moves between devices by JAX's collectives and lax.ppermute only.
A program may use at most 64 MiB of HBM per device.

```python
import math
import jax
import jax.numpy as jnp
import numpy as np
from jax import lax

DIM = 64
LEAF = 512
SK = 128
MEAN = 4
LPD = 2
DEVS = 8
LEVELS = 3
PTS_DEV = 1024
PER_PEER = 128
NPTS = 8192
R = 256
LPS = 8
NLEAVES = 16
NMAX = 16
UPPER = 6
N_LEAF = 2
N_SUB = 4


def shuffle_rows(key, rows, count):
    keys = jax.random.split(key, rows)
    return jax.vmap(lambda single: jax.random.permutation(single, count))(keys).astype(jnp.int32)


def draw_points(key, part):
    key = jax.random.fold_in(key, 5)
    first, second = jax.random.split(key)
    center = jax.random.normal(first, (DIM,), jnp.float32)
    spread = jax.random.normal(second, (NPTS, DIM), jnp.float32) * (80.0 / DIM) ** 0.5
    return jnp.clip(center[None, :] + spread, -12.0, 12.0).astype(jnp.float32)


def draw_tree_slot(key, part):
    key = jax.random.fold_in(key, 11)
    first, second = jax.random.split(key)
    sender = shuffle_rows(first, DEVS, PTS_DEV)
    receiver = shuffle_rows(second, DEVS, PTS_DEV)
    source = jnp.arange(DEVS, dtype=jnp.int32)[:, None]
    target = sender // PER_PEER
    within = source * PER_PEER + sender % PER_PEER
    slot = target * PTS_DEV + receiver[target, within]
    return slot.reshape(NPTS).astype(jnp.int32)


def draw_skeleton_base(key, part):
    key = jax.random.fold_in(key, 23)
    return shuffle_rows(key, DEVS, PTS_DEV)[:, :SK]


def draw_skeleton_upper(key, part):
    key = jax.random.fold_in(key, 37)
    return shuffle_rows(key, UPPER, 2 * SK)[:, :SK]


def touch_ends(values, rng, smallest, largest):
    longest = values.shape.index(max(values.shape))
    spots = []
    for shift in (0, 1):
        where = [jax.random.randint(jax.random.fold_in(rng, axis), (), 0, length) for axis, length in enumerate(values.shape)]
        where[longest] = (where[longest] + shift) % values.shape[longest]
        spots.append(tuple(where))
    return values.at[spots[0]].set(smallest).at[spots[1]].set(largest)


def level_of(rng, extent, cuts, low, largest):
    level, own = 1.0, jax.random.fold_in(rng, 6)
    for dim, blocks in cuts:
        steps = jnp.exp(jax.random.uniform(jax.random.fold_in(own, dim), (blocks,), jnp.float32, low / len(cuts), largest / len(cuts)))
        level = level * jnp.repeat(steps, extent[dim] // blocks).reshape([-1 if axis == dim else 1 for axis in range(len(extent))])
    return level


def profile(number_of, total, most, lean):
    weights = [(1 << 20) // math.isqrt(rank ** lean) + 1 for rank in range(2, number_of + 1)]
    rest, holding = total - most - (number_of - 1), [1] * (number_of - 1)
    while rest > 0:
        movable = [i for i in range(number_of - 1) if holding[i] < most]
        mass, left = sum([weights[i] for i in movable]), rest
        for i in movable:
            more = min(most - holding[i], max(1, left * weights[i] // mass), rest)
            holding[i] = holding[i] + more
            rest = rest - more
    return np.array([most] + holding)


def uneven_parts(rng, number_of, total, bound, lean):
    if number_of == 2:
        one = jax.random.randint(rng, (), max(1, total - bound), min(bound, total - 1) + 1)
        return jnp.stack([one, total - one])
    lengths = jnp.asarray(profile(number_of, total, bound, lean), jnp.int32)
    twos = (number_of - 1) // 2
    source_of, taker = lengths[1:1 + 2 * twos:2], lengths[2:2 + 2 * twos:2]
    slack = jnp.minimum(source_of - 1, bound - taker)
    shifted = jax.random.randint(jax.random.fold_in(rng, 1), (twos,), 0, 1 << 20) % (slack + 1)
    lengths = lengths.at[1:1 + 2 * twos:2].set(source_of - shifted).at[2:2 + 2 * twos:2].set(taker + shifted)
    return lengths[jax.random.permutation(jax.random.fold_in(rng, 2), number_of)]


def noise(rng, dims, width, limit, cuts=(), kind=jnp.bfloat16):
    factor_of = level_of(rng, dims, cuts, -0.22, 0.18) if cuts else 1.0
    drawn = jax.random.normal(rng, dims, jnp.float32) * width * factor_of
    return jnp.minimum(jnp.maximum(drawn, -limit), limit).astype(kind)


def setup_inputs(seed: int = 0, part: int = 0) -> dict:
    splits = jax.random.split(jax.random.key(seed), 9)
    own_keys = jax.random.split(jax.random.fold_in(splits[8], part), 9)
    return {
        "points": draw_points(jax.random.fold_in(jax.random.fold_in(splits[8], part), 71), part),
        "weights": noise(own_keys[1], (NPTS, R), 1.0, 6.0, ((0, 8), (1, 2)), jnp.float32),
        "tree_slot": draw_tree_slot(jax.random.fold_in(jax.random.fold_in(splits[8], part), 71), part),
        "near_count": jax.vmap(lambda own: uneven_parts(own, LPS, LPS * MEAN, NMAX, 2))(jax.random.split(own_keys[3], N_LEAF)).reshape((N_LEAF, LPS)).astype(jnp.int32),
        "near_list": touch_ends(jax.random.randint(own_keys[4], (N_LEAF, LPS, NMAX), 0, LPS), jax.random.fold_in(own_keys[4], 1), 0, LPS - 1).astype(jnp.int32),
        "skeleton_base": draw_skeleton_base(jax.random.fold_in(jax.random.fold_in(splits[8], part), 71), part),
        "skeleton_upper": draw_skeleton_upper(jax.random.fold_in(jax.random.fold_in(splits[8], part), 71), part),
        "far_use": touch_ends((jax.random.randint(own_keys[7], (NLEAVES, LEVELS), 0, 4) < 3).astype(jnp.int32), jax.random.fold_in(own_keys[7], 1), 0, 1),
    }


highest = lax.Precision.HIGHEST
kernel_scale = 1.0 / 32.0
ridge = 0.5


def kernel(targets, sources):
    inner = jnp.dot(targets, sources.T, precision=highest, preferred_element_type=jnp.float32)
    distance = jnp.sum(targets * targets, axis=1)[:, None] + jnp.sum(sources * sources, axis=1)[None, :] - 2.0 * inner
    return jnp.exp(-kernel_scale * distance)


def reference(points, weights, tree_slot, near_count, near_list, skeleton_base, skeleton_upper, far_use):
    devices = N_LEAF * N_SUB
    levels = devices.bit_length() - 1
    columns = weights.shape[1]
    wide = LPD * N_SUB
    tree_points = jnp.zeros_like(points).at[tree_slot].set(points)
    tree_weights = jnp.zeros_like(weights).at[tree_slot].set(weights)
    light = tree_weights.astype(jnp.bfloat16)

    block_points = tree_points.reshape(N_LEAF, wide, LEAF, DIM)
    block_light = light.reshape(N_LEAF, wide, LEAF, columns)

    def subtree(packed):
        coords, values, counts, lists = packed
        starts = (jnp.cumsum(counts) - counts).astype(jnp.int32)

        def tile(index):
            target = (jnp.sum((starts <= index).astype(jnp.int32)) - 1).astype(jnp.int32)
            slot = (index - starts[target]).astype(jnp.int32)
            source = lists[target, slot]
            block = kernel(coords[target], coords[source]).astype(jnp.bfloat16)
            return jnp.dot(block, values[source], preferred_element_type=jnp.float32), target

        terms, targets = lax.map(tile, jnp.arange(wide * MEAN, dtype=jnp.int32))
        listed = jax.ops.segment_sum(terms, targets, num_segments=wide)

        def own(packed_leaf):
            place, value = packed_leaf
            block = kernel(place, place).astype(jnp.bfloat16)
            return jnp.dot(block, value, preferred_element_type=jnp.float32)

        return listed + lax.map(own, (coords, values))

    near = lax.map(subtree, (block_points, block_light, near_count, near_list))
    near = near.reshape(NPTS, columns)

    node_points = tree_points.reshape(devices, PTS_DEV, DIM)
    node_light = light.reshape(devices, PTS_DEV, columns)

    def base(packed):
        coords, values, picks = packed
        chosen = coords[picks]
        block = kernel(chosen, coords).astype(jnp.bfloat16)
        return chosen, jnp.dot(block, values, preferred_element_type=jnp.float32)

    skeleton_points, coefficients = lax.map(base, (node_points, node_light, skeleton_base))
    level_points = [skeleton_points]
    level_coefs = [coefficients]

    def upward(coords, values, chosen_rows):
        chosen = coords[chosen_rows]
        return chosen, jnp.dot(kernel(chosen, coords), values, precision=highest, preferred_element_type=jnp.float32)

    offset = 0
    for level in range(1, levels):
        count = devices >> level
        pair_points = level_points[-1].reshape(count, 2 * SK, DIM)
        pair_coefs = level_coefs[-1].reshape(count, 2 * SK, columns)
        picks = skeleton_upper[offset:offset + count]
        offset += count
        chosen, values = jax.vmap(upward)(pair_points, pair_coefs, picks)
        level_points.append(chosen)
        level_coefs.append(values)

    flags = far_use.reshape(devices, LPD, levels).astype(jnp.float32)

    def far_device(index):
        targets = node_points[index]
        total = jnp.zeros((PTS_DEV, columns), jnp.float32)
        for level in range(levels):
            sibling = (index >> level) ^ 1
            block = kernel(targets, level_points[level][sibling])
            term = jnp.dot(block, level_coefs[level][sibling], precision=highest, preferred_element_type=jnp.float32)
            mask = jnp.repeat(flags[index][:, level], LEAF)[:, None]
            total = total + term * mask
        return total

    far = lax.map(far_device, jnp.arange(devices, dtype=jnp.int32)).reshape(NPTS, columns)
    tree_result = ridge * tree_weights + near + far
    return tree_result[tree_slot]
```

```python
import functools
import math

import jax
import jax.numpy as jnp
from jax import lax
from jax.experimental import pallas as pl
from jax.experimental.pallas import tpu as pltpu
from jax.sharding import PartitionSpec as P

DIM = 64
LEAF = 512
SK = 128
LANES = 128
FEAT = 256

highest = lax.Precision.HIGHEST
point_scale = math.sqrt(2.0 * math.log2(math.e) / 32.0)
ridge = 0.5
PLACE_ROWS = 72
SLOT_ROW = 64
NORM_ROW = 65
f32 = jnp.float32
bf16 = jnp.bfloat16
VMEM = pltpu.MemorySpace.VMEM
SMEM = pltpu.MemorySpace.SMEM


def spec(space=VMEM):
    return pl.BlockSpec(memory_space=space)


def params():
    return pltpu.CompilerParams(vmem_limit_bytes=56 * 1024 * 1024)


def nt(left, right):
    return lax.dot_general(left, right, (((1,), (1,)), ((), ())), preferred_element_type=f32)


def nn(left, right):
    return jnp.dot(left, right, preferred_element_type=f32)


def column(row):
    return jnp.transpose(jnp.broadcast_to(row, (LANES, LANES)))


def iota(shape, dim):
    return lax.broadcasted_iota(jnp.int32, shape, dim)


def onehot(mask):
    return jnp.where(mask, 1.0, 0.0).astype(bf16)


def two(value):
    high = value.astype(bf16)
    return high, (value - high.astype(f32)).astype(bf16)


def three(value):
    high = value.astype(bf16)
    rest = value - high.astype(f32)
    mid = rest.astype(bf16)
    return high.astype(f32), mid.astype(f32), (rest - mid.astype(f32)).astype(bf16).astype(f32)


def sort_kernel(slot_ref, points_ref, weights_ref, light_ref, place_ref, pos_ref, perm, vals):
    chunks, split = slot_ref.shape[0], light_ref.shape[-1]
    rows = chunks * LANES
    slots = slot_ref[...]
    slot = slots.astype(f32)
    within = slots & (rows - 1)
    high, low = (within >> 5).astype(f32), (within & 31).astype(f32)
    cols = jnp.concatenate([column(slot[c : c + 1]) for c in range(chunks)], 0)
    lane = iota((rows, LANES), 1)
    for c in range(chunks):
        before = jnp.where(cols < slot[c : c + 1], 1.0, 0.0)
        rank = jnp.sum(before, axis=0, keepdims=True)
        pos_ref[c : c + 1, :] = rank
        perm[:, c * LANES : (c + 1) * LANES] = onehot(iota((rows, LANES), 0) == rank.astype(jnp.int32))
    scaled = points_ref[...] * point_scale
    ph, plo = two(scaled)
    norm = -0.5 * jnp.sum(scaled * scaled, axis=1, keepdims=True)
    nh, nm, nl = three(jnp.broadcast_to(norm, (rows, LANES)))
    high = jnp.concatenate([column(high[c : c + 1]) for c in range(chunks)], 0)
    low = jnp.concatenate([column(low[c : c + 1]) for c in range(chunks)], 0)
    extra = jnp.where(lane == 0, high, jnp.where(lane == 1, low, 0.0))
    extra = jnp.where(lane == 2, nh, jnp.where(lane == 3, nm, jnp.where(lane == 4, nl, extra)))
    vals[:, 0:128] = weights_ref[...].astype(bf16)
    vals[:, 128:192] = ph
    vals[:, 192:256] = plo
    vals[:, 256:384] = extra.astype(bf16)
    step = 256
    for s in range(rows // step):
        sorted_rows = nn(perm[s * step : (s + 1) * step, :], vals[...])
        at = (s * step) // split
        off = (s * step) % split
        width = min(step, split)
        light = jnp.transpose(sorted_rows[:, 0:128])
        both = jnp.transpose(sorted_rows[:, 128:256])
        more = jnp.transpose(sorted_rows[:, 256:384])
        light_ref[at, :, off : off + width] = light
        place_ref[at, 0:64, off : off + width] = both[0:64] + both[64:128]
        tail = iota((8, step), 0)
        slot_row = more[0:1] * 32.0 + more[1:2]
        norm_row = more[2:3] + more[3:4] + more[4:5]
        place_ref[at, 64:72, off : off + width] = jnp.where(
            tail == 0, slot_row, jnp.where(tail == 1, norm_row, 0.0)
        )


def slot_matrix(out, slot_rows):
    rows = out.shape[0]
    for c, row in enumerate(slot_rows):
        out[:, c * LANES : (c + 1) * LANES] = onehot(iota((rows, LANES), 0) == row.astype(jnp.int32))


def lanes_of(blocks):
    return blocks[0] if len(blocks) == 1 else jnp.concatenate(blocks, 1)


def exact_product(block, coefs):
    high, low = two(block)
    first = nn(high, coefs)
    return first[:, :LANES] + first[:, LANES:] + nn(low, coefs[:, :LANES])


def split_coefs(value):
    high, low = two(value)
    return jnp.concatenate([high, low], 1)


def tree_kernel(
    blocks, trees, order, my_leaf_ref, light_ref, place_ref, small_ref, upper_ref,
    a_ref, b_ref, sk_ref, coef_ref, pack_ref, perm, feats, sk_a,
):
    groups, width = light_ref.shape[0], light_ref.shape[1]
    per = light_ref.shape[2] // blocks
    rows = groups * per
    step = 256
    lane = iota((SK, LANES), 1)
    keep = lane >= LANES - width

    def block(index, carry):
        at = pl.ds(pl.multiple_of(index * per, LANES), per)
        points = lanes_of([place_ref[order[g], 0:64, at] for g in range(groups)])
        tail = [place_ref[order[g], 64:72, at] for g in range(groups)]
        slot = lanes_of([t[0:1] for t in tail])
        norm = lanes_of([t[1:2] for t in tail])
        light = lanes_of([light_ref[g, :, at] for g in range(groups)])
        high, low = two(points)
        nh, nm, nl = three(norm)
        sub = iota((64, rows), 0)
        extra_a = jnp.where(sub == 0, nh, jnp.where(sub == 1, nm, jnp.where(sub == 2, nl, 0.0)))
        extra_a = jnp.where((sub >= 3) & (sub < 6), 1.0, extra_a)
        extra_b = jnp.where(sub == 3, nh, jnp.where(sub == 4, nm, jnp.where(sub == 5, nl, 0.0)))
        extra_b = jnp.where(sub < 3, 1.0, extra_b)
        feats[0:64, :] = high
        feats[64:128, :] = low
        feats[128:192, :] = high
        feats[192:256, :] = extra_a.astype(bf16)
        feats[FEAT - width : FEAT, :] = light.astype(bf16)
        feats[256:320, :] = high
        feats[320:384, :] = high
        feats[384:448, :] = low
        feats[448:512, :] = extra_b.astype(bf16)
        slot_matrix(perm, [slot[:, c * LANES : (c + 1) * LANES] for c in range(rows // LANES)])
        for s in range(rows // step):
            placed = nt(perm[s * step : (s + 1) * step, :], feats[...])
            here = pl.ds(pl.multiple_of(index * rows + s * step, step), step)
            a_ref[here, :] = placed[:, :FEAT].astype(bf16)
            b_ref[here, :] = placed[:, FEAT:].astype(bf16)
        picks = column(small_ref[index, 0:1, :].astype(f32)).astype(jnp.int32)
        for c in range(rows // LANES):
            perm[0:SK, c * LANES : (c + 1) * LANES] = onehot(lane + c * LANES == picks)
        chosen = perm[0:SK, :]
        mine = pl.ds(pl.multiple_of(index * rows, rows), rows)
        own_a = nn(chosen, a_ref[mine, :]).astype(bf16)
        node = pl.ds(pl.multiple_of(index * SK, SK), SK)
        sk_a[node, :] = own_a
        sk_ref[node, :] = nn(chosen, b_ref[mine, :]).astype(bf16)
        tile = jnp.exp2(nt(own_a, b_ref[mine, :])).astype(bf16)
        coef = jnp.where(keep, nn(tile, a_ref[mine, 128:256]), 0.0)
        coef_ref[node, :] = split_coefs(coef)
        pack_ref[...] = coef
        return carry

    lax.fori_loop(0, blocks, block, 0)
    start, count, offset, total = 0, blocks, 0, blocks * trees
    while count > 1:
        nodes = count // 2
        for j in range(nodes):
            pair = slice((start + 2 * j) * SK, (start + 2 * j + 2) * SK)
            row = offset + my_leaf_ref[0] * nodes + j
            picks = column(upper_ref[pl.ds(row, 1), :].astype(f32)).astype(jnp.int32)
            chosen = jnp.concatenate([onehot(lane == picks), onehot(lane + LANES == picks)], 1)
            new = slice((start + count + j) * SK, (start + count + j + 1) * SK)
            own_a = nn(chosen, sk_a[pair, :]).astype(bf16)
            sk_a[new, :] = own_a
            sk_ref[new, :] = nn(chosen, sk_ref[pair, :]).astype(bf16)
            coef = exact_product(jnp.exp2(nt(own_a, sk_ref[pair, :])), coef_ref[pair, :])
            coef = jnp.where(keep, coef, 0.0)
            coef_ref[new, :] = split_coefs(coef)
            pack_ref[...] = coef
        total = total // 2
        offset = offset + total
        start, count = start + count, nodes
    top = slice(start * SK, (start + 1) * SK)
    own_a = sk_a[top, :].astype(f32)
    exact = own_a[:, :128] + pltpu.roll(own_a[:, :128], 64, 1)
    pack_ref[...] = jnp.where(lane < 64, exact, jnp.where(keep, pack_ref[...], own_a[:, 128:]))


def near_kernel(
    blocks, levels, far_levels, count_ref, list_ref, flag_ref, a_ref, b_ref, sk_ref, coef_ref, out_ref, times
):
    leaves = count_ref.shape[1]
    per_block = leaves // blocks

    def tally(leaf, carry):
        for other in range(leaves):
            times[leaf * leaves + other] = (leaf == other).astype(jnp.int32)

        def add(slot, carry):
            at = leaf * leaves + list_ref[leaf, slot]
            times[at] = times[at] + 1
            return carry

        return lax.fori_loop(0, count_ref[0, leaf], add, carry)

    lax.fori_loop(0, leaves, tally, 0)

    def target(leaf, carry):
        here = pl.ds(pl.multiple_of(leaf * LEAF, LEAF), LEAF)
        out_ref[here, :] = jnp.zeros((LEAF, LANES), f32)
        node, start, count = leaf // per_block, 0, blocks
        for level in range(levels):

            @pl.when(flag_ref[leaf // per_block, 1, (leaf % per_block) * far_levels + level] > 0)
            def _():
                other = pl.ds(pl.multiple_of((start + (node ^ 1)) * SK, SK), SK)
                tile = jnp.exp2(nt(a_ref[here, :], sk_ref[other, :]))
                out_ref[here, :] += exact_product(tile, coef_ref[other, :])

            node, start, count = node // 2, start + count, count // 2

        def source(other, carry):
            many = times[leaf * leaves + other]

            @pl.when(many > 0)
            def _():
                there = pl.ds(pl.multiple_of(other * LEAF, LEAF), LEAF)
                tile = jnp.exp2(nt(a_ref[here, :], b_ref[there, :])).astype(bf16)
                out_ref[here, :] += many.astype(f32) * nn(tile, a_ref[there, 128:256])

            return carry

        return lax.fori_loop(0, leaves, source, carry)

    lax.fori_loop(0, leaves, target, 0)


def back_kernel(
    blocks, order, first, levels, width, flag_ref, a_ref, near_ref, pack_ref, place_ref, out_ref, perm, sk, coefs
):
    groups = out_ref.shape[0]
    per = out_ref.shape[2] // blocks
    rows = groups * per
    ups = pack_ref.shape[0]
    lane = iota((SK, LANES), 1)
    for up in range(ups):
        pack = pack_ref[up]
        points = jnp.where(lane < 64, pack, 0.0)
        high, low = two(points)
        high, low = high.astype(f32), low.astype(f32)
        norms = pltpu.roll(jnp.where((lane >= 64) & (lane < 67), pack, 0.0), 3, 1)
        tail = jnp.where((lane >= 64) & (lane < 67), 1.0, low + norms)
        here = slice(up * SK, (up + 1) * SK)
        sk[here, 0:128] = (high + pltpu.roll(high, 64, 1)).astype(bf16)
        sk[here, 128:256] = tail.astype(bf16)
        coefs[here, :] = split_coefs(jnp.where(lane >= LANES - width, pack, 0.0))

    per_block = rows // LEAF

    def block(index, carry):
        at = pl.ds(pl.multiple_of(index * per, LANES), per)
        for g in range(groups):
            row = place_ref[order[g], 64:72, at][0:1]
            for c in range(per // LANES):
                lo = g * per + c * LANES
                perm[:, lo : lo + LANES] = onehot(
                    iota((rows, LANES), 0) == row[:, c * LANES : (c + 1) * LANES].astype(jnp.int32)
                )
        halves = []
        for leaf in range(per_block):
            here = pl.ds(pl.multiple_of(index * rows + leaf * LEAF, LEAF), LEAF)
            total = near_ref[here, :]
            for up in range(ups):
                flag = flag_ref[index, 1, leaf * levels + first + up].astype(f32)
                src = slice(up * SK, (up + 1) * SK)
                tile = jnp.exp2(nt(a_ref[here, :], sk[src, :]))
                total = total + flag * exact_product(tile, coefs[src, :])
            halves.append(jnp.transpose(total)[LANES - width :, :])
        total = jnp.concatenate(halves, 1)
        high, low = two(total)
        moved = nn(jnp.concatenate([high, low], 0), perm[...])
        moved = moved[:width] + moved[width:]
        for g in range(groups):
            out_ref[g, :, at] = moved[:, g * per : (g + 1) * per]
        return carry

    lax.fori_loop(0, blocks, block, 0)


def final_kernel(pos_ref, back_ref, weights_ref, out_ref, perm, vals):
    chunks = pos_ref.shape[0]
    rows = chunks * LANES
    split = back_ref.shape[2]
    cols = jnp.concatenate([column(pos_ref[c : c + 1, :]) for c in range(chunks)], 0).astype(jnp.int32)
    for c in range(chunks):
        perm[:, c * LANES : (c + 1) * LANES] = onehot(iota((rows, LANES), 1) + c * LANES == cols)
    for part in range(rows // split):
        high, low = two(back_ref[part])
        vals[0:LANES, part * split : (part + 1) * split] = high
        vals[LANES:, part * split : (part + 1) * split] = low
    step = 256
    for s in range(rows // step):
        here = slice(s * step, (s + 1) * step)
        moved = nt(perm[here, :], vals[...])
        out_ref[here, :] = ridge * weights_ref[here, :] + moved[:, :LANES] + moved[:, LANES:]


def vm(shape, dtype):
    return pltpu.VMEM(shape, dtype)


def body(points, weights, tree_slot, near_count, near_list, skeleton_base, skeleton_upper, far_use):
    blocks = lax.axis_size("sub")
    trees = lax.axis_size("leaf")
    devices = blocks * trees
    rows, columns = weights.shape
    levels = devices.bit_length() - 1
    low_levels = blocks.bit_length() - 1
    width = columns // blocks
    part = rows // trees
    leaves = blocks * rows // LEAF
    my_leaf = lax.axis_index("leaf")
    fine = part % 256 == 0 or part == rows
    split = part if fine else rows

    info = jnp.concatenate(
        [skeleton_base, jnp.pad(far_use.reshape(1, -1), ((0, 0), (0, SK - far_use.size)))], 0
    )
    small = lax.all_gather(info, "sub", axis=0, tiled=False)

    light, place, pos = pl.pallas_call(
        sort_kernel,
        out_shape=(
            jax.ShapeDtypeStruct((rows // split, columns, split), f32),
            jax.ShapeDtypeStruct((rows // split, PLACE_ROWS, split), f32),
            jax.ShapeDtypeStruct((rows // LANES, LANES), f32),
        ),
        in_specs=[spec()] * 3,
        out_specs=(spec(),) * 3,
        scratch_shapes=[vm((rows, rows), bf16), vm((rows, 384), bf16)],
        compiler_params=params(),
        name="sort_rows",
    )(tree_slot.reshape(rows // LANES, LANES), points, weights)

    def by_tree(array):
        if fine:
            return array
        return array.reshape(array.shape[1], trees, part).transpose(1, 0, 2)

    place = lax.all_to_all(by_tree(place), "leaf", split_axis=0, concat_axis=0, tiled=True)
    place = lax.all_gather(place, "sub", axis=0, tiled=False)
    light = by_tree(light).reshape(devices, width, part)
    light = lax.all_to_all(light, ("leaf", "sub"), split_axis=0, concat_axis=0, tiled=True)
    per = part // blocks
    if per % LANES == 0:
        place = place.reshape(devices, PLACE_ROWS, part)
        order = [sub * trees + leaf for leaf in range(trees) for sub in range(blocks)]
        groups = devices
    else:
        place = place.transpose(1, 0, 2, 3).reshape(devices, PLACE_ROWS, blocks, per)
        place = place.transpose(1, 2, 0, 3).reshape(1, PLACE_ROWS, blocks * rows)
        light = light.reshape(devices, width, blocks, per)
        light = light.transpose(1, 2, 0, 3).reshape(1, width, blocks * rows)
        order, groups = [0], 1

    total = blocks * rows
    nodes = 2 * blocks - 1
    where = my_leaf.astype(jnp.int32).reshape(1)
    feat_a, feat_b, sk, coefs, pack = pl.pallas_call(
        functools.partial(tree_kernel, blocks, trees, order),
        out_shape=(
            jax.ShapeDtypeStruct((total, FEAT), bf16),
            jax.ShapeDtypeStruct((total, FEAT), bf16),
            jax.ShapeDtypeStruct((nodes * SK, FEAT), bf16),
            jax.ShapeDtypeStruct((nodes * SK, FEAT), bf16),
            jax.ShapeDtypeStruct((SK, LANES), f32),
        ),
        in_specs=[spec(SMEM)] + [spec()] * 4,
        out_specs=(spec(),) * 5,
        scratch_shapes=[vm((rows, rows), bf16), vm((2 * FEAT, rows), bf16), vm((nodes * SK, FEAT), bf16)],
        compiler_params=params(),
        name="to_tree",
    )(where, light, place, small, skeleton_upper)

    packs = []
    own = pack
    offset = sum(devices >> level for level in range(1, low_levels + 1))
    lanes = jnp.arange(LANES)
    is_point, is_norm = (lanes < DIM)[None], ((lanes >= DIM) & (lanes < DIM + 3))[None]
    is_coef = (lanes >= LANES - width)[None]
    for level in range(low_levels, levels):
        stride = 1 << (level - low_levels)
        other = lax.ppermute(own, "leaf", [(i, i ^ stride) for i in range(trees)])
        packs.append(other)
        if level + 1 < levels:
            second = (my_leaf // stride) % 2 == 1
            pair = jnp.where(second, jnp.concatenate([other, own], 0), jnp.concatenate([own, other], 0))
            chosen = pair[skeleton_upper[offset + my_leaf // (2 * stride)]]
            offset += devices >> (level + 1)
            coords = jnp.where(is_point, pair, 0.0)
            norms = jnp.sum(jnp.where(is_norm, pair, 0.0), axis=1)
            inner = jnp.dot(jnp.where(is_point, chosen, 0.0), coords.T, precision=highest)
            tile = jnp.exp2(inner + norms[None] + jnp.sum(jnp.where(is_norm, chosen, 0.0), axis=1)[:, None])
            value = jnp.dot(tile, pair, precision=highest)
            own = jnp.where(is_coef, value, chosen)
    packs = jnp.stack(packs)

    near = pl.pallas_call(
        functools.partial(near_kernel, blocks, low_levels, levels),
        out_shape=jax.ShapeDtypeStruct((total, LANES), f32),
        in_specs=[spec(SMEM)] * 3 + [spec()] * 4,
        out_specs=spec(),
        scratch_shapes=[pltpu.SMEM((leaves * leaves,), jnp.int32)],
        compiler_params=params(),
        name="near_and_far",
    )(near_count, near_list[0], small, feat_a, feat_b, sk, coefs)

    ups = levels - low_levels
    back = pl.pallas_call(
        functools.partial(back_kernel, blocks, order, low_levels, levels, width),
        out_shape=jax.ShapeDtypeStruct((groups, width, total // groups), f32),
        in_specs=[spec(SMEM)] + [spec()] * 4,
        out_specs=spec(),
        scratch_shapes=[vm((rows, rows), bf16), vm((ups * SK, FEAT), bf16), vm((ups * SK, FEAT), bf16)],
        compiler_params=params(),
        name="back_order",
    )(small, feat_a, near, packs, place)

    if groups == 1:
        back = back.reshape(width, blocks, devices, per).transpose(2, 0, 1, 3).reshape(devices, width, part)
    back = lax.all_to_all(back, ("leaf", "sub"), split_axis=0, concat_axis=0, tiled=True)
    back = back.reshape(trees, columns, part)
    if not fine:
        back = back.transpose(1, 0, 2).reshape(1, columns, rows)

    return pl.pallas_call(
        final_kernel,
        out_shape=jax.ShapeDtypeStruct((rows, columns), f32),
        in_specs=[spec()] * 3,
        out_specs=spec(),
        scratch_shapes=[vm((rows, rows), bf16), vm((2 * LANES, rows), bf16)],
        compiler_params=params(),
        name="to_input_order",
    )(pos, back, weights)


def solution(mesh):
    in_specs = (
        P(("groups", "leaf", "sub"), None),
        P(("groups", "leaf", "sub"), "rep"),
        P(("groups", "leaf", "sub")),
        P(("groups", "leaf"), None),
        P(("groups", "leaf"), None, None),
        P(("groups", "leaf", "sub"), None),
        P("groups", None),
        P(("groups", "leaf", "sub"), None),
    )
    out_specs = P(("groups", "leaf", "sub"), "rep")
    return jax.shard_map(body, mesh=mesh, in_specs=in_specs, out_specs=out_specs, check_vma=False)
```

```python
import functools
import math

import jax
import jax.numpy as jnp
from jax import lax
from jax.experimental import pallas as pl
from jax.experimental.pallas import tpu as pltpu
from jax.sharding import PartitionSpec as P

DIM = 64
LEAF = 512
SK = 128
LANES = 128
FEAT = 256

highest = lax.Precision.HIGHEST
point_scale = math.sqrt(2.0 * math.log2(math.e) / 32.0)
ridge = 0.5
PLACE_ROWS = 72
TAIL = 64
SLOT, NORM, BASE, FLAGS = 0, 1, 2, 3
f32 = jnp.float32
bf16 = jnp.bfloat16
VMEM = pltpu.MemorySpace.VMEM
SMEM = pltpu.MemorySpace.SMEM


def spec(space=VMEM):
    return pl.BlockSpec(memory_space=space)


def params():
    return pltpu.CompilerParams(vmem_limit_bytes=48 * 1024 * 1024)


def vm(shape, dtype):
    return pltpu.VMEM(shape, dtype)


def shaped(shape, dtype):
    return jax.ShapeDtypeStruct(shape, dtype)


def nt(left, right):
    return lax.dot_general(left, right, (((1,), (1,)), ((), ())), preferred_element_type=f32)


def nn(left, right):
    return jnp.dot(left, right, preferred_element_type=f32)


def column(row):
    return jnp.transpose(jnp.broadcast_to(row, (LANES, LANES)))


def iota(shape, dim):
    return lax.broadcasted_iota(jnp.int32, shape, dim)


def onehot(mask):
    return jnp.where(mask, 1.0, 0.0).astype(bf16)


def two(value):
    high = value.astype(bf16)
    return high, (value - high.astype(f32)).astype(bf16)


def three(value):
    high = value.astype(bf16).astype(f32)
    mid = (value - high).astype(bf16).astype(f32)
    return high, mid, (value - high - mid).astype(bf16).astype(f32)


def lanes_of(blocks):
    return blocks[0] if len(blocks) == 1 else jnp.concatenate(blocks, 1)


def aligned(start, size, unit):
    return pl.ds(pl.multiple_of(start, unit), size)


def exact_product(block, coefs):
    high, low = two(block)
    first = nn(high, coefs)
    return first[:, :LANES] + first[:, LANES:] + nn(low, coefs[:, :LANES])


def split_coefs(value):
    high, low = two(value)
    return jnp.concatenate([high, low], 1)


def sort_kernel(halves, where_ref, slot_ref, points_ref, weights_ref, base_ref, flag_ref, light_ref, *refs):
    place_refs, pos_ref, perm, vals, whole = refs[:-4], refs[-4], refs[-3], refs[-2], refs[-1]
    chunks, split = slot_ref.shape[0], light_ref.shape[-1]
    rows = chunks * LANES
    slots = slot_ref[...]
    slot = slots.astype(f32)
    within = slots & (rows - 1)
    high, low = (within >> 5).astype(f32), (within & 31).astype(f32)
    cols = jnp.concatenate([column(slot[c : c + 1]) for c in range(chunks)], 0)
    before = jnp.zeros((rows, LANES), f32)
    for c in range(chunks):
        before += jnp.where(slot[c : c + 1] < cols, 1.0, 0.0)
    rank = jnp.broadcast_to(jnp.sum(before, axis=1, keepdims=True), (rows, LANES))
    place_of = rank.astype(jnp.int32)
    for c in range(chunks):
        at = slice(c * LANES, (c + 1) * LANES)
        pos_ref[c : c + 1, :] = jnp.transpose(rank[at])[0:1]
        perm[:, at] = onehot(iota((rows, LANES), 1) + c * LANES == place_of)
        vals[0:LANES, at] = jnp.transpose(weights_ref[at, :]).astype(bf16)
    scaled = points_ref[...] * point_scale
    ph, plo = two(scaled)
    nh, nm, nl = three(-0.5 * jnp.sum(scaled * scaled, axis=0, keepdims=True))
    vals[128:192, :] = ph
    vals[192:256, :] = plo
    sub = iota((16, LANES), 0)
    for c in range(chunks):
        at = slice(c * LANES, (c + 1) * LANES)
        extra = jnp.where(sub == 0, high[c : c + 1], jnp.where(sub == 1, low[c : c + 1], 0.0))
        extra = jnp.where(sub == 2, nh[:, at], jnp.where(sub == 3, nm[:, at], extra))
        vals[256:272, at] = jnp.where(sub == 4, nl[:, at], extra).astype(bf16)
    step = 256
    for s in range(rows // step):
        moved = nn(vals[...], perm[:, s * step : (s + 1) * step])
        at = slice((s * step) % split, (s * step) % split + step)
        part = (s * step) // split
        light_ref[part, :, at] = moved[0:LANES]
        whole[part, 0:TAIL, at] = moved[128:192] + moved[192:256]
        tail = iota((8, step), 0)
        slot_row = moved[256:257] * 32.0 + moved[257:258]
        norm_row = moved[258:259] + moved[259:260] + moved[260:261]
        whole[part, TAIL:, at] = jnp.where(tail == SLOT, slot_row, jnp.where(tail == NORM, norm_row, 0.0))
    if not halves:
        place_refs[0][...] = whole[...]
        return
    size = split // halves
    mine = aligned(where_ref[1] * size, size, LANES)
    for other, place in enumerate(place_refs):
        place[...] = whole[where_ref[0] ^ other, :, mine]
        place[TAIL + BASE : TAIL + BASE + 1, 0:SK] = base_ref[...].astype(f32)
        place[TAIL + FLAGS : TAIL + FLAGS + flag_ref.shape[0], 0 : flag_ref.shape[1]] = flag_ref[...].astype(f32)


class Layout:
    def __init__(self, blocks, trees, rows, halves):
        self.blocks, self.rows, self.halves = blocks, rows, halves
        self.near = [(other, sub) for other in range(trees) for sub in range(blocks)] if halves else [(0, 0)]
        self.per = rows // len(self.near)

    def place(self, refs, group, index, part):
        other, sub = self.near[group]
        if not self.halves:
            return refs[0][0, part, aligned(index * self.per, self.per, LANES)]
        each = self.blocks // self.halves
        lead = sub * self.halves + index // each
        return refs[other][lead, part, aligned((index % each) * self.per, self.per, LANES)]

    def message(self, group, leaf):
        other, sub = self.near[group]
        return (leaf ^ other) * self.blocks + sub if self.halves else 0

    def lanes(self, index):
        return aligned(index * self.per, self.per, LANES)

    def tail(self, refs, index):
        return [self.place(refs, g, index, slice(TAIL, PLACE_ROWS)) for g in range(len(self.near))]

    def info(self, refs, small_ref, index, row):
        if self.halves:
            return refs[0][index * self.halves, TAIL + row : TAIL + row + 1, 0:SK]
        return small_ref[index, row : row + 1, :]


def fill_perm(out, slot_rows):
    for c in range(out.shape[1] // LANES):
        at = slice(c * LANES, (c + 1) * LANES)
        out[:, at] = onehot(iota((out.shape[0], LANES), 0) == slot_rows[:, at].astype(jnp.int32))


def slot_row(tails):
    return lanes_of([t[SLOT : SLOT + 1] for t in tails])


def points_kernel(layout, trees, width, where_ref, upper_ref, small_ref, *refs):
    place_refs = refs[: 2 if layout.halves else 1]
    a_ref, bt_ref, skt_ref, base_ref, upper_tiles_ref, top_ref, perm, feats, sk_a = refs[len(place_refs) :]
    blocks, rows = layout.blocks, layout.rows
    groups = range(len(layout.near))
    lane = iota((SK, LANES), 1)

    def block(index, carry):
        tails = layout.tail(place_refs, index)
        points = lanes_of([layout.place(place_refs, g, index, slice(0, TAIL)) for g in groups])
        high, low = two(points)
        nh, nm, nl = three(lanes_of([t[NORM : NORM + 1] for t in tails]))
        sub = iota((64, rows), 0)
        extra_a = jnp.where(sub == 0, nh, jnp.where(sub == 1, nm, jnp.where(sub == 2, nl, 0.0)))
        extra_a = jnp.where((sub >= 3) & (sub < 6), 1.0, extra_a)
        extra_b = jnp.where(sub == 3, nh, jnp.where(sub == 4, nm, jnp.where(sub == 5, nl, 0.0)))
        extra_b = jnp.where(sub < 3, 1.0, extra_b)
        feats[0:64, :] = high
        feats[64:128, :] = low
        feats[128:192, :] = high
        feats[192:256, :] = extra_a.astype(bf16)
        feats[256:320, :] = high
        feats[320:384, :] = high
        feats[384:448, :] = low
        feats[448:512, :] = extra_b.astype(bf16)
        fill_perm(perm, slot_row(tails))
        mine = aligned(index * rows, rows, rows)
        a_ref[mine, :] = nt(perm[...], feats[0:FEAT, :]).astype(bf16)
        bt_ref[:, mine] = nt(feats[FEAT:, :], perm[...]).astype(bf16)
        picks = column(layout.info(place_refs, small_ref, index, BASE)).astype(jnp.int32)
        chosen = jnp.concatenate([onehot(lane + c * LANES == picks) for c in range(rows // LANES)], 1)
        node = aligned(index * SK, SK, SK)
        own_a = nn(chosen, a_ref[mine, :]).astype(bf16)
        sk_a[node, :] = own_a
        skt_ref[:, node] = nt(bt_ref[:, mine], chosen).astype(bf16)
        base_ref[index] = jnp.exp2(nn(own_a, bt_ref[:, mine])).astype(bf16)
        return carry

    lax.fori_loop(0, blocks, block, 0)
    start, count, offset, total = 0, blocks, 0, blocks * trees
    while count > 1:
        nodes = count // 2
        for j in range(nodes):
            pair = slice((start + 2 * j) * SK, (start + 2 * j + 2) * SK)
            row = offset + where_ref[0] * nodes + j
            picks = column(upper_ref[pl.ds(row, 1), :].astype(f32)).astype(jnp.int32)
            chosen = jnp.concatenate([onehot(lane == picks), onehot(lane + LANES == picks)], 1)
            here = start + count + j
            new = slice(here * SK, (here + 1) * SK)
            own_a = nn(chosen, sk_a[pair, :]).astype(bf16)
            sk_a[new, :] = own_a
            skt_ref[:, new] = nt(skt_ref[:, pair], chosen).astype(bf16)
            upper_tiles_ref[here - blocks] = jnp.exp2(nn(own_a, skt_ref[:, pair]))
        total = total // 2
        offset = offset + total
        start, count = start + count, nodes
    own_a = sk_a[start * SK : (start + 1) * SK, :].astype(f32)
    exact = own_a[:, :128] + pltpu.roll(own_a[:, :128], 64, 1)
    top_ref[...] = jnp.where(lane < 64, exact, own_a[:, 128:])


def weights_kernel(layout, width, where_ref, light_ref, base_ref, upper_tiles_ref, top_ref, *refs):
    place_refs = refs[: 2 if layout.halves else 1]
    w_ref, coef_ref, pack_ref, perm, feats = refs[len(place_refs) :]
    blocks, rows = layout.blocks, layout.rows
    groups = range(len(layout.near))
    feats[...] = jnp.zeros_like(feats)

    def block(index, carry):
        fill_perm(perm, slot_row(layout.tail(place_refs, index)))
        light = [light_ref[layout.message(g, where_ref[0]), :, layout.lanes(index)] for g in groups]
        feats[LANES - width :, :] = lanes_of(light).astype(bf16)
        mine = aligned(index * rows, rows, rows)
        w_ref[mine, :] = nt(perm[...], feats[...]).astype(bf16)
        coef = nn(base_ref[index], w_ref[mine, :])
        coef_ref[aligned(index * SK, SK, SK), :] = split_coefs(coef)
        pack_ref[...] = coef
        return carry

    lax.fori_loop(0, blocks, block, 0)
    start, count = 0, blocks
    while count > 1:
        for j in range(count // 2):
            pair = slice((start + 2 * j) * SK, (start + 2 * j + 2) * SK)
            here = start + count + j
            coef = exact_product(upper_tiles_ref[here - blocks], coef_ref[pair, :])
            coef_ref[here * SK : (here + 1) * SK, :] = split_coefs(coef)
            pack_ref[...] = coef
        start, count = start + count, count // 2
    pack_ref[...] = top_ref[...] + pack_ref[...]


def near_phase(first, leaves, count_ref, list_ref, a_ref, bt_ref, w_ref, acc, times, tiles, ahead):
    every = count_ref.shape[1]

    def tally(leaf, filled):
        for other in range(every):
            times[other] = (leaf == other).astype(jnp.int32)

        def add(slot, carry):
            at = list_ref[leaf, slot]
            times[at] = times[at] + 1
            return carry

        lax.fori_loop(0, count_ref[0, leaf], add, 0)
        for other in range(every):
            tiles[0, filled] = leaf
            tiles[1, filled] = other
            tiles[2, filled] = times[other]
            filled = filled + (times[other] > 0).astype(jnp.int32)
        return filled

    filled = lax.fori_loop(first, first + leaves, tally, jnp.int32(0))
    tiles[0, filled] = first
    tiles[1, filled] = 0
    half = LEAF // 2
    acc[...] = jnp.zeros_like(acc)

    def exponents(tile, part):
        target = aligned(tiles[0, tile] * LEAF, LEAF, LEAF)
        source = aligned(tiles[1, tile] * LEAF + part * half, half, half)
        return nn(a_ref[target, :], bt_ref[:, source])

    def product(tile, part, block):
        source = aligned(tiles[1, tile] * LEAF + part * half, half, half)
        return nn(block, w_ref[source, :])

    ahead[...] = exponents(0, 0)

    def step(tile, carry):
        block = jnp.exp2(ahead[...]).astype(bf16)
        second = exponents(tile, 1)
        total = product(tile, 0, block)
        ahead[...] = exponents(tile + 1, 0)
        total = total + product(tile, 1, jnp.exp2(second).astype(bf16))
        here = aligned((tiles[0, tile] - first) * LEAF, LEAF, LEAF)
        acc[here, :] += tiles[2, tile].astype(f32) * total
        return carry

    lax.fori_loop(0, filled, step, 0)


def near_kernel(first, leaves, *refs):
    near_phase(first, leaves, *refs)


def far_phase(
    layout, first, held, low_levels, where_ref, pack_ref, small_ref, place_refs, a_ref, skt_ref, coef_ref,
    acc, out_ref, perm, tops, coefs, scaled,
):
    blocks, rows = layout.blocks, layout.rows
    groups = range(len(layout.near))
    ups, width = pack_ref.shape[0], out_ref.shape[1]
    levels = low_levels + ups
    lane = iota((SK, LANES), 1)
    for up in range(ups):
        pack = pack_ref[up]
        high, low = two(jnp.where(lane < 64, pack, 0.0))
        high, low = high.astype(f32), low.astype(f32)
        is_norm = (lane >= 64) & (lane < 67)
        norms = pltpu.roll(jnp.where(is_norm, pack, 0.0), 3, 1)
        at = slice((low_levels + up) * SK, (low_levels + up + 1) * SK)
        tops[0:128, at] = jnp.transpose(high + pltpu.roll(high, 64, 1)).astype(bf16)
        tops[128:256, at] = jnp.transpose(jnp.where(is_norm, 1.0, low + norms)).astype(bf16)
        coefs[at, :] = split_coefs(jnp.where(lane >= LANES - width, pack, 0.0))

    def block(index, carry):
        node, start, count = index, 0, blocks
        for level in range(low_levels):
            at = slice(level * SK, (level + 1) * SK)
            other = aligned((start + (node ^ 1)) * SK, SK, SK)
            tops[:, at] = skt_ref[:, other]
            coefs[at, :] = coef_ref[other, :]
            node, start, count = node // 2, start + count, count // 2
        fill_perm(perm, slot_row(layout.tail(place_refs, index)))
        halves = []
        for leaf in range(rows // LEAF):
            flags = layout.info(place_refs, small_ref, index, FLAGS + leaf)
            for level in range(levels):
                at = slice(level * SK, (level + 1) * SK)
                flag = jnp.sum(jnp.where(lane[0:1] == level, flags, 0.0), axis=1, keepdims=True)
                scaled[at, :] = (coefs[at, :].astype(f32) * flag).astype(bf16)
            here = aligned(index * rows + leaf * LEAF, LEAF, LEAF)
            near = aligned((index - first) * rows + leaf * LEAF, LEAF, LEAF)
            tile = jnp.exp2(nn(a_ref[here, :], tops[...]))
            total = acc[near, :] + exact_product(tile, scaled[...])
            halves.append(jnp.transpose(total)[LANES - width :, :])
        high, low = two(jnp.concatenate(halves, 1))
        moved = nn(jnp.concatenate([high, low], 0), perm[...])
        moved = moved[:width] + moved[width:]
        for g in groups:
            out_ref[layout.message(g, where_ref[0]), :, layout.lanes(index - first)] = moved[
                :, g * layout.per : (g + 1) * layout.per
            ]
        return carry

    lax.fori_loop(first, first + held, block, 0)


def far_kernel(layout, first, held, low_levels, where_ref, pack_ref, small_ref, *refs):
    count = 2 if layout.halves else 1
    far_phase(layout, first, held, low_levels, where_ref, pack_ref, small_ref, refs[:count], *refs[count:])


def both_kernel(layout, first, held, low_levels, where_ref, pack_ref, small_ref, *refs):
    count = 2 if layout.halves else 1
    place_refs, refs = refs[:count], refs[count:]
    count_ref, list_ref, a_ref, bt_ref, w_ref, skt_ref, coef_ref, out_ref = refs[:8]
    acc, times, tiles, ahead, perm, tops, coefs, scaled = refs[8:]
    leaves = held * layout.rows // LEAF
    first_leaf = first * layout.rows // LEAF
    near_phase(first_leaf, leaves, count_ref, list_ref, a_ref, bt_ref, w_ref, acc, times, tiles, ahead)
    far_phase(
        layout, first, held, low_levels, where_ref, pack_ref, small_ref, place_refs, a_ref, skt_ref, coef_ref,
        acc, out_ref, perm, tops, coefs, scaled,
    )


def final_kernel(pos_ref, *refs):
    back_refs, (weights_ref, out_ref, perm, vals) = refs[:-4], refs[-4:]
    chunks = pos_ref.shape[0]
    rows = chunks * LANES
    split = back_refs[0].shape[2]
    cols = jnp.concatenate([column(pos_ref[c : c + 1, :]) for c in range(chunks)], 0).astype(jnp.int32)
    for c in range(chunks):
        perm[:, c * LANES : (c + 1) * LANES] = onehot(iota((rows, LANES), 1) + c * LANES == cols)
    for part in range(back_refs[0].shape[0]):
        for half, back_ref in enumerate(back_refs):
            high, low = two(back_ref[part])
            at = (part * len(back_refs) + half) * split
            vals[0:LANES, at : at + split] = high
            vals[LANES:, at : at + split] = low
    step = 256
    for s in range(rows // step):
        here = slice(s * step, (s + 1) * step)
        moved = nt(perm[here, :], vals[...])
        out_ref[here, :] = ridge * weights_ref[here, :] + moved[:, :LANES] + moved[:, LANES:]


def upper_levels(pack, skeleton_upper, my_leaf, trees, blocks, width):
    devices = trees * blocks
    level = blocks.bit_length() - 1
    offset = sum(devices >> step for step in range(1, level + 1))
    lanes = jnp.arange(LANES)[None]
    is_point, is_norm = lanes < DIM, (lanes >= DIM) & (lanes < DIM + 3)
    is_coef = lanes >= LANES - width
    packs, own, stride = [], pack, 1
    while stride < trees:
        other = lax.ppermute(own, "leaf", [(i, i ^ stride) for i in range(trees)])
        packs.append(other)
        stride *= 2
        if stride < trees:
            second = (my_leaf // (stride // 2)) % 2 == 1
            pair = jnp.where(second, jnp.concatenate([other, own], 0), jnp.concatenate([own, other], 0))
            chosen = pair[skeleton_upper[offset + my_leaf // stride]]
            level += 1
            offset += devices >> level
            norms = jnp.sum(jnp.where(is_norm, pair, 0.0), axis=1)
            chosen_norms = jnp.sum(jnp.where(is_norm, chosen, 0.0), axis=1)
            inner = jnp.dot(
                jnp.where(is_point, chosen, 0.0), jnp.where(is_point, pair, 0.0).T, precision=highest
            )
            tile = jnp.exp2(inner + norms[None] + chosen_norms[:, None])
            own = jnp.where(is_coef, jnp.dot(tile, pair, precision=highest), chosen)
    return jnp.stack(packs)


def body(points, weights, tree_slot, near_count, near_list, skeleton_base, skeleton_upper, far_use):
    blocks, trees, reps = lax.axis_size("sub"), lax.axis_size("leaf"), lax.axis_size("rep")
    devices = blocks * trees
    rows, columns = weights.shape
    low_levels = blocks.bit_length() - 1
    ups = trees.bit_length() - 1
    width = columns // blocks
    part = rows // trees
    per = part // blocks
    total = blocks * rows
    leaves = total // LEAF
    my_leaf = lax.axis_index("leaf")
    fine = trees == 2 and per % LANES == 0 and blocks % reps == 0
    halves = reps if fine else 0
    layout = Layout(blocks, trees, rows, halves)
    split = part if fine else rows
    where = jnp.stack([my_leaf, lax.axis_index("rep")]).astype(jnp.int32)

    if fine:
        place_shapes = (shaped((PLACE_ROWS, split // halves), f32),) * trees
    else:
        place_shapes = (shaped((rows // split, PLACE_ROWS, split), f32),)
    light, *place, pos = pl.pallas_call(
        functools.partial(sort_kernel, halves),
        out_shape=(shaped((rows // split, columns, split), f32),) + place_shapes + (shaped((rows // LANES, LANES), f32),),
        in_specs=[spec(SMEM)] + [spec()] * 5,
        out_specs=(spec(),) * (2 + len(place_shapes)),
        scratch_shapes=[
            vm((rows, rows), bf16),
            vm((272, rows), bf16),
            vm((rows // split, PLACE_ROWS, split), f32),
        ],
        compiler_params=params(),
        name="sort_rows",
    )(where, tree_slot.reshape(rows // LANES, LANES), points.T, weights, skeleton_base, far_use)

    if fine:
        own, sent = place
        got = lax.ppermute(sent, "leaf", [(0, 1), (1, 0)])
        place = [lax.all_gather(one, ("sub", "rep"), axis=0, tiled=False) for one in (own, got)]
        light = light.reshape(devices, width, part)
        light = lax.all_to_all(light, ("leaf", "sub"), split_axis=0, concat_axis=0, tiled=True)
        small = jnp.zeros((1, 8, SK), f32)
    else:
        info = jnp.pad(far_use.astype(f32), ((FLAGS, 5 - far_use.shape[0]), (0, SK - far_use.shape[1])))
        small = lax.all_gather(info.at[BASE].set(skeleton_base[0].astype(f32)), "sub", axis=0, tiled=False)
        place = place[0].reshape(PLACE_ROWS, trees, part).transpose(1, 0, 2)
        place = lax.all_to_all(place, "leaf", split_axis=0, concat_axis=0, tiled=True)
        place = lax.all_gather(place, "sub", axis=0, tiled=False)
        place = place.transpose(1, 0, 2, 3).reshape(devices, PLACE_ROWS, blocks, per)
        place = [place.transpose(1, 2, 0, 3).reshape(1, PLACE_ROWS, total)]
        light = light.reshape(columns, trees, part).transpose(1, 0, 2).reshape(devices, width, part)
        light = lax.all_to_all(light, ("leaf", "sub"), split_axis=0, concat_axis=0, tiled=True)
        light = light.reshape(devices, width, blocks, per)
        light = light.transpose(1, 2, 0, 3).reshape(1, width, total)

    nodes = 2 * blocks - 1
    kept = len(place)
    feat_a, feat_bt, sk, base, upper_tiles, top = pl.pallas_call(
        functools.partial(points_kernel, layout, trees, width),
        out_shape=(
            shaped((total, FEAT), bf16),
            shaped((FEAT, total), bf16),
            shaped((FEAT, nodes * SK), bf16),
            shaped((blocks, SK, rows), bf16),
            shaped((blocks - 1, SK, 2 * SK), f32),
            shaped((SK, LANES), f32),
        ),
        in_specs=[spec(SMEM)] + [spec()] * (2 + kept),
        out_specs=(spec(),) * 6,
        scratch_shapes=[vm((rows, rows), bf16), vm((2 * FEAT, rows), bf16), vm((nodes * SK, FEAT), bf16)],
        compiler_params=params(),
        name="tree_points",
    )(where, skeleton_upper, small, *place)

    tree_light, coefs, pack = pl.pallas_call(
        functools.partial(weights_kernel, layout, width),
        out_shape=(
            shaped((total, LANES), bf16),
            shaped((nodes * SK, FEAT), bf16),
            shaped((SK, LANES), f32),
        ),
        in_specs=[spec(SMEM)] + [spec()] * (4 + kept),
        out_specs=(spec(),) * 3,
        scratch_shapes=[vm((rows, rows), bf16), vm((LANES, rows), bf16)],
        compiler_params=params(),
        name="tree_weights",
    )(where, light, base, upper_tiles, top, *place)

    packs = upper_levels(pack, skeleton_upper, my_leaf, trees, blocks, width)

    held = blocks // 2
    levels = low_levels + ups
    near_scratch = [
        pltpu.SMEM((leaves,), jnp.int32),
        pltpu.SMEM((3, leaves * leaves + 1), jnp.int32),
        vm((LEAF, LEAF // 2), f32),
    ]
    far_scratch = [
        vm((rows, rows), bf16),
        vm((FEAT, levels * SK), bf16),
        vm((levels * SK, FEAT), bf16),
        vm((levels * SK, FEAT), bf16),
    ]
    if fine:
        out_shape = shaped((devices, width, part // 2), f32)
    else:
        out_shape = shaped((1, width, total // 2), f32)
    near = pl.pallas_call(
        functools.partial(near_kernel, 0, leaves // 2),
        out_shape=shaped((total // 2, LANES), f32),
        in_specs=[spec(SMEM)] * 2 + [spec()] * 3,
        out_specs=spec(),
        scratch_shapes=near_scratch,
        compiler_params=params(),
        name="near_first",
    )(near_count, near_list[0], feat_a, feat_bt, tree_light)
    first_out = pl.pallas_call(
        functools.partial(far_kernel, layout, 0, held, low_levels),
        out_shape=out_shape,
        in_specs=[spec(SMEM)] + [spec()] * (6 + kept),
        out_specs=spec(),
        scratch_shapes=far_scratch,
        compiler_params=params(),
        name="far_first",
    )(where, packs, small, *place, feat_a, sk, coefs, near)
    second_out = pl.pallas_call(
        functools.partial(both_kernel, layout, held, blocks - held, low_levels),
        out_shape=out_shape,
        in_specs=[spec(SMEM)] + [spec()] * (2 + kept) + [spec(SMEM)] * 2 + [spec()] * 5,
        out_specs=spec(),
        scratch_shapes=[vm((total // 2, LANES), f32)] + near_scratch + far_scratch,
        compiler_params=params(),
        name="near_far_second",
    )(where, packs, small, *place, near_count, near_list[0], feat_a, feat_bt, tree_light, sk, coefs)

    def give_back(out):
        if not fine:
            out = out.reshape(width, held, devices, per).transpose(2, 0, 1, 3).reshape(devices, width, part // 2)
        out = lax.all_to_all(out, ("leaf", "sub"), split_axis=0, concat_axis=0, tiled=True)
        return out.reshape(trees, columns, part // 2)

    back = [give_back(first_out), give_back(second_out)]
    if not fine:
        back = jnp.concatenate(back, 2).transpose(1, 0, 2).reshape(1, columns, rows)
        back = [back]

    return pl.pallas_call(
        final_kernel,
        out_shape=shaped((rows, columns), f32),
        in_specs=[spec()] * (2 + len(back)),
        out_specs=spec(),
        scratch_shapes=[vm((rows, rows), bf16), vm((2 * LANES, rows), bf16)],
        compiler_params=params(),
        name="to_input_order",
    )(pos, *back, weights)


def solution(mesh):
    in_specs = (
        P(("groups", "leaf", "sub"), None),
        P(("groups", "leaf", "sub"), "rep"),
        P(("groups", "leaf", "sub")),
        P(("groups", "leaf"), None),
        P(("groups", "leaf"), None, None),
        P(("groups", "leaf", "sub"), None),
        P("groups", None),
        P(("groups", "leaf", "sub"), None),
    )
    out_specs = P(("groups", "leaf", "sub"), "rep")
    return jax.shard_map(body, mesh=mesh, in_specs=in_specs, out_specs=out_specs, check_vma=False)
```

```python
import functools
import math

import jax
import jax.numpy as jnp
from jax import lax
from jax.experimental import pallas as pl
from jax.experimental.pallas import tpu as pltpu
from jax.sharding import PartitionSpec as P

DIM = 64
LEAF = 512
SK = 128
LANES = 128
FEAT = 256

highest = lax.Precision.HIGHEST
point_scale = math.sqrt(2.0 * math.log2(math.e) / 32.0)
ridge = 0.5
PLACE_ROWS = 72
TAIL = 64
SLOT, NORM, BASE, FLAGS = 0, 1, 2, 3
f32 = jnp.float32
bf16 = jnp.bfloat16
VMEM = pltpu.MemorySpace.VMEM
SMEM = pltpu.MemorySpace.SMEM


def spec(space=VMEM):
    return pl.BlockSpec(memory_space=space)


def params():
    return pltpu.CompilerParams(vmem_limit_bytes=58 * 1024 * 1024)


def vm(shape, dtype):
    return pltpu.VMEM(shape, dtype)


def shaped(shape, dtype):
    return jax.ShapeDtypeStruct(shape, dtype)


def nt(left, right):
    return lax.dot_general(left, right, (((1,), (1,)), ((), ())), preferred_element_type=f32)


def nn(left, right):
    return jnp.dot(left, right, preferred_element_type=f32)


def column(row):
    return jnp.transpose(jnp.broadcast_to(row, (LANES, LANES)))


def iota(shape, dim):
    return lax.broadcasted_iota(jnp.int32, shape, dim)


def onehot(mask):
    return jnp.where(mask, 1.0, 0.0).astype(bf16)


def two(value):
    high = value.astype(bf16)
    return high, (value - high.astype(f32)).astype(bf16)


def three(value):
    high = value.astype(bf16).astype(f32)
    mid = (value - high).astype(bf16).astype(f32)
    return high, mid, (value - high - mid).astype(bf16).astype(f32)


def lanes_of(blocks):
    return blocks[0] if len(blocks) == 1 else jnp.concatenate(blocks, 1)


def aligned(start, size, unit):
    return pl.ds(pl.multiple_of(start, unit), size)


def exact_product(block, coefs):
    high, low = two(block)
    first = nn(high, coefs)
    return first[:, :LANES] + first[:, LANES:] + nn(low, coefs[:, :LANES])


def split_coefs(value):
    high, low = two(value)
    return jnp.concatenate([high, low], 1)


def sort_kernel(blocks, where_ref, slot_ref, points_ref, weights_ref, base_ref, flag_ref, place_ref, pos_ref, *refs):
    light_refs, (perm, vals, whole, light) = refs[:-4], refs[-4:]
    chunks, split = slot_ref.shape[0], light.shape[-1]
    rows = chunks * LANES
    slots = slot_ref[...]
    slot = slots.astype(f32)
    within = slots & (rows - 1)
    high, low = (within >> 5).astype(f32), (within & 31).astype(f32)
    cols = jnp.concatenate([column(slot[c : c + 1]) for c in range(chunks)], 0)
    before = jnp.zeros((rows, LANES), f32)
    for c in range(chunks):
        before += jnp.where(slot[c : c + 1] < cols, 1.0, 0.0)
    rank = jnp.broadcast_to(jnp.sum(before, axis=1, keepdims=True), (rows, LANES))
    place_of = rank.astype(jnp.int32)
    for c in range(chunks):
        at = slice(c * LANES, (c + 1) * LANES)
        pos_ref[c : c + 1, :] = jnp.transpose(rank[at])[0:1]
        perm[:, at] = onehot(iota((rows, LANES), 1) + c * LANES == place_of)
        vals[0:LANES, at] = jnp.transpose(weights_ref[at, :]).astype(bf16)
    scaled = points_ref[...] * point_scale
    ph, plo = two(scaled)
    nh, nm, nl = three(-0.5 * jnp.sum(scaled * scaled, axis=0, keepdims=True))
    vals[128:192, :] = ph
    vals[192:256, :] = plo
    sub = iota((16, LANES), 0)
    for c in range(chunks):
        at = slice(c * LANES, (c + 1) * LANES)
        extra = jnp.where(sub == 0, high[c : c + 1], jnp.where(sub == 1, low[c : c + 1], 0.0))
        extra = jnp.where(sub == 2, nh[:, at], jnp.where(sub == 3, nm[:, at], extra))
        vals[256:272, at] = jnp.where(sub == 4, nl[:, at], extra).astype(bf16)
    step = 256
    for s in range(rows // step):
        moved = nn(vals[...], perm[:, s * step : (s + 1) * step])
        at = slice((s * step) % split, (s * step) % split + step)
        part = (s * step) // split
        light[part, :, at] = moved[0:LANES]
        whole[part, 0:TAIL, at] = moved[128:192] + moved[192:256]
        tail = iota((8, step), 0)
        slot_row = moved[256:257] * 32.0 + moved[257:258]
        norm_row = moved[258:259] + moved[259:260] + moved[260:261]
        whole[part, TAIL:, at] = jnp.where(tail == SLOT, slot_row, jnp.where(tail == NORM, norm_row, 0.0))
    if not blocks:
        place_ref[...] = whole[0]
        light_refs[0][...] = light[0]
        return
    leaf, sub, core = where_ref[0], where_ref[1], where_ref[2]
    place_ref[...] = whole[leaf ^ core]
    place_ref[TAIL + BASE : TAIL + BASE + 1, 0:SK] = base_ref[...].astype(f32)
    place_ref[TAIL + FLAGS : TAIL + FLAGS + flag_ref.shape[0], 0 : flag_ref.shape[1]] = flag_ref[...].astype(f32)
    width = LANES // blocks
    for g, light_ref in enumerate(light_refs):
        columns = aligned((sub ^ (g % blocks)) * width, width, width)
        light_ref[...] = light[leaf ^ core ^ (g // blocks), columns, :]


class Layout:
    def __init__(self, blocks, trees, rows, fine):
        self.blocks, self.rows, self.fine = blocks, rows, fine
        self.count = blocks * trees if fine else 1
        self.per = rows // self.count

    def lanes(self, index):
        return aligned(index * self.per, self.per, LANES)

    def gather(self, refs, index, part):
        return lanes_of([ref[part, self.lanes(index)] for ref in refs])

    def info(self, where_ref, refs, small_ref, index):
        if not self.fine:
            return small_ref[index]
        core = where_ref[2]
        found = jnp.zeros((PLACE_ROWS - TAIL, SK), f32)
        for step in range(self.blocks):
            mine, theirs = refs[step][TAIL:, 0:SK], refs[self.blocks + step][TAIL:, 0:SK]
            here = jnp.where(core == 0, mine, theirs)
            found = jnp.where((where_ref[1] ^ step) == index, here, found)
        return found


def fill_perm(out, slot_rows):
    for c in range(out.shape[1] // LANES):
        at = slice(c * LANES, (c + 1) * LANES)
        out[:, at] = onehot(iota((out.shape[0], LANES), 0) == slot_rows[:, at].astype(jnp.int32))


def points_kernel(layout, trees, where_ref, upper_ref, small_ref, *refs):
    place_refs, refs = refs[: layout.count], refs[layout.count :]
    a_ref, bt_ref, skt_ref, base_ref, upper_tiles_ref, top_ref, slot_ref, info_ref, perm, feats, sk_a = refs
    blocks, rows = layout.blocks, layout.rows
    lane = iota((SK, LANES), 1)

    def block(index, carry):
        tail = layout.gather(place_refs, index, slice(TAIL, PLACE_ROWS))
        slots = tail[SLOT : SLOT + 1]
        slot_ref[pl.ds(index, 1), :] = slots
        info = layout.info(where_ref, place_refs, small_ref, index)
        info_ref[index] = info
        points = layout.gather(place_refs, index, slice(0, TAIL))
        high, low = two(points)
        nh, nm, nl = three(tail[NORM : NORM + 1])
        sub = iota((64, rows), 0)
        extra_a = jnp.where(sub == 0, nh, jnp.where(sub == 1, nm, jnp.where(sub == 2, nl, 0.0)))
        extra_a = jnp.where((sub >= 3) & (sub < 6), 1.0, extra_a)
        extra_b = jnp.where(sub == 3, nh, jnp.where(sub == 4, nm, jnp.where(sub == 5, nl, 0.0)))
        extra_b = jnp.where(sub < 3, 1.0, extra_b)
        feats[0:64, :] = high
        feats[64:128, :] = low
        feats[128:192, :] = high
        feats[192:256, :] = extra_a.astype(bf16)
        feats[256:320, :] = high
        feats[320:384, :] = high
        feats[384:448, :] = low
        feats[448:512, :] = extra_b.astype(bf16)
        fill_perm(perm, slots)
        mine = aligned(index * rows, rows, rows)
        a_ref[mine, :] = nt(perm[...], feats[0:FEAT, :]).astype(bf16)
        bt_ref[:, mine] = nt(feats[FEAT:, :], perm[...]).astype(bf16)
        picks = column(info[BASE : BASE + 1]).astype(jnp.int32)
        chosen = jnp.concatenate([onehot(lane + c * LANES == picks) for c in range(rows // LANES)], 1)
        node = aligned(index * SK, SK, SK)
        own_a = nn(chosen, a_ref[mine, :]).astype(bf16)
        sk_a[node, :] = own_a
        skt_ref[:, node] = nt(bt_ref[:, mine], chosen).astype(bf16)
        base_ref[index] = jnp.exp2(nn(own_a, bt_ref[:, mine])).astype(bf16)
        return carry

    lax.fori_loop(0, blocks, block, 0)
    start, count, offset, total = 0, blocks, 0, blocks * trees
    while count > 1:
        nodes = count // 2
        for j in range(nodes):
            pair = slice((start + 2 * j) * SK, (start + 2 * j + 2) * SK)
            row = offset + where_ref[0] * nodes + j
            picks = column(upper_ref[pl.ds(row, 1), :].astype(f32)).astype(jnp.int32)
            chosen = jnp.concatenate([onehot(lane == picks), onehot(lane + LANES == picks)], 1)
            here = start + count + j
            new = slice(here * SK, (here + 1) * SK)
            own_a = nn(chosen, sk_a[pair, :]).astype(bf16)
            sk_a[new, :] = own_a
            skt_ref[:, new] = nt(skt_ref[:, pair], chosen).astype(bf16)
            upper_tiles_ref[here - blocks] = jnp.exp2(nn(own_a, skt_ref[:, pair]))
        total = total // 2
        offset = offset + total
        start, count = start + count, nodes
    own_a = sk_a[start * SK : (start + 1) * SK, :].astype(f32)
    exact = own_a[:, :128] + pltpu.roll(own_a[:, :128], 64, 1)
    top_ref[...] = jnp.where(lane < 64, exact, own_a[:, 128:])


def weights_kernel(layout, base_ref, upper_tiles_ref, top_ref, slot_ref, *refs):
    light_refs, (w_ref, coef_ref, pack_ref, perm, feats) = refs[: layout.count], refs[layout.count :]
    blocks, rows = layout.blocks, layout.rows
    width = light_refs[0].shape[0]
    feats[...] = jnp.zeros_like(feats)

    def block(index, carry):
        fill_perm(perm, slot_ref[pl.ds(index, 1), :])
        feats[LANES - width :, :] = layout.gather(light_refs, index, slice(0, width)).astype(bf16)
        mine = aligned(index * rows, rows, rows)
        w_ref[mine, :] = nt(perm[...], feats[...]).astype(bf16)
        coef = nn(base_ref[index], w_ref[mine, :])
        coef_ref[aligned(index * SK, SK, SK), :] = split_coefs(coef)
        pack_ref[...] = coef
        return carry

    lax.fori_loop(0, blocks, block, 0)
    start, count = 0, blocks
    while count > 1:
        for j in range(count // 2):
            pair = slice((start + 2 * j) * SK, (start + 2 * j + 2) * SK)
            here = start + count + j
            coef = exact_product(upper_tiles_ref[here - blocks], coef_ref[pair, :])
            coef_ref[here * SK : (here + 1) * SK, :] = split_coefs(coef)
            pack_ref[...] = coef
        start, count = start + count, count // 2
    pack_ref[...] = top_ref[...] + pack_ref[...]


def near_kernel(count_ref, list_ref, a_ref, bt_ref, w_ref, acc, times, tiles, ahead):
    every = count_ref.shape[1]

    def tally(leaf, filled):
        for other in range(every):
            times[other] = (leaf == other).astype(jnp.int32)

        def add(slot, carry):
            at = list_ref[leaf, slot]
            times[at] = times[at] + 1
            return carry

        lax.fori_loop(0, count_ref[0, leaf], add, 0)
        for other in range(every):
            tiles[0, filled] = leaf
            tiles[1, filled] = other
            tiles[2, filled] = times[other]
            filled = filled + (times[other] > 0).astype(jnp.int32)
        return filled

    filled = lax.fori_loop(0, every, tally, jnp.int32(0))
    tiles[0, filled] = 0
    tiles[1, filled] = 0
    half = LEAF // 2
    acc[...] = jnp.zeros_like(acc)

    def exponents(tile, part):
        target = aligned(tiles[0, tile] * LEAF, LEAF, LEAF)
        source = aligned(tiles[1, tile] * LEAF + part * half, half, half)
        return nn(a_ref[target, :], bt_ref[:, source])

    def product(tile, part, block):
        source = aligned(tiles[1, tile] * LEAF + part * half, half, half)
        return nn(block, w_ref[source, :])

    ahead[...] = exponents(0, 0)

    def step(tile, carry):
        block = jnp.exp2(ahead[...]).astype(bf16)
        second = exponents(tile, 1)
        total = product(tile, 0, block)
        ahead[...] = exponents(tile + 1, 0)
        total = total + product(tile, 1, jnp.exp2(second).astype(bf16))
        here = aligned(tiles[0, tile] * LEAF, LEAF, LEAF)
        acc[here, :] += tiles[2, tile].astype(f32) * total
        return carry

    lax.fori_loop(0, filled, step, 0)


def far_kernel(layout, low_levels, pack_ref, slot_ref, info_ref, a_ref, skt_ref, coef_ref, near_ref, *refs):
    out_refs, (perm, tops, coefs, scaled) = refs[: layout.count], refs[layout.count :]
    blocks, rows = layout.blocks, layout.rows
    ups, width = pack_ref.shape[0], out_refs[0].shape[0]
    levels = low_levels + ups
    lane = iota((SK, LANES), 1)
    for up in range(ups):
        pack = pack_ref[up]
        high, low = two(jnp.where(lane < 64, pack, 0.0))
        high, low = high.astype(f32), low.astype(f32)
        is_norm = (lane >= 64) & (lane < 67)
        norms = pltpu.roll(jnp.where(is_norm, pack, 0.0), 3, 1)
        at = slice((low_levels + up) * SK, (low_levels + up + 1) * SK)
        tops[0:128, at] = jnp.transpose(high + pltpu.roll(high, 64, 1)).astype(bf16)
        tops[128:256, at] = jnp.transpose(jnp.where(is_norm, 1.0, low + norms)).astype(bf16)
        coefs[at, :] = split_coefs(jnp.where(lane >= LANES - width, pack, 0.0))

    def block(index, carry):
        node, start, count = index, 0, blocks
        for level in range(low_levels):
            at = slice(level * SK, (level + 1) * SK)
            other = aligned((start + (node ^ 1)) * SK, SK, SK)
            tops[:, at] = skt_ref[:, other]
            coefs[at, :] = coef_ref[other, :]
            node, start, count = node // 2, start + count, count // 2
        fill_perm(perm, slot_ref[pl.ds(index, 1), :])
        info = info_ref[index]
        halves = []
        for leaf in range(rows // LEAF):
            flags = info[FLAGS + leaf : FLAGS + leaf + 1]
            for level in range(levels):
                at = slice(level * SK, (level + 1) * SK)
                flag = jnp.sum(jnp.where(lane[0:1] == level, flags, 0.0), axis=1, keepdims=True)
                scaled[at, :] = (coefs[at, :].astype(f32) * flag).astype(bf16)
            here = aligned(index * rows + leaf * LEAF, LEAF, LEAF)
            tile = jnp.exp2(nn(a_ref[here, :], tops[...]))
            total = near_ref[here, :] + exact_product(tile, scaled[...])
            halves.append(jnp.transpose(total)[LANES - width :, :])
        high, low = two(jnp.concatenate(halves, 1))
        moved = nn(jnp.concatenate([high, low], 0), perm[...])
        moved = moved[:width] + moved[width:]
        for g, out_ref in enumerate(out_refs):
            out_ref[:, layout.lanes(index)] = moved[:, g * layout.per : (g + 1) * layout.per]
        return carry

    lax.fori_loop(0, blocks, block, 0)


def final_kernel(blocks, where_ref, pos_ref, *refs):
    back_refs, (weights_ref, out_ref, perm, vals) = refs[:-4], refs[-4:]
    chunks = pos_ref.shape[0]
    rows = chunks * LANES
    width, split = back_refs[0].shape
    cols = jnp.concatenate([column(pos_ref[c : c + 1, :]) for c in range(chunks)], 0).astype(jnp.int32)
    for c in range(chunks):
        perm[:, c * LANES : (c + 1) * LANES] = onehot(iota((rows, LANES), 1) + c * LANES == cols)
    for g, back_ref in enumerate(back_refs):
        high, low = two(back_ref[...])
        columns, at = 0, slice(0, rows)
        if blocks:
            columns = (where_ref[1] ^ (g % blocks)) * width
            at = aligned((where_ref[0] ^ where_ref[2] ^ (g // blocks)) * split, split, split)
        vals[aligned(columns, width, width), at] = high
        vals[aligned(columns + LANES, width, width), at] = low
    step = 256
    for s in range(rows // step):
        here = slice(s * step, (s + 1) * step)
        moved = nt(perm[here, :], vals[...])
        out_ref[here, :] = ridge * weights_ref[here, :] + moved[:, :LANES] + moved[:, LANES:]


def upper_levels(pack, skeleton_upper, my_leaf, trees, blocks, width):
    devices = trees * blocks
    level = blocks.bit_length() - 1
    offset = sum(devices >> step for step in range(1, level + 1))
    lanes = jnp.arange(LANES)[None]
    is_point, is_norm = lanes < DIM, (lanes >= DIM) & (lanes < DIM + 3)
    is_coef = lanes >= LANES - width
    packs, own, stride = [], pack, 1
    while stride < trees:
        other = lax.ppermute(own, "leaf", [(i, i ^ stride) for i in range(trees)])
        packs.append(other)
        stride *= 2
        if stride < trees:
            second = (my_leaf // (stride // 2)) % 2 == 1
            pair = jnp.where(second, jnp.concatenate([other, own], 0), jnp.concatenate([own, other], 0))
            chosen = pair[skeleton_upper[offset + my_leaf // stride]]
            level += 1
            offset += devices >> level
            norms = jnp.sum(jnp.where(is_norm, pair, 0.0), axis=1)
            chosen_norms = jnp.sum(jnp.where(is_norm, chosen, 0.0), axis=1)
            inner = jnp.dot(
                jnp.where(is_point, chosen, 0.0), jnp.where(is_point, pair, 0.0).T, precision=highest
            )
            tile = jnp.exp2(inner + norms[None] + chosen_norms[:, None])
            own = jnp.where(is_coef, jnp.dot(tile, pair, precision=highest), chosen)
    return jnp.stack(packs)


def body(points, weights, tree_slot, near_count, near_list, skeleton_base, skeleton_upper, far_use):
    blocks, trees, reps = lax.axis_size("sub"), lax.axis_size("leaf"), lax.axis_size("rep")
    devices = blocks * trees
    rows, columns = weights.shape
    low_levels = blocks.bit_length() - 1
    ups = trees.bit_length() - 1
    width = columns // blocks
    part = rows // trees
    per = part // blocks
    total = blocks * rows
    leaves = total // LEAF
    my_leaf = lax.axis_index("leaf")
    fine = trees == 2 and reps == 2 and per % LANES == 0
    layout = Layout(blocks, trees, rows, fine)
    split = part if fine else rows
    where = jnp.stack([my_leaf, lax.axis_index("sub"), lax.axis_index("rep")]).astype(jnp.int32)
    message = shaped((width, part), f32) if fine else shaped((columns, rows), f32)
    arrive = shaped((width, part), f32) if fine else shaped((width, total), f32)

    place, pos, *light = pl.pallas_call(
        functools.partial(sort_kernel, blocks if fine else 0),
        out_shape=(shaped((PLACE_ROWS, split), f32), shaped((rows // LANES, LANES), f32)) + (message,) * layout.count,
        in_specs=[spec(SMEM)] + [spec()] * 5,
        out_specs=(spec(),) * (2 + layout.count),
        scratch_shapes=[
            vm((rows, rows), bf16),
            vm((272, rows), bf16),
            vm((rows // split, PLACE_ROWS, split), f32),
            vm((rows // split, columns, split), f32),
        ],
        compiler_params=params(),
        name="sort_rows",
    )(where, tree_slot.reshape(rows // LANES, LANES), points.T, weights, skeleton_base, far_use)

    axes = ("leaf", "sub", "rep")

    def swap(value, step, other=0):
        pairs = []
        for leaf in range(trees):
            for sub in range(blocks):
                for core in range(reps):
                    to = ((leaf ^ core ^ other) * blocks + (sub ^ step)) * reps + core
                    pairs.append(((leaf * blocks + sub) * reps + core, to))
        return lax.ppermute(value, axes, pairs)

    def swap_all(values):
        return [swap(value, g % blocks, g // blocks) for g, value in enumerate(values)]

    if fine:
        place = {0: swap(place, 0)}
        stride = blocks // 2
        while stride:
            for step in sorted(place):
                place[step | stride] = lax.ppermute(place[step], "sub", [(i, i ^ stride) for i in range(blocks)])
            stride //= 2
        place = [place[step] for step in range(blocks)]
        place = place + [lax.ppermute(one, "rep", [(0, 1), (1, 0)]) for one in place]
        light = swap_all(light)
        small = jnp.zeros((1, 8, SK), f32)
    else:
        info = jnp.pad(far_use.astype(f32), ((FLAGS, 5 - far_use.shape[0]), (0, SK - far_use.shape[1])))
        small = lax.all_gather(info.at[BASE].set(skeleton_base[0].astype(f32)), "sub", axis=0, tiled=False)
        place = place.reshape(PLACE_ROWS, trees, part).transpose(1, 0, 2)
        place = lax.all_to_all(place, "leaf", split_axis=0, concat_axis=0, tiled=True)
        place = lax.all_gather(place, "sub", axis=0, tiled=False)
        place = place.transpose(1, 0, 2, 3).reshape(devices, PLACE_ROWS, blocks, per)
        place = [place.transpose(1, 2, 0, 3).reshape(PLACE_ROWS, total)]
        light = light[0].reshape(columns, trees, part).transpose(1, 0, 2).reshape(devices, width, part)
        light = lax.all_to_all(light, ("leaf", "sub"), split_axis=0, concat_axis=0, tiled=True)
        light = light.reshape(devices, width, blocks, per)
        light = [light.transpose(1, 2, 0, 3).reshape(width, total)]

    nodes = 2 * blocks - 1
    feat_a, feat_bt, sk, base, upper_tiles, top, slots, info = pl.pallas_call(
        functools.partial(points_kernel, layout, trees),
        out_shape=(
            shaped((total, FEAT), bf16),
            shaped((FEAT, total), bf16),
            shaped((FEAT, nodes * SK), bf16),
            shaped((blocks, SK, rows), bf16),
            shaped((blocks - 1, SK, 2 * SK), f32),
            shaped((SK, LANES), f32),
            shaped((blocks, rows), f32),
            shaped((blocks, 8, SK), f32),
        ),
        in_specs=[spec(SMEM)] + [spec()] * (2 + layout.count),
        out_specs=(spec(),) * 8,
        scratch_shapes=[vm((rows, rows), bf16), vm((2 * FEAT, rows), bf16), vm((nodes * SK, FEAT), bf16)],
        compiler_params=params(),
        name="tree_points",
    )(where, skeleton_upper, small, *place)

    tree_light, coefs, pack = pl.pallas_call(
        functools.partial(weights_kernel, layout),
        out_shape=(
            shaped((total, LANES), bf16),
            shaped((nodes * SK, FEAT), bf16),
            shaped((SK, LANES), f32),
        ),
        in_specs=[spec()] * (4 + layout.count),
        out_specs=(spec(),) * 3,
        scratch_shapes=[vm((rows, rows), bf16), vm((LANES, rows), bf16)],
        compiler_params=params(),
        name="tree_weights",
    )(base, upper_tiles, top, slots, *light)

    packs = upper_levels(pack, skeleton_upper, my_leaf, trees, blocks, width)

    near = pl.pallas_call(
        near_kernel,
        out_shape=shaped((total, LANES), f32),
        in_specs=[spec(SMEM)] * 2 + [spec()] * 3,
        out_specs=spec(),
        scratch_shapes=[
            pltpu.SMEM((leaves,), jnp.int32),
            pltpu.SMEM((3, leaves * leaves + 1), jnp.int32),
            vm((LEAF, LEAF // 2), f32),
        ],
        compiler_params=params(),
        name="near",
    )(near_count, near_list[0], feat_a, feat_bt, tree_light)

    levels = low_levels + ups
    back = pl.pallas_call(
        functools.partial(far_kernel, layout, low_levels),
        out_shape=(arrive,) * layout.count,
        in_specs=[spec()] * 7,
        out_specs=(spec(),) * layout.count,
        scratch_shapes=[
            vm((rows, rows), bf16),
            vm((FEAT, levels * SK), bf16),
            vm((levels * SK, FEAT), bf16),
            vm((levels * SK, FEAT), bf16),
        ],
        compiler_params=params(),
        name="far",
    )(packs, slots, info, feat_a, sk, coefs, near)

    if fine:
        back = swap_all(back)
    else:
        back = back[0].reshape(width, blocks, devices, per).transpose(2, 0, 1, 3).reshape(devices, width, part)
        back = lax.all_to_all(back, ("leaf", "sub"), split_axis=0, concat_axis=0, tiled=True)
        back = [back.reshape(trees, columns, part).transpose(1, 0, 2).reshape(columns, rows)]

    return pl.pallas_call(
        functools.partial(final_kernel, blocks if fine else 0),
        out_shape=shaped((rows, columns), f32),
        in_specs=[spec(SMEM)] + [spec()] * (2 + layout.count),
        out_specs=spec(),
        scratch_shapes=[vm((rows, rows), bf16), vm((2 * LANES, rows), bf16)],
        compiler_params=params(),
        name="to_input_order",
    )(where, pos, *back, weights)


def solution(mesh):
    in_specs = (
        P(("groups", "leaf", "sub"), None),
        P(("groups", "leaf", "sub"), "rep"),
        P(("groups", "leaf", "sub")),
        P(("groups", "leaf"), None),
        P(("groups", "leaf"), None, None),
        P(("groups", "leaf", "sub"), None),
        P("groups", None),
        P(("groups", "leaf", "sub"), None),
    )
    out_specs = P(("groups", "leaf", "sub"), "rep")
    return jax.shard_map(body, mesh=mesh, in_specs=in_specs, out_specs=out_specs, check_vma=False)
```

```python
import functools
import math

import jax
import jax.numpy as jnp
from jax import lax
from jax.experimental import pallas as pl
from jax.experimental.pallas import tpu as pltpu
from jax.sharding import PartitionSpec as P

DIM = 64
LEAF = 512
SK = 128
LANES = 128
FEAT = 256

highest = lax.Precision.HIGHEST
point_scale = math.sqrt(2.0 * math.log2(math.e) / 32.0)
ridge = 0.5
PLACE_ROWS = 72
TAIL = 64
SLOT, NORM, BASE, FLAGS = 0, 1, 2, 3
f32 = jnp.float32
bf16 = jnp.bfloat16
VMEM = pltpu.MemorySpace.VMEM
SMEM = pltpu.MemorySpace.SMEM


def spec(space=VMEM):
    return pl.BlockSpec(memory_space=space)


def params():
    return pltpu.CompilerParams(vmem_limit_bytes=58 * 1024 * 1024)


def vm(shape, dtype):
    return pltpu.VMEM(shape, dtype)


def shaped(shape, dtype):
    return jax.ShapeDtypeStruct(shape, dtype)


def nt(left, right):
    return lax.dot_general(left, right, (((1,), (1,)), ((), ())), preferred_element_type=f32)


def nn(left, right):
    return jnp.dot(left, right, preferred_element_type=f32)


def column(row):
    return jnp.transpose(jnp.broadcast_to(row, (LANES, LANES)))


def iota(shape, dim):
    return lax.broadcasted_iota(jnp.int32, shape, dim)


def onehot(mask):
    return jnp.where(mask, 1.0, 0.0).astype(bf16)


def two(value):
    high = value.astype(bf16)
    return high, (value - high.astype(f32)).astype(bf16)


def three(value):
    high = value.astype(bf16).astype(f32)
    mid = (value - high).astype(bf16).astype(f32)
    return high, mid, (value - high - mid).astype(bf16).astype(f32)


def lanes_of(blocks):
    return blocks[0] if len(blocks) == 1 else jnp.concatenate(blocks, 1)


def aligned(start, size, unit):
    return pl.ds(pl.multiple_of(start, unit), size)


def exact_product(block, coefs):
    high, low = two(block)
    first = nn(high, coefs)
    return first[:, :LANES] + first[:, LANES:] + nn(low, coefs[:, :LANES])


def split_coefs(value):
    high, low = two(value)
    return jnp.concatenate([high, low], 1)


def spread(perm, here, rank):
    lane = iota((LANES, LANES), 1).astype(f32)
    for c in range(perm.shape[1] // LANES):
        perm[here, c * LANES : (c + 1) * LANES] = onehot(lane + float(c * LANES) == rank)


def sort_kernel(
    fine, where_ref, slot_ref, points_ref, weights_ref, base_ref, flag_ref, place_ref, pos_ref, light_ref, perm, vals, whole
):
    chunks, split = slot_ref.shape[0], light_ref.shape[-1]
    rows = chunks * LANES
    slots = slot_ref[...]
    slot = slots.astype(f32)
    within = slots & (rows - 1)
    high, low = (within >> 5).astype(f32), (within & 31).astype(f32)
    for r in range(chunks):
        here = slice(r * LANES, (r + 1) * LANES)
        mine = column(slot[r : r + 1])
        before = jnp.zeros((LANES, LANES), f32)
        for c in range(chunks):
            before += jnp.where(slot[c : c + 1] < mine, 1.0, 0.0)
        rank = jnp.broadcast_to(jnp.sum(before, axis=1, keepdims=True), (LANES, LANES))
        pos_ref[r : r + 1, :] = jnp.transpose(rank)[0:1]
        spread(perm, here, rank)
        vals[0:LANES, here] = jnp.transpose(weights_ref[here, :]).astype(bf16)
    scaled = points_ref[...] * point_scale
    ph, plo = two(scaled)
    nh, nm, nl = three(-0.5 * jnp.sum(scaled * scaled, axis=0, keepdims=True))
    vals[128:192, :] = ph
    vals[192:256, :] = plo
    sub = iota((16, LANES), 0)
    for c in range(chunks):
        at = slice(c * LANES, (c + 1) * LANES)
        extra = jnp.where(sub == 0, high[c : c + 1], jnp.where(sub == 1, low[c : c + 1], 0.0))
        extra = jnp.where(sub == 2, nh[:, at], jnp.where(sub == 3, nm[:, at], extra))
        vals[256:272, at] = jnp.where(sub == 4, nl[:, at], extra).astype(bf16)
    step = 256
    for s in range(rows // step):
        moved = nn(vals[...], perm[:, s * step : (s + 1) * step])
        at = slice((s * step) % split, (s * step) % split + step)
        part = (s * step) // split
        light_ref[part, :, at] = moved[0:LANES]
        whole[part, 0:TAIL, at] = moved[128:192] + moved[192:256]
        tail = iota((8, step), 0)
        slot_row = moved[256:257] * 32.0 + moved[257:258]
        norm_row = moved[258:259] + moved[259:260] + moved[260:261]
        whole[part, TAIL:, at] = jnp.where(tail == SLOT, slot_row, jnp.where(tail == NORM, norm_row, 0.0))
    if not fine:
        place_ref[...] = whole[0]
        return
    place_ref[...] = whole[where_ref[0] ^ where_ref[2]]
    place_ref[TAIL + BASE : TAIL + BASE + 1, 0:SK] = base_ref[...].astype(f32)
    place_ref[TAIL + FLAGS : TAIL + FLAGS + flag_ref.shape[0], 0 : flag_ref.shape[1]] = flag_ref[...].astype(f32)


class Layout:
    def __init__(self, blocks, trees, rows, fine):
        self.blocks, self.rows, self.fine = blocks, rows, fine
        self.count = blocks * trees if fine else 1
        self.per = rows // self.count

    def lanes(self, index):
        return aligned(index * self.per, self.per, LANES)

    def message(self, where_ref, group):
        if not self.fine:
            return 0
        leaf = where_ref[0] ^ where_ref[2] ^ (group // self.blocks)
        return leaf * self.blocks + (where_ref[1] ^ (group % self.blocks))

    def gather(self, refs, index, part):
        return lanes_of([ref[part, self.lanes(index)] for ref in refs])

    def info(self, where_ref, refs, small_ref, index):
        if not self.fine:
            return small_ref[index]
        core = where_ref[2]
        found = jnp.zeros((PLACE_ROWS - TAIL, SK), f32)
        for step in range(self.blocks):
            mine, theirs = refs[step][TAIL:, 0:SK], refs[self.blocks + step][TAIL:, 0:SK]
            here = jnp.where(core == 0, mine, theirs)
            found = jnp.where((where_ref[1] ^ step) == index, here, found)
        return found


def fill_perm(out, slot_rows):
    def rows_of(r, carry):
        tree_row = (iota((LANES, LANES), 0) + r * LANES).astype(f32)
        for c in range(out.shape[1] // LANES):
            at = slice(c * LANES, (c + 1) * LANES)
            out[aligned(r * LANES, LANES, LANES), at] = onehot(tree_row == slot_rows[:, at])
        return carry

    lax.fori_loop(0, out.shape[0] // LANES, rows_of, 0)


def round_into(out, wide, rows, columns, base=0):
    step = max(8192 // columns, 16)
    for r in range(0, rows, step):
        out[pl.ds(base + r, step), :] = wide[r : r + step, 0:columns].astype(bf16)


def exp_into(out, wide):
    rows, columns = wide.shape
    for r in range(0, rows, 32):
        out[r : r + 32, :] = jnp.exp2(wide[r : r + 32, :]).astype(bf16)


def points_kernel(layout, trees, where_ref, upper_ref, small_ref, *refs):
    place_refs, refs = refs[: layout.count], refs[layout.count :]
    a_ref, bt_ref, skt_ref, base_ref, upper_tiles_ref, top_ref, slot_ref, info_ref, perm, feats, sk_a, wide, tall = refs
    blocks, rows = layout.blocks, layout.rows
    lane = iota((SK, LANES), 1)

    def block(index, carry):
        tail = layout.gather(place_refs, index, slice(TAIL, PLACE_ROWS))
        slots = tail[SLOT : SLOT + 1]
        slot_ref[pl.ds(index, 1), :] = slots
        info = layout.info(where_ref, place_refs, small_ref, index)
        info_ref[index] = info
        points = layout.gather(place_refs, index, slice(0, TAIL))
        high, low = two(points)
        nh, nm, nl = three(tail[NORM : NORM + 1])
        sub = iota((64, rows), 0)
        extra_a = jnp.where(sub == 0, nh, jnp.where(sub == 1, nm, jnp.where(sub == 2, nl, 0.0)))
        extra_a = jnp.where((sub >= 3) & (sub < 6), 1.0, extra_a)
        extra_b = jnp.where(sub == 3, nh, jnp.where(sub == 4, nm, jnp.where(sub == 5, nl, 0.0)))
        extra_b = jnp.where(sub < 3, 1.0, extra_b)
        feats[0:64, :] = high
        feats[64:128, :] = low
        feats[128:192, :] = high
        feats[192:256, :] = extra_a.astype(bf16)
        feats[256:320, :] = high
        feats[320:384, :] = high
        feats[384:448, :] = low
        feats[448:512, :] = extra_b.astype(bf16)
        fill_perm(perm, slots)
        mine = aligned(index * rows, rows, rows)
        tall[...] = nt(perm[...], feats[0:FEAT, :])
        wide[...] = nt(feats[FEAT:, :], perm[...])
        for r in range(0, rows, 32):
            a_ref[aligned(index * rows + r, 32, 32), :] = tall[r : r + 32, :].astype(bf16)
        for r in range(0, FEAT, 16):
            bt_ref[r : r + 16, mine] = wide[r : r + 16, :].astype(bf16)
        picks = column(info[BASE : BASE + 1]).astype(jnp.int32)
        chosen = jnp.concatenate([onehot(lane + c * LANES == picks) for c in range(rows // LANES)], 1)
        node = aligned(index * SK, SK, SK)
        own_a = nn(chosen, a_ref[mine, :]).astype(bf16)
        sk_a[node, :] = own_a
        skt_ref[:, node] = nt(bt_ref[:, mine], chosen).astype(bf16)
        wide[0:SK, :] = nn(own_a, bt_ref[:, mine])
        for r in range(0, SK, 16):
            base_ref[index, r : r + 16, :] = jnp.exp2(wide[r : r + 16, :]).astype(bf16)
        return carry

    lax.fori_loop(0, blocks, block, 0)
    start, count, offset, total = 0, blocks, 0, blocks * trees
    while count > 1:
        nodes = count // 2
        for j in range(nodes):
            pair = slice((start + 2 * j) * SK, (start + 2 * j + 2) * SK)
            row = offset + where_ref[0] * nodes + j
            picks = column(upper_ref[pl.ds(row, 1), :].astype(f32)).astype(jnp.int32)
            chosen = jnp.concatenate([onehot(lane == picks), onehot(lane + LANES == picks)], 1)
            here = start + count + j
            new = slice(here * SK, (here + 1) * SK)
            own_a = nn(chosen, sk_a[pair, :]).astype(bf16)
            sk_a[new, :] = own_a
            skt_ref[:, new] = nt(skt_ref[:, pair], chosen).astype(bf16)
            upper_tiles_ref[here - blocks] = jnp.exp2(nn(own_a, skt_ref[:, pair]))
        total = total // 2
        offset = offset + total
        start, count = start + count, nodes
    own_a = sk_a[start * SK : (start + 1) * SK, :].astype(f32)
    exact = own_a[:, :128] + pltpu.roll(own_a[:, :128], 64, 1)
    top_ref[...] = jnp.where(lane < 64, exact, own_a[:, 128:])


def weights_kernel(
    layout, where_ref, base_ref, upper_tiles_ref, top_ref, slot_ref, light_ref, w_ref, coef_ref, pack_ref, perm, feats, tall
):
    blocks, rows = layout.blocks, layout.rows
    width = light_ref.shape[1]
    feats[...] = jnp.zeros_like(feats)

    def block(index, carry):
        fill_perm(perm, slot_ref[pl.ds(index, 1), :])
        light = [light_ref[layout.message(where_ref, g), :, layout.lanes(index)] for g in range(layout.count)]
        feats[LANES - width :, :] = lanes_of(light).astype(bf16)
        mine = aligned(index * rows, rows, rows)
        tall[...] = nt(perm[...], feats[...])
        for r in range(0, rows, 64):
            w_ref[aligned(index * rows + r, 64, 64), :] = tall[r : r + 64, :].astype(bf16)
        coef = nn(base_ref[index], w_ref[mine, :])
        coef_ref[aligned(index * SK, SK, SK), :] = split_coefs(coef)
        pack_ref[...] = coef
        return carry

    lax.fori_loop(0, blocks, block, 0)
    start, count = 0, blocks
    while count > 1:
        for j in range(count // 2):
            pair = slice((start + 2 * j) * SK, (start + 2 * j + 2) * SK)
            here = start + count + j
            coef = exact_product(upper_tiles_ref[here - blocks], coef_ref[pair, :])
            coef_ref[here * SK : (here + 1) * SK, :] = split_coefs(coef)
            pack_ref[...] = coef
        start, count = start + count, count // 2
    pack_ref[...] = top_ref[...] + pack_ref[...]


def near_kernel(count_ref, list_ref, a_ref, bt_ref, w_ref, acc, times, tiles, ahead, second, tile_a, tile_b):
    every = count_ref.shape[1]

    def tally(leaf, filled):
        for other in range(every):
            times[other] = (leaf == other).astype(jnp.int32)

        def add(slot, carry):
            at = list_ref[leaf, slot]
            times[at] = times[at] + 1
            return carry

        lax.fori_loop(0, count_ref[0, leaf], add, 0)
        for other in range(every):
            tiles[0, filled] = leaf
            tiles[1, filled] = other
            tiles[2, filled] = times[other]
            filled = filled + (times[other] > 0).astype(jnp.int32)
        return filled

    filled = lax.fori_loop(0, every, tally, jnp.int32(0))
    tiles[0, filled] = 0
    tiles[1, filled] = 0
    half = LEAF // 2
    acc[...] = jnp.zeros_like(acc)

    def exponents(tile, part):
        target = aligned(tiles[0, tile] * LEAF, LEAF, LEAF)
        source = aligned(tiles[1, tile] * LEAF + part * half, half, half)
        return nn(a_ref[target, :], bt_ref[:, source])

    def product(tile, part, block):
        source = aligned(tiles[1, tile] * LEAF + part * half, half, half)
        return nn(block, w_ref[source, :])

    ahead[...] = exponents(0, 0)

    def step(tile, carry):
        here = aligned(tiles[0, tile] * LEAF, LEAF, LEAF)
        many = tiles[2, tile].astype(f32)
        second[...] = exponents(tile, 1)
        exp_into(tile_a, ahead)
        first = product(tile, 0, tile_a[...])
        ahead[...] = exponents(tile + 1, 0)
        exp_into(tile_b, second)
        acc[here, :] += many * (first + product(tile, 1, tile_b[...]))
        return carry

    lax.fori_loop(0, filled, step, 0)


def far_kernel(layout, low_levels, pack_ref, slot_ref, info_ref, a_ref, skt_ref, coef_ref, near_ref, *refs):
    out_refs, (perm, tops, coefs, scaled, wide, tile, turned) = refs[: layout.count], refs[layout.count :]
    blocks, rows = layout.blocks, layout.rows
    ups, width = pack_ref.shape[0], out_refs[0].shape[0]
    levels = low_levels + ups
    lane = iota((SK, LANES), 1)
    for up in range(ups):
        pack = pack_ref[up]
        high, low = two(jnp.where(lane < 64, pack, 0.0))
        high, low = high.astype(f32), low.astype(f32)
        is_norm = (lane >= 64) & (lane < 67)
        norms = pltpu.roll(jnp.where(is_norm, pack, 0.0), 3, 1)
        at = slice((low_levels + up) * SK, (low_levels + up + 1) * SK)
        tops[0:128, at] = jnp.transpose(high + pltpu.roll(high, 64, 1)).astype(bf16)
        tops[128:256, at] = jnp.transpose(jnp.where(is_norm, 1.0, low + norms)).astype(bf16)
        coefs[at, :] = split_coefs(jnp.where(lane >= LANES - width, pack, 0.0))

    def block(index, carry):
        node, start, count = index, 0, blocks
        for level in range(low_levels):
            at = slice(level * SK, (level + 1) * SK)
            other = aligned((start + (node ^ 1)) * SK, SK, SK)
            tops[:, at] = skt_ref[:, other]
            coefs[at, :] = coef_ref[other, :]
            node, start, count = node // 2, start + count, count // 2
        fill_perm(perm, slot_ref[pl.ds(index, 1), :])
        info = info_ref[index]
        for leaf in range(rows // LEAF):
            flags = info[FLAGS + leaf : FLAGS + leaf + 1]
            for level in range(levels):
                at = slice(level * SK, (level + 1) * SK)
                flag = jnp.sum(jnp.where(lane[0:1] == level, flags, 0.0), axis=1, keepdims=True)
                scaled[at, :] = (coefs[at, :].astype(f32) * flag).astype(bf16)
            here = aligned(index * rows + leaf * LEAF, LEAF, LEAF)
            wide[...] = nn(a_ref[here, :], tops[...])
            exp_into(tile, wide)
            wide[:, 0 : 2 * LANES] = nn(tile[...], scaled[...])
            for r in range(0, LEAF, LANES):
                near = near_ref[aligned(index * rows + leaf * LEAF + r, LANES, LANES), :]
                near = near + wide[r : r + LANES, 0:LANES] + wide[r : r + LANES, LANES : 2 * LANES]
                turned[:, leaf * LEAF + r : leaf * LEAF + r + LANES] = jnp.transpose(near)[LANES - width :]
        high, low = two(turned[...])
        moved = nn(jnp.concatenate([high, low], 0), perm[...])
        moved = moved[:width] + moved[width:]
        for g, out_ref in enumerate(out_refs):
            out_ref[:, layout.lanes(index)] = moved[:, g * layout.per : (g + 1) * layout.per]
        return carry

    lax.fori_loop(0, blocks, block, 0)


def final_kernel(blocks, where_ref, pos_ref, *refs):
    back_refs, (weights_ref, out_ref, perm, vals) = refs[:-4], refs[-4:]
    chunks = pos_ref.shape[0]
    rows = chunks * LANES
    width, split = back_refs[0].shape
    for r in range(chunks):
        spread(perm, slice(r * LANES, (r + 1) * LANES), column(pos_ref[r : r + 1, :]))
    for g, back_ref in enumerate(back_refs):
        high, low = two(back_ref[...])
        columns, at = 0, slice(0, rows)
        if blocks:
            columns = (where_ref[1] ^ (g % blocks)) * width
            at = aligned((where_ref[0] ^ where_ref[2] ^ (g // blocks)) * split, split, split)
        vals[aligned(columns, width, width), at] = high
        vals[aligned(columns + LANES, width, width), at] = low
    step = 256
    for s in range(rows // step):
        here = slice(s * step, (s + 1) * step)
        moved = nt(perm[here, :], vals[...])
        out_ref[here, :] = ridge * weights_ref[here, :] + moved[:, :LANES] + moved[:, LANES:]


def upper_levels(pack, skeleton_upper, my_leaf, trees, blocks, width):
    devices = trees * blocks
    level = blocks.bit_length() - 1
    offset = sum(devices >> step for step in range(1, level + 1))
    lanes = jnp.arange(LANES)[None]
    is_point, is_norm = lanes < DIM, (lanes >= DIM) & (lanes < DIM + 3)
    is_coef = lanes >= LANES - width
    packs, own, stride = [], pack, 1
    while stride < trees:
        other = lax.ppermute(own, "leaf", [(i, i ^ stride) for i in range(trees)])
        packs.append(other)
        stride *= 2
        if stride < trees:
            second = (my_leaf // (stride // 2)) % 2 == 1
            pair = jnp.where(second, jnp.concatenate([other, own], 0), jnp.concatenate([own, other], 0))
            chosen = pair[skeleton_upper[offset + my_leaf // stride]]
            level += 1
            offset += devices >> level
            norms = jnp.sum(jnp.where(is_norm, pair, 0.0), axis=1)
            chosen_norms = jnp.sum(jnp.where(is_norm, chosen, 0.0), axis=1)
            inner = jnp.dot(
                jnp.where(is_point, chosen, 0.0), jnp.where(is_point, pair, 0.0).T, precision=highest
            )
            tile = jnp.exp2(inner + norms[None] + chosen_norms[:, None])
            own = jnp.where(is_coef, jnp.dot(tile, pair, precision=highest), chosen)
    return jnp.stack(packs)


def body(points, weights, tree_slot, near_count, near_list, skeleton_base, skeleton_upper, far_use):
    blocks, trees, reps = lax.axis_size("sub"), lax.axis_size("leaf"), lax.axis_size("rep")
    devices = blocks * trees
    rows, columns = weights.shape
    low_levels = blocks.bit_length() - 1
    ups = trees.bit_length() - 1
    width = columns // blocks
    part = rows // trees
    per = part // blocks
    total = blocks * rows
    leaves = total // LEAF
    my_leaf = lax.axis_index("leaf")
    fine = trees == 2 and reps == 2 and per % LANES == 0
    layout = Layout(blocks, trees, rows, fine)
    split = part if fine else rows
    where = jnp.stack([my_leaf, lax.axis_index("sub"), lax.axis_index("rep")]).astype(jnp.int32)
    arrive = shaped((width, part), f32) if fine else shaped((width, total), f32)

    place, pos, light = pl.pallas_call(
        functools.partial(sort_kernel, fine),
        out_shape=(
            shaped((PLACE_ROWS, split), f32),
            shaped((rows // LANES, LANES), f32),
            shaped((rows // split, columns, split), f32),
        ),
        in_specs=[spec(SMEM)] + [spec()] * 5,
        out_specs=(spec(),) * 3,
        scratch_shapes=[
            vm((rows, rows), bf16),
            vm((272, rows), bf16),
            vm((rows // split, PLACE_ROWS, split), f32),
        ],
        compiler_params=params(),
        name="sort_rows",
    )(where, tree_slot.reshape(rows // LANES, LANES), points.T, weights, skeleton_base, far_use)

    axes = ("leaf", "sub", "rep")

    def swap(value, step, other=0):
        pairs = []
        for leaf in range(trees):
            for sub in range(blocks):
                for core in range(reps):
                    to = ((leaf ^ core ^ other) * blocks + (sub ^ step)) * reps + core
                    pairs.append(((leaf * blocks + sub) * reps + core, to))
        return lax.ppermute(value, axes, pairs)

    def swap_all(values):
        done = {}
        for g in sorted(range(len(values)), key=lambda g: -(g % blocks)):
            done[g] = swap(values[g], g % blocks, g // blocks)
        return [done[g] for g in range(len(values))]

    if fine:
        place = {0: swap(place, 0)}
        stride = blocks // 2
        while stride:
            for step in sorted(place):
                place[step | stride] = lax.ppermute(place[step], "sub", [(i, i ^ stride) for i in range(blocks)])
            stride //= 2
        place = [place[step] for step in range(blocks)]
        place, light = lax.optimization_barrier((place, light))
        place = place + [lax.ppermute(one, "rep", [(0, 1), (1, 0)]) for one in place]
        light = light.reshape(devices, width, part)
        light = lax.all_to_all(light, ("leaf", "sub"), split_axis=0, concat_axis=0, tiled=True)
        small = jnp.zeros((1, 8, SK), f32)
    else:
        info = jnp.pad(far_use.astype(f32), ((FLAGS, 5 - far_use.shape[0]), (0, SK - far_use.shape[1])))
        small = lax.all_gather(info.at[BASE].set(skeleton_base[0].astype(f32)), "sub", axis=0, tiled=False)
        place = place.reshape(PLACE_ROWS, trees, part).transpose(1, 0, 2)
        place = lax.all_to_all(place, "leaf", split_axis=0, concat_axis=0, tiled=True)
        place = lax.all_gather(place, "sub", axis=0, tiled=False)
        place = place.transpose(1, 0, 2, 3).reshape(devices, PLACE_ROWS, blocks, per)
        place = [place.transpose(1, 2, 0, 3).reshape(PLACE_ROWS, total)]
        light = light.reshape(columns, trees, part).transpose(1, 0, 2).reshape(devices, width, part)
        light = lax.all_to_all(light, ("leaf", "sub"), split_axis=0, concat_axis=0, tiled=True)
        light = light.reshape(devices, width, blocks, per)
        light = light.transpose(1, 2, 0, 3).reshape(1, width, total)

    nodes = 2 * blocks - 1
    feat_a, feat_bt, sk, base, upper_tiles, top, slots, info = pl.pallas_call(
        functools.partial(points_kernel, layout, trees),
        out_shape=(
            shaped((total, FEAT), bf16),
            shaped((FEAT, total), bf16),
            shaped((FEAT, nodes * SK), bf16),
            shaped((blocks, SK, rows), bf16),
            shaped((blocks - 1, SK, 2 * SK), f32),
            shaped((SK, LANES), f32),
            shaped((blocks, rows), f32),
            shaped((blocks, 8, SK), f32),
        ),
        in_specs=[spec(SMEM)] + [spec()] * (2 + layout.count),
        out_specs=(spec(),) * 8,
        scratch_shapes=[
            vm((rows, rows), bf16),
            vm((2 * FEAT, rows), bf16),
            vm((nodes * SK, FEAT), bf16),
            vm((FEAT, rows), f32),
            vm((rows, FEAT), f32),
        ],
        compiler_params=params(),
        name="tree_points",
    )(where, skeleton_upper, small, *place)

    tree_light, coefs, pack = pl.pallas_call(
        functools.partial(weights_kernel, layout),
        out_shape=(
            shaped((total, LANES), bf16),
            shaped((nodes * SK, FEAT), bf16),
            shaped((SK, LANES), f32),
        ),
        in_specs=[spec(SMEM)] + [spec()] * 5,
        out_specs=(spec(),) * 3,
        scratch_shapes=[vm((rows, rows), bf16), vm((LANES, rows), bf16), vm((rows, LANES), f32)],
        compiler_params=params(),
        name="tree_weights",
    )(where, base, upper_tiles, top, slots, light)

    packs = upper_levels(pack, skeleton_upper, my_leaf, trees, blocks, width)

    near = pl.pallas_call(
        near_kernel,
        out_shape=shaped((total, LANES), f32),
        in_specs=[spec(SMEM)] * 2 + [spec()] * 3,
        out_specs=spec(),
        scratch_shapes=[
            pltpu.SMEM((leaves,), jnp.int32),
            pltpu.SMEM((3, leaves * leaves + 1), jnp.int32),
            vm((LEAF, LEAF // 2), f32),
            vm((LEAF, LEAF // 2), f32),
            vm((LEAF, LEAF // 2), bf16),
            vm((LEAF, LEAF // 2), bf16),
        ],
        compiler_params=params(),
        name="near",
    )(near_count, near_list[0], feat_a, feat_bt, tree_light)

    levels = low_levels + ups
    back = pl.pallas_call(
        functools.partial(far_kernel, layout, low_levels),
        out_shape=(arrive,) * layout.count,
        in_specs=[spec()] * 7,
        out_specs=(spec(),) * layout.count,
        scratch_shapes=[
            vm((rows, rows), bf16),
            vm((FEAT, levels * SK), bf16),
            vm((levels * SK, FEAT), bf16),
            vm((levels * SK, FEAT), bf16),
            vm((LEAF, levels * SK), f32),
            vm((LEAF, levels * SK), bf16),
            vm((width, rows), f32),
        ],
        compiler_params=params(),
        name="far",
    )(packs, slots, info, feat_a, sk, coefs, near)

    if fine:
        back = swap_all(back)
    else:
        back = back[0].reshape(width, blocks, devices, per).transpose(2, 0, 1, 3).reshape(devices, width, part)
        back = lax.all_to_all(back, ("leaf", "sub"), split_axis=0, concat_axis=0, tiled=True)
        back = [back.reshape(trees, columns, part).transpose(1, 0, 2).reshape(columns, rows)]

    return pl.pallas_call(
        functools.partial(final_kernel, blocks if fine else 0),
        out_shape=shaped((rows, columns), f32),
        in_specs=[spec(SMEM)] + [spec()] * (2 + layout.count),
        out_specs=spec(),
        scratch_shapes=[vm((rows, rows), bf16), vm((2 * LANES, rows), bf16)],
        compiler_params=params(),
        name="to_input_order",
    )(where, pos, *back, weights)


def solution(mesh):
    in_specs = (
        P(("groups", "leaf", "sub"), None),
        P(("groups", "leaf", "sub"), "rep"),
        P(("groups", "leaf", "sub")),
        P(("groups", "leaf"), None),
        P(("groups", "leaf"), None, None),
        P(("groups", "leaf", "sub"), None),
        P("groups", None),
        P(("groups", "leaf", "sub"), None),
    )
    out_specs = P(("groups", "leaf", "sub"), "rep")
    return jax.shard_map(body, mesh=mesh, in_specs=in_specs, out_specs=out_specs, check_vma=False)
```

```python
import functools
import math

import jax
import jax.numpy as jnp
from jax import lax
from jax.experimental import pallas as pl
from jax.experimental.pallas import tpu as pltpu
from jax.sharding import PartitionSpec as P

DIM = 64
LEAF = 512
SK = 128
LANES = 128
FEAT = 256
LOW = 256
COORD = 144

highest = lax.Precision.HIGHEST
point_scale = math.sqrt(2.0 * math.log2(math.e) / 32.0)
ridge = 0.5
PLACE_ROWS = 72
TAIL = 64
SLOT, NORM, BASE, FLAGS = 0, 1, 2, 3
f32 = jnp.float32
bf16 = jnp.bfloat16
VMEM = pltpu.MemorySpace.VMEM
SMEM = pltpu.MemorySpace.SMEM


def spec(space=VMEM):
    return pl.BlockSpec(memory_space=space)


def params():
    return pltpu.CompilerParams(vmem_limit_bytes=58 * 1024 * 1024)


def vm(shape, dtype):
    return pltpu.VMEM(shape, dtype)


def shaped(shape, dtype):
    return jax.ShapeDtypeStruct(shape, dtype)


def nt(left, right):
    return lax.dot_general(left, right, (((1,), (1,)), ((), ())), preferred_element_type=f32)


def nn(left, right):
    return jnp.dot(left, right, preferred_element_type=f32)


def column(row):
    return jnp.transpose(jnp.broadcast_to(row, (LANES, LANES)))


def iota(shape, dim):
    return lax.broadcasted_iota(jnp.int32, shape, dim)


def onehot(mask):
    return jnp.where(mask, 1.0, 0.0).astype(bf16)


def two(value):
    high = value.astype(bf16)
    return high, (value - high.astype(f32)).astype(bf16)


def three(value):
    high = value.astype(bf16).astype(f32)
    mid = (value - high).astype(bf16).astype(f32)
    return high, mid, (value - high - mid).astype(bf16).astype(f32)


def lanes_of(blocks):
    return blocks[0] if len(blocks) == 1 else jnp.concatenate(blocks, 1)


def aligned(start, size, unit):
    return pl.ds(pl.multiple_of(start, unit), size)


def stack_two(value):
    high, low = two(value)
    return jnp.concatenate([high, low], 0)


def spread(perm, here, rank):
    lane = iota((LANES, LANES), 1).astype(f32)
    for c in range(perm.shape[1] // LANES):
        perm[here, c * LANES : (c + 1) * LANES] = onehot(lane + float(c * LANES) == rank)


def sort_kernel(
    fine, where_ref, slot_ref, points_ref, weights_ref, base_ref, flag_ref, place_ref, pos_ref, light_ref, perm, vals, whole
):
    chunks, split = slot_ref.shape[0], light_ref.shape[-1]
    rows = chunks * LANES
    slots = slot_ref[...]
    slot = slots.astype(f32)
    within = slots & (rows - 1)
    high, low = (within >> 5).astype(f32), (within & 31).astype(f32)
    for r in range(chunks):
        here = slice(r * LANES, (r + 1) * LANES)
        mine = column(slot[r : r + 1])
        before = jnp.zeros((LANES, LANES), f32)
        for c in range(chunks):
            before += jnp.where(slot[c : c + 1] < mine, 1.0, 0.0)
        rank = jnp.broadcast_to(jnp.sum(before, axis=1, keepdims=True), (LANES, LANES))
        pos_ref[r : r + 1, :] = jnp.transpose(rank)[0:1]
        spread(perm, here, rank)
        vals[0:LANES, here] = jnp.transpose(weights_ref[here, :]).astype(bf16)
    scaled = points_ref[...] * point_scale
    ph, plo = two(scaled)
    nh, nm, nl = three(-0.5 * jnp.sum(scaled * scaled, axis=0, keepdims=True))
    vals[128:192, :] = ph
    vals[192:256, :] = plo
    sub = iota((16, LANES), 0)
    for c in range(chunks):
        at = slice(c * LANES, (c + 1) * LANES)
        extra = jnp.where(sub == 0, high[c : c + 1], jnp.where(sub == 1, low[c : c + 1], 0.0))
        extra = jnp.where(sub == 2, nh[:, at], jnp.where(sub == 3, nm[:, at], extra))
        vals[256:272, at] = jnp.where(sub == 4, nl[:, at], extra).astype(bf16)
    step = 256
    for s in range(rows // step):
        moved = nn(vals[...], perm[:, s * step : (s + 1) * step])
        at = slice((s * step) % split, (s * step) % split + step)
        part = (s * step) // split
        light_ref[part, :, at] = moved[0:LANES]
        whole[part, 0:TAIL, at] = moved[128:192] + moved[192:256]
        tail = iota((8, step), 0)
        slot_row = moved[256:257] * 32.0 + moved[257:258]
        norm_row = moved[258:259] + moved[259:260] + moved[260:261]
        whole[part, TAIL:, at] = jnp.where(tail == SLOT, slot_row, jnp.where(tail == NORM, norm_row, 0.0))
    if not fine:
        place_ref[...] = whole[0]
        return
    place_ref[...] = whole[where_ref[0] ^ where_ref[2]]
    place_ref[TAIL + BASE : TAIL + BASE + 1, 0:SK] = base_ref[...].astype(f32)
    place_ref[TAIL + FLAGS : TAIL + FLAGS + flag_ref.shape[0], 0 : flag_ref.shape[1]] = flag_ref[...].astype(f32)


class Layout:
    def __init__(self, blocks, trees, rows, fine):
        self.blocks, self.rows, self.fine = blocks, rows, fine
        self.count = blocks * trees if fine else 1
        self.per = rows // self.count

    def lanes(self, index):
        return aligned(index * self.per, self.per, LANES)

    def message(self, where_ref, group):
        if not self.fine:
            return 0
        leaf = where_ref[0] ^ where_ref[2] ^ (group // self.blocks)
        return leaf * self.blocks + (where_ref[1] ^ (group % self.blocks))

    def gather(self, refs, index, part):
        return lanes_of([ref[part, self.lanes(index)] for ref in refs])

    def info(self, where_ref, refs, small_ref, index):
        if not self.fine:
            return small_ref[index]
        core = where_ref[2]
        found = jnp.zeros((PLACE_ROWS - TAIL, SK), f32)
        for step in range(self.blocks):
            mine, theirs = refs[step][TAIL:, 0:SK], refs[self.blocks + step][TAIL:, 0:SK]
            here = jnp.where(core == 0, mine, theirs)
            found = jnp.where((where_ref[1] ^ step) == index, here, found)
        return found


def low_by_column(out, low):
    for c in range(out.shape[0] // LANES):
        at = slice(c * LANES, (c + 1) * LANES)
        spread(out, at, column(low[:, at]))


def parts_of(slots):
    slots = slots.astype(jnp.int32)
    return slots & (LOW - 1), slots // LOW


def feature_columns(out, at, tree):
    out[0:64, at] = tree[0:64].astype(bf16)
    out[64:128, at] = tree[0:64].astype(bf16)
    out[128:192, at] = tree[64:128].astype(bf16)
    out[192:256, at] = jnp.concatenate([tree[128:136], jnp.zeros((56, tree.shape[1]), f32)], 0).astype(bf16)


def feature_rows(high, low, extra):
    first = jnp.transpose(jnp.concatenate([high, low], 0))
    second = jnp.transpose(jnp.concatenate([high, extra, jnp.zeros((56, high.shape[1]), f32)], 0))
    return first.astype(bf16), second.astype(bf16)


def points_kernel(layout, trees, where_ref, upper_ref, small_ref, *refs):
    place_refs, refs = refs[: layout.count], refs[layout.count :]
    a_ref, bt_ref, sk_ref, base_ref, upper_tiles_ref, top_ref, slot_ref, info_ref, masked, low_hot, tree, sk_t, sk_bt = refs
    blocks, rows = layout.blocks, layout.rows

    def keep(node, found):
        at = aligned(node * SK, SK, SK)
        sk_t[:, at] = found.astype(bf16)
        sk_ref[at, 0:128], sk_ref[at, 128:256] = feature_rows(found[0:64], found[64:128], found[136:144])
        feature_columns(sk_bt, slice(0, SK), found)

    def block(index, carry):
        tail = layout.gather(place_refs, index, slice(TAIL, PLACE_ROWS))
        slots = tail[SLOT : SLOT + 1]
        slot_ref[pl.ds(index, 1), :] = slots
        info = layout.info(where_ref, place_refs, small_ref, index)
        info_ref[index] = info
        points = layout.gather(place_refs, index, slice(0, TAIL))
        high, low = two(points)
        nh, nm, nl = three(tail[NORM : NORM + 1])
        sub = iota((16, rows), 0)
        norms = jnp.where((sub == 3) | (sub == 8), nh, jnp.where((sub == 4) | (sub == 9), nm, nl))
        is_norm = ((sub >= 3) & (sub < 6)) | ((sub >= 8) & (sub < 11))
        is_one = (sub < 3) | ((sub >= 11) & (sub < 14))
        extra = jnp.where(is_norm, norms, jnp.where(is_one, 1.0, 0.0))
        low_part, high_part = parts_of(slots)
        low_by_column(low_hot, low_part.astype(f32))
        for h in range(rows // LOW):
            here = high_part == h
            masked[h * COORD : h * COORD + 64, :] = jnp.where(here, high.astype(f32), 0.0).astype(bf16)
            masked[h * COORD + 64 : h * COORD + 128, :] = jnp.where(here, low.astype(f32), 0.0).astype(bf16)
            masked[h * COORD + 128 : (h + 1) * COORD, :] = jnp.where(here, extra, 0.0).astype(bf16)
        placed = nn(masked[...], low_hot[...])
        for h in range(rows // LOW):
            part = placed[h * COORD : (h + 1) * COORD]
            tree[:, h * LOW : (h + 1) * LOW] = part.astype(bf16)
            at = aligned(index * rows + h * LOW, LOW, LOW)
            feature_columns(bt_ref, at, part)
            a_ref[at, 0:128], a_ref[at, 128:256] = feature_rows(part[0:64], part[64:128], part[136:144])
        picked = onehot(iota((rows, SK), 0) == info[BASE : BASE + 1].astype(jnp.int32))
        keep(index, nn(tree[...], picked))
        mine = aligned(index * rows, rows, rows)
        base_ref[index] = jnp.exp2(nn(a_ref[mine, :], sk_bt[...])).astype(bf16)
        return carry

    lax.fori_loop(0, blocks, block, 0)
    start, count, offset, total = 0, blocks, 0, blocks * trees
    while count > 1:
        nodes = count // 2
        for j in range(nodes):
            pair = slice((start + 2 * j) * SK, (start + 2 * j + 2) * SK)
            row = offset + where_ref[0] * nodes + j
            picked = onehot(iota((2 * SK, SK), 0) == upper_ref[pl.ds(row, 1), :])
            here = start + count + j
            keep(here, nn(sk_t[:, pair], picked))
            upper_tiles_ref[here - blocks] = jnp.exp2(nn(sk_ref[pair, :], sk_bt[...]))
        total = total // 2
        offset = offset + total
        start, count = start + count, nodes
    found = sk_t[:, start * SK : (start + 1) * SK].astype(f32)
    top_ref[0:64, :] = found[0:64] + found[64:128]
    top_ref[64:72, :] = found[128:136]
    top_ref[72:128, :] = jnp.zeros((56, SK), f32)


def weights_kernel(
    layout, where_ref, base_ref, upper_tiles_ref, top_ref, slot_ref, light_ref, w_ref, coef_ref, pack_ref, masked, low_hot
):
    blocks, rows = layout.blocks, layout.rows
    width = light_ref.shape[1]
    pack_ref[...] = top_ref[...]

    def keep(node, coef):
        coef_ref[:, aligned(node * SK, SK, SK)] = stack_two(coef)
        pack_ref[LANES - width :, :] = coef

    def block(index, carry):
        low_part, high_part = parts_of(slot_ref[pl.ds(index, 1), :])
        low_by_column(low_hot, low_part.astype(f32))
        light = [light_ref[layout.message(where_ref, g), :, layout.lanes(index)] for g in range(layout.count)]
        light = lanes_of(light)
        for h in range(rows // LOW):
            masked[h * width : (h + 1) * width, :] = jnp.where(high_part == h, light, 0.0).astype(bf16)
        placed = nn(masked[...], low_hot[...])
        parts = [placed[h * width : (h + 1) * width] for h in range(rows // LOW)]
        own = jnp.concatenate(parts, 1).astype(bf16)
        w_ref[:, aligned(index * rows, rows, rows)] = own
        keep(index, nn(own, base_ref[index]))
        return carry

    lax.fori_loop(0, blocks, block, 0)
    start, count = 0, blocks
    while count > 1:
        for j in range(count // 2):
            pair = slice((start + 2 * j) * SK, (start + 2 * j + 2) * SK)
            here = start + count + j
            high, low = two(upper_tiles_ref[here - blocks])
            coef = nn(coef_ref[:, pair], high)
            keep(here, coef[:width] + coef[width:] + nn(coef_ref[0:width, pair], low))
        start, count = start + count, count // 2


def near_kernel(count_ref, list_ref, a_ref, bt_ref, w_ref, acc, times, tiles, ahead):
    every = count_ref.shape[1]

    def tally(leaf, filled):
        for other in range(every):
            times[other] = (leaf == other).astype(jnp.int32)

        def add(slot, carry):
            at = list_ref[leaf, slot]
            times[at] = times[at] + 1
            return carry

        lax.fori_loop(0, count_ref[0, leaf], add, 0)
        for other in range(every):
            tiles[0, filled] = leaf
            tiles[1, filled] = other
            tiles[2, filled] = times[other]
            filled = filled + (times[other] > 0).astype(jnp.int32)
        return filled

    filled = lax.fori_loop(0, every, tally, jnp.int32(0))
    tiles[0, filled] = 0
    tiles[1, filled] = 0
    half = LEAF // 2
    acc[...] = jnp.zeros_like(acc)

    def target(tile, part):
        return aligned(tiles[0, tile] * LEAF + part * half, half, half)

    def exponents(tile, part):
        source = aligned(tiles[1, tile] * LEAF, LEAF, LEAF)
        return nn(a_ref[source, :], bt_ref[:, target(tile, part)])

    def add(tile, part, block):
        source = aligned(tiles[1, tile] * LEAF, LEAF, LEAF)
        acc[:, target(tile, part)] += tiles[2, tile].astype(f32) * nn(w_ref[:, source], block)

    ahead[...] = exponents(0, 0)

    def step(tile, carry):
        block = jnp.exp2(ahead[...]).astype(bf16)
        second = exponents(tile, 1)
        add(tile, 0, block)
        ahead[...] = exponents(tile + 1, 0)
        add(tile, 1, jnp.exp2(second).astype(bf16))
        return carry

    lax.fori_loop(0, filled, step, 0)


def far_kernel(layout, low_levels, pack_ref, slot_ref, info_ref, bt_ref, sk_ref, coef_ref, near_ref, *refs):
    out_refs, (tops, coefs, low_hot) = refs[: layout.count], refs[layout.count :]
    blocks, rows = layout.blocks, layout.rows
    ups, width = pack_ref.shape[0], out_refs[0].shape[0]
    levels = low_levels + ups
    lane = iota((1, SK), 1)
    for up in range(ups):
        pack = pack_ref[up]
        high, low = two(pack[0:64])
        sub = iota((8, SK), 0)
        extra = jnp.where(sub == 0, pack[67:68], jnp.where(sub == 1, pack[68:69], pack[69:70]))
        extra = jnp.where(sub < 3, extra, jnp.where(sub < 6, 1.0, 0.0))
        at = slice((low_levels + up) * SK, (low_levels + up + 1) * SK)
        tops[at, 0:128], tops[at, 128:256] = feature_rows(high.astype(f32), low.astype(f32), extra)
        coefs[:, at] = stack_two(pack[LANES - width :])

    def block(index, carry):
        node, start, count = index, 0, blocks
        for level in range(low_levels):
            at = slice(level * SK, (level + 1) * SK)
            other = aligned((start + (node ^ 1)) * SK, SK, SK)
            tops[at, :] = sk_ref[other, :]
            coefs[:, at] = coef_ref[:, other]
            node, start, count = node // 2, start + count, count // 2
        low_part, high_part = parts_of(slot_ref[pl.ds(index, 1), :])
        for c in range(rows // LANES):
            at = slice(c * LANES, (c + 1) * LANES)
            low_hot[:, at] = onehot(iota((LOW, LANES), 0) == low_part[:, at])
        info = info_ref[index]
        totals = []
        for leaf in range(rows // LEAF):
            flags = info[FLAGS + leaf : FLAGS + leaf + 1]
            used = []
            for level in range(levels):
                flag = jnp.sum(jnp.where(lane == level, flags, 0.0), axis=1, keepdims=True)
                used.append(jnp.broadcast_to(flag, (1, SK)))
            here = aligned(index * rows + leaf * LEAF, LEAF, LEAF)
            tile = jnp.exp2(nn(tops[...], bt_ref[:, here])).astype(bf16)
            scaled = (coefs[...].astype(f32) * jnp.concatenate(used, 1)).astype(bf16)
            far = nn(scaled, tile)
            totals.append(near_ref[:, here] + far[:width] + far[width:])
        both = stack_two(jnp.concatenate(totals, 1))
        parts = [both[:, h * LOW : (h + 1) * LOW] for h in range(rows // LOW)]
        moved = nn(jnp.concatenate(parts, 0), low_hot[...])
        result = jnp.zeros((2 * width, rows), f32)
        for h in range(rows // LOW):
            result = jnp.where(high_part == h, moved[h * 2 * width : (h + 1) * 2 * width], result)
        result = result[:width] + result[width:]
        for g, out_ref in enumerate(out_refs):
            out_ref[:, layout.lanes(index)] = result[:, g * layout.per : (g + 1) * layout.per]
        return carry

    lax.fori_loop(0, blocks, block, 0)


def final_kernel(blocks, where_ref, pos_ref, *refs):
    back_refs, (weights_ref, out_ref, perm, vals) = refs[:-4], refs[-4:]
    chunks = pos_ref.shape[0]
    rows = chunks * LANES
    width, split = back_refs[0].shape
    for r in range(chunks):
        spread(perm, slice(r * LANES, (r + 1) * LANES), column(pos_ref[r : r + 1, :]))
    for g, back_ref in enumerate(back_refs):
        high, low = two(back_ref[...])
        columns, at = 0, slice(0, rows)
        if blocks:
            columns = (where_ref[1] ^ (g % blocks)) * width
            at = aligned((where_ref[0] ^ where_ref[2] ^ (g // blocks)) * split, split, split)
        vals[aligned(columns, width, width), at] = high
        vals[aligned(columns + LANES, width, width), at] = low
    step = 256
    for s in range(rows // step):
        here = slice(s * step, (s + 1) * step)
        moved = nt(perm[here, :], vals[...])
        out_ref[here, :] = ridge * weights_ref[here, :] + moved[:, :LANES] + moved[:, LANES:]


def upper_levels(pack, skeleton_upper, my_leaf, trees, blocks, width):
    devices = trees * blocks
    level = blocks.bit_length() - 1
    offset = sum(devices >> step for step in range(1, level + 1))
    line = jnp.arange(LANES)[:, None]
    is_point, is_norm = line < DIM, (line >= DIM + 3) & (line < DIM + 6)
    is_coef = line >= LANES - width
    packs, own, stride = [], pack, 1
    while stride < trees:
        other = lax.ppermute(own, "leaf", [(i, i ^ stride) for i in range(trees)])
        packs.append(other)
        stride *= 2
        if stride < trees:
            second = (my_leaf // (stride // 2)) % 2 == 1
            pair = jnp.where(second, jnp.concatenate([other, own], 1), jnp.concatenate([own, other], 1))
            chosen = pair[:, skeleton_upper[offset + my_leaf // stride]]
            level += 1
            offset += devices >> level
            norms = jnp.sum(jnp.where(is_norm, pair, 0.0), axis=0)
            chosen_norms = jnp.sum(jnp.where(is_norm, chosen, 0.0), axis=0)
            inner = jnp.dot(
                jnp.where(is_point, pair, 0.0).T, jnp.where(is_point, chosen, 0.0), precision=highest
            )
            tile = jnp.exp2(inner + norms[:, None] + chosen_norms[None])
            own = jnp.where(is_coef, jnp.dot(pair, tile, precision=highest), chosen)
    return jnp.stack(packs)


def body(points, weights, tree_slot, near_count, near_list, skeleton_base, skeleton_upper, far_use):
    blocks, trees, reps = lax.axis_size("sub"), lax.axis_size("leaf"), lax.axis_size("rep")
    devices = blocks * trees
    rows, columns = weights.shape
    low_levels = blocks.bit_length() - 1
    ups = trees.bit_length() - 1
    width = columns // blocks
    part = rows // trees
    per = part // blocks
    total = blocks * rows
    leaves = total // LEAF
    my_leaf = lax.axis_index("leaf")
    fine = trees == 2 and reps == 2 and per % LANES == 0
    layout = Layout(blocks, trees, rows, fine)
    split = part if fine else rows
    where = jnp.stack([my_leaf, lax.axis_index("sub"), lax.axis_index("rep")]).astype(jnp.int32)
    arrive = shaped((width, part), f32) if fine else shaped((width, total), f32)

    place, pos, light = pl.pallas_call(
        functools.partial(sort_kernel, fine),
        out_shape=(
            shaped((PLACE_ROWS, split), f32),
            shaped((rows // LANES, LANES), f32),
            shaped((rows // split, columns, split), f32),
        ),
        in_specs=[spec(SMEM)] + [spec()] * 5,
        out_specs=(spec(),) * 3,
        scratch_shapes=[
            vm((rows, rows), bf16),
            vm((272, rows), bf16),
            vm((rows // split, PLACE_ROWS, split), f32),
        ],
        compiler_params=params(),
        name="sort_rows",
    )(where, tree_slot.reshape(rows // LANES, LANES), points.T, weights, skeleton_base, far_use)

    axes = ("leaf", "sub", "rep")

    def swap(value, step, other=0):
        pairs = []
        for leaf in range(trees):
            for sub in range(blocks):
                for core in range(reps):
                    to = ((leaf ^ core ^ other) * blocks + (sub ^ step)) * reps + core
                    pairs.append(((leaf * blocks + sub) * reps + core, to))
        return lax.ppermute(value, axes, pairs)

    def swap_all(values):
        done = {}
        for g in sorted(range(len(values)), key=lambda g: -(g % blocks)):
            done[g] = swap(values[g], g % blocks, g // blocks)
        return [done[g] for g in range(len(values))]

    if fine:
        place = {0: swap(place, 0)}
        stride = blocks // 2
        while stride:
            for step in sorted(place):
                place[step | stride] = lax.ppermute(place[step], "sub", [(i, i ^ stride) for i in range(blocks)])
            stride //= 2
        place = [place[step] for step in range(blocks)]
        place, light = lax.optimization_barrier((place, light))
        place = place + [lax.ppermute(one, "rep", [(0, 1), (1, 0)]) for one in place]
        light = light.reshape(devices, width, part)
        light = lax.all_to_all(light, ("leaf", "sub"), split_axis=0, concat_axis=0, tiled=True)
        small = jnp.zeros((1, 8, SK), f32)
    else:
        info = jnp.pad(far_use.astype(f32), ((FLAGS, 5 - far_use.shape[0]), (0, SK - far_use.shape[1])))
        small = lax.all_gather(info.at[BASE].set(skeleton_base[0].astype(f32)), "sub", axis=0, tiled=False)
        place = place.reshape(PLACE_ROWS, trees, part).transpose(1, 0, 2)
        place = lax.all_to_all(place, "leaf", split_axis=0, concat_axis=0, tiled=True)
        place = lax.all_gather(place, "sub", axis=0, tiled=False)
        place = place.transpose(1, 0, 2, 3).reshape(devices, PLACE_ROWS, blocks, per)
        place = [place.transpose(1, 2, 0, 3).reshape(PLACE_ROWS, total)]
        light = light.reshape(columns, trees, part).transpose(1, 0, 2).reshape(devices, width, part)
        light = lax.all_to_all(light, ("leaf", "sub"), split_axis=0, concat_axis=0, tiled=True)
        light = light.reshape(devices, width, blocks, per)
        light = light.transpose(1, 2, 0, 3).reshape(1, width, total)

    nodes = 2 * blocks - 1
    feat_a, feat_bt, sk, base, upper_tiles, top, slots, info = pl.pallas_call(
        functools.partial(points_kernel, layout, trees),
        out_shape=(
            shaped((total, FEAT), bf16),
            shaped((FEAT, total), bf16),
            shaped((nodes * SK, FEAT), bf16),
            shaped((blocks, rows, SK), bf16),
            shaped((blocks - 1, 2 * SK, SK), f32),
            shaped((SK, LANES), f32),
            shaped((blocks, rows), f32),
            shaped((blocks, 8, SK), f32),
        ),
        in_specs=[spec(SMEM)] + [spec()] * (2 + layout.count),
        out_specs=(spec(),) * 8,
        scratch_shapes=[
            vm((rows // LOW * COORD, rows), bf16),
            vm((rows, LOW), bf16),
            vm((COORD, rows), bf16),
            vm((COORD, nodes * SK), bf16),
            vm((FEAT, SK), bf16),
        ],
        compiler_params=params(),
        name="tree_points",
    )(where, skeleton_upper, small, *place)

    tree_light, coefs, pack = pl.pallas_call(
        functools.partial(weights_kernel, layout),
        out_shape=(
            shaped((width, total), bf16),
            shaped((2 * width, nodes * SK), bf16),
            shaped((LANES, SK), f32),
        ),
        in_specs=[spec(SMEM)] + [spec()] * 5,
        out_specs=(spec(),) * 3,
        scratch_shapes=[vm((rows // LOW * width, rows), bf16), vm((rows, LOW), bf16)],
        compiler_params=params(),
        name="tree_weights",
    )(where, base, upper_tiles, top, slots, light)

    packs = upper_levels(pack, skeleton_upper, my_leaf, trees, blocks, width)

    near = pl.pallas_call(
        near_kernel,
        out_shape=shaped((width, total), f32),
        in_specs=[spec(SMEM)] * 2 + [spec()] * 3,
        out_specs=spec(),
        scratch_shapes=[
            pltpu.SMEM((leaves,), jnp.int32),
            pltpu.SMEM((3, leaves * leaves + 1), jnp.int32),
            vm((LEAF, LEAF // 2), f32),
        ],
        compiler_params=params(),
        name="near",
    )(near_count, near_list[0], feat_a, feat_bt, tree_light)

    levels = low_levels + ups
    back = pl.pallas_call(
        functools.partial(far_kernel, layout, low_levels),
        out_shape=(arrive,) * layout.count,
        in_specs=[spec()] * 7,
        out_specs=(spec(),) * layout.count,
        scratch_shapes=[vm((levels * SK, FEAT), bf16), vm((2 * width, levels * SK), bf16), vm((LOW, rows), bf16)],
        compiler_params=params(),
        name="far",
    )(packs, slots, info, feat_bt, sk, coefs, near)

    if fine:
        back = swap_all(back)
    else:
        back = back[0].reshape(width, blocks, devices, per).transpose(2, 0, 1, 3).reshape(devices, width, part)
        back = lax.all_to_all(back, ("leaf", "sub"), split_axis=0, concat_axis=0, tiled=True)
        back = [back.reshape(trees, columns, part).transpose(1, 0, 2).reshape(columns, rows)]

    return pl.pallas_call(
        functools.partial(final_kernel, blocks if fine else 0),
        out_shape=shaped((rows, columns), f32),
        in_specs=[spec(SMEM)] + [spec()] * (2 + layout.count),
        out_specs=spec(),
        scratch_shapes=[vm((rows, rows), bf16), vm((2 * LANES, rows), bf16)],
        compiler_params=params(),
        name="to_input_order",
    )(where, pos, *back, weights)


def solution(mesh):
    in_specs = (
        P(("groups", "leaf", "sub"), None),
        P(("groups", "leaf", "sub"), "rep"),
        P(("groups", "leaf", "sub")),
        P(("groups", "leaf"), None),
        P(("groups", "leaf"), None, None),
        P(("groups", "leaf", "sub"), None),
        P("groups", None),
        P(("groups", "leaf", "sub"), None),
    )
    out_specs = P(("groups", "leaf", "sub"), "rep")
    return jax.shard_map(body, mesh=mesh, in_specs=in_specs, out_specs=out_specs, check_vma=False)
```

```python
import functools

import jax
import jax.numpy as jnp
from jax import lax
from jax.experimental import pallas as pl
from jax.experimental.pallas import tpu as pltpu
from jax.sharding import PartitionSpec as P

DIM = 64
LEAF = 512
SK = 128
LANES = 128
FEAT = 256
LOW = 256
COORD = 144

highest = lax.Precision.HIGHEST
point_scale = 0.25
ridge = 0.5
PLACE_ROWS = 72
TAIL = 64
SLOT, NORM, BASE, FLAGS = 0, 1, 2, 3
f32 = jnp.float32
bf16 = jnp.bfloat16
VMEM = pltpu.MemorySpace.VMEM
SMEM = pltpu.MemorySpace.SMEM


def spec(space=VMEM):
    return pl.BlockSpec(memory_space=space)


def params(mib=58):
    return pltpu.CompilerParams(vmem_limit_bytes=mib * 1024 * 1024)


def held(array):
    return pltpu.with_memory_space_constraint(array, VMEM)


def vm(shape, dtype):
    return pltpu.VMEM(shape, dtype)


def shaped(shape, dtype):
    return jax.ShapeDtypeStruct(shape, dtype)


def nt(left, right):
    return lax.dot_general(left, right, (((1,), (1,)), ((), ())), preferred_element_type=f32)


def nn(left, right):
    return jnp.dot(left, right, preferred_element_type=f32)


def column(row):
    return jnp.transpose(jnp.broadcast_to(row, (LANES, LANES)))


def iota(shape, dim):
    return lax.broadcasted_iota(jnp.int32, shape, dim)


def onehot(mask):
    return jnp.where(mask, 1.0, 0.0).astype(bf16)


def two(value):
    high = value.astype(bf16)
    return high, (value - high.astype(f32)).astype(bf16)


def three(value):
    high = value.astype(bf16).astype(f32)
    mid = (value - high).astype(bf16).astype(f32)
    return high, mid, (value - high - mid).astype(bf16).astype(f32)


def lanes_of(blocks):
    return blocks[0] if len(blocks) == 1 else jnp.concatenate(blocks, 1)


def aligned(start, size, unit):
    return pl.ds(pl.multiple_of(start, unit), size)


def stack_two(value):
    high, low = two(value)
    return jnp.concatenate([high, low], 0)


def spread(perm, here, rank):
    lane = iota((LANES, LANES), 1).astype(f32)
    for c in range(perm.shape[1] // LANES):
        perm[here, c * LANES : (c + 1) * LANES] = onehot(lane + float(c * LANES) == rank)


def sort_kernel(
    fine, slot_ref, points_ref, weights_ref, base_ref, flag_ref, place_ref, pos_ref, light_ref, perm, vals, whole
):
    chunks, split = slot_ref.shape[0], light_ref.shape[-1]
    rows = chunks * LANES
    slots = slot_ref[...]
    slot = slots.astype(f32)
    within = slots & (rows - 1)
    high, low = (within >> 5).astype(f32), (within & 31).astype(f32)
    for r in range(chunks):
        here = slice(r * LANES, (r + 1) * LANES)
        mine = column(slot[r : r + 1])
        before = jnp.zeros((LANES, LANES), f32)
        for c in range(chunks):
            before += jnp.where(slot[c : c + 1] < mine, 1.0, 0.0)
        rank = jnp.broadcast_to(jnp.sum(before, axis=1, keepdims=True), (LANES, LANES))
        pos_ref[r : r + 1, :] = jnp.transpose(rank)[0:1]
        spread(perm, here, rank)
        vals[0:LANES, here] = jnp.transpose(weights_ref[here, :]).astype(bf16)
    scaled = points_ref[...] * point_scale
    ph, plo = two(scaled)
    nh, nm, nl = three(-0.5 * jnp.sum(scaled * scaled, axis=0, keepdims=True))
    vals[128:192, :] = ph
    vals[192:256, :] = plo
    sub = iota((16, LANES), 0)
    for c in range(chunks):
        at = slice(c * LANES, (c + 1) * LANES)
        extra = jnp.where(sub == 0, high[c : c + 1], jnp.where(sub == 1, low[c : c + 1], 0.0))
        extra = jnp.where(sub == 2, nh[:, at], jnp.where(sub == 3, nm[:, at], extra))
        vals[256:272, at] = jnp.where(sub == 4, nl[:, at], extra).astype(bf16)
    step = 256
    for s in range(rows // step):
        moved = nn(vals[...], perm[:, s * step : (s + 1) * step])
        at = slice((s * step) % split, (s * step) % split + step)
        part = (s * step) // split
        light_ref[part, :, at] = moved[0:LANES]
        whole[part, 0:TAIL, at] = moved[128:192] + moved[192:256]
        tail = iota((8, step), 0)
        slot_row = moved[256:257] * 32.0 + moved[257:258]
        norm_row = moved[258:259] + moved[259:260] + moved[260:261]
        whole[part, TAIL:, at] = jnp.where(tail == SLOT, slot_row, jnp.where(tail == NORM, norm_row, 0.0))
    if not fine:
        place_ref[...] = whole[0]
        return
    place_ref[...] = whole[lax.axis_index("leaf") ^ lax.axis_index("rep")]
    place_ref[TAIL + BASE : TAIL + BASE + 1, 0:SK] = base_ref[...].astype(f32)
    place_ref[TAIL + FLAGS : TAIL + FLAGS + flag_ref.shape[0], 0 : flag_ref.shape[1]] = flag_ref[...].astype(f32)


class Layout:
    def __init__(self, blocks, trees, rows, fine):
        self.blocks, self.rows, self.fine = blocks, rows, fine
        self.count = blocks * trees if fine else 1
        self.per = rows // self.count

    def lanes(self, index):
        return aligned(index * self.per, self.per, LANES)

    def message(self, group):
        if not self.fine:
            return 0
        leaf = lax.axis_index("leaf") ^ lax.axis_index("rep") ^ (group // self.blocks)
        return leaf * self.blocks + (lax.axis_index("sub") ^ (group % self.blocks))

    def gather(self, refs, index, part):
        return lanes_of([ref[part, self.lanes(index)] for ref in refs])

    def info(self, refs, small_ref, index):
        if not self.fine:
            return small_ref[index]
        core = lax.axis_index("rep")
        found = jnp.zeros((PLACE_ROWS - TAIL, SK), f32)
        for step in range(self.blocks):
            mine, theirs = refs[step][TAIL:, 0:SK], refs[self.blocks + step][TAIL:, 0:SK]
            here = jnp.where(core == 0, mine, theirs)
            found = jnp.where((lax.axis_index("sub") ^ step) == index, here, found)
        return found


def low_by_column(out, low):
    for c in range(out.shape[0] // LANES):
        at = slice(c * LANES, (c + 1) * LANES)
        spread(out, at, column(low[:, at]))


def parts_of(slots):
    slots = slots.astype(jnp.int32)
    return slots & (LOW - 1), slots // LOW


def feature_columns(out, at, tree):
    out[0:64, at] = tree[0:64].astype(bf16)
    out[64:128, at] = tree[0:64].astype(bf16)
    out[128:192, at] = tree[64:128].astype(bf16)
    out[192:256, at] = jnp.concatenate([tree[128:136], jnp.zeros((56, tree.shape[1]), f32)], 0).astype(bf16)


def feature_rows(high, low, extra):
    first = jnp.transpose(jnp.concatenate([high, low], 0))
    second = jnp.transpose(jnp.concatenate([high, extra, jnp.zeros((56, high.shape[1]), f32)], 0))
    return first.astype(bf16), second.astype(bf16)


def points_kernel(layout, trees, upper_ref, small_ref, *refs):
    place_refs, refs = refs[: layout.count], refs[layout.count :]
    a_ref, bt_ref, sk_ref, base_ref, upper_tiles_ref, top_ref, slot_ref, info_ref, masked, low_hot, tree, sk_t, sk_bt = refs
    blocks, rows = layout.blocks, layout.rows

    def keep(node, found):
        at = aligned(node * SK, SK, SK)
        sk_t[:, at] = found.astype(bf16)
        sk_ref[at, 0:128], sk_ref[at, 128:256] = feature_rows(found[0:64], found[64:128], found[136:144])
        feature_columns(sk_bt, slice(0, SK), found)

    def block(index, carry):
        tail = layout.gather(place_refs, index, slice(TAIL, PLACE_ROWS))
        slots = tail[SLOT : SLOT + 1]
        slot_ref[pl.ds(index, 1), :] = slots
        info = layout.info(place_refs, small_ref, index)
        info_ref[index] = info
        points = layout.gather(place_refs, index, slice(0, TAIL))
        high, low = two(points)
        nh, nm, nl = three(tail[NORM : NORM + 1])
        sub = iota((16, rows), 0)
        norms = jnp.where((sub == 3) | (sub == 8), nh, jnp.where((sub == 4) | (sub == 9), nm, nl))
        is_norm = ((sub >= 3) & (sub < 6)) | ((sub >= 8) & (sub < 11))
        is_one = (sub < 3) | ((sub >= 11) & (sub < 14))
        extra = jnp.where(is_norm, norms, jnp.where(is_one, 1.0, 0.0))
        low_part, high_part = parts_of(slots)
        low_by_column(low_hot, low_part.astype(f32))
        for h in range(rows // LOW):
            here = high_part == h
            masked[h * COORD : h * COORD + 64, :] = jnp.where(here, high.astype(f32), 0.0).astype(bf16)
            masked[h * COORD + 64 : h * COORD + 128, :] = jnp.where(here, low.astype(f32), 0.0).astype(bf16)
            masked[h * COORD + 128 : (h + 1) * COORD, :] = jnp.where(here, extra, 0.0).astype(bf16)
        placed = nn(masked[...], low_hot[...])
        for h in range(rows // LOW):
            part = placed[h * COORD : (h + 1) * COORD]
            tree[:, h * LOW : (h + 1) * LOW] = part.astype(bf16)
            at = aligned(index * rows + h * LOW, LOW, LOW)
            feature_columns(bt_ref, at, part)
            a_ref[at, 0:128], a_ref[at, 128:256] = feature_rows(part[0:64], part[64:128], part[136:144])
        picked = onehot(iota((rows, SK), 0) == info[BASE : BASE + 1].astype(jnp.int32))
        keep(index, nn(tree[...], picked))
        mine = aligned(index * rows, rows, rows)
        base_ref[index] = jnp.exp(nn(a_ref[mine, :], sk_bt[...])).astype(bf16)
        return carry

    lax.fori_loop(0, blocks, block, 0)
    start, count, offset, total = 0, blocks, 0, blocks * trees
    while count > 1:
        nodes = count // 2
        for j in range(nodes):
            pair = slice((start + 2 * j) * SK, (start + 2 * j + 2) * SK)
            row = offset + lax.axis_index("leaf") * nodes + j
            picked = onehot(iota((2 * SK, SK), 0) == upper_ref[pl.ds(row, 1), :])
            here = start + count + j
            keep(here, nn(sk_t[:, pair], picked))
            upper_tiles_ref[here - blocks] = jnp.exp(nn(sk_ref[pair, :], sk_bt[...]))
        total = total // 2
        offset = offset + total
        start, count = start + count, nodes
    found = sk_t[:, start * SK : (start + 1) * SK].astype(f32)
    top_ref[0:64, :] = found[0:64] + found[64:128]
    top_ref[64:72, :] = found[128:136]
    top_ref[72:128, :] = jnp.zeros((56, SK), f32)


def weights_kernel(
    layout, base_ref, upper_tiles_ref, top_ref, slot_ref, light_ref, w_ref, coef_ref, pack_ref, masked, low_hot
):
    blocks, rows = layout.blocks, layout.rows
    width = light_ref.shape[1]
    pack_ref[...] = top_ref[...]

    def keep(node, coef):
        coef_ref[:, aligned(node * SK, SK, SK)] = stack_two(coef)
        pack_ref[LANES - width :, :] = coef

    def block(index, carry):
        low_part, high_part = parts_of(slot_ref[pl.ds(index, 1), :])
        low_by_column(low_hot, low_part.astype(f32))
        light = [light_ref[layout.message(g), :, layout.lanes(index)] for g in range(layout.count)]
        light = lanes_of(light)
        for h in range(rows // LOW):
            masked[h * width : (h + 1) * width, :] = jnp.where(high_part == h, light, 0.0).astype(bf16)
        placed = nn(masked[...], low_hot[...])
        parts = [placed[h * width : (h + 1) * width] for h in range(rows // LOW)]
        own = jnp.concatenate(parts, 1).astype(bf16)
        w_ref[:, aligned(index * rows, rows, rows)] = own
        keep(index, nn(own, base_ref[index]))
        return carry

    lax.fori_loop(0, blocks, block, 0)
    start, count = 0, blocks
    while count > 1:
        for j in range(count // 2):
            pair = slice((start + 2 * j) * SK, (start + 2 * j + 2) * SK)
            here = start + count + j
            high, low = two(upper_tiles_ref[here - blocks])
            coef = nn(coef_ref[:, pair], high)
            keep(here, coef[:width] + coef[width:] + nn(coef_ref[0:width, pair], low))
        start, count = start + count, count // 2


def near_kernel(count_ref, list_ref, a_ref, bt_ref, w_ref, acc, times, tiles, ahead):
    every = count_ref.shape[1]

    def tally(leaf, filled):
        for other in range(every):
            times[other] = (leaf == other).astype(jnp.int32)

        def add(slot, carry):
            at = list_ref[leaf, slot]
            times[at] = times[at] + 1
            return carry

        lax.fori_loop(0, count_ref[0, leaf], add, 0)
        for other in range(every):
            tiles[0, filled] = leaf
            tiles[1, filled] = other
            tiles[2, filled] = times[other]
            filled = filled + (times[other] > 0).astype(jnp.int32)
        return filled

    filled = lax.fori_loop(0, every, tally, jnp.int32(0))
    tiles[0, filled] = 0
    tiles[1, filled] = 0
    half = LEAF // 2
    acc[...] = jnp.zeros_like(acc)

    def target(tile, part):
        return aligned(tiles[0, tile] * LEAF + part * half, half, half)

    def exponents(tile, part):
        source = aligned(tiles[1, tile] * LEAF, LEAF, LEAF)
        return nn(a_ref[source, :], bt_ref[:, target(tile, part)])

    def add(tile, part, block):
        source = aligned(tiles[1, tile] * LEAF, LEAF, LEAF)
        acc[:, target(tile, part)] += tiles[2, tile].astype(f32) * nn(w_ref[:, source], block)

    ahead[...] = exponents(0, 0)

    def step(tile, carry):
        block = jnp.exp(ahead[...]).astype(bf16)
        second = exponents(tile, 1)
        add(tile, 0, block)
        ahead[...] = exponents(tile + 1, 0)
        add(tile, 1, jnp.exp(second).astype(bf16))
        return carry

    lax.fori_loop(0, filled, step, 0)


def far_kernel(layout, low_levels, pack_ref, slot_ref, info_ref, bt_ref, sk_ref, coef_ref, near_ref, *refs):
    out_refs, (tops, coefs, low_hot) = refs[: layout.count], refs[layout.count :]
    blocks, rows = layout.blocks, layout.rows
    ups, width = pack_ref.shape[0], out_refs[0].shape[0]
    levels = low_levels + ups
    lane = iota((1, SK), 1)
    for up in range(ups):
        pack = pack_ref[up]
        high, low = two(pack[0:64])
        sub = iota((8, SK), 0)
        extra = jnp.where(sub == 0, pack[67:68], jnp.where(sub == 1, pack[68:69], pack[69:70]))
        extra = jnp.where(sub < 3, extra, jnp.where(sub < 6, 1.0, 0.0))
        at = slice((low_levels + up) * SK, (low_levels + up + 1) * SK)
        tops[at, 0:128], tops[at, 128:256] = feature_rows(high.astype(f32), low.astype(f32), extra)
        coefs[:, at] = stack_two(pack[LANES - width :])

    def block(index, carry):
        node, start, count = index, 0, blocks
        for level in range(low_levels):
            at = slice(level * SK, (level + 1) * SK)
            other = aligned((start + (node ^ 1)) * SK, SK, SK)
            tops[at, :] = sk_ref[other, :]
            coefs[:, at] = coef_ref[:, other]
            node, start, count = node // 2, start + count, count // 2
        low_part, high_part = parts_of(slot_ref[pl.ds(index, 1), :])
        for c in range(rows // LANES):
            at = slice(c * LANES, (c + 1) * LANES)
            low_hot[:, at] = onehot(iota((LOW, LANES), 0) == low_part[:, at])
        info = info_ref[index]
        totals = []
        for leaf in range(rows // LEAF):
            flags = info[FLAGS + leaf : FLAGS + leaf + 1]
            used = []
            for level in range(levels):
                flag = jnp.sum(jnp.where(lane == level, flags, 0.0), axis=1, keepdims=True)
                used.append(jnp.broadcast_to(flag, (1, SK)))
            here = aligned(index * rows + leaf * LEAF, LEAF, LEAF)
            tile = jnp.exp(nn(tops[...], bt_ref[:, here])).astype(bf16)
            scaled = (coefs[...].astype(f32) * jnp.concatenate(used, 1)).astype(bf16)
            far = nn(scaled, tile)
            totals.append(near_ref[:, here] + far[:width] + far[width:])
        both = stack_two(jnp.concatenate(totals, 1))
        parts = [both[:, h * LOW : (h + 1) * LOW] for h in range(rows // LOW)]
        moved = nn(jnp.concatenate(parts, 0), low_hot[...])
        result = jnp.zeros((2 * width, rows), f32)
        for h in range(rows // LOW):
            result = jnp.where(high_part == h, moved[h * 2 * width : (h + 1) * 2 * width], result)
        result = result[:width] + result[width:]
        for g, out_ref in enumerate(out_refs):
            out_ref[:, layout.lanes(index)] = result[:, g * layout.per : (g + 1) * layout.per]
        return carry

    lax.fori_loop(0, blocks, block, 0)


def final_kernel(blocks, pos_ref, *refs):
    back_refs, (weights_ref, out_ref, perm, vals) = refs[:-4], refs[-4:]
    chunks = pos_ref.shape[0]
    rows = chunks * LANES
    width, split = back_refs[0].shape
    for r in range(chunks):
        spread(perm, slice(r * LANES, (r + 1) * LANES), column(pos_ref[r : r + 1, :]))
    for g, back_ref in enumerate(back_refs):
        high, low = two(back_ref[...])
        columns, at = 0, slice(0, rows)
        if blocks:
            columns = (lax.axis_index("sub") ^ (g % blocks)) * width
            at = aligned((lax.axis_index("leaf") ^ lax.axis_index("rep") ^ (g // blocks)) * split, split, split)
        vals[aligned(columns, width, width), at] = high
        vals[aligned(columns + LANES, width, width), at] = low
    step = 256
    for s in range(rows // step):
        here = slice(s * step, (s + 1) * step)
        moved = nt(perm[here, :], vals[...])
        out_ref[here, :] = ridge * weights_ref[here, :] + moved[:, :LANES] + moved[:, LANES:]


def upper_levels(pack, skeleton_upper, my_leaf, trees, blocks, width):
    devices = trees * blocks
    level = blocks.bit_length() - 1
    offset = sum(devices >> step for step in range(1, level + 1))
    line = jnp.arange(LANES)[:, None]
    is_point, is_norm = line < DIM, (line >= DIM + 3) & (line < DIM + 6)
    is_coef = line >= LANES - width
    packs, own, stride = [], pack, 1
    while stride < trees:
        other = lax.ppermute(own, "leaf", [(i, i ^ stride) for i in range(trees)])
        packs.append(other)
        stride *= 2
        if stride < trees:
            second = (my_leaf // (stride // 2)) % 2 == 1
            pair = jnp.where(second, jnp.concatenate([other, own], 1), jnp.concatenate([own, other], 1))
            chosen = pair[:, skeleton_upper[offset + my_leaf // stride]]
            level += 1
            offset += devices >> level
            norms = jnp.sum(jnp.where(is_norm, pair, 0.0), axis=0)
            chosen_norms = jnp.sum(jnp.where(is_norm, chosen, 0.0), axis=0)
            inner = jnp.dot(
                jnp.where(is_point, pair, 0.0).T, jnp.where(is_point, chosen, 0.0), precision=highest
            )
            tile = jnp.exp(inner + norms[:, None] + chosen_norms[None])
            own = jnp.where(is_coef, jnp.dot(pair, tile, precision=highest), chosen)
    return jnp.stack(packs)


def body(points, weights, tree_slot, near_count, near_list, skeleton_base, skeleton_upper, far_use):
    blocks, trees, reps = lax.axis_size("sub"), lax.axis_size("leaf"), lax.axis_size("rep")
    devices = blocks * trees
    rows, columns = weights.shape
    low_levels = blocks.bit_length() - 1
    ups = trees.bit_length() - 1
    width = columns // blocks
    part = rows // trees
    per = part // blocks
    total = blocks * rows
    leaves = total // LEAF
    my_leaf = lax.axis_index("leaf")
    fine = trees == 2 and reps == 2 and per % LANES == 0
    layout = Layout(blocks, trees, rows, fine)
    split = part if fine else rows
    arrive = shaped((width, part), f32) if fine else shaped((width, total), f32)

    place, pos, light = pl.pallas_call(
        functools.partial(sort_kernel, fine),
        out_shape=(
            shaped((PLACE_ROWS, split), f32),
            shaped((rows // LANES, LANES), f32),
            shaped((rows // split, columns, split), f32),
        ),
        in_specs=[spec()] * 5,
        out_specs=(spec(),) * 3,
        scratch_shapes=[
            vm((rows, rows), bf16),
            vm((272, rows), bf16),
            vm((rows // split, PLACE_ROWS, split), f32),
        ],
        compiler_params=params(),
        name="sort_rows",
    )(tree_slot.reshape(rows // LANES, LANES), points.T, weights, skeleton_base, far_use)

    axes = ("leaf", "sub", "rep")

    def swap(value, step, other=0):
        pairs = []
        for leaf in range(trees):
            for sub in range(blocks):
                for core in range(reps):
                    to = ((leaf ^ core ^ other) * blocks + (sub ^ step)) * reps + core
                    pairs.append(((leaf * blocks + sub) * reps + core, to))
        return lax.ppermute(value, axes, pairs)

    def swap_all(values):
        done = {}
        for g in sorted(range(len(values)), key=lambda g: -(g % blocks)):
            done[g] = swap(values[g], g % blocks, g // blocks)
        return [done[g] for g in range(len(values))]

    if fine:
        place = {0: swap(place, 0)}
        stride = blocks // 2
        while stride:
            for step in sorted(place):
                place[step | stride] = lax.ppermute(place[step], "sub", [(i, i ^ stride) for i in range(blocks)])
            stride //= 2
        place = [place[step] for step in range(blocks)]
        place[1], light = lax.optimization_barrier((place[1], light))
        place = place + [lax.ppermute(one, "rep", [(0, 1), (1, 0)]) for one in place]
        light = light.reshape(devices, width, part)
        light = lax.all_to_all(light, ("leaf", "sub"), split_axis=0, concat_axis=0, tiled=True)
        small = pos
    else:
        info = jnp.pad(far_use.astype(f32), ((FLAGS, 5 - far_use.shape[0]), (0, SK - far_use.shape[1])))
        small = lax.all_gather(info.at[BASE].set(skeleton_base[0].astype(f32)), "sub", axis=0, tiled=False)
        place = place.reshape(PLACE_ROWS, trees, part).transpose(1, 0, 2)
        place = lax.all_to_all(place, "leaf", split_axis=0, concat_axis=0, tiled=True)
        place = lax.all_gather(place, "sub", axis=0, tiled=False)
        place = place.transpose(1, 0, 2, 3).reshape(devices, PLACE_ROWS, blocks, per)
        place = [place.transpose(1, 2, 0, 3).reshape(PLACE_ROWS, total)]
        light = light.reshape(columns, trees, part).transpose(1, 0, 2).reshape(devices, width, part)
        light = lax.all_to_all(light, ("leaf", "sub"), split_axis=0, concat_axis=0, tiled=True)
        light = light.reshape(devices, width, blocks, per)
        light = light.transpose(1, 2, 0, 3).reshape(1, width, total)

    nodes = 2 * blocks - 1
    feat_a, feat_bt, sk, base, upper_tiles, top, slots, info = pl.pallas_call(
        functools.partial(points_kernel, layout, trees),
        out_shape=(
            vm((total, FEAT), bf16),
            vm((FEAT, total), bf16),
            vm((nodes * SK, FEAT), bf16),
            vm((blocks, rows, SK), bf16),
            vm((blocks - 1, 2 * SK, SK), f32),
            vm((SK, LANES), f32),
            vm((blocks, rows), f32),
            vm((blocks, 8, SK), f32),
        ),
        in_specs=[spec()] * (2 + layout.count),
        out_specs=(spec(),) * 8,
        scratch_shapes=[
            vm((rows // LOW * COORD, rows), bf16),
            vm((rows, LOW), bf16),
            vm((COORD, rows), bf16),
            vm((COORD, nodes * SK), bf16),
            vm((FEAT, SK), bf16),
        ],
        compiler_params=params(40),
        name="tree_points",
    )(skeleton_upper, small, *place)

    tree_light, coefs, pack = pl.pallas_call(
        functools.partial(weights_kernel, layout),
        out_shape=(
            vm((width, total), bf16),
            vm((2 * width, nodes * SK), bf16),
            shaped((LANES, SK), f32),
        ),
        in_specs=[spec()] * 5,
        out_specs=(spec(),) * 3,
        scratch_shapes=[vm((rows // LOW * width, rows), bf16), vm((rows, LOW), bf16)],
        compiler_params=params(40),
        name="tree_weights",
    )(held(base), held(upper_tiles), held(top), held(slots), light)

    packs = upper_levels(pack, skeleton_upper, my_leaf, trees, blocks, width)

    near = pl.pallas_call(
        near_kernel,
        out_shape=vm((width, total), f32),
        in_specs=[spec(SMEM)] * 2 + [spec()] * 3,
        out_specs=spec(),
        scratch_shapes=[
            pltpu.SMEM((leaves,), jnp.int32),
            pltpu.SMEM((3, leaves * leaves + 1), jnp.int32),
            vm((LEAF, LEAF // 2), f32),
        ],
        compiler_params=params(40),
        name="near",
    )(near_count, near_list[0], held(feat_a), held(feat_bt), held(tree_light))

    levels = low_levels + ups
    back = pl.pallas_call(
        functools.partial(far_kernel, layout, low_levels),
        out_shape=(arrive,) * layout.count,
        in_specs=[spec()] * 7,
        out_specs=(spec(),) * layout.count,
        scratch_shapes=[vm((levels * SK, FEAT), bf16), vm((2 * width, levels * SK), bf16), vm((LOW, rows), bf16)],
        compiler_params=params(40),
        name="far",
    )(packs, *[held(one) for one in (slots, info, feat_bt, sk, coefs, near)])

    if fine:
        back = swap_all(back)
    else:
        back = back[0].reshape(width, blocks, devices, per).transpose(2, 0, 1, 3).reshape(devices, width, part)
        back = lax.all_to_all(back, ("leaf", "sub"), split_axis=0, concat_axis=0, tiled=True)
        back = [back.reshape(trees, columns, part).transpose(1, 0, 2).reshape(columns, rows)]

    return pl.pallas_call(
        functools.partial(final_kernel, blocks if fine else 0),
        out_shape=shaped((rows, columns), f32),
        in_specs=[spec()] * (2 + layout.count),
        out_specs=spec(),
        scratch_shapes=[vm((rows, rows), bf16), vm((2 * LANES, rows), bf16)],
        compiler_params=params(40),
        name="to_input_order",
    )(pos, *back, weights)


def solution(mesh):
    in_specs = (
        P(("groups", "leaf", "sub"), None),
        P(("groups", "leaf", "sub"), "rep"),
        P(("groups", "leaf", "sub")),
        P(("groups", "leaf"), None),
        P(("groups", "leaf"), None, None),
        P(("groups", "leaf", "sub"), None),
        P("groups", None),
        P(("groups", "leaf", "sub"), None),
    )
    out_specs = P(("groups", "leaf", "sub"), "rep")
    return jax.shard_map(body, mesh=mesh, in_specs=in_specs, out_specs=out_specs, check_vma=False)
```

```python
import functools

import jax
import jax.numpy as jnp
from jax import lax
from jax.experimental import pallas as pl
from jax.experimental.pallas import tpu as pltpu
from jax.sharding import PartitionSpec as P

DIM = 64
LEAF = 512
SK = 128
LANES = 128
FEAT = 256
LOW = 256
COORD = 144

highest = lax.Precision.HIGHEST
point_scale = 0.25
ridge = 0.5
PLACE_ROWS = 72
TAIL = 64
SLOT, NORM, BASE, FLAGS = 0, 1, 2, 3
f32 = jnp.float32
bf16 = jnp.bfloat16
VMEM = pltpu.MemorySpace.VMEM
SMEM = pltpu.MemorySpace.SMEM


def spec(space=VMEM):
    return pl.BlockSpec(memory_space=space)


def params(mib=58):
    return pltpu.CompilerParams(vmem_limit_bytes=mib * 1024 * 1024)


def in_hbm(array):
    return pltpu.with_memory_space_constraint(array, pltpu.MemorySpace.HBM)


def held(array):
    return pltpu.with_memory_space_constraint(array, VMEM)


def vm(shape, dtype):
    return pltpu.VMEM(shape, dtype)


def shaped(shape, dtype):
    return jax.ShapeDtypeStruct(shape, dtype)


def nt(left, right):
    return lax.dot_general(left, right, (((1,), (1,)), ((), ())), preferred_element_type=f32)


def nn(left, right):
    return jnp.dot(left, right, preferred_element_type=f32)


def column(row):
    return jnp.transpose(jnp.broadcast_to(row, (LANES, LANES)))


def iota(shape, dim):
    return lax.broadcasted_iota(jnp.int32, shape, dim)


def onehot(mask):
    return jnp.where(mask, 1.0, 0.0).astype(bf16)


def two(value):
    high = value.astype(bf16)
    return high, (value - high.astype(f32)).astype(bf16)


def three(value):
    high = value.astype(bf16).astype(f32)
    mid = (value - high).astype(bf16).astype(f32)
    return high, mid, (value - high - mid).astype(bf16).astype(f32)


def lanes_of(blocks):
    return blocks[0] if len(blocks) == 1 else jnp.concatenate(blocks, 1)


def aligned(start, size, unit):
    return pl.ds(pl.multiple_of(start, unit), size)


def stack_two(value):
    high, low = two(value)
    return jnp.concatenate([high, low], 0)


def spread(perm, here, rank):
    lane = iota((LANES, LANES), 1).astype(f32)
    for c in range(perm.shape[1] // LANES):
        perm[here, c * LANES : (c + 1) * LANES] = onehot(lane + float(c * LANES) == rank)


def sort_kernel(
    fine, slot_ref, points_ref, weights_ref, base_ref, flag_ref, place_ref, pos_ref, light_ref, perm, vals, whole
):
    chunks, split = slot_ref.shape[0], light_ref.shape[-1]
    rows = chunks * LANES
    slots = slot_ref[...]
    slot = slots.astype(f32)
    within = slots & (rows - 1)
    high, low = (within >> 5).astype(f32), (within & 31).astype(f32)
    for r in range(chunks):
        here = slice(r * LANES, (r + 1) * LANES)
        mine = column(slot[r : r + 1])
        before = jnp.zeros((LANES, LANES), f32)
        for c in range(chunks):
            before += jnp.where(slot[c : c + 1] < mine, 1.0, 0.0)
        rank = jnp.broadcast_to(jnp.sum(before, axis=1, keepdims=True), (LANES, LANES))
        pos_ref[r : r + 1, :] = jnp.transpose(rank)[0:1]
        spread(perm, here, rank)
        vals[0:LANES, here] = jnp.transpose(weights_ref[here, :]).astype(bf16)
    scaled = points_ref[...] * point_scale
    ph, plo = two(scaled)
    nh, nm, nl = three(-0.5 * jnp.sum(scaled * scaled, axis=0, keepdims=True))
    vals[128:192, :] = ph
    vals[192:256, :] = plo
    sub = iota((16, LANES), 0)
    for c in range(chunks):
        at = slice(c * LANES, (c + 1) * LANES)
        extra = jnp.where(sub == 0, high[c : c + 1], jnp.where(sub == 1, low[c : c + 1], 0.0))
        extra = jnp.where(sub == 2, nh[:, at], jnp.where(sub == 3, nm[:, at], extra))
        vals[256:272, at] = jnp.where(sub == 4, nl[:, at], extra).astype(bf16)
    step = 256
    for s in range(rows // step):
        moved = nn(vals[...], perm[:, s * step : (s + 1) * step])
        at = slice((s * step) % split, (s * step) % split + step)
        part = (s * step) // split
        light_ref[part, :, at] = moved[0:LANES]
        whole[part, 0:TAIL, at] = moved[128:192] + moved[192:256]
        tail = iota((8, step), 0)
        slot_row = moved[256:257] * 32.0 + moved[257:258]
        norm_row = moved[258:259] + moved[259:260] + moved[260:261]
        whole[part, TAIL:, at] = jnp.where(tail == SLOT, slot_row, jnp.where(tail == NORM, norm_row, 0.0))
    if not fine:
        place_ref[...] = whole[0]
        return
    place_ref[...] = whole[lax.axis_index("leaf") ^ lax.axis_index("rep")]
    place_ref[TAIL + BASE : TAIL + BASE + 1, 0:SK] = base_ref[...].astype(f32)
    place_ref[TAIL + FLAGS : TAIL + FLAGS + flag_ref.shape[0], 0 : flag_ref.shape[1]] = flag_ref[...].astype(f32)


class Layout:
    def __init__(self, blocks, trees, rows, fine):
        self.blocks, self.rows, self.fine = blocks, rows, fine
        self.count = blocks * trees if fine else 1
        self.per = rows // self.count

    def lanes(self, index):
        return aligned(index * self.per, self.per, LANES)

    def message(self, group):
        if not self.fine:
            return 0
        leaf = lax.axis_index("leaf") ^ lax.axis_index("rep") ^ (group // self.blocks)
        return leaf * self.blocks + (lax.axis_index("sub") ^ (group % self.blocks))

    def gather(self, refs, index, part):
        return lanes_of([ref[part, self.lanes(index)] for ref in refs])

    def info(self, refs, small_ref, index):
        if not self.fine:
            return small_ref[index]
        core = lax.axis_index("rep")
        found = jnp.zeros((PLACE_ROWS - TAIL, SK), f32)
        for step in range(self.blocks):
            mine, theirs = refs[step][TAIL:, 0:SK], refs[self.blocks + step][TAIL:, 0:SK]
            here = jnp.where(core == 0, mine, theirs)
            found = jnp.where((lax.axis_index("sub") ^ step) == index, here, found)
        return found


def low_by_column(out, low):
    for c in range(out.shape[0] // LANES):
        at = slice(c * LANES, (c + 1) * LANES)
        spread(out, at, column(low[:, at]))


def parts_of(slots):
    slots = slots.astype(jnp.int32)
    return slots & (LOW - 1), slots // LOW


def feature_columns(out, at, tree):
    out[0:64, at] = tree[0:64].astype(bf16)
    out[64:128, at] = tree[0:64].astype(bf16)
    out[128:192, at] = tree[64:128].astype(bf16)
    out[192:208, at] = jnp.where(iota((16, tree.shape[1]), 0) < 8, tree[128:144].astype(f32), 0.0).astype(bf16)
    out[208:256, at] = jnp.zeros((48, tree.shape[1]), bf16)


def feature_rows(high, low, extra):
    first = jnp.transpose(jnp.concatenate([high, low], 0))
    second = jnp.transpose(jnp.concatenate([high, extra, jnp.zeros((56, high.shape[1]), f32)], 0))
    return first.astype(bf16), second.astype(bf16)


def points_kernel(layout, trees, upper_ref, *refs):
    if not layout.fine:
        small_ref, refs = refs[0], refs[1:]
    else:
        small_ref = None
    place_refs, refs = refs[: layout.count], refs[layout.count :]
    tree_ref, a_hbm, base_hbm, sk_ref, upper_tiles_ref, top_ref, slot_ref, info_ref = refs[:8]
    masked, low_hot, a_ref, base_ref, sk_t, sk_bt, sems = refs[8:]
    blocks, rows = layout.blocks, layout.rows

    def keep(node, found):
        at = aligned(node * SK, SK, SK)
        sk_t[:, at] = found.astype(bf16)
        sk_ref[at, 0:128], sk_ref[at, 128:256] = feature_rows(found[0:64], found[64:128], found[136:144])
        feature_columns(sk_bt, slice(0, SK), found)

    def block(index, carry):
        tail = layout.gather(place_refs, index, slice(TAIL, PLACE_ROWS))
        slots = tail[SLOT : SLOT + 1]
        slot_ref[pl.ds(index, 1), :] = slots
        info = layout.info(place_refs, small_ref, index)
        info_ref[index] = info
        points = layout.gather(place_refs, index, slice(0, TAIL))
        high, low = two(points)
        nh, nm, nl = three(tail[NORM : NORM + 1])
        sub = iota((16, rows), 0)
        norms = jnp.where((sub == 3) | (sub == 8), nh, jnp.where((sub == 4) | (sub == 9), nm, nl))
        is_norm = ((sub >= 3) & (sub < 6)) | ((sub >= 8) & (sub < 11))
        is_one = (sub < 3) | ((sub >= 11) & (sub < 14))
        extra = jnp.where(is_norm, norms, jnp.where(is_one, 1.0, 0.0))
        low_part, high_part = parts_of(slots)
        low_by_column(low_hot, low_part.astype(f32))
        for h in range(rows // LOW):
            here = high_part == h
            masked[h * COORD : h * COORD + 64, :] = jnp.where(here, high.astype(f32), 0.0).astype(bf16)
            masked[h * COORD + 64 : h * COORD + 128, :] = jnp.where(here, low.astype(f32), 0.0).astype(bf16)
            masked[h * COORD + 128 : (h + 1) * COORD, :] = jnp.where(here, extra, 0.0).astype(bf16)
        placed = nn(masked[...], low_hot[...])
        for h in range(rows // LOW):
            part = placed[h * COORD : (h + 1) * COORD]
            at = aligned(index * rows + h * LOW, LOW, LOW)
            tree_ref[:, at] = part.astype(bf16)
            a_ref[at, 0:128], a_ref[at, 128:256] = feature_rows(part[0:64], part[64:128], part[136:144])
        picked = onehot(iota((rows, SK), 0) == info[BASE : BASE + 1].astype(jnp.int32))
        mine = aligned(index * rows, rows, rows)
        pltpu.make_async_copy(a_ref.at[mine], a_hbm.at[mine], sems.at[0, index]).start()
        keep(index, nn(tree_ref[:, mine], picked))
        base_ref[index] = jnp.exp(nn(a_ref[mine, :], sk_bt[...])).astype(bf16)
        pltpu.make_async_copy(base_ref.at[index], base_hbm.at[index], sems.at[1, index]).start()
        return carry

    lax.fori_loop(0, blocks, block, 0)
    start, count, offset, total = 0, blocks, 0, blocks * trees
    while count > 1:
        nodes = count // 2
        for j in range(nodes):
            pair = slice((start + 2 * j) * SK, (start + 2 * j + 2) * SK)
            row = offset + lax.axis_index("leaf") * nodes + j
            picked = onehot(iota((2 * SK, SK), 0) == upper_ref[pl.ds(row, 1), :])
            here = start + count + j
            keep(here, nn(sk_t[:, pair], picked))
            upper_tiles_ref[here - blocks] = jnp.exp(nn(sk_ref[pair, :], sk_bt[...]))
        total = total // 2
        offset = offset + total
        start, count = start + count, nodes
    found = sk_t[:, start * SK : (start + 1) * SK].astype(f32)
    top_ref[0:64, :] = found[0:64] + found[64:128]
    top_ref[64:72, :] = found[128:136]
    top_ref[72:128, :] = jnp.zeros((56, SK), f32)
    for index in range(blocks):
        mine = slice(index * rows, (index + 1) * rows)
        pltpu.make_async_copy(a_ref.at[mine], a_hbm.at[mine], sems.at[0, index]).wait()
        pltpu.make_async_copy(base_ref.at[index], base_hbm.at[index], sems.at[1, index]).wait()


def weights_kernel(
    layout, base_hbm, upper_tiles_ref, top_ref, slot_ref, light_ref, w_ref, coef_ref, pack_ref, masked, low_hot, base_ref, sems
):
    blocks, rows = layout.blocks, layout.rows
    width = light_ref.shape[1]
    pack_ref[...] = top_ref[...]
    for index in range(blocks):
        pltpu.make_async_copy(base_hbm.at[index], base_ref.at[index], sems.at[index]).start()

    def keep(node, coef):
        coef_ref[:, aligned(node * SK, SK, SK)] = stack_two(coef)
        pack_ref[LANES - width :, :] = coef

    def block(index, carry):
        low_part, high_part = parts_of(slot_ref[pl.ds(index, 1), :])
        low_by_column(low_hot, low_part.astype(f32))
        light = [light_ref[layout.message(g), :, layout.lanes(index)] for g in range(layout.count)]
        light = lanes_of(light)
        for h in range(rows // LOW):
            masked[h * width : (h + 1) * width, :] = jnp.where(high_part == h, light, 0.0).astype(bf16)
        placed = nn(masked[...], low_hot[...])
        parts = [placed[h * width : (h + 1) * width] for h in range(rows // LOW)]
        own = jnp.concatenate(parts, 1).astype(bf16)
        w_ref[:, aligned(index * rows, rows, rows)] = own
        pltpu.make_async_copy(base_hbm.at[index], base_ref.at[index], sems.at[index]).wait()
        keep(index, nn(own, base_ref[index]))
        return carry

    lax.fori_loop(0, blocks, block, 0)
    start, count = 0, blocks
    while count > 1:
        for j in range(count // 2):
            pair = slice((start + 2 * j) * SK, (start + 2 * j + 2) * SK)
            here = start + count + j
            high, low = two(upper_tiles_ref[here - blocks])
            coef = nn(coef_ref[:, pair], high)
            keep(here, coef[:width] + coef[width:] + nn(coef_ref[0:width, pair], low))
        start, count = start + count, count // 2


def near_kernel(count_ref, list_ref, a_hbm, tree_ref, w_ref, acc, times, tiles, a_ref, bt_ref, sem):
    every = count_ref.shape[1]
    copy = pltpu.make_async_copy(a_hbm, a_ref, sem)
    copy.start()
    for leaf in range(every):
        here = slice(leaf * LEAF, (leaf + 1) * LEAF)
        feature_columns(bt_ref, here, tree_ref[:, here])

    def tally(leaf, filled):
        for other in range(every):
            times[other] = (leaf == other).astype(jnp.int32)

        def add(slot, carry):
            at = list_ref[leaf, slot]
            times[at] = times[at] + 1
            return carry

        lax.fori_loop(0, count_ref[0, leaf], add, 0)
        for other in range(every):
            tiles[0, filled] = leaf
            tiles[1, filled] = other
            tiles[2, filled] = times[other]
            filled = filled + (times[other] > 0).astype(jnp.int32)
        return filled

    filled = lax.fori_loop(0, every, tally, jnp.int32(0))
    tiles[0, filled] = 0
    tiles[1, filled] = 0
    tiles[2, filled] = 0
    half = LEAF // 2
    acc[...] = jnp.zeros_like(acc)

    def target(tile, part):
        return aligned(tiles[0, tile] * LEAF + part * half, half, half)

    def exponents(tile, part):
        source = aligned(tiles[1, tile] * LEAF, LEAF, LEAF)
        return nn(a_ref[source, :], bt_ref[:, target(tile, part)])

    def add(tile, part, block):
        source = aligned(tiles[1, tile] * LEAF, LEAF, LEAF)
        acc[:, target(tile, part)] += tiles[2, tile].astype(f32) * nn(w_ref[:, source], block)

    copy.wait()

    def step(pair, carry):
        for tile in (2 * pair, 2 * pair + 1):
            for part in range(2):
                add(tile, part, jnp.exp(exponents(tile, part)).astype(bf16))
        return carry

    lax.fori_loop(0, (filled + 1) // 2, step, 0)


def far_kernel(layout, low_levels, pack_ref, slot_ref, info_ref, tree_ref, sk_ref, coef_ref, near_ref, *refs):
    out_refs, (tops, coefs, low_hot, bt_ref) = refs[: layout.count], refs[layout.count :]
    blocks, rows = layout.blocks, layout.rows
    ups, width = pack_ref.shape[0], out_refs[0].shape[0]
    levels = low_levels + ups
    lane = iota((1, SK), 1)
    for up in range(ups):
        pack = pack_ref[up]
        high, low = two(pack[0:64])
        sub = iota((8, SK), 0)
        extra = jnp.where(sub == 0, pack[67:68], jnp.where(sub == 1, pack[68:69], pack[69:70]))
        extra = jnp.where(sub < 3, extra, jnp.where(sub < 6, 1.0, 0.0))
        at = slice((low_levels + up) * SK, (low_levels + up + 1) * SK)
        tops[at, 0:128], tops[at, 128:256] = feature_rows(high.astype(f32), low.astype(f32), extra)
        coefs[:, at] = stack_two(pack[LANES - width :])

    def block(index, carry):
        node, start, count = index, 0, blocks
        for level in range(low_levels):
            at = slice(level * SK, (level + 1) * SK)
            other = aligned((start + (node ^ 1)) * SK, SK, SK)
            tops[at, :] = sk_ref[other, :]
            coefs[:, at] = coef_ref[:, other]
            node, start, count = node // 2, start + count, count // 2
        low_part, high_part = parts_of(slot_ref[pl.ds(index, 1), :])
        for c in range(rows // LANES):
            at = slice(c * LANES, (c + 1) * LANES)
            low_hot[:, at] = onehot(iota((LOW, LANES), 0) == low_part[:, at])
        info = info_ref[index]
        totals = []
        for leaf in range(rows // LEAF):
            flags = info[FLAGS + leaf : FLAGS + leaf + 1]
            used = []
            for level in range(levels):
                flag = jnp.sum(jnp.where(lane == level, flags, 0.0), axis=1, keepdims=True)
                used.append(jnp.broadcast_to(flag, (1, SK)))
            here = aligned(index * rows + leaf * LEAF, LEAF, LEAF)
            feature_columns(bt_ref, slice(0, LEAF), tree_ref[:, here])
            tile = jnp.exp(nn(tops[...], bt_ref[...])).astype(bf16)
            scaled = (coefs[...].astype(f32) * jnp.concatenate(used, 1)).astype(bf16)
            far = nn(scaled, tile)
            totals.append(near_ref[:, here] + far[:width] + far[width:])
        both = stack_two(jnp.concatenate(totals, 1))
        parts = [both[:, h * LOW : (h + 1) * LOW] for h in range(rows // LOW)]
        moved = nn(jnp.concatenate(parts, 0), low_hot[...])
        result = jnp.zeros((2 * width, rows), f32)
        for h in range(rows // LOW):
            result = jnp.where(high_part == h, moved[h * 2 * width : (h + 1) * 2 * width], result)
        result = result[:width] + result[width:]
        for g, out_ref in enumerate(out_refs):
            out_ref[:, layout.lanes(index)] = result[:, g * layout.per : (g + 1) * layout.per]
        return carry

    lax.fori_loop(0, blocks, block, 0)


def final_kernel(blocks, pos_ref, *refs):
    back_refs, (weights_ref, out_ref, perm, vals) = refs[:-4], refs[-4:]
    chunks = pos_ref.shape[0]
    rows = chunks * LANES
    width, split = back_refs[0].shape
    for r in range(chunks):
        spread(perm, slice(r * LANES, (r + 1) * LANES), column(pos_ref[r : r + 1, :]))
    for g, back_ref in enumerate(back_refs):
        high, low = two(back_ref[...])
        columns, at = 0, slice(0, rows)
        if blocks:
            columns = (lax.axis_index("sub") ^ (g % blocks)) * width
            at = aligned((lax.axis_index("leaf") ^ lax.axis_index("rep") ^ (g // blocks)) * split, split, split)
        vals[aligned(columns, width, width), at] = high
        vals[aligned(columns + LANES, width, width), at] = low
    step = 256
    for s in range(rows // step):
        here = slice(s * step, (s + 1) * step)
        moved = nt(perm[here, :], vals[...])
        out_ref[here, :] = ridge * weights_ref[here, :] + moved[:, :LANES] + moved[:, LANES:]


def upper_levels(pack, skeleton_upper, my_leaf, trees, blocks, width):
    devices = trees * blocks
    level = blocks.bit_length() - 1
    offset = sum(devices >> step for step in range(1, level + 1))
    line = jnp.arange(LANES)[:, None]
    is_point, is_norm = line < DIM, (line >= DIM + 3) & (line < DIM + 6)
    is_coef = line >= LANES - width
    packs, own, stride = [], pack, 1
    while stride < trees:
        other = lax.ppermute(own, "leaf", [(i, i ^ stride) for i in range(trees)])
        packs.append(other)
        stride *= 2
        if stride < trees:
            second = (my_leaf // (stride // 2)) % 2 == 1
            pair = jnp.where(second, jnp.concatenate([other, own], 1), jnp.concatenate([own, other], 1))
            chosen = pair[:, skeleton_upper[offset + my_leaf // stride]]
            level += 1
            offset += devices >> level
            norms = jnp.sum(jnp.where(is_norm, pair, 0.0), axis=0)
            chosen_norms = jnp.sum(jnp.where(is_norm, chosen, 0.0), axis=0)
            inner = jnp.dot(
                jnp.where(is_point, pair, 0.0).T, jnp.where(is_point, chosen, 0.0), precision=highest
            )
            tile = jnp.exp(inner + norms[:, None] + chosen_norms[None])
            own = jnp.where(is_coef, jnp.dot(pair, tile, precision=highest), chosen)
    return jnp.stack(packs)


def body(points, weights, tree_slot, near_count, near_list, skeleton_base, skeleton_upper, far_use):
    blocks, trees, reps = lax.axis_size("sub"), lax.axis_size("leaf"), lax.axis_size("rep")
    devices = blocks * trees
    rows, columns = weights.shape
    low_levels = blocks.bit_length() - 1
    ups = trees.bit_length() - 1
    width = columns // blocks
    part = rows // trees
    per = part // blocks
    total = blocks * rows
    leaves = total // LEAF
    my_leaf = lax.axis_index("leaf")
    fine = trees == 2 and reps == 2 and per % LANES == 0
    layout = Layout(blocks, trees, rows, fine)
    split = part if fine else rows
    arrive = shaped((width, part), f32) if fine else shaped((width, total), f32)

    place, pos, light = pl.pallas_call(
        functools.partial(sort_kernel, fine),
        out_shape=(
            shaped((PLACE_ROWS, split), f32),
            shaped((rows // LANES, LANES), f32),
            shaped((rows // split, columns, split), f32),
        ),
        in_specs=[spec()] * 5,
        out_specs=(spec(),) * 3,
        scratch_shapes=[
            vm((rows, rows), bf16),
            vm((272, rows), bf16),
            vm((rows // split, PLACE_ROWS, split), f32),
        ],
        compiler_params=params(),
        name="sort_rows",
    )(tree_slot.reshape(rows // LANES, LANES), points.T, weights, skeleton_base, far_use)

    axes = ("leaf", "sub", "rep")

    def swap(value, step, other=0):
        pairs = []
        for leaf in range(trees):
            for sub in range(blocks):
                for core in range(reps):
                    to = ((leaf ^ core ^ other) * blocks + (sub ^ step)) * reps + core
                    pairs.append(((leaf * blocks + sub) * reps + core, to))
        return lax.ppermute(value, axes, pairs)

    def swap_all(values):
        done = {}
        for g in sorted(range(len(values)), key=lambda g: -(g % blocks)):
            done[g] = swap(values[g], g % blocks, g // blocks)
        return [done[g] for g in range(len(values))]

    if fine:
        sent, far_off = place, blocks // 2
        place = {far_off: swap(sent, far_off)}
        step = 1
        while step < far_off:
            place[step] = swap(sent, step)
            step *= 2
        place[0] = swap(sent, 0)
        for step in range(1, blocks):
            if step not in place:
                last = step & -step
                place[step] = lax.ppermute(place[step ^ last], "sub", [(i, i ^ last) for i in range(blocks)])
        place[1], tied, light = lax.optimization_barrier((place[1], place[far_off], light))
        place = [place[step] for step in range(blocks)]
        place = place + [lax.ppermute(one, "rep", [(0, 1), (1, 0)]) for one in place]
        light = light.reshape(devices, width, part)
        light = lax.all_to_all(light, ("leaf", "sub"), split_axis=0, concat_axis=0, tiled=True)
        small = []
    else:
        info = jnp.pad(far_use.astype(f32), ((FLAGS, 5 - far_use.shape[0]), (0, SK - far_use.shape[1])))
        small = [lax.all_gather(info.at[BASE].set(skeleton_base[0].astype(f32)), "sub", axis=0, tiled=False)]
        place = place.reshape(PLACE_ROWS, trees, part).transpose(1, 0, 2)
        place = lax.all_to_all(place, "leaf", split_axis=0, concat_axis=0, tiled=True)
        place = lax.all_gather(place, "sub", axis=0, tiled=False)
        place = place.transpose(1, 0, 2, 3).reshape(devices, PLACE_ROWS, blocks, per)
        place = [place.transpose(1, 2, 0, 3).reshape(PLACE_ROWS, total)]
        light = light.reshape(columns, trees, part).transpose(1, 0, 2).reshape(devices, width, part)
        light = lax.all_to_all(light, ("leaf", "sub"), split_axis=0, concat_axis=0, tiled=True)
        light = light.reshape(devices, width, blocks, per)
        light = light.transpose(1, 2, 0, 3).reshape(1, width, total)

    nodes = 2 * blocks - 1
    tree, feat_a, base, sk, upper_tiles, top, slots, info = pl.pallas_call(
        functools.partial(points_kernel, layout, trees),
        out_shape=(
            vm((COORD, total), bf16),
            pltpu.MemorySpace.HBM((total, FEAT), bf16),
            pltpu.MemorySpace.HBM((blocks, rows, SK), bf16),
            vm((nodes * SK, FEAT), bf16),
            vm((blocks - 1, 2 * SK, SK), f32),
            vm((SK, LANES), f32),
            vm((blocks, rows), f32),
            vm((blocks, 8, SK), f32),
        ),
        in_specs=[spec()] * (1 + len(small) + layout.count),
        out_specs=(spec(), spec(pl.ANY), spec(pl.ANY)) + (spec(),) * 5,
        scratch_shapes=[
            vm((rows // LOW * COORD, rows), bf16),
            vm((rows, LOW), bf16),
            vm((total, FEAT), bf16),
            vm((blocks, rows, SK), bf16),
            vm((COORD, nodes * SK), bf16),
            vm((FEAT, SK), bf16),
            pltpu.SemaphoreType.DMA((2, blocks)),
        ],
        compiler_params=params(40),
        name="tree_points",
    )(in_hbm(skeleton_upper), *small, *place)

    tree_light, coefs, pack = pl.pallas_call(
        functools.partial(weights_kernel, layout),
        out_shape=(
            vm((width, total), bf16),
            vm((2 * width, nodes * SK), bf16),
            shaped((LANES, SK), f32),
        ),
        in_specs=[spec(pl.ANY)] + [spec()] * 4,
        out_specs=(spec(),) * 3,
        scratch_shapes=[
            vm((rows // LOW * width, rows), bf16),
            vm((rows, LOW), bf16),
            vm((blocks, rows, SK), bf16),
            pltpu.SemaphoreType.DMA((blocks,)),
        ],
        compiler_params=params(40),
        name="tree_weights",
    )(in_hbm(base), held(upper_tiles), held(top), held(slots), light)

    packs = upper_levels(pack, skeleton_upper, my_leaf, trees, blocks, width)

    near = pl.pallas_call(
        near_kernel,
        out_shape=vm((width, total), f32),
        in_specs=[spec(SMEM)] * 2 + [spec(pl.ANY)] + [spec()] * 2,
        out_specs=spec(),
        scratch_shapes=[
            pltpu.SMEM((leaves,), jnp.int32),
            pltpu.SMEM((3, leaves * leaves + 1), jnp.int32),
            vm((total, FEAT), bf16),
            vm((FEAT, total), bf16),
            pltpu.SemaphoreType.DMA(()),
        ],
        compiler_params=params(40),
        name="near",
    )(in_hbm(near_count), in_hbm(near_list[0]), in_hbm(feat_a), held(tree), held(tree_light))

    levels = low_levels + ups
    back = pl.pallas_call(
        functools.partial(far_kernel, layout, low_levels),
        out_shape=(arrive,) * layout.count,
        in_specs=[spec()] * 7,
        out_specs=(spec(),) * layout.count,
        scratch_shapes=[vm((levels * SK, FEAT), bf16), vm((2 * width, levels * SK), bf16), vm((LOW, rows), bf16), vm((FEAT, LEAF), bf16)],
        compiler_params=params(40),
        name="far",
    )(packs, *[held(one) for one in (slots, info, tree, sk, coefs, near)])

    if fine:
        back = swap_all(back)
    else:
        back = back[0].reshape(width, blocks, devices, per).transpose(2, 0, 1, 3).reshape(devices, width, part)
        back = lax.all_to_all(back, ("leaf", "sub"), split_axis=0, concat_axis=0, tiled=True)
        back = [back.reshape(trees, columns, part).transpose(1, 0, 2).reshape(columns, rows)]

    return pl.pallas_call(
        functools.partial(final_kernel, blocks if fine else 0),
        out_shape=shaped((rows, columns), f32),
        in_specs=[spec()] * (2 + layout.count),
        out_specs=spec(),
        scratch_shapes=[vm((rows, rows), bf16), vm((2 * LANES, rows), bf16)],
        compiler_params=params(40),
        name="to_input_order",
    )(pos, *back, weights)


def solution(mesh):
    in_specs = (
        P(("groups", "leaf", "sub"), None),
        P(("groups", "leaf", "sub"), "rep"),
        P(("groups", "leaf", "sub")),
        P(("groups", "leaf"), None),
        P(("groups", "leaf"), None, None),
        P(("groups", "leaf", "sub"), None),
        P("groups", None),
        P(("groups", "leaf", "sub"), None),
    )
    out_specs = P(("groups", "leaf", "sub"), "rep")
    return jax.shard_map(body, mesh=mesh, in_specs=in_specs, out_specs=out_specs, check_vma=False)
```

```python
import functools

import jax
import jax.numpy as jnp
from jax import lax
from jax.experimental import pallas as pl
from jax.experimental.pallas import tpu as pltpu
from jax.sharding import PartitionSpec as P

DIM = 64
LEAF = 512
SK = 128
LANES = 128
FEAT = 256
LOW = 256
COORD = 144

highest = lax.Precision.HIGHEST
point_scale = 0.25
ridge = 0.5
PLACE_ROWS = 72
TAIL = 64
SLOT, NORM, BASE, FLAGS = 0, 1, 2, 3
f32 = jnp.float32
bf16 = jnp.bfloat16
VMEM = pltpu.MemorySpace.VMEM
SMEM = pltpu.MemorySpace.SMEM


def spec(space=VMEM):
    return pl.BlockSpec(memory_space=space)


def params(mib=58):
    return pltpu.CompilerParams(vmem_limit_bytes=mib * 1024 * 1024)


def in_hbm(array):
    return pltpu.with_memory_space_constraint(array, pltpu.MemorySpace.HBM)


def held(array):
    return pltpu.with_memory_space_constraint(array, VMEM)


def vm(shape, dtype):
    return pltpu.VMEM(shape, dtype)


def shaped(shape, dtype):
    return jax.ShapeDtypeStruct(shape, dtype)


def nt(left, right):
    return lax.dot_general(left, right, (((1,), (1,)), ((), ())), preferred_element_type=f32)


def nn(left, right):
    return jnp.dot(left, right, preferred_element_type=f32)


def column(row):
    return jnp.transpose(jnp.broadcast_to(row, (LANES, LANES)))


def iota(shape, dim):
    return lax.broadcasted_iota(jnp.int32, shape, dim)


def onehot(mask):
    return jnp.where(mask, 1.0, 0.0).astype(bf16)


def two(value):
    high = value.astype(bf16)
    return high, (value - high.astype(f32)).astype(bf16)


def three(value):
    high = value.astype(bf16).astype(f32)
    mid = (value - high).astype(bf16).astype(f32)
    return high, mid, (value - high - mid).astype(bf16).astype(f32)


def lanes_of(blocks):
    return blocks[0] if len(blocks) == 1 else jnp.concatenate(blocks, 1)


def aligned(start, size, unit):
    return pl.ds(pl.multiple_of(start, unit), size)


def stack_two(value):
    high, low = two(value)
    return jnp.concatenate([high, low], 0)


def spread(perm, here, rank):
    lane = iota((LANES, LANES), 1).astype(f32)
    for c in range(perm.shape[1] // LANES):
        perm[here, c * LANES : (c + 1) * LANES] = onehot(lane + float(c * LANES) == rank)


def sort_kernel(
    fine, slot_ref, points_ref, weights_ref, base_ref, flag_ref, place_ref, pos_ref, light_ref, perm, vals, whole
):
    chunks, split = slot_ref.shape[0], light_ref.shape[-1]
    rows = chunks * LANES
    slots = slot_ref[...]
    slot = slots.astype(f32)
    within = slots & (rows - 1)
    high, low = (within >> 5).astype(f32), (within & 31).astype(f32)
    for r in range(chunks):
        here = slice(r * LANES, (r + 1) * LANES)
        mine = column(slot[r : r + 1])
        before = jnp.zeros((LANES, LANES), f32)
        for c in range(chunks):
            before += jnp.where(slot[c : c + 1] < mine, 1.0, 0.0)
        rank = jnp.broadcast_to(jnp.sum(before, axis=1, keepdims=True), (LANES, LANES))
        pos_ref[r : r + 1, :] = jnp.transpose(rank)[0:1]
        spread(perm, here, rank)
        vals[0:LANES, here] = jnp.transpose(weights_ref[here, :]).astype(bf16)
    scaled = points_ref[...] * point_scale
    ph, plo = two(scaled)
    nh, nm, nl = three(-0.5 * jnp.sum(scaled * scaled, axis=0, keepdims=True))
    vals[128:192, :] = ph
    vals[192:256, :] = plo
    sub = iota((16, LANES), 0)
    for c in range(chunks):
        at = slice(c * LANES, (c + 1) * LANES)
        extra = jnp.where(sub == 0, high[c : c + 1], jnp.where(sub == 1, low[c : c + 1], 0.0))
        extra = jnp.where(sub == 2, nh[:, at], jnp.where(sub == 3, nm[:, at], extra))
        vals[256:272, at] = jnp.where(sub == 4, nl[:, at], extra).astype(bf16)
    step = 256
    for s in range(rows // step):
        moved = nn(vals[...], perm[:, s * step : (s + 1) * step])
        at = slice((s * step) % split, (s * step) % split + step)
        part = (s * step) // split
        light_ref[part, :, at] = moved[0:LANES]
        whole[part, 0:TAIL, at] = moved[128:192] + moved[192:256]
        tail = iota((8, step), 0)
        slot_row = moved[256:257] * 32.0 + moved[257:258]
        norm_row = moved[258:259] + moved[259:260] + moved[260:261]
        whole[part, TAIL:, at] = jnp.where(tail == SLOT, slot_row, jnp.where(tail == NORM, norm_row, 0.0))
    if not fine:
        place_ref[...] = whole[0]
        return
    place_ref[...] = whole[lax.axis_index("leaf") ^ lax.axis_index("rep")]
    place_ref[TAIL + BASE : TAIL + BASE + 1, 0:SK] = base_ref[...].astype(f32)
    place_ref[TAIL + FLAGS : TAIL + FLAGS + flag_ref.shape[0], 0 : flag_ref.shape[1]] = flag_ref[...].astype(f32)


class Layout:
    def __init__(self, blocks, trees, rows, fine):
        self.blocks, self.rows, self.fine = blocks, rows, fine
        self.count = blocks * trees if fine else 1
        self.per = rows // self.count

    def lanes(self, index):
        return aligned(index * self.per, self.per, LANES)

    def message(self, group):
        if not self.fine:
            return 0
        leaf = lax.axis_index("leaf") ^ lax.axis_index("rep") ^ (group // self.blocks)
        return leaf * self.blocks + (lax.axis_index("sub") ^ (group % self.blocks))

    def gather(self, refs, index, part):
        return lanes_of([ref[part, self.lanes(index)] for ref in refs])

    def info(self, refs, small_ref, index):
        if not self.fine:
            return small_ref[index]
        core = lax.axis_index("rep")
        found = jnp.zeros((PLACE_ROWS - TAIL, SK), f32)
        for step in range(self.blocks):
            mine, theirs = refs[step][TAIL:, 0:SK], refs[self.blocks + step][TAIL:, 0:SK]
            here = jnp.where(core == 0, mine, theirs)
            found = jnp.where((lax.axis_index("sub") ^ step) == index, here, found)
        return found


def low_by_column(out, low):
    for c in range(out.shape[0] // LANES):
        at = slice(c * LANES, (c + 1) * LANES)
        spread(out, at, column(low[:, at]))


def parts_of(slots):
    slots = slots.astype(jnp.int32)
    return slots & (LOW - 1), slots // LOW


def feature_columns(out, at, tree):
    out[0:64, at] = tree[0:64].astype(bf16)
    out[64:128, at] = tree[0:64].astype(bf16)
    out[128:192, at] = tree[64:128].astype(bf16)
    out[192:208, at] = jnp.where(iota((16, tree.shape[1]), 0) < 8, tree[128:144].astype(f32), 0.0).astype(bf16)
    out[208:256, at] = jnp.zeros((48, tree.shape[1]), bf16)


def feature_rows(high, low, extra):
    first = jnp.transpose(jnp.concatenate([high, low], 0))
    second = jnp.transpose(jnp.concatenate([high, extra, jnp.zeros((56, high.shape[1]), f32)], 0))
    return first.astype(bf16), second.astype(bf16)


def points_kernel(layout, trees, upper_ref, *refs):
    if not layout.fine:
        small_ref, refs = refs[0], refs[1:]
    else:
        small_ref = None
    place_refs, refs = refs[: layout.count], refs[layout.count :]
    tree_ref, a_hbm, base_hbm, sk_ref, upper_tiles_ref, top_ref, slot_ref, info_ref = refs[:8]
    masked, low_hot, a_ref, base_ref, sk_t, sk_bt, sems = refs[8:]
    blocks, rows = layout.blocks, layout.rows

    def keep(node, found):
        at = aligned(node * SK, SK, SK)
        sk_t[:, at] = found.astype(bf16)
        sk_ref[at, 0:128], sk_ref[at, 128:256] = feature_rows(found[0:64], found[64:128], found[136:144])
        feature_columns(sk_bt, slice(0, SK), found)

    def block(index, carry):
        tail = layout.gather(place_refs, index, slice(TAIL, PLACE_ROWS))
        slots = tail[SLOT : SLOT + 1]
        slot_ref[pl.ds(index, 1), :] = slots
        info = layout.info(place_refs, small_ref, index)
        info_ref[index] = info
        points = layout.gather(place_refs, index, slice(0, TAIL))
        high, low = two(points)
        nh, nm, nl = three(tail[NORM : NORM + 1])
        sub = iota((16, rows), 0)
        norms = jnp.where((sub == 3) | (sub == 8), nh, jnp.where((sub == 4) | (sub == 9), nm, nl))
        is_norm = ((sub >= 3) & (sub < 6)) | ((sub >= 8) & (sub < 11))
        is_one = (sub < 3) | ((sub >= 11) & (sub < 14))
        extra = jnp.where(is_norm, norms, jnp.where(is_one, 1.0, 0.0))
        low_part, high_part = parts_of(slots)
        low_by_column(low_hot, low_part.astype(f32))
        for h in range(rows // LOW):
            here = high_part == h
            masked[h * COORD : h * COORD + 64, :] = jnp.where(here, high.astype(f32), 0.0).astype(bf16)
            masked[h * COORD + 64 : h * COORD + 128, :] = jnp.where(here, low.astype(f32), 0.0).astype(bf16)
            masked[h * COORD + 128 : (h + 1) * COORD, :] = jnp.where(here, extra, 0.0).astype(bf16)
        placed = nn(masked[...], low_hot[...])
        for h in range(rows // LOW):
            part = placed[h * COORD : (h + 1) * COORD]
            at = aligned(index * rows + h * LOW, LOW, LOW)
            tree_ref[:, at] = part.astype(bf16)
            a_ref[at, 0:128], a_ref[at, 128:256] = feature_rows(part[0:64], part[64:128], part[136:144])
        picked = onehot(iota((rows, SK), 0) == info[BASE : BASE + 1].astype(jnp.int32))
        mine = aligned(index * rows, rows, rows)
        pltpu.make_async_copy(a_ref.at[mine], a_hbm.at[mine], sems.at[0, index]).start()
        keep(index, nn(tree_ref[:, mine], picked))
        base_ref[index] = jnp.exp(nn(a_ref[mine, :], sk_bt[...])).astype(bf16)
        pltpu.make_async_copy(base_ref.at[index], base_hbm.at[index], sems.at[1, index]).start()
        return carry

    lax.fori_loop(0, blocks, block, 0)
    start, count, offset, total = 0, blocks, 0, blocks * trees
    while count > 1:
        nodes = count // 2
        for j in range(nodes):
            pair = slice((start + 2 * j) * SK, (start + 2 * j + 2) * SK)
            row = offset + lax.axis_index("leaf") * nodes + j
            picked = onehot(iota((2 * SK, SK), 0) == upper_ref[pl.ds(row, 1), :])
            here = start + count + j
            keep(here, nn(sk_t[:, pair], picked))
            upper_tiles_ref[here - blocks] = jnp.exp(nn(sk_ref[pair, :], sk_bt[...]))
        total = total // 2
        offset = offset + total
        start, count = start + count, nodes
    found = sk_t[:, start * SK : (start + 1) * SK].astype(f32)
    top_ref[0:64, :] = found[0:64] + found[64:128]
    top_ref[64:72, :] = found[128:136]
    top_ref[72:128, :] = jnp.zeros((56, SK), f32)
    for index in range(blocks):
        mine = slice(index * rows, (index + 1) * rows)
        pltpu.make_async_copy(a_ref.at[mine], a_hbm.at[mine], sems.at[0, index]).wait()
        pltpu.make_async_copy(base_ref.at[index], base_hbm.at[index], sems.at[1, index]).wait()


def weights_kernel(
    layout, base_hbm, upper_tiles_ref, top_ref, slot_ref, light_ref, w_ref, coef_ref, pack_ref, masked, low_hot, base_ref, sems
):
    blocks, rows = layout.blocks, layout.rows
    width = light_ref.shape[1]
    pack_ref[...] = top_ref[...]
    for index in range(blocks):
        pltpu.make_async_copy(base_hbm.at[index], base_ref.at[index], sems.at[index]).start()

    def keep(node, coef):
        coef_ref[:, aligned(node * SK, SK, SK)] = stack_two(coef)
        pack_ref[LANES - width :, :] = coef

    def block(index, carry):
        low_part, high_part = parts_of(slot_ref[pl.ds(index, 1), :])
        low_by_column(low_hot, low_part.astype(f32))
        light = [light_ref[layout.message(g), :, layout.lanes(index)] for g in range(layout.count)]
        light = lanes_of(light)
        for h in range(rows // LOW):
            masked[h * width : (h + 1) * width, :] = jnp.where(high_part == h, light, 0.0).astype(bf16)
        placed = nn(masked[...], low_hot[...])
        parts = [placed[h * width : (h + 1) * width] for h in range(rows // LOW)]
        own = jnp.concatenate(parts, 1).astype(bf16)
        w_ref[:, aligned(index * rows, rows, rows)] = own
        pltpu.make_async_copy(base_hbm.at[index], base_ref.at[index], sems.at[index]).wait()
        keep(index, nn(own, base_ref[index]))
        return carry

    lax.fori_loop(0, blocks, block, 0)
    start, count = 0, blocks
    while count > 1:
        for j in range(count // 2):
            pair = slice((start + 2 * j) * SK, (start + 2 * j + 2) * SK)
            here = start + count + j
            high, low = two(upper_tiles_ref[here - blocks])
            coef = nn(coef_ref[:, pair], high)
            keep(here, coef[:width] + coef[width:] + nn(coef_ref[0:width, pair], low))
        start, count = start + count, count // 2


def near_kernel(count_ref, list_ref, a_hbm, tree_ref, w_ref, acc, times, tiles, a_ref, bt_ref, sem, *halves):
    every = count_ref.shape[1]
    copy = pltpu.make_async_copy(a_hbm, a_ref, sem)
    copy.start()
    for leaf in range(every):
        here = slice(leaf * LEAF, (leaf + 1) * LEAF)
        feature_columns(bt_ref, here, tree_ref[:, here])

    def tally(leaf, filled):
        for other in range(every):
            times[other] = (leaf == other).astype(jnp.int32)

        def add(slot, carry):
            at = list_ref[leaf, slot]
            times[at] = times[at] + 1
            return carry

        lax.fori_loop(0, count_ref[0, leaf], add, 0)
        for other in range(every):
            tiles[0, filled] = leaf
            tiles[1, filled] = other
            tiles[2, filled] = times[other]
            filled = filled + (times[other] > 0).astype(jnp.int32)
        return filled

    filled = lax.fori_loop(0, every, tally, jnp.int32(0))
    for more in range(2):
        tiles[0, filled + more] = 0
        tiles[1, filled + more] = 0
    half = LEAF // 2
    acc[...] = jnp.zeros_like(acc)

    def target(tile, part):
        return aligned(tiles[0, tile] * LEAF + part * half, half, half)

    even, odd = halves[0:2], halves[2:4]
    even_tile, odd_tile = halves[4:6], halves[6:8]

    def exponents(tile, part):
        source = aligned(tiles[1, tile] * LEAF, LEAF, LEAF)
        return nn(a_ref[source, :], bt_ref[:, target(tile, part)])

    def add(tile, part, block):
        source = aligned(tiles[1, tile] * LEAF, LEAF, LEAF)
        acc[:, target(tile, part)] += tiles[2, tile].astype(f32) * nn(w_ref[:, source], block[part][...])

    def phase(tile, upcoming, ready, made, previous):
        for part in range(2):
            upcoming[part][...] = exponents(tile + 1, part)
            made[part][...] = jnp.exp(ready[part][...]).astype(bf16)
            add(tile - 1, part, previous)

    copy.wait()
    for part in range(2):
        even[part][...] = exponents(0, part)
        even_tile[part][...] = jnp.exp(even[part][...]).astype(bf16)
        odd[part][...] = exponents(1, part)

    def step(pair, carry):
        phase(2 * pair + 1, even, odd, odd_tile, even_tile)
        phase(2 * pair + 2, odd, even, even_tile, odd_tile)
        return carry

    lax.fori_loop(0, (filled - 1) // 2, step, 0)
    done = 2 * ((filled - 1) // 2)
    for part in range(2):
        add(done, part, even_tile)

    @pl.when(done + 1 < filled)
    def _():
        for part in range(2):
            odd_tile[part][...] = jnp.exp(odd[part][...]).astype(bf16)
            add(done + 1, part, odd_tile)


def far_kernel(layout, low_levels, pack_ref, slot_ref, info_ref, tree_ref, sk_ref, coef_ref, near_ref, *refs):
    out_refs, (tops, coefs, low_hot, bt_ref) = refs[: layout.count], refs[layout.count :]
    blocks, rows = layout.blocks, layout.rows
    ups, width = pack_ref.shape[0], out_refs[0].shape[0]
    levels = low_levels + ups
    lane = iota((1, SK), 1)
    for up in range(ups):
        pack = pack_ref[up]
        high, low = two(pack[0:64])
        sub = iota((8, SK), 0)
        extra = jnp.where(sub == 0, pack[67:68], jnp.where(sub == 1, pack[68:69], pack[69:70]))
        extra = jnp.where(sub < 3, extra, jnp.where(sub < 6, 1.0, 0.0))
        at = slice((low_levels + up) * SK, (low_levels + up + 1) * SK)
        tops[at, 0:128], tops[at, 128:256] = feature_rows(high.astype(f32), low.astype(f32), extra)
        coefs[:, at] = stack_two(pack[LANES - width :])

    def block(index, carry):
        node, start, count = index, 0, blocks
        for level in range(low_levels):
            at = slice(level * SK, (level + 1) * SK)
            other = aligned((start + (node ^ 1)) * SK, SK, SK)
            tops[at, :] = sk_ref[other, :]
            coefs[:, at] = coef_ref[:, other]
            node, start, count = node // 2, start + count, count // 2
        low_part, high_part = parts_of(slot_ref[pl.ds(index, 1), :])
        for c in range(rows // LANES):
            at = slice(c * LANES, (c + 1) * LANES)
            low_hot[:, at] = onehot(iota((LOW, LANES), 0) == low_part[:, at])
        info = info_ref[index]
        totals = []
        for leaf in range(rows // LEAF):
            flags = info[FLAGS + leaf : FLAGS + leaf + 1]
            used = []
            for level in range(levels):
                flag = jnp.sum(jnp.where(lane == level, flags, 0.0), axis=1, keepdims=True)
                used.append(jnp.broadcast_to(flag, (1, SK)))
            here = aligned(index * rows + leaf * LEAF, LEAF, LEAF)
            feature_columns(bt_ref, slice(0, LEAF), tree_ref[:, here])
            tile = jnp.exp(nn(tops[...], bt_ref[...])).astype(bf16)
            scaled = (coefs[...].astype(f32) * jnp.concatenate(used, 1)).astype(bf16)
            far = nn(scaled, tile)
            totals.append(near_ref[:, here] + far[:width] + far[width:])
        both = stack_two(jnp.concatenate(totals, 1))
        parts = [both[:, h * LOW : (h + 1) * LOW] for h in range(rows // LOW)]
        moved = nn(jnp.concatenate(parts, 0), low_hot[...])
        result = jnp.zeros((2 * width, rows), f32)
        for h in range(rows // LOW):
            result = jnp.where(high_part == h, moved[h * 2 * width : (h + 1) * 2 * width], result)
        result = result[:width] + result[width:]
        for g, out_ref in enumerate(out_refs):
            out_ref[:, layout.lanes(index)] = result[:, g * layout.per : (g + 1) * layout.per]
        return carry

    lax.fori_loop(0, blocks, block, 0)


def final_kernel(blocks, pos_ref, *refs):
    back_refs, (weights_ref, out_ref, perm, vals) = refs[:-4], refs[-4:]
    chunks = pos_ref.shape[0]
    rows = chunks * LANES
    width, split = back_refs[0].shape
    for r in range(chunks):
        spread(perm, slice(r * LANES, (r + 1) * LANES), column(pos_ref[r : r + 1, :]))
    for g, back_ref in enumerate(back_refs):
        high, low = two(back_ref[...])
        columns, at = 0, slice(0, rows)
        if blocks:
            columns = (lax.axis_index("sub") ^ (g % blocks)) * width
            at = aligned((lax.axis_index("leaf") ^ lax.axis_index("rep") ^ (g // blocks)) * split, split, split)
        vals[aligned(columns, width, width), at] = high
        vals[aligned(columns + LANES, width, width), at] = low
    step = 256
    for s in range(rows // step):
        here = slice(s * step, (s + 1) * step)
        moved = nt(perm[here, :], vals[...])
        out_ref[here, :] = ridge * weights_ref[here, :] + moved[:, :LANES] + moved[:, LANES:]


def upper_levels(pack, skeleton_upper, my_leaf, trees, blocks, width):
    devices = trees * blocks
    level = blocks.bit_length() - 1
    offset = sum(devices >> step for step in range(1, level + 1))
    line = jnp.arange(LANES)[:, None]
    is_point, is_norm = line < DIM, (line >= DIM + 3) & (line < DIM + 6)
    is_coef = line >= LANES - width
    packs, own, stride = [], pack, 1
    while stride < trees:
        other = lax.ppermute(own, "leaf", [(i, i ^ stride) for i in range(trees)])
        packs.append(other)
        stride *= 2
        if stride < trees:
            second = (my_leaf // (stride // 2)) % 2 == 1
            pair = jnp.where(second, jnp.concatenate([other, own], 1), jnp.concatenate([own, other], 1))
            chosen = pair[:, skeleton_upper[offset + my_leaf // stride]]
            level += 1
            offset += devices >> level
            norms = jnp.sum(jnp.where(is_norm, pair, 0.0), axis=0)
            chosen_norms = jnp.sum(jnp.where(is_norm, chosen, 0.0), axis=0)
            inner = jnp.dot(
                jnp.where(is_point, pair, 0.0).T, jnp.where(is_point, chosen, 0.0), precision=highest
            )
            tile = jnp.exp(inner + norms[:, None] + chosen_norms[None])
            own = jnp.where(is_coef, jnp.dot(pair, tile, precision=highest), chosen)
    return jnp.stack(packs)


def body(points, weights, tree_slot, near_count, near_list, skeleton_base, skeleton_upper, far_use):
    blocks, trees, reps = lax.axis_size("sub"), lax.axis_size("leaf"), lax.axis_size("rep")
    devices = blocks * trees
    rows, columns = weights.shape
    low_levels = blocks.bit_length() - 1
    ups = trees.bit_length() - 1
    width = columns // blocks
    part = rows // trees
    per = part // blocks
    total = blocks * rows
    leaves = total // LEAF
    my_leaf = lax.axis_index("leaf")
    fine = trees == 2 and reps == 2 and per % LANES == 0
    layout = Layout(blocks, trees, rows, fine)
    split = part if fine else rows
    arrive = shaped((width, part), f32) if fine else shaped((width, total), f32)

    place, pos, light = pl.pallas_call(
        functools.partial(sort_kernel, fine),
        out_shape=(
            shaped((PLACE_ROWS, split), f32),
            shaped((rows // LANES, LANES), f32),
            shaped((rows // split, columns, split), f32),
        ),
        in_specs=[spec()] * 5,
        out_specs=(spec(),) * 3,
        scratch_shapes=[
            vm((rows, rows), bf16),
            vm((272, rows), bf16),
            vm((rows // split, PLACE_ROWS, split), f32),
        ],
        compiler_params=params(),
        name="sort_rows",
    )(tree_slot.reshape(rows // LANES, LANES), points.T, weights, skeleton_base, far_use)

    axes = ("leaf", "sub", "rep")

    def swap(value, step, other=0):
        pairs = []
        for leaf in range(trees):
            for sub in range(blocks):
                for core in range(reps):
                    to = ((leaf ^ core ^ other) * blocks + (sub ^ step)) * reps + core
                    pairs.append(((leaf * blocks + sub) * reps + core, to))
        return lax.ppermute(value, axes, pairs)

    def swap_all(values):
        done = {}
        for g in sorted(range(len(values)), key=lambda g: -(g % blocks)):
            done[g] = swap(values[g], g % blocks, g // blocks)
        return [done[g] for g in range(len(values))]

    if fine:
        place = {0: swap(place, 0)}
        stride = blocks // 2
        while stride:
            for step in sorted(place):
                place[step | stride] = lax.ppermute(place[step], "sub", [(i, i ^ stride) for i in range(blocks)])
            stride //= 2
        theirs = {step: lax.ppermute(one, "rep", [(0, 1), (1, 0)]) for step, one in place.items()}
        theirs[blocks // 2], light = lax.optimization_barrier((theirs[blocks // 2], light))
        place = [place[step] for step in range(blocks)] + [theirs[step] for step in range(blocks)]
        light = light.reshape(devices, width, part)
        light = lax.all_to_all(light, ("leaf", "sub"), split_axis=0, concat_axis=0, tiled=True)
        small = []
    else:
        info = jnp.pad(far_use.astype(f32), ((FLAGS, 5 - far_use.shape[0]), (0, SK - far_use.shape[1])))
        small = [lax.all_gather(info.at[BASE].set(skeleton_base[0].astype(f32)), "sub", axis=0, tiled=False)]
        place = place.reshape(PLACE_ROWS, trees, part).transpose(1, 0, 2)
        place = lax.all_to_all(place, "leaf", split_axis=0, concat_axis=0, tiled=True)
        place = lax.all_gather(place, "sub", axis=0, tiled=False)
        place = place.transpose(1, 0, 2, 3).reshape(devices, PLACE_ROWS, blocks, per)
        place = [place.transpose(1, 2, 0, 3).reshape(PLACE_ROWS, total)]
        light = light.reshape(columns, trees, part).transpose(1, 0, 2).reshape(devices, width, part)
        light = lax.all_to_all(light, ("leaf", "sub"), split_axis=0, concat_axis=0, tiled=True)
        light = light.reshape(devices, width, blocks, per)
        light = light.transpose(1, 2, 0, 3).reshape(1, width, total)

    nodes = 2 * blocks - 1
    tree, feat_a, base, sk, upper_tiles, top, slots, info = pl.pallas_call(
        functools.partial(points_kernel, layout, trees),
        out_shape=(
            vm((COORD, total), bf16),
            pltpu.MemorySpace.HBM((total, FEAT), bf16),
            pltpu.MemorySpace.HBM((blocks, rows, SK), bf16),
            vm((nodes * SK, FEAT), bf16),
            vm((blocks - 1, 2 * SK, SK), f32),
            vm((SK, LANES), f32),
            vm((blocks, rows), f32),
            vm((blocks, 8, SK), f32),
        ),
        in_specs=[spec()] * (1 + len(small) + layout.count),
        out_specs=(spec(), spec(pl.ANY), spec(pl.ANY)) + (spec(),) * 5,
        scratch_shapes=[
            vm((rows // LOW * COORD, rows), bf16),
            vm((rows, LOW), bf16),
            vm((total, FEAT), bf16),
            vm((blocks, rows, SK), bf16),
            vm((COORD, nodes * SK), bf16),
            vm((FEAT, SK), bf16),
            pltpu.SemaphoreType.DMA((2, blocks)),
        ],
        compiler_params=params(40),
        name="tree_points",
    )(in_hbm(skeleton_upper), *small, *place)

    tree_light, coefs, pack = pl.pallas_call(
        functools.partial(weights_kernel, layout),
        out_shape=(
            vm((width, total), bf16),
            vm((2 * width, nodes * SK), bf16),
            shaped((LANES, SK), f32),
        ),
        in_specs=[spec(pl.ANY)] + [spec()] * 4,
        out_specs=(spec(),) * 3,
        scratch_shapes=[
            vm((rows // LOW * width, rows), bf16),
            vm((rows, LOW), bf16),
            vm((blocks, rows, SK), bf16),
            pltpu.SemaphoreType.DMA((blocks,)),
        ],
        compiler_params=params(40),
        name="tree_weights",
    )(in_hbm(base), held(upper_tiles), held(top), held(slots), light)

    packs = upper_levels(pack, skeleton_upper, my_leaf, trees, blocks, width)

    near = pl.pallas_call(
        near_kernel,
        out_shape=vm((width, total), f32),
        in_specs=[spec(SMEM)] * 2 + [spec(pl.ANY)] + [spec()] * 2,
        out_specs=spec(),
        scratch_shapes=[
            pltpu.SMEM((leaves,), jnp.int32),
            pltpu.SMEM((3, leaves * leaves + 2), jnp.int32),
            vm((total, FEAT), bf16),
            vm((FEAT, total), bf16),
            pltpu.SemaphoreType.DMA(()),
        ]
        + [vm((LEAF, LEAF // 2), f32)] * 4
        + [vm((LEAF, LEAF // 2), bf16)] * 4,
        compiler_params=params(40),
        name="near",
    )(in_hbm(near_count), in_hbm(near_list[0]), in_hbm(feat_a), held(tree), held(tree_light))

    levels = low_levels + ups
    back = pl.pallas_call(
        functools.partial(far_kernel, layout, low_levels),
        out_shape=(arrive,) * layout.count,
        in_specs=[spec()] * 7,
        out_specs=(spec(),) * layout.count,
        scratch_shapes=[vm((levels * SK, FEAT), bf16), vm((2 * width, levels * SK), bf16), vm((LOW, rows), bf16), vm((FEAT, LEAF), bf16)],
        compiler_params=params(40),
        name="far",
    )(packs, *[held(one) for one in (slots, info, tree, sk, coefs, near)])

    if fine:
        back = swap_all(back)
    else:
        back = back[0].reshape(width, blocks, devices, per).transpose(2, 0, 1, 3).reshape(devices, width, part)
        back = lax.all_to_all(back, ("leaf", "sub"), split_axis=0, concat_axis=0, tiled=True)
        back = [back.reshape(trees, columns, part).transpose(1, 0, 2).reshape(columns, rows)]

    return pl.pallas_call(
        functools.partial(final_kernel, blocks if fine else 0),
        out_shape=shaped((rows, columns), f32),
        in_specs=[spec()] * (2 + layout.count),
        out_specs=spec(),
        scratch_shapes=[vm((rows, rows), bf16), vm((2 * LANES, rows), bf16)],
        compiler_params=params(40),
        name="to_input_order",
    )(pos, *back, weights)


def solution(mesh):
    in_specs = (
        P(("groups", "leaf", "sub"), None),
        P(("groups", "leaf", "sub"), "rep"),
        P(("groups", "leaf", "sub")),
        P(("groups", "leaf"), None),
        P(("groups", "leaf"), None, None),
        P(("groups", "leaf", "sub"), None),
        P("groups", None),
        P(("groups", "leaf", "sub"), None),
    )
    out_specs = P(("groups", "leaf", "sub"), "rep")
    return jax.shard_map(body, mesh=mesh, in_specs=in_specs, out_specs=out_specs, check_vma=False)
```

```python
import functools

import jax
import jax.numpy as jnp
from jax import lax
from jax.experimental import pallas as pl
from jax.experimental.pallas import tpu as pltpu
from jax.sharding import PartitionSpec as P

DIM = 64
LEAF = 512
SK = 128
LANES = 128
FEAT = 256
LOW = 256
COORD = 144

highest = lax.Precision.HIGHEST
point_scale = 0.25
ridge = 0.5
PLACE_ROWS = 72
TAIL = 64
SLOT, NORM, BASE, FLAGS = 0, 1, 2, 3
f32 = jnp.float32
bf16 = jnp.bfloat16
VMEM = pltpu.MemorySpace.VMEM
SMEM = pltpu.MemorySpace.SMEM


def spec(space=VMEM):
    return pl.BlockSpec(memory_space=space)


def params(mib=58):
    return pltpu.CompilerParams(vmem_limit_bytes=mib * 1024 * 1024)


def in_hbm(array):
    return pltpu.with_memory_space_constraint(array, pltpu.MemorySpace.HBM)


def held(array):
    return pltpu.with_memory_space_constraint(array, VMEM)


def vm(shape, dtype):
    return pltpu.VMEM(shape, dtype)


def shaped(shape, dtype):
    return jax.ShapeDtypeStruct(shape, dtype)


def nt(left, right):
    return lax.dot_general(left, right, (((1,), (1,)), ((), ())), preferred_element_type=f32)


def nn(left, right):
    return jnp.dot(left, right, preferred_element_type=f32)


def column(row):
    return jnp.transpose(jnp.broadcast_to(row, (LANES, LANES)))


def iota(shape, dim):
    return lax.broadcasted_iota(jnp.int32, shape, dim)


def onehot(mask):
    return jnp.where(mask, 1.0, 0.0).astype(bf16)


def two(value):
    high = value.astype(bf16)
    return high, (value - high.astype(f32)).astype(bf16)


def three(value):
    high = value.astype(bf16).astype(f32)
    mid = (value - high).astype(bf16).astype(f32)
    return high, mid, (value - high - mid).astype(bf16).astype(f32)


def lanes_of(blocks):
    return blocks[0] if len(blocks) == 1 else jnp.concatenate(blocks, 1)


def aligned(start, size, unit):
    return pl.ds(pl.multiple_of(start, unit), size)


def stack_two(value):
    high, low = two(value)
    return jnp.concatenate([high, low], 0)


def spread(perm, here, rank):
    lane = iota((LANES, LANES), 1).astype(f32)
    for c in range(perm.shape[1] // LANES):
        perm[here, c * LANES : (c + 1) * LANES] = onehot(lane + float(c * LANES) == rank)


def sort_kernel(
    fine, slot_ref, points_ref, weights_ref, base_ref, flag_ref, place_ref, pos_ref, light_ref, perm, vals, whole
):
    chunks, split = slot_ref.shape[0], light_ref.shape[-1]
    rows = chunks * LANES
    slots = slot_ref[...]
    slot = slots.astype(f32)
    within = slots & (rows - 1)
    high, low = (within >> 5).astype(f32), (within & 31).astype(f32)
    for r in range(chunks):
        here = slice(r * LANES, (r + 1) * LANES)
        mine = column(slot[r : r + 1])
        before = jnp.zeros((LANES, LANES), f32)
        for c in range(chunks):
            before += jnp.where(slot[c : c + 1] < mine, 1.0, 0.0)
        rank = jnp.broadcast_to(jnp.sum(before, axis=1, keepdims=True), (LANES, LANES))
        pos_ref[r : r + 1, :] = jnp.transpose(rank)[0:1]
        spread(perm, here, rank)
        vals[0:LANES, here] = jnp.transpose(weights_ref[here, :]).astype(bf16)
    scaled = points_ref[...] * point_scale
    ph, plo = two(scaled)
    nh, nm, nl = three(-0.5 * jnp.sum(scaled * scaled, axis=0, keepdims=True))
    vals[128:192, :] = ph
    vals[192:256, :] = plo
    sub = iota((16, LANES), 0)
    for c in range(chunks):
        at = slice(c * LANES, (c + 1) * LANES)
        extra = jnp.where(sub == 0, high[c : c + 1], jnp.where(sub == 1, low[c : c + 1], 0.0))
        extra = jnp.where(sub == 2, nh[:, at], jnp.where(sub == 3, nm[:, at], extra))
        vals[256:272, at] = jnp.where(sub == 4, nl[:, at], extra).astype(bf16)
    step = 256
    for s in range(rows // step):
        moved = nn(vals[...], perm[:, s * step : (s + 1) * step])
        at = slice((s * step) % split, (s * step) % split + step)
        part = (s * step) // split
        light_ref[part, :, at] = moved[0:LANES]
        whole[part, 0:TAIL, at] = moved[128:192] + moved[192:256]
        tail = iota((8, step), 0)
        slot_row = moved[256:257] * 32.0 + moved[257:258]
        norm_row = moved[258:259] + moved[259:260] + moved[260:261]
        whole[part, TAIL:, at] = jnp.where(tail == SLOT, slot_row, jnp.where(tail == NORM, norm_row, 0.0))
    if not fine:
        place_ref[...] = whole[0]
        return
    place_ref[...] = whole[lax.axis_index("leaf") ^ lax.axis_index("rep")]
    place_ref[TAIL + BASE : TAIL + BASE + 1, 0:SK] = base_ref[...].astype(f32)
    place_ref[TAIL + FLAGS : TAIL + FLAGS + flag_ref.shape[0], 0 : flag_ref.shape[1]] = flag_ref[...].astype(f32)


class Layout:
    def __init__(self, blocks, trees, rows, fine):
        self.blocks, self.rows, self.fine = blocks, rows, fine
        self.count = blocks * trees if fine else 1
        self.per = rows // self.count

    def lanes(self, index):
        return aligned(index * self.per, self.per, LANES)

    def message(self, group):
        if not self.fine:
            return 0
        leaf = lax.axis_index("leaf") ^ lax.axis_index("rep") ^ (group // self.blocks)
        return leaf * self.blocks + (lax.axis_index("sub") ^ (group % self.blocks))

    def gather(self, refs, index, part):
        return lanes_of([ref[part, self.lanes(index)] for ref in refs])

    def info(self, refs, small_ref, index):
        if not self.fine:
            return small_ref[index]
        core = lax.axis_index("rep")
        found = jnp.zeros((PLACE_ROWS - TAIL, SK), f32)
        for step in range(self.blocks):
            mine, theirs = refs[step][TAIL:, 0:SK], refs[self.blocks + step][TAIL:, 0:SK]
            here = jnp.where(core == 0, mine, theirs)
            found = jnp.where((lax.axis_index("sub") ^ step) == index, here, found)
        return found


def low_by_column(out, low):
    for c in range(out.shape[0] // LANES):
        at = slice(c * LANES, (c + 1) * LANES)
        spread(out, at, column(low[:, at]))


def parts_of(slots):
    slots = slots.astype(jnp.int32)
    return slots & (LOW - 1), slots // LOW


def feature_columns(out, at, tree):
    out[0:64, at] = tree[0:64].astype(bf16)
    out[64:128, at] = tree[0:64].astype(bf16)
    out[128:192, at] = tree[64:128].astype(bf16)
    out[192:208, at] = jnp.where(iota((16, tree.shape[1]), 0) < 8, tree[128:144].astype(f32), 0.0).astype(bf16)
    out[208:256, at] = jnp.zeros((48, tree.shape[1]), bf16)


def feature_rows(high, low, extra):
    first = jnp.transpose(jnp.concatenate([high, low], 0))
    second = jnp.transpose(jnp.concatenate([high, extra, jnp.zeros((56, high.shape[1]), f32)], 0))
    return first.astype(bf16), second.astype(bf16)


def points_kernel(layout, trees, upper_ref, *refs):
    if not layout.fine:
        small_ref, refs = refs[0], refs[1:]
    else:
        small_ref = None
    place_refs, refs = refs[: layout.count], refs[layout.count :]
    tree_ref, a_hbm, base_hbm, sk_ref, upper_tiles_ref, top_ref, slot_ref, info_ref = refs[:8]
    masked, low_hot, a_ref, base_ref, sk_t, sk_bt, sems = refs[8:]
    blocks, rows = layout.blocks, layout.rows

    def keep(node, found):
        at = aligned(node * SK, SK, SK)
        sk_t[:, at] = found.astype(bf16)
        sk_ref[at, 0:128], sk_ref[at, 128:256] = feature_rows(found[0:64], found[64:128], found[136:144])
        feature_columns(sk_bt, slice(0, SK), found)

    def block(index, carry):
        tail = layout.gather(place_refs, index, slice(TAIL, PLACE_ROWS))
        slots = tail[SLOT : SLOT + 1]
        slot_ref[pl.ds(index, 1), :] = slots
        info = layout.info(place_refs, small_ref, index)
        info_ref[index] = info
        points = layout.gather(place_refs, index, slice(0, TAIL))
        high, low = two(points)
        nh, nm, nl = three(tail[NORM : NORM + 1])
        sub = iota((16, rows), 0)
        norms = jnp.where((sub == 3) | (sub == 8), nh, jnp.where((sub == 4) | (sub == 9), nm, nl))
        is_norm = ((sub >= 3) & (sub < 6)) | ((sub >= 8) & (sub < 11))
        is_one = (sub < 3) | ((sub >= 11) & (sub < 14))
        extra = jnp.where(is_norm, norms, jnp.where(is_one, 1.0, 0.0))
        low_part, high_part = parts_of(slots)
        low_by_column(low_hot, low_part.astype(f32))
        for h in range(rows // LOW):
            here = high_part == h
            masked[h * COORD : h * COORD + 64, :] = jnp.where(here, high.astype(f32), 0.0).astype(bf16)
            masked[h * COORD + 64 : h * COORD + 128, :] = jnp.where(here, low.astype(f32), 0.0).astype(bf16)
            masked[h * COORD + 128 : (h + 1) * COORD, :] = jnp.where(here, extra, 0.0).astype(bf16)
        placed = nn(masked[...], low_hot[...])
        for h in range(rows // LOW):
            part = placed[h * COORD : (h + 1) * COORD]
            at = aligned(index * rows + h * LOW, LOW, LOW)
            tree_ref[:, at] = part.astype(bf16)
            a_ref[at, 0:128], a_ref[at, 128:256] = feature_rows(part[0:64], part[64:128], part[136:144])
        picked = onehot(iota((rows, SK), 0) == info[BASE : BASE + 1].astype(jnp.int32))
        mine = aligned(index * rows, rows, rows)
        pltpu.make_async_copy(a_ref.at[mine], a_hbm.at[mine], sems.at[0, index]).start()
        keep(index, nn(tree_ref[:, mine], picked))
        base_ref[index] = jnp.exp(nn(a_ref[mine, :], sk_bt[...])).astype(bf16)
        pltpu.make_async_copy(base_ref.at[index], base_hbm.at[index], sems.at[1, index]).start()
        return carry

    lax.fori_loop(0, blocks, block, 0)
    start, count, offset, total = 0, blocks, 0, blocks * trees
    while count > 1:
        nodes = count // 2
        for j in range(nodes):
            pair = slice((start + 2 * j) * SK, (start + 2 * j + 2) * SK)
            row = offset + lax.axis_index("leaf") * nodes + j
            picked = onehot(iota((2 * SK, SK), 0) == upper_ref[pl.ds(row, 1), :])
            here = start + count + j
            keep(here, nn(sk_t[:, pair], picked))
            upper_tiles_ref[here - blocks] = jnp.exp(nn(sk_ref[pair, :], sk_bt[...]))
        total = total // 2
        offset = offset + total
        start, count = start + count, nodes
    found = sk_t[:, start * SK : (start + 1) * SK].astype(f32)
    top_ref[0:64, :] = found[0:64] + found[64:128]
    top_ref[64:72, :] = found[128:136]
    top_ref[72:128, :] = jnp.zeros((56, SK), f32)
    for index in range(blocks):
        mine = slice(index * rows, (index + 1) * rows)
        pltpu.make_async_copy(a_ref.at[mine], a_hbm.at[mine], sems.at[0, index]).wait()
        pltpu.make_async_copy(base_ref.at[index], base_hbm.at[index], sems.at[1, index]).wait()


def weights_kernel(
    layout, base_hbm, upper_tiles_ref, top_ref, slot_ref, light_ref, w_ref, coef_ref, pack_ref, masked, low_hot, base_ref, sems
):
    blocks, rows = layout.blocks, layout.rows
    width = light_ref.shape[1]
    pack_ref[...] = top_ref[...]
    for index in range(blocks):
        pltpu.make_async_copy(base_hbm.at[index], base_ref.at[index], sems.at[index]).start()

    def keep(node, coef):
        coef_ref[:, aligned(node * SK, SK, SK)] = stack_two(coef)
        pack_ref[LANES - width :, :] = coef

    def block(index, carry):
        low_part, high_part = parts_of(slot_ref[pl.ds(index, 1), :])
        low_by_column(low_hot, low_part.astype(f32))
        light = [light_ref[layout.message(g), :, layout.lanes(index)] for g in range(layout.count)]
        light = lanes_of(light)
        for h in range(rows // LOW):
            masked[h * width : (h + 1) * width, :] = jnp.where(high_part == h, light, 0.0).astype(bf16)
        placed = nn(masked[...], low_hot[...])
        parts = [placed[h * width : (h + 1) * width] for h in range(rows // LOW)]
        own = jnp.concatenate(parts, 1).astype(bf16)
        w_ref[:, aligned(index * rows, rows, rows)] = own
        pltpu.make_async_copy(base_hbm.at[index], base_ref.at[index], sems.at[index]).wait()
        keep(index, nn(own, base_ref[index]))
        return carry

    lax.fori_loop(0, blocks, block, 0)
    start, count = 0, blocks
    while count > 1:
        for j in range(count // 2):
            pair = slice((start + 2 * j) * SK, (start + 2 * j + 2) * SK)
            here = start + count + j
            high, low = two(upper_tiles_ref[here - blocks])
            coef = nn(coef_ref[:, pair], high)
            keep(here, coef[:width] + coef[width:] + nn(coef_ref[0:width, pair], low))
        start, count = start + count, count // 2


def near_kernel(count_ref, list_ref, a_hbm, tree_ref, w_ref, acc, times, tiles, a_ref, bt_ref, sem, *halves):
    every = count_ref.shape[1]
    copy = pltpu.make_async_copy(a_hbm, a_ref, sem)
    copy.start()
    for leaf in range(every):
        here = slice(leaf * LEAF, (leaf + 1) * LEAF)
        feature_columns(bt_ref, here, tree_ref[:, here])

    def tally(leaf, filled):
        for other in range(every):
            times[other] = (leaf == other).astype(jnp.int32)

        def add(slot, carry):
            at = list_ref[leaf, slot]
            times[at] = times[at] + 1
            return carry

        lax.fori_loop(0, count_ref[0, leaf], add, 0)
        for other in range(every):
            tiles[0, filled] = leaf
            tiles[1, filled] = other
            tiles[2, filled] = times[other]
            filled = filled + (times[other] > 0).astype(jnp.int32)
        return filled

    filled = lax.fori_loop(0, every, tally, jnp.int32(0))
    for more in range(2):
        tiles[0, filled + more] = 0
        tiles[1, filled + more] = 0
    half = LEAF // 2
    acc[...] = jnp.zeros_like(acc)

    def target(tile, part):
        return aligned(tiles[0, tile] * LEAF + part * half, half, half)

    even, odd = halves[0:2], halves[2:4]
    even_tile, odd_tile = halves[4:6], halves[6:8]

    def exponents(tile, part):
        source = aligned(tiles[1, tile] * LEAF, LEAF, LEAF)
        return nn(a_ref[source, :], bt_ref[:, target(tile, part)])

    def add(tile, part, block):
        source = aligned(tiles[1, tile] * LEAF, LEAF, LEAF)
        acc[:, target(tile, part)] += tiles[2, tile].astype(f32) * nn(w_ref[:, source], block[part][...])

    def phase(tile, upcoming, ready, made, previous):
        for part in range(2):
            upcoming[part][...] = exponents(tile + 1, part)
            made[part][...] = jnp.exp(ready[part][...]).astype(bf16)
            add(tile - 1, part, previous)

    copy.wait()
    for part in range(2):
        even[part][...] = exponents(0, part)
        even_tile[part][...] = jnp.exp(even[part][...]).astype(bf16)
        odd[part][...] = exponents(1, part)

    def step(pair, carry):
        phase(2 * pair + 1, even, odd, odd_tile, even_tile)
        phase(2 * pair + 2, odd, even, even_tile, odd_tile)
        return carry

    lax.fori_loop(0, (filled - 1) // 2, step, 0)
    done = 2 * ((filled - 1) // 2)
    for part in range(2):
        add(done, part, even_tile)

    @pl.when(done + 1 < filled)
    def _():
        for part in range(2):
            odd_tile[part][...] = jnp.exp(odd[part][...]).astype(bf16)
            add(done + 1, part, odd_tile)


def far_kernel(layout, low_levels, pack_ref, slot_ref, info_ref, tree_ref, sk_ref, coef_ref, near_ref, *refs):
    out_refs, (tops, coefs, low_hot, bt_ref) = refs[: layout.count], refs[layout.count :]
    blocks, rows = layout.blocks, layout.rows
    ups, width = pack_ref.shape[0], out_refs[0].shape[0]
    levels = low_levels + ups
    lane = iota((1, SK), 1)
    for up in range(ups):
        pack = pack_ref[up]
        high, low = two(pack[0:64])
        sub = iota((8, SK), 0)
        extra = jnp.where(sub == 0, pack[67:68], jnp.where(sub == 1, pack[68:69], pack[69:70]))
        extra = jnp.where(sub < 3, extra, jnp.where(sub < 6, 1.0, 0.0))
        at = slice((low_levels + up) * SK, (low_levels + up + 1) * SK)
        tops[at, 0:128], tops[at, 128:256] = feature_rows(high.astype(f32), low.astype(f32), extra)
        coefs[:, at] = stack_two(pack[LANES - width :])

    def block(index, carry):
        node, start, count = index, 0, blocks
        for level in range(low_levels):
            at = slice(level * SK, (level + 1) * SK)
            other = aligned((start + (node ^ 1)) * SK, SK, SK)
            tops[at, :] = sk_ref[other, :]
            coefs[:, at] = coef_ref[:, other]
            node, start, count = node // 2, start + count, count // 2
        low_part, high_part = parts_of(slot_ref[pl.ds(index, 1), :])
        for c in range(rows // LANES):
            at = slice(c * LANES, (c + 1) * LANES)
            low_hot[:, at] = onehot(iota((LOW, LANES), 0) == low_part[:, at])
        info = info_ref[index]
        totals = []
        for leaf in range(rows // LEAF):
            flags = info[FLAGS + leaf : FLAGS + leaf + 1]
            used = []
            for level in range(levels):
                flag = jnp.sum(jnp.where(lane == level, flags, 0.0), axis=1, keepdims=True)
                used.append(jnp.broadcast_to(flag, (1, SK)))
            here = aligned(index * rows + leaf * LEAF, LEAF, LEAF)
            feature_columns(bt_ref, slice(0, LEAF), tree_ref[:, here])
            tile = jnp.exp(nn(tops[...], bt_ref[...])).astype(bf16)
            scaled = (coefs[...].astype(f32) * jnp.concatenate(used, 1)).astype(bf16)
            far = nn(scaled, tile)
            totals.append(near_ref[:, here] + far[:width] + far[width:])
        both = stack_two(jnp.concatenate(totals, 1))
        parts = [both[:, h * LOW : (h + 1) * LOW] for h in range(rows // LOW)]
        moved = nn(jnp.concatenate(parts, 0), low_hot[...])
        result = jnp.zeros((2 * width, rows), f32)
        for h in range(rows // LOW):
            result = jnp.where(high_part == h, moved[h * 2 * width : (h + 1) * 2 * width], result)
        result = result[:width] + result[width:]
        for g, out_ref in enumerate(out_refs):
            out_ref[:, layout.lanes(index)] = result[:, g * layout.per : (g + 1) * layout.per]
        return carry

    lax.fori_loop(0, blocks, block, 0)


def final_kernel(blocks, pos_ref, *refs):
    back_refs, (weights_ref, out_ref, perm, vals) = refs[:-4], refs[-4:]
    chunks = pos_ref.shape[0]
    rows = chunks * LANES
    width, split = back_refs[0].shape
    for r in range(chunks):
        spread(perm, slice(r * LANES, (r + 1) * LANES), column(pos_ref[r : r + 1, :]))
    for g, back_ref in enumerate(back_refs):
        high, low = two(back_ref[...])
        columns, at = 0, slice(0, rows)
        if blocks:
            columns = (lax.axis_index("sub") ^ (g % blocks)) * width
            at = aligned((lax.axis_index("leaf") ^ lax.axis_index("rep") ^ (g // blocks)) * split, split, split)
        vals[aligned(columns, width, width), at] = high
        vals[aligned(columns + LANES, width, width), at] = low
    step = 256
    for s in range(rows // step):
        here = slice(s * step, (s + 1) * step)
        moved = nt(perm[here, :], vals[...])
        out_ref[here, :] = ridge * weights_ref[here, :] + moved[:, :LANES] + moved[:, LANES:]


def upper_levels(pack, skeleton_upper, my_leaf, trees, blocks, width):
    devices = trees * blocks
    level = blocks.bit_length() - 1
    offset = sum(devices >> step for step in range(1, level + 1))
    line = jnp.arange(LANES)[:, None]
    is_point, is_norm = line < DIM, (line >= DIM + 3) & (line < DIM + 6)
    is_coef = line >= LANES - width
    packs, own, stride = [], pack, 1
    while stride < trees:
        other = lax.ppermute(own, "leaf", [(i, i ^ stride) for i in range(trees)])
        packs.append(other)
        stride *= 2
        if stride < trees:
            second = (my_leaf // (stride // 2)) % 2 == 1
            pair = jnp.where(second, jnp.concatenate([other, own], 1), jnp.concatenate([own, other], 1))
            chosen = pair[:, skeleton_upper[offset + my_leaf // stride]]
            level += 1
            offset += devices >> level
            norms = jnp.sum(jnp.where(is_norm, pair, 0.0), axis=0)
            chosen_norms = jnp.sum(jnp.where(is_norm, chosen, 0.0), axis=0)
            inner = jnp.dot(
                jnp.where(is_point, pair, 0.0).T, jnp.where(is_point, chosen, 0.0), precision=highest
            )
            tile = jnp.exp(inner + norms[:, None] + chosen_norms[None])
            own = jnp.where(is_coef, jnp.dot(pair, tile, precision=highest), chosen)
    return jnp.stack(packs)


def body(points, weights, tree_slot, near_count, near_list, skeleton_base, skeleton_upper, far_use):
    blocks, trees, reps = lax.axis_size("sub"), lax.axis_size("leaf"), lax.axis_size("rep")
    devices = blocks * trees
    rows, columns = weights.shape
    low_levels = blocks.bit_length() - 1
    ups = trees.bit_length() - 1
    width = columns // blocks
    part = rows // trees
    per = part // blocks
    total = blocks * rows
    leaves = total // LEAF
    my_leaf = lax.axis_index("leaf")
    fine = trees == 2 and reps == 2 and per % LANES == 0
    layout = Layout(blocks, trees, rows, fine)
    split = part if fine else rows
    arrive = shaped((width, part), f32) if fine else shaped((width, total), f32)

    place, pos, light = pl.pallas_call(
        functools.partial(sort_kernel, fine),
        out_shape=(
            shaped((PLACE_ROWS, split), f32),
            shaped((rows // LANES, LANES), f32),
            shaped((rows // split, columns, split), f32),
        ),
        in_specs=[spec()] * 5,
        out_specs=(spec(),) * 3,
        scratch_shapes=[
            vm((rows, rows), bf16),
            vm((272, rows), bf16),
            vm((rows // split, PLACE_ROWS, split), f32),
        ],
        compiler_params=params(),
        name="sort_rows",
    )(tree_slot.reshape(rows // LANES, LANES), points.T, weights, skeleton_base, far_use)

    axes = ("leaf", "sub", "rep")

    def swap(value, step, other=0):
        pairs = []
        for leaf in range(trees):
            for sub in range(blocks):
                for core in range(reps):
                    to = ((leaf ^ core ^ other) * blocks + (sub ^ step)) * reps + core
                    pairs.append(((leaf * blocks + sub) * reps + core, to))
        return lax.ppermute(value, axes, pairs)

    def swap_all(values):
        done = {}
        for g in sorted(range(len(values)), key=lambda g: -(g % blocks)):
            done[g] = swap(values[g], g % blocks, g // blocks)
        return [done[g] for g in range(len(values))]

    if fine:
        place = {0: swap(place, 0)}
        stride = blocks // 2
        while stride:
            for step in sorted(place):
                place[step | stride] = lax.ppermute(place[step], "sub", [(i, i ^ stride) for i in range(blocks)])
            stride //= 2
        theirs = {step: lax.ppermute(one, "rep", [(0, 1), (1, 0)]) for step, one in place.items()}
        place = [place[step] for step in range(blocks)] + [theirs[step] for step in range(blocks)]
        light = light.reshape(devices, width, part)
        light = lax.all_to_all(light, ("leaf", "sub"), split_axis=0, concat_axis=0, tiled=True)
        small = []
    else:
        info = jnp.pad(far_use.astype(f32), ((FLAGS, 5 - far_use.shape[0]), (0, SK - far_use.shape[1])))
        small = [lax.all_gather(info.at[BASE].set(skeleton_base[0].astype(f32)), "sub", axis=0, tiled=False)]
        place = place.reshape(PLACE_ROWS, trees, part).transpose(1, 0, 2)
        place = lax.all_to_all(place, "leaf", split_axis=0, concat_axis=0, tiled=True)
        place = lax.all_gather(place, "sub", axis=0, tiled=False)
        place = place.transpose(1, 0, 2, 3).reshape(devices, PLACE_ROWS, blocks, per)
        place = [place.transpose(1, 2, 0, 3).reshape(PLACE_ROWS, total)]
        light = light.reshape(columns, trees, part).transpose(1, 0, 2).reshape(devices, width, part)
        light = lax.all_to_all(light, ("leaf", "sub"), split_axis=0, concat_axis=0, tiled=True)
        light = light.reshape(devices, width, blocks, per)
        light = light.transpose(1, 2, 0, 3).reshape(1, width, total)

    nodes = 2 * blocks - 1
    tree, feat_a, base, sk, upper_tiles, top, slots, info = pl.pallas_call(
        functools.partial(points_kernel, layout, trees),
        out_shape=(
            vm((COORD, total), bf16),
            pltpu.MemorySpace.HBM((total, FEAT), bf16),
            pltpu.MemorySpace.HBM((blocks, rows, SK), bf16),
            vm((nodes * SK, FEAT), bf16),
            vm((blocks - 1, 2 * SK, SK), f32),
            vm((SK, LANES), f32),
            vm((blocks, rows), f32),
            vm((blocks, 8, SK), f32),
        ),
        in_specs=[spec()] * (1 + len(small) + layout.count),
        out_specs=(spec(), spec(pl.ANY), spec(pl.ANY)) + (spec(),) * 5,
        scratch_shapes=[
            vm((rows // LOW * COORD, rows), bf16),
            vm((rows, LOW), bf16),
            vm((total, FEAT), bf16),
            vm((blocks, rows, SK), bf16),
            vm((COORD, nodes * SK), bf16),
            vm((FEAT, SK), bf16),
            pltpu.SemaphoreType.DMA((2, blocks)),
        ],
        compiler_params=params(40),
        name="tree_points",
    )(in_hbm(skeleton_upper), *small, *place)

    tree_light, coefs, pack = pl.pallas_call(
        functools.partial(weights_kernel, layout),
        out_shape=(
            vm((width, total), bf16),
            vm((2 * width, nodes * SK), bf16),
            shaped((LANES, SK), f32),
        ),
        in_specs=[spec(pl.ANY)] + [spec()] * 4,
        out_specs=(spec(),) * 3,
        scratch_shapes=[
            vm((rows // LOW * width, rows), bf16),
            vm((rows, LOW), bf16),
            vm((blocks, rows, SK), bf16),
            pltpu.SemaphoreType.DMA((blocks,)),
        ],
        compiler_params=params(40),
        name="tree_weights",
    )(in_hbm(base), held(upper_tiles), held(top), held(slots), light)

    packs = upper_levels(pack, skeleton_upper, my_leaf, trees, blocks, width)

    near = pl.pallas_call(
        near_kernel,
        out_shape=vm((width, total), f32),
        in_specs=[spec(SMEM)] * 2 + [spec(pl.ANY)] + [spec()] * 2,
        out_specs=spec(),
        scratch_shapes=[
            pltpu.SMEM((leaves,), jnp.int32),
            pltpu.SMEM((3, leaves * leaves + 2), jnp.int32),
            vm((total, FEAT), bf16),
            vm((FEAT, total), bf16),
            pltpu.SemaphoreType.DMA(()),
        ]
        + [vm((LEAF, LEAF // 2), f32)] * 4
        + [vm((LEAF, LEAF // 2), bf16)] * 4,
        compiler_params=params(40),
        name="near",
    )(in_hbm(near_count), in_hbm(near_list[0]), in_hbm(feat_a), held(tree), held(tree_light))

    levels = low_levels + ups
    back = pl.pallas_call(
        functools.partial(far_kernel, layout, low_levels),
        out_shape=(arrive,) * layout.count,
        in_specs=[spec()] * 7,
        out_specs=(spec(),) * layout.count,
        scratch_shapes=[vm((levels * SK, FEAT), bf16), vm((2 * width, levels * SK), bf16), vm((LOW, rows), bf16), vm((FEAT, LEAF), bf16)],
        compiler_params=params(40),
        name="far",
    )(packs, *[held(one) for one in (slots, info, tree, sk, coefs, near)])

    if fine:
        back = swap_all(back)
    else:
        back = back[0].reshape(width, blocks, devices, per).transpose(2, 0, 1, 3).reshape(devices, width, part)
        back = lax.all_to_all(back, ("leaf", "sub"), split_axis=0, concat_axis=0, tiled=True)
        back = [back.reshape(trees, columns, part).transpose(1, 0, 2).reshape(columns, rows)]

    return pl.pallas_call(
        functools.partial(final_kernel, blocks if fine else 0),
        out_shape=shaped((rows, columns), f32),
        in_specs=[spec()] * (2 + layout.count),
        out_specs=spec(),
        scratch_shapes=[vm((rows, rows), bf16), vm((2 * LANES, rows), bf16)],
        compiler_params=params(40),
        name="to_input_order",
    )(pos, *back, weights)


def solution(mesh):
    in_specs = (
        P(("groups", "leaf", "sub"), None),
        P(("groups", "leaf", "sub"), "rep"),
        P(("groups", "leaf", "sub")),
        P(("groups", "leaf"), None),
        P(("groups", "leaf"), None, None),
        P(("groups", "leaf", "sub"), None),
        P("groups", None),
        P(("groups", "leaf", "sub"), None),
    )
    out_specs = P(("groups", "leaf", "sub"), "rep")
    return jax.shard_map(body, mesh=mesh, in_specs=in_specs, out_specs=out_specs, check_vma=False)
```

```python
import functools

import jax
import jax.numpy as jnp
from jax import lax
from jax.experimental import pallas as pl
from jax.experimental.pallas import tpu as pltpu
from jax.sharding import PartitionSpec as P

DIM = 64
LEAF = 512
SK = 128
LANES = 128
FEAT = 256
LOW = 256
COORD = 144

highest = lax.Precision.HIGHEST
point_scale = 0.25
ridge = 0.5
PLACE_ROWS = 72
TAIL = 64
SLOT, NORM, BASE, FLAGS = 0, 1, 2, 3
f32 = jnp.float32
bf16 = jnp.bfloat16
VMEM = pltpu.MemorySpace.VMEM
SMEM = pltpu.MemorySpace.SMEM


def spec(space=VMEM):
    return pl.BlockSpec(memory_space=space)


def params(mib=58):
    return pltpu.CompilerParams(vmem_limit_bytes=mib * 1024 * 1024)


def in_hbm(array):
    return pltpu.with_memory_space_constraint(array, pltpu.MemorySpace.HBM)


def held(array):
    return pltpu.with_memory_space_constraint(array, VMEM)


def vm(shape, dtype):
    return pltpu.VMEM(shape, dtype)


def shaped(shape, dtype):
    return jax.ShapeDtypeStruct(shape, dtype)


def nt(left, right):
    return lax.dot_general(left, right, (((1,), (1,)), ((), ())), preferred_element_type=f32)


def nn(left, right):
    return jnp.dot(left, right, preferred_element_type=f32)


def column(row):
    return jnp.transpose(jnp.broadcast_to(row, (LANES, LANES)))


def iota(shape, dim):
    return lax.broadcasted_iota(jnp.int32, shape, dim)


def onehot(mask):
    return jnp.where(mask, 1.0, 0.0).astype(bf16)


def two(value):
    high = value.astype(bf16)
    return high, (value - high.astype(f32)).astype(bf16)


def three(value):
    high = value.astype(bf16).astype(f32)
    mid = (value - high).astype(bf16).astype(f32)
    return high, mid, (value - high - mid).astype(bf16).astype(f32)


def lanes_of(blocks):
    return blocks[0] if len(blocks) == 1 else jnp.concatenate(blocks, 1)


def aligned(start, size, unit):
    return pl.ds(pl.multiple_of(start, unit), size)


def stack_two(value):
    high, low = two(value)
    return jnp.concatenate([high, low], 0)


def spread(perm, here, rank):
    lane = iota((LANES, LANES), 1).astype(f32)
    for c in range(perm.shape[1] // LANES):
        perm[here, c * LANES : (c + 1) * LANES] = onehot(lane + float(c * LANES) == rank)


def place_kernel(fine, slot_ref, points_ref, base_ref, flag_ref, place_ref, pos_ref, masked, low_hot):
    chunks = slot_ref.shape[0]
    slots = slot_ref[...]
    slot = slots.astype(f32)
    within = slots & (chunks * LANES - 1)
    high, low = (within >> 5).astype(f32), (within & 31).astype(f32)
    ranks = []
    for r in range(chunks):
        here = slice(r * LANES, (r + 1) * LANES)
        mine = column(slot[r : r + 1])
        before = jnp.zeros((LANES, LANES), f32)
        for c in range(chunks):
            before += jnp.where(slot[c : c + 1] < mine, 1.0, 0.0)
        rank = jnp.broadcast_to(jnp.sum(before, axis=1, keepdims=True), (LANES, LANES))
        ranks.append(jnp.transpose(rank)[0:1])
        pos_ref[r : r + 1, :] = ranks[-1]
        spread(low_hot, here, (rank.astype(jnp.int32) & (LOW - 1)).astype(f32))
    scaled = points_ref[...] * point_scale
    ph, plo = two(scaled)
    nh, nm, nl = three(-0.5 * jnp.sum(scaled * scaled, axis=0, keepdims=True))
    high, low = lanes_of([high[c : c + 1] for c in range(chunks)]), lanes_of([low[c : c + 1] for c in range(chunks)])
    sub = iota((16, chunks * LANES), 0)
    extra = jnp.where(sub == 0, high, jnp.where(sub == 1, low, 0.0))
    extra = jnp.where(sub == 2, nh, jnp.where(sub == 3, nm, jnp.where(sub == 4, nl, extra)))
    high_part = lanes_of(ranks).astype(jnp.int32) // LOW
    parts = place_ref.shape[1] // LOW
    first = (lax.axis_index("leaf") ^ lax.axis_index("rep")) * parts if fine else 0
    for h in range(parts):
        here = high_part == first + h
        masked[h * COORD : h * COORD + 64, :] = jnp.where(here, ph.astype(f32), 0.0).astype(bf16)
        masked[h * COORD + 64 : h * COORD + 128, :] = jnp.where(here, plo.astype(f32), 0.0).astype(bf16)
        masked[h * COORD + 128 : (h + 1) * COORD, :] = jnp.where(here, extra, 0.0).astype(bf16)
    placed = nn(masked[...], low_hot[...])
    tail = iota((PLACE_ROWS - TAIL, LOW), 0)
    for h in range(parts):
        at = slice(h * LOW, (h + 1) * LOW)
        moved = placed[h * COORD : (h + 1) * COORD]
        place_ref[0:TAIL, at] = moved[0:64] + moved[64:128]
        slot_row = moved[128:129] * 32.0 + moved[129:130]
        norm_row = moved[130:131] + moved[131:132] + moved[132:133]
        place_ref[TAIL:, at] = jnp.where(tail == SLOT, slot_row, jnp.where(tail == NORM, norm_row, 0.0))
    if fine:
        place_ref[TAIL + BASE : TAIL + BASE + 1, 0:SK] = base_ref[...].astype(f32)
        place_ref[TAIL + FLAGS : TAIL + FLAGS + flag_ref.shape[0], 0 : flag_ref.shape[1]] = flag_ref[...].astype(f32)


def light_kernel(pos_ref, weights_ref, light_ref, masked, low_hot):
    chunks, split = pos_ref.shape[0], light_ref.shape[2]
    low_part, high_part = parts_of(lanes_of([pos_ref[c : c + 1, :] for c in range(chunks)]))
    low_by_column(low_hot, low_part.astype(f32))
    for c in range(chunks):
        at = slice(c * LANES, (c + 1) * LANES)
        turned = jnp.transpose(weights_ref[at, :])
        for h in range(chunks * LANES // LOW):
            masked[h * LANES : (h + 1) * LANES, at] = jnp.where(high_part[:, at] == h, turned, 0.0).astype(bf16)
    placed = nn(masked[...], low_hot[...])
    for h in range(chunks * LANES // LOW):
        at = h * LOW
        light_ref[at // split, :, at % split : at % split + LOW] = placed[h * LANES : (h + 1) * LANES]


class Layout:
    def __init__(self, blocks, trees, rows, fine):
        self.blocks, self.rows, self.fine = blocks, rows, fine
        self.count = blocks * trees if fine else 1
        self.per = rows // self.count

    def lanes(self, index):
        return aligned(index * self.per, self.per, LANES)

    def message(self, group):
        if not self.fine:
            return 0
        leaf = lax.axis_index("leaf") ^ lax.axis_index("rep") ^ (group // self.blocks)
        return leaf * self.blocks + (lax.axis_index("sub") ^ (group % self.blocks))

    def gather(self, refs, index, part):
        return lanes_of([ref[part, self.lanes(index)] for ref in refs])

    def info(self, refs, small_ref, index):
        if not self.fine:
            return small_ref[index]
        core = lax.axis_index("rep")
        found = jnp.zeros((PLACE_ROWS - TAIL, SK), f32)
        for step in range(self.blocks):
            mine, theirs = refs[step][TAIL:, 0:SK], refs[self.blocks + step][TAIL:, 0:SK]
            here = jnp.where(core == 0, mine, theirs)
            found = jnp.where((lax.axis_index("sub") ^ step) == index, here, found)
        return found


def low_by_column(out, low):
    for c in range(out.shape[0] // LANES):
        at = slice(c * LANES, (c + 1) * LANES)
        spread(out, at, column(low[:, at]))


def parts_of(slots):
    slots = slots.astype(jnp.int32)
    return slots & (LOW - 1), slots // LOW


def feature_columns(out, at, tree):
    out[0:64, at] = tree[0:64].astype(bf16)
    out[64:128, at] = tree[0:64].astype(bf16)
    out[128:192, at] = tree[64:128].astype(bf16)
    out[192:208, at] = jnp.where(iota((16, tree.shape[1]), 0) < 8, tree[128:144].astype(f32), 0.0).astype(bf16)
    out[208:256, at] = jnp.zeros((48, tree.shape[1]), bf16)


def feature_rows(high, low, extra):
    first = jnp.transpose(jnp.concatenate([high, low], 0))
    second = jnp.transpose(jnp.concatenate([high, extra, jnp.zeros((56, high.shape[1]), f32)], 0))
    return first.astype(bf16), second.astype(bf16)


def list_tiles(count_ref, list_ref, tiles, times):
    every = count_ref.shape[1]

    def tally(leaf, filled):
        for other in range(every):
            times[other] = (leaf == other).astype(jnp.int32)

        def add(slot, carry):
            at = list_ref[leaf, slot]
            times[at] = times[at] + 1
            return carry

        lax.fori_loop(0, count_ref[0, leaf], add, 0)
        for other in range(every):
            tiles[0, filled] = leaf
            tiles[1, filled] = other
            tiles[2, filled] = times[other]
            filled = filled + (times[other] > 0).astype(jnp.int32)
        return filled

    filled = lax.fori_loop(0, every, tally, jnp.int32(0))
    for more in range(2):
        tiles[0, filled + more] = 0
        tiles[1, filled + more] = 0
    tiles[0, tiles.shape[1] - 1] = filled


def points_kernel(layout, trees, count_ref, list_ref, upper_ref, *refs):
    if not layout.fine:
        small_ref, refs = refs[0], refs[1:]
    else:
        small_ref = None
    place_refs, refs = refs[: layout.count], refs[layout.count :]
    tree_ref, a_hbm, base_hbm, sk_ref, upper_tiles_ref, top_ref, slot_ref, info_ref, tiles = refs[:9]
    masked, low_hot, a_ref, base_ref, sk_t, sk_bt, sems, times = refs[9:]
    blocks, rows = layout.blocks, layout.rows

    def keep(node, found):
        at = aligned(node * SK, SK, SK)
        sk_t[:, at] = found.astype(bf16)
        sk_ref[at, 0:128], sk_ref[at, 128:256] = feature_rows(found[0:64], found[64:128], found[136:144])
        feature_columns(sk_bt, slice(0, SK), found)

    def block(index, carry):
        tail = layout.gather(place_refs, index, slice(TAIL, PLACE_ROWS))
        slots = tail[SLOT : SLOT + 1]
        slot_ref[pl.ds(index, 1), :] = slots
        info = layout.info(place_refs, small_ref, index)
        info_ref[index] = info
        points = layout.gather(place_refs, index, slice(0, TAIL))
        high, low = two(points)
        nh, nm, nl = three(tail[NORM : NORM + 1])
        sub = iota((16, rows), 0)
        norms = jnp.where((sub == 3) | (sub == 8), nh, jnp.where((sub == 4) | (sub == 9), nm, nl))
        is_norm = ((sub >= 3) & (sub < 6)) | ((sub >= 8) & (sub < 11))
        is_one = (sub < 3) | ((sub >= 11) & (sub < 14))
        extra = jnp.where(is_norm, norms, jnp.where(is_one, 1.0, 0.0))
        low_part, high_part = parts_of(slots)
        low_by_column(low_hot, low_part.astype(f32))
        for h in range(rows // LOW):
            here = high_part == h
            masked[h * COORD : h * COORD + 64, :] = jnp.where(here, high.astype(f32), 0.0).astype(bf16)
            masked[h * COORD + 64 : h * COORD + 128, :] = jnp.where(here, low.astype(f32), 0.0).astype(bf16)
            masked[h * COORD + 128 : (h + 1) * COORD, :] = jnp.where(here, extra, 0.0).astype(bf16)
        placed = nn(masked[...], low_hot[...])
        for h in range(rows // LOW):
            part = placed[h * COORD : (h + 1) * COORD]
            at = aligned(index * rows + h * LOW, LOW, LOW)
            tree_ref[:, at] = part.astype(bf16)
            a_ref[at, 0:128], a_ref[at, 128:256] = feature_rows(part[0:64], part[64:128], part[136:144])
        picked = onehot(iota((rows, SK), 0) == info[BASE : BASE + 1].astype(jnp.int32))
        mine = aligned(index * rows, rows, rows)
        pltpu.make_async_copy(a_ref.at[mine], a_hbm.at[mine], sems.at[0, index]).start()
        keep(index, nn(tree_ref[:, mine], picked))
        base_ref[index] = jnp.exp(nn(a_ref[mine, :], sk_bt[...])).astype(bf16)
        pltpu.make_async_copy(base_ref.at[index], base_hbm.at[index], sems.at[1, index]).start()
        return carry

    lax.fori_loop(0, blocks, block, 0)
    start, count, offset, total = 0, blocks, 0, blocks * trees
    while count > 1:
        nodes = count // 2
        for j in range(nodes):
            pair = slice((start + 2 * j) * SK, (start + 2 * j + 2) * SK)
            row = offset + lax.axis_index("leaf") * nodes + j
            picked = onehot(iota((2 * SK, SK), 0) == upper_ref[pl.ds(row, 1), :])
            here = start + count + j
            keep(here, nn(sk_t[:, pair], picked))
            upper_tiles_ref[here - blocks] = jnp.exp(nn(sk_ref[pair, :], sk_bt[...]))
        total = total // 2
        offset = offset + total
        start, count = start + count, nodes
    found = sk_t[:, start * SK : (start + 1) * SK].astype(f32)
    top_ref[0:64, :] = found[0:64] + found[64:128]
    top_ref[64:72, :] = found[128:136]
    top_ref[72:128, :] = jnp.zeros((56, SK), f32)
    list_tiles(count_ref, list_ref, tiles, times)
    for index in range(blocks):
        mine = slice(index * rows, (index + 1) * rows)
        pltpu.make_async_copy(a_ref.at[mine], a_hbm.at[mine], sems.at[0, index]).wait()
        pltpu.make_async_copy(base_ref.at[index], base_hbm.at[index], sems.at[1, index]).wait()


def weights_kernel(
    layout, base_hbm, upper_tiles_ref, top_ref, slot_ref, light_ref, w_ref, coef_ref, pack_ref, masked, low_hot, base_ref, sems
):
    blocks, rows = layout.blocks, layout.rows
    width = light_ref.shape[1]
    pack_ref[...] = top_ref[...]
    for index in range(blocks):
        pltpu.make_async_copy(base_hbm.at[index], base_ref.at[index], sems.at[index]).start()

    def keep(node, coef):
        coef_ref[:, aligned(node * SK, SK, SK)] = stack_two(coef)
        pack_ref[LANES - width :, :] = coef

    def block(index, carry):
        low_part, high_part = parts_of(slot_ref[pl.ds(index, 1), :])
        low_by_column(low_hot, low_part.astype(f32))
        light = [light_ref[layout.message(g), :, layout.lanes(index)] for g in range(layout.count)]
        light = lanes_of(light)
        for h in range(rows // LOW):
            masked[h * width : (h + 1) * width, :] = jnp.where(high_part == h, light, 0.0).astype(bf16)
        placed = nn(masked[...], low_hot[...])
        parts = [placed[h * width : (h + 1) * width] for h in range(rows // LOW)]
        own = jnp.concatenate(parts, 1).astype(bf16)
        w_ref[:, aligned(index * rows, rows, rows)] = own
        pltpu.make_async_copy(base_hbm.at[index], base_ref.at[index], sems.at[index]).wait()
        keep(index, nn(own, base_ref[index]))
        return carry

    lax.fori_loop(0, blocks, block, 0)
    start, count = 0, blocks
    while count > 1:
        for j in range(count // 2):
            pair = slice((start + 2 * j) * SK, (start + 2 * j + 2) * SK)
            here = start + count + j
            high, low = two(upper_tiles_ref[here - blocks])
            coef = nn(coef_ref[:, pair], high)
            keep(here, coef[:width] + coef[width:] + nn(coef_ref[0:width, pair], low))
        start, count = start + count, count // 2


def near_kernel(tiles, a_hbm, tree_ref, w_ref, acc, a_ref, bt_ref, sem, *halves):
    copy = pltpu.make_async_copy(a_hbm, a_ref, sem)
    copy.start()
    for leaf in range(bt_ref.shape[1] // LEAF):
        here = slice(leaf * LEAF, (leaf + 1) * LEAF)
        feature_columns(bt_ref, here, tree_ref[:, here])

    filled = tiles[0, tiles.shape[1] - 1]
    half = LEAF // 2
    acc[...] = jnp.zeros_like(acc)

    def target(tile, part):
        return aligned(tiles[0, tile] * LEAF + part * half, half, half)

    even, odd = halves[0:2], halves[2:4]
    even_tile, odd_tile = halves[4:6], halves[6:8]

    def exponents(tile, part):
        source = aligned(tiles[1, tile] * LEAF, LEAF, LEAF)
        return nn(a_ref[source, :], bt_ref[:, target(tile, part)])

    def add(tile, part, block):
        source = aligned(tiles[1, tile] * LEAF, LEAF, LEAF)
        acc[:, target(tile, part)] += tiles[2, tile].astype(f32) * nn(w_ref[:, source], block[part][...])

    def phase(tile, upcoming, ready, made, previous):
        for part in range(2):
            upcoming[part][...] = exponents(tile + 1, part)
            made[part][...] = jnp.exp(ready[part][...]).astype(bf16)
            add(tile - 1, part, previous)

    copy.wait()
    for part in range(2):
        even[part][...] = exponents(0, part)
        even_tile[part][...] = jnp.exp(even[part][...]).astype(bf16)
        odd[part][...] = exponents(1, part)

    def step(pair, carry):
        phase(2 * pair + 1, even, odd, odd_tile, even_tile)
        phase(2 * pair + 2, odd, even, even_tile, odd_tile)
        return carry

    lax.fori_loop(0, (filled - 1) // 2, step, 0)
    done = 2 * ((filled - 1) // 2)
    for part in range(2):
        add(done, part, even_tile)

    @pl.when(done + 1 < filled)
    def _():
        for part in range(2):
            odd_tile[part][...] = jnp.exp(odd[part][...]).astype(bf16)
            add(done + 1, part, odd_tile)


def far_kernel(layout, low_levels, pack_ref, slot_ref, info_ref, tree_ref, sk_ref, coef_ref, near_ref, *refs):
    out_refs, (tops, coefs, low_hot, bt_ref) = refs[: layout.count], refs[layout.count :]
    blocks, rows = layout.blocks, layout.rows
    ups, width = pack_ref.shape[0], out_refs[0].shape[0]
    levels = low_levels + ups
    lane = iota((1, SK), 1)
    for up in range(ups):
        pack = pack_ref[up]
        high, low = two(pack[0:64])
        sub = iota((8, SK), 0)
        extra = jnp.where(sub == 0, pack[67:68], jnp.where(sub == 1, pack[68:69], pack[69:70]))
        extra = jnp.where(sub < 3, extra, jnp.where(sub < 6, 1.0, 0.0))
        at = slice((low_levels + up) * SK, (low_levels + up + 1) * SK)
        tops[at, 0:128], tops[at, 128:256] = feature_rows(high.astype(f32), low.astype(f32), extra)
        coefs[:, at] = stack_two(pack[LANES - width :])

    def block(index, carry):
        node, start, count = index, 0, blocks
        for level in range(low_levels):
            at = slice(level * SK, (level + 1) * SK)
            other = aligned((start + (node ^ 1)) * SK, SK, SK)
            tops[at, :] = sk_ref[other, :]
            coefs[:, at] = coef_ref[:, other]
            node, start, count = node // 2, start + count, count // 2
        low_part, high_part = parts_of(slot_ref[pl.ds(index, 1), :])
        for c in range(rows // LANES):
            at = slice(c * LANES, (c + 1) * LANES)
            low_hot[:, at] = onehot(iota((LOW, LANES), 0) == low_part[:, at])
        info = info_ref[index]
        totals = []
        for leaf in range(rows // LEAF):
            flags = info[FLAGS + leaf : FLAGS + leaf + 1]
            used = []
            for level in range(levels):
                flag = jnp.sum(jnp.where(lane == level, flags, 0.0), axis=1, keepdims=True)
                used.append(jnp.broadcast_to(flag, (1, SK)))
            here = aligned(index * rows + leaf * LEAF, LEAF, LEAF)
            feature_columns(bt_ref, slice(0, LEAF), tree_ref[:, here])
            tile = jnp.exp(nn(tops[...], bt_ref[...])).astype(bf16)
            scaled = (coefs[...].astype(f32) * jnp.concatenate(used, 1)).astype(bf16)
            far = nn(scaled, tile)
            totals.append(near_ref[:, here] + far[:width] + far[width:])
        both = stack_two(jnp.concatenate(totals, 1))
        parts = [both[:, h * LOW : (h + 1) * LOW] for h in range(rows // LOW)]
        moved = nn(jnp.concatenate(parts, 0), low_hot[...])
        result = jnp.zeros((2 * width, rows), f32)
        for h in range(rows // LOW):
            result = jnp.where(high_part == h, moved[h * 2 * width : (h + 1) * 2 * width], result)
        result = result[:width] + result[width:]
        for g, out_ref in enumerate(out_refs):
            out_ref[:, layout.lanes(index)] = result[:, g * layout.per : (g + 1) * layout.per]
        return carry

    lax.fori_loop(0, blocks, block, 0)


def far_first(blocks, count):
    return sorted(range(count), key=lambda g: -((g % blocks) * 2 // blocks) if blocks else 0)


def final_kernel(blocks, pos_ref, *refs):
    back_refs, (weights_ref, out_ref, perm, vals) = refs[:-4], refs[-4:]
    chunks = pos_ref.shape[0]
    rows = chunks * LANES
    width, split = back_refs[0].shape
    for r in range(chunks):
        spread(perm, slice(r * LANES, (r + 1) * LANES), column(pos_ref[r : r + 1, :]))
    for g, back_ref in zip(far_first(blocks, len(back_refs)), back_refs):
        high, low = two(back_ref[...])
        columns, at = 0, slice(0, rows)
        if blocks:
            columns = (lax.axis_index("sub") ^ (g % blocks)) * width
            at = aligned((lax.axis_index("leaf") ^ lax.axis_index("rep") ^ (g // blocks)) * split, split, split)
        vals[aligned(columns, width, width), at] = high
        vals[aligned(columns + LANES, width, width), at] = low
    step = 256
    for s in range(rows // step):
        here = slice(s * step, (s + 1) * step)
        moved = nt(perm[here, :], vals[...])
        out_ref[here, :] = ridge * weights_ref[here, :] + moved[:, :LANES] + moved[:, LANES:]


def upper_levels(pack, skeleton_upper, my_leaf, trees, blocks, width):
    devices = trees * blocks
    level = blocks.bit_length() - 1
    offset = sum(devices >> step for step in range(1, level + 1))
    line = jnp.arange(LANES)[:, None]
    is_point, is_norm = line < DIM, (line >= DIM + 3) & (line < DIM + 6)
    is_coef = line >= LANES - width
    packs, own, stride = [], pack, 1
    while stride < trees:
        other = lax.ppermute(own, "leaf", [(i, i ^ stride) for i in range(trees)])
        packs.append(other)
        stride *= 2
        if stride < trees:
            second = (my_leaf // (stride // 2)) % 2 == 1
            pair = jnp.where(second, jnp.concatenate([other, own], 1), jnp.concatenate([own, other], 1))
            chosen = pair[:, skeleton_upper[offset + my_leaf // stride]]
            level += 1
            offset += devices >> level
            norms = jnp.sum(jnp.where(is_norm, pair, 0.0), axis=0)
            chosen_norms = jnp.sum(jnp.where(is_norm, chosen, 0.0), axis=0)
            inner = jnp.dot(
                jnp.where(is_point, pair, 0.0).T, jnp.where(is_point, chosen, 0.0), precision=highest
            )
            tile = jnp.exp(inner + norms[:, None] + chosen_norms[None])
            own = jnp.where(is_coef, jnp.dot(pair, tile, precision=highest), chosen)
    return jnp.stack(packs)


def body(points, weights, tree_slot, near_count, near_list, skeleton_base, skeleton_upper, far_use):
    blocks, trees, reps = lax.axis_size("sub"), lax.axis_size("leaf"), lax.axis_size("rep")
    devices = blocks * trees
    rows, columns = weights.shape
    low_levels = blocks.bit_length() - 1
    ups = trees.bit_length() - 1
    width = columns // blocks
    part = rows // trees
    per = part // blocks
    total = blocks * rows
    leaves = total // LEAF
    my_leaf = lax.axis_index("leaf")
    fine = trees == 2 and reps == 2 and per % LANES == 0
    layout = Layout(blocks, trees, rows, fine)
    split = part if fine else rows
    arrive = shaped((width, part), f32) if fine else shaped((width, total), f32)

    place, pos = pl.pallas_call(
        functools.partial(place_kernel, fine),
        out_shape=(shaped((PLACE_ROWS, split), f32), shaped((rows // LANES, LANES), f32)),
        in_specs=[spec()] * 4,
        out_specs=(spec(),) * 2,
        scratch_shapes=[vm((split // LOW * COORD, rows), bf16), vm((rows, LOW), bf16)],
        compiler_params=params(),
        name="sort_points",
    )(tree_slot.reshape(rows // LANES, LANES), points.T, skeleton_base, far_use)
    light = pl.pallas_call(
        light_kernel,
        out_shape=shaped((rows // split, columns, split), f32),
        in_specs=[spec()] * 2,
        out_specs=spec(),
        scratch_shapes=[vm((rows // LOW * LANES, rows), bf16), vm((rows, LOW), bf16)],
        compiler_params=params(),
        name="sort_weights",
    )(pos, weights)

    axes = ("leaf", "sub", "rep")

    def swap(value, step, other=0):
        pairs = []
        for leaf in range(trees):
            for sub in range(blocks):
                for core in range(reps):
                    to = ((leaf ^ core ^ other) * blocks + (sub ^ step)) * reps + core
                    pairs.append(((leaf * blocks + sub) * reps + core, to))
        return lax.ppermute(value, axes, pairs)

    def swap_all(values):
        return [swap(values[g], g % blocks, g // blocks) for g in far_first(blocks, len(values))]

    if fine:
        place = {0: swap(place, 0)}
        stride = blocks // 2
        while stride:
            for step in sorted(place):
                place[step | stride] = lax.ppermute(place[step], "sub", [(i, i ^ stride) for i in range(blocks)])
            stride //= 2
        place, light = lax.optimization_barrier((place, light))
        theirs = {step: lax.ppermute(one, "rep", [(0, 1), (1, 0)]) for step, one in place.items()}
        place = [place[step] for step in range(blocks)] + [theirs[step] for step in range(blocks)]
        light = light.reshape(devices, width, part)
        light = lax.all_to_all(light, ("leaf", "sub"), split_axis=0, concat_axis=0, tiled=True)
        small = []
    else:
        info = jnp.pad(far_use.astype(f32), ((FLAGS, 5 - far_use.shape[0]), (0, SK - far_use.shape[1])))
        small = [lax.all_gather(info.at[BASE].set(skeleton_base[0].astype(f32)), "sub", axis=0, tiled=False)]
        place = place.reshape(PLACE_ROWS, trees, part).transpose(1, 0, 2)
        place = lax.all_to_all(place, "leaf", split_axis=0, concat_axis=0, tiled=True)
        place = lax.all_gather(place, "sub", axis=0, tiled=False)
        place = place.transpose(1, 0, 2, 3).reshape(devices, PLACE_ROWS, blocks, per)
        place = [place.transpose(1, 2, 0, 3).reshape(PLACE_ROWS, total)]
        light = light.reshape(columns, trees, part).transpose(1, 0, 2).reshape(devices, width, part)
        light = lax.all_to_all(light, ("leaf", "sub"), split_axis=0, concat_axis=0, tiled=True)
        light = light.reshape(devices, width, blocks, per)
        light = light.transpose(1, 2, 0, 3).reshape(1, width, total)

    nodes = 2 * blocks - 1
    tree, feat_a, base, sk, upper_tiles, top, slots, info, tiles = pl.pallas_call(
        functools.partial(points_kernel, layout, trees),
        out_shape=(
            vm((COORD, total), bf16),
            pltpu.MemorySpace.HBM((total, FEAT), bf16),
            pltpu.MemorySpace.HBM((blocks, rows, SK), bf16),
            vm((nodes * SK, FEAT), bf16),
            vm((blocks - 1, 2 * SK, SK), f32),
            vm((SK, LANES), f32),
            vm((blocks, rows), f32),
            vm((blocks, 8, SK), f32),
            shaped((3, leaves * leaves + 3), jnp.int32),
        ),
        in_specs=[spec(SMEM)] * 2 + [spec()] * (1 + len(small) + layout.count),
        out_specs=(spec(), spec(pl.ANY), spec(pl.ANY)) + (spec(),) * 5 + (spec(SMEM),),
        scratch_shapes=[
            vm((rows // LOW * COORD, rows), bf16),
            vm((rows, LOW), bf16),
            vm((total, FEAT), bf16),
            vm((blocks, rows, SK), bf16),
            vm((COORD, nodes * SK), bf16),
            vm((FEAT, SK), bf16),
            pltpu.SemaphoreType.DMA((2, blocks)),
            pltpu.SMEM((leaves,), jnp.int32),
        ],
        compiler_params=params(40),
        name="tree_points",
    )(in_hbm(near_count), in_hbm(near_list[0]), in_hbm(skeleton_upper), *small, *place)

    tree_light, coefs, pack = pl.pallas_call(
        functools.partial(weights_kernel, layout),
        out_shape=(
            vm((width, total), bf16),
            vm((2 * width, nodes * SK), bf16),
            shaped((LANES, SK), f32),
        ),
        in_specs=[spec(pl.ANY)] + [spec()] * 4,
        out_specs=(spec(),) * 3,
        scratch_shapes=[
            vm((rows // LOW * width, rows), bf16),
            vm((rows, LOW), bf16),
            vm((blocks, rows, SK), bf16),
            pltpu.SemaphoreType.DMA((blocks,)),
        ],
        compiler_params=params(40),
        name="tree_weights",
    )(in_hbm(base), held(upper_tiles), held(top), held(slots), light)

    packs = upper_levels(pack, skeleton_upper, my_leaf, trees, blocks, width)

    near = pl.pallas_call(
        near_kernel,
        out_shape=vm((width, total), f32),
        in_specs=[spec(SMEM), spec(pl.ANY)] + [spec()] * 2,
        out_specs=spec(),
        scratch_shapes=[
            vm((total, FEAT), bf16),
            vm((FEAT, total), bf16),
            pltpu.SemaphoreType.DMA(()),
        ]
        + [vm((LEAF, LEAF // 2), f32)] * 4
        + [vm((LEAF, LEAF // 2), bf16)] * 4,
        compiler_params=params(40),
        name="near",
    )(in_hbm(tiles), in_hbm(feat_a), held(tree), held(tree_light))

    levels = low_levels + ups
    back = pl.pallas_call(
        functools.partial(far_kernel, layout, low_levels),
        out_shape=(arrive,) * layout.count,
        in_specs=[spec()] * 7,
        out_specs=(spec(),) * layout.count,
        scratch_shapes=[vm((levels * SK, FEAT), bf16), vm((2 * width, levels * SK), bf16), vm((LOW, rows), bf16), vm((FEAT, LEAF), bf16)],
        compiler_params=params(40),
        name="far",
    )(packs, *[held(one) for one in (slots, info, tree, sk, coefs, near)])

    if fine:
        back = swap_all(back)
    else:
        back = back[0].reshape(width, blocks, devices, per).transpose(2, 0, 1, 3).reshape(devices, width, part)
        back = lax.all_to_all(back, ("leaf", "sub"), split_axis=0, concat_axis=0, tiled=True)
        back = [back.reshape(trees, columns, part).transpose(1, 0, 2).reshape(columns, rows)]

    return pl.pallas_call(
        functools.partial(final_kernel, blocks if fine else 0),
        out_shape=shaped((rows, columns), f32),
        in_specs=[spec()] * (2 + layout.count),
        out_specs=spec(),
        scratch_shapes=[vm((rows, rows), bf16), vm((2 * LANES, rows), bf16)],
        compiler_params=params(40),
        name="to_input_order",
    )(pos, *back, weights)


def solution(mesh):
    in_specs = (
        P(("groups", "leaf", "sub"), None),
        P(("groups", "leaf", "sub"), "rep"),
        P(("groups", "leaf", "sub")),
        P(("groups", "leaf"), None),
        P(("groups", "leaf"), None, None),
        P(("groups", "leaf", "sub"), None),
        P("groups", None),
        P(("groups", "leaf", "sub"), None),
    )
    out_specs = P(("groups", "leaf", "sub"), "rep")
    return jax.shard_map(body, mesh=mesh, in_specs=in_specs, out_specs=out_specs, check_vma=False)
```

```python
import functools

import jax
import jax.numpy as jnp
from jax import lax
from jax.experimental import pallas as pl
from jax.experimental.pallas import tpu as pltpu
from jax.sharding import PartitionSpec as P

DIM = 64
LEAF = 512
SK = 128
LANES = 128
FEAT = 256
LOW = 256
COORD = 144

highest = lax.Precision.HIGHEST
point_scale = 0.25
ridge = 0.5
PLACE_ROWS = 72
TAIL = 64
SLOT, NORM, BASE, FLAGS = 0, 1, 2, 3
f32 = jnp.float32
bf16 = jnp.bfloat16
VMEM = pltpu.MemorySpace.VMEM
SMEM = pltpu.MemorySpace.SMEM


def spec(space=VMEM):
    return pl.BlockSpec(memory_space=space)


def params(mib=58):
    return pltpu.CompilerParams(vmem_limit_bytes=mib * 1024 * 1024)


def in_hbm(array):
    return pltpu.with_memory_space_constraint(array, pltpu.MemorySpace.HBM)


def held(array):
    return pltpu.with_memory_space_constraint(array, VMEM)


def vm(shape, dtype):
    return pltpu.VMEM(shape, dtype)


def shaped(shape, dtype):
    return jax.ShapeDtypeStruct(shape, dtype)


def nt(left, right):
    return lax.dot_general(left, right, (((1,), (1,)), ((), ())), preferred_element_type=f32)


def nn(left, right):
    return jnp.dot(left, right, preferred_element_type=f32)


def column(row):
    return jnp.transpose(jnp.broadcast_to(row, (LANES, LANES)))


def iota(shape, dim):
    return lax.broadcasted_iota(jnp.int32, shape, dim)


def onehot(mask):
    return jnp.where(mask, 1.0, 0.0).astype(bf16)


def two(value):
    high = value.astype(bf16)
    return high, (value - high.astype(f32)).astype(bf16)


def three(value):
    high = value.astype(bf16).astype(f32)
    mid = (value - high).astype(bf16).astype(f32)
    return high, mid, (value - high - mid).astype(bf16).astype(f32)


def lanes_of(blocks):
    return blocks[0] if len(blocks) == 1 else jnp.concatenate(blocks, 1)


def aligned(start, size, unit):
    return pl.ds(pl.multiple_of(start, unit), size)


def stack_two(value):
    high, low = two(value)
    return jnp.concatenate([high, low], 0)


def spread(perm, here, rank):
    lane = iota((LANES, LANES), 1).astype(f32)
    for c in range(perm.shape[1] // LANES):
        perm[here, c * LANES : (c + 1) * LANES] = onehot(lane + float(c * LANES) == rank)


def place_kernel(fine, slot_ref, points_ref, base_ref, flag_ref, place_ref, pos_ref, masked, low_hot):
    chunks = slot_ref.shape[0]
    slots = slot_ref[...]
    slot = slots.astype(f32)
    within = slots & (chunks * LANES - 1)
    high, low = (within >> 5).astype(f32), (within & 31).astype(f32)
    ranks = []
    for r in range(chunks):
        here = slice(r * LANES, (r + 1) * LANES)
        mine = column(slot[r : r + 1])
        before = jnp.zeros((LANES, LANES), f32)
        for c in range(chunks):
            before += jnp.where(slot[c : c + 1] < mine, 1.0, 0.0)
        rank = jnp.broadcast_to(jnp.sum(before, axis=1, keepdims=True), (LANES, LANES))
        ranks.append(jnp.transpose(rank)[0:1])
        pos_ref[r : r + 1, :] = ranks[-1]
        spread(low_hot, here, (rank.astype(jnp.int32) & (LOW - 1)).astype(f32))
    scaled = points_ref[...] * point_scale
    ph, plo = two(scaled)
    nh, nm, nl = three(-0.5 * jnp.sum(scaled * scaled, axis=0, keepdims=True))
    high, low = lanes_of([high[c : c + 1] for c in range(chunks)]), lanes_of([low[c : c + 1] for c in range(chunks)])
    sub = iota((16, chunks * LANES), 0)
    extra = jnp.where(sub == 0, high, jnp.where(sub == 1, low, 0.0))
    extra = jnp.where(sub == 2, nh, jnp.where(sub == 3, nm, jnp.where(sub == 4, nl, extra)))
    high_part = lanes_of(ranks).astype(jnp.int32) // LOW
    parts = place_ref.shape[1] // LOW
    first = (lax.axis_index("leaf") ^ lax.axis_index("rep")) * parts if fine else 0
    for h in range(parts):
        here = high_part == first + h
        masked[h * COORD : h * COORD + 64, :] = jnp.where(here, ph.astype(f32), 0.0).astype(bf16)
        masked[h * COORD + 64 : h * COORD + 128, :] = jnp.where(here, plo.astype(f32), 0.0).astype(bf16)
        masked[h * COORD + 128 : (h + 1) * COORD, :] = jnp.where(here, extra, 0.0).astype(bf16)
    placed = nn(masked[...], low_hot[...])
    tail = iota((PLACE_ROWS - TAIL, LOW), 0)
    for h in range(parts):
        at = slice(h * LOW, (h + 1) * LOW)
        moved = placed[h * COORD : (h + 1) * COORD]
        place_ref[0:TAIL, at] = moved[0:64] + moved[64:128]
        slot_row = moved[128:129] * 32.0 + moved[129:130]
        norm_row = moved[130:131] + moved[131:132] + moved[132:133]
        place_ref[TAIL:, at] = jnp.where(tail == SLOT, slot_row, jnp.where(tail == NORM, norm_row, 0.0))
    if fine:
        place_ref[TAIL + BASE : TAIL + BASE + 1, 0:SK] = base_ref[...].astype(f32)
        place_ref[TAIL + FLAGS : TAIL + FLAGS + flag_ref.shape[0], 0 : flag_ref.shape[1]] = flag_ref[...].astype(f32)


def light_kernel(pos_ref, weights_ref, light_ref, masked, low_hot):
    chunks, split = pos_ref.shape[0], light_ref.shape[2]
    low_part, high_part = parts_of(lanes_of([pos_ref[c : c + 1, :] for c in range(chunks)]))
    low_by_column(low_hot, low_part.astype(f32))
    for c in range(chunks):
        at = slice(c * LANES, (c + 1) * LANES)
        turned = jnp.transpose(weights_ref[at, :])
        for h in range(chunks * LANES // LOW):
            masked[h * LANES : (h + 1) * LANES, at] = jnp.where(high_part[:, at] == h, turned, 0.0).astype(bf16)
    placed = nn(masked[...], low_hot[...])
    for h in range(chunks * LANES // LOW):
        at = h * LOW
        light_ref[at // split, :, at % split : at % split + LOW] = placed[h * LANES : (h + 1) * LANES]


class Layout:
    def __init__(self, blocks, trees, rows, fine):
        self.blocks, self.rows, self.fine = blocks, rows, fine
        self.count = blocks * trees if fine else 1
        self.per = rows // self.count

    def lanes(self, index):
        return slice(index * self.per, (index + 1) * self.per)

    def message(self, group):
        if not self.fine:
            return 0
        leaf = lax.axis_index("leaf") ^ lax.axis_index("rep") ^ (group // self.blocks)
        return leaf * self.blocks + (lax.axis_index("sub") ^ (group % self.blocks))

    def gather(self, refs, index, part):
        return lanes_of([ref[part, self.lanes(index)] for ref in refs])

    def info(self, refs, small_ref, index):
        if not self.fine:
            return small_ref[index]
        core = lax.axis_index("rep")
        found = jnp.zeros((PLACE_ROWS - TAIL, SK), f32)
        for step in range(self.blocks):
            mine, theirs = refs[step][TAIL:, 0:SK], refs[self.blocks + step][TAIL:, 0:SK]
            here = jnp.where(core == 0, mine, theirs)
            found = jnp.where((lax.axis_index("sub") ^ step) == index, here, found)
        return found


def low_by_column(out, low):
    for c in range(out.shape[0] // LANES):
        at = slice(c * LANES, (c + 1) * LANES)
        spread(out, at, column(low[:, at]))


def parts_of(slots):
    slots = slots.astype(jnp.int32)
    return slots & (LOW - 1), slots // LOW


def feature_columns(out, at, tree):
    out[0:64, at] = tree[0:64].astype(bf16)
    out[64:128, at] = tree[0:64].astype(bf16)
    out[128:192, at] = tree[64:128].astype(bf16)
    out[192:208, at] = jnp.where(iota((16, tree.shape[1]), 0) < 8, tree[128:144].astype(f32), 0.0).astype(bf16)
    out[208:256, at] = jnp.zeros((48, tree.shape[1]), bf16)


def feature_rows(high, low, extra):
    first = jnp.transpose(jnp.concatenate([high, low], 0))
    second = jnp.transpose(jnp.concatenate([high, extra, jnp.zeros((56, high.shape[1]), f32)], 0))
    return first.astype(bf16), second.astype(bf16)


def list_tiles(count_ref, list_ref, tiles, times):
    every = count_ref.shape[1]

    def tally(leaf, filled):
        for other in range(every):
            times[other] = (leaf == other).astype(jnp.int32)

        def add(slot, carry):
            at = list_ref[leaf, slot]
            times[at] = times[at] + 1
            return carry

        lax.fori_loop(0, count_ref[0, leaf], add, 0)
        for other in range(every):
            tiles[0, filled] = leaf
            tiles[1, filled] = other
            tiles[2, filled] = times[other]
            filled = filled + (times[other] > 0).astype(jnp.int32)
        return filled

    filled = lax.fori_loop(0, every, tally, jnp.int32(0))
    for more in range(2):
        tiles[0, filled + more] = 0
        tiles[1, filled + more] = 0
    tiles[0, tiles.shape[1] - 1] = filled


def points_kernel(layout, trees, count_ref, list_ref, upper_ref, *refs):
    if not layout.fine:
        small_ref, refs = refs[0], refs[1:]
    else:
        small_ref = None
    place_refs, refs = refs[: layout.count], refs[layout.count :]
    tree_ref, a_hbm, base_hbm, sk_ref, upper_tiles_ref, top_ref, slot_ref, info_ref, tiles = refs[:9]
    masked, low_hot, a_ref, base_ref, sk_t, sk_bt, sems, times = refs[9:]
    blocks, rows = layout.blocks, layout.rows

    def keep(node, found):
        at = slice(node * SK, (node + 1) * SK)
        sk_t[:, at] = found.astype(bf16)
        sk_ref[at, 0:128], sk_ref[at, 128:256] = feature_rows(found[0:64], found[64:128], found[136:144])
        feature_columns(sk_bt, at, found)

    high_parts = rows // LOW
    infos = []
    for index in range(blocks):
        tail = layout.gather(place_refs, index, slice(TAIL, PLACE_ROWS))
        slots = tail[SLOT : SLOT + 1]
        slot_ref[index : index + 1, :] = slots
        infos.append(layout.info(place_refs, small_ref, index))
        info_ref[index] = infos[-1]
        low_part, high_part = parts_of(slots)
        low_by_column(low_hot.at[index], low_part.astype(f32))
        points = layout.gather(place_refs, index, slice(0, TAIL))
        high, low = two(points)
        nh, nm, nl = three(tail[NORM : NORM + 1])
        sub = iota((16, rows), 0)
        norms = jnp.where((sub == 3) | (sub == 8), nh, jnp.where((sub == 4) | (sub == 9), nm, nl))
        is_norm = ((sub >= 3) & (sub < 6)) | ((sub >= 8) & (sub < 11))
        is_one = (sub < 3) | ((sub >= 11) & (sub < 14))
        extra = jnp.where(is_norm, norms, jnp.where(is_one, 1.0, 0.0))
        for h in range(high_parts):
            here = high_part == h
            at = h * COORD
            masked[index, at : at + 64, :] = jnp.where(here, high.astype(f32), 0.0).astype(bf16)
            masked[index, at + 64 : at + 128, :] = jnp.where(here, low.astype(f32), 0.0).astype(bf16)
            masked[index, at + 128 : at + COORD, :] = jnp.where(here, extra, 0.0).astype(bf16)
    copies = []
    for index in range(blocks):
        placed = nn(masked[index], low_hot[index])
        for h in range(high_parts):
            part = placed[h * COORD : (h + 1) * COORD]
            at = slice(index * rows + h * LOW, index * rows + (h + 1) * LOW)
            tree_ref[:, at] = part.astype(bf16)
            a_ref[at, 0:128], a_ref[at, 128:256] = feature_rows(part[0:64], part[64:128], part[136:144])
        mine = slice(index * rows, (index + 1) * rows)
        copies.append(pltpu.make_async_copy(a_ref.at[mine], a_hbm.at[mine], sems.at[0, index]))
        copies[-1].start()
    for index in range(blocks):
        mine = slice(index * rows, (index + 1) * rows)
        picked = onehot(iota((rows, SK), 0) == infos[index][BASE : BASE + 1].astype(jnp.int32))
        keep(index, nn(tree_ref[:, mine], picked))
    for index in range(blocks):
        mine = slice(index * rows, (index + 1) * rows)
        base_ref[index] = jnp.exp(nn(a_ref[mine, :], sk_bt[:, index * SK : (index + 1) * SK])).astype(bf16)
        copies.append(pltpu.make_async_copy(base_ref.at[index], base_hbm.at[index], sems.at[1, index]))
        copies[-1].start()
    start, count, offset, total = 0, blocks, 0, blocks * trees
    while count > 1:
        nodes = count // 2
        for j in range(nodes):
            pair = slice((start + 2 * j) * SK, (start + 2 * j + 2) * SK)
            row = offset + lax.axis_index("leaf") * nodes + j
            picked = onehot(iota((2 * SK, SK), 0) == upper_ref[pl.ds(row, 1), :])
            here = start + count + j
            keep(here, nn(sk_t[:, pair], picked))
            upper_tiles_ref[here - blocks] = jnp.exp(nn(sk_ref[pair, :], sk_bt[:, here * SK : (here + 1) * SK]))
        total = total // 2
        offset = offset + total
        start, count = start + count, nodes
    found = sk_t[:, start * SK : (start + 1) * SK].astype(f32)
    top_ref[0:64, :] = found[0:64] + found[64:128]
    top_ref[64:72, :] = found[128:136]
    top_ref[72:128, :] = jnp.zeros((56, SK), f32)
    list_tiles(count_ref, list_ref, tiles, times)
    for copy in copies:
        copy.wait()


def weights_kernel(
    layout, base_hbm, upper_tiles_ref, top_ref, slot_ref, light_ref, w_ref, coef_ref, pack_ref, masked, low_hot, base_ref, sems
):
    blocks, rows = layout.blocks, layout.rows
    width = light_ref.shape[1]
    pack_ref[...] = top_ref[...]
    for index in range(blocks):
        pltpu.make_async_copy(base_hbm.at[index], base_ref.at[index], sems.at[index]).start()

    def keep(node, coef):
        coef_ref[:, node * SK : (node + 1) * SK] = stack_two(coef)
        pack_ref[LANES - width :, :] = coef

    for index in range(blocks):
        low_part, high_part = parts_of(slot_ref[index : index + 1, :])
        low_by_column(low_hot.at[index], low_part.astype(f32))
        light = [light_ref[layout.message(g), :, layout.lanes(index)] for g in range(layout.count)]
        light = lanes_of(light)
        for h in range(rows // LOW):
            masked[index, h * width : (h + 1) * width, :] = jnp.where(high_part == h, light, 0.0).astype(bf16)
    for index in range(blocks):
        placed = nn(masked[index], low_hot[index])
        for h in range(rows // LOW):
            at = index * rows + h * LOW
            w_ref[:, at : at + LOW] = placed[h * width : (h + 1) * width].astype(bf16)
    for index in range(blocks):
        pltpu.make_async_copy(base_hbm.at[index], base_ref.at[index], sems.at[index]).wait()
        keep(index, nn(w_ref[:, index * rows : (index + 1) * rows], base_ref[index]))
    start, count = 0, blocks
    while count > 1:
        for j in range(count // 2):
            pair = slice((start + 2 * j) * SK, (start + 2 * j + 2) * SK)
            here = start + count + j
            high, low = two(upper_tiles_ref[here - blocks])
            coef = nn(coef_ref[:, pair], high)
            keep(here, coef[:width] + coef[width:] + nn(coef_ref[0:width, pair], low))
        start, count = start + count, count // 2


def near_kernel(tiles, a_hbm, tree_ref, w_ref, acc, a_ref, bt_ref, sem, *halves):
    copy = pltpu.make_async_copy(a_hbm, a_ref, sem)
    copy.start()
    for leaf in range(bt_ref.shape[1] // LEAF):
        here = slice(leaf * LEAF, (leaf + 1) * LEAF)
        feature_columns(bt_ref, here, tree_ref[:, here])

    filled = tiles[0, tiles.shape[1] - 1]
    half = LEAF // 2
    acc[...] = jnp.zeros_like(acc)

    def target(tile, part):
        return aligned(tiles[0, tile] * LEAF + part * half, half, half)

    even, odd = halves[0:2], halves[2:4]
    even_tile, odd_tile = halves[4:6], halves[6:8]

    def exponents(tile, part):
        source = aligned(tiles[1, tile] * LEAF, LEAF, LEAF)
        return nn(a_ref[source, :], bt_ref[:, target(tile, part)])

    def add(tile, part, block):
        source = aligned(tiles[1, tile] * LEAF, LEAF, LEAF)
        acc[:, target(tile, part)] += tiles[2, tile].astype(f32) * nn(w_ref[:, source], block[part][...])

    def phase(tile, upcoming, ready, made, previous):
        for part in range(2):
            upcoming[part][...] = exponents(tile + 1, part)
            made[part][...] = jnp.exp(ready[part][...]).astype(bf16)
            add(tile - 1, part, previous)

    copy.wait()
    for part in range(2):
        even[part][...] = exponents(0, part)
        even_tile[part][...] = jnp.exp(even[part][...]).astype(bf16)
        odd[part][...] = exponents(1, part)

    def step(pair, carry):
        phase(2 * pair + 1, even, odd, odd_tile, even_tile)
        phase(2 * pair + 2, odd, even, even_tile, odd_tile)
        return carry

    lax.fori_loop(0, (filled - 1) // 2, step, 0)
    done = 2 * ((filled - 1) // 2)
    for part in range(2):
        add(done, part, even_tile)

    @pl.when(done + 1 < filled)
    def _():
        for part in range(2):
            odd_tile[part][...] = jnp.exp(odd[part][...]).astype(bf16)
            add(done + 1, part, odd_tile)


def far_kernel(layout, low_levels, pack_ref, slot_ref, info_ref, tree_ref, sk_ref, coef_ref, near_ref, *refs):
    out_refs, refs = refs[: layout.count], refs[layout.count :]
    tops, coefs, scaled, low_hot, bt_ref, sums, masked = refs[:7]
    powers, tiles = refs[7:9], refs[9:11]
    blocks, rows = layout.blocks, layout.rows
    ups, width = pack_ref.shape[0], out_refs[0].shape[0]
    levels = low_levels + ups
    per_block = rows // LEAF
    lane = iota((1, SK), 1)
    for up in range(ups):
        pack = pack_ref[up]
        high, low = two(pack[0:64])
        sub = iota((8, SK), 0)
        extra = jnp.where(sub == 0, pack[67:68], jnp.where(sub == 1, pack[68:69], pack[69:70]))
        extra = jnp.where(sub < 3, extra, jnp.where(sub < 6, 1.0, 0.0))
        at = slice((low_levels + up) * SK, (low_levels + up + 1) * SK)
        rows_of = feature_rows(high.astype(f32), low.astype(f32), extra)
        coef = stack_two(pack[LANES - width :])
        for index in range(blocks):
            tops[index, at, 0:128], tops[index, at, 128:256] = rows_of
            coefs[index, :, at] = coef
    for index in range(blocks):
        node, start, count = index, 0, blocks
        for level in range(low_levels):
            at = slice(level * SK, (level + 1) * SK)
            other = slice((start + (node ^ 1)) * SK, (start + (node ^ 1) + 1) * SK)
            tops[index, at, :] = sk_ref[other, :]
            coefs[index, :, at] = coef_ref[:, other]
            node, start, count = node // 2, start + count, count // 2
        for leaf in range(per_block):
            here = (index * per_block + leaf) * LEAF
            feature_columns(bt_ref, slice(here, here + LEAF), tree_ref[:, here : here + LEAF])
            flags = info_ref[index, FLAGS + leaf : FLAGS + leaf + 1, :]
            used = []
            for level in range(levels):
                flag = jnp.sum(jnp.where(lane == level, flags, 0.0), axis=1, keepdims=True)
                used.append(jnp.broadcast_to(flag, (1, SK)))
            used = jnp.concatenate(used, 1)
            scaled[index * per_block + leaf] = (coefs[index].astype(f32) * used).astype(bf16)

    def exponents(leaf):
        powers[leaf % 2][...] = nn(tops[leaf // per_block], bt_ref[:, leaf * LEAF : (leaf + 1) * LEAF])

    def product(leaf):
        here = slice(leaf * LEAF, (leaf + 1) * LEAF)
        far = nn(scaled[leaf], tiles[leaf % 2][...])
        sums[:, here] = near_ref[:, here] + far[:width] + far[width:]

    leaves = blocks * per_block
    exponents(0)
    for leaf in range(leaves):
        if leaf + 1 < leaves:
            exponents(leaf + 1)
        tiles[leaf % 2][...] = jnp.exp(powers[leaf % 2][...]).astype(bf16)
        if leaf:
            product(leaf - 1)
    product(leaves - 1)

    high_parts = []
    for index in range(blocks):
        low_part, high_part = parts_of(slot_ref[index : index + 1, :])
        high_parts.append(high_part)
        for c in range(rows // LANES):
            at = slice(c * LANES, (c + 1) * LANES)
            low_hot[index, :, at] = onehot(iota((LOW, LANES), 0) == low_part[:, at])
        for h in range(rows // LOW):
            at = index * rows + h * LOW
            masked[index, h * 2 * width : (h + 1) * 2 * width, :] = stack_two(sums[:, at : at + LOW])
    for index in range(blocks):
        moved = nn(masked[index], low_hot[index])
        result = jnp.zeros((2 * width, rows), f32)
        for h in range(rows // LOW):
            result = jnp.where(high_parts[index] == h, moved[h * 2 * width : (h + 1) * 2 * width], result)
        result = result[:width] + result[width:]
        for g, out_ref in enumerate(out_refs):
            out_ref[:, layout.lanes(index)] = result[:, g * layout.per : (g + 1) * layout.per]


def far_first(blocks, count):
    return sorted(range(count), key=lambda g: -((g % blocks) * 2 // blocks) if blocks else 0)


def final_kernel(blocks, pos_ref, *refs):
    back_refs, (weights_ref, out_ref, perm, vals) = refs[:-4], refs[-4:]
    chunks = pos_ref.shape[0]
    rows = chunks * LANES
    width, split = back_refs[0].shape
    for r in range(chunks):
        spread(perm, slice(r * LANES, (r + 1) * LANES), column(pos_ref[r : r + 1, :]))
    for g, back_ref in zip(far_first(blocks, len(back_refs)), back_refs):
        high, low = two(back_ref[...])
        columns, at = 0, slice(0, rows)
        if blocks:
            columns = (lax.axis_index("sub") ^ (g % blocks)) * width
            at = aligned((lax.axis_index("leaf") ^ lax.axis_index("rep") ^ (g // blocks)) * split, split, split)
        vals[aligned(columns, width, width), at] = high
        vals[aligned(columns + LANES, width, width), at] = low
    step = 256
    for s in range(rows // step):
        here = slice(s * step, (s + 1) * step)
        moved = nt(perm[here, :], vals[...])
        out_ref[here, :] = ridge * weights_ref[here, :] + moved[:, :LANES] + moved[:, LANES:]


def upper_levels(pack, skeleton_upper, my_leaf, trees, blocks, width):
    devices = trees * blocks
    level = blocks.bit_length() - 1
    offset = sum(devices >> step for step in range(1, level + 1))
    line = jnp.arange(LANES)[:, None]
    is_point, is_norm = line < DIM, (line >= DIM + 3) & (line < DIM + 6)
    is_coef = line >= LANES - width
    packs, own, stride = [], pack, 1
    while stride < trees:
        other = lax.ppermute(own, "leaf", [(i, i ^ stride) for i in range(trees)])
        packs.append(other)
        stride *= 2
        if stride < trees:
            second = (my_leaf // (stride // 2)) % 2 == 1
            pair = jnp.where(second, jnp.concatenate([other, own], 1), jnp.concatenate([own, other], 1))
            chosen = pair[:, skeleton_upper[offset + my_leaf // stride]]
            level += 1
            offset += devices >> level
            norms = jnp.sum(jnp.where(is_norm, pair, 0.0), axis=0)
            chosen_norms = jnp.sum(jnp.where(is_norm, chosen, 0.0), axis=0)
            inner = jnp.dot(
                jnp.where(is_point, pair, 0.0).T, jnp.where(is_point, chosen, 0.0), precision=highest
            )
            tile = jnp.exp(inner + norms[:, None] + chosen_norms[None])
            own = jnp.where(is_coef, jnp.dot(pair, tile, precision=highest), chosen)
    return jnp.stack(packs)


def body(points, weights, tree_slot, near_count, near_list, skeleton_base, skeleton_upper, far_use):
    blocks, trees, reps = lax.axis_size("sub"), lax.axis_size("leaf"), lax.axis_size("rep")
    devices = blocks * trees
    rows, columns = weights.shape
    low_levels = blocks.bit_length() - 1
    ups = trees.bit_length() - 1
    width = columns // blocks
    part = rows // trees
    per = part // blocks
    total = blocks * rows
    leaves = total // LEAF
    my_leaf = lax.axis_index("leaf")
    fine = trees == 2 and reps == 2 and per % LANES == 0
    layout = Layout(blocks, trees, rows, fine)
    split = part if fine else rows
    arrive = shaped((width, part), f32) if fine else shaped((width, total), f32)

    place, pos = pl.pallas_call(
        functools.partial(place_kernel, fine),
        out_shape=(shaped((PLACE_ROWS, split), f32), shaped((rows // LANES, LANES), f32)),
        in_specs=[spec()] * 4,
        out_specs=(spec(),) * 2,
        scratch_shapes=[vm((split // LOW * COORD, rows), bf16), vm((rows, LOW), bf16)],
        compiler_params=params(),
        name="sort_points",
    )(tree_slot.reshape(rows // LANES, LANES), points.T, skeleton_base, far_use)
    axes = ("leaf", "sub", "rep")

    def swap(value, step, other=0):
        pairs = []
        for leaf in range(trees):
            for sub in range(blocks):
                for core in range(reps):
                    to = ((leaf ^ core ^ other) * blocks + (sub ^ step)) * reps + core
                    pairs.append(((leaf * blocks + sub) * reps + core, to))
        return lax.ppermute(value, axes, pairs)

    def swap_all(values):
        return [swap(values[g], g % blocks, g // blocks) for g in far_first(blocks, len(values))]

    def sorted_light():
        return pl.pallas_call(
            light_kernel,
            out_shape=shaped((rows // split, columns, split), f32),
            in_specs=[spec()] * 2,
            out_specs=spec(),
            scratch_shapes=[vm((rows // LOW * LANES, rows), bf16), vm((rows, LOW), bf16)],
            compiler_params=params(),
            name="sort_weights",
        )(pos, weights)

    if fine:
        place = {0: swap(place, 0)}
        stride = blocks // 2
        while stride:
            for step in sorted(place):
                place[step | stride] = lax.ppermute(place[step], "sub", [(i, i ^ stride) for i in range(blocks)])
            stride //= 2
        place[blocks // 2], pos = lax.optimization_barrier((place[blocks // 2], pos))
        theirs = {step: lax.ppermute(one, "rep", [(0, 1), (1, 0)]) for step, one in place.items()}
        place = [place[step] for step in range(blocks)] + [theirs[step] for step in range(blocks)]
        light = sorted_light().reshape(devices, width, part)
        light = lax.all_to_all(light, ("leaf", "sub"), split_axis=0, concat_axis=0, tiled=True)
        small = []
    else:
        info = jnp.pad(far_use.astype(f32), ((FLAGS, 5 - far_use.shape[0]), (0, SK - far_use.shape[1])))
        small = [lax.all_gather(info.at[BASE].set(skeleton_base[0].astype(f32)), "sub", axis=0, tiled=False)]
        place = place.reshape(PLACE_ROWS, trees, part).transpose(1, 0, 2)
        place = lax.all_to_all(place, "leaf", split_axis=0, concat_axis=0, tiled=True)
        place = lax.all_gather(place, "sub", axis=0, tiled=False)
        place = place.transpose(1, 0, 2, 3).reshape(devices, PLACE_ROWS, blocks, per)
        place = [place.transpose(1, 2, 0, 3).reshape(PLACE_ROWS, total)]
        light = sorted_light().reshape(columns, trees, part).transpose(1, 0, 2).reshape(devices, width, part)
        light = lax.all_to_all(light, ("leaf", "sub"), split_axis=0, concat_axis=0, tiled=True)
        light = light.reshape(devices, width, blocks, per)
        light = light.transpose(1, 2, 0, 3).reshape(1, width, total)

    nodes = 2 * blocks - 1
    tree, feat_a, base, sk, upper_tiles, top, slots, info, tiles = pl.pallas_call(
        functools.partial(points_kernel, layout, trees),
        out_shape=(
            vm((COORD, total), bf16),
            pltpu.MemorySpace.HBM((total, FEAT), bf16),
            pltpu.MemorySpace.HBM((blocks, rows, SK), bf16),
            vm((nodes * SK, FEAT), bf16),
            vm((blocks - 1, 2 * SK, SK), f32),
            vm((SK, LANES), f32),
            vm((blocks, rows), f32),
            vm((blocks, 8, SK), f32),
            pltpu.MemorySpace.HBM((3, leaves * leaves + 3), jnp.int32),
        ),
        in_specs=[spec(SMEM)] * 2 + [spec()] * (1 + len(small) + layout.count),
        out_specs=(spec(), spec(pl.ANY), spec(pl.ANY)) + (spec(),) * 5 + (spec(SMEM),),
        scratch_shapes=[
            vm((blocks, rows // LOW * COORD, rows), bf16),
            vm((blocks, rows, LOW), bf16),
            vm((total, FEAT), bf16),
            vm((blocks, rows, SK), bf16),
            vm((COORD, nodes * SK), bf16),
            vm((FEAT, nodes * SK), bf16),
            pltpu.SemaphoreType.DMA((2, blocks)),
            pltpu.SMEM((leaves,), jnp.int32),
        ],
        compiler_params=params(40),
        name="tree_points",
    )(in_hbm(near_count), in_hbm(near_list[0]), in_hbm(skeleton_upper), *small, *place)

    tree_light, coefs, pack = pl.pallas_call(
        functools.partial(weights_kernel, layout),
        out_shape=(
            vm((width, total), bf16),
            vm((2 * width, nodes * SK), bf16),
            shaped((LANES, SK), f32),
        ),
        in_specs=[spec(pl.ANY)] + [spec()] * 4,
        out_specs=(spec(),) * 3,
        scratch_shapes=[
            vm((blocks, rows // LOW * width, rows), bf16),
            vm((blocks, rows, LOW), bf16),
            vm((blocks, rows, SK), bf16),
            pltpu.SemaphoreType.DMA((blocks,)),
        ],
        compiler_params=params(40),
        name="tree_weights",
    )(in_hbm(base), held(upper_tiles), held(top), held(slots), light)

    packs = upper_levels(pack, skeleton_upper, my_leaf, trees, blocks, width)

    near = pl.pallas_call(
        near_kernel,
        out_shape=vm((width, total), f32),
        in_specs=[spec(SMEM), spec(pl.ANY)] + [spec()] * 2,
        out_specs=spec(),
        scratch_shapes=[
            vm((total, FEAT), bf16),
            vm((FEAT, total), bf16),
            pltpu.SemaphoreType.DMA(()),
        ]
        + [vm((LEAF, LEAF // 2), f32)] * 4
        + [vm((LEAF, LEAF // 2), bf16)] * 4,
        compiler_params=params(40),
        name="near",
    )(in_hbm(tiles), in_hbm(feat_a), held(tree), held(tree_light))

    levels = low_levels + ups
    back = pl.pallas_call(
        functools.partial(far_kernel, layout, low_levels),
        out_shape=(arrive,) * layout.count,
        in_specs=[spec()] * 7,
        out_specs=(spec(),) * layout.count,
        scratch_shapes=[
            vm((blocks, levels * SK, FEAT), bf16),
            vm((blocks, 2 * width, levels * SK), bf16),
            vm((leaves, 2 * width, levels * SK), bf16),
            vm((blocks, LOW, rows), bf16),
            vm((FEAT, total), bf16),
            vm((width, total), f32),
            vm((blocks, rows // LOW * 2 * width, LOW), bf16),
        ]
        + [vm((levels * SK, LEAF), f32)] * 2
        + [vm((levels * SK, LEAF), bf16)] * 2,
        compiler_params=params(40),
        name="far",
    )(packs, *[held(one) for one in (slots, info, tree, sk, coefs, near)])

    if fine:
        back = swap_all(back)
    else:
        back = back[0].reshape(width, blocks, devices, per).transpose(2, 0, 1, 3).reshape(devices, width, part)
        back = lax.all_to_all(back, ("leaf", "sub"), split_axis=0, concat_axis=0, tiled=True)
        back = [back.reshape(trees, columns, part).transpose(1, 0, 2).reshape(columns, rows)]

    return pl.pallas_call(
        functools.partial(final_kernel, blocks if fine else 0),
        out_shape=shaped((rows, columns), f32),
        in_specs=[spec()] * (2 + layout.count),
        out_specs=spec(),
        scratch_shapes=[vm((rows, rows), bf16), vm((2 * LANES, rows), bf16)],
        compiler_params=params(40),
        name="to_input_order",
    )(pos, *back, weights)


def solution(mesh):
    in_specs = (
        P(("groups", "leaf", "sub"), None),
        P(("groups", "leaf", "sub"), "rep"),
        P(("groups", "leaf", "sub")),
        P(("groups", "leaf"), None),
        P(("groups", "leaf"), None, None),
        P(("groups", "leaf", "sub"), None),
        P("groups", None),
        P(("groups", "leaf", "sub"), None),
    )
    out_specs = P(("groups", "leaf", "sub"), "rep")
    return jax.shard_map(body, mesh=mesh, in_specs=in_specs, out_specs=out_specs, check_vma=False)
```

```python
import functools

import jax
import jax.numpy as jnp
from jax import lax
from jax.experimental import pallas as pl
from jax.experimental.pallas import tpu as pltpu
from jax.sharding import PartitionSpec as P

DIM = 64
LEAF = 512
SK = 128
LANES = 128
FEAT = 256
LOW = 256
COORD = 144

highest = lax.Precision.HIGHEST
point_scale = 0.25
ridge = 0.5
PLACE_ROWS = 72
TAIL = 64
SLOT, NORM, BASE, FLAGS = 0, 1, 2, 3
f32 = jnp.float32
bf16 = jnp.bfloat16
VMEM = pltpu.MemorySpace.VMEM
SMEM = pltpu.MemorySpace.SMEM


def spec(space=VMEM):
    return pl.BlockSpec(memory_space=space)


def params(mib=58):
    return pltpu.CompilerParams(vmem_limit_bytes=mib * 1024 * 1024)


def in_hbm(array):
    return pltpu.with_memory_space_constraint(array, pltpu.MemorySpace.HBM)


def held(array):
    return pltpu.with_memory_space_constraint(array, VMEM)


def vm(shape, dtype):
    return pltpu.VMEM(shape, dtype)


def shaped(shape, dtype):
    return jax.ShapeDtypeStruct(shape, dtype)


def nt(left, right):
    return lax.dot_general(left, right, (((1,), (1,)), ((), ())), preferred_element_type=f32)


def nn(left, right):
    return jnp.dot(left, right, preferred_element_type=f32)


def column(row):
    return jnp.transpose(jnp.broadcast_to(row, (LANES, LANES)))


def iota(shape, dim):
    return lax.broadcasted_iota(jnp.int32, shape, dim)


def onehot(mask):
    return jnp.where(mask, 1.0, 0.0).astype(bf16)


def two(value):
    high = value.astype(bf16)
    return high, (value - high.astype(f32)).astype(bf16)


def three(value):
    high = value.astype(bf16).astype(f32)
    mid = (value - high).astype(bf16).astype(f32)
    return high, mid, (value - high - mid).astype(bf16).astype(f32)


def lanes_of(blocks):
    return blocks[0] if len(blocks) == 1 else jnp.concatenate(blocks, 1)


def aligned(start, size, unit):
    return pl.ds(pl.multiple_of(start, unit), size)


def stack_two(value):
    high, low = two(value)
    return jnp.concatenate([high, low], 0)


def spread(perm, here, rank):
    lane = iota((LANES, LANES), 1).astype(f32)
    for c in range(perm.shape[1] // LANES):
        perm[here, c * LANES : (c + 1) * LANES] = onehot(lane + float(c * LANES) == rank)


def place_kernel(fine, slot_ref, points_ref, base_ref, flag_ref, place_ref, pos_ref, masked, low_hot):
    chunks = slot_ref.shape[0]
    slots = slot_ref[...]
    slot = slots.astype(f32)
    within = slots & (chunks * LANES - 1)
    high, low = (within >> 5).astype(f32), (within & 31).astype(f32)
    ranks = []
    for r in range(chunks):
        here = slice(r * LANES, (r + 1) * LANES)
        mine = column(slot[r : r + 1])
        before = jnp.zeros((LANES, LANES), f32)
        for c in range(chunks):
            before += jnp.where(slot[c : c + 1] < mine, 1.0, 0.0)
        rank = jnp.broadcast_to(jnp.sum(before, axis=1, keepdims=True), (LANES, LANES))
        ranks.append(jnp.transpose(rank)[0:1])
        pos_ref[r : r + 1, :] = ranks[-1]
        spread(low_hot, here, (rank.astype(jnp.int32) & (LOW - 1)).astype(f32))
    scaled = points_ref[...] * point_scale
    ph, plo = two(scaled)
    nh, nm, nl = three(-0.5 * jnp.sum(scaled * scaled, axis=0, keepdims=True))
    high, low = lanes_of([high[c : c + 1] for c in range(chunks)]), lanes_of([low[c : c + 1] for c in range(chunks)])
    sub = iota((16, chunks * LANES), 0)
    extra = jnp.where(sub == 0, high, jnp.where(sub == 1, low, 0.0))
    extra = jnp.where(sub == 2, nh, jnp.where(sub == 3, nm, jnp.where(sub == 4, nl, extra)))
    high_part = lanes_of(ranks).astype(jnp.int32) // LOW
    parts = place_ref.shape[1] // LOW
    first = (lax.axis_index("leaf") ^ lax.axis_index("rep")) * parts if fine else 0
    for h in range(parts):
        here = high_part == first + h
        masked[h * COORD : h * COORD + 64, :] = jnp.where(here, ph.astype(f32), 0.0).astype(bf16)
        masked[h * COORD + 64 : h * COORD + 128, :] = jnp.where(here, plo.astype(f32), 0.0).astype(bf16)
        masked[h * COORD + 128 : (h + 1) * COORD, :] = jnp.where(here, extra, 0.0).astype(bf16)
    placed = nn(masked[...], low_hot[...])
    tail = iota((PLACE_ROWS - TAIL, LOW), 0)
    for h in range(parts):
        at = slice(h * LOW, (h + 1) * LOW)
        moved = placed[h * COORD : (h + 1) * COORD]
        place_ref[0:TAIL, at] = moved[0:64] + moved[64:128]
        slot_row = moved[128:129] * 32.0 + moved[129:130]
        norm_row = moved[130:131] + moved[131:132] + moved[132:133]
        place_ref[TAIL:, at] = jnp.where(tail == SLOT, slot_row, jnp.where(tail == NORM, norm_row, 0.0))
    if fine:
        place_ref[TAIL + BASE : TAIL + BASE + 1, 0:SK] = base_ref[...].astype(f32)
        place_ref[TAIL + FLAGS : TAIL + FLAGS + flag_ref.shape[0], 0 : flag_ref.shape[1]] = flag_ref[...].astype(f32)


def light_kernel(pos_ref, weights_ref, light_ref, masked, low_hot):
    chunks, split = pos_ref.shape[0], light_ref.shape[2]
    low_part, high_part = parts_of(lanes_of([pos_ref[c : c + 1, :] for c in range(chunks)]))
    low_by_column(low_hot, low_part.astype(f32))
    for c in range(chunks):
        at = slice(c * LANES, (c + 1) * LANES)
        turned = jnp.transpose(weights_ref[at, :])
        for h in range(chunks * LANES // LOW):
            masked[h * LANES : (h + 1) * LANES, at] = jnp.where(high_part[:, at] == h, turned, 0.0).astype(bf16)
    placed = nn(masked[...], low_hot[...])
    for h in range(chunks * LANES // LOW):
        at = h * LOW
        light_ref[at // split, :, at % split : at % split + LOW] = placed[h * LANES : (h + 1) * LANES]


class Layout:
    def __init__(self, blocks, trees, rows, fine):
        self.blocks, self.rows, self.fine = blocks, rows, fine
        self.count = blocks * trees if fine else 1
        self.per = rows // self.count

    def lanes(self, index):
        return slice(index * self.per, (index + 1) * self.per)

    def message(self, group):
        if not self.fine:
            return 0
        leaf = lax.axis_index("leaf") ^ lax.axis_index("rep") ^ (group // self.blocks)
        return leaf * self.blocks + (lax.axis_index("sub") ^ (group % self.blocks))

    def gather(self, refs, index, part):
        return lanes_of([ref[part, self.lanes(index)] for ref in refs])

    def info(self, refs, small_ref, index):
        if not self.fine:
            return small_ref[index]
        core = lax.axis_index("rep")
        found = jnp.zeros((PLACE_ROWS - TAIL, SK), f32)
        for step in range(self.blocks):
            mine, theirs = refs[step][TAIL:, 0:SK], refs[self.blocks + step][TAIL:, 0:SK]
            here = jnp.where(core == 0, mine, theirs)
            found = jnp.where((lax.axis_index("sub") ^ step) == index, here, found)
        return found


def low_by_column(out, low):
    for c in range(out.shape[0] // LANES):
        at = slice(c * LANES, (c + 1) * LANES)
        spread(out, at, column(low[:, at]))


def parts_of(slots):
    slots = slots.astype(jnp.int32)
    return slots & (LOW - 1), slots // LOW


def feature_columns(out, at, tree):
    out[0:64, at] = tree[0:64].astype(bf16)
    out[64:128, at] = tree[0:64].astype(bf16)
    out[128:192, at] = tree[64:128].astype(bf16)
    out[192:208, at] = jnp.where(iota((16, tree.shape[1]), 0) < 8, tree[128:144].astype(f32), 0.0).astype(bf16)
    out[208:256, at] = jnp.zeros((48, tree.shape[1]), bf16)


def feature_rows(high, low, extra):
    first = jnp.transpose(jnp.concatenate([high, low], 0))
    second = jnp.transpose(jnp.concatenate([high, extra, jnp.zeros((56, high.shape[1]), f32)], 0))
    return first.astype(bf16), second.astype(bf16)


def list_tiles(count_ref, list_ref, tiles, times):
    every = count_ref.shape[1]

    def tally(leaf, filled):
        for other in range(every):
            times[other] = (leaf == other).astype(jnp.int32)

        def add(slot, carry):
            at = list_ref[leaf, slot]
            times[at] = times[at] + 1
            return carry

        lax.fori_loop(0, count_ref[0, leaf], add, 0)
        for other in range(every):
            tiles[0, filled] = leaf
            tiles[1, filled] = other
            tiles[2, filled] = times[other]
            filled = filled + (times[other] > 0).astype(jnp.int32)
        return filled

    filled = lax.fori_loop(0, every, tally, jnp.int32(0))
    for more in range(2):
        tiles[0, filled + more] = 0
        tiles[1, filled + more] = 0
    tiles[0, tiles.shape[1] - 1] = filled


def points_kernel(layout, trees, count_ref, list_ref, upper_ref, *refs):
    if not layout.fine:
        small_ref, refs = refs[0], refs[1:]
    else:
        small_ref = None
    place_refs, refs = refs[: layout.count], refs[layout.count :]
    tree_ref, a_hbm, base_hbm, sk_ref, upper_tiles_ref, top_ref, slot_ref, info_ref, tiles = refs[:9]
    masked, low_hot, a_ref, base_ref, sk_t, sk_bt, sems, times = refs[9:]
    blocks, rows = layout.blocks, layout.rows

    def keep(node, found):
        at = slice(node * SK, (node + 1) * SK)
        sk_t[:, at] = found.astype(bf16)
        sk_ref[at, 0:128], sk_ref[at, 128:256] = feature_rows(found[0:64], found[64:128], found[136:144])
        feature_columns(sk_bt, at, found)

    high_parts = rows // LOW
    infos = []
    for index in range(blocks):
        tail = layout.gather(place_refs, index, slice(TAIL, PLACE_ROWS))
        slots = tail[SLOT : SLOT + 1]
        slot_ref[index : index + 1, :] = slots
        infos.append(layout.info(place_refs, small_ref, index))
        info_ref[index] = infos[-1]
        low_part, high_part = parts_of(slots)
        low_by_column(low_hot.at[index], low_part.astype(f32))
        points = layout.gather(place_refs, index, slice(0, TAIL))
        high, low = two(points)
        nh, nm, nl = three(tail[NORM : NORM + 1])
        sub = iota((16, rows), 0)
        norms = jnp.where((sub == 3) | (sub == 8), nh, jnp.where((sub == 4) | (sub == 9), nm, nl))
        is_norm = ((sub >= 3) & (sub < 6)) | ((sub >= 8) & (sub < 11))
        is_one = (sub < 3) | ((sub >= 11) & (sub < 14))
        extra = jnp.where(is_norm, norms, jnp.where(is_one, 1.0, 0.0))
        for h in range(high_parts):
            here = high_part == h
            at = h * COORD
            masked[index, at : at + 64, :] = jnp.where(here, high.astype(f32), 0.0).astype(bf16)
            masked[index, at + 64 : at + 128, :] = jnp.where(here, low.astype(f32), 0.0).astype(bf16)
            masked[index, at + 128 : at + COORD, :] = jnp.where(here, extra, 0.0).astype(bf16)
    copies = []
    for index in range(blocks):
        placed = nn(masked[index], low_hot[index])
        for h in range(high_parts):
            part = placed[h * COORD : (h + 1) * COORD]
            at = slice(index * rows + h * LOW, index * rows + (h + 1) * LOW)
            tree_ref[:, at] = part.astype(bf16)
            a_ref[at, 0:128], a_ref[at, 128:256] = feature_rows(part[0:64], part[64:128], part[136:144])
        mine = slice(index * rows, (index + 1) * rows)
        copies.append(pltpu.make_async_copy(a_ref.at[mine], a_hbm.at[mine], sems.at[0, index]))
        copies[-1].start()
    for index in range(blocks):
        mine = slice(index * rows, (index + 1) * rows)
        picked = onehot(iota((rows, SK), 0) == infos[index][BASE : BASE + 1].astype(jnp.int32))
        keep(index, nn(tree_ref[:, mine], picked))
    for index in range(blocks):
        mine = slice(index * rows, (index + 1) * rows)
        base_ref[index] = jnp.exp(nn(a_ref[mine, :], sk_bt[:, index * SK : (index + 1) * SK])).astype(bf16)
        copies.append(pltpu.make_async_copy(base_ref.at[index], base_hbm.at[index], sems.at[1, index]))
        copies[-1].start()
    start, count, offset, total = 0, blocks, 0, blocks * trees
    while count > 1:
        nodes = count // 2
        for j in range(nodes):
            pair = slice((start + 2 * j) * SK, (start + 2 * j + 2) * SK)
            row = offset + lax.axis_index("leaf") * nodes + j
            picked = onehot(iota((2 * SK, SK), 0) == upper_ref[pl.ds(row, 1), :])
            here = start + count + j
            keep(here, nn(sk_t[:, pair], picked))
            upper_tiles_ref[here - blocks] = jnp.exp(nn(sk_ref[pair, :], sk_bt[:, here * SK : (here + 1) * SK]))
        total = total // 2
        offset = offset + total
        start, count = start + count, nodes
    found = sk_t[:, start * SK : (start + 1) * SK].astype(f32)
    top_ref[0:64, :] = found[0:64] + found[64:128]
    top_ref[64:72, :] = found[128:136]
    top_ref[72:128, :] = jnp.zeros((56, SK), f32)
    list_tiles(count_ref, list_ref, tiles, times)
    for copy in copies:
        copy.wait()


def weights_kernel(
    layout, base_hbm, upper_tiles_ref, top_ref, slot_ref, light_ref, w_ref, coef_ref, pack_ref, masked, low_hot, base_ref, sems
):
    blocks, rows = layout.blocks, layout.rows
    width = light_ref.shape[1]
    pack_ref[...] = top_ref[...]
    for index in range(blocks):
        pltpu.make_async_copy(base_hbm.at[index], base_ref.at[index], sems.at[index]).start()

    def keep(node, coef):
        coef_ref[:, node * SK : (node + 1) * SK] = stack_two(coef)
        pack_ref[LANES - width :, :] = coef

    for index in range(blocks):
        low_part, high_part = parts_of(slot_ref[index : index + 1, :])
        low_by_column(low_hot.at[index], low_part.astype(f32))
        light = [light_ref[layout.message(g), :, layout.lanes(index)] for g in range(layout.count)]
        light = lanes_of(light)
        for h in range(rows // LOW):
            masked[index, h * width : (h + 1) * width, :] = jnp.where(high_part == h, light, 0.0).astype(bf16)
    for index in range(blocks):
        placed = nn(masked[index], low_hot[index])
        for h in range(rows // LOW):
            at = index * rows + h * LOW
            w_ref[:, at : at + LOW] = placed[h * width : (h + 1) * width].astype(bf16)
    for index in range(blocks):
        pltpu.make_async_copy(base_hbm.at[index], base_ref.at[index], sems.at[index]).wait()
        keep(index, nn(w_ref[:, index * rows : (index + 1) * rows], base_ref[index]))
    start, count = 0, blocks
    while count > 1:
        for j in range(count // 2):
            pair = slice((start + 2 * j) * SK, (start + 2 * j + 2) * SK)
            here = start + count + j
            high, low = two(upper_tiles_ref[here - blocks])
            coef = nn(coef_ref[:, pair], high)
            keep(here, coef[:width] + coef[width:] + nn(coef_ref[0:width, pair], low))
        start, count = start + count, count // 2


def near_kernel(tiles, a_hbm, tree_ref, w_ref, acc, a_ref, bt_ref, sem, *halves):
    copy = pltpu.make_async_copy(a_hbm, a_ref, sem)
    copy.start()
    for leaf in range(bt_ref.shape[1] // LEAF):
        here = slice(leaf * LEAF, (leaf + 1) * LEAF)
        feature_columns(bt_ref, here, tree_ref[:, here])

    filled = tiles[0, tiles.shape[1] - 1]
    half = LEAF // 2
    acc[...] = jnp.zeros_like(acc)

    def target(tile, part):
        return aligned(tiles[0, tile] * LEAF + part * half, half, half)

    even, odd = halves[0:2], halves[2:4]
    even_tile, odd_tile = halves[4:6], halves[6:8]

    def exponents(tile, part):
        source = aligned(tiles[1, tile] * LEAF, LEAF, LEAF)
        return nn(a_ref[source, :], bt_ref[:, target(tile, part)])

    def add(tile, part, block):
        source = aligned(tiles[1, tile] * LEAF, LEAF, LEAF)
        acc[:, target(tile, part)] += tiles[2, tile].astype(f32) * nn(w_ref[:, source], block[part][...])

    def phase(tile, upcoming, ready, made, previous):
        for part in range(2):
            upcoming[part][...] = exponents(tile + 1, part)
            made[part][...] = jnp.exp(ready[part][...]).astype(bf16)
            add(tile - 1, part, previous)

    copy.wait()
    for part in range(2):
        even[part][...] = exponents(0, part)
        even_tile[part][...] = jnp.exp(even[part][...]).astype(bf16)
        odd[part][...] = exponents(1, part)

    def step(pair, carry):
        phase(2 * pair + 1, even, odd, odd_tile, even_tile)
        phase(2 * pair + 2, odd, even, even_tile, odd_tile)
        return carry

    lax.fori_loop(0, (filled - 1) // 2, step, 0)
    done = 2 * ((filled - 1) // 2)
    for part in range(2):
        add(done, part, even_tile)

    @pl.when(done + 1 < filled)
    def _():
        for part in range(2):
            odd_tile[part][...] = jnp.exp(odd[part][...]).astype(bf16)
            add(done + 1, part, odd_tile)


def far_kernel(layout, low_levels, pack_ref, slot_ref, info_ref, tree_ref, sk_ref, coef_ref, near_ref, *refs):
    out_refs, refs = refs[: layout.count], refs[layout.count :]
    tops, coefs, scaled, low_hot, bt_ref, sums, masked = refs[:7]
    powers, tiles = refs[7:9], refs[9:11]
    blocks, rows = layout.blocks, layout.rows
    ups, width = pack_ref.shape[0], out_refs[0].shape[0]
    levels = low_levels + ups
    per_block = rows // LEAF
    lane = iota((1, SK), 1)
    for up in range(ups):
        pack = pack_ref[up]
        high, low = two(pack[0:64])
        sub = iota((8, SK), 0)
        extra = jnp.where(sub == 0, pack[67:68], jnp.where(sub == 1, pack[68:69], pack[69:70]))
        extra = jnp.where(sub < 3, extra, jnp.where(sub < 6, 1.0, 0.0))
        at = slice((low_levels + up) * SK, (low_levels + up + 1) * SK)
        rows_of = feature_rows(high.astype(f32), low.astype(f32), extra)
        coef = stack_two(pack[LANES - width :])
        for index in range(blocks):
            tops[index, at, 0:128], tops[index, at, 128:256] = rows_of
            coefs[index, :, at] = coef
    for index in range(blocks):
        node, start, count = index, 0, blocks
        for level in range(low_levels):
            at = slice(level * SK, (level + 1) * SK)
            other = slice((start + (node ^ 1)) * SK, (start + (node ^ 1) + 1) * SK)
            tops[index, at, :] = sk_ref[other, :]
            coefs[index, :, at] = coef_ref[:, other]
            node, start, count = node // 2, start + count, count // 2
        for leaf in range(per_block):
            here = (index * per_block + leaf) * LEAF
            feature_columns(bt_ref, slice(here, here + LEAF), tree_ref[:, here : here + LEAF])
            flags = info_ref[index, FLAGS + leaf : FLAGS + leaf + 1, :]
            used = []
            for level in range(levels):
                flag = jnp.sum(jnp.where(lane == level, flags, 0.0), axis=1, keepdims=True)
                used.append(jnp.broadcast_to(flag, (1, SK)))
            used = jnp.concatenate(used, 1)
            scaled[index * per_block + leaf] = (coefs[index].astype(f32) * used).astype(bf16)

    def exponents(leaf):
        powers[leaf % 2][...] = nn(tops[leaf // per_block], bt_ref[:, leaf * LEAF : (leaf + 1) * LEAF])

    def product(leaf):
        here = slice(leaf * LEAF, (leaf + 1) * LEAF)
        far = nn(scaled[leaf], tiles[leaf % 2][...])
        sums[:, here] = near_ref[:, here] + far[:width] + far[width:]

    leaves = blocks * per_block
    exponents(0)
    for leaf in range(leaves):
        if leaf + 1 < leaves:
            exponents(leaf + 1)
        tiles[leaf % 2][...] = jnp.exp(powers[leaf % 2][...]).astype(bf16)
        if leaf:
            product(leaf - 1)
    product(leaves - 1)

    high_parts = []
    for index in range(blocks):
        low_part, high_part = parts_of(slot_ref[index : index + 1, :])
        high_parts.append(high_part)
        for c in range(rows // LANES):
            at = slice(c * LANES, (c + 1) * LANES)
            low_hot[index, :, at] = onehot(iota((LOW, LANES), 0) == low_part[:, at])
        for h in range(rows // LOW):
            at = index * rows + h * LOW
            masked[index, h * 2 * width : (h + 1) * 2 * width, :] = stack_two(sums[:, at : at + LOW])
    for index in range(blocks):
        moved = nn(masked[index], low_hot[index])
        result = jnp.zeros((2 * width, rows), f32)
        for h in range(rows // LOW):
            result = jnp.where(high_parts[index] == h, moved[h * 2 * width : (h + 1) * 2 * width], result)
        result = result[:width] + result[width:]
        for g, out_ref in enumerate(out_refs):
            out_ref[:, layout.lanes(index)] = result[:, g * layout.per : (g + 1) * layout.per]


def far_first(blocks, count):
    return sorted(range(count), key=lambda g: -((g % blocks) * 2 // blocks) if blocks else 0)


def final_kernel(blocks, pos_ref, *refs):
    back_refs, (weights_ref, out_ref, perm, vals) = refs[:-4], refs[-4:]
    chunks = pos_ref.shape[0]
    rows = chunks * LANES
    width, split = back_refs[0].shape
    for r in range(chunks):
        spread(perm, slice(r * LANES, (r + 1) * LANES), column(pos_ref[r : r + 1, :]))
    for g, back_ref in zip(far_first(blocks, len(back_refs)), back_refs):
        high, low = two(back_ref[...])
        columns, at = 0, slice(0, rows)
        if blocks:
            columns = (lax.axis_index("sub") ^ (g % blocks)) * width
            at = aligned((lax.axis_index("leaf") ^ lax.axis_index("rep") ^ (g // blocks)) * split, split, split)
        vals[aligned(columns, width, width), at] = high
        vals[aligned(columns + LANES, width, width), at] = low
    step = 256
    for s in range(rows // step):
        here = slice(s * step, (s + 1) * step)
        moved = nt(perm[here, :], vals[...])
        out_ref[here, :] = ridge * weights_ref[here, :] + moved[:, :LANES] + moved[:, LANES:]


def upper_levels(pack, skeleton_upper, my_leaf, trees, blocks, width):
    devices = trees * blocks
    level = blocks.bit_length() - 1
    offset = sum(devices >> step for step in range(1, level + 1))
    line = jnp.arange(LANES)[:, None]
    is_point, is_norm = line < DIM, (line >= DIM + 3) & (line < DIM + 6)
    is_coef = line >= LANES - width
    packs, own, stride = [], pack, 1
    while stride < trees:
        other = lax.ppermute(own, "leaf", [(i, i ^ stride) for i in range(trees)])
        packs.append(other)
        stride *= 2
        if stride < trees:
            second = (my_leaf // (stride // 2)) % 2 == 1
            pair = jnp.where(second, jnp.concatenate([other, own], 1), jnp.concatenate([own, other], 1))
            chosen = pair[:, skeleton_upper[offset + my_leaf // stride]]
            level += 1
            offset += devices >> level
            norms = jnp.sum(jnp.where(is_norm, pair, 0.0), axis=0)
            chosen_norms = jnp.sum(jnp.where(is_norm, chosen, 0.0), axis=0)
            inner = jnp.dot(
                jnp.where(is_point, pair, 0.0).T, jnp.where(is_point, chosen, 0.0), precision=highest
            )
            tile = jnp.exp(inner + norms[:, None] + chosen_norms[None])
            own = jnp.where(is_coef, jnp.dot(pair, tile, precision=highest), chosen)
    return jnp.stack(packs)


def body(points, weights, tree_slot, near_count, near_list, skeleton_base, skeleton_upper, far_use):
    blocks, trees, reps = lax.axis_size("sub"), lax.axis_size("leaf"), lax.axis_size("rep")
    devices = blocks * trees
    rows, columns = weights.shape
    low_levels = blocks.bit_length() - 1
    ups = trees.bit_length() - 1
    width = columns // blocks
    part = rows // trees
    per = part // blocks
    total = blocks * rows
    leaves = total // LEAF
    my_leaf = lax.axis_index("leaf")
    fine = trees == 2 and reps == 2 and per % LANES == 0
    layout = Layout(blocks, trees, rows, fine)
    split = part if fine else rows
    arrive = shaped((width, part), f32) if fine else shaped((width, total), f32)

    place, pos = pl.pallas_call(
        functools.partial(place_kernel, fine),
        out_shape=(shaped((PLACE_ROWS, split), f32), shaped((rows // LANES, LANES), f32)),
        in_specs=[spec()] * 4,
        out_specs=(spec(),) * 2,
        scratch_shapes=[vm((split // LOW * COORD, rows), bf16), vm((rows, LOW), bf16)],
        compiler_params=params(),
        name="sort_points",
    )(tree_slot.reshape(rows // LANES, LANES), points.T, skeleton_base, far_use)
    axes = ("leaf", "sub", "rep")

    def swap(value, step, other=0):
        pairs = []
        for leaf in range(trees):
            for sub in range(blocks):
                for core in range(reps):
                    to = ((leaf ^ core ^ other) * blocks + (sub ^ step)) * reps + core
                    pairs.append(((leaf * blocks + sub) * reps + core, to))
        return lax.ppermute(value, axes, pairs)

    def swap_all(values):
        return [swap(values[g], g % blocks, g // blocks) for g in far_first(blocks, len(values))]

    def sorted_light():
        return pl.pallas_call(
            light_kernel,
            out_shape=shaped((rows // split, columns, split), f32),
            in_specs=[spec()] * 2,
            out_specs=spec(),
            scratch_shapes=[vm((rows // LOW * LANES, rows), bf16), vm((rows, LOW), bf16)],
            compiler_params=params(),
            name="sort_weights",
        )(pos, weights)

    if fine:
        place = {0: swap(place, 0)}
        stride = blocks // 2
        while stride:
            for step in sorted(place):
                place[step | stride] = lax.ppermute(place[step], "sub", [(i, i ^ stride) for i in range(blocks)])
            stride //= 2
        light = sorted_light()
        place, light = lax.optimization_barrier((place, light))
        theirs = {step: lax.ppermute(one, "rep", [(0, 1), (1, 0)]) for step, one in place.items()}
        place = [place[step] for step in range(blocks)] + [theirs[step] for step in range(blocks)]
        light = light.reshape(devices, width, part)
        light = lax.all_to_all(light, ("leaf", "sub"), split_axis=0, concat_axis=0, tiled=True)
        small = []
    else:
        info = jnp.pad(far_use.astype(f32), ((FLAGS, 5 - far_use.shape[0]), (0, SK - far_use.shape[1])))
        small = [lax.all_gather(info.at[BASE].set(skeleton_base[0].astype(f32)), "sub", axis=0, tiled=False)]
        place = place.reshape(PLACE_ROWS, trees, part).transpose(1, 0, 2)
        place = lax.all_to_all(place, "leaf", split_axis=0, concat_axis=0, tiled=True)
        place = lax.all_gather(place, "sub", axis=0, tiled=False)
        place = place.transpose(1, 0, 2, 3).reshape(devices, PLACE_ROWS, blocks, per)
        place = [place.transpose(1, 2, 0, 3).reshape(PLACE_ROWS, total)]
        light = sorted_light().reshape(columns, trees, part).transpose(1, 0, 2).reshape(devices, width, part)
        light = lax.all_to_all(light, ("leaf", "sub"), split_axis=0, concat_axis=0, tiled=True)
        light = light.reshape(devices, width, blocks, per)
        light = light.transpose(1, 2, 0, 3).reshape(1, width, total)

    nodes = 2 * blocks - 1
    tree, feat_a, base, sk, upper_tiles, top, slots, info, tiles = pl.pallas_call(
        functools.partial(points_kernel, layout, trees),
        out_shape=(
            vm((COORD, total), bf16),
            pltpu.MemorySpace.HBM((total, FEAT), bf16),
            pltpu.MemorySpace.HBM((blocks, rows, SK), bf16),
            vm((nodes * SK, FEAT), bf16),
            vm((blocks - 1, 2 * SK, SK), f32),
            vm((SK, LANES), f32),
            vm((blocks, rows), f32),
            vm((blocks, 8, SK), f32),
            pltpu.MemorySpace.HBM((3, leaves * leaves + 3), jnp.int32),
        ),
        in_specs=[spec(SMEM)] * 2 + [spec()] * (1 + len(small) + layout.count),
        out_specs=(spec(), spec(pl.ANY), spec(pl.ANY)) + (spec(),) * 5 + (spec(SMEM),),
        scratch_shapes=[
            vm((blocks, rows // LOW * COORD, rows), bf16),
            vm((blocks, rows, LOW), bf16),
            vm((total, FEAT), bf16),
            vm((blocks, rows, SK), bf16),
            vm((COORD, nodes * SK), bf16),
            vm((FEAT, nodes * SK), bf16),
            pltpu.SemaphoreType.DMA((2, blocks)),
            pltpu.SMEM((leaves,), jnp.int32),
        ],
        compiler_params=params(40),
        name="tree_points",
    )(in_hbm(near_count), in_hbm(near_list[0]), in_hbm(skeleton_upper), *small, *place)

    tree_light, coefs, pack = pl.pallas_call(
        functools.partial(weights_kernel, layout),
        out_shape=(
            vm((width, total), bf16),
            vm((2 * width, nodes * SK), bf16),
            shaped((LANES, SK), f32),
        ),
        in_specs=[spec(pl.ANY)] + [spec()] * 4,
        out_specs=(spec(),) * 3,
        scratch_shapes=[
            vm((blocks, rows // LOW * width, rows), bf16),
            vm((blocks, rows, LOW), bf16),
            vm((blocks, rows, SK), bf16),
            pltpu.SemaphoreType.DMA((blocks,)),
        ],
        compiler_params=params(40),
        name="tree_weights",
    )(in_hbm(base), held(upper_tiles), held(top), held(slots), light)

    packs = upper_levels(pack, skeleton_upper, my_leaf, trees, blocks, width)

    near = pl.pallas_call(
        near_kernel,
        out_shape=vm((width, total), f32),
        in_specs=[spec(SMEM), spec(pl.ANY)] + [spec()] * 2,
        out_specs=spec(),
        scratch_shapes=[
            vm((total, FEAT), bf16),
            vm((FEAT, total), bf16),
            pltpu.SemaphoreType.DMA(()),
        ]
        + [vm((LEAF, LEAF // 2), f32)] * 4
        + [vm((LEAF, LEAF // 2), bf16)] * 4,
        compiler_params=params(40),
        name="near",
    )(in_hbm(tiles), in_hbm(feat_a), held(tree), held(tree_light))

    levels = low_levels + ups
    back = pl.pallas_call(
        functools.partial(far_kernel, layout, low_levels),
        out_shape=(arrive,) * layout.count,
        in_specs=[spec()] * 7,
        out_specs=(spec(),) * layout.count,
        scratch_shapes=[
            vm((blocks, levels * SK, FEAT), bf16),
            vm((blocks, 2 * width, levels * SK), bf16),
            vm((leaves, 2 * width, levels * SK), bf16),
            vm((blocks, LOW, rows), bf16),
            vm((FEAT, total), bf16),
            vm((width, total), f32),
            vm((blocks, rows // LOW * 2 * width, LOW), bf16),
        ]
        + [vm((levels * SK, LEAF), f32)] * 2
        + [vm((levels * SK, LEAF), bf16)] * 2,
        compiler_params=params(40),
        name="far",
    )(packs, *[held(one) for one in (slots, info, tree, sk, coefs, near)])

    if fine:
        back = swap_all(back)
    else:
        back = back[0].reshape(width, blocks, devices, per).transpose(2, 0, 1, 3).reshape(devices, width, part)
        back = lax.all_to_all(back, ("leaf", "sub"), split_axis=0, concat_axis=0, tiled=True)
        back = [back.reshape(trees, columns, part).transpose(1, 0, 2).reshape(columns, rows)]

    return pl.pallas_call(
        functools.partial(final_kernel, blocks if fine else 0),
        out_shape=shaped((rows, columns), f32),
        in_specs=[spec()] * (2 + layout.count),
        out_specs=spec(),
        scratch_shapes=[vm((rows, rows), bf16), vm((2 * LANES, rows), bf16)],
        compiler_params=params(40),
        name="to_input_order",
    )(pos, *back, weights)


def solution(mesh):
    in_specs = (
        P(("groups", "leaf", "sub"), None),
        P(("groups", "leaf", "sub"), "rep"),
        P(("groups", "leaf", "sub")),
        P(("groups", "leaf"), None),
        P(("groups", "leaf"), None, None),
        P(("groups", "leaf", "sub"), None),
        P("groups", None),
        P(("groups", "leaf", "sub"), None),
    )
    out_specs = P(("groups", "leaf", "sub"), "rep")
    return jax.shard_map(body, mesh=mesh, in_specs=in_specs, out_specs=out_specs, check_vma=False)
```

```python
import functools

import jax
import jax.numpy as jnp
from jax import lax
from jax.experimental import pallas as pl
from jax.experimental.pallas import tpu as pltpu
from jax.sharding import PartitionSpec as P

DIM = 64
LEAF = 512
SK = 128
LANES = 128
FEAT = 256
LOW = 256
COORD = 144

highest = lax.Precision.HIGHEST
point_scale = 0.25
ridge = 0.5
PLACE_ROWS = 72
TAIL = 64
SLOT, NORM, BASE, FLAGS = 0, 1, 2, 3
f32 = jnp.float32
bf16 = jnp.bfloat16
VMEM = pltpu.MemorySpace.VMEM
SMEM = pltpu.MemorySpace.SMEM


def spec(space=VMEM):
    return pl.BlockSpec(memory_space=space)


def params(mib=58):
    return pltpu.CompilerParams(vmem_limit_bytes=mib * 1024 * 1024)


def in_hbm(array):
    return pltpu.with_memory_space_constraint(array, pltpu.MemorySpace.HBM)


def held(array):
    return pltpu.with_memory_space_constraint(array, VMEM)


def vm(shape, dtype):
    return pltpu.VMEM(shape, dtype)


def shaped(shape, dtype):
    return jax.ShapeDtypeStruct(shape, dtype)


def nt(left, right):
    return lax.dot_general(left, right, (((1,), (1,)), ((), ())), preferred_element_type=f32)


def nn(left, right):
    return jnp.dot(left, right, preferred_element_type=f32)


def column(row):
    return jnp.transpose(jnp.broadcast_to(row, (LANES, LANES)))


def iota(shape, dim):
    return lax.broadcasted_iota(jnp.int32, shape, dim)


def onehot(mask):
    return jnp.where(mask, 1.0, 0.0).astype(bf16)


def two(value):
    high = value.astype(bf16)
    return high, (value - high.astype(f32)).astype(bf16)


def three(value):
    high = value.astype(bf16).astype(f32)
    mid = (value - high).astype(bf16).astype(f32)
    return high, mid, (value - high - mid).astype(bf16).astype(f32)


def lanes_of(blocks):
    return blocks[0] if len(blocks) == 1 else jnp.concatenate(blocks, 1)


def aligned(start, size, unit):
    return pl.ds(pl.multiple_of(start, unit), size)


def stack_two(value):
    high, low = two(value)
    return jnp.concatenate([high, low], 0)


def spread(perm, here, rank):
    lane = iota((LANES, LANES), 1).astype(f32)
    for c in range(perm.shape[1] // LANES):
        perm[here, c * LANES : (c + 1) * LANES] = onehot(lane + float(c * LANES) == rank)


def place_kernel(fine, slot_ref, points_ref, base_ref, flag_ref, place_ref, pos_ref, masked, low_hot):
    chunks = slot_ref.shape[0]
    slots = slot_ref[...]
    slot = slots.astype(f32)
    within = slots & (chunks * LANES - 1)
    high, low = (within >> 5).astype(f32), (within & 31).astype(f32)
    ranks = []
    for r in range(chunks):
        here = slice(r * LANES, (r + 1) * LANES)
        mine = column(slot[r : r + 1])
        before = jnp.zeros((LANES, LANES), f32)
        for c in range(chunks):
            before += jnp.where(slot[c : c + 1] < mine, 1.0, 0.0)
        rank = jnp.broadcast_to(jnp.sum(before, axis=1, keepdims=True), (LANES, LANES))
        ranks.append(jnp.transpose(rank)[0:1])
        pos_ref[r : r + 1, :] = ranks[-1]
        spread(low_hot, here, (rank.astype(jnp.int32) & (LOW - 1)).astype(f32))
    scaled = points_ref[...] * point_scale
    ph, plo = two(scaled)
    nh, nm, nl = three(-0.5 * jnp.sum(scaled * scaled, axis=0, keepdims=True))
    high, low = lanes_of([high[c : c + 1] for c in range(chunks)]), lanes_of([low[c : c + 1] for c in range(chunks)])
    sub = iota((16, chunks * LANES), 0)
    extra = jnp.where(sub == 0, high, jnp.where(sub == 1, low, 0.0))
    extra = jnp.where(sub == 2, nh, jnp.where(sub == 3, nm, jnp.where(sub == 4, nl, extra)))
    high_part = lanes_of(ranks).astype(jnp.int32) // LOW
    parts = place_ref.shape[1] // LOW
    first = (lax.axis_index("leaf") ^ lax.axis_index("rep")) * parts if fine else 0
    for h in range(parts):
        here = high_part == first + h
        masked[h * COORD : h * COORD + 64, :] = jnp.where(here, ph.astype(f32), 0.0).astype(bf16)
        masked[h * COORD + 64 : h * COORD + 128, :] = jnp.where(here, plo.astype(f32), 0.0).astype(bf16)
        masked[h * COORD + 128 : (h + 1) * COORD, :] = jnp.where(here, extra, 0.0).astype(bf16)
    placed = nn(masked[...], low_hot[...])
    tail = iota((PLACE_ROWS - TAIL, LOW), 0)
    for h in range(parts):
        at = slice(h * LOW, (h + 1) * LOW)
        moved = placed[h * COORD : (h + 1) * COORD]
        place_ref[0:TAIL, at] = moved[0:64] + moved[64:128]
        slot_row = moved[128:129] * 32.0 + moved[129:130]
        norm_row = moved[130:131] + moved[131:132] + moved[132:133]
        place_ref[TAIL:, at] = jnp.where(tail == SLOT, slot_row, jnp.where(tail == NORM, norm_row, 0.0))
    if fine:
        place_ref[TAIL + BASE : TAIL + BASE + 1, 0:SK] = base_ref[...].astype(f32)
        place_ref[TAIL + FLAGS : TAIL + FLAGS + flag_ref.shape[0], 0 : flag_ref.shape[1]] = flag_ref[...].astype(f32)


def light_kernel(pos_ref, weights_ref, light_ref, masked, low_hot):
    chunks, split = pos_ref.shape[0], light_ref.shape[2]
    low_part, high_part = parts_of(lanes_of([pos_ref[c : c + 1, :] for c in range(chunks)]))
    low_by_column(low_hot, low_part.astype(f32))
    for c in range(chunks):
        at = slice(c * LANES, (c + 1) * LANES)
        turned = jnp.transpose(weights_ref[at, :])
        for h in range(chunks * LANES // LOW):
            masked[h * LANES : (h + 1) * LANES, at] = jnp.where(high_part[:, at] == h, turned, 0.0).astype(bf16)
    placed = nn(masked[...], low_hot[...])
    for h in range(chunks * LANES // LOW):
        at = h * LOW
        light_ref[at // split, :, at % split : at % split + LOW] = placed[h * LANES : (h + 1) * LANES]


class Layout:
    def __init__(self, blocks, trees, rows, fine):
        self.blocks, self.rows, self.fine = blocks, rows, fine
        self.count = blocks * trees if fine else 1
        self.per = rows // self.count
        self.halves = 2 if fine else 1
        self.span = LEAF // self.halves

    def core(self):
        return lax.axis_index("rep") if self.fine else 0

    def lanes(self, index):
        return slice(index * self.per, (index + 1) * self.per)

    def message(self, group):
        if not self.fine:
            return 0
        leaf = lax.axis_index("leaf") ^ lax.axis_index("rep") ^ (group // self.blocks)
        return leaf * self.blocks + (lax.axis_index("sub") ^ (group % self.blocks))

    def gather(self, refs, index, part):
        return lanes_of([ref[part, self.lanes(index)] for ref in refs])

    def info(self, refs, small_ref, index):
        if not self.fine:
            return small_ref[index]
        core = lax.axis_index("rep")
        found = jnp.zeros((PLACE_ROWS - TAIL, SK), f32)
        for step in range(self.blocks):
            mine, theirs = refs[step][TAIL:, 0:SK], refs[self.blocks + step][TAIL:, 0:SK]
            here = jnp.where(core == 0, mine, theirs)
            found = jnp.where((lax.axis_index("sub") ^ step) == index, here, found)
        return found


def low_by_column(out, low):
    for c in range(out.shape[0] // LANES):
        at = slice(c * LANES, (c + 1) * LANES)
        spread(out, at, column(low[:, at]))


def parts_of(slots):
    slots = slots.astype(jnp.int32)
    return slots & (LOW - 1), slots // LOW


def feature_columns(out, at, tree):
    out[0:64, at] = tree[0:64].astype(bf16)
    out[64:128, at] = tree[0:64].astype(bf16)
    out[128:192, at] = tree[64:128].astype(bf16)
    out[192:208, at] = jnp.where(iota((16, tree.shape[1]), 0) < 8, tree[128:144].astype(f32), 0.0).astype(bf16)
    out[208:256, at] = jnp.zeros((48, tree.shape[1]), bf16)


def feature_rows(high, low, extra):
    first = jnp.transpose(jnp.concatenate([high, low], 0))
    second = jnp.transpose(jnp.concatenate([high, extra, jnp.zeros((56, high.shape[1]), f32)], 0))
    return first.astype(bf16), second.astype(bf16)


def list_tiles(count_ref, list_ref, tiles, times):
    every = count_ref.shape[1]

    def tally(leaf, filled):
        for other in range(every):
            times[other] = (leaf == other).astype(jnp.int32)

        def add(slot, carry):
            at = list_ref[leaf, slot]
            times[at] = times[at] + 1
            return carry

        lax.fori_loop(0, count_ref[0, leaf], add, 0)
        for other in range(every):
            tiles[0, filled] = leaf
            tiles[1, filled] = other
            tiles[2, filled] = times[other]
            filled = filled + (times[other] > 0).astype(jnp.int32)
        return filled

    filled = lax.fori_loop(0, every, tally, jnp.int32(0))
    for more in range(2):
        tiles[0, filled + more] = 0
        tiles[1, filled + more] = 0
    tiles[0, tiles.shape[1] - 1] = filled


def points_kernel(layout, trees, count_ref, list_ref, upper_ref, *refs):
    if not layout.fine:
        small_ref, refs = refs[0], refs[1:]
    else:
        small_ref = None
    place_refs, refs = refs[: layout.count], refs[layout.count :]
    tree_ref, a_hbm, base_hbm, sk_ref, upper_tiles_ref, top_ref, slot_ref, info_ref, tiles = refs[:9]
    masked, low_hot, a_ref, base_ref, sk_t, sk_bt, sems, times = refs[9:]
    blocks, rows = layout.blocks, layout.rows

    def keep(node, found):
        at = slice(node * SK, (node + 1) * SK)
        sk_t[:, at] = found.astype(bf16)
        sk_ref[at, 0:128], sk_ref[at, 128:256] = feature_rows(found[0:64], found[64:128], found[136:144])
        feature_columns(sk_bt, at, found)

    high_parts = rows // LOW
    infos = []
    for index in range(blocks):
        tail = layout.gather(place_refs, index, slice(TAIL, PLACE_ROWS))
        slots = tail[SLOT : SLOT + 1]
        slot_ref[index : index + 1, :] = slots
        infos.append(layout.info(place_refs, small_ref, index))
        info_ref[index] = infos[-1]
        low_part, high_part = parts_of(slots)
        low_by_column(low_hot.at[index], low_part.astype(f32))
        points = layout.gather(place_refs, index, slice(0, TAIL))
        high, low = two(points)
        nh, nm, nl = three(tail[NORM : NORM + 1])
        sub = iota((16, rows), 0)
        norms = jnp.where((sub == 3) | (sub == 8), nh, jnp.where((sub == 4) | (sub == 9), nm, nl))
        is_norm = ((sub >= 3) & (sub < 6)) | ((sub >= 8) & (sub < 11))
        is_one = (sub < 3) | ((sub >= 11) & (sub < 14))
        extra = jnp.where(is_norm, norms, jnp.where(is_one, 1.0, 0.0))
        for h in range(high_parts):
            here = high_part == h
            at = h * COORD
            masked[index, at : at + 64, :] = jnp.where(here, high.astype(f32), 0.0).astype(bf16)
            masked[index, at + 64 : at + 128, :] = jnp.where(here, low.astype(f32), 0.0).astype(bf16)
            masked[index, at + 128 : at + COORD, :] = jnp.where(here, extra, 0.0).astype(bf16)
    copies = []
    for index in range(blocks):
        placed = nn(masked[index], low_hot[index])
        for h in range(high_parts):
            part = placed[h * COORD : (h + 1) * COORD]
            at = slice(index * rows + h * LOW, index * rows + (h + 1) * LOW)
            tree_ref[:, at] = part.astype(bf16)
            a_ref[at, 0:128], a_ref[at, 128:256] = feature_rows(part[0:64], part[64:128], part[136:144])
        mine = slice(index * rows, (index + 1) * rows)
        copies.append(pltpu.make_async_copy(a_ref.at[mine], a_hbm.at[mine], sems.at[0, index]))
        copies[-1].start()
    for index in range(blocks):
        mine = slice(index * rows, (index + 1) * rows)
        picked = onehot(iota((rows, SK), 0) == infos[index][BASE : BASE + 1].astype(jnp.int32))
        keep(index, nn(tree_ref[:, mine], picked))
    for index in range(blocks):
        mine = slice(index * rows, (index + 1) * rows)
        base_ref[index] = jnp.exp(nn(a_ref[mine, :], sk_bt[:, index * SK : (index + 1) * SK])).astype(bf16)
        copies.append(pltpu.make_async_copy(base_ref.at[index], base_hbm.at[index], sems.at[1, index]))
        copies[-1].start()
    start, count, offset, total = 0, blocks, 0, blocks * trees
    while count > 1:
        nodes = count // 2
        for j in range(nodes):
            pair = slice((start + 2 * j) * SK, (start + 2 * j + 2) * SK)
            row = offset + lax.axis_index("leaf") * nodes + j
            picked = onehot(iota((2 * SK, SK), 0) == upper_ref[pl.ds(row, 1), :])
            here = start + count + j
            keep(here, nn(sk_t[:, pair], picked))
            upper_tiles_ref[here - blocks] = jnp.exp(nn(sk_ref[pair, :], sk_bt[:, here * SK : (here + 1) * SK]))
        total = total // 2
        offset = offset + total
        start, count = start + count, nodes
    found = sk_t[:, start * SK : (start + 1) * SK].astype(f32)
    top_ref[0:64, :] = found[0:64] + found[64:128]
    top_ref[64:72, :] = found[128:136]
    list_tiles(count_ref, list_ref, tiles, times)
    for copy in copies:
        copy.wait()


def weights_kernel(layout, base_hbm, upper_tiles_ref, top_ref, slot_ref, *refs):
    light_refs, refs = refs[: layout.halves], refs[layout.halves :]
    w_ref, coef_ref, pack_ref, masked, low_hot, base_ref, sems = refs
    blocks, rows = layout.blocks, layout.rows
    each = light_refs[0].shape[1]
    width = each * layout.halves
    pack_ref[0:PLACE_ROWS, :] = top_ref[...]
    for index in range(blocks):
        pltpu.make_async_copy(base_hbm.at[index], base_ref.at[index], sems.at[index]).start()

    def keep(node, coef):
        coef_ref[:, node * SK : (node + 1) * SK] = stack_two(coef)
        pack_ref[PLACE_ROWS:, :] = coef

    for index in range(blocks):
        low_part, high_part = parts_of(slot_ref[index : index + 1, :])
        low_by_column(low_hot.at[index], low_part.astype(f32))
        for half, light_ref in enumerate(light_refs):
            light = lanes_of([light_ref[layout.message(g), :, layout.lanes(index)] for g in range(layout.count)])
            for h in range(rows // LOW):
                at = h * width + half * each
                masked[index, at : at + each, :] = jnp.where(high_part == h, light, 0.0).astype(bf16)
    for index in range(blocks):
        placed = nn(masked[index], low_hot[index])
        for h in range(rows // LOW):
            at = index * rows + h * LOW
            w_ref[:, at : at + LOW] = placed[h * width : (h + 1) * width].astype(bf16)
    for index in range(blocks):
        pltpu.make_async_copy(base_hbm.at[index], base_ref.at[index], sems.at[index]).wait()
        keep(index, nn(w_ref[:, index * rows : (index + 1) * rows], base_ref[index]))
    start, count = 0, blocks
    while count > 1:
        for j in range(count // 2):
            pair = slice((start + 2 * j) * SK, (start + 2 * j + 2) * SK)
            here = start + count + j
            high, low = two(upper_tiles_ref[here - blocks])
            coef = nn(coef_ref[:, pair], high)
            keep(here, coef[:width] + coef[width:] + nn(coef_ref[0:width, pair], low))
        start, count = start + count, count // 2


def near_kernel(layout, tiles, a_hbm, tree_ref, w_ref, acc, a_ref, bt_ref, sem, *halves):
    copy = pltpu.make_async_copy(a_hbm, a_ref, sem)
    copy.start()
    span, half = layout.span, LEAF // 2
    parts = range(span // half)
    for leaf in range(bt_ref.shape[1] // span):
        here = aligned(leaf * LEAF + layout.core() * span, span, span)
        feature_columns(bt_ref, slice(leaf * span, (leaf + 1) * span), tree_ref[:, here])
    filled = tiles[0, tiles.shape[1] - 1]
    acc[...] = jnp.zeros_like(acc)

    def target(tile, part):
        return aligned(tiles[0, tile] * span + part * half, half, half)

    even, odd = halves[0:2], halves[2:4]
    even_tile, odd_tile = halves[4:6], halves[6:8]

    def exponents(tile, part):
        source = aligned(tiles[1, tile] * LEAF, LEAF, LEAF)
        return nn(a_ref[source, :], bt_ref[:, target(tile, part)])

    def add(tile, part, block):
        source = aligned(tiles[1, tile] * LEAF, LEAF, LEAF)
        acc[:, target(tile, part)] += tiles[2, tile].astype(f32) * nn(w_ref[:, source], block[part][...])

    def phase(tile, upcoming, ready, made, previous):
        for part in parts:
            upcoming[part][...] = exponents(tile + 1, part)
            made[part][...] = jnp.exp(ready[part][...]).astype(bf16)
            add(tile - 1, part, previous)

    copy.wait()
    for part in parts:
        even[part][...] = exponents(0, part)
        even_tile[part][...] = jnp.exp(even[part][...]).astype(bf16)
        odd[part][...] = exponents(1, part)

    def step(pair, carry):
        phase(2 * pair + 1, even, odd, odd_tile, even_tile)
        phase(2 * pair + 2, odd, even, even_tile, odd_tile)
        return carry

    lax.fori_loop(0, (filled - 1) // 2, step, 0)
    done = 2 * ((filled - 1) // 2)
    for part in parts:
        add(done, part, even_tile)

    @pl.when(done + 1 < filled)
    def _():
        for part in parts:
            odd_tile[part][...] = jnp.exp(odd[part][...]).astype(bf16)
            add(done + 1, part, odd_tile)


def far_kernel(layout, low_levels, pack_ref, slot_ref, info_ref, tree_ref, sk_ref, coef_ref, near_ref, *refs):
    out_refs, refs = refs[: layout.halves], refs[layout.halves :]
    tops, coefs, scaled, low_hot, bt_ref, sums, masked = refs[:7]
    powers, tiles = refs[7:9], refs[9:11]
    blocks, rows = layout.blocks, layout.rows
    ups, width = pack_ref.shape[0], near_ref.shape[0]
    levels = low_levels + ups
    span, core = layout.span, layout.core()
    per_block = rows // LEAF
    lane = iota((1, SK), 1)
    for up in range(ups):
        pack = pack_ref[up]
        high, low = two(pack[0:64])
        sub = iota((8, SK), 0)
        extra = jnp.where(sub == 0, pack[67:68], jnp.where(sub == 1, pack[68:69], pack[69:70]))
        extra = jnp.where(sub < 3, extra, jnp.where(sub < 6, 1.0, 0.0))
        at = slice((low_levels + up) * SK, (low_levels + up + 1) * SK)
        rows_of = feature_rows(high.astype(f32), low.astype(f32), extra)
        coef = stack_two(pack[PLACE_ROWS:])
        for index in range(blocks):
            tops[index, at, 0:128], tops[index, at, 128:256] = rows_of
            coefs[index, :, at] = coef
    for index in range(blocks):
        node, start, count = index, 0, blocks
        for level in range(low_levels):
            at = slice(level * SK, (level + 1) * SK)
            other = slice((start + (node ^ 1)) * SK, (start + (node ^ 1) + 1) * SK)
            tops[index, at, :] = sk_ref[other, :]
            coefs[index, :, at] = coef_ref[:, other]
            node, start, count = node // 2, start + count, count // 2
        for leaf in range(per_block):
            here = (index * per_block + leaf) * LEAF
            at = slice(here // layout.halves, here // layout.halves + span)
            feature_columns(bt_ref, at, tree_ref[:, aligned(here + core * span, span, span)])
            flags = info_ref[index, FLAGS + leaf : FLAGS + leaf + 1, :]
            used = []
            for level in range(levels):
                flag = jnp.sum(jnp.where(lane == level, flags, 0.0), axis=1, keepdims=True)
                used.append(jnp.broadcast_to(flag, (1, SK)))
            used = jnp.concatenate(used, 1)
            scaled[index * per_block + leaf] = (coefs[index].astype(f32) * used).astype(bf16)

    def exponents(leaf):
        powers[leaf % 2][...] = nn(tops[leaf // per_block], bt_ref[:, leaf * span : (leaf + 1) * span])

    def product(leaf):
        here = slice(leaf * span, (leaf + 1) * span)
        far = nn(scaled[leaf], tiles[leaf % 2][...])
        sums[:, here] = near_ref[:, here] + far[:width] + far[width:]

    leaves = blocks * per_block
    exponents(0)
    for leaf in range(leaves):
        if leaf + 1 < leaves:
            exponents(leaf + 1)
        tiles[leaf % 2][...] = jnp.exp(powers[leaf % 2][...]).astype(bf16)
        if leaf:
            product(leaf - 1)
    product(leaves - 1)

    high_parts = []
    pieces = rows // LOW // layout.halves
    for index in range(blocks):
        low_part, high_part = parts_of(slot_ref[index : index + 1, :])
        high_parts.append(high_part)
        for c in range(rows // LANES):
            at = slice(c * LANES, (c + 1) * LANES)
            low_hot[index, :, at] = onehot(iota((LOW, LANES), 0) == low_part[:, at])
        for k in range(pieces):
            at = (index * pieces + k) * LOW
            masked[index, k * 2 * width : (k + 1) * 2 * width, :] = stack_two(sums[:, at : at + LOW])
    for index in range(blocks):
        moved = nn(masked[index], low_hot[index])
        result = jnp.zeros((2 * width, rows), f32)
        for k in range(pieces):
            here = high_parts[index] == k * layout.halves + core
            result = jnp.where(here, moved[k * 2 * width : (k + 1) * 2 * width], result)
        result = result[:width] + result[width:]
        if not layout.fine:
            out_refs[0][0, :, layout.lanes(index)] = result
            continue
        for g in range(layout.count):
            out_ref = out_refs[g // blocks]
            out_ref[g % blocks, :, layout.lanes(index)] = result[:, g * layout.per : (g + 1) * layout.per]


def add_kernel(kept_ref, got_ref, *out_refs):
    half = kept_ref.shape[1] // 2
    for step, out_ref in enumerate(out_refs):
        out_ref[0:half, :] = kept_ref[step, 0:half, :] + got_ref[step, half:, :]
        out_ref[half:, :] = kept_ref[step, half:, :] + got_ref[step, 0:half, :]


def final_kernel(blocks, pos_ref, *refs):
    back_refs, (weights_ref, out_ref, perm, vals) = refs[:-4], refs[-4:]
    chunks = pos_ref.shape[0]
    rows = chunks * LANES
    width, split = back_refs[0].shape
    width = LANES // blocks if blocks else width
    for r in range(chunks):
        spread(perm, slice(r * LANES, (r + 1) * LANES), column(pos_ref[r : r + 1, :]))
    for g, back_ref in enumerate(back_refs):
        columns, at = 0, slice(0, rows)
        value = back_ref[...]
        if blocks:
            columns = (lax.axis_index("sub") ^ (g % blocks)) * width
            at = aligned((lax.axis_index("leaf") ^ lax.axis_index("rep") ^ (g // blocks)) * split, split, split)
            value = value[0:width] if g < blocks else value[width:]
        high, low = two(value)
        vals[aligned(columns, width, width), at] = high
        vals[aligned(columns + LANES, width, width), at] = low
    step = 256
    for s in range(rows // step):
        here = slice(s * step, (s + 1) * step)
        moved = nt(perm[here, :], vals[...])
        out_ref[here, :] = ridge * weights_ref[here, :] + moved[:, :LANES] + moved[:, LANES:]


def upper_levels(pack, skeleton_upper, my_leaf, trees, blocks):
    devices = trees * blocks
    level = blocks.bit_length() - 1
    offset = sum(devices >> step for step in range(1, level + 1))
    line = jnp.arange(pack.shape[0])[:, None]
    is_point, is_norm = line < DIM, (line >= DIM + 3) & (line < DIM + 6)
    is_coef = line >= PLACE_ROWS
    packs, own, stride = [], pack, 1
    while stride < trees:
        other = lax.ppermute(own, "leaf", [(i, i ^ stride) for i in range(trees)])
        packs.append(other)
        stride *= 2
        if stride < trees:
            second = (my_leaf // (stride // 2)) % 2 == 1
            pair = jnp.where(second, jnp.concatenate([other, own], 1), jnp.concatenate([own, other], 1))
            chosen = pair[:, skeleton_upper[offset + my_leaf // stride]]
            level += 1
            offset += devices >> level
            norms = jnp.sum(jnp.where(is_norm, pair, 0.0), axis=0)
            chosen_norms = jnp.sum(jnp.where(is_norm, chosen, 0.0), axis=0)
            inner = jnp.dot(
                jnp.where(is_point, pair, 0.0).T, jnp.where(is_point, chosen, 0.0), precision=highest
            )
            tile = jnp.exp(inner + norms[:, None] + chosen_norms[None])
            own = jnp.where(is_coef, jnp.dot(pair, tile, precision=highest), chosen)
    return jnp.stack(packs)


def body(points, weights, tree_slot, near_count, near_list, skeleton_base, skeleton_upper, far_use):
    blocks, trees, reps = lax.axis_size("sub"), lax.axis_size("leaf"), lax.axis_size("rep")
    devices = blocks * trees
    rows, columns = weights.shape
    low_levels = blocks.bit_length() - 1
    ups = trees.bit_length() - 1
    width = columns // blocks
    part = rows // trees
    per = part // blocks
    total = blocks * rows
    leaves = total // LEAF
    my_leaf = lax.axis_index("leaf")
    fine = trees == 2 and reps == 2 and per % LANES == 0
    layout = Layout(blocks, trees, rows, fine)
    split = part if fine else rows
    cols = width * layout.halves

    place, pos = pl.pallas_call(
        functools.partial(place_kernel, fine),
        out_shape=(shaped((PLACE_ROWS, split), f32), shaped((rows // LANES, LANES), f32)),
        in_specs=[spec()] * 4,
        out_specs=(spec(),) * 2,
        scratch_shapes=[vm((split // LOW * COORD, rows), bf16), vm((rows, LOW), bf16)],
        compiler_params=params(),
        name="sort_points",
    )(tree_slot.reshape(rows // LANES, LANES), points.T, skeleton_base, far_use)
    axes = ("leaf", "sub", "rep")

    def swap(value, step, other=0):
        pairs = []
        for leaf in range(trees):
            for sub in range(blocks):
                for core in range(reps):
                    to = ((leaf ^ core ^ other) * blocks + (sub ^ step)) * reps + core
                    pairs.append(((leaf * blocks + sub) * reps + core, to))
        return lax.ppermute(value, axes, pairs)

    def other_core(value):
        return lax.ppermute(value, "rep", [(0, 1), (1, 0)])

    def sorted_light():
        return pl.pallas_call(
            light_kernel,
            out_shape=shaped((rows // split, columns, split), f32),
            in_specs=[spec()] * 2,
            out_specs=spec(),
            scratch_shapes=[vm((rows // LOW * LANES, rows), bf16), vm((rows, LOW), bf16)],
            compiler_params=params(),
            name="sort_weights",
        )(pos, weights)

    if fine:
        place = {0: swap(place, 0)}
        stride = blocks // 2
        while stride:
            for step in sorted(place):
                place[step | stride] = lax.ppermute(place[step], "sub", [(i, i ^ stride) for i in range(blocks)])
            stride //= 2
        light = sorted_light()
        place, light = lax.optimization_barrier((place, light))
        theirs = {step: other_core(one) for step, one in place.items()}
        place = [place[step] for step in range(blocks)] + [theirs[step] for step in range(blocks)]
        light = light.reshape(devices, width, part)
        light = lax.all_to_all(light, ("leaf", "sub"), split_axis=0, concat_axis=0, tiled=True)
        light = [light, other_core(light)]
        small = []
    else:
        info = jnp.pad(far_use.astype(f32), ((FLAGS, 5 - far_use.shape[0]), (0, SK - far_use.shape[1])))
        small = [lax.all_gather(info.at[BASE].set(skeleton_base[0].astype(f32)), "sub", axis=0, tiled=False)]
        place = place.reshape(PLACE_ROWS, trees, part).transpose(1, 0, 2)
        place = lax.all_to_all(place, "leaf", split_axis=0, concat_axis=0, tiled=True)
        place = lax.all_gather(place, "sub", axis=0, tiled=False)
        place = place.transpose(1, 0, 2, 3).reshape(devices, PLACE_ROWS, blocks, per)
        place = [place.transpose(1, 2, 0, 3).reshape(PLACE_ROWS, total)]
        light = sorted_light().reshape(columns, trees, part).transpose(1, 0, 2).reshape(devices, width, part)
        light = lax.all_to_all(light, ("leaf", "sub"), split_axis=0, concat_axis=0, tiled=True)
        light = light.reshape(devices, width, blocks, per)
        light = [light.transpose(1, 2, 0, 3).reshape(1, width, total)]

    nodes = 2 * blocks - 1
    tree, feat_a, base, sk, upper_tiles, top, slots, info, tiles = pl.pallas_call(
        functools.partial(points_kernel, layout, trees),
        out_shape=(
            vm((COORD, total), bf16),
            pltpu.MemorySpace.HBM((total, FEAT), bf16),
            pltpu.MemorySpace.HBM((blocks, rows, SK), bf16),
            vm((nodes * SK, FEAT), bf16),
            vm((blocks - 1, 2 * SK, SK), f32),
            vm((PLACE_ROWS, SK), f32),
            vm((blocks, rows), f32),
            vm((blocks, 8, SK), f32),
            pltpu.MemorySpace.HBM((3, leaves * leaves + 3), jnp.int32),
        ),
        in_specs=[spec(SMEM)] * 2 + [spec()] * (1 + len(small) + layout.count),
        out_specs=(spec(), spec(pl.ANY), spec(pl.ANY)) + (spec(),) * 5 + (spec(SMEM),),
        scratch_shapes=[
            vm((blocks, rows // LOW * COORD, rows), bf16),
            vm((blocks, rows, LOW), bf16),
            vm((total, FEAT), bf16),
            vm((blocks, rows, SK), bf16),
            vm((COORD, nodes * SK), bf16),
            vm((FEAT, nodes * SK), bf16),
            pltpu.SemaphoreType.DMA((2, blocks)),
            pltpu.SMEM((leaves,), jnp.int32),
        ],
        compiler_params=params(40),
        name="tree_points",
    )(in_hbm(near_count), in_hbm(near_list[0]), in_hbm(skeleton_upper), *small, *place)

    tree_light, coefs, pack = pl.pallas_call(
        functools.partial(weights_kernel, layout),
        out_shape=(
            vm((cols, total), bf16),
            vm((2 * cols, nodes * SK), bf16),
            shaped((PLACE_ROWS + cols, SK), f32),
        ),
        in_specs=[spec(pl.ANY)] + [spec()] * (3 + layout.halves),
        out_specs=(spec(),) * 3,
        scratch_shapes=[
            vm((blocks, rows // LOW * cols, rows), bf16),
            vm((blocks, rows, LOW), bf16),
            vm((blocks, rows, SK), bf16),
            pltpu.SemaphoreType.DMA((blocks,)),
        ],
        compiler_params=params(40),
        name="tree_weights",
    )(in_hbm(base), held(upper_tiles), held(top), held(slots), *light)

    packs = upper_levels(pack, skeleton_upper, my_leaf, trees, blocks)

    near = pl.pallas_call(
        functools.partial(near_kernel, layout),
        out_shape=vm((cols, total // layout.halves), f32),
        in_specs=[spec(SMEM), spec(pl.ANY)] + [spec()] * 2,
        out_specs=spec(),
        scratch_shapes=[
            vm((total, FEAT), bf16),
            vm((FEAT, total // layout.halves), bf16),
            pltpu.SemaphoreType.DMA(()),
        ]
        + [vm((LEAF, LEAF // 2), f32)] * 4
        + [vm((LEAF, LEAF // 2), bf16)] * 4,
        compiler_params=params(40),
        name="near",
    )(in_hbm(tiles), in_hbm(feat_a), held(tree), held(tree_light))

    levels = low_levels + ups
    back = pl.pallas_call(
        functools.partial(far_kernel, layout, low_levels),
        out_shape=(shaped((layout.count // layout.halves, cols, total // layout.count), f32),) * layout.halves,
        in_specs=[spec()] * 7,
        out_specs=(spec(),) * layout.halves,
        scratch_shapes=[
            vm((blocks, levels * SK, FEAT), bf16),
            vm((blocks, 2 * cols, levels * SK), bf16),
            vm((leaves, 2 * cols, levels * SK), bf16),
            vm((blocks, LOW, rows), bf16),
            vm((FEAT, total // layout.halves), bf16),
            vm((cols, total // layout.halves), f32),
            vm((blocks, rows // LOW // layout.halves * 2 * cols, LOW), bf16),
        ]
        + [vm((levels * SK, layout.span), f32)] * 2
        + [vm((levels * SK, layout.span), bf16)] * 2,
        compiler_params=params(40),
        name="far",
    )(packs, *[held(one) for one in (slots, info, tree, sk, coefs, near)])

    if fine:
        kept, sent = back
        sums = pl.pallas_call(
            add_kernel,
            out_shape=(shaped((cols, part), f32),) * blocks,
            in_specs=[spec()] * 2,
            out_specs=(spec(),) * blocks,
            compiler_params=params(40),
            name="add_cores",
        )(kept, other_core(sent))
        back = {step: swap(sums[step], step) for step in reversed(range(blocks))}
        back = [back[step] for step in range(blocks)]
        back = back + [other_core(one) for one in back]
    else:
        back = back[0].reshape(cols, blocks, devices, per).transpose(2, 0, 1, 3).reshape(devices, width, part)
        back = lax.all_to_all(back, ("leaf", "sub"), split_axis=0, concat_axis=0, tiled=True)
        back = [back.reshape(trees, columns, part).transpose(1, 0, 2).reshape(columns, rows)]

    return pl.pallas_call(
        functools.partial(final_kernel, blocks if fine else 0),
        out_shape=shaped((rows, columns), f32),
        in_specs=[spec()] * (2 + layout.count),
        out_specs=spec(),
        scratch_shapes=[vm((rows, rows), bf16), vm((2 * LANES, rows), bf16)],
        compiler_params=params(40),
        name="to_input_order",
    )(pos, *back, weights)


def solution(mesh):
    in_specs = (
        P(("groups", "leaf", "sub"), None),
        P(("groups", "leaf", "sub"), "rep"),
        P(("groups", "leaf", "sub")),
        P(("groups", "leaf"), None),
        P(("groups", "leaf"), None, None),
        P(("groups", "leaf", "sub"), None),
        P("groups", None),
        P(("groups", "leaf", "sub"), None),
    )
    out_specs = P(("groups", "leaf", "sub"), "rep")
    return jax.shard_map(body, mesh=mesh, in_specs=in_specs, out_specs=out_specs, check_vma=False)
```

```python
import functools

import jax
import jax.numpy as jnp
from jax import lax
from jax.experimental import pallas as pl
from jax.experimental.pallas import tpu as pltpu
from jax.sharding import PartitionSpec as P

DIM = 64
LEAF = 512
SK = 128
LANES = 128
FEAT = 256
LOW = 256
AHEAD = 24
COORD = 144

highest = lax.Precision.HIGHEST
point_scale = 0.25
ridge = 0.5
PLACE_ROWS = 72
TAIL = 64
SLOT, NORM, BASE, FLAGS = 0, 1, 2, 3
f32 = jnp.float32
bf16 = jnp.bfloat16
VMEM = pltpu.MemorySpace.VMEM
SMEM = pltpu.MemorySpace.SMEM


def spec(space=VMEM):
    return pl.BlockSpec(memory_space=space)


def params(mib=58):
    return pltpu.CompilerParams(vmem_limit_bytes=mib * 1024 * 1024)


def in_hbm(array):
    return pltpu.with_memory_space_constraint(array, pltpu.MemorySpace.HBM)


def held(array):
    return pltpu.with_memory_space_constraint(array, VMEM)


def vm(shape, dtype):
    return pltpu.VMEM(shape, dtype)


def shaped(shape, dtype):
    return jax.ShapeDtypeStruct(shape, dtype)


def nt(left, right):
    return lax.dot_general(left, right, (((1,), (1,)), ((), ())), preferred_element_type=f32)


def nn(left, right):
    return jnp.dot(left, right, preferred_element_type=f32)


def column(row):
    return jnp.transpose(jnp.broadcast_to(row, (LANES, LANES)))


def iota(shape, dim):
    return lax.broadcasted_iota(jnp.int32, shape, dim)


def onehot(mask):
    return jnp.where(mask, 1.0, 0.0).astype(bf16)


def two(value):
    high = value.astype(bf16)
    return high, (value - high.astype(f32)).astype(bf16)


def three(value):
    high = value.astype(bf16).astype(f32)
    mid = (value - high).astype(bf16).astype(f32)
    return high, mid, (value - high - mid).astype(bf16).astype(f32)


def lanes_of(blocks):
    return blocks[0] if len(blocks) == 1 else jnp.concatenate(blocks, 1)


def aligned(start, size, unit):
    return pl.ds(pl.multiple_of(start, unit), size)


def stack_two(value):
    high, low = two(value)
    return jnp.concatenate([high, low], 0)


def spread(perm, here, rank):
    lane = iota((LANES, LANES), 1).astype(f32)
    for c in range(perm.shape[1] // LANES):
        perm[here, c * LANES : (c + 1) * LANES] = onehot(lane + float(c * LANES) == rank)


def place_kernel(fine, slot_ref, points_ref, base_ref, flag_ref, place_ref, pos_ref, masked, low_hot):
    chunks = slot_ref.shape[0]
    slots = slot_ref[...]
    slot = slots.astype(f32)
    within = slots & (chunks * LANES - 1)
    high, low = (within >> 5).astype(f32), (within & 31).astype(f32)
    ranks = []
    for r in range(chunks):
        here = slice(r * LANES, (r + 1) * LANES)
        mine = column(slot[r : r + 1])
        before = jnp.zeros((LANES, LANES), f32)
        for c in range(chunks):
            before += jnp.where(slot[c : c + 1] < mine, 1.0, 0.0)
        rank = jnp.broadcast_to(jnp.sum(before, axis=1, keepdims=True), (LANES, LANES))
        ranks.append(jnp.transpose(rank)[0:1])
        pos_ref[r : r + 1, :] = ranks[-1]
        spread(low_hot, here, (rank.astype(jnp.int32) & (LOW - 1)).astype(f32))
    scaled = points_ref[...] * point_scale
    ph, plo = two(scaled)
    nh, nm, nl = three(-0.5 * jnp.sum(scaled * scaled, axis=0, keepdims=True))
    high, low = lanes_of([high[c : c + 1] for c in range(chunks)]), lanes_of([low[c : c + 1] for c in range(chunks)])
    sub = iota((16, chunks * LANES), 0)
    extra = jnp.where(sub == 0, high, jnp.where(sub == 1, low, 0.0))
    extra = jnp.where(sub == 2, nh, jnp.where(sub == 3, nm, jnp.where(sub == 4, nl, extra)))
    high_part = lanes_of(ranks).astype(jnp.int32) // LOW
    parts = place_ref.shape[1] // LOW
    first = (lax.axis_index("leaf") ^ lax.axis_index("rep")) * parts if fine else 0
    for h in range(parts):
        here = high_part == first + h
        masked[h * COORD : h * COORD + 64, :] = jnp.where(here, ph.astype(f32), 0.0).astype(bf16)
        masked[h * COORD + 64 : h * COORD + 128, :] = jnp.where(here, plo.astype(f32), 0.0).astype(bf16)
        masked[h * COORD + 128 : (h + 1) * COORD, :] = jnp.where(here, extra, 0.0).astype(bf16)
    placed = nn(masked[...], low_hot[...])
    tail = iota((PLACE_ROWS - TAIL, LOW), 0)
    for h in range(parts):
        at = slice(h * LOW, (h + 1) * LOW)
        moved = placed[h * COORD : (h + 1) * COORD]
        place_ref[0:TAIL, at] = moved[0:64] + moved[64:128]
        slot_row = moved[128:129] * 32.0 + moved[129:130]
        norm_row = moved[130:131] + moved[131:132] + moved[132:133]
        place_ref[TAIL:, at] = jnp.where(tail == SLOT, slot_row, jnp.where(tail == NORM, norm_row, 0.0))
    if fine:
        place_ref[TAIL + BASE : TAIL + BASE + 1, 0:SK] = base_ref[...].astype(f32)
        place_ref[TAIL + FLAGS : TAIL + FLAGS + flag_ref.shape[0], 0 : flag_ref.shape[1]] = flag_ref[...].astype(f32)


def light_kernel(pos_ref, weights_ref, light_ref, masked, low_hot):
    chunks, split = pos_ref.shape[0], light_ref.shape[2]
    low_part, high_part = parts_of(lanes_of([pos_ref[c : c + 1, :] for c in range(chunks)]))
    low_by_column(low_hot, low_part.astype(f32))
    for c in range(chunks):
        at = slice(c * LANES, (c + 1) * LANES)
        turned = jnp.transpose(weights_ref[at, :])
        for h in range(chunks * LANES // LOW):
            masked[h * LANES : (h + 1) * LANES, at] = jnp.where(high_part[:, at] == h, turned, 0.0).astype(bf16)
    placed = nn(masked[...], low_hot[...])
    for h in range(chunks * LANES // LOW):
        at = h * LOW
        light_ref[at // split, :, at % split : at % split + LOW] = placed[h * LANES : (h + 1) * LANES]


class Layout:
    def __init__(self, blocks, trees, rows, fine):
        self.blocks, self.rows, self.fine = blocks, rows, fine
        self.count = blocks * trees if fine else 1
        self.per = rows // self.count
        self.halves = 2 if fine else 1
        self.span = LEAF // self.halves
        self.ahead = AHEAD // 4 * 4 if fine else 4

    def core(self):
        return lax.axis_index("rep") if self.fine else 0

    def lanes(self, index):
        return slice(index * self.per, (index + 1) * self.per)

    def message(self, group):
        if not self.fine:
            return 0
        leaf = lax.axis_index("leaf") ^ lax.axis_index("rep") ^ (group // self.blocks)
        return leaf * self.blocks + (lax.axis_index("sub") ^ (group % self.blocks))

    def gather(self, refs, index, part):
        return lanes_of([ref[part, self.lanes(index)] for ref in refs])

    def info(self, refs, small_ref, index):
        if not self.fine:
            return small_ref[index]
        core = lax.axis_index("rep")
        found = jnp.zeros((PLACE_ROWS - TAIL, SK), f32)
        for step in range(self.blocks):
            mine, theirs = refs[step][TAIL:, 0:SK], refs[self.blocks + step][TAIL:, 0:SK]
            here = jnp.where(core == 0, mine, theirs)
            found = jnp.where((lax.axis_index("sub") ^ step) == index, here, found)
        return found


def low_by_column(out, low):
    for c in range(out.shape[0] // LANES):
        at = slice(c * LANES, (c + 1) * LANES)
        spread(out, at, column(low[:, at]))


def parts_of(slots):
    slots = slots.astype(jnp.int32)
    return slots & (LOW - 1), slots // LOW


def feature_columns(out, at, tree):
    out[0:64, at] = tree[0:64].astype(bf16)
    out[64:128, at] = tree[0:64].astype(bf16)
    out[128:192, at] = tree[64:128].astype(bf16)
    out[192:208, at] = jnp.where(iota((16, tree.shape[1]), 0) < 8, tree[128:144].astype(f32), 0.0).astype(bf16)
    out[208:256, at] = jnp.zeros((48, tree.shape[1]), bf16)


def feature_rows(high, low, extra):
    first = jnp.transpose(jnp.concatenate([high, low], 0))
    second = jnp.transpose(jnp.concatenate([high, extra, jnp.zeros((56, high.shape[1]), f32)], 0))
    return first.astype(bf16), second.astype(bf16)


def target_columns(layout, out, tree_ref):
    span = layout.span
    for leaf in range(out.shape[1] // span):
        here = aligned(leaf * LEAF + layout.core() * span, span, span)
        feature_columns(out, slice(leaf * span, (leaf + 1) * span), tree_ref[:, here])


def tile_exponents(layout, tiles, tile, a_ref, bt_ref):
    source = aligned(tiles[1, tile] * LEAF, LEAF, LEAF)
    target = aligned(tiles[0, tile] * layout.span, layout.span, layout.span)
    return nn(a_ref[source, :], bt_ref[:, target])


def tiles_ahead(layout, tiles, a_ref, bt_ref, even, odd, made, made_hbm, sems):
    def send(tile):
        return pltpu.make_async_copy(made.at[tile], made_hbm.at[tile], sems.at[tile])

    even[...] = tile_exponents(layout, tiles, 0, a_ref, bt_ref)

    def step(pair, carry):
        for tile, ready, upcoming in ((2 * pair, even, odd), (2 * pair + 1, odd, even)):
            upcoming[...] = tile_exponents(layout, tiles, tile + 1, a_ref, bt_ref)
            made[tile] = jnp.exp(ready[...]).astype(bf16)
            send(tile).start()
        return carry

    lax.fori_loop(0, layout.ahead // 2, step, 0)
    return [send(tile) for tile in range(layout.ahead)]


def list_tiles(count_ref, list_ref, tiles, times):
    every = count_ref.shape[1]

    def tally(leaf, filled):
        for other in range(every):
            times[other] = (leaf == other).astype(jnp.int32)

        def add(slot, carry):
            at = list_ref[leaf, slot]
            times[at] = times[at] + 1
            return carry

        lax.fori_loop(0, count_ref[0, leaf], add, 0)
        for other in range(every):
            tiles[0, filled] = leaf
            tiles[1, filled] = other
            tiles[2, filled] = times[other]
            filled = filled + (times[other] > 0).astype(jnp.int32)
        return filled

    filled = lax.fori_loop(0, every, tally, jnp.int32(0))

    def pad(more, carry):
        tiles[0, more] = 0
        tiles[1, more] = 0
        return carry

    lax.fori_loop(filled, tiles.shape[1] - 1, pad, 0)
    tiles[0, tiles.shape[1] - 1] = filled


def points_kernel(layout, trees, count_ref, list_ref, upper_ref, *refs):
    if not layout.fine:
        small_ref, refs = refs[0], refs[1:]
    else:
        small_ref = None
    place_refs, refs = refs[: layout.count], refs[layout.count :]
    tree_ref, a_hbm, base_hbm, sk_ref, upper_tiles_ref, top_ref, slot_ref, info_ref, tiles, made_hbm = refs[:10]
    masked, low_hot, a_ref, base_ref, sk_t, sk_bt, sems, times, bt_ref, even, odd, made, made_sems = refs[10:]
    blocks, rows = layout.blocks, layout.rows

    def keep(node, found):
        at = slice(node * SK, (node + 1) * SK)
        sk_t[:, at] = found.astype(bf16)
        sk_ref[at, 0:128], sk_ref[at, 128:256] = feature_rows(found[0:64], found[64:128], found[136:144])
        feature_columns(sk_bt, at, found)

    high_parts = rows // LOW
    infos = []
    for index in range(blocks):
        tail = layout.gather(place_refs, index, slice(TAIL, PLACE_ROWS))
        slots = tail[SLOT : SLOT + 1]
        slot_ref[index : index + 1, :] = slots
        infos.append(layout.info(place_refs, small_ref, index))
        info_ref[index] = infos[-1]
        low_part, high_part = parts_of(slots)
        low_by_column(low_hot.at[index], low_part.astype(f32))
        points = layout.gather(place_refs, index, slice(0, TAIL))
        high, low = two(points)
        nh, nm, nl = three(tail[NORM : NORM + 1])
        sub = iota((16, rows), 0)
        norms = jnp.where((sub == 3) | (sub == 8), nh, jnp.where((sub == 4) | (sub == 9), nm, nl))
        is_norm = ((sub >= 3) & (sub < 6)) | ((sub >= 8) & (sub < 11))
        is_one = (sub < 3) | ((sub >= 11) & (sub < 14))
        extra = jnp.where(is_norm, norms, jnp.where(is_one, 1.0, 0.0))
        for h in range(high_parts):
            here = high_part == h
            at = h * COORD
            masked[index, at : at + 64, :] = jnp.where(here, high.astype(f32), 0.0).astype(bf16)
            masked[index, at + 64 : at + 128, :] = jnp.where(here, low.astype(f32), 0.0).astype(bf16)
            masked[index, at + 128 : at + COORD, :] = jnp.where(here, extra, 0.0).astype(bf16)
    copies = []
    for index in range(blocks):
        placed = nn(masked[index], low_hot[index])
        for h in range(high_parts):
            part = placed[h * COORD : (h + 1) * COORD]
            at = slice(index * rows + h * LOW, index * rows + (h + 1) * LOW)
            tree_ref[:, at] = part.astype(bf16)
            a_ref[at, 0:128], a_ref[at, 128:256] = feature_rows(part[0:64], part[64:128], part[136:144])
        mine = slice(index * rows, (index + 1) * rows)
        copies.append(pltpu.make_async_copy(a_ref.at[mine], a_hbm.at[mine], sems.at[0, index]))
        copies[-1].start()
    for index in range(blocks):
        mine = slice(index * rows, (index + 1) * rows)
        picked = onehot(iota((rows, SK), 0) == infos[index][BASE : BASE + 1].astype(jnp.int32))
        keep(index, nn(tree_ref[:, mine], picked))
    for index in range(blocks):
        mine = slice(index * rows, (index + 1) * rows)
        base_ref[index] = jnp.exp(nn(a_ref[mine, :], sk_bt[:, index * SK : (index + 1) * SK])).astype(bf16)
        copies.append(pltpu.make_async_copy(base_ref.at[index], base_hbm.at[index], sems.at[1, index]))
        copies[-1].start()
    start, count, offset, total = 0, blocks, 0, blocks * trees
    while count > 1:
        nodes = count // 2
        for j in range(nodes):
            pair = slice((start + 2 * j) * SK, (start + 2 * j + 2) * SK)
            row = offset + lax.axis_index("leaf") * nodes + j
            picked = onehot(iota((2 * SK, SK), 0) == upper_ref[pl.ds(row, 1), :])
            here = start + count + j
            keep(here, nn(sk_t[:, pair], picked))
            upper_tiles_ref[here - blocks] = jnp.exp(nn(sk_ref[pair, :], sk_bt[:, here * SK : (here + 1) * SK]))
        total = total // 2
        offset = offset + total
        start, count = start + count, nodes
    found = sk_t[:, start * SK : (start + 1) * SK].astype(f32)
    top_ref[0:64, :] = found[0:64] + found[64:128]
    top_ref[64:72, :] = found[128:136]
    list_tiles(count_ref, list_ref, tiles, times)
    target_columns(layout, bt_ref, tree_ref)
    copies += tiles_ahead(layout, tiles, a_ref, bt_ref, even, odd, made, made_hbm, made_sems)
    for copy in copies:
        copy.wait()


def weights_kernel(layout, base_hbm, upper_tiles_ref, top_ref, slot_ref, *refs):
    light_refs, refs = refs[: layout.halves], refs[layout.halves :]
    w_ref, coef_ref, pack_ref, masked, low_hot, base_ref, sems = refs
    blocks, rows = layout.blocks, layout.rows
    each = light_refs[0].shape[1]
    width = each * layout.halves
    pack_ref[0:PLACE_ROWS, :] = top_ref[...]
    for index in range(blocks):
        pltpu.make_async_copy(base_hbm.at[index], base_ref.at[index], sems.at[index]).start()

    def keep(node, coef):
        coef_ref[:, node * SK : (node + 1) * SK] = stack_two(coef)
        pack_ref[PLACE_ROWS:, :] = coef

    for index in range(blocks):
        low_part, high_part = parts_of(slot_ref[index : index + 1, :])
        low_by_column(low_hot.at[index], low_part.astype(f32))
        for half, light_ref in enumerate(light_refs):
            light = lanes_of([light_ref[layout.message(g), :, layout.lanes(index)] for g in range(layout.count)])
            for h in range(rows // LOW):
                at = h * width + half * each
                masked[index, at : at + each, :] = jnp.where(high_part == h, light, 0.0).astype(bf16)
    for index in range(blocks):
        placed = nn(masked[index], low_hot[index])
        for h in range(rows // LOW):
            at = index * rows + h * LOW
            w_ref[:, at : at + LOW] = placed[h * width : (h + 1) * width].astype(bf16)
    for index in range(blocks):
        pltpu.make_async_copy(base_hbm.at[index], base_ref.at[index], sems.at[index]).wait()
        keep(index, nn(w_ref[:, index * rows : (index + 1) * rows], base_ref[index]))
    start, count = 0, blocks
    while count > 1:
        for j in range(count // 2):
            pair = slice((start + 2 * j) * SK, (start + 2 * j + 2) * SK)
            here = start + count + j
            high, low = two(upper_tiles_ref[here - blocks])
            coef = nn(coef_ref[:, pair], high)
            keep(here, coef[:width] + coef[width:] + nn(coef_ref[0:width, pair], low))
        start, count = start + count, count // 2


def near_kernel(layout, tiles, a_hbm, made_hbm, tree_ref, w_ref, acc, a_ref, bt_ref, made, sems, even, odd, even_tile, odd_tile):
    ahead, span = layout.ahead, layout.span

    def fetch(tile):
        return pltpu.make_async_copy(made_hbm.at[tile], made.at[tile], sems.at[tile])

    copy = pltpu.make_async_copy(a_hbm, a_ref, sems.at[ahead])
    for tile in range(ahead):
        fetch(tile).start()
    copy.start()
    filled = tiles[0, tiles.shape[1] - 1]
    acc[...] = jnp.zeros_like(acc)
    target_columns(layout, bt_ref, tree_ref)

    def exponents(tile):
        return tile_exponents(layout, tiles, tile, a_ref, bt_ref)

    def add(tile, block):
        source = aligned(tiles[1, tile] * LEAF, LEAF, LEAF)
        target = aligned(tiles[0, tile] * span, span, span)
        acc[:, target] += tiles[2, tile].astype(f32) * nn(w_ref[:, source], block)

    def arrived(quad, carry):
        for more in range(4):
            fetch(4 * quad + more).wait()
            tile = 4 * quad + more

            @pl.when(tile < filled)
            def _():
                add(tile, made[tile])

        return carry

    lax.fori_loop(0, ahead // 4, arrived, 0)
    copy.wait()

    @pl.when(filled > ahead)
    def _():
        even[...] = exponents(ahead)
        even_tile[...] = jnp.exp(even[...]).astype(bf16)
        odd[...] = exponents(ahead + 1)

        def phase(tile, upcoming, ready, finished, previous):
            upcoming[...] = exponents(tile + 1)
            finished[...] = jnp.exp(ready[...]).astype(bf16)
            add(tile - 1, previous[...])

        def step(pair, carry):
            phase(ahead + 2 * pair + 1, even, odd, odd_tile, even_tile)
            phase(ahead + 2 * pair + 2, odd, even, even_tile, odd_tile)
            return carry

        pairs = (filled - ahead - 1) // 2
        lax.fori_loop(0, pairs, step, 0)
        add(ahead + 2 * pairs, even_tile[...])

        @pl.when(ahead + 2 * pairs + 1 < filled)
        def _():
            odd_tile[...] = jnp.exp(odd[...]).astype(bf16)
            add(ahead + 2 * pairs + 1, odd_tile[...])


def far_kernel(layout, low_levels, pack_ref, slot_ref, info_ref, tree_ref, sk_ref, coef_ref, near_ref, *refs):
    out_refs, refs = refs[: layout.halves], refs[layout.halves :]
    tops, coefs, scaled, low_hot, bt_ref, sums, masked = refs[:7]
    powers, tiles = refs[7:9], refs[9:11]
    blocks, rows = layout.blocks, layout.rows
    ups, width = pack_ref.shape[0], near_ref.shape[0]
    levels = low_levels + ups
    span, core = layout.span, layout.core()
    per_block = rows // LEAF
    lane = iota((1, SK), 1)
    for up in range(ups):
        pack = pack_ref[up]
        high, low = two(pack[0:64])
        sub = iota((8, SK), 0)
        extra = jnp.where(sub == 0, pack[67:68], jnp.where(sub == 1, pack[68:69], pack[69:70]))
        extra = jnp.where(sub < 3, extra, jnp.where(sub < 6, 1.0, 0.0))
        at = slice((low_levels + up) * SK, (low_levels + up + 1) * SK)
        rows_of = feature_rows(high.astype(f32), low.astype(f32), extra)
        coef = stack_two(pack[PLACE_ROWS:])
        for index in range(blocks):
            tops[index, at, 0:128], tops[index, at, 128:256] = rows_of
            coefs[index, :, at] = coef
    for index in range(blocks):
        node, start, count = index, 0, blocks
        for level in range(low_levels):
            at = slice(level * SK, (level + 1) * SK)
            other = slice((start + (node ^ 1)) * SK, (start + (node ^ 1) + 1) * SK)
            tops[index, at, :] = sk_ref[other, :]
            coefs[index, :, at] = coef_ref[:, other]
            node, start, count = node // 2, start + count, count // 2
        for leaf in range(per_block):
            flags = info_ref[index, FLAGS + leaf : FLAGS + leaf + 1, :]
            used = []
            for level in range(levels):
                flag = jnp.sum(jnp.where(lane == level, flags, 0.0), axis=1, keepdims=True)
                used.append(jnp.broadcast_to(flag, (1, SK)))
            used = jnp.concatenate(used, 1)
            scaled[index * per_block + leaf] = (coefs[index].astype(f32) * used).astype(bf16)

    target_columns(layout, bt_ref, tree_ref)

    def exponents(leaf):
        powers[leaf % 2][...] = nn(tops[leaf // per_block], bt_ref[:, leaf * span : (leaf + 1) * span])

    def product(leaf):
        here = slice(leaf * span, (leaf + 1) * span)
        far = nn(scaled[leaf], tiles[leaf % 2][...])
        sums[:, here] = near_ref[:, here] + far[:width] + far[width:]

    leaves = blocks * per_block
    exponents(0)
    for leaf in range(leaves):
        if leaf + 1 < leaves:
            exponents(leaf + 1)
        tiles[leaf % 2][...] = jnp.exp(powers[leaf % 2][...]).astype(bf16)
        if leaf:
            product(leaf - 1)
    product(leaves - 1)

    high_parts = []
    pieces = rows // LOW // layout.halves
    for index in range(blocks):
        low_part, high_part = parts_of(slot_ref[index : index + 1, :])
        high_parts.append(high_part)
        for c in range(rows // LANES):
            at = slice(c * LANES, (c + 1) * LANES)
            low_hot[index, :, at] = onehot(iota((LOW, LANES), 0) == low_part[:, at])
        for k in range(pieces):
            at = (index * pieces + k) * LOW
            masked[index, k * 2 * width : (k + 1) * 2 * width, :] = stack_two(sums[:, at : at + LOW])
    for index in range(blocks):
        moved = nn(masked[index], low_hot[index])
        result = jnp.zeros((2 * width, rows), f32)
        for k in range(pieces):
            here = high_parts[index] == k * layout.halves + core
            result = jnp.where(here, moved[k * 2 * width : (k + 1) * 2 * width], result)
        result = result[:width] + result[width:]
        if not layout.fine:
            out_refs[0][0, :, layout.lanes(index)] = result
            continue
        for g in range(layout.count):
            out_ref = out_refs[g // blocks]
            out_ref[g % blocks, :, layout.lanes(index)] = result[:, g * layout.per : (g + 1) * layout.per]


def add_kernel(kept_ref, got_ref, *out_refs):
    half = kept_ref.shape[1] // 2
    for step, out_ref in enumerate(out_refs):
        out_ref[0:half, :] = kept_ref[step, 0:half, :] + got_ref[step, half:, :]
        out_ref[half:, :] = kept_ref[step, half:, :] + got_ref[step, 0:half, :]


def far_first(blocks):
    return sorted(range(blocks), key=lambda step: -(step * 2 // blocks))


def final_kernel(blocks, pos_ref, *refs):
    back_refs, (weights_ref, out_ref, perm, vals) = refs[:-4], refs[-4:]
    chunks = pos_ref.shape[0]
    rows = chunks * LANES
    width, split = back_refs[0].shape
    width = LANES // blocks if blocks else width
    for r in range(chunks):
        spread(perm, slice(r * LANES, (r + 1) * LANES), column(pos_ref[r : r + 1, :]))
    for g, back_ref in enumerate(back_refs):
        columns, at = 0, slice(0, rows)
        value = back_ref[...]
        if blocks:
            columns = (lax.axis_index("sub") ^ far_first(blocks)[g % blocks]) * width
            at = aligned((lax.axis_index("leaf") ^ lax.axis_index("rep") ^ (g // blocks)) * split, split, split)
            value = value[0:width] if g < blocks else value[width:]
        high, low = two(value)
        vals[aligned(columns, width, width), at] = high
        vals[aligned(columns + LANES, width, width), at] = low
    step = 256
    for s in range(rows // step):
        here = slice(s * step, (s + 1) * step)
        moved = nt(perm[here, :], vals[...])
        out_ref[here, :] = ridge * weights_ref[here, :] + moved[:, :LANES] + moved[:, LANES:]


def upper_levels(pack, skeleton_upper, my_leaf, trees, blocks):
    devices = trees * blocks
    level = blocks.bit_length() - 1
    offset = sum(devices >> step for step in range(1, level + 1))
    line = jnp.arange(pack.shape[0])[:, None]
    is_point, is_norm = line < DIM, (line >= DIM + 3) & (line < DIM + 6)
    is_coef = line >= PLACE_ROWS
    packs, own, stride = [], pack, 1
    while stride < trees:
        other = lax.ppermute(own, "leaf", [(i, i ^ stride) for i in range(trees)])
        packs.append(other)
        stride *= 2
        if stride < trees:
            second = (my_leaf // (stride // 2)) % 2 == 1
            pair = jnp.where(second, jnp.concatenate([other, own], 1), jnp.concatenate([own, other], 1))
            chosen = pair[:, skeleton_upper[offset + my_leaf // stride]]
            level += 1
            offset += devices >> level
            norms = jnp.sum(jnp.where(is_norm, pair, 0.0), axis=0)
            chosen_norms = jnp.sum(jnp.where(is_norm, chosen, 0.0), axis=0)
            inner = jnp.dot(
                jnp.where(is_point, pair, 0.0).T, jnp.where(is_point, chosen, 0.0), precision=highest
            )
            tile = jnp.exp(inner + norms[:, None] + chosen_norms[None])
            own = jnp.where(is_coef, jnp.dot(pair, tile, precision=highest), chosen)
    return jnp.stack(packs)


def body(points, weights, tree_slot, near_count, near_list, skeleton_base, skeleton_upper, far_use):
    blocks, trees, reps = lax.axis_size("sub"), lax.axis_size("leaf"), lax.axis_size("rep")
    devices = blocks * trees
    rows, columns = weights.shape
    low_levels = blocks.bit_length() - 1
    ups = trees.bit_length() - 1
    width = columns // blocks
    part = rows // trees
    per = part // blocks
    total = blocks * rows
    leaves = total // LEAF
    my_leaf = lax.axis_index("leaf")
    fine = trees == 2 and reps == 2 and per % LANES == 0
    layout = Layout(blocks, trees, rows, fine)
    split = part if fine else rows
    cols = width * layout.halves

    place, pos = pl.pallas_call(
        functools.partial(place_kernel, fine),
        out_shape=(shaped((PLACE_ROWS, split), f32), shaped((rows // LANES, LANES), f32)),
        in_specs=[spec()] * 4,
        out_specs=(spec(),) * 2,
        scratch_shapes=[vm((split // LOW * COORD, rows), bf16), vm((rows, LOW), bf16)],
        compiler_params=params(),
        name="sort_points",
    )(tree_slot.reshape(rows // LANES, LANES), points.T, skeleton_base, far_use)
    axes = ("leaf", "sub", "rep")

    def swap(value, step, other=0):
        pairs = []
        for leaf in range(trees):
            for sub in range(blocks):
                for core in range(reps):
                    to = ((leaf ^ core ^ other) * blocks + (sub ^ step)) * reps + core
                    pairs.append(((leaf * blocks + sub) * reps + core, to))
        return lax.ppermute(value, axes, pairs)

    def other_core(value):
        return lax.ppermute(value, "rep", [(0, 1), (1, 0)])

    def sorted_light():
        return pl.pallas_call(
            light_kernel,
            out_shape=shaped((rows // split, columns, split), f32),
            in_specs=[spec()] * 2,
            out_specs=spec(),
            scratch_shapes=[vm((rows // LOW * LANES, rows), bf16), vm((rows, LOW), bf16)],
            compiler_params=params(),
            name="sort_weights",
        )(pos, weights)

    if fine:
        place = {0: swap(place, 0)}
        stride = blocks // 2
        while stride:
            for step in sorted(place):
                place[step | stride] = lax.ppermute(place[step], "sub", [(i, i ^ stride) for i in range(blocks)])
            stride //= 2
        light = sorted_light()
        place, light = lax.optimization_barrier((place, light))
        theirs = {step: other_core(one) for step, one in place.items()}
        place = [place[step] for step in range(blocks)] + [theirs[step] for step in range(blocks)]
        light = light.reshape(devices, width, part)
        light = lax.all_to_all(light, ("leaf", "sub"), split_axis=0, concat_axis=0, tiled=True)
        small = []
    else:
        info = jnp.pad(far_use.astype(f32), ((FLAGS, 5 - far_use.shape[0]), (0, SK - far_use.shape[1])))
        small = [lax.all_gather(info.at[BASE].set(skeleton_base[0].astype(f32)), "sub", axis=0, tiled=False)]
        place = place.reshape(PLACE_ROWS, trees, part).transpose(1, 0, 2)
        place = lax.all_to_all(place, "leaf", split_axis=0, concat_axis=0, tiled=True)
        place = lax.all_gather(place, "sub", axis=0, tiled=False)
        place = place.transpose(1, 0, 2, 3).reshape(devices, PLACE_ROWS, blocks, per)
        place = [place.transpose(1, 2, 0, 3).reshape(PLACE_ROWS, total)]
        light = sorted_light().reshape(columns, trees, part).transpose(1, 0, 2).reshape(devices, width, part)
        light = lax.all_to_all(light, ("leaf", "sub"), split_axis=0, concat_axis=0, tiled=True)
        light = light.reshape(devices, width, blocks, per)
        light = [light.transpose(1, 2, 0, 3).reshape(1, width, total)]

    nodes = 2 * blocks - 1
    tree, feat_a, base, sk, upper_tiles, top, slots, info, tiles, made = pl.pallas_call(
        functools.partial(points_kernel, layout, trees),
        out_shape=(
            vm((COORD, total), bf16),
            pltpu.MemorySpace.HBM((total, FEAT), bf16),
            pltpu.MemorySpace.HBM((blocks, rows, SK), bf16),
            vm((nodes * SK, FEAT), bf16),
            vm((blocks - 1, 2 * SK, SK), f32),
            vm((PLACE_ROWS, SK), f32),
            vm((blocks, rows), f32),
            vm((blocks, 8, SK), f32),
            pltpu.MemorySpace.HBM((3, leaves * leaves + 3), jnp.int32),
            pltpu.MemorySpace.HBM((layout.ahead, LEAF, layout.span), bf16),
        ),
        in_specs=[spec(SMEM)] * 2 + [spec()] * (1 + len(small) + layout.count),
        out_specs=(spec(), spec(pl.ANY), spec(pl.ANY)) + (spec(),) * 5 + (spec(SMEM), spec(pl.ANY)),
        scratch_shapes=[
            vm((blocks, rows // LOW * COORD, rows), bf16),
            vm((blocks, rows, LOW), bf16),
            vm((total, FEAT), bf16),
            vm((blocks, rows, SK), bf16),
            vm((COORD, nodes * SK), bf16),
            vm((FEAT, nodes * SK), bf16),
            pltpu.SemaphoreType.DMA((2, blocks)),
            pltpu.SMEM((leaves,), jnp.int32),
            vm((FEAT, total // layout.halves), bf16),
            vm((LEAF, layout.span), f32),
            vm((LEAF, layout.span), f32),
            vm((layout.ahead, LEAF, layout.span), bf16),
            pltpu.SemaphoreType.DMA((layout.ahead,)),
        ],
        compiler_params=params(40),
        name="tree_points",
    )(in_hbm(near_count), in_hbm(near_list[0]), in_hbm(skeleton_upper), *small, *place)

    if fine:
        light, slots = lax.optimization_barrier((light, slots))
        light = [light, other_core(light)]
    tree_light, coefs, pack = pl.pallas_call(
        functools.partial(weights_kernel, layout),
        out_shape=(
            vm((cols, total), bf16),
            vm((2 * cols, nodes * SK), bf16),
            shaped((PLACE_ROWS + cols, SK), f32),
        ),
        in_specs=[spec(pl.ANY)] + [spec()] * (3 + layout.halves),
        out_specs=(spec(),) * 3,
        scratch_shapes=[
            vm((blocks, rows // LOW * cols, rows), bf16),
            vm((blocks, rows, LOW), bf16),
            vm((blocks, rows, SK), bf16),
            pltpu.SemaphoreType.DMA((blocks,)),
        ],
        compiler_params=params(40),
        name="tree_weights",
    )(in_hbm(base), held(upper_tiles), held(top), held(slots), *light)

    packs = upper_levels(pack, skeleton_upper, my_leaf, trees, blocks)

    near = pl.pallas_call(
        functools.partial(near_kernel, layout),
        out_shape=vm((cols, total // layout.halves), f32),
        in_specs=[spec(SMEM), spec(pl.ANY), spec(pl.ANY)] + [spec()] * 2,
        out_specs=spec(),
        scratch_shapes=[
            vm((total, FEAT), bf16),
            vm((FEAT, total // layout.halves), bf16),
            vm((layout.ahead, LEAF, layout.span), bf16),
            pltpu.SemaphoreType.DMA((layout.ahead + 1,)),
        ]
        + [vm((LEAF, layout.span), f32)] * 2
        + [vm((LEAF, layout.span), bf16)] * 2,
        compiler_params=params(40),
        name="near",
    )(in_hbm(tiles), in_hbm(feat_a), in_hbm(made), held(tree), held(tree_light))

    levels = low_levels + ups
    back = pl.pallas_call(
        functools.partial(far_kernel, layout, low_levels),
        out_shape=(shaped((layout.count // layout.halves, cols, total // layout.count), f32),) * layout.halves,
        in_specs=[spec()] * 7,
        out_specs=(spec(),) * layout.halves,
        scratch_shapes=[
            vm((blocks, levels * SK, FEAT), bf16),
            vm((blocks, 2 * cols, levels * SK), bf16),
            vm((leaves, 2 * cols, levels * SK), bf16),
            vm((blocks, LOW, rows), bf16),
            vm((FEAT, total // layout.halves), bf16),
            vm((cols, total // layout.halves), f32),
            vm((blocks, rows // LOW // layout.halves * 2 * cols, LOW), bf16),
        ]
        + [vm((levels * SK, layout.span), f32)] * 2
        + [vm((levels * SK, layout.span), bf16)] * 2,
        compiler_params=params(40),
        name="far",
    )(packs, *[held(one) for one in (slots, info, tree, sk, coefs, near)])

    if fine:
        kept, sent = back
        sums = pl.pallas_call(
            add_kernel,
            out_shape=(shaped((cols, part), f32),) * blocks,
            in_specs=[spec()] * 2,
            out_specs=(spec(),) * blocks,
            compiler_params=params(40),
            name="add_cores",
        )(kept, other_core(sent))
        back = [swap(sums[step], step) for step in far_first(blocks)]
        back = back + [other_core(one) for one in back]
    else:
        back = back[0].reshape(cols, blocks, devices, per).transpose(2, 0, 1, 3).reshape(devices, width, part)
        back = lax.all_to_all(back, ("leaf", "sub"), split_axis=0, concat_axis=0, tiled=True)
        back = [back.reshape(trees, columns, part).transpose(1, 0, 2).reshape(columns, rows)]

    return pl.pallas_call(
        functools.partial(final_kernel, blocks if fine else 0),
        out_shape=shaped((rows, columns), f32),
        in_specs=[spec()] * (2 + layout.count),
        out_specs=spec(),
        scratch_shapes=[vm((rows, rows), bf16), vm((2 * LANES, rows), bf16)],
        compiler_params=params(40),
        name="to_input_order",
    )(pos, *back, weights)


def solution(mesh):
    in_specs = (
        P(("groups", "leaf", "sub"), None),
        P(("groups", "leaf", "sub"), "rep"),
        P(("groups", "leaf", "sub")),
        P(("groups", "leaf"), None),
        P(("groups", "leaf"), None, None),
        P(("groups", "leaf", "sub"), None),
        P("groups", None),
        P(("groups", "leaf", "sub"), None),
    )
    out_specs = P(("groups", "leaf", "sub"), "rep")
    return jax.shard_map(body, mesh=mesh, in_specs=in_specs, out_specs=out_specs, check_vma=False)
```

```python
import functools

import jax
import jax.numpy as jnp
from jax import lax
from jax.experimental import pallas as pl
from jax.experimental.pallas import tpu as pltpu
from jax.sharding import PartitionSpec as P

DIM = 64
LEAF = 512
SK = 128
LANES = 128
FEAT = 256
LOW = 256
AHEAD = 8
COORD = 144

highest = lax.Precision.HIGHEST
point_scale = 0.25
ridge = 0.5
PLACE_ROWS = 72
TAIL = 64
SLOT, NORM, BASE, FLAGS = 0, 1, 2, 3
f32 = jnp.float32
bf16 = jnp.bfloat16
VMEM = pltpu.MemorySpace.VMEM
SMEM = pltpu.MemorySpace.SMEM


def spec(space=VMEM):
    return pl.BlockSpec(memory_space=space)


def params(mib=58):
    return pltpu.CompilerParams(vmem_limit_bytes=mib * 1024 * 1024)


def in_hbm(array):
    return pltpu.with_memory_space_constraint(array, pltpu.MemorySpace.HBM)


def held(array):
    return pltpu.with_memory_space_constraint(array, VMEM)


def vm(shape, dtype):
    return pltpu.VMEM(shape, dtype)


def shaped(shape, dtype):
    return jax.ShapeDtypeStruct(shape, dtype)


def nt(left, right):
    return lax.dot_general(left, right, (((1,), (1,)), ((), ())), preferred_element_type=f32)


def nn(left, right):
    return jnp.dot(left, right, preferred_element_type=f32)


def column(row):
    return jnp.transpose(jnp.broadcast_to(row, (LANES, LANES)))


def iota(shape, dim):
    return lax.broadcasted_iota(jnp.int32, shape, dim)


def onehot(mask):
    return jnp.where(mask, 1.0, 0.0).astype(bf16)


def two(value):
    high = value.astype(bf16)
    return high, (value - high.astype(f32)).astype(bf16)


def three(value):
    high = value.astype(bf16).astype(f32)
    mid = (value - high).astype(bf16).astype(f32)
    return high, mid, (value - high - mid).astype(bf16).astype(f32)


def lanes_of(blocks):
    return blocks[0] if len(blocks) == 1 else jnp.concatenate(blocks, 1)


def aligned(start, size, unit):
    return pl.ds(pl.multiple_of(start, unit), size)


def stack_two(value):
    high, low = two(value)
    return jnp.concatenate([high, low], 0)


def spread(perm, here, rank):
    lane = iota((LANES, LANES), 1).astype(f32)
    for c in range(perm.shape[1] // LANES):
        perm[here, c * LANES : (c + 1) * LANES] = onehot(lane + float(c * LANES) == rank)


def place_kernel(fine, slot_ref, points_ref, base_ref, flag_ref, place_ref, pos_ref, masked, low_hot):
    chunks = slot_ref.shape[0]
    slots = slot_ref[...]
    slot = slots.astype(f32)
    within = slots & (chunks * LANES - 1)
    high, low = (within >> 5).astype(f32), (within & 31).astype(f32)
    ranks = []
    for r in range(chunks):
        here = slice(r * LANES, (r + 1) * LANES)
        mine = column(slot[r : r + 1])
        before = jnp.zeros((LANES, LANES), f32)
        for c in range(chunks):
            before += jnp.where(slot[c : c + 1] < mine, 1.0, 0.0)
        rank = jnp.broadcast_to(jnp.sum(before, axis=1, keepdims=True), (LANES, LANES))
        ranks.append(jnp.transpose(rank)[0:1])
        pos_ref[r : r + 1, :] = ranks[-1]
        spread(low_hot, here, (rank.astype(jnp.int32) & (LOW - 1)).astype(f32))
    scaled = points_ref[...] * point_scale
    ph, plo = two(scaled)
    nh, nm, nl = three(-0.5 * jnp.sum(scaled * scaled, axis=0, keepdims=True))
    high, low = lanes_of([high[c : c + 1] for c in range(chunks)]), lanes_of([low[c : c + 1] for c in range(chunks)])
    sub = iota((16, chunks * LANES), 0)
    extra = jnp.where(sub == 0, high, jnp.where(sub == 1, low, 0.0))
    extra = jnp.where(sub == 2, nh, jnp.where(sub == 3, nm, jnp.where(sub == 4, nl, extra)))
    high_part = lanes_of(ranks).astype(jnp.int32) // LOW
    parts = place_ref.shape[1] // LOW
    first = (lax.axis_index("leaf") ^ lax.axis_index("rep")) * parts if fine else 0
    for h in range(parts):
        here = high_part == first + h
        masked[h * COORD : h * COORD + 64, :] = jnp.where(here, ph.astype(f32), 0.0).astype(bf16)
        masked[h * COORD + 64 : h * COORD + 128, :] = jnp.where(here, plo.astype(f32), 0.0).astype(bf16)
        masked[h * COORD + 128 : (h + 1) * COORD, :] = jnp.where(here, extra, 0.0).astype(bf16)
    placed = nn(masked[...], low_hot[...])
    tail = iota((PLACE_ROWS - TAIL, LOW), 0)
    for h in range(parts):
        at = slice(h * LOW, (h + 1) * LOW)
        moved = placed[h * COORD : (h + 1) * COORD]
        place_ref[0:TAIL, at] = moved[0:64] + moved[64:128]
        slot_row = moved[128:129] * 32.0 + moved[129:130]
        norm_row = moved[130:131] + moved[131:132] + moved[132:133]
        place_ref[TAIL:, at] = jnp.where(tail == SLOT, slot_row, jnp.where(tail == NORM, norm_row, 0.0))
    if fine:
        place_ref[TAIL + BASE : TAIL + BASE + 1, 0:SK] = base_ref[...].astype(f32)
        place_ref[TAIL + FLAGS : TAIL + FLAGS + flag_ref.shape[0], 0 : flag_ref.shape[1]] = flag_ref[...].astype(f32)


def light_kernel(blocks, pos_ref, weights_ref, *refs):
    light_refs, (masked, low_hot, placed) = refs[:-3], refs[-3:]
    chunks = pos_ref.shape[0]
    high_count = chunks * LANES // LOW
    low_part, high_part = parts_of(lanes_of([pos_ref[c : c + 1, :] for c in range(chunks)]))
    low_by_column(low_hot, low_part.astype(f32))
    for c in range(chunks):
        at = slice(c * LANES, (c + 1) * LANES)
        turned = jnp.transpose(weights_ref[at, :])
        for h in range(high_count):
            masked[h * LANES : (h + 1) * LANES, at] = jnp.where(high_part[:, at] == h, turned, 0.0).astype(bf16)
    moved = nn(masked[...], low_hot[...])
    for h in range(high_count):
        if not blocks:
            light_refs[0][:, h * LOW : (h + 1) * LOW] = moved[h * LANES : (h + 1) * LANES]
        placed[h] = moved[h * LANES : (h + 1) * LANES]
    if not blocks:
        return
    width, parts = LANES // blocks, high_count // 2
    for other, light_ref in enumerate(light_refs):
        first = (lax.axis_index("leaf") ^ lax.axis_index("rep") ^ other) * parts
        for step in range(blocks):
            columns = aligned((lax.axis_index("sub") ^ step) * width, width, width)
            for h in range(parts):
                light_ref[step, :, h * LOW : (h + 1) * LOW] = placed[first + h, columns, :]


def join_kernel(kept_ref, got_ref, *out_refs):
    half = kept_ref.shape[1]
    for step, out_ref in enumerate(out_refs):
        out_ref[0:half, :] = kept_ref[step]
        out_ref[half:, :] = got_ref[step]


class Layout:
    def __init__(self, blocks, trees, rows, fine):
        self.blocks, self.rows, self.fine = blocks, rows, fine
        self.count = blocks * trees if fine else 1
        self.per = rows // self.count
        self.halves = 2 if fine else 1
        self.span = LEAF // self.halves
        self.ahead = AHEAD // 4 * 4 if fine else 4

    def core(self):
        return lax.axis_index("rep") if self.fine else 0

    def lanes(self, index):
        return slice(index * self.per, (index + 1) * self.per)

    def columns(self, group, half, each):
        if self.fine and group >= self.blocks:
            half = 1 - half
        return slice(half * each, (half + 1) * each)

    def gather(self, refs, index, part):
        return lanes_of([ref[part, self.lanes(index)] for ref in refs])

    def info(self, refs, small_ref, index):
        if not self.fine:
            return small_ref[index]
        core = lax.axis_index("rep")
        found = jnp.zeros((PLACE_ROWS - TAIL, SK), f32)
        for step in range(self.blocks):
            mine, theirs = refs[step][TAIL:, 0:SK], refs[self.blocks + step][TAIL:, 0:SK]
            here = jnp.where(core == 0, mine, theirs)
            found = jnp.where((lax.axis_index("sub") ^ step) == index, here, found)
        return found


def low_by_column(out, low):
    for c in range(out.shape[0] // LANES):
        at = slice(c * LANES, (c + 1) * LANES)
        spread(out, at, column(low[:, at]))


def parts_of(slots):
    slots = slots.astype(jnp.int32)
    return slots & (LOW - 1), slots // LOW


def feature_columns(out, at, tree):
    out[0:64, at] = tree[0:64].astype(bf16)
    out[64:128, at] = tree[0:64].astype(bf16)
    out[128:192, at] = tree[64:128].astype(bf16)
    out[192:208, at] = jnp.where(iota((16, tree.shape[1]), 0) < 8, tree[128:144].astype(f32), 0.0).astype(bf16)
    out[208:256, at] = jnp.zeros((48, tree.shape[1]), bf16)


def feature_rows(high, low, extra):
    first = jnp.transpose(jnp.concatenate([high, low], 0))
    second = jnp.transpose(jnp.concatenate([high, extra, jnp.zeros((56, high.shape[1]), f32)], 0))
    return first.astype(bf16), second.astype(bf16)


def target_columns(layout, out, tree_ref):
    span = layout.span
    for leaf in range(out.shape[1] // span):
        here = aligned(leaf * LEAF + layout.core() * span, span, span)
        feature_columns(out, slice(leaf * span, (leaf + 1) * span), tree_ref[:, here])


def tile_exponents(layout, tiles, tile, a_ref, bt_ref):
    source = aligned(tiles[1, tile] * LEAF, LEAF, LEAF)
    target = aligned(tiles[0, tile] * layout.span, layout.span, layout.span)
    return nn(a_ref[source, :], bt_ref[:, target])


def tiles_ahead(layout, tiles, a_ref, bt_ref, even, odd, made, made_hbm, sems):
    def send(tile):
        return pltpu.make_async_copy(made.at[tile], made_hbm.at[tile], sems.at[tile])

    even[...] = tile_exponents(layout, tiles, 0, a_ref, bt_ref)

    def step(pair, carry):
        for tile, ready, upcoming in ((2 * pair, even, odd), (2 * pair + 1, odd, even)):
            upcoming[...] = tile_exponents(layout, tiles, tile + 1, a_ref, bt_ref)
            made[tile] = jnp.exp(ready[...]).astype(bf16)
            send(tile).start()
        return carry

    lax.fori_loop(0, layout.ahead // 2, step, 0)
    return [send(tile) for tile in range(layout.ahead)]


def list_tiles(count_ref, list_ref, tiles, times):
    every = count_ref.shape[1]

    def tally(leaf, filled):
        for other in range(every):
            times[other] = (leaf == other).astype(jnp.int32)

        def add(slot, carry):
            at = list_ref[leaf, slot]
            times[at] = times[at] + 1
            return carry

        lax.fori_loop(0, count_ref[0, leaf], add, 0)
        for other in range(every):
            tiles[0, filled] = leaf
            tiles[1, filled] = other
            tiles[2, filled] = times[other]
            filled = filled + (times[other] > 0).astype(jnp.int32)
        return filled

    filled = lax.fori_loop(0, every, tally, jnp.int32(0))

    def pad(more, carry):
        tiles[0, more] = 0
        tiles[1, more] = 0
        return carry

    lax.fori_loop(filled, tiles.shape[1] - 1, pad, 0)
    tiles[0, tiles.shape[1] - 1] = filled


def points_kernel(layout, trees, count_ref, list_ref, upper_ref, *refs):
    if not layout.fine:
        small_ref, refs = refs[0], refs[1:]
    else:
        small_ref = None
    place_refs, refs = refs[: layout.count], refs[layout.count :]
    tree_ref, a_hbm, base_hbm, sk_ref, upper_tiles_ref, top_ref, slot_ref, info_ref, tiles, made_hbm = refs[:10]
    masked, low_hot, a_ref, base_ref, sk_t, sk_bt, sems, times, bt_ref, even, odd, made, made_sems = refs[10:]
    blocks, rows = layout.blocks, layout.rows

    def keep(node, found):
        at = slice(node * SK, (node + 1) * SK)
        sk_t[:, at] = found.astype(bf16)
        sk_ref[at, 0:128], sk_ref[at, 128:256] = feature_rows(found[0:64], found[64:128], found[136:144])
        feature_columns(sk_bt, at, found)

    high_parts = rows // LOW
    infos = []
    for index in range(blocks):
        tail = layout.gather(place_refs, index, slice(TAIL, PLACE_ROWS))
        slots = tail[SLOT : SLOT + 1]
        slot_ref[index : index + 1, :] = slots
        infos.append(layout.info(place_refs, small_ref, index))
        info_ref[index] = infos[-1]
        low_part, high_part = parts_of(slots)
        low_by_column(low_hot.at[index], low_part.astype(f32))
        points = layout.gather(place_refs, index, slice(0, TAIL))
        high, low = two(points)
        nh, nm, nl = three(tail[NORM : NORM + 1])
        sub = iota((16, rows), 0)
        norms = jnp.where((sub == 3) | (sub == 8), nh, jnp.where((sub == 4) | (sub == 9), nm, nl))
        is_norm = ((sub >= 3) & (sub < 6)) | ((sub >= 8) & (sub < 11))
        is_one = (sub < 3) | ((sub >= 11) & (sub < 14))
        extra = jnp.where(is_norm, norms, jnp.where(is_one, 1.0, 0.0))
        for h in range(high_parts):
            here = high_part == h
            at = h * COORD
            masked[index, at : at + 64, :] = jnp.where(here, high.astype(f32), 0.0).astype(bf16)
            masked[index, at + 64 : at + 128, :] = jnp.where(here, low.astype(f32), 0.0).astype(bf16)
            masked[index, at + 128 : at + COORD, :] = jnp.where(here, extra, 0.0).astype(bf16)
    copies = []
    for index in range(blocks):
        placed = nn(masked[index], low_hot[index])
        for h in range(high_parts):
            part = placed[h * COORD : (h + 1) * COORD]
            at = slice(index * rows + h * LOW, index * rows + (h + 1) * LOW)
            tree_ref[:, at] = part.astype(bf16)
            a_ref[at, 0:128], a_ref[at, 128:256] = feature_rows(part[0:64], part[64:128], part[136:144])
        mine = slice(index * rows, (index + 1) * rows)
        copies.append(pltpu.make_async_copy(a_ref.at[mine], a_hbm.at[mine], sems.at[0, index]))
        copies[-1].start()
    for index in range(blocks):
        mine = slice(index * rows, (index + 1) * rows)
        picked = onehot(iota((rows, SK), 0) == infos[index][BASE : BASE + 1].astype(jnp.int32))
        keep(index, nn(tree_ref[:, mine], picked))
    for index in range(blocks):
        mine = slice(index * rows, (index + 1) * rows)
        base_ref[index] = jnp.exp(nn(a_ref[mine, :], sk_bt[:, index * SK : (index + 1) * SK])).astype(bf16)
        copies.append(pltpu.make_async_copy(base_ref.at[index], base_hbm.at[index], sems.at[1, index]))
        copies[-1].start()
    start, count, offset, total = 0, blocks, 0, blocks * trees
    while count > 1:
        nodes = count // 2
        for j in range(nodes):
            pair = slice((start + 2 * j) * SK, (start + 2 * j + 2) * SK)
            row = offset + lax.axis_index("leaf") * nodes + j
            picked = onehot(iota((2 * SK, SK), 0) == upper_ref[pl.ds(row, 1), :])
            here = start + count + j
            keep(here, nn(sk_t[:, pair], picked))
            upper_tiles_ref[here - blocks] = jnp.exp(nn(sk_ref[pair, :], sk_bt[:, here * SK : (here + 1) * SK]))
        total = total // 2
        offset = offset + total
        start, count = start + count, nodes
    found = sk_t[:, start * SK : (start + 1) * SK].astype(f32)
    top_ref[0:64, :] = found[0:64] + found[64:128]
    top_ref[64:72, :] = found[128:136]
    list_tiles(count_ref, list_ref, tiles, times)
    target_columns(layout, bt_ref, tree_ref)
    copies += tiles_ahead(layout, tiles, a_ref, bt_ref, even, odd, made, made_hbm, made_sems)
    for copy in copies:
        copy.wait()


def weights_kernel(layout, base_hbm, upper_tiles_ref, top_ref, slot_ref, *refs):
    light_refs, refs = refs[: layout.count], refs[layout.count :]
    if layout.fine:
        order = far_first(layout.blocks)
        order = order + [layout.blocks + step for step in order]
        light_refs = [light_refs[order.index(g)] for g in range(layout.count)]
    w_ref, coef_ref, pack_ref, masked, low_hot, base_ref, sems = refs
    blocks, rows = layout.blocks, layout.rows
    width = light_refs[0].shape[0]
    each = width // layout.halves
    pack_ref[0:PLACE_ROWS, :] = top_ref[...]
    for index in range(blocks):
        pltpu.make_async_copy(base_hbm.at[index], base_ref.at[index], sems.at[index]).start()

    def keep(node, coef):
        coef_ref[:, node * SK : (node + 1) * SK] = stack_two(coef)
        pack_ref[PLACE_ROWS:, :] = coef

    for index in range(blocks):
        low_part, high_part = parts_of(slot_ref[index : index + 1, :])
        low_by_column(low_hot.at[index], low_part.astype(f32))
        for half in range(layout.halves):
            light = [ref[layout.columns(g, half, each), layout.lanes(index)] for g, ref in enumerate(light_refs)]
            light = lanes_of(light)
            for h in range(rows // LOW):
                at = h * width + half * each
                masked[index, at : at + each, :] = jnp.where(high_part == h, light, 0.0).astype(bf16)
    for index in range(blocks):
        placed = nn(masked[index], low_hot[index])
        for h in range(rows // LOW):
            at = index * rows + h * LOW
            w_ref[:, at : at + LOW] = placed[h * width : (h + 1) * width].astype(bf16)
    for index in range(blocks):
        pltpu.make_async_copy(base_hbm.at[index], base_ref.at[index], sems.at[index]).wait()
        keep(index, nn(w_ref[:, index * rows : (index + 1) * rows], base_ref[index]))
    start, count = 0, blocks
    while count > 1:
        for j in range(count // 2):
            pair = slice((start + 2 * j) * SK, (start + 2 * j + 2) * SK)
            here = start + count + j
            high, low = two(upper_tiles_ref[here - blocks])
            coef = nn(coef_ref[:, pair], high)
            keep(here, coef[:width] + coef[width:] + nn(coef_ref[0:width, pair], low))
        start, count = start + count, count // 2


def near_kernel(layout, tiles, a_hbm, made_hbm, tree_ref, w_ref, acc, a_ref, bt_ref, made, sems, even, odd, even_tile, odd_tile):
    ahead, span = layout.ahead, layout.span

    def fetch(tile):
        return pltpu.make_async_copy(made_hbm.at[tile], made.at[tile], sems.at[tile])

    copy = pltpu.make_async_copy(a_hbm, a_ref, sems.at[ahead])
    copy.start()
    for tile in range(ahead):
        fetch(tile).start()
    filled = tiles[0, tiles.shape[1] - 1]
    acc[...] = jnp.zeros_like(acc)
    target_columns(layout, bt_ref, tree_ref)

    def exponents(tile):
        return tile_exponents(layout, tiles, tile, a_ref, bt_ref)

    def add(tile, block):
        source = aligned(tiles[1, tile] * LEAF, LEAF, LEAF)
        target = aligned(tiles[0, tile] * span, span, span)
        acc[:, target] += tiles[2, tile].astype(f32) * nn(w_ref[:, source], block)

    copy.wait()

    @pl.when(filled > ahead)
    def _():
        even[...] = exponents(ahead)
        even_tile[...] = jnp.exp(even[...]).astype(bf16)
        odd[...] = exponents(ahead + 1)

        def phase(tile, upcoming, ready, finished, previous):
            upcoming[...] = exponents(tile + 1)
            finished[...] = jnp.exp(ready[...]).astype(bf16)
            add(tile - 1, previous[...])

        def step(pair, carry):
            phase(ahead + 2 * pair + 1, even, odd, odd_tile, even_tile)
            phase(ahead + 2 * pair + 2, odd, even, even_tile, odd_tile)
            return carry

        pairs = (filled - ahead - 1) // 2
        lax.fori_loop(0, pairs, step, 0)
        add(ahead + 2 * pairs, even_tile[...])

        @pl.when(ahead + 2 * pairs + 1 < filled)
        def _():
            odd_tile[...] = jnp.exp(odd[...]).astype(bf16)
            add(ahead + 2 * pairs + 1, odd_tile[...])

    def arrived(quad, carry):
        for more in range(4):
            fetch(4 * quad + more).wait()
            tile = 4 * quad + more

            @pl.when(tile < filled)
            def _():
                add(tile, made[tile])

        return carry

    lax.fori_loop(0, ahead // 4, arrived, 0)


def far_kernel(layout, low_levels, pack_ref, slot_ref, info_ref, tree_ref, sk_ref, coef_ref, near_ref, *refs):
    out_refs, refs = refs[: layout.halves], refs[layout.halves :]
    tops, coefs, scaled, low_hot, bt_ref, sums, masked = refs[:7]
    powers, tiles = refs[7:9], refs[9:11]
    blocks, rows = layout.blocks, layout.rows
    ups, width = pack_ref.shape[0], near_ref.shape[0]
    levels = low_levels + ups
    span, core = layout.span, layout.core()
    per_block = rows // LEAF
    lane = iota((1, SK), 1)
    for up in range(ups):
        pack = pack_ref[up]
        high, low = two(pack[0:64])
        sub = iota((8, SK), 0)
        extra = jnp.where(sub == 0, pack[67:68], jnp.where(sub == 1, pack[68:69], pack[69:70]))
        extra = jnp.where(sub < 3, extra, jnp.where(sub < 6, 1.0, 0.0))
        at = slice((low_levels + up) * SK, (low_levels + up + 1) * SK)
        rows_of = feature_rows(high.astype(f32), low.astype(f32), extra)
        coef = stack_two(pack[PLACE_ROWS:])
        for index in range(blocks):
            tops[index, at, 0:128], tops[index, at, 128:256] = rows_of
            coefs[index, :, at] = coef
    for index in range(blocks):
        node, start, count = index, 0, blocks
        for level in range(low_levels):
            at = slice(level * SK, (level + 1) * SK)
            other = slice((start + (node ^ 1)) * SK, (start + (node ^ 1) + 1) * SK)
            tops[index, at, :] = sk_ref[other, :]
            coefs[index, :, at] = coef_ref[:, other]
            node, start, count = node // 2, start + count, count // 2
        for leaf in range(per_block):
            flags = info_ref[index, FLAGS + leaf : FLAGS + leaf + 1, :]
            used = []
            for level in range(levels):
                flag = jnp.sum(jnp.where(lane == level, flags, 0.0), axis=1, keepdims=True)
                used.append(jnp.broadcast_to(flag, (1, SK)))
            used = jnp.concatenate(used, 1)
            scaled[index * per_block + leaf] = (coefs[index].astype(f32) * used).astype(bf16)

    target_columns(layout, bt_ref, tree_ref)

    def exponents(leaf):
        powers[leaf % 2][...] = nn(tops[leaf // per_block], bt_ref[:, leaf * span : (leaf + 1) * span])

    def product(leaf):
        here = slice(leaf * span, (leaf + 1) * span)
        far = nn(scaled[leaf], tiles[leaf % 2][...])
        sums[:, here] = near_ref[:, here] + far[:width] + far[width:]

    leaves = blocks * per_block
    exponents(0)
    for leaf in range(leaves):
        if leaf + 1 < leaves:
            exponents(leaf + 1)
        tiles[leaf % 2][...] = jnp.exp(powers[leaf % 2][...]).astype(bf16)
        if leaf:
            product(leaf - 1)
    product(leaves - 1)

    high_parts = []
    pieces = rows // LOW // layout.halves
    for index in range(blocks):
        low_part, high_part = parts_of(slot_ref[index : index + 1, :])
        high_parts.append(high_part)
        for c in range(rows // LANES):
            at = slice(c * LANES, (c + 1) * LANES)
            low_hot[index, :, at] = onehot(iota((LOW, LANES), 0) == low_part[:, at])
        for k in range(pieces):
            at = (index * pieces + k) * LOW
            masked[index, k * 2 * width : (k + 1) * 2 * width, :] = stack_two(sums[:, at : at + LOW])
    for index in range(blocks):
        moved = nn(masked[index], low_hot[index])
        result = jnp.zeros((2 * width, rows), f32)
        for k in range(pieces):
            here = high_parts[index] == k * layout.halves + core
            result = jnp.where(here, moved[k * 2 * width : (k + 1) * 2 * width], result)
        result = result[:width] + result[width:]
        if not layout.fine:
            out_refs[0][0, :, layout.lanes(index)] = result
            continue
        for g in range(layout.count):
            out_ref = out_refs[g // blocks]
            out_ref[g % blocks, :, layout.lanes(index)] = result[:, g * layout.per : (g + 1) * layout.per]


def add_kernel(kept_ref, got_ref, *out_refs):
    half = kept_ref.shape[1] // 2
    for step, out_ref in enumerate(out_refs):
        out_ref[0:half, :] = kept_ref[step, 0:half, :] + got_ref[step, half:, :]
        out_ref[half:, :] = kept_ref[step, half:, :] + got_ref[step, 0:half, :]


def far_first(blocks):
    return sorted(range(blocks), key=lambda step: -(step * 2 // blocks))


def final_kernel(blocks, pos_ref, *refs):
    back_refs, (weights_ref, out_ref, perm, vals) = refs[:-4], refs[-4:]
    chunks = pos_ref.shape[0]
    rows = chunks * LANES
    width, split = back_refs[0].shape
    width = LANES // blocks if blocks else width
    for r in range(chunks):
        spread(perm, slice(r * LANES, (r + 1) * LANES), column(pos_ref[r : r + 1, :]))
    for g, back_ref in enumerate(back_refs):
        columns, at = 0, slice(0, rows)
        value = back_ref[...]
        if blocks:
            columns = (lax.axis_index("sub") ^ far_first(blocks)[g % blocks]) * width
            at = aligned((lax.axis_index("leaf") ^ lax.axis_index("rep") ^ (g // blocks)) * split, split, split)
            value = value[0:width] if g < blocks else value[width:]
        high, low = two(value)
        vals[aligned(columns, width, width), at] = high
        vals[aligned(columns + LANES, width, width), at] = low
    step = 256
    for s in range(rows // step):
        here = slice(s * step, (s + 1) * step)
        moved = nt(perm[here, :], vals[...])
        out_ref[here, :] = ridge * weights_ref[here, :] + moved[:, :LANES] + moved[:, LANES:]


def upper_levels(pack, skeleton_upper, my_leaf, trees, blocks):
    devices = trees * blocks
    level = blocks.bit_length() - 1
    offset = sum(devices >> step for step in range(1, level + 1))
    line = jnp.arange(pack.shape[0])[:, None]
    is_point, is_norm = line < DIM, (line >= DIM + 3) & (line < DIM + 6)
    is_coef = line >= PLACE_ROWS
    packs, own, stride = [], pack, 1
    while stride < trees:
        other = lax.ppermute(own, "leaf", [(i, i ^ stride) for i in range(trees)])
        packs.append(other)
        stride *= 2
        if stride < trees:
            second = (my_leaf // (stride // 2)) % 2 == 1
            pair = jnp.where(second, jnp.concatenate([other, own], 1), jnp.concatenate([own, other], 1))
            chosen = pair[:, skeleton_upper[offset + my_leaf // stride]]
            level += 1
            offset += devices >> level
            norms = jnp.sum(jnp.where(is_norm, pair, 0.0), axis=0)
            chosen_norms = jnp.sum(jnp.where(is_norm, chosen, 0.0), axis=0)
            inner = jnp.dot(
                jnp.where(is_point, pair, 0.0).T, jnp.where(is_point, chosen, 0.0), precision=highest
            )
            tile = jnp.exp(inner + norms[:, None] + chosen_norms[None])
            own = jnp.where(is_coef, jnp.dot(pair, tile, precision=highest), chosen)
    return jnp.stack(packs)


def body(points, weights, tree_slot, near_count, near_list, skeleton_base, skeleton_upper, far_use):
    blocks, trees, reps = lax.axis_size("sub"), lax.axis_size("leaf"), lax.axis_size("rep")
    devices = blocks * trees
    rows, columns = weights.shape
    low_levels = blocks.bit_length() - 1
    ups = trees.bit_length() - 1
    width = columns // blocks
    part = rows // trees
    per = part // blocks
    total = blocks * rows
    leaves = total // LEAF
    my_leaf = lax.axis_index("leaf")
    fine = trees == 2 and reps == 2 and per % LANES == 0
    layout = Layout(blocks, trees, rows, fine)
    split = part if fine else rows
    cols = width * layout.halves

    place, pos = pl.pallas_call(
        functools.partial(place_kernel, fine),
        out_shape=(shaped((PLACE_ROWS, split), f32), shaped((rows // LANES, LANES), f32)),
        in_specs=[spec()] * 4,
        out_specs=(spec(),) * 2,
        scratch_shapes=[vm((split // LOW * COORD, rows), bf16), vm((rows, LOW), bf16)],
        compiler_params=params(),
        name="sort_points",
    )(tree_slot.reshape(rows // LANES, LANES), points.T, skeleton_base, far_use)
    axes = ("leaf", "sub", "rep")

    def swap(value, step, other=0):
        pairs = []
        for leaf in range(trees):
            for sub in range(blocks):
                for core in range(reps):
                    to = ((leaf ^ core ^ other) * blocks + (sub ^ step)) * reps + core
                    pairs.append(((leaf * blocks + sub) * reps + core, to))
        return lax.ppermute(value, axes, pairs)

    def other_core(value):
        return lax.ppermute(value, "rep", [(0, 1), (1, 0)])

    def sorted_light():
        if fine:
            shapes = (shaped((blocks, width, part), f32),) * 2
        else:
            shapes = (shaped((columns, rows), f32),)
        return pl.pallas_call(
            functools.partial(light_kernel, blocks if fine else 0),
            out_shape=shapes,
            in_specs=[spec()] * 2,
            out_specs=(spec(),) * len(shapes),
            scratch_shapes=[
                vm((rows // LOW * LANES, rows), bf16),
                vm((rows, LOW), bf16),
                vm((rows // LOW, LANES, LOW), f32),
            ],
            compiler_params=params(40),
            name="sort_weights",
        )(in_hbm(pos), in_hbm(weights))

    if fine:
        place = {0: swap(place, 0)}
        stride = blocks // 2
        while stride:
            for step in sorted(place):
                place[step | stride] = lax.ppermute(place[step], "sub", [(i, i ^ stride) for i in range(blocks)])
            stride //= 2
        kept, sent = sorted_light()
        light = pl.pallas_call(
            join_kernel,
            out_shape=(shaped((cols, part), f32),) * blocks,
            in_specs=[spec()] * 2,
            out_specs=(spec(),) * blocks,
            compiler_params=params(40),
            name="join_cores",
        )(kept, other_core(sent))
        place, light = lax.optimization_barrier((place, light))
        theirs = {step: other_core(one) for step, one in place.items()}
        place = [place[step] for step in range(blocks)] + [theirs[step] for step in range(blocks)]
        light = [swap(light[step], step) for step in far_first(blocks)]
        small = []
    else:
        info = jnp.pad(far_use.astype(f32), ((FLAGS, 5 - far_use.shape[0]), (0, SK - far_use.shape[1])))
        small = [lax.all_gather(info.at[BASE].set(skeleton_base[0].astype(f32)), "sub", axis=0, tiled=False)]
        place = place.reshape(PLACE_ROWS, trees, part).transpose(1, 0, 2)
        place = lax.all_to_all(place, "leaf", split_axis=0, concat_axis=0, tiled=True)
        place = lax.all_gather(place, "sub", axis=0, tiled=False)
        place = place.transpose(1, 0, 2, 3).reshape(devices, PLACE_ROWS, blocks, per)
        place = [place.transpose(1, 2, 0, 3).reshape(PLACE_ROWS, total)]
        light = sorted_light()[0].reshape(columns, trees, part).transpose(1, 0, 2).reshape(devices, width, part)
        light = lax.all_to_all(light, ("leaf", "sub"), split_axis=0, concat_axis=0, tiled=True)
        light = light.reshape(devices, width, blocks, per)
        light = [light.transpose(1, 2, 0, 3).reshape(width, total)]

    nodes = 2 * blocks - 1
    tree, feat_a, base, sk, upper_tiles, top, slots, info, tiles, made = pl.pallas_call(
        functools.partial(points_kernel, layout, trees),
        out_shape=(
            vm((COORD, total), bf16),
            pltpu.MemorySpace.HBM((total, FEAT), bf16),
            pltpu.MemorySpace.HBM((blocks, rows, SK), bf16),
            vm((nodes * SK, FEAT), bf16),
            vm((blocks - 1, 2 * SK, SK), f32),
            vm((PLACE_ROWS, SK), f32),
            vm((blocks, rows), f32),
            vm((blocks, 8, SK), f32),
            pltpu.MemorySpace.HBM((3, leaves * leaves + 3), jnp.int32),
            pltpu.MemorySpace.HBM((layout.ahead, LEAF, layout.span), bf16),
        ),
        in_specs=[spec(SMEM)] * 2 + [spec()] * (1 + len(small) + layout.count),
        out_specs=(spec(), spec(pl.ANY), spec(pl.ANY)) + (spec(),) * 5 + (spec(SMEM), spec(pl.ANY)),
        scratch_shapes=[
            vm((blocks, rows // LOW * COORD, rows), bf16),
            vm((blocks, rows, LOW), bf16),
            vm((total, FEAT), bf16),
            vm((blocks, rows, SK), bf16),
            vm((COORD, nodes * SK), bf16),
            vm((FEAT, nodes * SK), bf16),
            pltpu.SemaphoreType.DMA((2, blocks)),
            pltpu.SMEM((leaves,), jnp.int32),
            vm((FEAT, total // layout.halves), bf16),
            vm((LEAF, layout.span), f32),
            vm((LEAF, layout.span), f32),
            vm((layout.ahead, LEAF, layout.span), bf16),
            pltpu.SemaphoreType.DMA((layout.ahead,)),
        ],
        compiler_params=params(40),
        name="tree_points",
    )(in_hbm(near_count), in_hbm(near_list[0]), in_hbm(skeleton_upper), *small, *place)

    if fine:
        light, slots = lax.optimization_barrier((light, slots))
        light = light + [other_core(one) for one in light]
    tree_light, coefs, pack = pl.pallas_call(
        functools.partial(weights_kernel, layout),
        out_shape=(
            vm((cols, total), bf16),
            vm((2 * cols, nodes * SK), bf16),
            shaped((PLACE_ROWS + cols, SK), f32),
        ),
        in_specs=[spec(pl.ANY)] + [spec()] * (3 + layout.count),
        out_specs=(spec(),) * 3,
        scratch_shapes=[
            vm((blocks, rows // LOW * cols, rows), bf16),
            vm((blocks, rows, LOW), bf16),
            vm((blocks, rows, SK), bf16),
            pltpu.SemaphoreType.DMA((blocks,)),
        ],
        compiler_params=params(40),
        name="tree_weights",
    )(in_hbm(base), held(upper_tiles), held(top), held(slots), *light)

    packs = upper_levels(pack, skeleton_upper, my_leaf, trees, blocks)

    near = pl.pallas_call(
        functools.partial(near_kernel, layout),
        out_shape=vm((cols, total // layout.halves), f32),
        in_specs=[spec(SMEM), spec(pl.ANY), spec(pl.ANY)] + [spec()] * 2,
        out_specs=spec(),
        scratch_shapes=[
            vm((total, FEAT), bf16),
            vm((FEAT, total // layout.halves), bf16),
            vm((layout.ahead, LEAF, layout.span), bf16),
            pltpu.SemaphoreType.DMA((layout.ahead + 1,)),
        ]
        + [vm((LEAF, layout.span), f32)] * 2
        + [vm((LEAF, layout.span), bf16)] * 2,
        compiler_params=params(40),
        name="near",
    )(in_hbm(tiles), in_hbm(feat_a), in_hbm(made), held(tree), held(tree_light))

    levels = low_levels + ups
    back = pl.pallas_call(
        functools.partial(far_kernel, layout, low_levels),
        out_shape=(shaped((layout.count // layout.halves, cols, total // layout.count), f32),) * layout.halves,
        in_specs=[spec()] * 7,
        out_specs=(spec(),) * layout.halves,
        scratch_shapes=[
            vm((blocks, levels * SK, FEAT), bf16),
            vm((blocks, 2 * cols, levels * SK), bf16),
            vm((leaves, 2 * cols, levels * SK), bf16),
            vm((blocks, LOW, rows), bf16),
            vm((FEAT, total // layout.halves), bf16),
            vm((cols, total // layout.halves), f32),
            vm((blocks, rows // LOW // layout.halves * 2 * cols, LOW), bf16),
        ]
        + [vm((levels * SK, layout.span), f32)] * 2
        + [vm((levels * SK, layout.span), bf16)] * 2,
        compiler_params=params(40),
        name="far",
    )(packs, *[held(one) for one in (slots, info, tree, sk, coefs, near)])

    if fine:
        kept, sent = back
        sums = pl.pallas_call(
            add_kernel,
            out_shape=(shaped((cols, part), f32),) * blocks,
            in_specs=[spec()] * 2,
            out_specs=(spec(),) * blocks,
            compiler_params=params(40),
            name="add_cores",
        )(kept, other_core(sent))
        back = [swap(sums[step], step) for step in far_first(blocks)]
        back = back + [other_core(one) for one in back]
    else:
        back = back[0].reshape(cols, blocks, devices, per).transpose(2, 0, 1, 3).reshape(devices, width, part)
        back = lax.all_to_all(back, ("leaf", "sub"), split_axis=0, concat_axis=0, tiled=True)
        back = [back.reshape(trees, columns, part).transpose(1, 0, 2).reshape(columns, rows)]

    return pl.pallas_call(
        functools.partial(final_kernel, blocks if fine else 0),
        out_shape=shaped((rows, columns), f32),
        in_specs=[spec()] * (2 + layout.count),
        out_specs=spec(),
        scratch_shapes=[vm((rows, rows), bf16), vm((2 * LANES, rows), bf16)],
        compiler_params=params(40),
        name="to_input_order",
    )(pos, *back, weights)


def solution(mesh):
    in_specs = (
        P(("groups", "leaf", "sub"), None),
        P(("groups", "leaf", "sub"), "rep"),
        P(("groups", "leaf", "sub")),
        P(("groups", "leaf"), None),
        P(("groups", "leaf"), None, None),
        P(("groups", "leaf", "sub"), None),
        P("groups", None),
        P(("groups", "leaf", "sub"), None),
    )
    out_specs = P(("groups", "leaf", "sub"), "rep")
    return jax.shard_map(body, mesh=mesh, in_specs=in_specs, out_specs=out_specs, check_vma=False)
```

```python
import functools

import jax
import jax.numpy as jnp
from jax import lax
from jax.experimental import pallas as pl
from jax.experimental.pallas import tpu as pltpu
from jax.sharding import PartitionSpec as P

DIM = 64
LEAF = 512
SK = 128
LANES = 128
FEAT = 256
LOW = 256
AHEAD = 8
COORD = 144

highest = lax.Precision.HIGHEST
point_scale = 0.25
ridge = 0.5
PLACE_ROWS = 72
TAIL = 64
SLOT, NORM, BASE, FLAGS = 0, 1, 2, 3
f32 = jnp.float32
bf16 = jnp.bfloat16
VMEM = pltpu.MemorySpace.VMEM
SMEM = pltpu.MemorySpace.SMEM


def spec(space=VMEM):
    return pl.BlockSpec(memory_space=space)


def params(mib=58):
    return pltpu.CompilerParams(vmem_limit_bytes=mib * 1024 * 1024)


def in_hbm(array):
    return pltpu.with_memory_space_constraint(array, pltpu.MemorySpace.HBM)


def held(array):
    return pltpu.with_memory_space_constraint(array, VMEM)


def vm(shape, dtype):
    return pltpu.VMEM(shape, dtype)


def shaped(shape, dtype):
    return jax.ShapeDtypeStruct(shape, dtype)


def nt(left, right):
    return lax.dot_general(left, right, (((1,), (1,)), ((), ())), preferred_element_type=f32)


def nn(left, right):
    return jnp.dot(left, right, preferred_element_type=f32)


def column(row):
    return jnp.transpose(jnp.broadcast_to(row, (LANES, LANES)))


def iota(shape, dim):
    return lax.broadcasted_iota(jnp.int32, shape, dim)


def onehot(mask):
    return jnp.where(mask, 1.0, 0.0).astype(bf16)


def two(value):
    high = value.astype(bf16)
    return high, (value - high.astype(f32)).astype(bf16)


def three(value):
    high = value.astype(bf16).astype(f32)
    mid = (value - high).astype(bf16).astype(f32)
    return high, mid, (value - high - mid).astype(bf16).astype(f32)


def lanes_of(blocks):
    return blocks[0] if len(blocks) == 1 else jnp.concatenate(blocks, 1)


def aligned(start, size, unit):
    return pl.ds(pl.multiple_of(start, unit), size)


def stack_two(value):
    high, low = two(value)
    return jnp.concatenate([high, low], 0)


def spread(perm, here, rank):
    lane = iota((LANES, LANES), 1).astype(f32)
    for c in range(perm.shape[1] // LANES):
        perm[here, c * LANES : (c + 1) * LANES] = onehot(lane + float(c * LANES) == rank)


def place_kernel(fine, slot_ref, points_ref, base_ref, flag_ref, place_ref, pos_ref, masked, low_hot):
    chunks = slot_ref.shape[0]
    slots = slot_ref[...]
    slot = slots.astype(f32)
    within = slots & (chunks * LANES - 1)
    high, low = (within >> 5).astype(f32), (within & 31).astype(f32)
    ranks = []
    for r in range(chunks):
        here = slice(r * LANES, (r + 1) * LANES)
        mine = column(slot[r : r + 1])
        before = jnp.zeros((LANES, LANES), f32)
        for c in range(chunks):
            before += jnp.where(slot[c : c + 1] < mine, 1.0, 0.0)
        rank = jnp.broadcast_to(jnp.sum(before, axis=1, keepdims=True), (LANES, LANES))
        ranks.append(jnp.transpose(rank)[0:1])
        pos_ref[r : r + 1, :] = ranks[-1]
        spread(low_hot, here, (rank.astype(jnp.int32) & (LOW - 1)).astype(f32))
    scaled = points_ref[...] * point_scale
    ph, plo = two(scaled)
    nh, nm, nl = three(-0.5 * jnp.sum(scaled * scaled, axis=0, keepdims=True))
    high, low = lanes_of([high[c : c + 1] for c in range(chunks)]), lanes_of([low[c : c + 1] for c in range(chunks)])
    sub = iota((16, chunks * LANES), 0)
    extra = jnp.where(sub == 0, high, jnp.where(sub == 1, low, 0.0))
    extra = jnp.where(sub == 2, nh, jnp.where(sub == 3, nm, jnp.where(sub == 4, nl, extra)))
    high_part = lanes_of(ranks).astype(jnp.int32) // LOW
    parts = place_ref.shape[1] // LOW
    first = (lax.axis_index("leaf") ^ lax.axis_index("rep")) * parts if fine else 0
    for h in range(parts):
        here = high_part == first + h
        masked[h * COORD : h * COORD + 64, :] = jnp.where(here, ph.astype(f32), 0.0).astype(bf16)
        masked[h * COORD + 64 : h * COORD + 128, :] = jnp.where(here, plo.astype(f32), 0.0).astype(bf16)
        masked[h * COORD + 128 : (h + 1) * COORD, :] = jnp.where(here, extra, 0.0).astype(bf16)
    placed = nn(masked[...], low_hot[...])
    tail = iota((PLACE_ROWS - TAIL, LOW), 0)
    for h in range(parts):
        at = slice(h * LOW, (h + 1) * LOW)
        moved = placed[h * COORD : (h + 1) * COORD]
        place_ref[0:TAIL, at] = moved[0:64] + moved[64:128]
        slot_row = moved[128:129] * 32.0 + moved[129:130]
        norm_row = moved[130:131] + moved[131:132] + moved[132:133]
        place_ref[TAIL:, at] = jnp.where(tail == SLOT, slot_row, jnp.where(tail == NORM, norm_row, 0.0))
    if fine:
        place_ref[TAIL + BASE : TAIL + BASE + 1, 0:SK] = base_ref[...].astype(f32)
        place_ref[TAIL + FLAGS : TAIL + FLAGS + flag_ref.shape[0], 0 : flag_ref.shape[1]] = flag_ref[...].astype(f32)


def light_kernel(blocks, pos_ref, weights_ref, *refs):
    light_refs, (masked, low_hot, placed) = refs[:-3], refs[-3:]
    chunks = pos_ref.shape[0]
    high_count = chunks * LANES // LOW
    low_part, high_part = parts_of(lanes_of([pos_ref[c : c + 1, :] for c in range(chunks)]))
    low_by_column(low_hot, low_part.astype(f32))
    for c in range(chunks):
        at = slice(c * LANES, (c + 1) * LANES)
        turned = jnp.transpose(weights_ref[at, :])
        for h in range(high_count):
            masked[h * LANES : (h + 1) * LANES, at] = jnp.where(high_part[:, at] == h, turned, 0.0).astype(bf16)
    moved = nn(masked[...], low_hot[...])
    for h in range(high_count):
        if not blocks:
            light_refs[0][:, h * LOW : (h + 1) * LOW] = moved[h * LANES : (h + 1) * LANES]
        placed[h] = moved[h * LANES : (h + 1) * LANES]
    if not blocks:
        return
    width, parts = LANES // blocks, high_count // 2
    for other, light_ref in enumerate(light_refs):
        first = (lax.axis_index("leaf") ^ lax.axis_index("rep") ^ other) * parts
        for step in range(blocks):
            columns = aligned((lax.axis_index("sub") ^ step) * width, width, width)
            for h in range(parts):
                light_ref[step, :, h * LOW : (h + 1) * LOW] = placed[first + h, columns, :]


def join_kernel(kept_ref, got_ref, *out_refs):
    half = kept_ref.shape[1]
    for step, out_ref in enumerate(out_refs):
        out_ref[0:half, :] = kept_ref[step]
        out_ref[half:, :] = got_ref[step]


class Layout:
    def __init__(self, blocks, trees, rows, fine):
        self.blocks, self.rows, self.fine = blocks, rows, fine
        self.count = blocks * trees if fine else 1
        self.per = rows // self.count
        self.halves = 2 if fine else 1
        self.span = LEAF // self.halves
        self.ahead = AHEAD // 4 * 4 if fine else 4

    def core(self):
        return lax.axis_index("rep") if self.fine else 0

    def lanes(self, index):
        return slice(index * self.per, (index + 1) * self.per)

    def columns(self, group, half, each):
        if self.fine and group >= self.blocks:
            half = 1 - half
        return slice(half * each, (half + 1) * each)

    def gather(self, refs, index, part):
        return lanes_of([ref[part, self.lanes(index)] for ref in refs])

    def info(self, refs, small_ref, index):
        if not self.fine:
            return small_ref[index]
        core = lax.axis_index("rep")
        found = jnp.zeros((PLACE_ROWS - TAIL, SK), f32)
        for step in range(self.blocks):
            mine, theirs = refs[step][TAIL:, 0:SK], refs[self.blocks + step][TAIL:, 0:SK]
            here = jnp.where(core == 0, mine, theirs)
            found = jnp.where((lax.axis_index("sub") ^ step) == index, here, found)
        return found


def low_by_column(out, low):
    for c in range(out.shape[0] // LANES):
        at = slice(c * LANES, (c + 1) * LANES)
        spread(out, at, column(low[:, at]))


def parts_of(slots):
    slots = slots.astype(jnp.int32)
    return slots & (LOW - 1), slots // LOW


def feature_columns(out, at, tree):
    out[0:64, at] = tree[0:64].astype(bf16)
    out[64:128, at] = tree[0:64].astype(bf16)
    out[128:192, at] = tree[64:128].astype(bf16)
    out[192:208, at] = jnp.where(iota((16, tree.shape[1]), 0) < 8, tree[128:144].astype(f32), 0.0).astype(bf16)
    out[208:256, at] = jnp.zeros((48, tree.shape[1]), bf16)


def feature_rows(high, low, extra):
    first = jnp.transpose(jnp.concatenate([high, low], 0))
    second = jnp.transpose(jnp.concatenate([high, extra, jnp.zeros((56, high.shape[1]), f32)], 0))
    return first.astype(bf16), second.astype(bf16)


def target_columns(layout, out, tree_ref):
    span = layout.span
    for leaf in range(out.shape[1] // span):
        here = aligned(leaf * LEAF + layout.core() * span, span, span)
        feature_columns(out, slice(leaf * span, (leaf + 1) * span), tree_ref[:, here])


def tile_exponents(layout, tiles, tile, a_ref, bt_ref):
    source = aligned(tiles[1, tile] * LEAF, LEAF, LEAF)
    target = aligned(tiles[0, tile] * layout.span, layout.span, layout.span)
    return nn(a_ref[source, :], bt_ref[:, target])


def tiles_ahead(layout, tiles, a_ref, bt_ref, even, odd, made, made_hbm, sems):
    def send(tile):
        return pltpu.make_async_copy(made.at[tile], made_hbm.at[tile], sems.at[tile])

    for k in range(2):
        even[k] = tile_exponents(layout, tiles, k, a_ref, bt_ref)

    def step(pair, carry):
        for unit, ready, upcoming in ((2 * pair, even, odd), (2 * pair + 1, odd, even)):
            for k in range(2):
                tile = 2 * unit + k
                upcoming[k] = tile_exponents(layout, tiles, tile + 2, a_ref, bt_ref)
                made[tile] = jnp.exp(ready[k]).astype(bf16)
                send(tile).start()
        return carry

    lax.fori_loop(0, layout.ahead // 4, step, 0)
    return [send(tile) for tile in range(layout.ahead)]


def list_tiles(count_ref, list_ref, tiles, times):
    every = count_ref.shape[1]

    def tally(leaf, filled):
        for other in range(every):
            times[other] = (leaf == other).astype(jnp.int32)

        def add(slot, carry):
            at = list_ref[leaf, slot]
            times[at] = times[at] + 1
            return carry

        lax.fori_loop(0, count_ref[0, leaf], add, 0)
        for other in range(every):
            tiles[0, filled] = leaf
            tiles[1, filled] = other
            tiles[2, filled] = times[other]
            filled = filled + (times[other] > 0).astype(jnp.int32)
        return filled

    filled = lax.fori_loop(0, every, tally, jnp.int32(0))

    def pad(more, carry):
        tiles[0, more] = 0
        tiles[1, more] = 0
        tiles[2, more] = 0
        return carry

    lax.fori_loop(filled, tiles.shape[1] - 1, pad, 0)
    tiles[0, tiles.shape[1] - 1] = filled


def points_kernel(layout, trees, count_ref, list_ref, upper_ref, *refs):
    if not layout.fine:
        small_ref, refs = refs[0], refs[1:]
    else:
        small_ref = None
    place_refs, refs = refs[: layout.count], refs[layout.count :]
    tree_ref, a_hbm, base_hbm, sk_ref, upper_tiles_ref, top_ref, slot_ref, info_ref, tiles, made_hbm = refs[:10]
    masked, low_hot, a_ref, base_ref, sk_t, sk_bt, sems, times, bt_ref, even, odd, made, made_sems = refs[10:]
    blocks, rows = layout.blocks, layout.rows

    def keep(node, found):
        at = slice(node * SK, (node + 1) * SK)
        sk_t[:, at] = found.astype(bf16)
        sk_ref[at, 0:128], sk_ref[at, 128:256] = feature_rows(found[0:64], found[64:128], found[136:144])
        feature_columns(sk_bt, at, found)

    high_parts = rows // LOW
    infos = []
    for index in range(blocks):
        tail = layout.gather(place_refs, index, slice(TAIL, PLACE_ROWS))
        slots = tail[SLOT : SLOT + 1]
        slot_ref[index : index + 1, :] = slots
        infos.append(layout.info(place_refs, small_ref, index))
        info_ref[index] = infos[-1]
        low_part, high_part = parts_of(slots)
        low_by_column(low_hot.at[index], low_part.astype(f32))
        points = layout.gather(place_refs, index, slice(0, TAIL))
        high, low = two(points)
        nh, nm, nl = three(tail[NORM : NORM + 1])
        sub = iota((16, rows), 0)
        norms = jnp.where((sub == 3) | (sub == 8), nh, jnp.where((sub == 4) | (sub == 9), nm, nl))
        is_norm = ((sub >= 3) & (sub < 6)) | ((sub >= 8) & (sub < 11))
        is_one = (sub < 3) | ((sub >= 11) & (sub < 14))
        extra = jnp.where(is_norm, norms, jnp.where(is_one, 1.0, 0.0))
        for h in range(high_parts):
            here = high_part == h
            at = h * COORD
            masked[index, at : at + 64, :] = jnp.where(here, high.astype(f32), 0.0).astype(bf16)
            masked[index, at + 64 : at + 128, :] = jnp.where(here, low.astype(f32), 0.0).astype(bf16)
            masked[index, at + 128 : at + COORD, :] = jnp.where(here, extra, 0.0).astype(bf16)
    copies = []
    for index in range(blocks):
        placed = nn(masked[index], low_hot[index])
        for h in range(high_parts):
            part = placed[h * COORD : (h + 1) * COORD]
            at = slice(index * rows + h * LOW, index * rows + (h + 1) * LOW)
            tree_ref[:, at] = part.astype(bf16)
            a_ref[at, 0:128], a_ref[at, 128:256] = feature_rows(part[0:64], part[64:128], part[136:144])
        mine = slice(index * rows, (index + 1) * rows)
        copies.append(pltpu.make_async_copy(a_ref.at[mine], a_hbm.at[mine], sems.at[0, index]))
        copies[-1].start()
    for index in range(blocks):
        mine = slice(index * rows, (index + 1) * rows)
        picked = onehot(iota((rows, SK), 0) == infos[index][BASE : BASE + 1].astype(jnp.int32))
        keep(index, nn(tree_ref[:, mine], picked))
    for index in range(blocks):
        mine = slice(index * rows, (index + 1) * rows)
        base_ref[index] = jnp.exp(nn(a_ref[mine, :], sk_bt[:, index * SK : (index + 1) * SK])).astype(bf16)
        copies.append(pltpu.make_async_copy(base_ref.at[index], base_hbm.at[index], sems.at[1, index]))
        copies[-1].start()
    start, count, offset, total = 0, blocks, 0, blocks * trees
    while count > 1:
        nodes = count // 2
        for j in range(nodes):
            pair = slice((start + 2 * j) * SK, (start + 2 * j + 2) * SK)
            row = offset + lax.axis_index("leaf") * nodes + j
            picked = onehot(iota((2 * SK, SK), 0) == upper_ref[pl.ds(row, 1), :])
            here = start + count + j
            keep(here, nn(sk_t[:, pair], picked))
            upper_tiles_ref[here - blocks] = jnp.exp(nn(sk_ref[pair, :], sk_bt[:, here * SK : (here + 1) * SK]))
        total = total // 2
        offset = offset + total
        start, count = start + count, nodes
    found = sk_t[:, start * SK : (start + 1) * SK].astype(f32)
    top_ref[0:64, :] = found[0:64] + found[64:128]
    top_ref[64:72, :] = found[128:136]
    list_tiles(count_ref, list_ref, tiles, times)
    target_columns(layout, bt_ref, tree_ref)
    copies += tiles_ahead(layout, tiles, a_ref, bt_ref, even, odd, made, made_hbm, made_sems)
    for copy in copies:
        copy.wait()


def weights_kernel(layout, base_hbm, upper_tiles_ref, top_ref, slot_ref, *refs):
    light_refs, refs = refs[: layout.count], refs[layout.count :]
    if layout.fine:
        order = far_first(layout.blocks)
        order = order + [layout.blocks + step for step in order]
        light_refs = [light_refs[order.index(g)] for g in range(layout.count)]
    w_ref, coef_ref, pack_ref, masked, low_hot, base_ref, sems = refs
    blocks, rows = layout.blocks, layout.rows
    width = light_refs[0].shape[0]
    each = width // layout.halves
    pack_ref[0:PLACE_ROWS, :] = top_ref[...]
    for index in range(blocks):
        pltpu.make_async_copy(base_hbm.at[index], base_ref.at[index], sems.at[index]).start()

    def keep(node, coef):
        coef_ref[:, node * SK : (node + 1) * SK] = stack_two(coef)
        pack_ref[PLACE_ROWS:, :] = coef

    for index in range(blocks):
        low_part, high_part = parts_of(slot_ref[index : index + 1, :])
        low_by_column(low_hot.at[index], low_part.astype(f32))
        for half in range(layout.halves):
            light = [ref[layout.columns(g, half, each), layout.lanes(index)] for g, ref in enumerate(light_refs)]
            light = lanes_of(light)
            for h in range(rows // LOW):
                at = h * width + half * each
                masked[index, at : at + each, :] = jnp.where(high_part == h, light, 0.0).astype(bf16)
    for index in range(blocks):
        placed = nn(masked[index], low_hot[index])
        for h in range(rows // LOW):
            at = index * rows + h * LOW
            w_ref[:, at : at + LOW] = placed[h * width : (h + 1) * width].astype(bf16)
    for index in range(blocks):
        pltpu.make_async_copy(base_hbm.at[index], base_ref.at[index], sems.at[index]).wait()
        keep(index, nn(w_ref[:, index * rows : (index + 1) * rows], base_ref[index]))
    start, count = 0, blocks
    while count > 1:
        for j in range(count // 2):
            pair = slice((start + 2 * j) * SK, (start + 2 * j + 2) * SK)
            here = start + count + j
            high, low = two(upper_tiles_ref[here - blocks])
            coef = nn(coef_ref[:, pair], high)
            keep(here, coef[:width] + coef[width:] + nn(coef_ref[0:width, pair], low))
        start, count = start + count, count // 2


def near_kernel(layout, tiles, a_hbm, made_hbm, tree_ref, w_ref, acc, a_ref, bt_ref, made, sems, even, odd, even_tile, odd_tile):
    ahead, span = layout.ahead, layout.span

    def fetch(tile):
        return pltpu.make_async_copy(made_hbm.at[tile], made.at[tile], sems.at[tile])

    copy = pltpu.make_async_copy(a_hbm, a_ref, sems.at[ahead])
    copy.start()
    for tile in range(ahead):
        fetch(tile).start()
    filled = tiles[0, tiles.shape[1] - 1]
    acc[...] = jnp.zeros_like(acc)
    target_columns(layout, bt_ref, tree_ref)

    def exponents(unit, out):
        for k in range(2):
            out[k] = tile_exponents(layout, tiles, ahead + 2 * unit + k, a_ref, bt_ref)

    def add(tile, block):
        source = aligned(tiles[1, tile] * LEAF, LEAF, LEAF)
        target = aligned(tiles[0, tile] * span, span, span)
        acc[:, target] += tiles[2, tile].astype(f32) * nn(w_ref[:, source], block)

    copy.wait()

    @pl.when(filled > ahead)
    def _():
        exponents(0, even)
        for k in range(2):
            even_tile[k] = jnp.exp(even[k]).astype(bf16)
        exponents(1, odd)

        def phase(unit, upcoming, ready, finished, previous):
            for k in range(2):
                upcoming[k] = tile_exponents(layout, tiles, ahead + 2 * (unit + 1) + k, a_ref, bt_ref)
                finished[k] = jnp.exp(ready[k]).astype(bf16)
                add(ahead + 2 * (unit - 1) + k, previous[k])

        def step(pair, carry):
            phase(2 * pair + 1, even, odd, odd_tile, even_tile)
            phase(2 * pair + 2, odd, even, even_tile, odd_tile)
            return carry

        units = (filled - ahead + 1) // 2
        pairs = (units - 1) // 2
        lax.fori_loop(0, pairs, step, 0)
        for k in range(2):
            add(ahead + 4 * pairs + k, even_tile[k])

        @pl.when(2 * pairs + 1 < units)
        def _():
            for k in range(2):
                odd_tile[k] = jnp.exp(odd[k]).astype(bf16)
                add(ahead + 4 * pairs + 2 + k, odd_tile[k])

    def arrived(quad, carry):
        for more in range(4):
            fetch(4 * quad + more).wait()
            tile = 4 * quad + more

            @pl.when(tile < filled)
            def _():
                add(tile, made[tile])

        return carry

    lax.fori_loop(0, ahead // 4, arrived, 0)


def far_kernel(layout, low_levels, pack_ref, slot_ref, info_ref, tree_ref, sk_ref, coef_ref, near_ref, *refs):
    out_refs, refs = refs[: layout.halves], refs[layout.halves :]
    tops, coefs, scaled, low_hot, bt_ref, sums, masked = refs[:7]
    powers, tiles = refs[7:9], refs[9:11]
    blocks, rows = layout.blocks, layout.rows
    ups, width = pack_ref.shape[0], near_ref.shape[0]
    levels = low_levels + ups
    span, core = layout.span, layout.core()
    per_block = rows // LEAF
    lane = iota((1, SK), 1)
    for up in range(ups):
        pack = pack_ref[up]
        high, low = two(pack[0:64])
        sub = iota((8, SK), 0)
        extra = jnp.where(sub == 0, pack[67:68], jnp.where(sub == 1, pack[68:69], pack[69:70]))
        extra = jnp.where(sub < 3, extra, jnp.where(sub < 6, 1.0, 0.0))
        at = slice((low_levels + up) * SK, (low_levels + up + 1) * SK)
        rows_of = feature_rows(high.astype(f32), low.astype(f32), extra)
        coef = stack_two(pack[PLACE_ROWS:])
        for index in range(blocks):
            tops[index, at, 0:128], tops[index, at, 128:256] = rows_of
            coefs[index, :, at] = coef
    for index in range(blocks):
        node, start, count = index, 0, blocks
        for level in range(low_levels):
            at = slice(level * SK, (level + 1) * SK)
            other = slice((start + (node ^ 1)) * SK, (start + (node ^ 1) + 1) * SK)
            tops[index, at, :] = sk_ref[other, :]
            coefs[index, :, at] = coef_ref[:, other]
            node, start, count = node // 2, start + count, count // 2
        for leaf in range(per_block):
            flags = info_ref[index, FLAGS + leaf : FLAGS + leaf + 1, :]
            used = []
            for level in range(levels):
                flag = jnp.sum(jnp.where(lane == level, flags, 0.0), axis=1, keepdims=True)
                used.append(jnp.broadcast_to(flag, (1, SK)))
            used = jnp.concatenate(used, 1)
            scaled[index * per_block + leaf] = (coefs[index].astype(f32) * used).astype(bf16)

    target_columns(layout, bt_ref, tree_ref)

    def exponents(leaf):
        powers[leaf % 2][...] = nn(tops[leaf // per_block], bt_ref[:, leaf * span : (leaf + 1) * span])

    def product(leaf):
        here = slice(leaf * span, (leaf + 1) * span)
        far = nn(scaled[leaf], tiles[leaf % 2][...])
        sums[:, here] = near_ref[:, here] + far[:width] + far[width:]

    leaves = blocks * per_block
    exponents(0)
    for leaf in range(leaves):
        if leaf + 1 < leaves:
            exponents(leaf + 1)
        tiles[leaf % 2][...] = jnp.exp(powers[leaf % 2][...]).astype(bf16)
        if leaf:
            product(leaf - 1)
    product(leaves - 1)

    high_parts = []
    pieces = rows // LOW // layout.halves
    for index in range(blocks):
        low_part, high_part = parts_of(slot_ref[index : index + 1, :])
        high_parts.append(high_part)
        for c in range(rows // LANES):
            at = slice(c * LANES, (c + 1) * LANES)
            low_hot[index, :, at] = onehot(iota((LOW, LANES), 0) == low_part[:, at])
        for k in range(pieces):
            at = (index * pieces + k) * LOW
            masked[index, k * 2 * width : (k + 1) * 2 * width, :] = stack_two(sums[:, at : at + LOW])
    for index in range(blocks):
        moved = nn(masked[index], low_hot[index])
        result = jnp.zeros((2 * width, rows), f32)
        for k in range(pieces):
            here = high_parts[index] == k * layout.halves + core
            result = jnp.where(here, moved[k * 2 * width : (k + 1) * 2 * width], result)
        result = result[:width] + result[width:]
        if not layout.fine:
            out_refs[0][0, :, layout.lanes(index)] = result
            continue
        for g in range(layout.count):
            out_ref = out_refs[g // blocks]
            out_ref[g % blocks, :, layout.lanes(index)] = result[:, g * layout.per : (g + 1) * layout.per]


def add_kernel(kept_ref, got_ref, *out_refs):
    half = kept_ref.shape[1] // 2
    for step, out_ref in enumerate(out_refs):
        out_ref[0:half, :] = kept_ref[step, 0:half, :] + got_ref[step, half:, :]
        out_ref[half:, :] = kept_ref[step, half:, :] + got_ref[step, 0:half, :]


def far_first(blocks):
    return sorted(range(blocks), key=lambda step: -(step * 2 // blocks))


def final_kernel(blocks, pos_ref, *refs):
    back_refs, (weights_ref, out_ref, perm, vals) = refs[:-4], refs[-4:]
    chunks = pos_ref.shape[0]
    rows = chunks * LANES
    width, split = back_refs[0].shape
    width = LANES // blocks if blocks else width
    for r in range(chunks):
        spread(perm, slice(r * LANES, (r + 1) * LANES), column(pos_ref[r : r + 1, :]))
    for g, back_ref in enumerate(back_refs):
        columns, at = 0, slice(0, rows)
        value = back_ref[...]
        if blocks:
            columns = (lax.axis_index("sub") ^ far_first(blocks)[g % blocks]) * width
            at = aligned((lax.axis_index("leaf") ^ lax.axis_index("rep") ^ (g // blocks)) * split, split, split)
            value = value[0:width] if g < blocks else value[width:]
        high, low = two(value)
        vals[aligned(columns, width, width), at] = high
        vals[aligned(columns + LANES, width, width), at] = low
    step = 256
    for s in range(rows // step):
        here = slice(s * step, (s + 1) * step)
        moved = nt(perm[here, :], vals[...])
        out_ref[here, :] = ridge * weights_ref[here, :] + moved[:, :LANES] + moved[:, LANES:]


def upper_levels(pack, skeleton_upper, my_leaf, trees, blocks):
    devices = trees * blocks
    level = blocks.bit_length() - 1
    offset = sum(devices >> step for step in range(1, level + 1))
    line = jnp.arange(pack.shape[0])[:, None]
    is_point, is_norm = line < DIM, (line >= DIM + 3) & (line < DIM + 6)
    is_coef = line >= PLACE_ROWS
    packs, own, stride = [], pack, 1
    while stride < trees:
        other = lax.ppermute(own, "leaf", [(i, i ^ stride) for i in range(trees)])
        packs.append(other)
        stride *= 2
        if stride < trees:
            second = (my_leaf // (stride // 2)) % 2 == 1
            pair = jnp.where(second, jnp.concatenate([other, own], 1), jnp.concatenate([own, other], 1))
            chosen = pair[:, skeleton_upper[offset + my_leaf // stride]]
            level += 1
            offset += devices >> level
            norms = jnp.sum(jnp.where(is_norm, pair, 0.0), axis=0)
            chosen_norms = jnp.sum(jnp.where(is_norm, chosen, 0.0), axis=0)
            inner = jnp.dot(
                jnp.where(is_point, pair, 0.0).T, jnp.where(is_point, chosen, 0.0), precision=highest
            )
            tile = jnp.exp(inner + norms[:, None] + chosen_norms[None])
            own = jnp.where(is_coef, jnp.dot(pair, tile, precision=highest), chosen)
    return jnp.stack(packs)


def body(points, weights, tree_slot, near_count, near_list, skeleton_base, skeleton_upper, far_use):
    blocks, trees, reps = lax.axis_size("sub"), lax.axis_size("leaf"), lax.axis_size("rep")
    devices = blocks * trees
    rows, columns = weights.shape
    low_levels = blocks.bit_length() - 1
    ups = trees.bit_length() - 1
    width = columns // blocks
    part = rows // trees
    per = part // blocks
    total = blocks * rows
    leaves = total // LEAF
    my_leaf = lax.axis_index("leaf")
    fine = trees == 2 and reps == 2 and per % LANES == 0
    layout = Layout(blocks, trees, rows, fine)
    split = part if fine else rows
    cols = width * layout.halves

    place, pos = pl.pallas_call(
        functools.partial(place_kernel, fine),
        out_shape=(shaped((PLACE_ROWS, split), f32), shaped((rows // LANES, LANES), f32)),
        in_specs=[spec()] * 4,
        out_specs=(spec(),) * 2,
        scratch_shapes=[vm((split // LOW * COORD, rows), bf16), vm((rows, LOW), bf16)],
        compiler_params=params(),
        name="sort_points",
    )(tree_slot.reshape(rows // LANES, LANES), points.T, skeleton_base, far_use)
    axes = ("leaf", "sub", "rep")

    def swap(value, step, other=0):
        pairs = []
        for leaf in range(trees):
            for sub in range(blocks):
                for core in range(reps):
                    to = ((leaf ^ core ^ other) * blocks + (sub ^ step)) * reps + core
                    pairs.append(((leaf * blocks + sub) * reps + core, to))
        return lax.ppermute(value, axes, pairs)

    def other_core(value):
        return lax.ppermute(value, "rep", [(0, 1), (1, 0)])

    def sorted_light(pos):
        if fine:
            shapes = (shaped((blocks, width, part), f32),) * 2
        else:
            shapes = (shaped((columns, rows), f32),)
        return pl.pallas_call(
            functools.partial(light_kernel, blocks if fine else 0),
            out_shape=shapes,
            in_specs=[spec()] * 2,
            out_specs=(spec(),) * len(shapes),
            scratch_shapes=[
                vm((rows // LOW * LANES, rows), bf16),
                vm((rows, LOW), bf16),
                vm((rows // LOW, LANES, LOW), f32),
            ],
            compiler_params=params(40),
            name="sort_weights",
        )(in_hbm(pos), in_hbm(weights))

    if fine:
        kept, sent = sorted_light(pos)
        place, kept, sent = lax.optimization_barrier((swap(place, 0), kept, sent))
        place = {0: place}
        stride = blocks // 2
        while stride:
            for step in sorted(place):
                place[step | stride] = lax.ppermute(place[step], "sub", [(i, i ^ stride) for i in range(blocks)])
            stride //= 2
        light = pl.pallas_call(
            join_kernel,
            out_shape=(shaped((cols, part), f32),) * blocks,
            in_specs=[spec()] * 2,
            out_specs=(spec(),) * blocks,
            compiler_params=params(40),
            name="join_cores",
        )(kept, other_core(sent))
        place, light = lax.optimization_barrier((place, light))
        theirs = {step: other_core(one) for step, one in place.items()}
        place = [place[step] for step in range(blocks)] + [theirs[step] for step in range(blocks)]
        light = [swap(light[step], step) for step in far_first(blocks)]
        small = []
    else:
        info = jnp.pad(far_use.astype(f32), ((FLAGS, 5 - far_use.shape[0]), (0, SK - far_use.shape[1])))
        small = [lax.all_gather(info.at[BASE].set(skeleton_base[0].astype(f32)), "sub", axis=0, tiled=False)]
        place = place.reshape(PLACE_ROWS, trees, part).transpose(1, 0, 2)
        place = lax.all_to_all(place, "leaf", split_axis=0, concat_axis=0, tiled=True)
        place = lax.all_gather(place, "sub", axis=0, tiled=False)
        place = place.transpose(1, 0, 2, 3).reshape(devices, PLACE_ROWS, blocks, per)
        place = [place.transpose(1, 2, 0, 3).reshape(PLACE_ROWS, total)]
        light = sorted_light(pos)[0].reshape(columns, trees, part).transpose(1, 0, 2).reshape(devices, width, part)
        light = lax.all_to_all(light, ("leaf", "sub"), split_axis=0, concat_axis=0, tiled=True)
        light = light.reshape(devices, width, blocks, per)
        light = [light.transpose(1, 2, 0, 3).reshape(width, total)]

    nodes = 2 * blocks - 1
    tree, feat_a, base, sk, upper_tiles, top, slots, info, tiles, made = pl.pallas_call(
        functools.partial(points_kernel, layout, trees),
        out_shape=(
            vm((COORD, total), bf16),
            pltpu.MemorySpace.HBM((total, FEAT), bf16),
            pltpu.MemorySpace.HBM((blocks, rows, SK), bf16),
            vm((nodes * SK, FEAT), bf16),
            vm((blocks - 1, 2 * SK, SK), f32),
            vm((PLACE_ROWS, SK), f32),
            vm((blocks, rows), f32),
            vm((blocks, 8, SK), f32),
            pltpu.MemorySpace.HBM((3, leaves * leaves + 8), jnp.int32),
            pltpu.MemorySpace.HBM((layout.ahead, LEAF, layout.span), bf16),
        ),
        in_specs=[spec(SMEM)] * 2 + [spec()] * (1 + len(small) + layout.count),
        out_specs=(spec(), spec(pl.ANY), spec(pl.ANY)) + (spec(),) * 5 + (spec(SMEM), spec(pl.ANY)),
        scratch_shapes=[
            vm((blocks, rows // LOW * COORD, rows), bf16),
            vm((blocks, rows, LOW), bf16),
            vm((total, FEAT), bf16),
            vm((blocks, rows, SK), bf16),
            vm((COORD, nodes * SK), bf16),
            vm((FEAT, nodes * SK), bf16),
            pltpu.SemaphoreType.DMA((2, blocks)),
            pltpu.SMEM((leaves,), jnp.int32),
            vm((FEAT, total // layout.halves), bf16),
            vm((2, LEAF, layout.span), f32),
            vm((2, LEAF, layout.span), f32),
            vm((layout.ahead, LEAF, layout.span), bf16),
            pltpu.SemaphoreType.DMA((layout.ahead,)),
        ],
        compiler_params=params(40),
        name="tree_points",
    )(in_hbm(near_count), in_hbm(near_list[0]), in_hbm(skeleton_upper), *small, *place)

    if fine:
        light, slots = lax.optimization_barrier((light, slots))
        light = light + [other_core(one) for one in light]
    tree_light, coefs, pack = pl.pallas_call(
        functools.partial(weights_kernel, layout),
        out_shape=(
            vm((cols, total), bf16),
            vm((2 * cols, nodes * SK), bf16),
            shaped((PLACE_ROWS + cols, SK), f32),
        ),
        in_specs=[spec(pl.ANY)] + [spec()] * (3 + layout.count),
        out_specs=(spec(),) * 3,
        scratch_shapes=[
            vm((blocks, rows // LOW * cols, rows), bf16),
            vm((blocks, rows, LOW), bf16),
            vm((blocks, rows, SK), bf16),
            pltpu.SemaphoreType.DMA((blocks,)),
        ],
        compiler_params=params(40),
        name="tree_weights",
    )(in_hbm(base), held(upper_tiles), held(top), held(slots), *light)

    packs = upper_levels(pack, skeleton_upper, my_leaf, trees, blocks)

    near = pl.pallas_call(
        functools.partial(near_kernel, layout),
        out_shape=vm((cols, total // layout.halves), f32),
        in_specs=[spec(SMEM), spec(pl.ANY), spec(pl.ANY)] + [spec()] * 2,
        out_specs=spec(),
        scratch_shapes=[
            vm((total, FEAT), bf16),
            vm((FEAT, total // layout.halves), bf16),
            vm((layout.ahead, LEAF, layout.span), bf16),
            pltpu.SemaphoreType.DMA((layout.ahead + 1,)),
        ]
        + [vm((2, LEAF, layout.span), f32)] * 2
        + [vm((2, LEAF, layout.span), bf16)] * 2,
        compiler_params=params(40),
        name="near",
    )(in_hbm(tiles), in_hbm(feat_a), in_hbm(made), held(tree), held(tree_light))

    levels = low_levels + ups
    back = pl.pallas_call(
        functools.partial(far_kernel, layout, low_levels),
        out_shape=(shaped((layout.count // layout.halves, cols, total // layout.count), f32),) * layout.halves,
        in_specs=[spec()] * 7,
        out_specs=(spec(),) * layout.halves,
        scratch_shapes=[
            vm((blocks, levels * SK, FEAT), bf16),
            vm((blocks, 2 * cols, levels * SK), bf16),
            vm((leaves, 2 * cols, levels * SK), bf16),
            vm((blocks, LOW, rows), bf16),
            vm((FEAT, total // layout.halves), bf16),
            vm((cols, total // layout.halves), f32),
            vm((blocks, rows // LOW // layout.halves * 2 * cols, LOW), bf16),
        ]
        + [vm((levels * SK, layout.span), f32)] * 2
        + [vm((levels * SK, layout.span), bf16)] * 2,
        compiler_params=params(40),
        name="far",
    )(packs, *[held(one) for one in (slots, info, tree, sk, coefs, near)])

    if fine:
        kept, sent = back
        sums = pl.pallas_call(
            add_kernel,
            out_shape=(shaped((cols, part), f32),) * blocks,
            in_specs=[spec()] * 2,
            out_specs=(spec(),) * blocks,
            compiler_params=params(40),
            name="add_cores",
        )(kept, other_core(sent))
        back = [swap(sums[step], step) for step in far_first(blocks)]
        back = back + [other_core(one) for one in back]
    else:
        back = back[0].reshape(cols, blocks, devices, per).transpose(2, 0, 1, 3).reshape(devices, width, part)
        back = lax.all_to_all(back, ("leaf", "sub"), split_axis=0, concat_axis=0, tiled=True)
        back = [back.reshape(trees, columns, part).transpose(1, 0, 2).reshape(columns, rows)]

    return pl.pallas_call(
        functools.partial(final_kernel, blocks if fine else 0),
        out_shape=shaped((rows, columns), f32),
        in_specs=[spec()] * (2 + layout.count),
        out_specs=spec(),
        scratch_shapes=[vm((rows, rows), bf16), vm((2 * LANES, rows), bf16)],
        compiler_params=params(40),
        name="to_input_order",
    )(pos, *back, weights)


def solution(mesh):
    in_specs = (
        P(("groups", "leaf", "sub"), None),
        P(("groups", "leaf", "sub"), "rep"),
        P(("groups", "leaf", "sub")),
        P(("groups", "leaf"), None),
        P(("groups", "leaf"), None, None),
        P(("groups", "leaf", "sub"), None),
        P("groups", None),
        P(("groups", "leaf", "sub"), None),
    )
    out_specs = P(("groups", "leaf", "sub"), "rep")
    return jax.shard_map(body, mesh=mesh, in_specs=in_specs, out_specs=out_specs, check_vma=False)
```

```python
import functools

import jax
import jax.numpy as jnp
from jax import lax
from jax.experimental import pallas as pl
from jax.experimental.pallas import tpu as pltpu
from jax.sharding import PartitionSpec as P

DIM = 64
LEAF = 512
SK = 128
LANES = 128
FEAT = 256
LOW = 256
AHEAD = 4
COORD = 144

highest = lax.Precision.HIGHEST
point_scale = 0.25
ridge = 0.5
PLACE_ROWS = 72
TAIL = 64
SLOT, NORM, BASE, FLAGS = 0, 1, 2, 3
f32 = jnp.float32
bf16 = jnp.bfloat16
VMEM = pltpu.MemorySpace.VMEM
SMEM = pltpu.MemorySpace.SMEM


def spec(space=VMEM):
    return pl.BlockSpec(memory_space=space)


def params(mib=58):
    return pltpu.CompilerParams(vmem_limit_bytes=mib * 1024 * 1024)


def in_hbm(array):
    return pltpu.with_memory_space_constraint(array, pltpu.MemorySpace.HBM)


def held(array):
    return pltpu.with_memory_space_constraint(array, VMEM)


def vm(shape, dtype):
    return pltpu.VMEM(shape, dtype)


def shaped(shape, dtype):
    return jax.ShapeDtypeStruct(shape, dtype)


def nt(left, right):
    return lax.dot_general(left, right, (((1,), (1,)), ((), ())), preferred_element_type=f32)


def nn(left, right):
    return jnp.dot(left, right, preferred_element_type=f32)


def column(row):
    return jnp.transpose(jnp.broadcast_to(row, (LANES, LANES)))


def iota(shape, dim):
    return lax.broadcasted_iota(jnp.int32, shape, dim)


def onehot(mask):
    return jnp.where(mask, 1.0, 0.0).astype(bf16)


def two(value):
    high = value.astype(bf16)
    return high, (value - high.astype(f32)).astype(bf16)


def three(value):
    high = value.astype(bf16).astype(f32)
    mid = (value - high).astype(bf16).astype(f32)
    return high, mid, (value - high - mid).astype(bf16).astype(f32)


def lanes_of(blocks):
    return blocks[0] if len(blocks) == 1 else jnp.concatenate(blocks, 1)


def aligned(start, size, unit):
    return pl.ds(pl.multiple_of(start, unit), size)


def stack_two(value):
    high, low = two(value)
    return jnp.concatenate([high, low], 0)


def spread(perm, here, rank):
    lane = iota((LANES, LANES), 1).astype(f32)
    for c in range(perm.shape[1] // LANES):
        perm[here, c * LANES : (c + 1) * LANES] = onehot(lane + float(c * LANES) == rank)


def place_kernel(fine, slot_ref, points_ref, base_ref, flag_ref, place_ref, pos_ref, masked, low_hot):
    chunks = slot_ref.shape[0]
    slots = slot_ref[...]
    slot = slots.astype(f32)
    within = slots & (chunks * LANES - 1)
    high, low = (within >> 5).astype(f32), (within & 31).astype(f32)
    ranks = []
    for r in range(chunks):
        here = slice(r * LANES, (r + 1) * LANES)
        mine = column(slot[r : r + 1])
        before = jnp.zeros((LANES, LANES), f32)
        for c in range(chunks):
            before += jnp.where(slot[c : c + 1] < mine, 1.0, 0.0)
        rank = jnp.broadcast_to(jnp.sum(before, axis=1, keepdims=True), (LANES, LANES))
        ranks.append(jnp.transpose(rank)[0:1])
        pos_ref[r : r + 1, :] = ranks[-1]
        spread(low_hot, here, (rank.astype(jnp.int32) & (LOW - 1)).astype(f32))
    scaled = points_ref[...] * point_scale
    ph, plo = two(scaled)
    nh, nm, nl = three(-0.5 * jnp.sum(scaled * scaled, axis=0, keepdims=True))
    high, low = lanes_of([high[c : c + 1] for c in range(chunks)]), lanes_of([low[c : c + 1] for c in range(chunks)])
    sub = iota((16, chunks * LANES), 0)
    extra = jnp.where(sub == 0, high, jnp.where(sub == 1, low, 0.0))
    extra = jnp.where(sub == 2, nh, jnp.where(sub == 3, nm, jnp.where(sub == 4, nl, extra)))
    high_part = lanes_of(ranks).astype(jnp.int32) // LOW
    parts = place_ref.shape[1] // LOW
    first = (lax.axis_index("leaf") ^ lax.axis_index("rep")) * parts if fine else 0
    for h in range(parts):
        here = high_part == first + h
        masked[h * COORD : h * COORD + 64, :] = jnp.where(here, ph.astype(f32), 0.0).astype(bf16)
        masked[h * COORD + 64 : h * COORD + 128, :] = jnp.where(here, plo.astype(f32), 0.0).astype(bf16)
        masked[h * COORD + 128 : (h + 1) * COORD, :] = jnp.where(here, extra, 0.0).astype(bf16)
    placed = nn(masked[...], low_hot[...])
    tail = iota((PLACE_ROWS - TAIL, LOW), 0)
    for h in range(parts):
        at = slice(h * LOW, (h + 1) * LOW)
        moved = placed[h * COORD : (h + 1) * COORD]
        place_ref[0:TAIL, at] = moved[0:64] + moved[64:128]
        slot_row = moved[128:129] * 32.0 + moved[129:130]
        norm_row = moved[130:131] + moved[131:132] + moved[132:133]
        place_ref[TAIL:, at] = jnp.where(tail == SLOT, slot_row, jnp.where(tail == NORM, norm_row, 0.0))
    if fine:
        place_ref[TAIL + BASE : TAIL + BASE + 1, 0:SK] = base_ref[...].astype(f32)
        place_ref[TAIL + FLAGS : TAIL + FLAGS + flag_ref.shape[0], 0 : flag_ref.shape[1]] = flag_ref[...].astype(f32)


def light_kernel(blocks, pos_ref, weights_ref, *refs):
    light_refs, (masked, low_hot, placed) = refs[:-3], refs[-3:]
    chunks = pos_ref.shape[0]
    high_count = chunks * LANES // LOW
    low_part, high_part = parts_of(lanes_of([pos_ref[c : c + 1, :] for c in range(chunks)]))
    low_by_column(low_hot, low_part.astype(f32))
    for c in range(chunks):
        at = slice(c * LANES, (c + 1) * LANES)
        turned = jnp.transpose(weights_ref[at, :])
        for h in range(high_count):
            masked[h * LANES : (h + 1) * LANES, at] = jnp.where(high_part[:, at] == h, turned, 0.0).astype(bf16)
    moved = nn(masked[...], low_hot[...])
    for h in range(high_count):
        if not blocks:
            light_refs[0][:, h * LOW : (h + 1) * LOW] = moved[h * LANES : (h + 1) * LANES]
        placed[h] = moved[h * LANES : (h + 1) * LANES]
    if not blocks:
        return
    width, parts = LANES // blocks, high_count // 2
    for other, light_ref in enumerate(light_refs):
        first = (lax.axis_index("leaf") ^ lax.axis_index("rep") ^ other) * parts
        for step in range(blocks):
            columns = aligned((lax.axis_index("sub") ^ step) * width, width, width)
            for h in range(parts):
                light_ref[step, :, h * LOW : (h + 1) * LOW] = placed[first + h, columns, :]


def join_kernel(kept_ref, got_ref, *out_refs):
    half = kept_ref.shape[1]
    for step, out_ref in enumerate(out_refs):
        out_ref[0:half, :] = kept_ref[step]
        out_ref[half:, :] = got_ref[step]


class Layout:
    def __init__(self, blocks, trees, rows, fine):
        self.blocks, self.rows, self.fine = blocks, rows, fine
        self.count = blocks * trees if fine else 1
        self.per = rows // self.count
        self.halves = 2 if fine else 1
        self.span = LEAF // self.halves
        self.ahead = AHEAD // 4 * 4 if fine else 4

    def core(self):
        return lax.axis_index("rep") if self.fine else 0

    def lanes(self, index):
        return slice(index * self.per, (index + 1) * self.per)

    def columns(self, group, half, each):
        if self.fine and group >= self.blocks:
            half = 1 - half
        return slice(half * each, (half + 1) * each)

    def gather(self, refs, index, part):
        return lanes_of([ref[part, self.lanes(index)] for ref in refs])

    def info(self, refs, small_ref, index):
        if not self.fine:
            return small_ref[index]
        core = lax.axis_index("rep")
        found = jnp.zeros((PLACE_ROWS - TAIL, SK), f32)
        for step in range(self.blocks):
            mine, theirs = refs[step][TAIL:, 0:SK], refs[self.blocks + step][TAIL:, 0:SK]
            here = jnp.where(core == 0, mine, theirs)
            found = jnp.where((lax.axis_index("sub") ^ step) == index, here, found)
        return found


def low_by_column(out, low):
    for c in range(out.shape[0] // LANES):
        at = slice(c * LANES, (c + 1) * LANES)
        spread(out, at, column(low[:, at]))


def parts_of(slots):
    slots = slots.astype(jnp.int32)
    return slots & (LOW - 1), slots // LOW


def feature_columns(out, at, tree):
    out[0:64, at] = tree[0:64].astype(bf16)
    out[64:128, at] = tree[0:64].astype(bf16)
    out[128:192, at] = tree[64:128].astype(bf16)
    out[192:208, at] = jnp.where(iota((16, tree.shape[1]), 0) < 8, tree[128:144].astype(f32), 0.0).astype(bf16)
    out[208:256, at] = jnp.zeros((48, tree.shape[1]), bf16)


def feature_rows(high, low, extra):
    first = jnp.transpose(jnp.concatenate([high, low], 0))
    second = jnp.transpose(jnp.concatenate([high, extra, jnp.zeros((56, high.shape[1]), f32)], 0))
    return first.astype(bf16), second.astype(bf16)


def target_columns(layout, out, tree_ref):
    span = layout.span
    for leaf in range(out.shape[1] // span):
        here = aligned(leaf * LEAF + layout.core() * span, span, span)
        feature_columns(out, slice(leaf * span, (leaf + 1) * span), tree_ref[:, here])


def tile_exponents(layout, tiles, tile, a_ref, bt_ref):
    source = aligned(tiles[1, tile] * LEAF, LEAF, LEAF)
    target = aligned(tiles[0, tile] * layout.span, layout.span, layout.span)
    return nn(a_ref[source, :], bt_ref[:, target])


def tiles_ahead(layout, tiles, a_ref, bt_ref, even, odd, made, made_hbm, sems):
    def send(tile):
        return pltpu.make_async_copy(made.at[tile], made_hbm.at[tile], sems.at[tile])

    for k in range(2):
        even[k] = tile_exponents(layout, tiles, k, a_ref, bt_ref)

    def step(pair, carry):
        for unit, ready, upcoming in ((2 * pair, even, odd), (2 * pair + 1, odd, even)):
            for k in range(2):
                tile = 2 * unit + k
                upcoming[k] = tile_exponents(layout, tiles, tile + 2, a_ref, bt_ref)
                made[tile] = jnp.exp(ready[k]).astype(bf16)
                send(tile).start()
        return carry

    lax.fori_loop(0, layout.ahead // 4, step, 0)
    return [send(tile) for tile in range(layout.ahead)]


def list_tiles(count_ref, list_ref, tiles, times):
    every = count_ref.shape[1]

    def tally(leaf, filled):
        for other in range(every):
            times[other] = (leaf == other).astype(jnp.int32)

        def add(slot, carry):
            at = list_ref[leaf, slot]
            times[at] = times[at] + 1
            return carry

        lax.fori_loop(0, count_ref[0, leaf], add, 0)
        for other in range(every):
            tiles[0, filled] = leaf
            tiles[1, filled] = other
            tiles[2, filled] = times[other]
            filled = filled + (times[other] > 0).astype(jnp.int32)
        return filled

    filled = lax.fori_loop(0, every, tally, jnp.int32(0))

    def pad(more, carry):
        tiles[0, more] = 0
        tiles[1, more] = 0
        tiles[2, more] = 0
        return carry

    lax.fori_loop(filled, tiles.shape[1] - 1, pad, 0)
    tiles[0, tiles.shape[1] - 1] = filled


def points_kernel(layout, trees, count_ref, list_ref, upper_ref, *refs):
    if not layout.fine:
        small_ref, refs = refs[0], refs[1:]
    else:
        small_ref = None
    place_refs, refs = refs[: layout.count], refs[layout.count :]
    tree_ref, a_hbm, base_hbm, sk_ref, upper_tiles_ref, top_ref, slot_ref, info_ref, tiles, made_hbm = refs[:10]
    masked, low_hot, a_ref, base_ref, sk_t, sk_bt, sems, times, bt_ref, even, odd, made, made_sems = refs[10:]
    blocks, rows = layout.blocks, layout.rows

    def keep(node, found):
        at = slice(node * SK, (node + 1) * SK)
        sk_t[:, at] = found.astype(bf16)
        sk_ref[at, 0:128], sk_ref[at, 128:256] = feature_rows(found[0:64], found[64:128], found[136:144])
        feature_columns(sk_bt, at, found)

    high_parts = rows // LOW
    infos = []
    for index in range(blocks):
        tail = layout.gather(place_refs, index, slice(TAIL, PLACE_ROWS))
        slots = tail[SLOT : SLOT + 1]
        slot_ref[index : index + 1, :] = slots
        infos.append(layout.info(place_refs, small_ref, index))
        info_ref[index] = infos[-1]
        low_part, high_part = parts_of(slots)
        low_by_column(low_hot.at[index], low_part.astype(f32))
        points = layout.gather(place_refs, index, slice(0, TAIL))
        high, low = two(points)
        nh, nm, nl = three(tail[NORM : NORM + 1])
        sub = iota((16, rows), 0)
        norms = jnp.where((sub == 3) | (sub == 8), nh, jnp.where((sub == 4) | (sub == 9), nm, nl))
        is_norm = ((sub >= 3) & (sub < 6)) | ((sub >= 8) & (sub < 11))
        is_one = (sub < 3) | ((sub >= 11) & (sub < 14))
        extra = jnp.where(is_norm, norms, jnp.where(is_one, 1.0, 0.0))
        for h in range(high_parts):
            here = high_part == h
            at = h * COORD
            masked[index, at : at + 64, :] = jnp.where(here, high.astype(f32), 0.0).astype(bf16)
            masked[index, at + 64 : at + 128, :] = jnp.where(here, low.astype(f32), 0.0).astype(bf16)
            masked[index, at + 128 : at + COORD, :] = jnp.where(here, extra, 0.0).astype(bf16)
    copies = []
    for index in range(blocks):
        placed = nn(masked[index], low_hot[index])
        for h in range(high_parts):
            part = placed[h * COORD : (h + 1) * COORD]
            at = slice(index * rows + h * LOW, index * rows + (h + 1) * LOW)
            tree_ref[:, at] = part.astype(bf16)
            a_ref[at, 0:128], a_ref[at, 128:256] = feature_rows(part[0:64], part[64:128], part[136:144])
        mine = slice(index * rows, (index + 1) * rows)
        copies.append(pltpu.make_async_copy(a_ref.at[mine], a_hbm.at[mine], sems.at[0, index]))
        copies[-1].start()
    for index in range(blocks):
        mine = slice(index * rows, (index + 1) * rows)
        picked = onehot(iota((rows, SK), 0) == infos[index][BASE : BASE + 1].astype(jnp.int32))
        keep(index, nn(tree_ref[:, mine], picked))
    for index in range(blocks):
        mine = slice(index * rows, (index + 1) * rows)
        base_ref[index] = jnp.exp(nn(a_ref[mine, :], sk_bt[:, index * SK : (index + 1) * SK])).astype(bf16)
        copies.append(pltpu.make_async_copy(base_ref.at[index], base_hbm.at[index], sems.at[1, index]))
        copies[-1].start()
    start, count, offset, total = 0, blocks, 0, blocks * trees
    while count > 1:
        nodes = count // 2
        for j in range(nodes):
            pair = slice((start + 2 * j) * SK, (start + 2 * j + 2) * SK)
            row = offset + lax.axis_index("leaf") * nodes + j
            picked = onehot(iota((2 * SK, SK), 0) == upper_ref[pl.ds(row, 1), :])
            here = start + count + j
            keep(here, nn(sk_t[:, pair], picked))
            upper_tiles_ref[here - blocks] = jnp.exp(nn(sk_ref[pair, :], sk_bt[:, here * SK : (here + 1) * SK]))
        total = total // 2
        offset = offset + total
        start, count = start + count, nodes
    found = sk_t[:, start * SK : (start + 1) * SK].astype(f32)
    top_ref[0:64, :] = found[0:64] + found[64:128]
    top_ref[64:72, :] = found[128:136]
    list_tiles(count_ref, list_ref, tiles, times)
    target_columns(layout, bt_ref, tree_ref)
    copies += tiles_ahead(layout, tiles, a_ref, bt_ref, even, odd, made, made_hbm, made_sems)
    for copy in copies:
        copy.wait()


def weights_kernel(layout, base_hbm, upper_tiles_ref, top_ref, slot_ref, *refs):
    light_refs, refs = refs[: layout.count], refs[layout.count :]
    if layout.fine:
        order = far_first(layout.blocks)
        order = order + [layout.blocks + step for step in order]
        light_refs = [light_refs[order.index(g)] for g in range(layout.count)]
    w_ref, coef_ref, pack_ref, masked, low_hot, base_ref, sems = refs
    blocks, rows = layout.blocks, layout.rows
    width = light_refs[0].shape[0]
    each = width // layout.halves
    pack_ref[0:PLACE_ROWS, :] = top_ref[...]
    for index in range(blocks):
        pltpu.make_async_copy(base_hbm.at[index], base_ref.at[index], sems.at[index]).start()

    def keep(node, coef):
        coef_ref[:, node * SK : (node + 1) * SK] = stack_two(coef)
        pack_ref[PLACE_ROWS:, :] = coef

    for index in range(blocks):
        low_part, high_part = parts_of(slot_ref[index : index + 1, :])
        low_by_column(low_hot.at[index], low_part.astype(f32))
        for half in range(layout.halves):
            light = [ref[layout.columns(g, half, each), layout.lanes(index)] for g, ref in enumerate(light_refs)]
            light = lanes_of(light)
            for h in range(rows // LOW):
                at = h * width + half * each
                masked[index, at : at + each, :] = jnp.where(high_part == h, light, 0.0).astype(bf16)
    for index in range(blocks):
        placed = nn(masked[index], low_hot[index])
        for h in range(rows // LOW):
            at = index * rows + h * LOW
            w_ref[:, at : at + LOW] = placed[h * width : (h + 1) * width].astype(bf16)
    for index in range(blocks):
        pltpu.make_async_copy(base_hbm.at[index], base_ref.at[index], sems.at[index]).wait()
        keep(index, nn(w_ref[:, index * rows : (index + 1) * rows], base_ref[index]))
    start, count = 0, blocks
    while count > 1:
        for j in range(count // 2):
            pair = slice((start + 2 * j) * SK, (start + 2 * j + 2) * SK)
            here = start + count + j
            high, low = two(upper_tiles_ref[here - blocks])
            coef = nn(coef_ref[:, pair], high)
            keep(here, coef[:width] + coef[width:] + nn(coef_ref[0:width, pair], low))
        start, count = start + count, count // 2


def near_kernel(layout, tiles, a_hbm, made_hbm, tree_ref, w_ref, acc, a_ref, bt_ref, made, sems, even, odd, even_tile, odd_tile):
    ahead, span = layout.ahead, layout.span

    def fetch(tile):
        return pltpu.make_async_copy(made_hbm.at[tile], made.at[tile], sems.at[tile])

    copy = pltpu.make_async_copy(a_hbm, a_ref, sems.at[ahead])
    copy.start()
    for tile in range(ahead):
        fetch(tile).start()
    filled = tiles[0, tiles.shape[1] - 1]
    acc[...] = jnp.zeros_like(acc)
    target_columns(layout, bt_ref, tree_ref)

    def exponents(unit, out):
        for k in range(2):
            out[k] = tile_exponents(layout, tiles, ahead + 2 * unit + k, a_ref, bt_ref)

    def add(tile, block):
        source = aligned(tiles[1, tile] * LEAF, LEAF, LEAF)
        target = aligned(tiles[0, tile] * span, span, span)
        acc[:, target] += tiles[2, tile].astype(f32) * nn(w_ref[:, source], block)

    copy.wait()

    @pl.when(filled > ahead)
    def _():
        exponents(0, even)
        for k in range(2):
            even_tile[k] = jnp.exp(even[k]).astype(bf16)
        exponents(1, odd)

        def phase(unit, upcoming, ready, finished, previous):
            for k in range(2):
                upcoming[k] = tile_exponents(layout, tiles, ahead + 2 * (unit + 1) + k, a_ref, bt_ref)
                finished[k] = jnp.exp(ready[k]).astype(bf16)
                add(ahead + 2 * (unit - 1) + k, previous[k])

        def step(pair, carry):
            phase(2 * pair + 1, even, odd, odd_tile, even_tile)
            phase(2 * pair + 2, odd, even, even_tile, odd_tile)
            return carry

        units = (filled - ahead + 1) // 2
        pairs = (units - 1) // 2
        lax.fori_loop(0, pairs, step, 0)
        for k in range(2):
            add(ahead + 4 * pairs + k, even_tile[k])

        @pl.when(2 * pairs + 1 < units)
        def _():
            for k in range(2):
                odd_tile[k] = jnp.exp(odd[k]).astype(bf16)
                add(ahead + 4 * pairs + 2 + k, odd_tile[k])

    def arrived(quad, carry):
        for more in range(4):
            fetch(4 * quad + more).wait()
            tile = 4 * quad + more

            @pl.when(tile < filled)
            def _():
                add(tile, made[tile])

        return carry

    lax.fori_loop(0, ahead // 4, arrived, 0)


def far_kernel(layout, low_levels, pack_ref, slot_ref, info_ref, tree_ref, sk_ref, coef_ref, near_ref, *refs):
    out_refs, refs = refs[: layout.halves], refs[layout.halves :]
    tops, coefs, scaled, low_hot, bt_ref, sums, masked = refs[:7]
    powers, tiles = refs[7:9], refs[9:11]
    blocks, rows = layout.blocks, layout.rows
    ups, width = pack_ref.shape[0], near_ref.shape[0]
    levels = low_levels + ups
    span, core = layout.span, layout.core()
    per_block = rows // LEAF
    lane = iota((1, SK), 1)
    for up in range(ups):
        pack = pack_ref[up]
        high, low = two(pack[0:64])
        sub = iota((8, SK), 0)
        extra = jnp.where(sub == 0, pack[67:68], jnp.where(sub == 1, pack[68:69], pack[69:70]))
        extra = jnp.where(sub < 3, extra, jnp.where(sub < 6, 1.0, 0.0))
        at = slice((low_levels + up) * SK, (low_levels + up + 1) * SK)
        rows_of = feature_rows(high.astype(f32), low.astype(f32), extra)
        coef = stack_two(pack[PLACE_ROWS:])
        for index in range(blocks):
            tops[index, at, 0:128], tops[index, at, 128:256] = rows_of
            coefs[index, :, at] = coef
    for index in range(blocks):
        node, start, count = index, 0, blocks
        for level in range(low_levels):
            at = slice(level * SK, (level + 1) * SK)
            other = slice((start + (node ^ 1)) * SK, (start + (node ^ 1) + 1) * SK)
            tops[index, at, :] = sk_ref[other, :]
            coefs[index, :, at] = coef_ref[:, other]
            node, start, count = node // 2, start + count, count // 2
        for leaf in range(per_block):
            flags = info_ref[index, FLAGS + leaf : FLAGS + leaf + 1, :]
            used = []
            for level in range(levels):
                flag = jnp.sum(jnp.where(lane == level, flags, 0.0), axis=1, keepdims=True)
                used.append(jnp.broadcast_to(flag, (1, SK)))
            used = jnp.concatenate(used, 1)
            scaled[index * per_block + leaf] = (coefs[index].astype(f32) * used).astype(bf16)

    target_columns(layout, bt_ref, tree_ref)

    def exponents(leaf):
        powers[leaf % 2][...] = nn(tops[leaf // per_block], bt_ref[:, leaf * span : (leaf + 1) * span])

    def product(leaf):
        here = slice(leaf * span, (leaf + 1) * span)
        far = nn(scaled[leaf], tiles[leaf % 2][...])
        sums[:, here] = near_ref[:, here] + far[:width] + far[width:]

    leaves = blocks * per_block
    exponents(0)
    for leaf in range(leaves):
        if leaf + 1 < leaves:
            exponents(leaf + 1)
        tiles[leaf % 2][...] = jnp.exp(powers[leaf % 2][...]).astype(bf16)
        if leaf:
            product(leaf - 1)
    product(leaves - 1)

    high_parts = []
    pieces = rows // LOW // layout.halves
    for index in range(blocks):
        low_part, high_part = parts_of(slot_ref[index : index + 1, :])
        high_parts.append(high_part)
        for c in range(rows // LANES):
            at = slice(c * LANES, (c + 1) * LANES)
            low_hot[index, :, at] = onehot(iota((LOW, LANES), 0) == low_part[:, at])
        for k in range(pieces):
            at = (index * pieces + k) * LOW
            masked[index, k * 2 * width : (k + 1) * 2 * width, :] = stack_two(sums[:, at : at + LOW])
    for index in range(blocks):
        moved = nn(masked[index], low_hot[index])
        result = jnp.zeros((2 * width, rows), f32)
        for k in range(pieces):
            here = high_parts[index] == k * layout.halves + core
            result = jnp.where(here, moved[k * 2 * width : (k + 1) * 2 * width], result)
        result = result[:width] + result[width:]
        if not layout.fine:
            out_refs[0][0, :, layout.lanes(index)] = result
            continue
        for g in range(layout.count):
            out_ref = out_refs[g // blocks]
            out_ref[g % blocks, :, layout.lanes(index)] = result[:, g * layout.per : (g + 1) * layout.per]


def add_kernel(kept_ref, got_ref, *out_refs):
    half = kept_ref.shape[1] // 2
    for step, out_ref in enumerate(out_refs):
        out_ref[0:half, :] = kept_ref[step, 0:half, :] + got_ref[step, half:, :]
        out_ref[half:, :] = kept_ref[step, half:, :] + got_ref[step, 0:half, :]


def far_first(blocks):
    return sorted(range(blocks), key=lambda step: -(step * 2 // blocks))


def final_kernel(blocks, pos_ref, *refs):
    back_refs, (weights_ref, out_ref, perm, vals) = refs[:-4], refs[-4:]
    chunks = pos_ref.shape[0]
    rows = chunks * LANES
    width, split = back_refs[0].shape
    width = LANES // blocks if blocks else width
    for r in range(chunks):
        spread(perm, slice(r * LANES, (r + 1) * LANES), column(pos_ref[r : r + 1, :]))
    for g, back_ref in enumerate(back_refs):
        columns, at = 0, slice(0, rows)
        value = back_ref[...]
        if blocks:
            columns = (lax.axis_index("sub") ^ far_first(blocks)[g % blocks]) * width
            at = aligned((lax.axis_index("leaf") ^ lax.axis_index("rep") ^ (g // blocks)) * split, split, split)
            value = value[0:width] if g < blocks else value[width:]
        high, low = two(value)
        vals[aligned(columns, width, width), at] = high
        vals[aligned(columns + LANES, width, width), at] = low
    step = 256
    for s in range(rows // step):
        here = slice(s * step, (s + 1) * step)
        moved = nt(perm[here, :], vals[...])
        out_ref[here, :] = ridge * weights_ref[here, :] + moved[:, :LANES] + moved[:, LANES:]


def upper_levels(pack, skeleton_upper, my_leaf, trees, blocks):
    devices = trees * blocks
    level = blocks.bit_length() - 1
    offset = sum(devices >> step for step in range(1, level + 1))
    line = jnp.arange(pack.shape[0])[:, None]
    is_point, is_norm = line < DIM, (line >= DIM + 3) & (line < DIM + 6)
    is_coef = line >= PLACE_ROWS
    packs, own, stride = [], pack, 1
    while stride < trees:
        other = lax.ppermute(own, "leaf", [(i, i ^ stride) for i in range(trees)])
        packs.append(other)
        stride *= 2
        if stride < trees:
            second = (my_leaf // (stride // 2)) % 2 == 1
            pair = jnp.where(second, jnp.concatenate([other, own], 1), jnp.concatenate([own, other], 1))
            chosen = pair[:, skeleton_upper[offset + my_leaf // stride]]
            level += 1
            offset += devices >> level
            norms = jnp.sum(jnp.where(is_norm, pair, 0.0), axis=0)
            chosen_norms = jnp.sum(jnp.where(is_norm, chosen, 0.0), axis=0)
            inner = jnp.dot(
                jnp.where(is_point, pair, 0.0).T, jnp.where(is_point, chosen, 0.0), precision=highest
            )
            tile = jnp.exp(inner + norms[:, None] + chosen_norms[None])
            own = jnp.where(is_coef, jnp.dot(pair, tile, precision=highest), chosen)
    return jnp.stack(packs)


def body(points, weights, tree_slot, near_count, near_list, skeleton_base, skeleton_upper, far_use):
    blocks, trees, reps = lax.axis_size("sub"), lax.axis_size("leaf"), lax.axis_size("rep")
    devices = blocks * trees
    rows, columns = weights.shape
    low_levels = blocks.bit_length() - 1
    ups = trees.bit_length() - 1
    width = columns // blocks
    part = rows // trees
    per = part // blocks
    total = blocks * rows
    leaves = total // LEAF
    my_leaf = lax.axis_index("leaf")
    fine = trees == 2 and reps == 2 and per % LANES == 0
    layout = Layout(blocks, trees, rows, fine)
    split = part if fine else rows
    cols = width * layout.halves

    place, pos = pl.pallas_call(
        functools.partial(place_kernel, fine),
        out_shape=(shaped((PLACE_ROWS, split), f32), shaped((rows // LANES, LANES), f32)),
        in_specs=[spec()] * 4,
        out_specs=(spec(),) * 2,
        scratch_shapes=[vm((split // LOW * COORD, rows), bf16), vm((rows, LOW), bf16)],
        compiler_params=params(),
        name="sort_points",
    )(tree_slot.reshape(rows // LANES, LANES), points.T, skeleton_base, far_use)
    axes = ("leaf", "sub", "rep")

    def swap(value, step, other=0):
        pairs = []
        for leaf in range(trees):
            for sub in range(blocks):
                for core in range(reps):
                    to = ((leaf ^ core ^ other) * blocks + (sub ^ step)) * reps + core
                    pairs.append(((leaf * blocks + sub) * reps + core, to))
        return lax.ppermute(value, axes, pairs)

    def other_core(value):
        return lax.ppermute(value, "rep", [(0, 1), (1, 0)])

    def sorted_light(pos):
        if fine:
            shapes = (shaped((blocks, width, part), f32),) * 2
        else:
            shapes = (shaped((columns, rows), f32),)
        return pl.pallas_call(
            functools.partial(light_kernel, blocks if fine else 0),
            out_shape=shapes,
            in_specs=[spec()] * 2,
            out_specs=(spec(),) * len(shapes),
            scratch_shapes=[
                vm((rows // LOW * LANES, rows), bf16),
                vm((rows, LOW), bf16),
                vm((rows // LOW, LANES, LOW), f32),
            ],
            compiler_params=params(40),
            name="sort_weights",
        )(in_hbm(pos), in_hbm(weights))

    if fine:
        place = {0: swap(place, 0)}
        stride = blocks // 2
        while stride:
            for step in sorted(place):
                place[step | stride] = lax.ppermute(place[step], "sub", [(i, i ^ stride) for i in range(blocks)])
            stride //= 2
        kept, sent = sorted_light(pos)
        place, kept, sent = lax.optimization_barrier((place, kept, sent))
        light = pl.pallas_call(
            join_kernel,
            out_shape=(shaped((cols, part), f32),) * blocks,
            in_specs=[spec()] * 2,
            out_specs=(spec(),) * blocks,
            compiler_params=params(40),
            name="join_cores",
        )(kept, other_core(sent))
        theirs = {step: other_core(one) for step, one in place.items()}
        place = [place[step] for step in range(blocks)] + [theirs[step] for step in range(blocks)]
        light = [swap(light[step], step) for step in far_first(blocks)]
        small = []
    else:
        info = jnp.pad(far_use.astype(f32), ((FLAGS, 5 - far_use.shape[0]), (0, SK - far_use.shape[1])))
        small = [lax.all_gather(info.at[BASE].set(skeleton_base[0].astype(f32)), "sub", axis=0, tiled=False)]
        place = place.reshape(PLACE_ROWS, trees, part).transpose(1, 0, 2)
        place = lax.all_to_all(place, "leaf", split_axis=0, concat_axis=0, tiled=True)
        place = lax.all_gather(place, "sub", axis=0, tiled=False)
        place = place.transpose(1, 0, 2, 3).reshape(devices, PLACE_ROWS, blocks, per)
        place = [place.transpose(1, 2, 0, 3).reshape(PLACE_ROWS, total)]
        light = sorted_light(pos)[0].reshape(columns, trees, part).transpose(1, 0, 2).reshape(devices, width, part)
        light = lax.all_to_all(light, ("leaf", "sub"), split_axis=0, concat_axis=0, tiled=True)
        light = light.reshape(devices, width, blocks, per)
        light = [light.transpose(1, 2, 0, 3).reshape(width, total)]

    nodes = 2 * blocks - 1
    tree, feat_a, base, sk, upper_tiles, top, slots, info, tiles, made = pl.pallas_call(
        functools.partial(points_kernel, layout, trees),
        out_shape=(
            vm((COORD, total), bf16),
            pltpu.MemorySpace.HBM((total, FEAT), bf16),
            pltpu.MemorySpace.HBM((blocks, rows, SK), bf16),
            vm((nodes * SK, FEAT), bf16),
            vm((blocks - 1, 2 * SK, SK), f32),
            vm((PLACE_ROWS, SK), f32),
            vm((blocks, rows), f32),
            vm((blocks, 8, SK), f32),
            pltpu.MemorySpace.HBM((3, leaves * leaves + 8), jnp.int32),
            pltpu.MemorySpace.HBM((layout.ahead, LEAF, layout.span), bf16),
        ),
        in_specs=[spec(SMEM)] * 2 + [spec()] * (1 + len(small) + layout.count),
        out_specs=(spec(), spec(pl.ANY), spec(pl.ANY)) + (spec(),) * 5 + (spec(SMEM), spec(pl.ANY)),
        scratch_shapes=[
            vm((blocks, rows // LOW * COORD, rows), bf16),
            vm((blocks, rows, LOW), bf16),
            vm((total, FEAT), bf16),
            vm((blocks, rows, SK), bf16),
            vm((COORD, nodes * SK), bf16),
            vm((FEAT, nodes * SK), bf16),
            pltpu.SemaphoreType.DMA((2, blocks)),
            pltpu.SMEM((leaves,), jnp.int32),
            vm((FEAT, total // layout.halves), bf16),
            vm((2, LEAF, layout.span), f32),
            vm((2, LEAF, layout.span), f32),
            vm((layout.ahead, LEAF, layout.span), bf16),
            pltpu.SemaphoreType.DMA((layout.ahead,)),
        ],
        compiler_params=params(40),
        name="tree_points",
    )(in_hbm(near_count), in_hbm(near_list[0]), in_hbm(skeleton_upper), *small, *place)

    if fine:
        light, slots = lax.optimization_barrier((light, slots))
        light = light + [other_core(one) for one in light]
    tree_light, coefs, pack = pl.pallas_call(
        functools.partial(weights_kernel, layout),
        out_shape=(
            vm((cols, total), bf16),
            vm((2 * cols, nodes * SK), bf16),
            shaped((PLACE_ROWS + cols, SK), f32),
        ),
        in_specs=[spec(pl.ANY)] + [spec()] * (3 + layout.count),
        out_specs=(spec(),) * 3,
        scratch_shapes=[
            vm((blocks, rows // LOW * cols, rows), bf16),
            vm((blocks, rows, LOW), bf16),
            vm((blocks, rows, SK), bf16),
            pltpu.SemaphoreType.DMA((blocks,)),
        ],
        compiler_params=params(40),
        name="tree_weights",
    )(in_hbm(base), held(upper_tiles), held(top), held(slots), *light)

    packs = upper_levels(pack, skeleton_upper, my_leaf, trees, blocks)

    near = pl.pallas_call(
        functools.partial(near_kernel, layout),
        out_shape=vm((cols, total // layout.halves), f32),
        in_specs=[spec(SMEM), spec(pl.ANY), spec(pl.ANY)] + [spec()] * 2,
        out_specs=spec(),
        scratch_shapes=[
            vm((total, FEAT), bf16),
            vm((FEAT, total // layout.halves), bf16),
            vm((layout.ahead, LEAF, layout.span), bf16),
            pltpu.SemaphoreType.DMA((layout.ahead + 1,)),
        ]
        + [vm((2, LEAF, layout.span), f32)] * 2
        + [vm((2, LEAF, layout.span), bf16)] * 2,
        compiler_params=params(40),
        name="near",
    )(in_hbm(tiles), in_hbm(feat_a), in_hbm(made), held(tree), held(tree_light))

    levels = low_levels + ups
    back = pl.pallas_call(
        functools.partial(far_kernel, layout, low_levels),
        out_shape=(shaped((layout.count // layout.halves, cols, total // layout.count), f32),) * layout.halves,
        in_specs=[spec()] * 7,
        out_specs=(spec(),) * layout.halves,
        scratch_shapes=[
            vm((blocks, levels * SK, FEAT), bf16),
            vm((blocks, 2 * cols, levels * SK), bf16),
            vm((leaves, 2 * cols, levels * SK), bf16),
            vm((blocks, LOW, rows), bf16),
            vm((FEAT, total // layout.halves), bf16),
            vm((cols, total // layout.halves), f32),
            vm((blocks, rows // LOW // layout.halves * 2 * cols, LOW), bf16),
        ]
        + [vm((levels * SK, layout.span), f32)] * 2
        + [vm((levels * SK, layout.span), bf16)] * 2,
        compiler_params=params(40),
        name="far",
    )(packs, *[held(one) for one in (slots, info, tree, sk, coefs, near)])

    if fine:
        kept, sent = back
        sums = pl.pallas_call(
            add_kernel,
            out_shape=(shaped((cols, part), f32),) * blocks,
            in_specs=[spec()] * 2,
            out_specs=(spec(),) * blocks,
            compiler_params=params(40),
            name="add_cores",
        )(kept, other_core(sent))
        back = [swap(sums[step], step) for step in far_first(blocks)]
        back = back + [other_core(one) for one in back]
    else:
        back = back[0].reshape(cols, blocks, devices, per).transpose(2, 0, 1, 3).reshape(devices, width, part)
        back = lax.all_to_all(back, ("leaf", "sub"), split_axis=0, concat_axis=0, tiled=True)
        back = [back.reshape(trees, columns, part).transpose(1, 0, 2).reshape(columns, rows)]

    return pl.pallas_call(
        functools.partial(final_kernel, blocks if fine else 0),
        out_shape=shaped((rows, columns), f32),
        in_specs=[spec()] * (2 + layout.count),
        out_specs=spec(),
        scratch_shapes=[vm((rows, rows), bf16), vm((2 * LANES, rows), bf16)],
        compiler_params=params(40),
        name="to_input_order",
    )(pos, *back, weights)


def solution(mesh):
    in_specs = (
        P(("groups", "leaf", "sub"), None),
        P(("groups", "leaf", "sub"), "rep"),
        P(("groups", "leaf", "sub")),
        P(("groups", "leaf"), None),
        P(("groups", "leaf"), None, None),
        P(("groups", "leaf", "sub"), None),
        P("groups", None),
        P(("groups", "leaf", "sub"), None),
    )
    out_specs = P(("groups", "leaf", "sub"), "rep")
    return jax.shard_map(body, mesh=mesh, in_specs=in_specs, out_specs=out_specs, check_vma=False)
```

```python
import functools

import jax
import jax.numpy as jnp
from jax import lax
from jax.experimental import pallas as pl
from jax.experimental.pallas import tpu as pltpu
from jax.sharding import PartitionSpec as P

DIM = 64
LEAF = 512
SK = 128
LANES = 128
FEAT = 256
LOW = 256
AHEAD = 8
COORD = 144

highest = lax.Precision.HIGHEST
point_scale = 0.25
ridge = 0.5
PLACE_ROWS = 72
TAIL = 64
SLOT, NORM, BASE, FLAGS = 0, 1, 2, 3
f32 = jnp.float32
bf16 = jnp.bfloat16
VMEM = pltpu.MemorySpace.VMEM
SMEM = pltpu.MemorySpace.SMEM


def spec(space=VMEM):
    return pl.BlockSpec(memory_space=space)


def params(mib=58):
    return pltpu.CompilerParams(vmem_limit_bytes=mib * 1024 * 1024)


def in_hbm(array):
    return pltpu.with_memory_space_constraint(array, pltpu.MemorySpace.HBM)


def held(array):
    return pltpu.with_memory_space_constraint(array, VMEM)


def vm(shape, dtype):
    return pltpu.VMEM(shape, dtype)


def shaped(shape, dtype):
    return jax.ShapeDtypeStruct(shape, dtype)


def nt(left, right):
    return lax.dot_general(left, right, (((1,), (1,)), ((), ())), preferred_element_type=f32)


def nn(left, right):
    return jnp.dot(left, right, preferred_element_type=f32)


def column(row):
    return jnp.transpose(jnp.broadcast_to(row, (LANES, LANES)))


def iota(shape, dim):
    return lax.broadcasted_iota(jnp.int32, shape, dim)


def onehot(mask):
    return jnp.where(mask, 1.0, 0.0).astype(bf16)


def two(value):
    high = value.astype(bf16)
    return high, (value - high.astype(f32)).astype(bf16)


def three(value):
    high = value.astype(bf16).astype(f32)
    mid = (value - high).astype(bf16).astype(f32)
    return high, mid, (value - high - mid).astype(bf16).astype(f32)


def lanes_of(blocks):
    return blocks[0] if len(blocks) == 1 else jnp.concatenate(blocks, 1)


def aligned(start, size, unit):
    return pl.ds(pl.multiple_of(start, unit), size)


def stack_two(value):
    high, low = two(value)
    return jnp.concatenate([high, low], 0)


def spread(perm, here, rank):
    lane = iota((LANES, LANES), 1).astype(f32)
    for c in range(perm.shape[1] // LANES):
        perm[here, c * LANES : (c + 1) * LANES] = onehot(lane + float(c * LANES) == rank)


def place_kernel(fine, slot_ref, points_ref, base_ref, flag_ref, place_ref, pos_ref, masked, low_hot):
    chunks = slot_ref.shape[0]
    slots = slot_ref[...]
    slot = slots.astype(f32)
    within = slots & (chunks * LANES - 1)
    high, low = (within >> 5).astype(f32), (within & 31).astype(f32)
    ranks = []
    for r in range(chunks):
        here = slice(r * LANES, (r + 1) * LANES)
        mine = column(slot[r : r + 1])
        before = jnp.zeros((LANES, LANES), f32)
        for c in range(chunks):
            before += jnp.where(slot[c : c + 1] < mine, 1.0, 0.0)
        rank = jnp.broadcast_to(jnp.sum(before, axis=1, keepdims=True), (LANES, LANES))
        ranks.append(jnp.transpose(rank)[0:1])
        pos_ref[r : r + 1, :] = ranks[-1]
        spread(low_hot, here, (rank.astype(jnp.int32) & (LOW - 1)).astype(f32))
    scaled = points_ref[...] * point_scale
    ph, plo = two(scaled)
    nh, nm, nl = three(-0.5 * jnp.sum(scaled * scaled, axis=0, keepdims=True))
    high, low = lanes_of([high[c : c + 1] for c in range(chunks)]), lanes_of([low[c : c + 1] for c in range(chunks)])
    sub = iota((16, chunks * LANES), 0)
    extra = jnp.where(sub == 0, high, jnp.where(sub == 1, low, 0.0))
    extra = jnp.where(sub == 2, nh, jnp.where(sub == 3, nm, jnp.where(sub == 4, nl, extra)))
    high_part = lanes_of(ranks).astype(jnp.int32) // LOW
    parts = place_ref.shape[1] // LOW
    first = (lax.axis_index("leaf") ^ lax.axis_index("rep")) * parts if fine else 0
    for h in range(parts):
        here = high_part == first + h
        masked[h * COORD : h * COORD + 64, :] = jnp.where(here, ph.astype(f32), 0.0).astype(bf16)
        masked[h * COORD + 64 : h * COORD + 128, :] = jnp.where(here, plo.astype(f32), 0.0).astype(bf16)
        masked[h * COORD + 128 : (h + 1) * COORD, :] = jnp.where(here, extra, 0.0).astype(bf16)
    placed = nn(masked[...], low_hot[...])
    tail = iota((PLACE_ROWS - TAIL, LOW), 0)
    for h in range(parts):
        at = slice(h * LOW, (h + 1) * LOW)
        moved = placed[h * COORD : (h + 1) * COORD]
        place_ref[0:TAIL, at] = moved[0:64] + moved[64:128]
        slot_row = moved[128:129] * 32.0 + moved[129:130]
        norm_row = moved[130:131] + moved[131:132] + moved[132:133]
        place_ref[TAIL:, at] = jnp.where(tail == SLOT, slot_row, jnp.where(tail == NORM, norm_row, 0.0))
    if fine:
        place_ref[TAIL + BASE : TAIL + BASE + 1, 0:SK] = base_ref[...].astype(f32)
        place_ref[TAIL + FLAGS : TAIL + FLAGS + flag_ref.shape[0], 0 : flag_ref.shape[1]] = flag_ref[...].astype(f32)


def light_kernel(blocks, pos_ref, weights_ref, *refs):
    light_refs, (masked, low_hot, placed) = refs[:-3], refs[-3:]
    chunks = pos_ref.shape[0]
    high_count = chunks * LANES // LOW
    low_part, high_part = parts_of(lanes_of([pos_ref[c : c + 1, :] for c in range(chunks)]))
    low_by_column(low_hot, low_part.astype(f32))
    for c in range(chunks):
        at = slice(c * LANES, (c + 1) * LANES)
        turned = jnp.transpose(weights_ref[at, :])
        for h in range(high_count):
            masked[h * LANES : (h + 1) * LANES, at] = jnp.where(high_part[:, at] == h, turned, 0.0).astype(bf16)
    moved = nn(masked[...], low_hot[...])
    for h in range(high_count):
        if not blocks:
            light_refs[0][:, h * LOW : (h + 1) * LOW] = moved[h * LANES : (h + 1) * LANES]
        placed[h] = moved[h * LANES : (h + 1) * LANES]
    if not blocks:
        return
    width, parts = LANES // blocks, high_count // 2
    for other, light_ref in enumerate(light_refs):
        first = (lax.axis_index("leaf") ^ lax.axis_index("rep") ^ other) * parts
        for step in range(blocks):
            columns = aligned((lax.axis_index("sub") ^ step) * width, width, width)
            for h in range(parts):
                light_ref[step, :, h * LOW : (h + 1) * LOW] = placed[first + h, columns, :]


def join_kernel(kept_ref, got_ref, *out_refs):
    half = kept_ref.shape[1]
    for step, out_ref in enumerate(out_refs):
        out_ref[0:half, :] = kept_ref[step]
        out_ref[half:, :] = got_ref[step]


class Layout:
    def __init__(self, blocks, trees, rows, fine):
        self.blocks, self.rows, self.fine = blocks, rows, fine
        self.count = blocks * trees if fine else 1
        self.per = rows // self.count
        self.halves = 2 if fine else 1
        self.span = LEAF // self.halves
        self.ahead = AHEAD // 4 * 4 if fine else 4

    def core(self):
        return lax.axis_index("rep") if self.fine else 0

    def lanes(self, index):
        return slice(index * self.per, (index + 1) * self.per)

    def columns(self, group, half, each):
        if self.fine and group >= self.blocks:
            half = 1 - half
        return slice(half * each, (half + 1) * each)

    def gather(self, refs, index, part):
        return lanes_of([ref[part, self.lanes(index)] for ref in refs])

    def info(self, refs, small_ref, index):
        if not self.fine:
            return small_ref[index]
        core = lax.axis_index("rep")
        found = jnp.zeros((PLACE_ROWS - TAIL, SK), f32)
        for step in range(self.blocks):
            mine, theirs = refs[step][TAIL:, 0:SK], refs[self.blocks + step][TAIL:, 0:SK]
            here = jnp.where(core == 0, mine, theirs)
            found = jnp.where((lax.axis_index("sub") ^ step) == index, here, found)
        return found


def low_by_column(out, low):
    for c in range(out.shape[0] // LANES):
        at = slice(c * LANES, (c + 1) * LANES)
        spread(out, at, column(low[:, at]))


def parts_of(slots):
    slots = slots.astype(jnp.int32)
    return slots & (LOW - 1), slots // LOW


def feature_columns(out, at, tree):
    out[0:64, at] = tree[0:64].astype(bf16)
    out[64:128, at] = tree[0:64].astype(bf16)
    out[128:192, at] = tree[64:128].astype(bf16)
    out[192:208, at] = jnp.where(iota((16, tree.shape[1]), 0) < 8, tree[128:144].astype(f32), 0.0).astype(bf16)
    out[208:256, at] = jnp.zeros((48, tree.shape[1]), bf16)


def feature_rows(high, low, extra):
    first = jnp.transpose(jnp.concatenate([high, low], 0))
    second = jnp.transpose(jnp.concatenate([high, extra, jnp.zeros((56, high.shape[1]), f32)], 0))
    return first.astype(bf16), second.astype(bf16)


def target_columns(layout, out, tree_ref):
    span = layout.span
    for leaf in range(out.shape[1] // span):
        here = aligned(leaf * LEAF + layout.core() * span, span, span)
        feature_columns(out, slice(leaf * span, (leaf + 1) * span), tree_ref[:, here])


def tile_exponents(layout, tiles, tile, a_ref, bt_ref):
    source = aligned(tiles[1, tile] * LEAF, LEAF, LEAF)
    target = aligned(tiles[0, tile] * layout.span, layout.span, layout.span)
    return nn(a_ref[source, :], bt_ref[:, target])


def tiles_ahead(layout, tiles, a_ref, bt_ref, even, odd, made, made_hbm, sems):
    def send(tile):
        return pltpu.make_async_copy(made.at[tile], made_hbm.at[tile], sems.at[tile])

    for k in range(2):
        even[k] = tile_exponents(layout, tiles, k, a_ref, bt_ref)

    def step(pair, carry):
        for unit, ready, upcoming in ((2 * pair, even, odd), (2 * pair + 1, odd, even)):
            for k in range(2):
                tile = 2 * unit + k
                upcoming[k] = tile_exponents(layout, tiles, tile + 2, a_ref, bt_ref)
                made[tile] = jnp.exp(ready[k]).astype(bf16)
                send(tile).start()
        return carry

    lax.fori_loop(0, layout.ahead // 4, step, 0)
    return [send(tile) for tile in range(layout.ahead)]


def list_tiles(count_ref, list_ref, tiles, times):
    every = count_ref.shape[1]

    def tally(leaf, filled):
        for other in range(every):
            times[other] = (leaf == other).astype(jnp.int32)

        def add(slot, carry):
            at = list_ref[leaf, slot]
            times[at] = times[at] + 1
            return carry

        lax.fori_loop(0, count_ref[0, leaf], add, 0)
        for other in range(every):
            tiles[0, filled] = leaf
            tiles[1, filled] = other
            tiles[2, filled] = times[other]
            filled = filled + (times[other] > 0).astype(jnp.int32)
        return filled

    filled = lax.fori_loop(0, every, tally, jnp.int32(0))

    def pad(more, carry):
        tiles[0, more] = 0
        tiles[1, more] = 0
        tiles[2, more] = 0
        return carry

    lax.fori_loop(filled, tiles.shape[1] - 1, pad, 0)
    tiles[0, tiles.shape[1] - 1] = filled


def points_kernel(layout, trees, count_ref, list_ref, upper_ref, *refs):
    if not layout.fine:
        small_ref, refs = refs[0], refs[1:]
    else:
        small_ref = None
    place_refs, refs = refs[: layout.count], refs[layout.count :]
    tree_ref, a_hbm, base_hbm, sk_ref, upper_tiles_ref, top_ref, slot_ref, info_ref, tiles, made_hbm = refs[:10]
    masked, low_hot, a_ref, base_ref, sk_t, sk_bt, sems, times, bt_ref, even, odd, made, made_sems = refs[10:]
    blocks, rows = layout.blocks, layout.rows

    def keep(node, found):
        at = slice(node * SK, (node + 1) * SK)
        sk_t[:, at] = found.astype(bf16)
        sk_ref[at, 0:128], sk_ref[at, 128:256] = feature_rows(found[0:64], found[64:128], found[136:144])
        feature_columns(sk_bt, at, found)

    high_parts = rows // LOW
    infos = []
    for index in range(blocks):
        tail = layout.gather(place_refs, index, slice(TAIL, PLACE_ROWS))
        slots = tail[SLOT : SLOT + 1]
        slot_ref[index : index + 1, :] = slots
        infos.append(layout.info(place_refs, small_ref, index))
        info_ref[index] = infos[-1]
        low_part, high_part = parts_of(slots)
        low_by_column(low_hot.at[index], low_part.astype(f32))
        points = layout.gather(place_refs, index, slice(0, TAIL))
        high, low = two(points)
        nh, nm, nl = three(tail[NORM : NORM + 1])
        sub = iota((16, rows), 0)
        norms = jnp.where((sub == 3) | (sub == 8), nh, jnp.where((sub == 4) | (sub == 9), nm, nl))
        is_norm = ((sub >= 3) & (sub < 6)) | ((sub >= 8) & (sub < 11))
        is_one = (sub < 3) | ((sub >= 11) & (sub < 14))
        extra = jnp.where(is_norm, norms, jnp.where(is_one, 1.0, 0.0))
        for h in range(high_parts):
            here = high_part == h
            at = h * COORD
            masked[index, at : at + 64, :] = jnp.where(here, high.astype(f32), 0.0).astype(bf16)
            masked[index, at + 64 : at + 128, :] = jnp.where(here, low.astype(f32), 0.0).astype(bf16)
            masked[index, at + 128 : at + COORD, :] = jnp.where(here, extra, 0.0).astype(bf16)
    copies = []
    for index in range(blocks):
        placed = nn(masked[index], low_hot[index])
        for h in range(high_parts):
            part = placed[h * COORD : (h + 1) * COORD]
            at = slice(index * rows + h * LOW, index * rows + (h + 1) * LOW)
            tree_ref[:, at] = part.astype(bf16)
            a_ref[at, 0:128], a_ref[at, 128:256] = feature_rows(part[0:64], part[64:128], part[136:144])
        mine = slice(index * rows, (index + 1) * rows)
        copies.append(pltpu.make_async_copy(a_ref.at[mine], a_hbm.at[mine], sems.at[0, index]))
        copies[-1].start()
    for index in range(blocks):
        mine = slice(index * rows, (index + 1) * rows)
        picked = onehot(iota((rows, SK), 0) == infos[index][BASE : BASE + 1].astype(jnp.int32))
        keep(index, nn(tree_ref[:, mine], picked))
    for index in range(blocks):
        mine = slice(index * rows, (index + 1) * rows)
        base_ref[index] = jnp.exp(nn(a_ref[mine, :], sk_bt[:, index * SK : (index + 1) * SK])).astype(bf16)
        copies.append(pltpu.make_async_copy(base_ref.at[index], base_hbm.at[index], sems.at[1, index]))
        copies[-1].start()
    start, count, offset, total = 0, blocks, 0, blocks * trees
    while count > 1:
        nodes = count // 2
        for j in range(nodes):
            pair = slice((start + 2 * j) * SK, (start + 2 * j + 2) * SK)
            row = offset + lax.axis_index("leaf") * nodes + j
            picked = onehot(iota((2 * SK, SK), 0) == upper_ref[pl.ds(row, 1), :])
            here = start + count + j
            keep(here, nn(sk_t[:, pair], picked))
            upper_tiles_ref[here - blocks] = jnp.exp(nn(sk_ref[pair, :], sk_bt[:, here * SK : (here + 1) * SK]))
        total = total // 2
        offset = offset + total
        start, count = start + count, nodes
    found = sk_t[:, start * SK : (start + 1) * SK].astype(f32)
    top_ref[0:64, :] = found[0:64] + found[64:128]
    top_ref[64:72, :] = found[128:136]
    list_tiles(count_ref, list_ref, tiles, times)
    target_columns(layout, bt_ref, tree_ref)
    copies += tiles_ahead(layout, tiles, a_ref, bt_ref, even, odd, made, made_hbm, made_sems)
    for copy in copies:
        copy.wait()


def weights_kernel(layout, base_hbm, upper_tiles_ref, top_ref, slot_ref, *refs):
    light_refs, refs = refs[: layout.count], refs[layout.count :]
    if layout.fine:
        order = far_first(layout.blocks)
        order = order + [layout.blocks + step for step in order]
        light_refs = [light_refs[order.index(g)] for g in range(layout.count)]
    w_ref, coef_ref, pack_ref, masked, low_hot, base_ref, sems = refs
    blocks, rows = layout.blocks, layout.rows
    width = light_refs[0].shape[0]
    each = width // layout.halves
    pack_ref[0:PLACE_ROWS, :] = top_ref[...]
    for index in range(blocks):
        pltpu.make_async_copy(base_hbm.at[index], base_ref.at[index], sems.at[index]).start()

    def keep(node, coef):
        coef_ref[:, node * SK : (node + 1) * SK] = stack_two(coef)
        pack_ref[PLACE_ROWS:, :] = coef

    for index in range(blocks):
        low_part, high_part = parts_of(slot_ref[index : index + 1, :])
        low_by_column(low_hot.at[index], low_part.astype(f32))
        for half in range(layout.halves):
            light = [ref[layout.columns(g, half, each), layout.lanes(index)] for g, ref in enumerate(light_refs)]
            light = lanes_of(light)
            for h in range(rows // LOW):
                at = h * width + half * each
                masked[index, at : at + each, :] = jnp.where(high_part == h, light, 0.0).astype(bf16)
    for index in range(blocks):
        placed = nn(masked[index], low_hot[index])
        for h in range(rows // LOW):
            at = index * rows + h * LOW
            w_ref[:, at : at + LOW] = placed[h * width : (h + 1) * width].astype(bf16)
    for index in range(blocks):
        pltpu.make_async_copy(base_hbm.at[index], base_ref.at[index], sems.at[index]).wait()
        keep(index, nn(w_ref[:, index * rows : (index + 1) * rows], base_ref[index]))
    start, count = 0, blocks
    while count > 1:
        for j in range(count // 2):
            pair = slice((start + 2 * j) * SK, (start + 2 * j + 2) * SK)
            here = start + count + j
            high, low = two(upper_tiles_ref[here - blocks])
            coef = nn(coef_ref[:, pair], high)
            keep(here, coef[:width] + coef[width:] + nn(coef_ref[0:width, pair], low))
        start, count = start + count, count // 2


def near_kernel(layout, tiles, a_hbm, made_hbm, tree_ref, w_ref, acc, a_ref, bt_ref, made, sems, even, odd, even_tile, odd_tile):
    ahead, span = layout.ahead, layout.span

    def fetch(tile):
        return pltpu.make_async_copy(made_hbm.at[tile], made.at[tile], sems.at[tile])

    copy = pltpu.make_async_copy(a_hbm, a_ref, sems.at[ahead])
    copy.start()
    for tile in range(ahead):
        fetch(tile).start()
    filled = tiles[0, tiles.shape[1] - 1]
    acc[...] = jnp.zeros_like(acc)
    target_columns(layout, bt_ref, tree_ref)

    def exponents(unit, out):
        for k in range(2):
            out[k] = tile_exponents(layout, tiles, ahead + 2 * unit + k, a_ref, bt_ref)

    def add(tile, block):
        source = aligned(tiles[1, tile] * LEAF, LEAF, LEAF)
        target = aligned(tiles[0, tile] * span, span, span)
        acc[:, target] += tiles[2, tile].astype(f32) * nn(w_ref[:, source], block)

    copy.wait()

    @pl.when(filled > ahead)
    def _():
        exponents(0, even)
        for k in range(2):
            even_tile[k] = jnp.exp(even[k]).astype(bf16)
        exponents(1, odd)

        def phase(unit, upcoming, ready, finished, previous):
            for k in range(2):
                upcoming[k] = tile_exponents(layout, tiles, ahead + 2 * (unit + 1) + k, a_ref, bt_ref)
                finished[k] = jnp.exp(ready[k]).astype(bf16)
                add(ahead + 2 * (unit - 1) + k, previous[k])

        def step(pair, carry):
            phase(2 * pair + 1, even, odd, odd_tile, even_tile)
            phase(2 * pair + 2, odd, even, even_tile, odd_tile)
            return carry

        units = (filled - ahead + 1) // 2
        pairs = (units - 1) // 2
        lax.fori_loop(0, pairs, step, 0)
        for k in range(2):
            add(ahead + 4 * pairs + k, even_tile[k])

        @pl.when(2 * pairs + 1 < units)
        def _():
            for k in range(2):
                odd_tile[k] = jnp.exp(odd[k]).astype(bf16)
                add(ahead + 4 * pairs + 2 + k, odd_tile[k])

    def arrived(quad, carry):
        for more in range(4):
            fetch(4 * quad + more).wait()
            tile = 4 * quad + more

            @pl.when(tile < filled)
            def _():
                add(tile, made[tile])

        return carry

    lax.fori_loop(0, ahead // 4, arrived, 0)


def far_kernel(layout, low_levels, pack_ref, slot_ref, info_ref, tree_ref, sk_ref, coef_ref, near_ref, *refs):
    out_refs, refs = refs[: layout.halves], refs[layout.halves :]
    tops, coefs, scaled, low_hot, bt_ref, sums, masked = refs[:7]
    powers, tiles = refs[7:9], refs[9:11]
    blocks, rows = layout.blocks, layout.rows
    ups, width = pack_ref.shape[0], near_ref.shape[0]
    levels = low_levels + ups
    span, core = layout.span, layout.core()
    per_block = rows // LEAF
    lane = iota((1, SK), 1)
    for up in range(ups):
        pack = pack_ref[up]
        high, low = two(pack[0:64])
        sub = iota((8, SK), 0)
        extra = jnp.where(sub == 0, pack[67:68], jnp.where(sub == 1, pack[68:69], pack[69:70]))
        extra = jnp.where(sub < 3, extra, jnp.where(sub < 6, 1.0, 0.0))
        at = slice((low_levels + up) * SK, (low_levels + up + 1) * SK)
        rows_of = feature_rows(high.astype(f32), low.astype(f32), extra)
        coef = stack_two(pack[PLACE_ROWS:])
        for index in range(blocks):
            tops[index, at, 0:128], tops[index, at, 128:256] = rows_of
            coefs[index, :, at] = coef
    for index in range(blocks):
        node, start, count = index, 0, blocks
        for level in range(low_levels):
            at = slice(level * SK, (level + 1) * SK)
            other = slice((start + (node ^ 1)) * SK, (start + (node ^ 1) + 1) * SK)
            tops[index, at, :] = sk_ref[other, :]
            coefs[index, :, at] = coef_ref[:, other]
            node, start, count = node // 2, start + count, count // 2
        for leaf in range(per_block):
            flags = info_ref[index, FLAGS + leaf : FLAGS + leaf + 1, :]
            used = []
            for level in range(levels):
                flag = jnp.sum(jnp.where(lane == level, flags, 0.0), axis=1, keepdims=True)
                used.append(jnp.broadcast_to(flag, (1, SK)))
            used = jnp.concatenate(used, 1)
            scaled[index * per_block + leaf] = (coefs[index].astype(f32) * used).astype(bf16)

    target_columns(layout, bt_ref, tree_ref)

    def exponents(leaf):
        powers[leaf % 2][...] = nn(tops[leaf // per_block], bt_ref[:, leaf * span : (leaf + 1) * span])

    def product(leaf):
        here = slice(leaf * span, (leaf + 1) * span)
        far = nn(scaled[leaf], tiles[leaf % 2][...])
        sums[:, here] = near_ref[:, here] + far[:width] + far[width:]

    leaves = blocks * per_block
    exponents(0)
    for leaf in range(leaves):
        if leaf + 1 < leaves:
            exponents(leaf + 1)
        tiles[leaf % 2][...] = jnp.exp(powers[leaf % 2][...]).astype(bf16)
        if leaf:
            product(leaf - 1)
    product(leaves - 1)

    high_parts = []
    pieces = rows // LOW // layout.halves
    for index in range(blocks):
        low_part, high_part = parts_of(slot_ref[index : index + 1, :])
        high_parts.append(high_part)
        for c in range(rows // LANES):
            at = slice(c * LANES, (c + 1) * LANES)
            low_hot[index, :, at] = onehot(iota((LOW, LANES), 0) == low_part[:, at])
        for k in range(pieces):
            at = (index * pieces + k) * LOW
            masked[index, k * 2 * width : (k + 1) * 2 * width, :] = stack_two(sums[:, at : at + LOW])
    for index in range(blocks):
        moved = nn(masked[index], low_hot[index])
        result = jnp.zeros((2 * width, rows), f32)
        for k in range(pieces):
            here = high_parts[index] == k * layout.halves + core
            result = jnp.where(here, moved[k * 2 * width : (k + 1) * 2 * width], result)
        result = result[:width] + result[width:]
        if not layout.fine:
            out_refs[0][0, :, layout.lanes(index)] = result
            continue
        for g in range(layout.count):
            out_ref = out_refs[g // blocks]
            out_ref[g % blocks, :, layout.lanes(index)] = result[:, g * layout.per : (g + 1) * layout.per]


def add_kernel(kept_ref, got_ref, *out_refs):
    half = kept_ref.shape[1] // 2
    for step, out_ref in enumerate(out_refs):
        out_ref[0:half, :] = kept_ref[step, 0:half, :] + got_ref[step, half:, :]
        out_ref[half:, :] = kept_ref[step, half:, :] + got_ref[step, 0:half, :]


def far_first(blocks):
    return sorted(range(blocks), key=lambda step: -(step * 2 // blocks))


def final_kernel(blocks, pos_ref, *refs):
    back_refs, (weights_ref, out_ref, perm, vals) = refs[:-4], refs[-4:]
    chunks = pos_ref.shape[0]
    rows = chunks * LANES
    width, split = back_refs[0].shape
    width = LANES // blocks if blocks else width
    for r in range(chunks):
        spread(perm, slice(r * LANES, (r + 1) * LANES), column(pos_ref[r : r + 1, :]))
    for g, back_ref in enumerate(back_refs):
        columns, at = 0, slice(0, rows)
        value = back_ref[...]
        if blocks:
            columns = (lax.axis_index("sub") ^ far_first(blocks)[g % blocks]) * width
            at = aligned((lax.axis_index("leaf") ^ lax.axis_index("rep") ^ (g // blocks)) * split, split, split)
            value = value[0:width] if g < blocks else value[width:]
        high, low = two(value)
        vals[aligned(columns, width, width), at] = high
        vals[aligned(columns + LANES, width, width), at] = low
    step = 256
    for s in range(rows // step):
        here = slice(s * step, (s + 1) * step)
        moved = nt(perm[here, :], vals[...])
        out_ref[here, :] = ridge * weights_ref[here, :] + moved[:, :LANES] + moved[:, LANES:]


def upper_levels(pack, skeleton_upper, my_leaf, trees, blocks):
    devices = trees * blocks
    level = blocks.bit_length() - 1
    offset = sum(devices >> step for step in range(1, level + 1))
    line = jnp.arange(pack.shape[0])[:, None]
    is_point, is_norm = line < DIM, (line >= DIM + 3) & (line < DIM + 6)
    is_coef = line >= PLACE_ROWS
    packs, own, stride = [], pack, 1
    while stride < trees:
        other = lax.ppermute(own, "leaf", [(i, i ^ stride) for i in range(trees)])
        packs.append(other)
        stride *= 2
        if stride < trees:
            second = (my_leaf // (stride // 2)) % 2 == 1
            pair = jnp.where(second, jnp.concatenate([other, own], 1), jnp.concatenate([own, other], 1))
            chosen = pair[:, skeleton_upper[offset + my_leaf // stride]]
            level += 1
            offset += devices >> level
            norms = jnp.sum(jnp.where(is_norm, pair, 0.0), axis=0)
            chosen_norms = jnp.sum(jnp.where(is_norm, chosen, 0.0), axis=0)
            inner = jnp.dot(
                jnp.where(is_point, pair, 0.0).T, jnp.where(is_point, chosen, 0.0), precision=highest
            )
            tile = jnp.exp(inner + norms[:, None] + chosen_norms[None])
            own = jnp.where(is_coef, jnp.dot(pair, tile, precision=highest), chosen)
    return jnp.stack(packs)


def body(points, weights, tree_slot, near_count, near_list, skeleton_base, skeleton_upper, far_use):
    blocks, trees, reps = lax.axis_size("sub"), lax.axis_size("leaf"), lax.axis_size("rep")
    devices = blocks * trees
    rows, columns = weights.shape
    low_levels = blocks.bit_length() - 1
    ups = trees.bit_length() - 1
    width = columns // blocks
    part = rows // trees
    per = part // blocks
    total = blocks * rows
    leaves = total // LEAF
    my_leaf = lax.axis_index("leaf")
    fine = trees == 2 and reps == 2 and per % LANES == 0
    layout = Layout(blocks, trees, rows, fine)
    split = part if fine else rows
    cols = width * layout.halves

    place, pos = pl.pallas_call(
        functools.partial(place_kernel, fine),
        out_shape=(shaped((PLACE_ROWS, split), f32), shaped((rows // LANES, LANES), f32)),
        in_specs=[spec()] * 4,
        out_specs=(spec(),) * 2,
        scratch_shapes=[vm((split // LOW * COORD, rows), bf16), vm((rows, LOW), bf16)],
        compiler_params=params(),
        name="sort_points",
    )(tree_slot.reshape(rows // LANES, LANES), points.T, skeleton_base, far_use)
    axes = ("leaf", "sub", "rep")

    def swap(value, step, other=0):
        pairs = []
        for leaf in range(trees):
            for sub in range(blocks):
                for core in range(reps):
                    to = ((leaf ^ core ^ other) * blocks + (sub ^ step)) * reps + core
                    pairs.append(((leaf * blocks + sub) * reps + core, to))
        return lax.ppermute(value, axes, pairs)

    def other_core(value):
        return lax.ppermute(value, "rep", [(0, 1), (1, 0)])

    def sorted_light(pos):
        if fine:
            shapes = (shaped((blocks, width, part), f32),) * 2
        else:
            shapes = (shaped((columns, rows), f32),)
        return pl.pallas_call(
            functools.partial(light_kernel, blocks if fine else 0),
            out_shape=shapes,
            in_specs=[spec()] * 2,
            out_specs=(spec(),) * len(shapes),
            scratch_shapes=[
                vm((rows // LOW * LANES, rows), bf16),
                vm((rows, LOW), bf16),
                vm((rows // LOW, LANES, LOW), f32),
            ],
            compiler_params=params(40),
            name="sort_weights",
        )(in_hbm(pos), in_hbm(weights))

    if fine:
        place = {0: swap(place, 0)}
        stride = blocks // 2
        while stride:
            for step in sorted(place):
                place[step | stride] = lax.ppermute(place[step], "sub", [(i, i ^ stride) for i in range(blocks)])
            stride //= 2
        kept, sent = sorted_light(pos)
        place, kept, sent = lax.optimization_barrier((place, kept, sent))
        light = pl.pallas_call(
            join_kernel,
            out_shape=(shaped((cols, part), f32),) * blocks,
            in_specs=[spec()] * 2,
            out_specs=(spec(),) * blocks,
            compiler_params=params(40),
            name="join_cores",
        )(kept, other_core(sent))
        theirs = {step: other_core(one) for step, one in place.items()}
        place = [place[step] for step in range(blocks)] + [theirs[step] for step in range(blocks)]
        light = [swap(light[step], step) for step in far_first(blocks)]
        small = []
    else:
        info = jnp.pad(far_use.astype(f32), ((FLAGS, 5 - far_use.shape[0]), (0, SK - far_use.shape[1])))
        small = [lax.all_gather(info.at[BASE].set(skeleton_base[0].astype(f32)), "sub", axis=0, tiled=False)]
        place = place.reshape(PLACE_ROWS, trees, part).transpose(1, 0, 2)
        place = lax.all_to_all(place, "leaf", split_axis=0, concat_axis=0, tiled=True)
        place = lax.all_gather(place, "sub", axis=0, tiled=False)
        place = place.transpose(1, 0, 2, 3).reshape(devices, PLACE_ROWS, blocks, per)
        place = [place.transpose(1, 2, 0, 3).reshape(PLACE_ROWS, total)]
        light = sorted_light(pos)[0].reshape(columns, trees, part).transpose(1, 0, 2).reshape(devices, width, part)
        light = lax.all_to_all(light, ("leaf", "sub"), split_axis=0, concat_axis=0, tiled=True)
        light = light.reshape(devices, width, blocks, per)
        light = [light.transpose(1, 2, 0, 3).reshape(width, total)]

    nodes = 2 * blocks - 1
    tree, feat_a, base, sk, upper_tiles, top, slots, info, tiles, made = pl.pallas_call(
        functools.partial(points_kernel, layout, trees),
        out_shape=(
            vm((COORD, total), bf16),
            pltpu.MemorySpace.HBM((total, FEAT), bf16),
            pltpu.MemorySpace.HBM((blocks, rows, SK), bf16),
            vm((nodes * SK, FEAT), bf16),
            vm((blocks - 1, 2 * SK, SK), f32),
            vm((PLACE_ROWS, SK), f32),
            vm((blocks, rows), f32),
            vm((blocks, 8, SK), f32),
            pltpu.MemorySpace.HBM((3, leaves * leaves + 8), jnp.int32),
            pltpu.MemorySpace.HBM((layout.ahead, LEAF, layout.span), bf16),
        ),
        in_specs=[spec(SMEM)] * 2 + [spec()] * (1 + len(small) + layout.count),
        out_specs=(spec(), spec(pl.ANY), spec(pl.ANY)) + (spec(),) * 5 + (spec(SMEM), spec(pl.ANY)),
        scratch_shapes=[
            vm((blocks, rows // LOW * COORD, rows), bf16),
            vm((blocks, rows, LOW), bf16),
            vm((total, FEAT), bf16),
            vm((blocks, rows, SK), bf16),
            vm((COORD, nodes * SK), bf16),
            vm((FEAT, nodes * SK), bf16),
            pltpu.SemaphoreType.DMA((2, blocks)),
            pltpu.SMEM((leaves,), jnp.int32),
            vm((FEAT, total // layout.halves), bf16),
            vm((2, LEAF, layout.span), f32),
            vm((2, LEAF, layout.span), f32),
            vm((layout.ahead, LEAF, layout.span), bf16),
            pltpu.SemaphoreType.DMA((layout.ahead,)),
        ],
        compiler_params=params(40),
        name="tree_points",
    )(in_hbm(near_count), in_hbm(near_list[0]), in_hbm(skeleton_upper), *small, *place)

    if fine:
        theirs = []
        for step in range(blocks):
            light[step], slots = lax.optimization_barrier((light[step], slots))
            theirs.append(other_core(light[step]))
        light = light + theirs
    tree_light, coefs, pack = pl.pallas_call(
        functools.partial(weights_kernel, layout),
        out_shape=(
            vm((cols, total), bf16),
            vm((2 * cols, nodes * SK), bf16),
            shaped((PLACE_ROWS + cols, SK), f32),
        ),
        in_specs=[spec(pl.ANY)] + [spec()] * (3 + layout.count),
        out_specs=(spec(),) * 3,
        scratch_shapes=[
            vm((blocks, rows // LOW * cols, rows), bf16),
            vm((blocks, rows, LOW), bf16),
            vm((blocks, rows, SK), bf16),
            pltpu.SemaphoreType.DMA((blocks,)),
        ],
        compiler_params=params(40),
        name="tree_weights",
    )(in_hbm(base), held(upper_tiles), held(top), held(slots), *light)

    packs = upper_levels(pack, skeleton_upper, my_leaf, trees, blocks)

    near = pl.pallas_call(
        functools.partial(near_kernel, layout),
        out_shape=vm((cols, total // layout.halves), f32),
        in_specs=[spec(SMEM), spec(pl.ANY), spec(pl.ANY)] + [spec()] * 2,
        out_specs=spec(),
        scratch_shapes=[
            vm((total, FEAT), bf16),
            vm((FEAT, total // layout.halves), bf16),
            vm((layout.ahead, LEAF, layout.span), bf16),
            pltpu.SemaphoreType.DMA((layout.ahead + 1,)),
        ]
        + [vm((2, LEAF, layout.span), f32)] * 2
        + [vm((2, LEAF, layout.span), bf16)] * 2,
        compiler_params=params(40),
        name="near",
    )(in_hbm(tiles), in_hbm(feat_a), in_hbm(made), held(tree), held(tree_light))

    levels = low_levels + ups
    back = pl.pallas_call(
        functools.partial(far_kernel, layout, low_levels),
        out_shape=(shaped((layout.count // layout.halves, cols, total // layout.count), f32),) * layout.halves,
        in_specs=[spec()] * 7,
        out_specs=(spec(),) * layout.halves,
        scratch_shapes=[
            vm((blocks, levels * SK, FEAT), bf16),
            vm((blocks, 2 * cols, levels * SK), bf16),
            vm((leaves, 2 * cols, levels * SK), bf16),
            vm((blocks, LOW, rows), bf16),
            vm((FEAT, total // layout.halves), bf16),
            vm((cols, total // layout.halves), f32),
            vm((blocks, rows // LOW // layout.halves * 2 * cols, LOW), bf16),
        ]
        + [vm((levels * SK, layout.span), f32)] * 2
        + [vm((levels * SK, layout.span), bf16)] * 2,
        compiler_params=params(40),
        name="far",
    )(packs, *[held(one) for one in (slots, info, tree, sk, coefs, near)])

    if fine:
        kept, sent = back
        sums = pl.pallas_call(
            add_kernel,
            out_shape=(shaped((cols, part), f32),) * blocks,
            in_specs=[spec()] * 2,
            out_specs=(spec(),) * blocks,
            compiler_params=params(40),
            name="add_cores",
        )(kept, other_core(sent))
        back = [swap(sums[step], step) for step in far_first(blocks)]
        back = back + [other_core(one) for one in back]
    else:
        back = back[0].reshape(cols, blocks, devices, per).transpose(2, 0, 1, 3).reshape(devices, width, part)
        back = lax.all_to_all(back, ("leaf", "sub"), split_axis=0, concat_axis=0, tiled=True)
        back = [back.reshape(trees, columns, part).transpose(1, 0, 2).reshape(columns, rows)]

    return pl.pallas_call(
        functools.partial(final_kernel, blocks if fine else 0),
        out_shape=shaped((rows, columns), f32),
        in_specs=[spec()] * (2 + layout.count),
        out_specs=spec(),
        scratch_shapes=[vm((rows, rows), bf16), vm((2 * LANES, rows), bf16)],
        compiler_params=params(40),
        name="to_input_order",
    )(pos, *back, weights)


def solution(mesh):
    in_specs = (
        P(("groups", "leaf", "sub"), None),
        P(("groups", "leaf", "sub"), "rep"),
        P(("groups", "leaf", "sub")),
        P(("groups", "leaf"), None),
        P(("groups", "leaf"), None, None),
        P(("groups", "leaf", "sub"), None),
        P("groups", None),
        P(("groups", "leaf", "sub"), None),
    )
    out_specs = P(("groups", "leaf", "sub"), "rep")
    return jax.shard_map(body, mesh=mesh, in_specs=in_specs, out_specs=out_specs, check_vma=False)
```

```python
import functools

import jax
import jax.numpy as jnp
from jax import lax
from jax.experimental import pallas as pl
from jax.experimental.pallas import tpu as pltpu
from jax.sharding import PartitionSpec as P

DIM = 64
LEAF = 512
SK = 128
LANES = 128
FEAT = 256
LOW = 256
COORD = 144

highest = lax.Precision.HIGHEST
point_scale = 0.25
ridge = 0.5
PLACE_ROWS = 72
TAIL = 64
SLOT, NORM, BASE, FLAGS = 0, 1, 2, 3
f32 = jnp.float32
bf16 = jnp.bfloat16
VMEM = pltpu.MemorySpace.VMEM
SMEM = pltpu.MemorySpace.SMEM


def spec(space=VMEM):
    return pl.BlockSpec(memory_space=space)


def params(mib=58):
    return pltpu.CompilerParams(vmem_limit_bytes=mib * 1024 * 1024)


def in_hbm(array):
    return pltpu.with_memory_space_constraint(array, pltpu.MemorySpace.HBM)


def held(array):
    return pltpu.with_memory_space_constraint(array, VMEM)


def vm(shape, dtype):
    return pltpu.VMEM(shape, dtype)


def shaped(shape, dtype):
    return jax.ShapeDtypeStruct(shape, dtype)


def nt(left, right):
    return lax.dot_general(left, right, (((1,), (1,)), ((), ())), preferred_element_type=f32)


def nn(left, right):
    return jnp.dot(left, right, preferred_element_type=f32)


def column(row):
    return jnp.transpose(jnp.broadcast_to(row, (LANES, LANES)))


def iota(shape, dim):
    return lax.broadcasted_iota(jnp.int32, shape, dim)


def onehot(mask):
    return jnp.where(mask, 1.0, 0.0).astype(bf16)


def two(value):
    high = value.astype(bf16)
    return high, (value - high.astype(f32)).astype(bf16)


def three(value):
    high = value.astype(bf16).astype(f32)
    mid = (value - high).astype(bf16).astype(f32)
    return high, mid, (value - high - mid).astype(bf16).astype(f32)


def lanes_of(blocks):
    return blocks[0] if len(blocks) == 1 else jnp.concatenate(blocks, 1)


def aligned(start, size, unit):
    return pl.ds(pl.multiple_of(start, unit), size)


def stack_two(value):
    high, low = two(value)
    return jnp.concatenate([high, low], 0)


def spread(perm, here, rank):
    lane = iota((LANES, LANES), 1).astype(f32)
    for c in range(perm.shape[1] // LANES):
        perm[here, c * LANES : (c + 1) * LANES] = onehot(lane + float(c * LANES) == rank)


def place_kernel(fine, slot_ref, points_ref, base_ref, flag_ref, place_ref, pos_ref, masked, low_hot):
    chunks = slot_ref.shape[0]
    slots = slot_ref[...]
    slot = slots.astype(f32)
    within = slots & (chunks * LANES - 1)
    high, low = (within >> 5).astype(f32), (within & 31).astype(f32)
    ranks = []
    for r in range(chunks):
        here = slice(r * LANES, (r + 1) * LANES)
        mine = column(slot[r : r + 1])
        before = jnp.zeros((LANES, LANES), f32)
        for c in range(chunks):
            before += jnp.where(slot[c : c + 1] < mine, 1.0, 0.0)
        rank = jnp.broadcast_to(jnp.sum(before, axis=1, keepdims=True), (LANES, LANES))
        ranks.append(jnp.transpose(rank)[0:1])
        pos_ref[r : r + 1, :] = ranks[-1]
        spread(low_hot, here, (rank.astype(jnp.int32) & (LOW - 1)).astype(f32))
    scaled = points_ref[...] * point_scale
    ph, plo = two(scaled)
    nh, nm, nl = three(-0.5 * jnp.sum(scaled * scaled, axis=0, keepdims=True))
    high, low = lanes_of([high[c : c + 1] for c in range(chunks)]), lanes_of([low[c : c + 1] for c in range(chunks)])
    sub = iota((16, chunks * LANES), 0)
    extra = jnp.where(sub == 0, high, jnp.where(sub == 1, low, 0.0))
    extra = jnp.where(sub == 2, nh, jnp.where(sub == 3, nm, jnp.where(sub == 4, nl, extra)))
    high_part = lanes_of(ranks).astype(jnp.int32) // LOW
    parts = place_ref.shape[1] // LOW
    first = (lax.axis_index("leaf") ^ lax.axis_index("rep")) * parts if fine else 0
    for h in range(parts):
        here = high_part == first + h
        masked[h * COORD : h * COORD + 64, :] = jnp.where(here, ph.astype(f32), 0.0).astype(bf16)
        masked[h * COORD + 64 : h * COORD + 128, :] = jnp.where(here, plo.astype(f32), 0.0).astype(bf16)
        masked[h * COORD + 128 : (h + 1) * COORD, :] = jnp.where(here, extra, 0.0).astype(bf16)
    placed = nn(masked[...], low_hot[...])
    tail = iota((PLACE_ROWS - TAIL, LOW), 0)
    for h in range(parts):
        at = slice(h * LOW, (h + 1) * LOW)
        moved = placed[h * COORD : (h + 1) * COORD]
        place_ref[0:TAIL, at] = moved[0:64] + moved[64:128]
        slot_row = moved[128:129] * 32.0 + moved[129:130]
        norm_row = moved[130:131] + moved[131:132] + moved[132:133]
        place_ref[TAIL:, at] = jnp.where(tail == SLOT, slot_row, jnp.where(tail == NORM, norm_row, 0.0))
    if fine:
        place_ref[TAIL + BASE : TAIL + BASE + 1, 0:SK] = base_ref[...].astype(f32)
        place_ref[TAIL + FLAGS : TAIL + FLAGS + flag_ref.shape[0], 0 : flag_ref.shape[1]] = flag_ref[...].astype(f32)


def light_kernel(blocks, pos_ref, weights_ref, *refs):
    light_refs, (masked, low_hot, placed) = refs[:-3], refs[-3:]
    chunks = pos_ref.shape[0]
    high_count = chunks * LANES // LOW
    low_part, high_part = parts_of(lanes_of([pos_ref[c : c + 1, :] for c in range(chunks)]))
    low_by_column(low_hot, low_part.astype(f32))
    for c in range(chunks):
        at = slice(c * LANES, (c + 1) * LANES)
        turned = jnp.transpose(weights_ref[at, :])
        for h in range(high_count):
            masked[h * LANES : (h + 1) * LANES, at] = jnp.where(high_part[:, at] == h, turned, 0.0).astype(bf16)
    moved = nn(masked[...], low_hot[...])
    for h in range(high_count):
        if not blocks:
            light_refs[0][:, h * LOW : (h + 1) * LOW] = moved[h * LANES : (h + 1) * LANES]
        placed[h] = moved[h * LANES : (h + 1) * LANES]
    if not blocks:
        return
    width, parts = LANES // blocks, high_count // 2
    for other, light_ref in enumerate(light_refs):
        first = (lax.axis_index("leaf") ^ lax.axis_index("rep") ^ other) * parts
        for step in range(blocks):
            columns = aligned((lax.axis_index("sub") ^ step) * width, width, width)
            for h in range(parts):
                light_ref[step, :, h * LOW : (h + 1) * LOW] = placed[first + h, columns, :]


def join_kernel(kept_ref, got_ref, *out_refs):
    half = kept_ref.shape[1]
    for step, out_ref in enumerate(out_refs):
        out_ref[0:half, :] = kept_ref[step]
        out_ref[half:, :] = got_ref[step]


class Layout:
    def __init__(self, blocks, trees, rows, fine):
        self.blocks, self.rows, self.fine = blocks, rows, fine
        self.count = blocks * trees if fine else 1
        self.per = rows // self.count
        self.halves = 2 if fine else 1
        self.span = LEAF // self.halves

    def core(self):
        return lax.axis_index("rep") if self.fine else 0

    def lanes(self, index):
        return slice(index * self.per, (index + 1) * self.per)

    def columns(self, group, half, each):
        if self.fine and group >= self.blocks:
            half = 1 - half
        return slice(half * each, (half + 1) * each)

    def gather(self, refs, index, part):
        return lanes_of([ref[part, self.lanes(index)] for ref in refs])

    def info(self, refs, small_ref, index):
        if not self.fine:
            return small_ref[index]
        core = lax.axis_index("rep")
        found = jnp.zeros((PLACE_ROWS - TAIL, SK), f32)
        for step in range(self.blocks):
            mine, theirs = refs[step][TAIL:, 0:SK], refs[self.blocks + step][TAIL:, 0:SK]
            here = jnp.where(core == 0, mine, theirs)
            found = jnp.where((lax.axis_index("sub") ^ step) == index, here, found)
        return found


def low_by_column(out, low):
    for c in range(out.shape[0] // LANES):
        at = slice(c * LANES, (c + 1) * LANES)
        spread(out, at, column(low[:, at]))


def parts_of(slots):
    slots = slots.astype(jnp.int32)
    return slots & (LOW - 1), slots // LOW


def feature_columns(out, at, tree):
    out[0:64, at] = tree[0:64].astype(bf16)
    out[64:128, at] = tree[0:64].astype(bf16)
    out[128:192, at] = tree[64:128].astype(bf16)
    out[192:208, at] = jnp.where(iota((16, tree.shape[1]), 0) < 8, tree[128:144].astype(f32), 0.0).astype(bf16)
    out[208:256, at] = jnp.zeros((48, tree.shape[1]), bf16)


def feature_rows(high, low, extra):
    first = jnp.transpose(jnp.concatenate([high, low], 0))
    second = jnp.transpose(jnp.concatenate([high, extra, jnp.zeros((56, high.shape[1]), f32)], 0))
    return first.astype(bf16), second.astype(bf16)


def target_columns(layout, out, tree_ref):
    span = layout.span
    for leaf in range(out.shape[1] // span):
        here = aligned(leaf * LEAF + layout.core() * span, span, span)
        feature_columns(out, slice(leaf * span, (leaf + 1) * span), tree_ref[:, here])


def tile_exponents(layout, tiles, tile, a_ref, bt_ref):
    source = aligned(tiles[1, tile] * LEAF, LEAF, LEAF)
    target = aligned(tiles[0, tile] * layout.span, layout.span, layout.span)
    return nn(a_ref[source, :], bt_ref[:, target])


def list_tiles(count_ref, list_ref, tiles, times):
    every = count_ref.shape[1]

    def tally(leaf, filled):
        for other in range(every):
            times[other] = (leaf == other).astype(jnp.int32)

        def add(slot, carry):
            at = list_ref[leaf, slot]
            times[at] = times[at] + 1
            return carry

        lax.fori_loop(0, count_ref[0, leaf], add, 0)
        for other in range(every):
            tiles[0, filled] = leaf
            tiles[1, filled] = other
            tiles[2, filled] = times[other]
            filled = filled + (times[other] > 0).astype(jnp.int32)
        return filled

    filled = lax.fori_loop(0, every, tally, jnp.int32(0))

    def pad(more, carry):
        tiles[0, more] = 0
        tiles[1, more] = 0
        tiles[2, more] = 0
        return carry

    lax.fori_loop(filled, tiles.shape[1] - 1, pad, 0)
    tiles[0, tiles.shape[1] - 1] = filled


def points_kernel(layout, trees, count_ref, list_ref, upper_ref, *refs):
    if not layout.fine:
        small_ref, refs = refs[0], refs[1:]
    else:
        small_ref = None
    place_refs, refs = refs[: layout.count], refs[layout.count :]
    tree_ref, a_hbm, base_hbm, sk_ref, upper_tiles_ref, top_ref, slot_ref, info_ref, tiles = refs[:9]
    masked, low_hot, a_ref, base_ref, sk_t, sk_bt, sems, times = refs[9:]
    blocks, rows = layout.blocks, layout.rows

    def keep(node, found):
        at = slice(node * SK, (node + 1) * SK)
        sk_t[:, at] = found.astype(bf16)
        sk_ref[at, 0:128], sk_ref[at, 128:256] = feature_rows(found[0:64], found[64:128], found[136:144])
        feature_columns(sk_bt, at, found)

    high_parts = rows // LOW
    infos = []
    for index in range(blocks):
        tail = layout.gather(place_refs, index, slice(TAIL, PLACE_ROWS))
        slots = tail[SLOT : SLOT + 1]
        slot_ref[index : index + 1, :] = slots
        infos.append(layout.info(place_refs, small_ref, index))
        info_ref[index] = infos[-1]
        low_part, high_part = parts_of(slots)
        low_by_column(low_hot.at[index], low_part.astype(f32))
        points = layout.gather(place_refs, index, slice(0, TAIL))
        high, low = two(points)
        nh, nm, nl = three(tail[NORM : NORM + 1])
        sub = iota((16, rows), 0)
        norms = jnp.where((sub == 3) | (sub == 8), nh, jnp.where((sub == 4) | (sub == 9), nm, nl))
        is_norm = ((sub >= 3) & (sub < 6)) | ((sub >= 8) & (sub < 11))
        is_one = (sub < 3) | ((sub >= 11) & (sub < 14))
        extra = jnp.where(is_norm, norms, jnp.where(is_one, 1.0, 0.0))
        for h in range(high_parts):
            here = high_part == h
            at = h * COORD
            masked[index, at : at + 64, :] = jnp.where(here, high.astype(f32), 0.0).astype(bf16)
            masked[index, at + 64 : at + 128, :] = jnp.where(here, low.astype(f32), 0.0).astype(bf16)
            masked[index, at + 128 : at + COORD, :] = jnp.where(here, extra, 0.0).astype(bf16)
    copies = []
    for index in range(blocks):
        placed = nn(masked[index], low_hot[index])
        for h in range(high_parts):
            part = placed[h * COORD : (h + 1) * COORD]
            at = slice(index * rows + h * LOW, index * rows + (h + 1) * LOW)
            tree_ref[:, at] = part.astype(bf16)
            a_ref[at, 0:128], a_ref[at, 128:256] = feature_rows(part[0:64], part[64:128], part[136:144])
        mine = slice(index * rows, (index + 1) * rows)
        copies.append(pltpu.make_async_copy(a_ref.at[mine], a_hbm.at[mine], sems.at[0, index]))
        copies[-1].start()
    for index in range(blocks):
        mine = slice(index * rows, (index + 1) * rows)
        picked = onehot(iota((rows, SK), 0) == infos[index][BASE : BASE + 1].astype(jnp.int32))
        keep(index, nn(tree_ref[:, mine], picked))
    for index in range(blocks):
        mine = slice(index * rows, (index + 1) * rows)
        base_ref[index] = jnp.exp(nn(a_ref[mine, :], sk_bt[:, index * SK : (index + 1) * SK])).astype(bf16)
        copies.append(pltpu.make_async_copy(base_ref.at[index], base_hbm.at[index], sems.at[1, index]))
        copies[-1].start()
    start, count, offset, total = 0, blocks, 0, blocks * trees
    while count > 1:
        nodes = count // 2
        for j in range(nodes):
            pair = slice((start + 2 * j) * SK, (start + 2 * j + 2) * SK)
            row = offset + lax.axis_index("leaf") * nodes + j
            picked = onehot(iota((2 * SK, SK), 0) == upper_ref[pl.ds(row, 1), :])
            here = start + count + j
            keep(here, nn(sk_t[:, pair], picked))
            upper_tiles_ref[here - blocks] = jnp.exp(nn(sk_ref[pair, :], sk_bt[:, here * SK : (here + 1) * SK]))
        total = total // 2
        offset = offset + total
        start, count = start + count, nodes
    found = sk_t[:, start * SK : (start + 1) * SK].astype(f32)
    top_ref[0:64, :] = found[0:64] + found[64:128]
    top_ref[64:72, :] = found[128:136]
    list_tiles(count_ref, list_ref, tiles, times)
    for copy in copies:
        copy.wait()


def weights_kernel(layout, base_hbm, upper_tiles_ref, top_ref, slot_ref, *refs):
    light_refs, refs = refs[: layout.count], refs[layout.count :]
    if layout.fine:
        order = far_first(layout.blocks)
        order = order + [layout.blocks + step for step in order]
        light_refs = [light_refs[order.index(g)] for g in range(layout.count)]
    w_ref, coef_ref, pack_ref, masked, low_hot, base_ref, sems = refs
    blocks, rows = layout.blocks, layout.rows
    width = light_refs[0].shape[0]
    each = width // layout.halves
    pack_ref[0:PLACE_ROWS, :] = top_ref[...]
    for index in range(blocks):
        pltpu.make_async_copy(base_hbm.at[index], base_ref.at[index], sems.at[index]).start()

    def keep(node, coef):
        coef_ref[:, node * SK : (node + 1) * SK] = stack_two(coef)
        pack_ref[PLACE_ROWS:, :] = coef

    for index in range(blocks):
        low_part, high_part = parts_of(slot_ref[index : index + 1, :])
        low_by_column(low_hot.at[index], low_part.astype(f32))
        for half in range(layout.halves):
            light = [ref[layout.columns(g, half, each), layout.lanes(index)] for g, ref in enumerate(light_refs)]
            light = lanes_of(light)
            for h in range(rows // LOW):
                at = h * width + half * each
                masked[index, at : at + each, :] = jnp.where(high_part == h, light, 0.0).astype(bf16)
    for index in range(blocks):
        placed = nn(masked[index], low_hot[index])
        for h in range(rows // LOW):
            at = index * rows + h * LOW
            w_ref[:, at : at + LOW] = placed[h * width : (h + 1) * width].astype(bf16)
    for index in range(blocks):
        pltpu.make_async_copy(base_hbm.at[index], base_ref.at[index], sems.at[index]).wait()
        keep(index, nn(w_ref[:, index * rows : (index + 1) * rows], base_ref[index]))
    start, count = 0, blocks
    while count > 1:
        for j in range(count // 2):
            pair = slice((start + 2 * j) * SK, (start + 2 * j + 2) * SK)
            here = start + count + j
            high, low = two(upper_tiles_ref[here - blocks])
            coef = nn(coef_ref[:, pair], high)
            keep(here, coef[:width] + coef[width:] + nn(coef_ref[0:width, pair], low))
        start, count = start + count, count // 2


def near_kernel(layout, tiles, a_hbm, tree_ref, w_ref, acc, a_ref, bt_ref, sem, even, odd, even_tile, odd_tile):
    span = layout.span
    copy = pltpu.make_async_copy(a_hbm, a_ref, sem)
    copy.start()
    filled = tiles[0, tiles.shape[1] - 1]
    acc[...] = jnp.zeros_like(acc)
    target_columns(layout, bt_ref, tree_ref)

    def exponents(unit, out):
        for k in range(2):
            out[k] = tile_exponents(layout, tiles, 2 * unit + k, a_ref, bt_ref)

    def add(tile, block):
        source = aligned(tiles[1, tile] * LEAF, LEAF, LEAF)
        target = aligned(tiles[0, tile] * span, span, span)
        acc[:, target] += tiles[2, tile].astype(f32) * nn(w_ref[:, source], block)

    copy.wait()
    exponents(0, even)
    for k in range(2):
        even_tile[k] = jnp.exp(even[k]).astype(bf16)
    exponents(1, odd)

    def phase(unit, upcoming, ready, finished, previous):
        for k in range(2):
            upcoming[k] = tile_exponents(layout, tiles, 2 * (unit + 1) + k, a_ref, bt_ref)
            finished[k] = jnp.exp(ready[k]).astype(bf16)
            add(2 * (unit - 1) + k, previous[k])

    def step(pair, carry):
        phase(2 * pair + 1, even, odd, odd_tile, even_tile)
        phase(2 * pair + 2, odd, even, even_tile, odd_tile)
        return carry

    units = (filled + 1) // 2
    pairs = (units - 1) // 2
    lax.fori_loop(0, pairs, step, 0)
    for k in range(2):
        add(4 * pairs + k, even_tile[k])

    @pl.when(2 * pairs + 1 < units)
    def _():
        for k in range(2):
            odd_tile[k] = jnp.exp(odd[k]).astype(bf16)
            add(4 * pairs + 2 + k, odd_tile[k])


def far_kernel(layout, low_levels, pack_ref, slot_ref, info_ref, tree_ref, sk_ref, coef_ref, near_ref, *refs):
    out_refs, refs = refs[: layout.halves], refs[layout.halves :]
    tops, coefs, scaled, low_hot, bt_ref, sums, masked = refs[:7]
    powers, tiles = refs[7:9], refs[9:11]
    blocks, rows = layout.blocks, layout.rows
    ups, width = pack_ref.shape[0], near_ref.shape[0]
    levels = low_levels + ups
    span, core = layout.span, layout.core()
    per_block = rows // LEAF
    lane = iota((1, SK), 1)
    for up in range(ups):
        pack = pack_ref[up]
        high, low = two(pack[0:64])
        sub = iota((8, SK), 0)
        extra = jnp.where(sub == 0, pack[67:68], jnp.where(sub == 1, pack[68:69], pack[69:70]))
        extra = jnp.where(sub < 3, extra, jnp.where(sub < 6, 1.0, 0.0))
        at = slice((low_levels + up) * SK, (low_levels + up + 1) * SK)
        rows_of = feature_rows(high.astype(f32), low.astype(f32), extra)
        coef = stack_two(pack[PLACE_ROWS:])
        for index in range(blocks):
            tops[index, at, 0:128], tops[index, at, 128:256] = rows_of
            coefs[index, :, at] = coef
    for index in range(blocks):
        node, start, count = index, 0, blocks
        for level in range(low_levels):
            at = slice(level * SK, (level + 1) * SK)
            other = slice((start + (node ^ 1)) * SK, (start + (node ^ 1) + 1) * SK)
            tops[index, at, :] = sk_ref[other, :]
            coefs[index, :, at] = coef_ref[:, other]
            node, start, count = node // 2, start + count, count // 2
        for leaf in range(per_block):
            flags = info_ref[index, FLAGS + leaf : FLAGS + leaf + 1, :]
            used = []
            for level in range(levels):
                flag = jnp.sum(jnp.where(lane == level, flags, 0.0), axis=1, keepdims=True)
                used.append(jnp.broadcast_to(flag, (1, SK)))
            used = jnp.concatenate(used, 1)
            scaled[index * per_block + leaf] = (coefs[index].astype(f32) * used).astype(bf16)

    target_columns(layout, bt_ref, tree_ref)

    def exponents(leaf):
        powers[leaf % 2][...] = nn(tops[leaf // per_block], bt_ref[:, leaf * span : (leaf + 1) * span])

    def product(leaf):
        here = slice(leaf * span, (leaf + 1) * span)
        far = nn(scaled[leaf], tiles[leaf % 2][...])
        sums[:, here] = near_ref[:, here] + far[:width] + far[width:]

    leaves = blocks * per_block
    exponents(0)
    for leaf in range(leaves):
        if leaf + 1 < leaves:
            exponents(leaf + 1)
        tiles[leaf % 2][...] = jnp.exp(powers[leaf % 2][...]).astype(bf16)
        if leaf:
            product(leaf - 1)
    product(leaves - 1)

    high_parts = []
    pieces = rows // LOW // layout.halves
    for index in range(blocks):
        low_part, high_part = parts_of(slot_ref[index : index + 1, :])
        high_parts.append(high_part)
        for c in range(rows // LANES):
            at = slice(c * LANES, (c + 1) * LANES)
            low_hot[index, :, at] = onehot(iota((LOW, LANES), 0) == low_part[:, at])
        for k in range(pieces):
            at = (index * pieces + k) * LOW
            masked[index, k * 2 * width : (k + 1) * 2 * width, :] = stack_two(sums[:, at : at + LOW])
    for index in range(blocks):
        moved = nn(masked[index], low_hot[index])
        result = jnp.zeros((2 * width, rows), f32)
        for k in range(pieces):
            here = high_parts[index] == k * layout.halves + core
            result = jnp.where(here, moved[k * 2 * width : (k + 1) * 2 * width], result)
        result = result[:width] + result[width:]
        if not layout.fine:
            out_refs[0][0, :, layout.lanes(index)] = result
            continue
        for g in range(layout.count):
            out_ref = out_refs[g // blocks]
            out_ref[g % blocks, :, layout.lanes(index)] = result[:, g * layout.per : (g + 1) * layout.per]


def add_kernel(kept_ref, got_ref, *out_refs):
    half = kept_ref.shape[1] // 2
    for step, out_ref in enumerate(out_refs):
        out_ref[0:half, :] = kept_ref[step, 0:half, :] + got_ref[step, half:, :]
        out_ref[half:, :] = kept_ref[step, half:, :] + got_ref[step, 0:half, :]


def far_first(blocks):
    return sorted(range(blocks), key=lambda step: -(step * 2 // blocks))


def final_kernel(blocks, pos_ref, *refs):
    back_refs, (weights_ref, out_ref, perm, vals) = refs[:-4], refs[-4:]
    chunks = pos_ref.shape[0]
    rows = chunks * LANES
    width, split = back_refs[0].shape
    width = LANES // blocks if blocks else width
    for r in range(chunks):
        spread(perm, slice(r * LANES, (r + 1) * LANES), column(pos_ref[r : r + 1, :]))
    for g, back_ref in enumerate(back_refs):
        columns, at = 0, slice(0, rows)
        value = back_ref[...]
        if blocks:
            columns = (lax.axis_index("sub") ^ far_first(blocks)[g % blocks]) * width
            at = aligned((lax.axis_index("leaf") ^ lax.axis_index("rep") ^ (g // blocks)) * split, split, split)
            value = value[0:width] if g < blocks else value[width:]
        high, low = two(value)
        vals[aligned(columns, width, width), at] = high
        vals[aligned(columns + LANES, width, width), at] = low
    step = 256
    for s in range(rows // step):
        here = slice(s * step, (s + 1) * step)
        moved = nt(perm[here, :], vals[...])
        out_ref[here, :] = ridge * weights_ref[here, :] + moved[:, :LANES] + moved[:, LANES:]


def upper_levels(pack, skeleton_upper, my_leaf, trees, blocks):
    devices = trees * blocks
    level = blocks.bit_length() - 1
    offset = sum(devices >> step for step in range(1, level + 1))
    line = jnp.arange(pack.shape[0])[:, None]
    is_point, is_norm = line < DIM, (line >= DIM + 3) & (line < DIM + 6)
    is_coef = line >= PLACE_ROWS
    packs, own, stride = [], pack, 1
    while stride < trees:
        other = lax.ppermute(own, "leaf", [(i, i ^ stride) for i in range(trees)])
        packs.append(other)
        stride *= 2
        if stride < trees:
            second = (my_leaf // (stride // 2)) % 2 == 1
            pair = jnp.where(second, jnp.concatenate([other, own], 1), jnp.concatenate([own, other], 1))
            chosen = pair[:, skeleton_upper[offset + my_leaf // stride]]
            level += 1
            offset += devices >> level
            norms = jnp.sum(jnp.where(is_norm, pair, 0.0), axis=0)
            chosen_norms = jnp.sum(jnp.where(is_norm, chosen, 0.0), axis=0)
            inner = jnp.dot(
                jnp.where(is_point, pair, 0.0).T, jnp.where(is_point, chosen, 0.0), precision=highest
            )
            tile = jnp.exp(inner + norms[:, None] + chosen_norms[None])
            own = jnp.where(is_coef, jnp.dot(pair, tile, precision=highest), chosen)
    return jnp.stack(packs)


def body(points, weights, tree_slot, near_count, near_list, skeleton_base, skeleton_upper, far_use):
    blocks, trees, reps = lax.axis_size("sub"), lax.axis_size("leaf"), lax.axis_size("rep")
    devices = blocks * trees
    rows, columns = weights.shape
    low_levels = blocks.bit_length() - 1
    ups = trees.bit_length() - 1
    width = columns // blocks
    part = rows // trees
    per = part // blocks
    total = blocks * rows
    leaves = total // LEAF
    my_leaf = lax.axis_index("leaf")
    fine = trees == 2 and reps == 2 and per % LANES == 0
    layout = Layout(blocks, trees, rows, fine)
    split = part if fine else rows
    cols = width * layout.halves

    place, pos = pl.pallas_call(
        functools.partial(place_kernel, fine),
        out_shape=(shaped((PLACE_ROWS, split), f32), shaped((rows // LANES, LANES), f32)),
        in_specs=[spec()] * 4,
        out_specs=(spec(),) * 2,
        scratch_shapes=[vm((split // LOW * COORD, rows), bf16), vm((rows, LOW), bf16)],
        compiler_params=params(),
        name="sort_points",
    )(tree_slot.reshape(rows // LANES, LANES), points.T, skeleton_base, far_use)
    axes = ("leaf", "sub", "rep")

    def swap(value, step, other=0):
        pairs = []
        for leaf in range(trees):
            for sub in range(blocks):
                for core in range(reps):
                    to = ((leaf ^ core ^ other) * blocks + (sub ^ step)) * reps + core
                    pairs.append(((leaf * blocks + sub) * reps + core, to))
        return lax.ppermute(value, axes, pairs)

    def other_core(value):
        return lax.ppermute(value, "rep", [(0, 1), (1, 0)])

    def sorted_light(pos):
        if fine:
            shapes = (shaped((blocks, width, part), f32),) * 2
        else:
            shapes = (shaped((columns, rows), f32),)
        return pl.pallas_call(
            functools.partial(light_kernel, blocks if fine else 0),
            out_shape=shapes,
            in_specs=[spec()] * 2,
            out_specs=(spec(),) * len(shapes),
            scratch_shapes=[
                vm((rows // LOW * LANES, rows), bf16),
                vm((rows, LOW), bf16),
                vm((rows // LOW, LANES, LOW), f32),
            ],
            compiler_params=params(40),
            name="sort_weights",
        )(in_hbm(pos), in_hbm(weights))

    if fine:
        place = {0: swap(place, 0)}
        stride = blocks // 2
        while stride:
            for step in sorted(place):
                place[step | stride] = lax.ppermute(place[step], "sub", [(i, i ^ stride) for i in range(blocks)])
            stride //= 2
        kept, sent = sorted_light(pos)
        place, kept, sent = lax.optimization_barrier((place, kept, sent))
        light = pl.pallas_call(
            join_kernel,
            out_shape=(shaped((cols, part), f32),) * blocks,
            in_specs=[spec()] * 2,
            out_specs=(spec(),) * blocks,
            compiler_params=params(40),
            name="join_cores",
        )(kept, other_core(sent))
        theirs = {step: other_core(one) for step, one in place.items()}
        place = [place[step] for step in range(blocks)] + [theirs[step] for step in range(blocks)]
        light = [swap(light[step], step) for step in far_first(blocks)]
        small = []
    else:
        info = jnp.pad(far_use.astype(f32), ((FLAGS, 5 - far_use.shape[0]), (0, SK - far_use.shape[1])))
        small = [lax.all_gather(info.at[BASE].set(skeleton_base[0].astype(f32)), "sub", axis=0, tiled=False)]
        place = place.reshape(PLACE_ROWS, trees, part).transpose(1, 0, 2)
        place = lax.all_to_all(place, "leaf", split_axis=0, concat_axis=0, tiled=True)
        place = lax.all_gather(place, "sub", axis=0, tiled=False)
        place = place.transpose(1, 0, 2, 3).reshape(devices, PLACE_ROWS, blocks, per)
        place = [place.transpose(1, 2, 0, 3).reshape(PLACE_ROWS, total)]
        light = sorted_light(pos)[0].reshape(columns, trees, part).transpose(1, 0, 2).reshape(devices, width, part)
        light = lax.all_to_all(light, ("leaf", "sub"), split_axis=0, concat_axis=0, tiled=True)
        light = light.reshape(devices, width, blocks, per)
        light = [light.transpose(1, 2, 0, 3).reshape(width, total)]

    nodes = 2 * blocks - 1
    tree, feat_a, base, sk, upper_tiles, top, slots, info, tiles = pl.pallas_call(
        functools.partial(points_kernel, layout, trees),
        out_shape=(
            vm((COORD, total), bf16),
            pltpu.MemorySpace.HBM((total, FEAT), bf16),
            pltpu.MemorySpace.HBM((blocks, rows, SK), bf16),
            vm((nodes * SK, FEAT), bf16),
            vm((blocks - 1, 2 * SK, SK), f32),
            vm((PLACE_ROWS, SK), f32),
            vm((blocks, rows), f32),
            vm((blocks, 8, SK), f32),
            pltpu.MemorySpace.HBM((3, leaves * leaves + 8), jnp.int32),
        ),
        in_specs=[spec(SMEM)] * 2 + [spec()] * (1 + len(small) + layout.count),
        out_specs=(spec(), spec(pl.ANY), spec(pl.ANY)) + (spec(),) * 5 + (spec(SMEM),),
        scratch_shapes=[
            vm((blocks, rows // LOW * COORD, rows), bf16),
            vm((blocks, rows, LOW), bf16),
            vm((total, FEAT), bf16),
            vm((blocks, rows, SK), bf16),
            vm((COORD, nodes * SK), bf16),
            vm((FEAT, nodes * SK), bf16),
            pltpu.SemaphoreType.DMA((2, blocks)),
            pltpu.SMEM((leaves,), jnp.int32),
        ],
        compiler_params=params(40),
        name="tree_points",
    )(in_hbm(near_count), in_hbm(near_list[0]), in_hbm(skeleton_upper), *small, *place)

    if fine:
        light, slots = lax.optimization_barrier((light, slots))
        light = light + [other_core(one) for one in light]
    tree_light, coefs, pack = pl.pallas_call(
        functools.partial(weights_kernel, layout),
        out_shape=(
            vm((cols, total), bf16),
            vm((2 * cols, nodes * SK), bf16),
            shaped((PLACE_ROWS + cols, SK), f32),
        ),
        in_specs=[spec(pl.ANY)] + [spec()] * (3 + layout.count),
        out_specs=(spec(),) * 3,
        scratch_shapes=[
            vm((blocks, rows // LOW * cols, rows), bf16),
            vm((blocks, rows, LOW), bf16),
            vm((blocks, rows, SK), bf16),
            pltpu.SemaphoreType.DMA((blocks,)),
        ],
        compiler_params=params(40),
        name="tree_weights",
    )(in_hbm(base), held(upper_tiles), held(top), held(slots), *light)

    packs = upper_levels(pack, skeleton_upper, my_leaf, trees, blocks)

    near = pl.pallas_call(
        functools.partial(near_kernel, layout),
        out_shape=vm((cols, total // layout.halves), f32),
        in_specs=[spec(SMEM), spec(pl.ANY)] + [spec()] * 2,
        out_specs=spec(),
        scratch_shapes=[
            vm((total, FEAT), bf16),
            vm((FEAT, total // layout.halves), bf16),
            pltpu.SemaphoreType.DMA(()),
        ]
        + [vm((2, LEAF, layout.span), f32)] * 2
        + [vm((2, LEAF, layout.span), bf16)] * 2,
        compiler_params=params(40),
        name="near",
    )(in_hbm(tiles), in_hbm(feat_a), held(tree), held(tree_light))

    levels = low_levels + ups
    back = pl.pallas_call(
        functools.partial(far_kernel, layout, low_levels),
        out_shape=(shaped((layout.count // layout.halves, cols, total // layout.count), f32),) * layout.halves,
        in_specs=[spec()] * 7,
        out_specs=(spec(),) * layout.halves,
        scratch_shapes=[
            vm((blocks, levels * SK, FEAT), bf16),
            vm((blocks, 2 * cols, levels * SK), bf16),
            vm((leaves, 2 * cols, levels * SK), bf16),
            vm((blocks, LOW, rows), bf16),
            vm((FEAT, total // layout.halves), bf16),
            vm((cols, total // layout.halves), f32),
            vm((blocks, rows // LOW // layout.halves * 2 * cols, LOW), bf16),
        ]
        + [vm((levels * SK, layout.span), f32)] * 2
        + [vm((levels * SK, layout.span), bf16)] * 2,
        compiler_params=params(40),
        name="far",
    )(packs, *[held(one) for one in (slots, info, tree, sk, coefs, near)])

    if fine:
        kept, sent = back
        sums = pl.pallas_call(
            add_kernel,
            out_shape=(shaped((cols, part), f32),) * blocks,
            in_specs=[spec()] * 2,
            out_specs=(spec(),) * blocks,
            compiler_params=params(40),
            name="add_cores",
        )(kept, other_core(sent))
        back = [swap(sums[step], step) for step in far_first(blocks)]
        back = back + [other_core(one) for one in back]
    else:
        back = back[0].reshape(cols, blocks, devices, per).transpose(2, 0, 1, 3).reshape(devices, width, part)
        back = lax.all_to_all(back, ("leaf", "sub"), split_axis=0, concat_axis=0, tiled=True)
        back = [back.reshape(trees, columns, part).transpose(1, 0, 2).reshape(columns, rows)]

    return pl.pallas_call(
        functools.partial(final_kernel, blocks if fine else 0),
        out_shape=shaped((rows, columns), f32),
        in_specs=[spec()] * (2 + layout.count),
        out_specs=spec(),
        scratch_shapes=[vm((rows, rows), bf16), vm((2 * LANES, rows), bf16)],
        compiler_params=params(40),
        name="to_input_order",
    )(pos, *back, weights)


def solution(mesh):
    in_specs = (
        P(("groups", "leaf", "sub"), None),
        P(("groups", "leaf", "sub"), "rep"),
        P(("groups", "leaf", "sub")),
        P(("groups", "leaf"), None),
        P(("groups", "leaf"), None, None),
        P(("groups", "leaf", "sub"), None),
        P("groups", None),
        P(("groups", "leaf", "sub"), None),
    )
    out_specs = P(("groups", "leaf", "sub"), "rep")
    return jax.shard_map(body, mesh=mesh, in_specs=in_specs, out_specs=out_specs, check_vma=False)
```

```python
import functools

import jax
import jax.numpy as jnp
from jax import lax
from jax.experimental import pallas as pl
from jax.experimental.pallas import tpu as pltpu
from jax.sharding import PartitionSpec as P

DIM = 64
LEAF = 512
SK = 128
LANES = 128
FEAT = 256
LOW = 256
COORD = 144

highest = lax.Precision.HIGHEST
point_scale = 0.25
ridge = 0.5
PLACE_ROWS = 72
TAIL = 64
SLOT, NORM, BASE, FLAGS = 0, 1, 2, 3
f32 = jnp.float32
bf16 = jnp.bfloat16
VMEM = pltpu.MemorySpace.VMEM
SMEM = pltpu.MemorySpace.SMEM


def spec(space=VMEM):
    return pl.BlockSpec(memory_space=space)


def params(mib=58):
    return pltpu.CompilerParams(vmem_limit_bytes=mib * 1024 * 1024)


def in_hbm(array):
    return pltpu.with_memory_space_constraint(array, pltpu.MemorySpace.HBM)


def held(array):
    return pltpu.with_memory_space_constraint(array, VMEM)


def vm(shape, dtype):
    return pltpu.VMEM(shape, dtype)


def shaped(shape, dtype):
    return jax.ShapeDtypeStruct(shape, dtype)


def nt(left, right):
    return lax.dot_general(left, right, (((1,), (1,)), ((), ())), preferred_element_type=f32)


def nn(left, right):
    return jnp.dot(left, right, preferred_element_type=f32)


def column(row):
    return jnp.transpose(jnp.broadcast_to(row, (LANES, LANES)))


def iota(shape, dim):
    return lax.broadcasted_iota(jnp.int32, shape, dim)


def onehot(mask):
    return jnp.where(mask, 1.0, 0.0).astype(bf16)


def two(value):
    high = value.astype(bf16)
    return high, (value - high.astype(f32)).astype(bf16)


def three(value):
    high = value.astype(bf16).astype(f32)
    mid = (value - high).astype(bf16).astype(f32)
    return high, mid, (value - high - mid).astype(bf16).astype(f32)


def lanes_of(blocks):
    return blocks[0] if len(blocks) == 1 else jnp.concatenate(blocks, 1)


def aligned(start, size, unit):
    return pl.ds(pl.multiple_of(start, unit), size)


def stack_two(value):
    high, low = two(value)
    return jnp.concatenate([high, low], 0)


def spread(perm, here, rank):
    lane = iota((LANES, LANES), 1).astype(f32)
    for c in range(perm.shape[1] // LANES):
        perm[here, c * LANES : (c + 1) * LANES] = onehot(lane + float(c * LANES) == rank)


def place_kernel(fine, slot_ref, points_ref, base_ref, flag_ref, place_ref, pos_ref, masked, low_hot):
    chunks = slot_ref.shape[0]
    slots = slot_ref[...]
    slot = slots.astype(f32)
    within = slots & (chunks * LANES - 1)
    high, low = (within >> 5).astype(f32), (within & 31).astype(f32)
    ranks = []
    for r in range(chunks):
        here = slice(r * LANES, (r + 1) * LANES)
        mine = column(slot[r : r + 1])
        before = jnp.zeros((LANES, LANES), f32)
        for c in range(chunks):
            before += jnp.where(slot[c : c + 1] < mine, 1.0, 0.0)
        rank = jnp.broadcast_to(jnp.sum(before, axis=1, keepdims=True), (LANES, LANES))
        ranks.append(jnp.transpose(rank)[0:1])
        pos_ref[r : r + 1, :] = ranks[-1]
        spread(low_hot, here, (rank.astype(jnp.int32) & (LOW - 1)).astype(f32))
    scaled = points_ref[...] * point_scale
    ph, plo = two(scaled)
    nh, nm, nl = three(-0.5 * jnp.sum(scaled * scaled, axis=0, keepdims=True))
    high, low = lanes_of([high[c : c + 1] for c in range(chunks)]), lanes_of([low[c : c + 1] for c in range(chunks)])
    sub = iota((16, chunks * LANES), 0)
    extra = jnp.where(sub == 0, high, jnp.where(sub == 1, low, 0.0))
    extra = jnp.where(sub == 2, nh, jnp.where(sub == 3, nm, jnp.where(sub == 4, nl, extra)))
    high_part = lanes_of(ranks).astype(jnp.int32) // LOW
    parts = place_ref.shape[1] // LOW
    first = (lax.axis_index("leaf") ^ lax.axis_index("rep")) * parts if fine else 0
    for h in range(parts):
        here = high_part == first + h
        masked[h * COORD : h * COORD + 64, :] = jnp.where(here, ph.astype(f32), 0.0).astype(bf16)
        masked[h * COORD + 64 : h * COORD + 128, :] = jnp.where(here, plo.astype(f32), 0.0).astype(bf16)
        masked[h * COORD + 128 : (h + 1) * COORD, :] = jnp.where(here, extra, 0.0).astype(bf16)
    placed = nn(masked[...], low_hot[...])
    tail = iota((PLACE_ROWS - TAIL, LOW), 0)
    for h in range(parts):
        at = slice(h * LOW, (h + 1) * LOW)
        moved = placed[h * COORD : (h + 1) * COORD]
        place_ref[0:TAIL, at] = moved[0:64] + moved[64:128]
        slot_row = moved[128:129] * 32.0 + moved[129:130]
        norm_row = moved[130:131] + moved[131:132] + moved[132:133]
        place_ref[TAIL:, at] = jnp.where(tail == SLOT, slot_row, jnp.where(tail == NORM, norm_row, 0.0))
    if fine:
        place_ref[TAIL + BASE : TAIL + BASE + 1, 0:SK] = base_ref[...].astype(f32)
        place_ref[TAIL + FLAGS : TAIL + FLAGS + flag_ref.shape[0], 0 : flag_ref.shape[1]] = flag_ref[...].astype(f32)


def light_kernel(blocks, pos_ref, weights_ref, *refs):
    light_refs, (masked, low_hot, placed) = refs[:-3], refs[-3:]
    chunks = pos_ref.shape[0]
    high_count = chunks * LANES // LOW
    low_part, high_part = parts_of(lanes_of([pos_ref[c : c + 1, :] for c in range(chunks)]))
    low_by_column(low_hot, low_part.astype(f32))
    for c in range(chunks):
        at = slice(c * LANES, (c + 1) * LANES)
        turned = jnp.transpose(weights_ref[at, :])
        for h in range(high_count):
            masked[h * LANES : (h + 1) * LANES, at] = jnp.where(high_part[:, at] == h, turned, 0.0).astype(bf16)
    moved = nn(masked[...], low_hot[...])
    for h in range(high_count):
        if not blocks:
            light_refs[0][:, h * LOW : (h + 1) * LOW] = moved[h * LANES : (h + 1) * LANES]
        placed[h] = moved[h * LANES : (h + 1) * LANES]
    if not blocks:
        return
    width, parts = LANES // blocks, high_count // 2
    for other, light_ref in enumerate(light_refs):
        first = (lax.axis_index("leaf") ^ lax.axis_index("rep") ^ other) * parts
        for step in range(blocks):
            columns = aligned((lax.axis_index("sub") ^ step) * width, width, width)
            for h in range(parts):
                light_ref[step, :, h * LOW : (h + 1) * LOW] = placed[first + h, columns, :]


def join_kernel(kept_ref, got_ref, *out_refs):
    half = kept_ref.shape[1]
    for step, out_ref in enumerate(out_refs):
        out_ref[0:half, :] = kept_ref[step]
        out_ref[half:, :] = got_ref[step]


class Layout:
    def __init__(self, blocks, trees, rows, fine):
        self.blocks, self.rows, self.fine = blocks, rows, fine
        self.count = blocks * trees if fine else 1
        self.per = rows // self.count
        self.halves = 2 if fine else 1
        self.span = LEAF // self.halves

    def core(self):
        return lax.axis_index("rep") if self.fine else 0

    def lanes(self, index):
        return slice(index * self.per, (index + 1) * self.per)

    def columns(self, group, half, each):
        if self.fine and group >= self.blocks:
            half = 1 - half
        return slice(half * each, (half + 1) * each)

    def gather(self, refs, index, part):
        return lanes_of([ref[part, self.lanes(index)] for ref in refs])

    def info(self, refs, small_ref, index):
        if not self.fine:
            return small_ref[index]
        core = lax.axis_index("rep")
        found = jnp.zeros((PLACE_ROWS - TAIL, SK), f32)
        for step in range(self.blocks):
            mine, theirs = refs[step][TAIL:, 0:SK], refs[self.blocks + step][TAIL:, 0:SK]
            here = jnp.where(core == 0, mine, theirs)
            found = jnp.where((lax.axis_index("sub") ^ step) == index, here, found)
        return found


def low_by_column(out, low):
    for c in range(out.shape[0] // LANES):
        at = slice(c * LANES, (c + 1) * LANES)
        spread(out, at, column(low[:, at]))


def parts_of(slots):
    slots = slots.astype(jnp.int32)
    return slots & (LOW - 1), slots // LOW


def feature_columns(out, at, tree):
    out[0:64, at] = tree[0:64].astype(bf16)
    out[64:128, at] = tree[0:64].astype(bf16)
    out[128:192, at] = tree[64:128].astype(bf16)
    out[192:208, at] = jnp.where(iota((16, tree.shape[1]), 0) < 8, tree[128:144].astype(f32), 0.0).astype(bf16)
    out[208:256, at] = jnp.zeros((48, tree.shape[1]), bf16)


def feature_rows(high, low, extra):
    first = jnp.transpose(jnp.concatenate([high, low], 0))
    second = jnp.transpose(jnp.concatenate([high, extra, jnp.zeros((56, high.shape[1]), f32)], 0))
    return first.astype(bf16), second.astype(bf16)


def target_columns(layout, out, tree_ref):
    span = layout.span
    for leaf in range(out.shape[1] // span):
        here = aligned(leaf * LEAF + layout.core() * span, span, span)
        feature_columns(out, slice(leaf * span, (leaf + 1) * span), tree_ref[:, here])


def tile_exponents(layout, tiles, tile, a_ref, bt_ref):
    source = aligned(tiles[1, tile] * LEAF, LEAF, LEAF)
    target = aligned(tiles[0, tile] * layout.span, layout.span, layout.span)
    return nn(a_ref[source, :], bt_ref[:, target])


def list_tiles(count_ref, list_ref, tiles, times):
    every = count_ref.shape[1]

    def tally(leaf, filled):
        for other in range(every):
            times[other] = (leaf == other).astype(jnp.int32)

        def add(slot, carry):
            at = list_ref[leaf, slot]
            times[at] = times[at] + 1
            return carry

        lax.fori_loop(0, count_ref[0, leaf], add, 0)
        for other in range(every):
            tiles[0, filled] = leaf
            tiles[1, filled] = other
            tiles[2, filled] = times[other]
            filled = filled + (times[other] > 0).astype(jnp.int32)
        return filled

    filled = lax.fori_loop(0, every, tally, jnp.int32(0))

    def pad(more, carry):
        tiles[0, more] = 0
        tiles[1, more] = 0
        tiles[2, more] = 0
        return carry

    lax.fori_loop(filled, tiles.shape[1] - 1, pad, 0)
    tiles[0, tiles.shape[1] - 1] = filled


def points_kernel(layout, trees, count_ref, list_ref, upper_ref, *refs):
    if not layout.fine:
        small_ref, refs = refs[0], refs[1:]
    else:
        small_ref = None
    place_refs, refs = refs[: layout.count], refs[layout.count :]
    tree_ref, a_hbm, base_hbm, sk_ref, upper_tiles_ref, top_ref, slot_ref, info_ref, tiles = refs[:9]
    masked, low_hot, a_ref, base_ref, sk_t, sk_bt, sems, times = refs[9:]
    blocks, rows = layout.blocks, layout.rows

    def keep(node, found):
        at = slice(node * SK, (node + 1) * SK)
        sk_t[:, at] = found.astype(bf16)
        sk_ref[at, 0:128], sk_ref[at, 128:256] = feature_rows(found[0:64], found[64:128], found[136:144])
        feature_columns(sk_bt, at, found)

    high_parts = rows // LOW
    infos = []
    for index in range(blocks):
        tail = layout.gather(place_refs, index, slice(TAIL, PLACE_ROWS))
        slots = tail[SLOT : SLOT + 1]
        slot_ref[index : index + 1, :] = slots
        infos.append(layout.info(place_refs, small_ref, index))
        info_ref[index] = infos[-1]
        low_part, high_part = parts_of(slots)
        low_by_column(low_hot.at[index], low_part.astype(f32))
        points = layout.gather(place_refs, index, slice(0, TAIL))
        high, low = two(points)
        nh, nm, nl = three(tail[NORM : NORM + 1])
        sub = iota((16, rows), 0)
        norms = jnp.where((sub == 3) | (sub == 8), nh, jnp.where((sub == 4) | (sub == 9), nm, nl))
        is_norm = ((sub >= 3) & (sub < 6)) | ((sub >= 8) & (sub < 11))
        is_one = (sub < 3) | ((sub >= 11) & (sub < 14))
        extra = jnp.where(is_norm, norms, jnp.where(is_one, 1.0, 0.0))
        for h in range(high_parts):
            here = high_part == h
            at = h * COORD
            masked[index, at : at + 64, :] = jnp.where(here, high.astype(f32), 0.0).astype(bf16)
            masked[index, at + 64 : at + 128, :] = jnp.where(here, low.astype(f32), 0.0).astype(bf16)
            masked[index, at + 128 : at + COORD, :] = jnp.where(here, extra, 0.0).astype(bf16)
    copies = []
    for index in range(blocks):
        placed = nn(masked[index], low_hot[index])
        for h in range(high_parts):
            part = placed[h * COORD : (h + 1) * COORD]
            at = slice(index * rows + h * LOW, index * rows + (h + 1) * LOW)
            tree_ref[:, at] = part.astype(bf16)
            a_ref[at, 0:128], a_ref[at, 128:256] = feature_rows(part[0:64], part[64:128], part[136:144])
        mine = slice(index * rows, (index + 1) * rows)
        copies.append(pltpu.make_async_copy(a_ref.at[mine], a_hbm.at[mine], sems.at[0, index]))
        copies[-1].start()
    for index in range(blocks):
        mine = slice(index * rows, (index + 1) * rows)
        picked = onehot(iota((rows, SK), 0) == infos[index][BASE : BASE + 1].astype(jnp.int32))
        keep(index, nn(tree_ref[:, mine], picked))
    for index in range(blocks):
        mine = slice(index * rows, (index + 1) * rows)
        base_ref[index] = jnp.exp(nn(a_ref[mine, :], sk_bt[:, index * SK : (index + 1) * SK])).astype(bf16)
        copies.append(pltpu.make_async_copy(base_ref.at[index], base_hbm.at[index], sems.at[1, index]))
        copies[-1].start()
    start, count, offset, total = 0, blocks, 0, blocks * trees
    while count > 1:
        nodes = count // 2
        for j in range(nodes):
            pair = slice((start + 2 * j) * SK, (start + 2 * j + 2) * SK)
            row = offset + lax.axis_index("leaf") * nodes + j
            picked = onehot(iota((2 * SK, SK), 0) == upper_ref[pl.ds(row, 1), :])
            here = start + count + j
            keep(here, nn(sk_t[:, pair], picked))
            upper_tiles_ref[here - blocks] = jnp.exp(nn(sk_ref[pair, :], sk_bt[:, here * SK : (here + 1) * SK]))
        total = total // 2
        offset = offset + total
        start, count = start + count, nodes
    found = sk_t[:, start * SK : (start + 1) * SK].astype(f32)
    top_ref[0:64, :] = found[0:64] + found[64:128]
    top_ref[64:72, :] = found[128:136]
    list_tiles(count_ref, list_ref, tiles, times)
    for copy in copies:
        copy.wait()


def weights_kernel(layout, base_hbm, upper_tiles_ref, top_ref, slot_ref, *refs):
    light_refs, refs = refs[: layout.count], refs[layout.count :]
    if layout.fine:
        order = far_first(layout.blocks)
        order = order + [layout.blocks + step for step in order]
        light_refs = [light_refs[order.index(g)] for g in range(layout.count)]
    w_ref, coef_ref, pack_ref, masked, low_hot, base_ref, sems = refs
    blocks, rows = layout.blocks, layout.rows
    width = light_refs[0].shape[0]
    each = width // layout.halves
    pack_ref[0:PLACE_ROWS, :] = top_ref[...]
    for index in range(blocks):
        pltpu.make_async_copy(base_hbm.at[index], base_ref.at[index], sems.at[index]).start()

    def keep(node, coef):
        coef_ref[:, node * SK : (node + 1) * SK] = stack_two(coef)
        pack_ref[PLACE_ROWS:, :] = coef

    for index in range(blocks):
        low_part, high_part = parts_of(slot_ref[index : index + 1, :])
        low_by_column(low_hot.at[index], low_part.astype(f32))
        for half in range(layout.halves):
            light = [ref[layout.columns(g, half, each), layout.lanes(index)] for g, ref in enumerate(light_refs)]
            light = lanes_of(light)
            for h in range(rows // LOW):
                at = h * width + half * each
                masked[index, at : at + each, :] = jnp.where(high_part == h, light, 0.0).astype(bf16)
    for index in range(blocks):
        placed = nn(masked[index], low_hot[index])
        for h in range(rows // LOW):
            at = index * rows + h * LOW
            w_ref[:, at : at + LOW] = placed[h * width : (h + 1) * width].astype(bf16)
    for index in range(blocks):
        pltpu.make_async_copy(base_hbm.at[index], base_ref.at[index], sems.at[index]).wait()
        keep(index, nn(w_ref[:, index * rows : (index + 1) * rows], base_ref[index]))
    start, count = 0, blocks
    while count > 1:
        for j in range(count // 2):
            pair = slice((start + 2 * j) * SK, (start + 2 * j + 2) * SK)
            here = start + count + j
            high, low = two(upper_tiles_ref[here - blocks])
            coef = nn(coef_ref[:, pair], high)
            keep(here, coef[:width] + coef[width:] + nn(coef_ref[0:width, pair], low))
        start, count = start + count, count // 2


def near_kernel(layout, tiles, a_hbm, tree_ref, w_ref, acc, a_ref, bt_ref, sem, even, odd, even_tile, odd_tile):
    span = layout.span
    copy = pltpu.make_async_copy(a_hbm, a_ref, sem)
    copy.start()
    filled = tiles[0, tiles.shape[1] - 1]
    acc[...] = jnp.zeros_like(acc)
    target_columns(layout, bt_ref, tree_ref)

    def exponents(unit, out):
        for k in range(2):
            out[k] = tile_exponents(layout, tiles, 2 * unit + k, a_ref, bt_ref)

    def add(tile, block):
        source = aligned(tiles[1, tile] * LEAF, LEAF, LEAF)
        target = aligned(tiles[0, tile] * span, span, span)
        acc[:, target] += tiles[2, tile].astype(f32) * nn(w_ref[:, source], block)

    copy.wait()
    exponents(0, even)
    for k in range(2):
        even_tile[k] = jnp.exp(even[k]).astype(bf16)
    exponents(1, odd)

    def phase(unit, upcoming, ready, finished, previous):
        for k in range(2):
            upcoming[k] = tile_exponents(layout, tiles, 2 * (unit + 1) + k, a_ref, bt_ref)
            finished[k] = jnp.exp(ready[k]).astype(bf16)
            add(2 * (unit - 1) + k, previous[k])

    def step(pair, carry):
        phase(2 * pair + 1, even, odd, odd_tile, even_tile)
        phase(2 * pair + 2, odd, even, even_tile, odd_tile)
        return carry

    units = (filled + 1) // 2
    pairs = (units - 1) // 2
    lax.fori_loop(0, pairs, step, 0)
    for k in range(2):
        add(4 * pairs + k, even_tile[k])

    @pl.when(2 * pairs + 1 < units)
    def _():
        for k in range(2):
            odd_tile[k] = jnp.exp(odd[k]).astype(bf16)
            add(4 * pairs + 2 + k, odd_tile[k])


def far_kernel(layout, low_levels, pack_ref, slot_ref, info_ref, tree_ref, sk_ref, coef_ref, near_ref, *refs):
    out_refs, refs = refs[: layout.halves], refs[layout.halves :]
    tops, coefs, scaled, low_hot, bt_ref, sums, masked = refs[:7]
    powers, tiles = refs[7:9], refs[9:11]
    blocks, rows = layout.blocks, layout.rows
    ups, width = pack_ref.shape[0], near_ref.shape[0]
    levels = low_levels + ups
    span, core = layout.span, layout.core()
    per_block = rows // LEAF
    lane = iota((1, SK), 1)
    for up in range(ups):
        pack = pack_ref[up]
        high, low = two(pack[0:64])
        sub = iota((8, SK), 0)
        extra = jnp.where(sub == 0, pack[67:68], jnp.where(sub == 1, pack[68:69], pack[69:70]))
        extra = jnp.where(sub < 3, extra, jnp.where(sub < 6, 1.0, 0.0))
        at = slice((low_levels + up) * SK, (low_levels + up + 1) * SK)
        rows_of = feature_rows(high.astype(f32), low.astype(f32), extra)
        coef = stack_two(pack[PLACE_ROWS:])
        for index in range(blocks):
            tops[index, at, 0:128], tops[index, at, 128:256] = rows_of
            coefs[index, :, at] = coef
    for index in range(blocks):
        node, start, count = index, 0, blocks
        for level in range(low_levels):
            at = slice(level * SK, (level + 1) * SK)
            other = slice((start + (node ^ 1)) * SK, (start + (node ^ 1) + 1) * SK)
            tops[index, at, :] = sk_ref[other, :]
            coefs[index, :, at] = coef_ref[:, other]
            node, start, count = node // 2, start + count, count // 2
        for leaf in range(per_block):
            flags = info_ref[index, FLAGS + leaf : FLAGS + leaf + 1, :]
            used = []
            for level in range(levels):
                flag = jnp.sum(jnp.where(lane == level, flags, 0.0), axis=1, keepdims=True)
                used.append(jnp.broadcast_to(flag, (1, SK)))
            used = jnp.concatenate(used, 1)
            scaled[index * per_block + leaf] = (coefs[index].astype(f32) * used).astype(bf16)

    target_columns(layout, bt_ref, tree_ref)

    def exponents(leaf):
        powers[leaf % 2][...] = nn(tops[leaf // per_block], bt_ref[:, leaf * span : (leaf + 1) * span])

    def product(leaf):
        here = slice(leaf * span, (leaf + 1) * span)
        far = nn(scaled[leaf], tiles[leaf % 2][...])
        sums[:, here] = near_ref[:, here] + far[:width] + far[width:]

    leaves = blocks * per_block
    exponents(0)
    for leaf in range(leaves):
        if leaf + 1 < leaves:
            exponents(leaf + 1)
        tiles[leaf % 2][...] = jnp.exp(powers[leaf % 2][...]).astype(bf16)
        if leaf:
            product(leaf - 1)
    product(leaves - 1)

    high_parts = []
    pieces = rows // LOW // layout.halves
    for index in range(blocks):
        low_part, high_part = parts_of(slot_ref[index : index + 1, :])
        high_parts.append(high_part)
        for c in range(rows // LANES):
            at = slice(c * LANES, (c + 1) * LANES)
            low_hot[index, :, at] = onehot(iota((LOW, LANES), 0) == low_part[:, at])
        for k in range(pieces):
            at = (index * pieces + k) * LOW
            masked[index, k * 2 * width : (k + 1) * 2 * width, :] = stack_two(sums[:, at : at + LOW])
    for index in range(blocks):
        moved = nn(masked[index], low_hot[index])
        result = jnp.zeros((2 * width, rows), f32)
        for k in range(pieces):
            here = high_parts[index] == k * layout.halves + core
            result = jnp.where(here, moved[k * 2 * width : (k + 1) * 2 * width], result)
        result = result[:width] + result[width:]
        if not layout.fine:
            out_refs[0][0, :, layout.lanes(index)] = result
            continue
        for g in range(layout.count):
            out_ref = out_refs[g // blocks]
            out_ref[g % blocks, :, layout.lanes(index)] = result[:, g * layout.per : (g + 1) * layout.per]


def add_kernel(kept_ref, got_ref, *out_refs):
    half = kept_ref.shape[1] // 2
    for step, out_ref in enumerate(out_refs):
        out_ref[0:half, :] = kept_ref[step, 0:half, :] + got_ref[step, half:, :]
        out_ref[half:, :] = kept_ref[step, half:, :] + got_ref[step, 0:half, :]


def far_first(blocks):
    return list(reversed(range(blocks)))


def final_kernel(blocks, pos_ref, *refs):
    back_refs, (weights_ref, out_ref, perm, vals) = refs[:-4], refs[-4:]
    chunks = pos_ref.shape[0]
    rows = chunks * LANES
    width, split = back_refs[0].shape
    width = LANES // blocks if blocks else width
    for r in range(chunks):
        spread(perm, slice(r * LANES, (r + 1) * LANES), column(pos_ref[r : r + 1, :]))
    for g, back_ref in enumerate(back_refs):
        columns, at = 0, slice(0, rows)
        value = back_ref[...]
        if blocks:
            columns = (lax.axis_index("sub") ^ far_first(blocks)[g % blocks]) * width
            at = aligned((lax.axis_index("leaf") ^ lax.axis_index("rep") ^ (g // blocks)) * split, split, split)
            value = value[0:width] if g < blocks else value[width:]
        high, low = two(value)
        vals[aligned(columns, width, width), at] = high
        vals[aligned(columns + LANES, width, width), at] = low
    step = 256
    for s in range(rows // step):
        here = slice(s * step, (s + 1) * step)
        moved = nt(perm[here, :], vals[...])
        out_ref[here, :] = ridge * weights_ref[here, :] + moved[:, :LANES] + moved[:, LANES:]


def upper_levels(pack, skeleton_upper, my_leaf, trees, blocks):
    devices = trees * blocks
    level = blocks.bit_length() - 1
    offset = sum(devices >> step for step in range(1, level + 1))
    line = jnp.arange(pack.shape[0])[:, None]
    is_point, is_norm = line < DIM, (line >= DIM + 3) & (line < DIM + 6)
    is_coef = line >= PLACE_ROWS
    packs, own, stride = [], pack, 1
    while stride < trees:
        other = lax.ppermute(own, "leaf", [(i, i ^ stride) for i in range(trees)])
        packs.append(other)
        stride *= 2
        if stride < trees:
            second = (my_leaf // (stride // 2)) % 2 == 1
            pair = jnp.where(second, jnp.concatenate([other, own], 1), jnp.concatenate([own, other], 1))
            chosen = pair[:, skeleton_upper[offset + my_leaf // stride]]
            level += 1
            offset += devices >> level
            norms = jnp.sum(jnp.where(is_norm, pair, 0.0), axis=0)
            chosen_norms = jnp.sum(jnp.where(is_norm, chosen, 0.0), axis=0)
            inner = jnp.dot(
                jnp.where(is_point, pair, 0.0).T, jnp.where(is_point, chosen, 0.0), precision=highest
            )
            tile = jnp.exp(inner + norms[:, None] + chosen_norms[None])
            own = jnp.where(is_coef, jnp.dot(pair, tile, precision=highest), chosen)
    return jnp.stack(packs)


def body(points, weights, tree_slot, near_count, near_list, skeleton_base, skeleton_upper, far_use):
    blocks, trees, reps = lax.axis_size("sub"), lax.axis_size("leaf"), lax.axis_size("rep")
    devices = blocks * trees
    rows, columns = weights.shape
    low_levels = blocks.bit_length() - 1
    ups = trees.bit_length() - 1
    width = columns // blocks
    part = rows // trees
    per = part // blocks
    total = blocks * rows
    leaves = total // LEAF
    my_leaf = lax.axis_index("leaf")
    fine = trees == 2 and reps == 2 and per % LANES == 0
    layout = Layout(blocks, trees, rows, fine)
    split = part if fine else rows
    cols = width * layout.halves

    place, pos = pl.pallas_call(
        functools.partial(place_kernel, fine),
        out_shape=(shaped((PLACE_ROWS, split), f32), shaped((rows // LANES, LANES), f32)),
        in_specs=[spec()] * 4,
        out_specs=(spec(),) * 2,
        scratch_shapes=[vm((split // LOW * COORD, rows), bf16), vm((rows, LOW), bf16)],
        compiler_params=params(),
        name="sort_points",
    )(tree_slot.reshape(rows // LANES, LANES), points.T, skeleton_base, far_use)
    axes = ("leaf", "sub", "rep")

    def swap(value, step, other=0):
        pairs = []
        for leaf in range(trees):
            for sub in range(blocks):
                for core in range(reps):
                    to = ((leaf ^ core ^ other) * blocks + (sub ^ step)) * reps + core
                    pairs.append(((leaf * blocks + sub) * reps + core, to))
        return lax.ppermute(value, axes, pairs)

    def other_core(value):
        return lax.ppermute(value, "rep", [(0, 1), (1, 0)])

    def sorted_light(pos):
        if fine:
            shapes = (shaped((blocks, width, part), f32),) * 2
        else:
            shapes = (shaped((columns, rows), f32),)
        return pl.pallas_call(
            functools.partial(light_kernel, blocks if fine else 0),
            out_shape=shapes,
            in_specs=[spec()] * 2,
            out_specs=(spec(),) * len(shapes),
            scratch_shapes=[
                vm((rows // LOW * LANES, rows), bf16),
                vm((rows, LOW), bf16),
                vm((rows // LOW, LANES, LOW), f32),
            ],
            compiler_params=params(40),
            name="sort_weights",
        )(in_hbm(pos), in_hbm(weights))

    if fine:
        place = {0: swap(place, 0)}
        stride = blocks // 2
        while stride:
            for step in sorted(place):
                place[step | stride] = lax.ppermute(place[step], "sub", [(i, i ^ stride) for i in range(blocks)])
            stride //= 2
        kept, sent = sorted_light(pos)
        place, kept, sent = lax.optimization_barrier((place, kept, sent))
        light = pl.pallas_call(
            join_kernel,
            out_shape=(shaped((cols, part), f32),) * blocks,
            in_specs=[spec()] * 2,
            out_specs=(spec(),) * blocks,
            compiler_params=params(40),
            name="join_cores",
        )(kept, other_core(sent))
        theirs = {step: other_core(one) for step, one in place.items()}
        place = [place[step] for step in range(blocks)] + [theirs[step] for step in range(blocks)]
        light = [swap(light[step], step) for step in far_first(blocks)]
        small = []
    else:
        info = jnp.pad(far_use.astype(f32), ((FLAGS, 5 - far_use.shape[0]), (0, SK - far_use.shape[1])))
        small = [lax.all_gather(info.at[BASE].set(skeleton_base[0].astype(f32)), "sub", axis=0, tiled=False)]
        place = place.reshape(PLACE_ROWS, trees, part).transpose(1, 0, 2)
        place = lax.all_to_all(place, "leaf", split_axis=0, concat_axis=0, tiled=True)
        place = lax.all_gather(place, "sub", axis=0, tiled=False)
        place = place.transpose(1, 0, 2, 3).reshape(devices, PLACE_ROWS, blocks, per)
        place = [place.transpose(1, 2, 0, 3).reshape(PLACE_ROWS, total)]
        light = sorted_light(pos)[0].reshape(columns, trees, part).transpose(1, 0, 2).reshape(devices, width, part)
        light = lax.all_to_all(light, ("leaf", "sub"), split_axis=0, concat_axis=0, tiled=True)
        light = light.reshape(devices, width, blocks, per)
        light = [light.transpose(1, 2, 0, 3).reshape(width, total)]

    nodes = 2 * blocks - 1
    tree, feat_a, base, sk, upper_tiles, top, slots, info, tiles = pl.pallas_call(
        functools.partial(points_kernel, layout, trees),
        out_shape=(
            vm((COORD, total), bf16),
            pltpu.MemorySpace.HBM((total, FEAT), bf16),
            pltpu.MemorySpace.HBM((blocks, rows, SK), bf16),
            vm((nodes * SK, FEAT), bf16),
            vm((blocks - 1, 2 * SK, SK), f32),
            vm((PLACE_ROWS, SK), f32),
            vm((blocks, rows), f32),
            vm((blocks, 8, SK), f32),
            pltpu.MemorySpace.HBM((3, leaves * leaves + 8), jnp.int32),
        ),
        in_specs=[spec(SMEM)] * 2 + [spec()] * (1 + len(small) + layout.count),
        out_specs=(spec(), spec(pl.ANY), spec(pl.ANY)) + (spec(),) * 5 + (spec(SMEM),),
        scratch_shapes=[
            vm((blocks, rows // LOW * COORD, rows), bf16),
            vm((blocks, rows, LOW), bf16),
            vm((total, FEAT), bf16),
            vm((blocks, rows, SK), bf16),
            vm((COORD, nodes * SK), bf16),
            vm((FEAT, nodes * SK), bf16),
            pltpu.SemaphoreType.DMA((2, blocks)),
            pltpu.SMEM((leaves,), jnp.int32),
        ],
        compiler_params=params(40),
        name="tree_points",
    )(in_hbm(near_count), in_hbm(near_list[0]), in_hbm(skeleton_upper), *small, *place)

    if fine:
        light, slots = lax.optimization_barrier((light, slots))
        light = light + [other_core(one) for one in light]
    tree_light, coefs, pack = pl.pallas_call(
        functools.partial(weights_kernel, layout),
        out_shape=(
            vm((cols, total), bf16),
            vm((2 * cols, nodes * SK), bf16),
            shaped((PLACE_ROWS + cols, SK), f32),
        ),
        in_specs=[spec(pl.ANY)] + [spec()] * (3 + layout.count),
        out_specs=(spec(),) * 3,
        scratch_shapes=[
            vm((blocks, rows // LOW * cols, rows), bf16),
            vm((blocks, rows, LOW), bf16),
            vm((blocks, rows, SK), bf16),
            pltpu.SemaphoreType.DMA((blocks,)),
        ],
        compiler_params=params(40),
        name="tree_weights",
    )(in_hbm(base), held(upper_tiles), held(top), held(slots), *light)

    packs = upper_levels(pack, skeleton_upper, my_leaf, trees, blocks)

    near = pl.pallas_call(
        functools.partial(near_kernel, layout),
        out_shape=vm((cols, total // layout.halves), f32),
        in_specs=[spec(SMEM), spec(pl.ANY)] + [spec()] * 2,
        out_specs=spec(),
        scratch_shapes=[
            vm((total, FEAT), bf16),
            vm((FEAT, total // layout.halves), bf16),
            pltpu.SemaphoreType.DMA(()),
        ]
        + [vm((2, LEAF, layout.span), f32)] * 2
        + [vm((2, LEAF, layout.span), bf16)] * 2,
        compiler_params=params(40),
        name="near",
    )(in_hbm(tiles), in_hbm(feat_a), held(tree), held(tree_light))

    levels = low_levels + ups
    back = pl.pallas_call(
        functools.partial(far_kernel, layout, low_levels),
        out_shape=(shaped((layout.count // layout.halves, cols, total // layout.count), f32),) * layout.halves,
        in_specs=[spec()] * 7,
        out_specs=(spec(),) * layout.halves,
        scratch_shapes=[
            vm((blocks, levels * SK, FEAT), bf16),
            vm((blocks, 2 * cols, levels * SK), bf16),
            vm((leaves, 2 * cols, levels * SK), bf16),
            vm((blocks, LOW, rows), bf16),
            vm((FEAT, total // layout.halves), bf16),
            vm((cols, total // layout.halves), f32),
            vm((blocks, rows // LOW // layout.halves * 2 * cols, LOW), bf16),
        ]
        + [vm((levels * SK, layout.span), f32)] * 2
        + [vm((levels * SK, layout.span), bf16)] * 2,
        compiler_params=params(40),
        name="far",
    )(packs, *[held(one) for one in (slots, info, tree, sk, coefs, near)])

    if fine:
        kept, sent = back
        sums = pl.pallas_call(
            add_kernel,
            out_shape=(shaped((cols, part), f32),) * blocks,
            in_specs=[spec()] * 2,
            out_specs=(spec(),) * blocks,
            compiler_params=params(40),
            name="add_cores",
        )(kept, other_core(sent))
        back = [swap(sums[step], step) for step in far_first(blocks)]
        back = back + [other_core(one) for one in back]
    else:
        back = back[0].reshape(cols, blocks, devices, per).transpose(2, 0, 1, 3).reshape(devices, width, part)
        back = lax.all_to_all(back, ("leaf", "sub"), split_axis=0, concat_axis=0, tiled=True)
        back = [back.reshape(trees, columns, part).transpose(1, 0, 2).reshape(columns, rows)]

    return pl.pallas_call(
        functools.partial(final_kernel, blocks if fine else 0),
        out_shape=shaped((rows, columns), f32),
        in_specs=[spec()] * (2 + layout.count),
        out_specs=spec(),
        scratch_shapes=[vm((rows, rows), bf16), vm((2 * LANES, rows), bf16)],
        compiler_params=params(40),
        name="to_input_order",
    )(pos, *back, weights)


def solution(mesh):
    in_specs = (
        P(("groups", "leaf", "sub"), None),
        P(("groups", "leaf", "sub"), "rep"),
        P(("groups", "leaf", "sub")),
        P(("groups", "leaf"), None),
        P(("groups", "leaf"), None, None),
        P(("groups", "leaf", "sub"), None),
        P("groups", None),
        P(("groups", "leaf", "sub"), None),
    )
    out_specs = P(("groups", "leaf", "sub"), "rep")
    return jax.shard_map(body, mesh=mesh, in_specs=in_specs, out_specs=out_specs, check_vma=False)
```

```python
import functools

import jax
import jax.numpy as jnp
from jax import lax
from jax.experimental import pallas as pl
from jax.experimental.pallas import tpu as pltpu
from jax.sharding import PartitionSpec as P

DIM = 64
LEAF = 512
SK = 128
LANES = 128
FEAT = 256
LOW = 256
COORD = 144

highest = lax.Precision.HIGHEST
point_scale = 0.25
ridge = 0.5
PLACE_ROWS = 72
TAIL = 64
SLOT, NORM, BASE, FLAGS = 0, 1, 2, 3
f32 = jnp.float32
bf16 = jnp.bfloat16
VMEM = pltpu.MemorySpace.VMEM
SMEM = pltpu.MemorySpace.SMEM


def spec(space=VMEM):
    return pl.BlockSpec(memory_space=space)


def params(mib=58):
    return pltpu.CompilerParams(vmem_limit_bytes=mib * 1024 * 1024)


def in_hbm(array):
    return pltpu.with_memory_space_constraint(array, pltpu.MemorySpace.HBM)


def held(array):
    return pltpu.with_memory_space_constraint(array, VMEM)


def vm(shape, dtype):
    return pltpu.VMEM(shape, dtype)


def shaped(shape, dtype):
    return jax.ShapeDtypeStruct(shape, dtype)


def nt(left, right):
    return lax.dot_general(left, right, (((1,), (1,)), ((), ())), preferred_element_type=f32)


def nn(left, right):
    return jnp.dot(left, right, preferred_element_type=f32)


def column(row):
    return jnp.transpose(jnp.broadcast_to(row, (LANES, LANES)))


def iota(shape, dim):
    return lax.broadcasted_iota(jnp.int32, shape, dim)


def onehot(mask):
    return jnp.where(mask, 1.0, 0.0).astype(bf16)


def two(value):
    high = value.astype(bf16)
    return high, (value - high.astype(f32)).astype(bf16)


def three(value):
    high = value.astype(bf16).astype(f32)
    mid = (value - high).astype(bf16).astype(f32)
    return high, mid, (value - high - mid).astype(bf16).astype(f32)


def lanes_of(blocks):
    return blocks[0] if len(blocks) == 1 else jnp.concatenate(blocks, 1)


def aligned(start, size, unit):
    return pl.ds(pl.multiple_of(start, unit), size)


def stack_two(value):
    high, low = two(value)
    return jnp.concatenate([high, low], 0)


def spread(perm, here, rank):
    lane = iota((LANES, LANES), 1).astype(f32)
    for c in range(perm.shape[1] // LANES):
        perm[here, c * LANES : (c + 1) * LANES] = onehot(lane + float(c * LANES) == rank)


def place_kernel(fine, slot_ref, points_ref, base_ref, flag_ref, place_ref, pos_ref, masked, low_hot):
    chunks = slot_ref.shape[0]
    slots = slot_ref[...]
    slot = slots.astype(f32)
    within = slots & (chunks * LANES - 1)
    high, low = (within >> 5).astype(f32), (within & 31).astype(f32)
    ranks = []
    for r in range(chunks):
        here = slice(r * LANES, (r + 1) * LANES)
        mine = column(slot[r : r + 1])
        before = jnp.zeros((LANES, LANES), f32)
        for c in range(chunks):
            before += jnp.where(slot[c : c + 1] < mine, 1.0, 0.0)
        rank = jnp.broadcast_to(jnp.sum(before, axis=1, keepdims=True), (LANES, LANES))
        ranks.append(jnp.transpose(rank)[0:1])
        pos_ref[r : r + 1, :] = ranks[-1]
        spread(low_hot, here, (rank.astype(jnp.int32) & (LOW - 1)).astype(f32))
    scaled = points_ref[...] * point_scale
    ph, plo = two(scaled)
    nh, nm, nl = three(-0.5 * jnp.sum(scaled * scaled, axis=0, keepdims=True))
    high, low = lanes_of([high[c : c + 1] for c in range(chunks)]), lanes_of([low[c : c + 1] for c in range(chunks)])
    sub = iota((16, chunks * LANES), 0)
    extra = jnp.where(sub == 0, high, jnp.where(sub == 1, low, 0.0))
    extra = jnp.where(sub == 2, nh, jnp.where(sub == 3, nm, jnp.where(sub == 4, nl, extra)))
    high_part = lanes_of(ranks).astype(jnp.int32) // LOW
    parts = place_ref.shape[1] // LOW
    first = (lax.axis_index("leaf") ^ lax.axis_index("rep")) * parts if fine else 0
    for h in range(parts):
        here = high_part == first + h
        masked[h * COORD : h * COORD + 64, :] = jnp.where(here, ph.astype(f32), 0.0).astype(bf16)
        masked[h * COORD + 64 : h * COORD + 128, :] = jnp.where(here, plo.astype(f32), 0.0).astype(bf16)
        masked[h * COORD + 128 : (h + 1) * COORD, :] = jnp.where(here, extra, 0.0).astype(bf16)
    placed = nn(masked[...], low_hot[...])
    tail = iota((PLACE_ROWS - TAIL, LOW), 0)
    for h in range(parts):
        at = slice(h * LOW, (h + 1) * LOW)
        moved = placed[h * COORD : (h + 1) * COORD]
        place_ref[0:TAIL, at] = moved[0:64] + moved[64:128]
        slot_row = moved[128:129] * 32.0 + moved[129:130]
        norm_row = moved[130:131] + moved[131:132] + moved[132:133]
        place_ref[TAIL:, at] = jnp.where(tail == SLOT, slot_row, jnp.where(tail == NORM, norm_row, 0.0))
    if fine:
        place_ref[TAIL + BASE : TAIL + BASE + 1, 0:SK] = base_ref[...].astype(f32)
        place_ref[TAIL + FLAGS : TAIL + FLAGS + flag_ref.shape[0], 0 : flag_ref.shape[1]] = flag_ref[...].astype(f32)


def light_kernel(blocks, pos_ref, weights_ref, *refs):
    light_refs, (masked, low_hot, placed) = refs[:-3], refs[-3:]
    chunks = pos_ref.shape[0]
    high_count = chunks * LANES // LOW
    low_part, high_part = parts_of(lanes_of([pos_ref[c : c + 1, :] for c in range(chunks)]))
    low_by_column(low_hot, low_part.astype(f32))
    for c in range(chunks):
        at = slice(c * LANES, (c + 1) * LANES)
        turned = jnp.transpose(weights_ref[at, :])
        for h in range(high_count):
            masked[h * LANES : (h + 1) * LANES, at] = jnp.where(high_part[:, at] == h, turned, 0.0).astype(bf16)
    moved = nn(masked[...], low_hot[...])
    for h in range(high_count):
        if not blocks:
            light_refs[0][:, h * LOW : (h + 1) * LOW] = moved[h * LANES : (h + 1) * LANES]
        placed[h] = moved[h * LANES : (h + 1) * LANES]
    if not blocks:
        return
    width, parts = LANES // blocks, high_count // 2
    for other, light_ref in enumerate(light_refs):
        first = (lax.axis_index("leaf") ^ lax.axis_index("rep") ^ other) * parts
        for step in range(blocks):
            columns = aligned((lax.axis_index("sub") ^ step) * width, width, width)
            for h in range(parts):
                light_ref[step, :, h * LOW : (h + 1) * LOW] = placed[first + h, columns, :]


def join_kernel(kept_ref, got_ref, *out_refs):
    half = kept_ref.shape[1]
    for step, out_ref in enumerate(out_refs):
        out_ref[0:half, :] = kept_ref[step]
        out_ref[half:, :] = got_ref[step]


class Layout:
    def __init__(self, blocks, trees, rows, fine):
        self.blocks, self.rows, self.fine = blocks, rows, fine
        self.count = blocks * trees if fine else 1
        self.per = rows // self.count
        self.halves = 2 if fine else 1
        self.span = LEAF // self.halves

    def core(self):
        return lax.axis_index("rep") if self.fine else 0

    def lanes(self, index):
        return slice(index * self.per, (index + 1) * self.per)

    def columns(self, group, half, each):
        if self.fine and group >= self.blocks:
            half = 1 - half
        return slice(half * each, (half + 1) * each)

    def gather(self, refs, index, part):
        return lanes_of([ref[part, self.lanes(index)] for ref in refs])

    def info(self, refs, small_ref, index):
        if not self.fine:
            return small_ref[index]
        core = lax.axis_index("rep")
        found = jnp.zeros((PLACE_ROWS - TAIL, SK), f32)
        for step in range(self.blocks):
            mine, theirs = refs[step][TAIL:, 0:SK], refs[self.blocks + step][TAIL:, 0:SK]
            here = jnp.where(core == 0, mine, theirs)
            found = jnp.where((lax.axis_index("sub") ^ step) == index, here, found)
        return found


def low_by_column(out, low):
    for c in range(out.shape[0] // LANES):
        at = slice(c * LANES, (c + 1) * LANES)
        spread(out, at, column(low[:, at]))


def parts_of(slots):
    slots = slots.astype(jnp.int32)
    return slots & (LOW - 1), slots // LOW


def feature_columns(out, at, tree):
    out[0:64, at] = tree[0:64].astype(bf16)
    out[64:128, at] = tree[0:64].astype(bf16)
    out[128:192, at] = tree[64:128].astype(bf16)
    out[192:208, at] = jnp.where(iota((16, tree.shape[1]), 0) < 8, tree[128:144].astype(f32), 0.0).astype(bf16)
    out[208:256, at] = jnp.zeros((48, tree.shape[1]), bf16)


def feature_rows(high, low, extra):
    first = jnp.transpose(jnp.concatenate([high, low], 0))
    second = jnp.transpose(jnp.concatenate([high, extra, jnp.zeros((56, high.shape[1]), f32)], 0))
    return first.astype(bf16), second.astype(bf16)


def target_columns(layout, out, tree_ref):
    span = layout.span
    for leaf in range(out.shape[1] // span):
        here = aligned(leaf * LEAF + layout.core() * span, span, span)
        feature_columns(out, slice(leaf * span, (leaf + 1) * span), tree_ref[:, here])


def tile_exponents(layout, tiles, tile, a_ref, bt_ref):
    source = aligned(tiles[1, tile] * LEAF, LEAF, LEAF)
    target = aligned(tiles[0, tile] * layout.span, layout.span, layout.span)
    return nn(a_ref[source, :], bt_ref[:, target])


def list_tiles(count_ref, list_ref, tiles, times):
    every = count_ref.shape[1]

    def tally(leaf, filled):
        for other in range(every):
            times[other] = (leaf == other).astype(jnp.int32)

        def add(slot, carry):
            at = list_ref[leaf, slot]
            times[at] = times[at] + 1
            return carry

        lax.fori_loop(0, count_ref[0, leaf], add, 0)
        for other in range(every):
            tiles[0, filled] = leaf
            tiles[1, filled] = other
            tiles[2, filled] = times[other]
            filled = filled + (times[other] > 0).astype(jnp.int32)
        return filled

    filled = lax.fori_loop(0, every, tally, jnp.int32(0))

    def pad(more, carry):
        tiles[0, more] = 0
        tiles[1, more] = 0
        tiles[2, more] = 0
        return carry

    lax.fori_loop(filled, tiles.shape[1] - 1, pad, 0)
    tiles[0, tiles.shape[1] - 1] = filled


def points_kernel(layout, trees, count_ref, list_ref, upper_ref, *refs):
    if not layout.fine:
        small_ref, refs = refs[0], refs[1:]
    else:
        small_ref = None
    place_refs, refs = refs[: layout.count], refs[layout.count :]
    tree_ref, a_hbm, base_hbm, sk_ref, upper_tiles_ref, top_ref, slot_ref, info_ref, tiles = refs[:9]
    masked, low_hot, a_ref, base_ref, sk_t, sk_bt, sems, times = refs[9:]
    blocks, rows = layout.blocks, layout.rows

    def keep(node, found):
        at = slice(node * SK, (node + 1) * SK)
        sk_t[:, at] = found.astype(bf16)
        sk_ref[at, 0:128], sk_ref[at, 128:256] = feature_rows(found[0:64], found[64:128], found[136:144])
        feature_columns(sk_bt, at, found)

    high_parts = rows // LOW
    infos = []
    for index in range(blocks):
        tail = layout.gather(place_refs, index, slice(TAIL, PLACE_ROWS))
        slots = tail[SLOT : SLOT + 1]
        slot_ref[index : index + 1, :] = slots
        infos.append(layout.info(place_refs, small_ref, index))
        info_ref[index] = infos[-1]
        low_part, high_part = parts_of(slots)
        low_by_column(low_hot.at[index], low_part.astype(f32))
        points = layout.gather(place_refs, index, slice(0, TAIL))
        high, low = two(points)
        nh, nm, nl = three(tail[NORM : NORM + 1])
        sub = iota((16, rows), 0)
        norms = jnp.where((sub == 3) | (sub == 8), nh, jnp.where((sub == 4) | (sub == 9), nm, nl))
        is_norm = ((sub >= 3) & (sub < 6)) | ((sub >= 8) & (sub < 11))
        is_one = (sub < 3) | ((sub >= 11) & (sub < 14))
        extra = jnp.where(is_norm, norms, jnp.where(is_one, 1.0, 0.0))
        for h in range(high_parts):
            here = high_part == h
            at = h * COORD
            masked[index, at : at + 64, :] = jnp.where(here, high.astype(f32), 0.0).astype(bf16)
            masked[index, at + 64 : at + 128, :] = jnp.where(here, low.astype(f32), 0.0).astype(bf16)
            masked[index, at + 128 : at + COORD, :] = jnp.where(here, extra, 0.0).astype(bf16)
    copies = []
    for index in range(blocks):
        placed = nn(masked[index], low_hot[index])
        for h in range(high_parts):
            part = placed[h * COORD : (h + 1) * COORD]
            at = slice(index * rows + h * LOW, index * rows + (h + 1) * LOW)
            tree_ref[:, at] = part.astype(bf16)
            a_ref[at, 0:128], a_ref[at, 128:256] = feature_rows(part[0:64], part[64:128], part[136:144])
        mine = slice(index * rows, (index + 1) * rows)
        copies.append(pltpu.make_async_copy(a_ref.at[mine], a_hbm.at[mine], sems.at[0, index]))
        copies[-1].start()
    for index in range(blocks):
        mine = slice(index * rows, (index + 1) * rows)
        picked = onehot(iota((rows, SK), 0) == infos[index][BASE : BASE + 1].astype(jnp.int32))
        keep(index, nn(tree_ref[:, mine], picked))
    for index in range(blocks):
        mine = slice(index * rows, (index + 1) * rows)
        base_ref[index] = jnp.exp(nn(a_ref[mine, :], sk_bt[:, index * SK : (index + 1) * SK])).astype(bf16)
        copies.append(pltpu.make_async_copy(base_ref.at[index], base_hbm.at[index], sems.at[1, index]))
        copies[-1].start()
    start, count, offset, total = 0, blocks, 0, blocks * trees
    while count > 1:
        nodes = count // 2
        for j in range(nodes):
            pair = slice((start + 2 * j) * SK, (start + 2 * j + 2) * SK)
            row = offset + lax.axis_index("leaf") * nodes + j
            picked = onehot(iota((2 * SK, SK), 0) == upper_ref[pl.ds(row, 1), :])
            here = start + count + j
            keep(here, nn(sk_t[:, pair], picked))
            upper_tiles_ref[here - blocks] = jnp.exp(nn(sk_ref[pair, :], sk_bt[:, here * SK : (here + 1) * SK]))
        total = total // 2
        offset = offset + total
        start, count = start + count, nodes
    found = sk_t[:, start * SK : (start + 1) * SK].astype(f32)
    top_ref[0:64, :] = found[0:64] + found[64:128]
    top_ref[64:72, :] = found[128:136]
    list_tiles(count_ref, list_ref, tiles, times)
    for copy in copies:
        copy.wait()


def weights_kernel(layout, base_hbm, upper_tiles_ref, top_ref, slot_ref, *refs):
    light_refs, refs = refs[: layout.count], refs[layout.count :]
    if layout.fine:
        order = far_first(layout.blocks)
        order = order + [layout.blocks + step for step in order]
        light_refs = [light_refs[order.index(g)] for g in range(layout.count)]
    w_ref, coef_ref, pack_ref, masked, low_hot, base_ref, sems = refs
    blocks, rows = layout.blocks, layout.rows
    width = light_refs[0].shape[0]
    each = width // layout.halves
    pack_ref[0:PLACE_ROWS, :] = top_ref[...]
    for index in range(blocks):
        pltpu.make_async_copy(base_hbm.at[index], base_ref.at[index], sems.at[index]).start()

    def keep(node, coef):
        coef_ref[:, node * SK : (node + 1) * SK] = stack_two(coef)
        pack_ref[PLACE_ROWS:, :] = coef

    for index in range(blocks):
        low_part, high_part = parts_of(slot_ref[index : index + 1, :])
        low_by_column(low_hot.at[index], low_part.astype(f32))
        for half in range(layout.halves):
            light = [ref[layout.columns(g, half, each), layout.lanes(index)] for g, ref in enumerate(light_refs)]
            light = lanes_of(light)
            for h in range(rows // LOW):
                at = h * width + half * each
                masked[index, at : at + each, :] = jnp.where(high_part == h, light, 0.0).astype(bf16)
    for index in range(blocks):
        placed = nn(masked[index], low_hot[index])
        for h in range(rows // LOW):
            at = index * rows + h * LOW
            w_ref[:, at : at + LOW] = placed[h * width : (h + 1) * width].astype(bf16)
    for index in range(blocks):
        pltpu.make_async_copy(base_hbm.at[index], base_ref.at[index], sems.at[index]).wait()
        keep(index, nn(w_ref[:, index * rows : (index + 1) * rows], base_ref[index]))
    start, count = 0, blocks
    while count > 1:
        for j in range(count // 2):
            pair = slice((start + 2 * j) * SK, (start + 2 * j + 2) * SK)
            here = start + count + j
            high, low = two(upper_tiles_ref[here - blocks])
            coef = nn(coef_ref[:, pair], high)
            keep(here, coef[:width] + coef[width:] + nn(coef_ref[0:width, pair], low))
        start, count = start + count, count // 2


def near_kernel(layout, tiles, a_hbm, tree_ref, w_ref, acc, a_ref, bt_ref, sem, even, odd, even_tile, odd_tile):
    span = layout.span
    copy = pltpu.make_async_copy(a_hbm, a_ref, sem)
    copy.start()
    filled = tiles[0, tiles.shape[1] - 1]
    acc[...] = jnp.zeros_like(acc)
    target_columns(layout, bt_ref, tree_ref)

    def exponents(unit, out):
        for k in range(2):
            out[k] = tile_exponents(layout, tiles, 2 * unit + k, a_ref, bt_ref)

    def add(tile, block):
        source = aligned(tiles[1, tile] * LEAF, LEAF, LEAF)
        target = aligned(tiles[0, tile] * span, span, span)
        acc[:, target] += tiles[2, tile].astype(f32) * nn(w_ref[:, source], block)

    copy.wait()
    exponents(0, even)
    for k in range(2):
        even_tile[k] = jnp.exp(even[k]).astype(bf16)
    exponents(1, odd)

    def phase(unit, upcoming, ready, finished, previous):
        for k in range(2):
            upcoming[k] = tile_exponents(layout, tiles, 2 * (unit + 1) + k, a_ref, bt_ref)
            finished[k] = jnp.exp(ready[k]).astype(bf16)
            add(2 * (unit - 1) + k, previous[k])

    def step(pair, carry):
        phase(2 * pair + 1, even, odd, odd_tile, even_tile)
        phase(2 * pair + 2, odd, even, even_tile, odd_tile)
        return carry

    units = (filled + 1) // 2
    pairs = (units - 1) // 2
    lax.fori_loop(0, pairs, step, 0)
    for k in range(2):
        add(4 * pairs + k, even_tile[k])

    @pl.when(2 * pairs + 1 < units)
    def _():
        for k in range(2):
            odd_tile[k] = jnp.exp(odd[k]).astype(bf16)
            add(4 * pairs + 2 + k, odd_tile[k])


def far_kernel(layout, low_levels, pack_ref, slot_ref, info_ref, tree_ref, sk_ref, coef_ref, near_ref, *refs):
    out_refs, refs = refs[: layout.halves], refs[layout.halves :]
    tops, coefs, scaled, low_hot, bt_ref, sums, masked = refs[:7]
    powers, tiles = refs[7:9], refs[9:11]
    blocks, rows = layout.blocks, layout.rows
    ups, width = pack_ref.shape[0], near_ref.shape[0]
    levels = low_levels + ups
    span, core = layout.span, layout.core()
    per_block = rows // LEAF
    lane = iota((1, SK), 1)
    for up in range(ups):
        pack = pack_ref[up]
        high, low = two(pack[0:64])
        sub = iota((8, SK), 0)
        extra = jnp.where(sub == 0, pack[67:68], jnp.where(sub == 1, pack[68:69], pack[69:70]))
        extra = jnp.where(sub < 3, extra, jnp.where(sub < 6, 1.0, 0.0))
        at = slice((low_levels + up) * SK, (low_levels + up + 1) * SK)
        rows_of = feature_rows(high.astype(f32), low.astype(f32), extra)
        coef = stack_two(pack[PLACE_ROWS:])
        for index in range(blocks):
            tops[index, at, 0:128], tops[index, at, 128:256] = rows_of
            coefs[index, :, at] = coef
    for index in range(blocks):
        node, start, count = index, 0, blocks
        for level in range(low_levels):
            at = slice(level * SK, (level + 1) * SK)
            other = slice((start + (node ^ 1)) * SK, (start + (node ^ 1) + 1) * SK)
            tops[index, at, :] = sk_ref[other, :]
            coefs[index, :, at] = coef_ref[:, other]
            node, start, count = node // 2, start + count, count // 2
        for leaf in range(per_block):
            flags = info_ref[index, FLAGS + leaf : FLAGS + leaf + 1, :]
            used = []
            for level in range(levels):
                flag = jnp.sum(jnp.where(lane == level, flags, 0.0), axis=1, keepdims=True)
                used.append(jnp.broadcast_to(flag, (1, SK)))
            used = jnp.concatenate(used, 1)
            scaled[index * per_block + leaf] = (coefs[index].astype(f32) * used).astype(bf16)

    target_columns(layout, bt_ref, tree_ref)

    def exponents(leaf):
        powers[leaf % 2][...] = nn(tops[leaf // per_block], bt_ref[:, leaf * span : (leaf + 1) * span])

    def product(leaf):
        here = slice(leaf * span, (leaf + 1) * span)
        far = nn(scaled[leaf], tiles[leaf % 2][...])
        sums[:, here] = near_ref[:, here] + far[:width] + far[width:]

    leaves = blocks * per_block
    exponents(0)
    for leaf in range(leaves):
        if leaf + 1 < leaves:
            exponents(leaf + 1)
        tiles[leaf % 2][...] = jnp.exp(powers[leaf % 2][...]).astype(bf16)
        if leaf:
            product(leaf - 1)
    product(leaves - 1)

    high_parts = []
    pieces = rows // LOW // layout.halves
    for index in range(blocks):
        low_part, high_part = parts_of(slot_ref[index : index + 1, :])
        high_parts.append(high_part)
        for c in range(rows // LANES):
            at = slice(c * LANES, (c + 1) * LANES)
            low_hot[index, :, at] = onehot(iota((LOW, LANES), 0) == low_part[:, at])
        for k in range(pieces):
            at = (index * pieces + k) * LOW
            masked[index, k * 2 * width : (k + 1) * 2 * width, :] = stack_two(sums[:, at : at + LOW])
    for index in range(blocks):
        moved = nn(masked[index], low_hot[index])
        result = jnp.zeros((2 * width, rows), f32)
        for k in range(pieces):
            here = high_parts[index] == k * layout.halves + core
            result = jnp.where(here, moved[k * 2 * width : (k + 1) * 2 * width], result)
        result = result[:width] + result[width:]
        if not layout.fine:
            out_refs[0][0, :, layout.lanes(index)] = result
            continue
        for g in range(layout.count):
            out_ref = out_refs[g // blocks]
            out_ref[g % blocks, :, layout.lanes(index)] = result[:, g * layout.per : (g + 1) * layout.per]


def add_kernel(kept_ref, got_ref, *out_refs):
    half = kept_ref.shape[1] // 2
    for step, out_ref in enumerate(out_refs):
        out_ref[0:half, :] = kept_ref[step, 0:half, :] + got_ref[step, half:, :]
        out_ref[half:, :] = kept_ref[step, half:, :] + got_ref[step, 0:half, :]


def far_first(blocks):
    return list(reversed(range(blocks)))


def final_kernel(blocks, pos_ref, *refs):
    back_refs, (weights_ref, out_ref, perm, vals) = refs[:-4], refs[-4:]
    chunks = pos_ref.shape[0]
    rows = chunks * LANES
    width, split = back_refs[0].shape
    width = LANES // blocks if blocks else width
    for r in range(chunks):
        spread(perm, slice(r * LANES, (r + 1) * LANES), column(pos_ref[r : r + 1, :]))
    for g, back_ref in enumerate(back_refs):
        columns, at = 0, slice(0, rows)
        value = back_ref[...]
        if blocks:
            columns = (lax.axis_index("sub") ^ far_first(blocks)[g % blocks]) * width
            at = aligned((lax.axis_index("leaf") ^ lax.axis_index("rep") ^ (g // blocks)) * split, split, split)
            value = value[0:width] if g < blocks else value[width:]
        high, low = two(value)
        vals[aligned(columns, width, width), at] = high
        vals[aligned(columns + LANES, width, width), at] = low
    step = 256
    for s in range(rows // step):
        here = slice(s * step, (s + 1) * step)
        moved = nt(perm[here, :], vals[...])
        out_ref[here, :] = ridge * weights_ref[here, :] + moved[:, :LANES] + moved[:, LANES:]


def upper_levels(pack, skeleton_upper, my_leaf, trees, blocks):
    devices = trees * blocks
    level = blocks.bit_length() - 1
    offset = sum(devices >> step for step in range(1, level + 1))
    line = jnp.arange(pack.shape[0])[:, None]
    is_point, is_norm = line < DIM, (line >= DIM + 3) & (line < DIM + 6)
    is_coef = line >= PLACE_ROWS
    packs, own, stride = [], pack, 1
    while stride < trees:
        other = lax.ppermute(own, "leaf", [(i, i ^ stride) for i in range(trees)])
        packs.append(other)
        stride *= 2
        if stride < trees:
            second = (my_leaf // (stride // 2)) % 2 == 1
            pair = jnp.where(second, jnp.concatenate([other, own], 1), jnp.concatenate([own, other], 1))
            chosen = pair[:, skeleton_upper[offset + my_leaf // stride]]
            level += 1
            offset += devices >> level
            norms = jnp.sum(jnp.where(is_norm, pair, 0.0), axis=0)
            chosen_norms = jnp.sum(jnp.where(is_norm, chosen, 0.0), axis=0)
            inner = jnp.dot(
                jnp.where(is_point, pair, 0.0).T, jnp.where(is_point, chosen, 0.0), precision=highest
            )
            tile = jnp.exp(inner + norms[:, None] + chosen_norms[None])
            own = jnp.where(is_coef, jnp.dot(pair, tile, precision=highest), chosen)
    return jnp.stack(packs)


def body(points, weights, tree_slot, near_count, near_list, skeleton_base, skeleton_upper, far_use):
    blocks, trees, reps = lax.axis_size("sub"), lax.axis_size("leaf"), lax.axis_size("rep")
    devices = blocks * trees
    rows, columns = weights.shape
    low_levels = blocks.bit_length() - 1
    ups = trees.bit_length() - 1
    width = columns // blocks
    part = rows // trees
    per = part // blocks
    total = blocks * rows
    leaves = total // LEAF
    my_leaf = lax.axis_index("leaf")
    fine = trees == 2 and reps == 2 and per % LANES == 0
    layout = Layout(blocks, trees, rows, fine)
    split = part if fine else rows
    cols = width * layout.halves

    place, pos = pl.pallas_call(
        functools.partial(place_kernel, fine),
        out_shape=(shaped((PLACE_ROWS, split), f32), shaped((rows // LANES, LANES), f32)),
        in_specs=[spec()] * 4,
        out_specs=(spec(),) * 2,
        scratch_shapes=[vm((split // LOW * COORD, rows), bf16), vm((rows, LOW), bf16)],
        compiler_params=params(),
        name="sort_points",
    )(tree_slot.reshape(rows // LANES, LANES), points.T, skeleton_base, far_use)
    axes = ("leaf", "sub", "rep")

    def swap(value, step, other=0):
        pairs = []
        for leaf in range(trees):
            for sub in range(blocks):
                for core in range(reps):
                    to = ((leaf ^ core ^ other) * blocks + (sub ^ step)) * reps + core
                    pairs.append(((leaf * blocks + sub) * reps + core, to))
        return lax.ppermute(value, axes, pairs)

    def other_core(value):
        return lax.ppermute(value, "rep", [(0, 1), (1, 0)])

    def sorted_light(pos):
        if fine:
            shapes = (shaped((blocks, width, part), f32),) * 2
        else:
            shapes = (shaped((columns, rows), f32),)
        return pl.pallas_call(
            functools.partial(light_kernel, blocks if fine else 0),
            out_shape=shapes,
            in_specs=[spec()] * 2,
            out_specs=(spec(),) * len(shapes),
            scratch_shapes=[
                vm((rows // LOW * LANES, rows), bf16),
                vm((rows, LOW), bf16),
                vm((rows // LOW, LANES, LOW), f32),
            ],
            compiler_params=params(40),
            name="sort_weights",
        )(in_hbm(pos), in_hbm(weights))

    if fine:
        place = {0: swap(place, 0)}
        stride = blocks // 2
        while stride:
            for step in sorted(place):
                place[step | stride] = lax.ppermute(place[step], "sub", [(i, i ^ stride) for i in range(blocks)])
            stride //= 2
        kept, sent = sorted_light(pos)
        tied, kept, sent = lax.optimization_barrier((place[1], kept, sent))
        light = pl.pallas_call(
            join_kernel,
            out_shape=(shaped((cols, part), f32),) * blocks,
            in_specs=[spec()] * 2,
            out_specs=(spec(),) * blocks,
            compiler_params=params(40),
            name="join_cores",
        )(kept, other_core(sent))
        place, light = lax.optimization_barrier((place, light))
        theirs = {step: other_core(one) for step, one in place.items()}
        place = [place[step] for step in range(blocks)] + [theirs[step] for step in range(blocks)]
        light = [swap(light[step], step) for step in far_first(blocks)]
        small = []
    else:
        info = jnp.pad(far_use.astype(f32), ((FLAGS, 5 - far_use.shape[0]), (0, SK - far_use.shape[1])))
        small = [lax.all_gather(info.at[BASE].set(skeleton_base[0].astype(f32)), "sub", axis=0, tiled=False)]
        place = place.reshape(PLACE_ROWS, trees, part).transpose(1, 0, 2)
        place = lax.all_to_all(place, "leaf", split_axis=0, concat_axis=0, tiled=True)
        place = lax.all_gather(place, "sub", axis=0, tiled=False)
        place = place.transpose(1, 0, 2, 3).reshape(devices, PLACE_ROWS, blocks, per)
        place = [place.transpose(1, 2, 0, 3).reshape(PLACE_ROWS, total)]
        light = sorted_light(pos)[0].reshape(columns, trees, part).transpose(1, 0, 2).reshape(devices, width, part)
        light = lax.all_to_all(light, ("leaf", "sub"), split_axis=0, concat_axis=0, tiled=True)
        light = light.reshape(devices, width, blocks, per)
        light = [light.transpose(1, 2, 0, 3).reshape(width, total)]

    nodes = 2 * blocks - 1
    tree, feat_a, base, sk, upper_tiles, top, slots, info, tiles = pl.pallas_call(
        functools.partial(points_kernel, layout, trees),
        out_shape=(
            vm((COORD, total), bf16),
            pltpu.MemorySpace.HBM((total, FEAT), bf16),
            pltpu.MemorySpace.HBM((blocks, rows, SK), bf16),
            vm((nodes * SK, FEAT), bf16),
            vm((blocks - 1, 2 * SK, SK), f32),
            vm((PLACE_ROWS, SK), f32),
            vm((blocks, rows), f32),
            vm((blocks, 8, SK), f32),
            pltpu.MemorySpace.HBM((3, leaves * leaves + 8), jnp.int32),
        ),
        in_specs=[spec(SMEM)] * 2 + [spec()] * (1 + len(small) + layout.count),
        out_specs=(spec(), spec(pl.ANY), spec(pl.ANY)) + (spec(),) * 5 + (spec(SMEM),),
        scratch_shapes=[
            vm((blocks, rows // LOW * COORD, rows), bf16),
            vm((blocks, rows, LOW), bf16),
            vm((total, FEAT), bf16),
            vm((blocks, rows, SK), bf16),
            vm((COORD, nodes * SK), bf16),
            vm((FEAT, nodes * SK), bf16),
            pltpu.SemaphoreType.DMA((2, blocks)),
            pltpu.SMEM((leaves,), jnp.int32),
        ],
        compiler_params=params(40),
        name="tree_points",
    )(in_hbm(near_count), in_hbm(near_list[0]), in_hbm(skeleton_upper), *small, *place)

    if fine:
        light, slots = lax.optimization_barrier((light, slots))
        light = light + [other_core(one) for one in light]
    tree_light, coefs, pack = pl.pallas_call(
        functools.partial(weights_kernel, layout),
        out_shape=(
            vm((cols, total), bf16),
            vm((2 * cols, nodes * SK), bf16),
            shaped((PLACE_ROWS + cols, SK), f32),
        ),
        in_specs=[spec(pl.ANY)] + [spec()] * (3 + layout.count),
        out_specs=(spec(),) * 3,
        scratch_shapes=[
            vm((blocks, rows // LOW * cols, rows), bf16),
            vm((blocks, rows, LOW), bf16),
            vm((blocks, rows, SK), bf16),
            pltpu.SemaphoreType.DMA((blocks,)),
        ],
        compiler_params=params(40),
        name="tree_weights",
    )(in_hbm(base), held(upper_tiles), held(top), held(slots), *light)

    packs = upper_levels(pack, skeleton_upper, my_leaf, trees, blocks)

    near = pl.pallas_call(
        functools.partial(near_kernel, layout),
        out_shape=vm((cols, total // layout.halves), f32),
        in_specs=[spec(SMEM), spec(pl.ANY)] + [spec()] * 2,
        out_specs=spec(),
        scratch_shapes=[
            vm((total, FEAT), bf16),
            vm((FEAT, total // layout.halves), bf16),
            pltpu.SemaphoreType.DMA(()),
        ]
        + [vm((2, LEAF, layout.span), f32)] * 2
        + [vm((2, LEAF, layout.span), bf16)] * 2,
        compiler_params=params(40),
        name="near",
    )(in_hbm(tiles), in_hbm(feat_a), held(tree), held(tree_light))

    levels = low_levels + ups
    back = pl.pallas_call(
        functools.partial(far_kernel, layout, low_levels),
        out_shape=(shaped((layout.count // layout.halves, cols, total // layout.count), f32),) * layout.halves,
        in_specs=[spec()] * 7,
        out_specs=(spec(),) * layout.halves,
        scratch_shapes=[
            vm((blocks, levels * SK, FEAT), bf16),
            vm((blocks, 2 * cols, levels * SK), bf16),
            vm((leaves, 2 * cols, levels * SK), bf16),
            vm((blocks, LOW, rows), bf16),
            vm((FEAT, total // layout.halves), bf16),
            vm((cols, total // layout.halves), f32),
            vm((blocks, rows // LOW // layout.halves * 2 * cols, LOW), bf16),
        ]
        + [vm((levels * SK, layout.span), f32)] * 2
        + [vm((levels * SK, layout.span), bf16)] * 2,
        compiler_params=params(40),
        name="far",
    )(packs, *[held(one) for one in (slots, info, tree, sk, coefs, near)])

    if fine:
        kept, sent = back
        sums = pl.pallas_call(
            add_kernel,
            out_shape=(shaped((cols, part), f32),) * blocks,
            in_specs=[spec()] * 2,
            out_specs=(spec(),) * blocks,
            compiler_params=params(40),
            name="add_cores",
        )(kept, other_core(sent))
        back = [swap(sums[step], step) for step in far_first(blocks)]
        back = back + [other_core(one) for one in back]
    else:
        back = back[0].reshape(cols, blocks, devices, per).transpose(2, 0, 1, 3).reshape(devices, width, part)
        back = lax.all_to_all(back, ("leaf", "sub"), split_axis=0, concat_axis=0, tiled=True)
        back = [back.reshape(trees, columns, part).transpose(1, 0, 2).reshape(columns, rows)]

    return pl.pallas_call(
        functools.partial(final_kernel, blocks if fine else 0),
        out_shape=shaped((rows, columns), f32),
        in_specs=[spec()] * (2 + layout.count),
        out_specs=spec(),
        scratch_shapes=[vm((rows, rows), bf16), vm((2 * LANES, rows), bf16)],
        compiler_params=params(40),
        name="to_input_order",
    )(pos, *back, weights)


def solution(mesh):
    in_specs = (
        P(("groups", "leaf", "sub"), None),
        P(("groups", "leaf", "sub"), "rep"),
        P(("groups", "leaf", "sub")),
        P(("groups", "leaf"), None),
        P(("groups", "leaf"), None, None),
        P(("groups", "leaf", "sub"), None),
        P("groups", None),
        P(("groups", "leaf", "sub"), None),
    )
    out_specs = P(("groups", "leaf", "sub"), "rep")
    return jax.shard_map(body, mesh=mesh, in_specs=in_specs, out_specs=out_specs, check_vma=False)
```

```python
import functools

import jax
import jax.numpy as jnp
from jax import lax
from jax.experimental import pallas as pl
from jax.experimental.pallas import tpu as pltpu
from jax.sharding import PartitionSpec as P

DIM = 64
LEAF = 512
SK = 128
LANES = 128
FEAT = 256
LOW = 256
COORD = 144

highest = lax.Precision.HIGHEST
point_scale = 0.25
ridge = 0.5
PLACE_ROWS = 72
TAIL = 64
SLOT, NORM, BASE, FLAGS = 0, 1, 2, 3
f32 = jnp.float32
bf16 = jnp.bfloat16
VMEM = pltpu.MemorySpace.VMEM
SMEM = pltpu.MemorySpace.SMEM


def spec(space=VMEM):
    return pl.BlockSpec(memory_space=space)


def params(mib=58):
    return pltpu.CompilerParams(vmem_limit_bytes=mib * 1024 * 1024)


def in_hbm(array):
    return pltpu.with_memory_space_constraint(array, pltpu.MemorySpace.HBM)


def held(array):
    return pltpu.with_memory_space_constraint(array, VMEM)


def vm(shape, dtype):
    return pltpu.VMEM(shape, dtype)


def shaped(shape, dtype):
    return jax.ShapeDtypeStruct(shape, dtype)


def nt(left, right):
    return lax.dot_general(left, right, (((1,), (1,)), ((), ())), preferred_element_type=f32)


def nn(left, right):
    return jnp.dot(left, right, preferred_element_type=f32)


def column(row):
    return jnp.transpose(jnp.broadcast_to(row, (LANES, LANES)))


def iota(shape, dim):
    return lax.broadcasted_iota(jnp.int32, shape, dim)


def onehot(mask):
    return jnp.where(mask, 1.0, 0.0).astype(bf16)


def two(value):
    high = value.astype(bf16)
    return high, (value - high.astype(f32)).astype(bf16)


def three(value):
    high = value.astype(bf16).astype(f32)
    mid = (value - high).astype(bf16).astype(f32)
    return high, mid, (value - high - mid).astype(bf16).astype(f32)


def lanes_of(blocks):
    return blocks[0] if len(blocks) == 1 else jnp.concatenate(blocks, 1)


def aligned(start, size, unit):
    return pl.ds(pl.multiple_of(start, unit), size)


def stack_two(value):
    high, low = two(value)
    return jnp.concatenate([high, low], 0)


def spread(perm, here, rank):
    lane = iota((LANES, LANES), 1).astype(f32)
    for c in range(perm.shape[1] // LANES):
        perm[here, c * LANES : (c + 1) * LANES] = onehot(lane + float(c * LANES) == rank)


def place_kernel(fine, slot_ref, points_ref, base_ref, flag_ref, place_ref, pos_ref, masked, low_hot):
    chunks = slot_ref.shape[0]
    slots = slot_ref[...]
    slot = slots.astype(f32)
    within = slots & (chunks * LANES - 1)
    high, low = (within >> 5).astype(f32), (within & 31).astype(f32)
    ranks = []
    for r in range(chunks):
        here = slice(r * LANES, (r + 1) * LANES)
        mine = column(slot[r : r + 1])
        before = jnp.zeros((LANES, LANES), f32)
        for c in range(chunks):
            before += jnp.where(slot[c : c + 1] < mine, 1.0, 0.0)
        rank = jnp.broadcast_to(jnp.sum(before, axis=1, keepdims=True), (LANES, LANES))
        ranks.append(jnp.transpose(rank)[0:1])
        pos_ref[r : r + 1, :] = ranks[-1]
        spread(low_hot, here, (rank.astype(jnp.int32) & (LOW - 1)).astype(f32))
    scaled = points_ref[...] * point_scale
    ph, plo = two(scaled)
    nh, nm, nl = three(-0.5 * jnp.sum(scaled * scaled, axis=0, keepdims=True))
    high, low = lanes_of([high[c : c + 1] for c in range(chunks)]), lanes_of([low[c : c + 1] for c in range(chunks)])
    sub = iota((16, chunks * LANES), 0)
    extra = jnp.where(sub == 0, high, jnp.where(sub == 1, low, 0.0))
    extra = jnp.where(sub == 2, nh, jnp.where(sub == 3, nm, jnp.where(sub == 4, nl, extra)))
    high_part = lanes_of(ranks).astype(jnp.int32) // LOW
    parts = place_ref.shape[1] // LOW
    first = (lax.axis_index("leaf") ^ lax.axis_index("rep")) * parts if fine else 0
    for h in range(parts):
        here = high_part == first + h
        masked[h * COORD : h * COORD + 64, :] = jnp.where(here, ph.astype(f32), 0.0).astype(bf16)
        masked[h * COORD + 64 : h * COORD + 128, :] = jnp.where(here, plo.astype(f32), 0.0).astype(bf16)
        masked[h * COORD + 128 : (h + 1) * COORD, :] = jnp.where(here, extra, 0.0).astype(bf16)
    placed = nn(masked[...], low_hot[...])
    tail = iota((PLACE_ROWS - TAIL, LOW), 0)
    for h in range(parts):
        at = slice(h * LOW, (h + 1) * LOW)
        moved = placed[h * COORD : (h + 1) * COORD]
        place_ref[0:TAIL, at] = moved[0:64] + moved[64:128]
        slot_row = moved[128:129] * 32.0 + moved[129:130]
        norm_row = moved[130:131] + moved[131:132] + moved[132:133]
        place_ref[TAIL:, at] = jnp.where(tail == SLOT, slot_row, jnp.where(tail == NORM, norm_row, 0.0))
    if fine:
        place_ref[TAIL + BASE : TAIL + BASE + 1, 0:SK] = base_ref[...].astype(f32)
        place_ref[TAIL + FLAGS : TAIL + FLAGS + flag_ref.shape[0], 0 : flag_ref.shape[1]] = flag_ref[...].astype(f32)


def light_kernel(blocks, pos_ref, weights_ref, *refs):
    light_refs, (masked, low_hot, placed) = refs[:-3], refs[-3:]
    chunks = pos_ref.shape[0]
    high_count = chunks * LANES // LOW
    low_part, high_part = parts_of(lanes_of([pos_ref[c : c + 1, :] for c in range(chunks)]))
    low_by_column(low_hot, low_part.astype(f32))
    for c in range(chunks):
        at = slice(c * LANES, (c + 1) * LANES)
        turned = jnp.transpose(weights_ref[at, :])
        for h in range(high_count):
            masked[h * LANES : (h + 1) * LANES, at] = jnp.where(high_part[:, at] == h, turned, 0.0).astype(bf16)
    moved = nn(masked[...], low_hot[...])
    for h in range(high_count):
        if not blocks:
            light_refs[0][:, h * LOW : (h + 1) * LOW] = moved[h * LANES : (h + 1) * LANES]
        placed[h] = moved[h * LANES : (h + 1) * LANES]
    if not blocks:
        return
    width, parts = LANES // blocks, high_count // 2
    for other, light_ref in enumerate(light_refs):
        first = (lax.axis_index("leaf") ^ lax.axis_index("rep") ^ other) * parts
        for step in range(blocks):
            columns = aligned((lax.axis_index("sub") ^ step) * width, width, width)
            for h in range(parts):
                light_ref[step, :, h * LOW : (h + 1) * LOW] = placed[first + h, columns, :]


def join_kernel(kept_ref, got_ref, *out_refs):
    half = kept_ref.shape[1]
    for step, out_ref in enumerate(out_refs):
        out_ref[0:half, :] = kept_ref[step]
        out_ref[half:, :] = got_ref[step]


class Layout:
    def __init__(self, blocks, trees, rows, fine):
        self.blocks, self.rows, self.fine = blocks, rows, fine
        self.count = blocks * trees if fine else 1
        self.per = rows // self.count
        self.halves = 2 if fine else 1
        self.span = LEAF // self.halves

    def core(self):
        return lax.axis_index("rep") if self.fine else 0

    def lanes(self, index):
        return slice(index * self.per, (index + 1) * self.per)

    def columns(self, group, half, each):
        if self.fine and group >= self.blocks:
            half = 1 - half
        return slice(half * each, (half + 1) * each)

    def gather(self, refs, index, part):
        return lanes_of([ref[part, self.lanes(index)] for ref in refs])

    def info(self, refs, small_ref, index):
        if not self.fine:
            return small_ref[index]
        core = lax.axis_index("rep")
        found = jnp.zeros((PLACE_ROWS - TAIL, SK), f32)
        for step in range(self.blocks):
            mine, theirs = refs[step][TAIL:, 0:SK], refs[self.blocks + step][TAIL:, 0:SK]
            here = jnp.where(core == 0, mine, theirs)
            found = jnp.where((lax.axis_index("sub") ^ step) == index, here, found)
        return found


def low_by_column(out, low):
    for c in range(out.shape[0] // LANES):
        at = slice(c * LANES, (c + 1) * LANES)
        spread(out, at, column(low[:, at]))


def parts_of(slots):
    slots = slots.astype(jnp.int32)
    return slots & (LOW - 1), slots // LOW


def feature_columns(out, at, tree):
    out[0:64, at] = tree[0:64].astype(bf16)
    out[64:128, at] = tree[0:64].astype(bf16)
    out[128:192, at] = tree[64:128].astype(bf16)
    out[192:208, at] = jnp.where(iota((16, tree.shape[1]), 0) < 8, tree[128:144].astype(f32), 0.0).astype(bf16)
    out[208:256, at] = jnp.zeros((48, tree.shape[1]), bf16)


def feature_rows(high, low, extra):
    first = jnp.transpose(jnp.concatenate([high, low], 0))
    second = jnp.transpose(jnp.concatenate([high, extra, jnp.zeros((56, high.shape[1]), f32)], 0))
    return first.astype(bf16), second.astype(bf16)


def target_columns(layout, out, tree_ref):
    span = layout.span
    for leaf in range(out.shape[1] // span):
        here = aligned(leaf * LEAF + layout.core() * span, span, span)
        feature_columns(out, slice(leaf * span, (leaf + 1) * span), tree_ref[:, here])


def tile_exponents(layout, tiles, tile, a_ref, bt_ref):
    source = aligned(tiles[1, tile] * LEAF, LEAF, LEAF)
    target = aligned(tiles[0, tile] * layout.span, layout.span, layout.span)
    return nn(a_ref[source, :], bt_ref[:, target])


def list_tiles(count_ref, list_ref, tiles, times):
    every = count_ref.shape[1]

    def tally(leaf, carry):
        for other in range(every):
            times[leaf * every + other] = (leaf == other).astype(jnp.int32)

        def add(slot, carry):
            at = leaf * every + list_ref[leaf, slot]
            times[at] = times[at] + 1
            return carry

        return lax.fori_loop(0, count_ref[0, leaf], add, carry)

    lax.fori_loop(0, every, tally, 0)

    def write(other, filled):
        for leaf in range(every):
            many = times[leaf * every + other]
            tiles[0, filled] = leaf
            tiles[1, filled] = other
            tiles[2, filled] = many
            filled = filled + (many > 0).astype(jnp.int32)
        return filled

    filled = lax.fori_loop(0, every, write, jnp.int32(0))

    def pad(more, carry):
        tiles[0, more] = 0
        tiles[1, more] = 0
        tiles[2, more] = 0
        return carry

    lax.fori_loop(filled, tiles.shape[1] - 1, pad, 0)
    tiles[0, tiles.shape[1] - 1] = filled


def points_kernel(layout, trees, count_ref, list_ref, upper_ref, *refs):
    if not layout.fine:
        small_ref, refs = refs[0], refs[1:]
    else:
        small_ref = None
    place_refs, refs = refs[: layout.count], refs[layout.count :]
    tree_ref, a_hbm, base_hbm, sk_ref, upper_tiles_ref, top_ref, slot_ref, info_ref, tiles = refs[:9]
    masked, low_hot, a_ref, base_ref, sk_t, sk_bt, sems, times = refs[9:]
    blocks, rows = layout.blocks, layout.rows

    def keep(node, found):
        at = slice(node * SK, (node + 1) * SK)
        sk_t[:, at] = found.astype(bf16)
        sk_ref[at, 0:128], sk_ref[at, 128:256] = feature_rows(found[0:64], found[64:128], found[136:144])
        feature_columns(sk_bt, at, found)

    high_parts = rows // LOW
    infos = []
    for index in range(blocks):
        tail = layout.gather(place_refs, index, slice(TAIL, PLACE_ROWS))
        slots = tail[SLOT : SLOT + 1]
        slot_ref[index : index + 1, :] = slots
        infos.append(layout.info(place_refs, small_ref, index))
        info_ref[index] = infos[-1]
        low_part, high_part = parts_of(slots)
        low_by_column(low_hot.at[index], low_part.astype(f32))
        points = layout.gather(place_refs, index, slice(0, TAIL))
        high, low = two(points)
        nh, nm, nl = three(tail[NORM : NORM + 1])
        sub = iota((16, rows), 0)
        norms = jnp.where((sub == 3) | (sub == 8), nh, jnp.where((sub == 4) | (sub == 9), nm, nl))
        is_norm = ((sub >= 3) & (sub < 6)) | ((sub >= 8) & (sub < 11))
        is_one = (sub < 3) | ((sub >= 11) & (sub < 14))
        extra = jnp.where(is_norm, norms, jnp.where(is_one, 1.0, 0.0))
        for h in range(high_parts):
            here = high_part == h
            at = h * COORD
            masked[index, at : at + 64, :] = jnp.where(here, high.astype(f32), 0.0).astype(bf16)
            masked[index, at + 64 : at + 128, :] = jnp.where(here, low.astype(f32), 0.0).astype(bf16)
            masked[index, at + 128 : at + COORD, :] = jnp.where(here, extra, 0.0).astype(bf16)
    copies = []
    for index in range(blocks):
        placed = nn(masked[index], low_hot[index])
        for h in range(high_parts):
            part = placed[h * COORD : (h + 1) * COORD]
            at = slice(index * rows + h * LOW, index * rows + (h + 1) * LOW)
            tree_ref[:, at] = part.astype(bf16)
            a_ref[at, 0:128], a_ref[at, 128:256] = feature_rows(part[0:64], part[64:128], part[136:144])
        mine = slice(index * rows, (index + 1) * rows)
        copies.append(pltpu.make_async_copy(a_ref.at[mine], a_hbm.at[mine], sems.at[0, index]))
        copies[-1].start()
    for index in range(blocks):
        mine = slice(index * rows, (index + 1) * rows)
        picked = onehot(iota((rows, SK), 0) == infos[index][BASE : BASE + 1].astype(jnp.int32))
        keep(index, nn(tree_ref[:, mine], picked))
    for index in range(blocks):
        mine = slice(index * rows, (index + 1) * rows)
        base_ref[index] = jnp.exp(nn(a_ref[mine, :], sk_bt[:, index * SK : (index + 1) * SK])).astype(bf16)
        copies.append(pltpu.make_async_copy(base_ref.at[index], base_hbm.at[index], sems.at[1, index]))
        copies[-1].start()
    start, count, offset, total = 0, blocks, 0, blocks * trees
    while count > 1:
        nodes = count // 2
        for j in range(nodes):
            pair = slice((start + 2 * j) * SK, (start + 2 * j + 2) * SK)
            row = offset + lax.axis_index("leaf") * nodes + j
            picked = onehot(iota((2 * SK, SK), 0) == upper_ref[pl.ds(row, 1), :])
            here = start + count + j
            keep(here, nn(sk_t[:, pair], picked))
            upper_tiles_ref[here - blocks] = jnp.exp(nn(sk_ref[pair, :], sk_bt[:, here * SK : (here + 1) * SK]))
        total = total // 2
        offset = offset + total
        start, count = start + count, nodes
    found = sk_t[:, start * SK : (start + 1) * SK].astype(f32)
    top_ref[0:64, :] = found[0:64] + found[64:128]
    top_ref[64:72, :] = found[128:136]
    list_tiles(count_ref, list_ref, tiles, times)
    for copy in copies:
        copy.wait()


def weights_kernel(layout, base_hbm, upper_tiles_ref, top_ref, slot_ref, *refs):
    light_refs, refs = refs[: layout.count], refs[layout.count :]
    if layout.fine:
        order = far_first(layout.blocks)
        order = order + [layout.blocks + step for step in order]
        light_refs = [light_refs[order.index(g)] for g in range(layout.count)]
    w_ref, coef_ref, pack_ref, masked, low_hot, base_ref, sems = refs
    blocks, rows = layout.blocks, layout.rows
    width = light_refs[0].shape[0]
    each = width // layout.halves
    pack_ref[0:PLACE_ROWS, :] = top_ref[...]
    for index in range(blocks):
        pltpu.make_async_copy(base_hbm.at[index], base_ref.at[index], sems.at[index]).start()

    def keep(node, coef):
        coef_ref[:, node * SK : (node + 1) * SK] = stack_two(coef)
        pack_ref[PLACE_ROWS:, :] = coef

    for index in range(blocks):
        low_part, high_part = parts_of(slot_ref[index : index + 1, :])
        low_by_column(low_hot.at[index], low_part.astype(f32))
        for half in range(layout.halves):
            light = [ref[layout.columns(g, half, each), layout.lanes(index)] for g, ref in enumerate(light_refs)]
            light = lanes_of(light)
            for h in range(rows // LOW):
                at = h * width + half * each
                masked[index, at : at + each, :] = jnp.where(high_part == h, light, 0.0).astype(bf16)
    for index in range(blocks):
        placed = nn(masked[index], low_hot[index])
        for h in range(rows // LOW):
            at = index * rows + h * LOW
            w_ref[:, at : at + LOW] = placed[h * width : (h + 1) * width].astype(bf16)
    for index in range(blocks):
        pltpu.make_async_copy(base_hbm.at[index], base_ref.at[index], sems.at[index]).wait()
        keep(index, nn(w_ref[:, index * rows : (index + 1) * rows], base_ref[index]))
    start, count = 0, blocks
    while count > 1:
        for j in range(count // 2):
            pair = slice((start + 2 * j) * SK, (start + 2 * j + 2) * SK)
            here = start + count + j
            high, low = two(upper_tiles_ref[here - blocks])
            coef = nn(coef_ref[:, pair], high)
            keep(here, coef[:width] + coef[width:] + nn(coef_ref[0:width, pair], low))
        start, count = start + count, count // 2


def near_kernel(layout, tiles, a_hbm, tree_ref, w_ref, acc, a_ref, bt_ref, sems, even, odd, even_tile, odd_tile):
    span = layout.span
    size = a_ref.shape[0] // 2
    copies = []
    for half in range(2):
        rows = slice(half * size, (half + 1) * size)
        copies.append(pltpu.make_async_copy(a_hbm.at[rows], a_ref.at[rows], sems.at[half]))
        copies[-1].start()
    filled = tiles[0, tiles.shape[1] - 1]
    acc[...] = jnp.zeros_like(acc)
    target_columns(layout, bt_ref, tree_ref)

    def exponents(unit, out):
        for k in range(2):
            out[k] = tile_exponents(layout, tiles, 2 * unit + k, a_ref, bt_ref)

    def add(tile, block):
        source = aligned(tiles[1, tile] * LEAF, LEAF, LEAF)
        target = aligned(tiles[0, tile] * span, span, span)
        acc[:, target] += tiles[2, tile].astype(f32) * nn(w_ref[:, source], block)

    copies[0].wait()
    exponents(0, even)
    for k in range(2):
        even_tile[k] = jnp.exp(even[k]).astype(bf16)
    exponents(1, odd)
    copies[1].wait()

    def phase(unit, upcoming, ready, finished, previous):
        for k in range(2):
            upcoming[k] = tile_exponents(layout, tiles, 2 * (unit + 1) + k, a_ref, bt_ref)
            finished[k] = jnp.exp(ready[k]).astype(bf16)
            add(2 * (unit - 1) + k, previous[k])

    def step(pair, carry):
        phase(2 * pair + 1, even, odd, odd_tile, even_tile)
        phase(2 * pair + 2, odd, even, even_tile, odd_tile)
        return carry

    units = (filled + 1) // 2
    pairs = (units - 1) // 2
    lax.fori_loop(0, pairs, step, 0)
    for k in range(2):
        add(4 * pairs + k, even_tile[k])

    @pl.when(2 * pairs + 1 < units)
    def _():
        for k in range(2):
            odd_tile[k] = jnp.exp(odd[k]).astype(bf16)
            add(4 * pairs + 2 + k, odd_tile[k])


def far_kernel(layout, low_levels, pack_ref, slot_ref, info_ref, tree_ref, sk_ref, coef_ref, near_ref, *refs):
    out_refs, refs = refs[: layout.halves], refs[layout.halves :]
    tops, coefs, scaled, low_hot, bt_ref, sums, masked = refs[:7]
    powers, tiles = refs[7:9], refs[9:11]
    blocks, rows = layout.blocks, layout.rows
    ups, width = pack_ref.shape[0], near_ref.shape[0]
    levels = low_levels + ups
    span, core = layout.span, layout.core()
    per_block = rows // LEAF
    lane = iota((1, SK), 1)
    for up in range(ups):
        pack = pack_ref[up]
        high, low = two(pack[0:64])
        sub = iota((8, SK), 0)
        extra = jnp.where(sub == 0, pack[67:68], jnp.where(sub == 1, pack[68:69], pack[69:70]))
        extra = jnp.where(sub < 3, extra, jnp.where(sub < 6, 1.0, 0.0))
        at = slice((low_levels + up) * SK, (low_levels + up + 1) * SK)
        rows_of = feature_rows(high.astype(f32), low.astype(f32), extra)
        coef = stack_two(pack[PLACE_ROWS:])
        for index in range(blocks):
            tops[index, at, 0:128], tops[index, at, 128:256] = rows_of
            coefs[index, :, at] = coef
    for index in range(blocks):
        node, start, count = index, 0, blocks
        for level in range(low_levels):
            at = slice(level * SK, (level + 1) * SK)
            other = slice((start + (node ^ 1)) * SK, (start + (node ^ 1) + 1) * SK)
            tops[index, at, :] = sk_ref[other, :]
            coefs[index, :, at] = coef_ref[:, other]
            node, start, count = node // 2, start + count, count // 2
        for leaf in range(per_block):
            flags = info_ref[index, FLAGS + leaf : FLAGS + leaf + 1, :]
            used = []
            for level in range(levels):
                flag = jnp.sum(jnp.where(lane == level, flags, 0.0), axis=1, keepdims=True)
                used.append(jnp.broadcast_to(flag, (1, SK)))
            used = jnp.concatenate(used, 1)
            scaled[index * per_block + leaf] = (coefs[index].astype(f32) * used).astype(bf16)

    target_columns(layout, bt_ref, tree_ref)

    def exponents(leaf):
        powers[leaf % 2][...] = nn(tops[leaf // per_block], bt_ref[:, leaf * span : (leaf + 1) * span])

    def product(leaf):
        here = slice(leaf * span, (leaf + 1) * span)
        far = nn(scaled[leaf], tiles[leaf % 2][...])
        sums[:, here] = near_ref[:, here] + far[:width] + far[width:]

    leaves = blocks * per_block
    exponents(0)
    for leaf in range(leaves):
        if leaf + 1 < leaves:
            exponents(leaf + 1)
        tiles[leaf % 2][...] = jnp.exp(powers[leaf % 2][...]).astype(bf16)
        if leaf:
            product(leaf - 1)
    product(leaves - 1)

    high_parts = []
    pieces = rows // LOW // layout.halves
    for index in range(blocks):
        low_part, high_part = parts_of(slot_ref[index : index + 1, :])
        high_parts.append(high_part)
        for c in range(rows // LANES):
            at = slice(c * LANES, (c + 1) * LANES)
            low_hot[index, :, at] = onehot(iota((LOW, LANES), 0) == low_part[:, at])
        for k in range(pieces):
            at = (index * pieces + k) * LOW
            masked[index, k * 2 * width : (k + 1) * 2 * width, :] = stack_two(sums[:, at : at + LOW])
    for index in range(blocks):
        moved = nn(masked[index], low_hot[index])
        result = jnp.zeros((2 * width, rows), f32)
        for k in range(pieces):
            here = high_parts[index] == k * layout.halves + core
            result = jnp.where(here, moved[k * 2 * width : (k + 1) * 2 * width], result)
        result = result[:width] + result[width:]
        if not layout.fine:
            out_refs[0][0, :, layout.lanes(index)] = result
            continue
        for g in range(layout.count):
            out_ref = out_refs[g // blocks]
            out_ref[g % blocks, :, layout.lanes(index)] = result[:, g * layout.per : (g + 1) * layout.per]


def add_kernel(kept_ref, got_ref, *out_refs):
    half = kept_ref.shape[1] // 2
    for step, out_ref in enumerate(out_refs):
        out_ref[0:half, :] = kept_ref[step, 0:half, :] + got_ref[step, half:, :]
        out_ref[half:, :] = kept_ref[step, half:, :] + got_ref[step, 0:half, :]


def far_first(blocks):
    return list(reversed(range(blocks)))


def final_kernel(blocks, pos_ref, *refs):
    back_refs, (weights_ref, out_ref, perm, vals) = refs[:-4], refs[-4:]
    chunks = pos_ref.shape[0]
    rows = chunks * LANES
    width, split = back_refs[0].shape
    width = LANES // blocks if blocks else width
    for r in range(chunks):
        spread(perm, slice(r * LANES, (r + 1) * LANES), column(pos_ref[r : r + 1, :]))
    for g, back_ref in enumerate(back_refs):
        columns, at = 0, slice(0, rows)
        value = back_ref[...]
        if blocks:
            columns = (lax.axis_index("sub") ^ far_first(blocks)[g % blocks]) * width
            at = aligned((lax.axis_index("leaf") ^ lax.axis_index("rep") ^ (g // blocks)) * split, split, split)
            value = value[0:width] if g < blocks else value[width:]
        high, low = two(value)
        vals[aligned(columns, width, width), at] = high
        vals[aligned(columns + LANES, width, width), at] = low
    step = 256
    for s in range(rows // step):
        here = slice(s * step, (s + 1) * step)
        moved = nt(perm[here, :], vals[...])
        out_ref[here, :] = ridge * weights_ref[here, :] + moved[:, :LANES] + moved[:, LANES:]


def upper_levels(pack, skeleton_upper, my_leaf, trees, blocks):
    devices = trees * blocks
    level = blocks.bit_length() - 1
    offset = sum(devices >> step for step in range(1, level + 1))
    line = jnp.arange(pack.shape[0])[:, None]
    is_point, is_norm = line < DIM, (line >= DIM + 3) & (line < DIM + 6)
    is_coef = line >= PLACE_ROWS
    packs, own, stride = [], pack, 1
    while stride < trees:
        other = lax.ppermute(own, "leaf", [(i, i ^ stride) for i in range(trees)])
        packs.append(other)
        stride *= 2
        if stride < trees:
            second = (my_leaf // (stride // 2)) % 2 == 1
            pair = jnp.where(second, jnp.concatenate([other, own], 1), jnp.concatenate([own, other], 1))
            chosen = pair[:, skeleton_upper[offset + my_leaf // stride]]
            level += 1
            offset += devices >> level
            norms = jnp.sum(jnp.where(is_norm, pair, 0.0), axis=0)
            chosen_norms = jnp.sum(jnp.where(is_norm, chosen, 0.0), axis=0)
            inner = jnp.dot(
                jnp.where(is_point, pair, 0.0).T, jnp.where(is_point, chosen, 0.0), precision=highest
            )
            tile = jnp.exp(inner + norms[:, None] + chosen_norms[None])
            own = jnp.where(is_coef, jnp.dot(pair, tile, precision=highest), chosen)
    return jnp.stack(packs)


def body(points, weights, tree_slot, near_count, near_list, skeleton_base, skeleton_upper, far_use):
    blocks, trees, reps = lax.axis_size("sub"), lax.axis_size("leaf"), lax.axis_size("rep")
    devices = blocks * trees
    rows, columns = weights.shape
    low_levels = blocks.bit_length() - 1
    ups = trees.bit_length() - 1
    width = columns // blocks
    part = rows // trees
    per = part // blocks
    total = blocks * rows
    leaves = total // LEAF
    my_leaf = lax.axis_index("leaf")
    fine = trees == 2 and reps == 2 and per % LANES == 0
    layout = Layout(blocks, trees, rows, fine)
    split = part if fine else rows
    cols = width * layout.halves

    place, pos = pl.pallas_call(
        functools.partial(place_kernel, fine),
        out_shape=(shaped((PLACE_ROWS, split), f32), shaped((rows // LANES, LANES), f32)),
        in_specs=[spec()] * 4,
        out_specs=(spec(),) * 2,
        scratch_shapes=[vm((split // LOW * COORD, rows), bf16), vm((rows, LOW), bf16)],
        compiler_params=params(),
        name="sort_points",
    )(tree_slot.reshape(rows // LANES, LANES), points.T, skeleton_base, far_use)
    axes = ("leaf", "sub", "rep")

    def swap(value, step, other=0):
        pairs = []
        for leaf in range(trees):
            for sub in range(blocks):
                for core in range(reps):
                    to = ((leaf ^ core ^ other) * blocks + (sub ^ step)) * reps + core
                    pairs.append(((leaf * blocks + sub) * reps + core, to))
        return lax.ppermute(value, axes, pairs)

    def other_core(value):
        return lax.ppermute(value, "rep", [(0, 1), (1, 0)])

    def sorted_light(pos):
        if fine:
            shapes = (shaped((blocks, width, part), f32),) * 2
        else:
            shapes = (shaped((columns, rows), f32),)
        return pl.pallas_call(
            functools.partial(light_kernel, blocks if fine else 0),
            out_shape=shapes,
            in_specs=[spec()] * 2,
            out_specs=(spec(),) * len(shapes),
            scratch_shapes=[
                vm((rows // LOW * LANES, rows), bf16),
                vm((rows, LOW), bf16),
                vm((rows // LOW, LANES, LOW), f32),
            ],
            compiler_params=params(40),
            name="sort_weights",
        )(in_hbm(pos), in_hbm(weights))

    if fine:
        place = {0: swap(place, 0)}
        stride = blocks // 2
        while stride:
            for step in sorted(place):
                place[step | stride] = lax.ppermute(place[step], "sub", [(i, i ^ stride) for i in range(blocks)])
            stride //= 2
        kept, sent = sorted_light(pos)
        place, kept, sent = lax.optimization_barrier((place, kept, sent))
        light = pl.pallas_call(
            join_kernel,
            out_shape=(shaped((cols, part), f32),) * blocks,
            in_specs=[spec()] * 2,
            out_specs=(spec(),) * blocks,
            compiler_params=params(40),
            name="join_cores",
        )(kept, other_core(sent))
        theirs = {step: other_core(one) for step, one in place.items()}
        place = [place[step] for step in range(blocks)] + [theirs[step] for step in range(blocks)]
        light = [swap(light[step], step) for step in far_first(blocks)]
        small = []
    else:
        info = jnp.pad(far_use.astype(f32), ((FLAGS, 5 - far_use.shape[0]), (0, SK - far_use.shape[1])))
        small = [lax.all_gather(info.at[BASE].set(skeleton_base[0].astype(f32)), "sub", axis=0, tiled=False)]
        place = place.reshape(PLACE_ROWS, trees, part).transpose(1, 0, 2)
        place = lax.all_to_all(place, "leaf", split_axis=0, concat_axis=0, tiled=True)
        place = lax.all_gather(place, "sub", axis=0, tiled=False)
        place = place.transpose(1, 0, 2, 3).reshape(devices, PLACE_ROWS, blocks, per)
        place = [place.transpose(1, 2, 0, 3).reshape(PLACE_ROWS, total)]
        light = sorted_light(pos)[0].reshape(columns, trees, part).transpose(1, 0, 2).reshape(devices, width, part)
        light = lax.all_to_all(light, ("leaf", "sub"), split_axis=0, concat_axis=0, tiled=True)
        light = light.reshape(devices, width, blocks, per)
        light = [light.transpose(1, 2, 0, 3).reshape(width, total)]

    nodes = 2 * blocks - 1
    tree, feat_a, base, sk, upper_tiles, top, slots, info, tiles = pl.pallas_call(
        functools.partial(points_kernel, layout, trees),
        out_shape=(
            vm((COORD, total), bf16),
            pltpu.MemorySpace.HBM((total, FEAT), bf16),
            pltpu.MemorySpace.HBM((blocks, rows, SK), bf16),
            vm((nodes * SK, FEAT), bf16),
            vm((blocks - 1, 2 * SK, SK), f32),
            vm((PLACE_ROWS, SK), f32),
            vm((blocks, rows), f32),
            vm((blocks, 8, SK), f32),
            pltpu.MemorySpace.HBM((3, leaves * leaves + 8), jnp.int32),
        ),
        in_specs=[spec(SMEM)] * 2 + [spec()] * (1 + len(small) + layout.count),
        out_specs=(spec(), spec(pl.ANY), spec(pl.ANY)) + (spec(),) * 5 + (spec(SMEM),),
        scratch_shapes=[
            vm((blocks, rows // LOW * COORD, rows), bf16),
            vm((blocks, rows, LOW), bf16),
            vm((total, FEAT), bf16),
            vm((blocks, rows, SK), bf16),
            vm((COORD, nodes * SK), bf16),
            vm((FEAT, nodes * SK), bf16),
            pltpu.SemaphoreType.DMA((2, blocks)),
            pltpu.SMEM((leaves * leaves,), jnp.int32),
        ],
        compiler_params=params(40),
        name="tree_points",
    )(in_hbm(near_count), in_hbm(near_list[0]), in_hbm(skeleton_upper), *small, *place)

    if fine:
        light, slots = lax.optimization_barrier((light, slots))
        light = light + [other_core(one) for one in light]
    tree_light, coefs, pack = pl.pallas_call(
        functools.partial(weights_kernel, layout),
        out_shape=(
            vm((cols, total), bf16),
            vm((2 * cols, nodes * SK), bf16),
            shaped((PLACE_ROWS + cols, SK), f32),
        ),
        in_specs=[spec(pl.ANY)] + [spec()] * (3 + layout.count),
        out_specs=(spec(),) * 3,
        scratch_shapes=[
            vm((blocks, rows // LOW * cols, rows), bf16),
            vm((blocks, rows, LOW), bf16),
            vm((blocks, rows, SK), bf16),
            pltpu.SemaphoreType.DMA((blocks,)),
        ],
        compiler_params=params(40),
        name="tree_weights",
    )(in_hbm(base), held(upper_tiles), held(top), held(slots), *light)

    packs = upper_levels(pack, skeleton_upper, my_leaf, trees, blocks)

    near = pl.pallas_call(
        functools.partial(near_kernel, layout),
        out_shape=vm((cols, total // layout.halves), f32),
        in_specs=[spec(SMEM), spec(pl.ANY)] + [spec()] * 2,
        out_specs=spec(),
        scratch_shapes=[
            vm((total, FEAT), bf16),
            vm((FEAT, total // layout.halves), bf16),
            pltpu.SemaphoreType.DMA((2,)),
        ]
        + [vm((2, LEAF, layout.span), f32)] * 2
        + [vm((2, LEAF, layout.span), bf16)] * 2,
        compiler_params=params(40),
        name="near",
    )(in_hbm(tiles), in_hbm(feat_a), held(tree), held(tree_light))

    levels = low_levels + ups
    back = pl.pallas_call(
        functools.partial(far_kernel, layout, low_levels),
        out_shape=(shaped((layout.count // layout.halves, cols, total // layout.count), f32),) * layout.halves,
        in_specs=[spec()] * 7,
        out_specs=(spec(),) * layout.halves,
        scratch_shapes=[
            vm((blocks, levels * SK, FEAT), bf16),
            vm((blocks, 2 * cols, levels * SK), bf16),
            vm((leaves, 2 * cols, levels * SK), bf16),
            vm((blocks, LOW, rows), bf16),
            vm((FEAT, total // layout.halves), bf16),
            vm((cols, total // layout.halves), f32),
            vm((blocks, rows // LOW // layout.halves * 2 * cols, LOW), bf16),
        ]
        + [vm((levels * SK, layout.span), f32)] * 2
        + [vm((levels * SK, layout.span), bf16)] * 2,
        compiler_params=params(40),
        name="far",
    )(packs, *[held(one) for one in (slots, info, tree, sk, coefs, near)])

    if fine:
        kept, sent = back
        sums = pl.pallas_call(
            add_kernel,
            out_shape=(shaped((cols, part), f32),) * blocks,
            in_specs=[spec()] * 2,
            out_specs=(spec(),) * blocks,
            compiler_params=params(40),
            name="add_cores",
        )(kept, other_core(sent))
        back = [swap(sums[step], step) for step in far_first(blocks)]
        back = back + [other_core(one) for one in back]
    else:
        back = back[0].reshape(cols, blocks, devices, per).transpose(2, 0, 1, 3).reshape(devices, width, part)
        back = lax.all_to_all(back, ("leaf", "sub"), split_axis=0, concat_axis=0, tiled=True)
        back = [back.reshape(trees, columns, part).transpose(1, 0, 2).reshape(columns, rows)]

    return pl.pallas_call(
        functools.partial(final_kernel, blocks if fine else 0),
        out_shape=shaped((rows, columns), f32),
        in_specs=[spec()] * (2 + layout.count),
        out_specs=spec(),
        scratch_shapes=[vm((rows, rows), bf16), vm((2 * LANES, rows), bf16)],
        compiler_params=params(40),
        name="to_input_order",
    )(pos, *back, weights)


def solution(mesh):
    in_specs = (
        P(("groups", "leaf", "sub"), None),
        P(("groups", "leaf", "sub"), "rep"),
        P(("groups", "leaf", "sub")),
        P(("groups", "leaf"), None),
        P(("groups", "leaf"), None, None),
        P(("groups", "leaf", "sub"), None),
        P("groups", None),
        P(("groups", "leaf", "sub"), None),
    )
    out_specs = P(("groups", "leaf", "sub"), "rep")
    return jax.shard_map(body, mesh=mesh, in_specs=in_specs, out_specs=out_specs, check_vma=False)
```

```python
import functools

import jax
import jax.numpy as jnp
from jax import lax
from jax.experimental import pallas as pl
from jax.experimental.pallas import tpu as pltpu
from jax.sharding import PartitionSpec as P

DIM = 64
LEAF = 512
SK = 128
LANES = 128
FEAT = 256
LOW = 256
COORD = 144

highest = lax.Precision.HIGHEST
point_scale = 0.25
ridge = 0.5
PLACE_ROWS = 72
TAIL = 64
SLOT, NORM, BASE, FLAGS = 0, 1, 2, 3
f32 = jnp.float32
bf16 = jnp.bfloat16
VMEM = pltpu.MemorySpace.VMEM
SMEM = pltpu.MemorySpace.SMEM


def spec(space=VMEM):
    return pl.BlockSpec(memory_space=space)


def params(mib=58):
    return pltpu.CompilerParams(vmem_limit_bytes=mib * 1024 * 1024)


def in_hbm(array):
    return pltpu.with_memory_space_constraint(array, pltpu.MemorySpace.HBM)


def held(array):
    return pltpu.with_memory_space_constraint(array, VMEM)


def vm(shape, dtype):
    return pltpu.VMEM(shape, dtype)


def shaped(shape, dtype):
    return jax.ShapeDtypeStruct(shape, dtype)


def nt(left, right):
    return lax.dot_general(left, right, (((1,), (1,)), ((), ())), preferred_element_type=f32)


def nn(left, right):
    return jnp.dot(left, right, preferred_element_type=f32)


def column(row):
    return jnp.transpose(jnp.broadcast_to(row, (LANES, LANES)))


def iota(shape, dim):
    return lax.broadcasted_iota(jnp.int32, shape, dim)


def onehot(mask):
    return jnp.where(mask, 1.0, 0.0).astype(bf16)


def two(value):
    high = value.astype(bf16)
    return high, (value - high.astype(f32)).astype(bf16)


def three(value):
    high = value.astype(bf16).astype(f32)
    mid = (value - high).astype(bf16).astype(f32)
    return high, mid, (value - high - mid).astype(bf16).astype(f32)


def lanes_of(blocks):
    return blocks[0] if len(blocks) == 1 else jnp.concatenate(blocks, 1)


def aligned(start, size, unit):
    return pl.ds(pl.multiple_of(start, unit), size)


def stack_two(value):
    high, low = two(value)
    return jnp.concatenate([high, low], 0)


def spread(perm, here, rank):
    lane = iota((LANES, LANES), 1).astype(f32)
    for c in range(perm.shape[1] // LANES):
        perm[here, c * LANES : (c + 1) * LANES] = onehot(lane + float(c * LANES) == rank)


def place_kernel(fine, slot_ref, points_ref, base_ref, flag_ref, place_ref, pos_ref, masked, low_hot):
    chunks = slot_ref.shape[0]
    slots = slot_ref[...]
    slot = slots.astype(f32)
    within = slots & (chunks * LANES - 1)
    high, low = (within >> 5).astype(f32), (within & 31).astype(f32)
    ranks = []
    for r in range(chunks):
        here = slice(r * LANES, (r + 1) * LANES)
        mine = column(slot[r : r + 1])
        before = jnp.zeros((LANES, LANES), f32)
        for c in range(chunks):
            before += jnp.where(slot[c : c + 1] < mine, 1.0, 0.0)
        rank = jnp.broadcast_to(jnp.sum(before, axis=1, keepdims=True), (LANES, LANES))
        ranks.append(jnp.transpose(rank)[0:1])
        pos_ref[r : r + 1, :] = ranks[-1]
        spread(low_hot, here, (rank.astype(jnp.int32) & (LOW - 1)).astype(f32))
    scaled = points_ref[...] * point_scale
    ph, plo = two(scaled)
    nh, nm, nl = three(-0.5 * jnp.sum(scaled * scaled, axis=0, keepdims=True))
    high, low = lanes_of([high[c : c + 1] for c in range(chunks)]), lanes_of([low[c : c + 1] for c in range(chunks)])
    sub = iota((16, chunks * LANES), 0)
    extra = jnp.where(sub == 0, high, jnp.where(sub == 1, low, 0.0))
    extra = jnp.where(sub == 2, nh, jnp.where(sub == 3, nm, jnp.where(sub == 4, nl, extra)))
    high_part = lanes_of(ranks).astype(jnp.int32) // LOW
    parts = place_ref.shape[1] // LOW
    first = (lax.axis_index("leaf") ^ lax.axis_index("rep")) * parts if fine else 0
    for h in range(parts):
        here = high_part == first + h
        masked[h * COORD : h * COORD + 64, :] = jnp.where(here, ph.astype(f32), 0.0).astype(bf16)
        masked[h * COORD + 64 : h * COORD + 128, :] = jnp.where(here, plo.astype(f32), 0.0).astype(bf16)
        masked[h * COORD + 128 : (h + 1) * COORD, :] = jnp.where(here, extra, 0.0).astype(bf16)
    placed = nn(masked[...], low_hot[...])
    tail = iota((PLACE_ROWS - TAIL, LOW), 0)
    for h in range(parts):
        at = slice(h * LOW, (h + 1) * LOW)
        moved = placed[h * COORD : (h + 1) * COORD]
        place_ref[0:TAIL, at] = moved[0:64] + moved[64:128]
        slot_row = moved[128:129] * 32.0 + moved[129:130]
        norm_row = moved[130:131] + moved[131:132] + moved[132:133]
        place_ref[TAIL:, at] = jnp.where(tail == SLOT, slot_row, jnp.where(tail == NORM, norm_row, 0.0))
    if fine:
        place_ref[TAIL + BASE : TAIL + BASE + 1, 0:SK] = base_ref[...].astype(f32)
        place_ref[TAIL + FLAGS : TAIL + FLAGS + flag_ref.shape[0], 0 : flag_ref.shape[1]] = flag_ref[...].astype(f32)


def light_kernel(blocks, pos_ref, weights_ref, *refs):
    light_refs, (masked, low_hot, placed) = refs[:-3], refs[-3:]
    chunks = pos_ref.shape[0]
    high_count = chunks * LANES // LOW
    low_part, high_part = parts_of(lanes_of([pos_ref[c : c + 1, :] for c in range(chunks)]))
    low_by_column(low_hot, low_part.astype(f32))
    for c in range(chunks):
        at = slice(c * LANES, (c + 1) * LANES)
        turned = jnp.transpose(weights_ref[at, :])
        for h in range(high_count):
            masked[h * LANES : (h + 1) * LANES, at] = jnp.where(high_part[:, at] == h, turned, 0.0).astype(bf16)
    moved = nn(masked[...], low_hot[...])
    for h in range(high_count):
        if not blocks:
            light_refs[0][:, h * LOW : (h + 1) * LOW] = moved[h * LANES : (h + 1) * LANES]
        placed[h] = moved[h * LANES : (h + 1) * LANES]
    if not blocks:
        return
    width, parts = LANES // blocks, high_count // 2
    for other, light_ref in enumerate(light_refs):
        first = (lax.axis_index("leaf") ^ lax.axis_index("rep") ^ other) * parts
        for step in range(blocks):
            columns = aligned((lax.axis_index("sub") ^ step) * width, width, width)
            for h in range(parts):
                light_ref[step, :, h * LOW : (h + 1) * LOW] = placed[first + h, columns, :]


def join_kernel(kept_ref, got_ref, *out_refs):
    half = kept_ref.shape[1]
    for step, out_ref in enumerate(out_refs):
        out_ref[0:half, :] = kept_ref[step]
        out_ref[half:, :] = got_ref[step]


class Layout:
    def __init__(self, blocks, trees, rows, fine):
        self.blocks, self.rows, self.fine = blocks, rows, fine
        self.count = blocks * trees if fine else 1
        self.per = rows // self.count
        self.halves = 2 if fine else 1
        self.span = LEAF // self.halves

    def core(self):
        return lax.axis_index("rep") if self.fine else 0

    def lanes(self, index):
        return slice(index * self.per, (index + 1) * self.per)

    def columns(self, group, half, each):
        if self.fine and group >= self.blocks:
            half = 1 - half
        return slice(half * each, (half + 1) * each)

    def gather(self, refs, index, part):
        return lanes_of([ref[part, self.lanes(index)] for ref in refs])

    def info(self, refs, small_ref, index):
        if not self.fine:
            return small_ref[index]
        core = lax.axis_index("rep")
        found = jnp.zeros((PLACE_ROWS - TAIL, SK), f32)
        for step in range(self.blocks):
            mine, theirs = refs[step][TAIL:, 0:SK], refs[self.blocks + step][TAIL:, 0:SK]
            here = jnp.where(core == 0, mine, theirs)
            found = jnp.where((lax.axis_index("sub") ^ step) == index, here, found)
        return found


def low_by_column(out, low):
    for c in range(out.shape[0] // LANES):
        at = slice(c * LANES, (c + 1) * LANES)
        spread(out, at, column(low[:, at]))


def parts_of(slots):
    slots = slots.astype(jnp.int32)
    return slots & (LOW - 1), slots // LOW


def feature_columns(out, at, tree):
    out[0:64, at] = tree[0:64].astype(bf16)
    out[64:128, at] = tree[0:64].astype(bf16)
    out[128:192, at] = tree[64:128].astype(bf16)
    out[192:208, at] = jnp.where(iota((16, tree.shape[1]), 0) < 8, tree[128:144].astype(f32), 0.0).astype(bf16)
    out[208:256, at] = jnp.zeros((48, tree.shape[1]), bf16)


def feature_rows(high, low, extra):
    first = jnp.transpose(jnp.concatenate([high, low], 0))
    second = jnp.transpose(jnp.concatenate([high, extra, jnp.zeros((56, high.shape[1]), f32)], 0))
    return first.astype(bf16), second.astype(bf16)


def target_columns(layout, out, tree_ref):
    span = layout.span
    for leaf in range(out.shape[1] // span):
        here = aligned(leaf * LEAF + layout.core() * span, span, span)
        feature_columns(out, slice(leaf * span, (leaf + 1) * span), tree_ref[:, here])


def tile_exponents(layout, tiles, tile, a_ref, bt_ref):
    source = aligned(tiles[1, tile] * LEAF, LEAF, LEAF)
    target = aligned(tiles[0, tile] * layout.span, layout.span, layout.span)
    return nn(a_ref[source, :], bt_ref[:, target])


def list_tiles(count_ref, list_ref, tiles, times):
    every = count_ref.shape[1]

    def tally(leaf, carry):
        for other in range(every):
            times[leaf * every + other] = (leaf == other).astype(jnp.int32)

        def add(slot, carry):
            at = leaf * every + list_ref[leaf, slot]
            times[at] = times[at] + 1
            return carry

        return lax.fori_loop(0, count_ref[0, leaf], add, carry)

    lax.fori_loop(0, every, tally, 0)

    def write(other, filled):
        for leaf in range(every):
            many = times[leaf * every + other]
            tiles[0, filled] = leaf
            tiles[1, filled] = other
            tiles[2, filled] = many
            filled = filled + (many > 0).astype(jnp.int32)
        return filled

    filled = lax.fori_loop(0, every, write, jnp.int32(0))

    def pad(more, carry):
        tiles[0, more] = 0
        tiles[1, more] = 0
        tiles[2, more] = 0
        return carry

    lax.fori_loop(filled, tiles.shape[1] - 1, pad, 0)
    tiles[0, tiles.shape[1] - 1] = filled


def points_kernel(layout, trees, count_ref, list_ref, upper_ref, *refs):
    if not layout.fine:
        small_ref, refs = refs[0], refs[1:]
    else:
        small_ref = None
    place_refs, refs = refs[: layout.count], refs[layout.count :]
    tree_ref, a_hbm, base_hbm, sk_ref, upper_tiles_ref, top_ref, slot_ref, info_ref, tiles = refs[:9]
    masked, low_hot, a_ref, base_ref, sk_t, sk_bt, sems, times = refs[9:]
    blocks, rows = layout.blocks, layout.rows

    def keep(node, found):
        at = slice(node * SK, (node + 1) * SK)
        sk_t[:, at] = found.astype(bf16)
        sk_ref[at, 0:128], sk_ref[at, 128:256] = feature_rows(found[0:64], found[64:128], found[136:144])
        feature_columns(sk_bt, at, found)

    high_parts = rows // LOW
    infos = []
    for index in range(blocks):
        tail = layout.gather(place_refs, index, slice(TAIL, PLACE_ROWS))
        slots = tail[SLOT : SLOT + 1]
        slot_ref[index : index + 1, :] = slots
        infos.append(layout.info(place_refs, small_ref, index))
        info_ref[index] = infos[-1]
        low_part, high_part = parts_of(slots)
        low_by_column(low_hot.at[index], low_part.astype(f32))
        points = layout.gather(place_refs, index, slice(0, TAIL))
        high, low = two(points)
        nh, nm, nl = three(tail[NORM : NORM + 1])
        sub = iota((16, rows), 0)
        norms = jnp.where((sub == 3) | (sub == 8), nh, jnp.where((sub == 4) | (sub == 9), nm, nl))
        is_norm = ((sub >= 3) & (sub < 6)) | ((sub >= 8) & (sub < 11))
        is_one = (sub < 3) | ((sub >= 11) & (sub < 14))
        extra = jnp.where(is_norm, norms, jnp.where(is_one, 1.0, 0.0))
        for h in range(high_parts):
            here = high_part == h
            at = h * COORD
            masked[index, at : at + 64, :] = jnp.where(here, high.astype(f32), 0.0).astype(bf16)
            masked[index, at + 64 : at + 128, :] = jnp.where(here, low.astype(f32), 0.0).astype(bf16)
            masked[index, at + 128 : at + COORD, :] = jnp.where(here, extra, 0.0).astype(bf16)
    copies = []
    for index in range(blocks):
        placed = nn(masked[index], low_hot[index])
        for h in range(high_parts):
            part = placed[h * COORD : (h + 1) * COORD]
            at = slice(index * rows + h * LOW, index * rows + (h + 1) * LOW)
            tree_ref[:, at] = part.astype(bf16)
            a_ref[at, 0:128], a_ref[at, 128:256] = feature_rows(part[0:64], part[64:128], part[136:144])
        mine = slice(index * rows, (index + 1) * rows)
        copies.append(pltpu.make_async_copy(a_ref.at[mine], a_hbm.at[mine], sems.at[0, index]))
        copies[-1].start()
    for index in range(blocks):
        mine = slice(index * rows, (index + 1) * rows)
        picked = onehot(iota((rows, SK), 0) == infos[index][BASE : BASE + 1].astype(jnp.int32))
        keep(index, nn(tree_ref[:, mine], picked))
    for index in range(blocks):
        mine = slice(index * rows, (index + 1) * rows)
        base_ref[index] = jnp.exp(nn(a_ref[mine, :], sk_bt[:, index * SK : (index + 1) * SK])).astype(bf16)
        copies.append(pltpu.make_async_copy(base_ref.at[index], base_hbm.at[index], sems.at[1, index]))
        copies[-1].start()
    start, count, offset, total = 0, blocks, 0, blocks * trees
    while count > 1:
        nodes = count // 2
        for j in range(nodes):
            pair = slice((start + 2 * j) * SK, (start + 2 * j + 2) * SK)
            row = offset + lax.axis_index("leaf") * nodes + j
            picked = onehot(iota((2 * SK, SK), 0) == upper_ref[pl.ds(row, 1), :])
            here = start + count + j
            keep(here, nn(sk_t[:, pair], picked))
            upper_tiles_ref[here - blocks] = jnp.exp(nn(sk_ref[pair, :], sk_bt[:, here * SK : (here + 1) * SK]))
        total = total // 2
        offset = offset + total
        start, count = start + count, nodes
    found = sk_t[:, start * SK : (start + 1) * SK].astype(f32)
    top_ref[0:64, :] = found[0:64] + found[64:128]
    top_ref[64:72, :] = found[128:136]
    list_tiles(count_ref, list_ref, tiles, times)
    for copy in copies:
        copy.wait()


def weights_kernel(layout, base_hbm, upper_tiles_ref, top_ref, slot_ref, *refs):
    light_refs, refs = refs[: layout.count], refs[layout.count :]
    if layout.fine:
        order = far_first(layout.blocks)
        order = order + [layout.blocks + step for step in order]
        light_refs = [light_refs[order.index(g)] for g in range(layout.count)]
    w_ref, coef_ref, pack_ref, masked, low_hot, base_ref, sems = refs
    blocks, rows = layout.blocks, layout.rows
    width = light_refs[0].shape[0]
    each = width // layout.halves
    pack_ref[0:PLACE_ROWS, :] = top_ref[...]
    for index in range(blocks):
        pltpu.make_async_copy(base_hbm.at[index], base_ref.at[index], sems.at[index]).start()

    def keep(node, coef):
        coef_ref[:, node * SK : (node + 1) * SK] = stack_two(coef)
        pack_ref[PLACE_ROWS:, :] = coef

    for index in range(blocks):
        low_part, high_part = parts_of(slot_ref[index : index + 1, :])
        low_by_column(low_hot.at[index], low_part.astype(f32))
        for half in range(layout.halves):
            light = [ref[layout.columns(g, half, each), layout.lanes(index)] for g, ref in enumerate(light_refs)]
            light = lanes_of(light)
            for h in range(rows // LOW):
                at = h * width + half * each
                masked[index, at : at + each, :] = jnp.where(high_part == h, light, 0.0).astype(bf16)
    for index in range(blocks):
        placed = nn(masked[index], low_hot[index])
        for h in range(rows // LOW):
            at = index * rows + h * LOW
            w_ref[:, at : at + LOW] = placed[h * width : (h + 1) * width].astype(bf16)
    for index in range(blocks):
        pltpu.make_async_copy(base_hbm.at[index], base_ref.at[index], sems.at[index]).wait()
        keep(index, nn(w_ref[:, index * rows : (index + 1) * rows], base_ref[index]))
    start, count = 0, blocks
    while count > 1:
        for j in range(count // 2):
            pair = slice((start + 2 * j) * SK, (start + 2 * j + 2) * SK)
            here = start + count + j
            high, low = two(upper_tiles_ref[here - blocks])
            coef = nn(coef_ref[:, pair], high)
            keep(here, coef[:width] + coef[width:] + nn(coef_ref[0:width, pair], low))
        start, count = start + count, count // 2


def near_kernel(layout, tiles, a_hbm, tree_ref, w_ref, acc, a_ref, bt_ref, sems, even, odd, even_tile, odd_tile):
    span = layout.span
    size = a_ref.shape[0] // 2
    copies = []
    for half in range(2):
        rows = slice(half * size, (half + 1) * size)
        copies.append(pltpu.make_async_copy(a_hbm.at[rows], a_ref.at[rows], sems.at[half]))
        copies[-1].start()
    filled = tiles[0, tiles.shape[1] - 1]
    acc[...] = jnp.zeros_like(acc)
    target_columns(layout, bt_ref, tree_ref)

    def exponents(unit, out):
        for k in range(2):
            out[k] = tile_exponents(layout, tiles, 2 * unit + k, a_ref, bt_ref)

    def add(tile, block):
        source = aligned(tiles[1, tile] * LEAF, LEAF, LEAF)
        target = aligned(tiles[0, tile] * span, span, span)
        acc[:, target] += tiles[2, tile].astype(f32) * nn(w_ref[:, source], block)

    copies[0].wait()
    exponents(0, even)
    for k in range(2):
        even_tile[k] = jnp.exp(even[k]).astype(bf16)
    exponents(1, odd)
    copies[1].wait()

    def phase(unit, upcoming, ready, finished, previous):
        for k in range(2):
            upcoming[k] = tile_exponents(layout, tiles, 2 * (unit + 1) + k, a_ref, bt_ref)
            finished[k] = jnp.exp(ready[k]).astype(bf16)
            add(2 * (unit - 1) + k, previous[k])

    def step(pair, carry):
        phase(2 * pair + 1, even, odd, odd_tile, even_tile)
        phase(2 * pair + 2, odd, even, even_tile, odd_tile)
        return carry

    units = (filled + 1) // 2
    pairs = (units - 1) // 2
    lax.fori_loop(0, pairs, step, 0)
    for k in range(2):
        add(4 * pairs + k, even_tile[k])

    @pl.when(2 * pairs + 1 < units)
    def _():
        for k in range(2):
            odd_tile[k] = jnp.exp(odd[k]).astype(bf16)
            add(4 * pairs + 2 + k, odd_tile[k])


def far_kernel(layout, low_levels, pack_ref, slot_ref, info_ref, tree_ref, sk_ref, coef_ref, near_ref, *refs):
    out_refs, refs = refs[: layout.halves], refs[layout.halves :]
    tops, coefs, scaled, low_hot, bt_ref, sums, masked = refs[:7]
    powers, tiles = refs[7:9], refs[9:11]
    blocks, rows = layout.blocks, layout.rows
    ups, width = pack_ref.shape[0], near_ref.shape[0]
    levels = low_levels + ups
    span, core = layout.span, layout.core()
    per_block = rows // LEAF
    lane = iota((1, SK), 1)
    for up in range(ups):
        pack = pack_ref[up]
        high, low = two(pack[0:64])
        sub = iota((8, SK), 0)
        extra = jnp.where(sub == 0, pack[67:68], jnp.where(sub == 1, pack[68:69], pack[69:70]))
        extra = jnp.where(sub < 3, extra, jnp.where(sub < 6, 1.0, 0.0))
        at = slice((low_levels + up) * SK, (low_levels + up + 1) * SK)
        rows_of = feature_rows(high.astype(f32), low.astype(f32), extra)
        coef = stack_two(pack[PLACE_ROWS:])
        for index in range(blocks):
            tops[index, at, 0:128], tops[index, at, 128:256] = rows_of
            coefs[index, :, at] = coef
    for index in range(blocks):
        node, start, count = index, 0, blocks
        for level in range(low_levels):
            at = slice(level * SK, (level + 1) * SK)
            other = slice((start + (node ^ 1)) * SK, (start + (node ^ 1) + 1) * SK)
            tops[index, at, :] = sk_ref[other, :]
            coefs[index, :, at] = coef_ref[:, other]
            node, start, count = node // 2, start + count, count // 2
        for leaf in range(per_block):
            flags = info_ref[index, FLAGS + leaf : FLAGS + leaf + 1, :]
            used = []
            for level in range(levels):
                flag = jnp.sum(jnp.where(lane == level, flags, 0.0), axis=1, keepdims=True)
                used.append(jnp.broadcast_to(flag, (1, SK)))
            used = jnp.concatenate(used, 1)
            scaled[index * per_block + leaf] = (coefs[index].astype(f32) * used).astype(bf16)

    target_columns(layout, bt_ref, tree_ref)

    def exponents(leaf):
        powers[leaf % 2][...] = nn(tops[leaf // per_block], bt_ref[:, leaf * span : (leaf + 1) * span])

    def product(leaf):
        here = slice(leaf * span, (leaf + 1) * span)
        far = nn(scaled[leaf], tiles[leaf % 2][...])
        sums[:, here] = near_ref[:, here] + far[:width] + far[width:]

    leaves = blocks * per_block
    exponents(0)
    for leaf in range(leaves):
        if leaf + 1 < leaves:
            exponents(leaf + 1)
        tiles[leaf % 2][...] = jnp.exp(powers[leaf % 2][...]).astype(bf16)
        if leaf:
            product(leaf - 1)
    product(leaves - 1)

    high_parts = []
    pieces = rows // LOW // layout.halves
    for index in range(blocks):
        low_part, high_part = parts_of(slot_ref[index : index + 1, :])
        high_parts.append(high_part)
        for c in range(rows // LANES):
            at = slice(c * LANES, (c + 1) * LANES)
            low_hot[index, :, at] = onehot(iota((LOW, LANES), 0) == low_part[:, at])
        for k in range(pieces):
            at = (index * pieces + k) * LOW
            masked[index, k * 2 * width : (k + 1) * 2 * width, :] = stack_two(sums[:, at : at + LOW])
    for index in range(blocks):
        moved = nn(masked[index], low_hot[index])
        result = jnp.zeros((2 * width, rows), f32)
        for k in range(pieces):
            here = high_parts[index] == k * layout.halves + core
            result = jnp.where(here, moved[k * 2 * width : (k + 1) * 2 * width], result)
        result = result[:width] + result[width:]
        if not layout.fine:
            out_refs[0][0, :, layout.lanes(index)] = result
            continue
        for g in range(layout.count):
            out_ref = out_refs[g // blocks]
            out_ref[g % blocks, :, layout.lanes(index)] = result[:, g * layout.per : (g + 1) * layout.per]


def add_kernel(kept_ref, got_ref, *out_refs):
    half = kept_ref.shape[1] // 2
    for step, out_ref in enumerate(out_refs):
        out_ref[0:half, :] = kept_ref[step, 0:half, :] + got_ref[step, half:, :]
        out_ref[half:, :] = kept_ref[step, half:, :] + got_ref[step, 0:half, :]


def far_first(blocks):
    return list(range(blocks // 2, blocks)) + list(reversed(range(blocks // 2)))


def final_kernel(blocks, pos_ref, *refs):
    back_refs, (weights_ref, out_ref, perm, vals) = refs[:-4], refs[-4:]
    chunks = pos_ref.shape[0]
    rows = chunks * LANES
    width, split = back_refs[0].shape
    width = LANES // blocks if blocks else width
    for r in range(chunks):
        spread(perm, slice(r * LANES, (r + 1) * LANES), column(pos_ref[r : r + 1, :]))
    for g, back_ref in enumerate(back_refs):
        columns, at = 0, slice(0, rows)
        value = back_ref[...]
        if blocks:
            columns = (lax.axis_index("sub") ^ far_first(blocks)[g % blocks]) * width
            at = aligned((lax.axis_index("leaf") ^ lax.axis_index("rep") ^ (g // blocks)) * split, split, split)
            value = value[0:width] if g < blocks else value[width:]
        high, low = two(value)
        vals[aligned(columns, width, width), at] = high
        vals[aligned(columns + LANES, width, width), at] = low
    step = 256
    for s in range(rows // step):
        here = slice(s * step, (s + 1) * step)
        moved = nt(perm[here, :], vals[...])
        out_ref[here, :] = ridge * weights_ref[here, :] + moved[:, :LANES] + moved[:, LANES:]


def upper_levels(pack, skeleton_upper, my_leaf, trees, blocks):
    devices = trees * blocks
    level = blocks.bit_length() - 1
    offset = sum(devices >> step for step in range(1, level + 1))
    line = jnp.arange(pack.shape[0])[:, None]
    is_point, is_norm = line < DIM, (line >= DIM + 3) & (line < DIM + 6)
    is_coef = line >= PLACE_ROWS
    packs, own, stride = [], pack, 1
    while stride < trees:
        other = lax.ppermute(own, "leaf", [(i, i ^ stride) for i in range(trees)])
        packs.append(other)
        stride *= 2
        if stride < trees:
            second = (my_leaf // (stride // 2)) % 2 == 1
            pair = jnp.where(second, jnp.concatenate([other, own], 1), jnp.concatenate([own, other], 1))
            chosen = pair[:, skeleton_upper[offset + my_leaf // stride]]
            level += 1
            offset += devices >> level
            norms = jnp.sum(jnp.where(is_norm, pair, 0.0), axis=0)
            chosen_norms = jnp.sum(jnp.where(is_norm, chosen, 0.0), axis=0)
            inner = jnp.dot(
                jnp.where(is_point, pair, 0.0).T, jnp.where(is_point, chosen, 0.0), precision=highest
            )
            tile = jnp.exp(inner + norms[:, None] + chosen_norms[None])
            own = jnp.where(is_coef, jnp.dot(pair, tile, precision=highest), chosen)
    return jnp.stack(packs)


def body(points, weights, tree_slot, near_count, near_list, skeleton_base, skeleton_upper, far_use):
    blocks, trees, reps = lax.axis_size("sub"), lax.axis_size("leaf"), lax.axis_size("rep")
    devices = blocks * trees
    rows, columns = weights.shape
    low_levels = blocks.bit_length() - 1
    ups = trees.bit_length() - 1
    width = columns // blocks
    part = rows // trees
    per = part // blocks
    total = blocks * rows
    leaves = total // LEAF
    my_leaf = lax.axis_index("leaf")
    fine = trees == 2 and reps == 2 and per % LANES == 0
    layout = Layout(blocks, trees, rows, fine)
    split = part if fine else rows
    cols = width * layout.halves

    place, pos = pl.pallas_call(
        functools.partial(place_kernel, fine),
        out_shape=(shaped((PLACE_ROWS, split), f32), shaped((rows // LANES, LANES), f32)),
        in_specs=[spec()] * 4,
        out_specs=(spec(),) * 2,
        scratch_shapes=[vm((split // LOW * COORD, rows), bf16), vm((rows, LOW), bf16)],
        compiler_params=params(),
        name="sort_points",
    )(tree_slot.reshape(rows // LANES, LANES), points.T, skeleton_base, far_use)
    axes = ("leaf", "sub", "rep")

    def swap(value, step, other=0):
        pairs = []
        for leaf in range(trees):
            for sub in range(blocks):
                for core in range(reps):
                    to = ((leaf ^ core ^ other) * blocks + (sub ^ step)) * reps + core
                    pairs.append(((leaf * blocks + sub) * reps + core, to))
        return lax.ppermute(value, axes, pairs)

    def other_core(value):
        return lax.ppermute(value, "rep", [(0, 1), (1, 0)])

    def sorted_light(pos):
        if fine:
            shapes = (shaped((blocks, width, part), f32),) * 2
        else:
            shapes = (shaped((columns, rows), f32),)
        return pl.pallas_call(
            functools.partial(light_kernel, blocks if fine else 0),
            out_shape=shapes,
            in_specs=[spec()] * 2,
            out_specs=(spec(),) * len(shapes),
            scratch_shapes=[
                vm((rows // LOW * LANES, rows), bf16),
                vm((rows, LOW), bf16),
                vm((rows // LOW, LANES, LOW), f32),
            ],
            compiler_params=params(40),
            name="sort_weights",
        )(in_hbm(pos), in_hbm(weights))

    if fine:
        place = {0: swap(place, 0)}
        stride = blocks // 2
        while stride:
            for step in sorted(place):
                place[step | stride] = lax.ppermute(place[step], "sub", [(i, i ^ stride) for i in range(blocks)])
            stride //= 2
        kept, sent = sorted_light(pos)
        place, kept, sent = lax.optimization_barrier((place, kept, sent))
        light = pl.pallas_call(
            join_kernel,
            out_shape=(shaped((cols, part), f32),) * blocks,
            in_specs=[spec()] * 2,
            out_specs=(spec(),) * blocks,
            compiler_params=params(40),
            name="join_cores",
        )(kept, other_core(sent))
        theirs = {step: other_core(one) for step, one in place.items()}
        place = [place[step] for step in range(blocks)] + [theirs[step] for step in range(blocks)]
        light = [swap(light[step], step) for step in far_first(blocks)]
        small = []
    else:
        info = jnp.pad(far_use.astype(f32), ((FLAGS, 5 - far_use.shape[0]), (0, SK - far_use.shape[1])))
        small = [lax.all_gather(info.at[BASE].set(skeleton_base[0].astype(f32)), "sub", axis=0, tiled=False)]
        place = place.reshape(PLACE_ROWS, trees, part).transpose(1, 0, 2)
        place = lax.all_to_all(place, "leaf", split_axis=0, concat_axis=0, tiled=True)
        place = lax.all_gather(place, "sub", axis=0, tiled=False)
        place = place.transpose(1, 0, 2, 3).reshape(devices, PLACE_ROWS, blocks, per)
        place = [place.transpose(1, 2, 0, 3).reshape(PLACE_ROWS, total)]
        light = sorted_light(pos)[0].reshape(columns, trees, part).transpose(1, 0, 2).reshape(devices, width, part)
        light = lax.all_to_all(light, ("leaf", "sub"), split_axis=0, concat_axis=0, tiled=True)
        light = light.reshape(devices, width, blocks, per)
        light = [light.transpose(1, 2, 0, 3).reshape(width, total)]

    nodes = 2 * blocks - 1
    tree, feat_a, base, sk, upper_tiles, top, slots, info, tiles = pl.pallas_call(
        functools.partial(points_kernel, layout, trees),
        out_shape=(
            vm((COORD, total), bf16),
            pltpu.MemorySpace.HBM((total, FEAT), bf16),
            pltpu.MemorySpace.HBM((blocks, rows, SK), bf16),
            vm((nodes * SK, FEAT), bf16),
            vm((blocks - 1, 2 * SK, SK), f32),
            vm((PLACE_ROWS, SK), f32),
            vm((blocks, rows), f32),
            vm((blocks, 8, SK), f32),
            pltpu.MemorySpace.HBM((3, leaves * leaves + 8), jnp.int32),
        ),
        in_specs=[spec(SMEM)] * 2 + [spec()] * (1 + len(small) + layout.count),
        out_specs=(spec(), spec(pl.ANY), spec(pl.ANY)) + (spec(),) * 5 + (spec(SMEM),),
        scratch_shapes=[
            vm((blocks, rows // LOW * COORD, rows), bf16),
            vm((blocks, rows, LOW), bf16),
            vm((total, FEAT), bf16),
            vm((blocks, rows, SK), bf16),
            vm((COORD, nodes * SK), bf16),
            vm((FEAT, nodes * SK), bf16),
            pltpu.SemaphoreType.DMA((2, blocks)),
            pltpu.SMEM((leaves * leaves,), jnp.int32),
        ],
        compiler_params=params(40),
        name="tree_points",
    )(in_hbm(near_count), in_hbm(near_list[0]), in_hbm(skeleton_upper), *small, *place)

    if fine:
        light, slots = lax.optimization_barrier((light, slots))
        light = light + [other_core(one) for one in light]
    tree_light, coefs, pack = pl.pallas_call(
        functools.partial(weights_kernel, layout),
        out_shape=(
            vm((cols, total), bf16),
            vm((2 * cols, nodes * SK), bf16),
            shaped((PLACE_ROWS + cols, SK), f32),
        ),
        in_specs=[spec(pl.ANY)] + [spec()] * (3 + layout.count),
        out_specs=(spec(),) * 3,
        scratch_shapes=[
            vm((blocks, rows // LOW * cols, rows), bf16),
            vm((blocks, rows, LOW), bf16),
            vm((blocks, rows, SK), bf16),
            pltpu.SemaphoreType.DMA((blocks,)),
        ],
        compiler_params=params(40),
        name="tree_weights",
    )(in_hbm(base), held(upper_tiles), held(top), held(slots), *light)

    packs = upper_levels(pack, skeleton_upper, my_leaf, trees, blocks)

    near = pl.pallas_call(
        functools.partial(near_kernel, layout),
        out_shape=vm((cols, total // layout.halves), f32),
        in_specs=[spec(SMEM), spec(pl.ANY)] + [spec()] * 2,
        out_specs=spec(),
        scratch_shapes=[
            vm((total, FEAT), bf16),
            vm((FEAT, total // layout.halves), bf16),
            pltpu.SemaphoreType.DMA((2,)),
        ]
        + [vm((2, LEAF, layout.span), f32)] * 2
        + [vm((2, LEAF, layout.span), bf16)] * 2,
        compiler_params=params(40),
        name="near",
    )(in_hbm(tiles), in_hbm(feat_a), held(tree), held(tree_light))

    levels = low_levels + ups
    back = pl.pallas_call(
        functools.partial(far_kernel, layout, low_levels),
        out_shape=(shaped((layout.count // layout.halves, cols, total // layout.count), f32),) * layout.halves,
        in_specs=[spec()] * 7,
        out_specs=(spec(),) * layout.halves,
        scratch_shapes=[
            vm((blocks, levels * SK, FEAT), bf16),
            vm((blocks, 2 * cols, levels * SK), bf16),
            vm((leaves, 2 * cols, levels * SK), bf16),
            vm((blocks, LOW, rows), bf16),
            vm((FEAT, total // layout.halves), bf16),
            vm((cols, total // layout.halves), f32),
            vm((blocks, rows // LOW // layout.halves * 2 * cols, LOW), bf16),
        ]
        + [vm((levels * SK, layout.span), f32)] * 2
        + [vm((levels * SK, layout.span), bf16)] * 2,
        compiler_params=params(40),
        name="far",
    )(packs, *[held(one) for one in (slots, info, tree, sk, coefs, near)])

    if fine:
        kept, sent = back
        sums = pl.pallas_call(
            add_kernel,
            out_shape=(shaped((cols, part), f32),) * blocks,
            in_specs=[spec()] * 2,
            out_specs=(spec(),) * blocks,
            compiler_params=params(40),
            name="add_cores",
        )(kept, other_core(sent))
        back = [swap(sums[step], step) for step in far_first(blocks)]
        back = back + [other_core(one) for one in back]
    else:
        back = back[0].reshape(cols, blocks, devices, per).transpose(2, 0, 1, 3).reshape(devices, width, part)
        back = lax.all_to_all(back, ("leaf", "sub"), split_axis=0, concat_axis=0, tiled=True)
        back = [back.reshape(trees, columns, part).transpose(1, 0, 2).reshape(columns, rows)]

    return pl.pallas_call(
        functools.partial(final_kernel, blocks if fine else 0),
        out_shape=shaped((rows, columns), f32),
        in_specs=[spec()] * (2 + layout.count),
        out_specs=spec(),
        scratch_shapes=[vm((rows, rows), bf16), vm((2 * LANES, rows), bf16)],
        compiler_params=params(40),
        name="to_input_order",
    )(pos, *back, weights)


def solution(mesh):
    in_specs = (
        P(("groups", "leaf", "sub"), None),
        P(("groups", "leaf", "sub"), "rep"),
        P(("groups", "leaf", "sub")),
        P(("groups", "leaf"), None),
        P(("groups", "leaf"), None, None),
        P(("groups", "leaf", "sub"), None),
        P("groups", None),
        P(("groups", "leaf", "sub"), None),
    )
    out_specs = P(("groups", "leaf", "sub"), "rep")
    return jax.shard_map(body, mesh=mesh, in_specs=in_specs, out_specs=out_specs, check_vma=False)
```

```python
import functools

import jax
import jax.numpy as jnp
from jax import lax
from jax.experimental import pallas as pl
from jax.experimental.pallas import tpu as pltpu
from jax.sharding import PartitionSpec as P

DIM = 64
LEAF = 512
SK = 128
LANES = 128
FEAT = 256
LOW = 256
COORD = 144

highest = lax.Precision.HIGHEST
point_scale = 0.25
ridge = 0.5
PLACE_ROWS = 72
TAIL = 64
SLOT, NORM, BASE, FLAGS = 0, 1, 2, 3
f32 = jnp.float32
bf16 = jnp.bfloat16
VMEM = pltpu.MemorySpace.VMEM
SMEM = pltpu.MemorySpace.SMEM


def spec(space=VMEM):
    return pl.BlockSpec(memory_space=space)


def params(mib=58):
    return pltpu.CompilerParams(vmem_limit_bytes=mib * 1024 * 1024)


def in_hbm(array):
    return pltpu.with_memory_space_constraint(array, pltpu.MemorySpace.HBM)


def held(array):
    return pltpu.with_memory_space_constraint(array, VMEM)


def vm(shape, dtype):
    return pltpu.VMEM(shape, dtype)


def shaped(shape, dtype):
    return jax.ShapeDtypeStruct(shape, dtype)


def nt(left, right):
    return lax.dot_general(left, right, (((1,), (1,)), ((), ())), preferred_element_type=f32)


def nn(left, right):
    return jnp.dot(left, right, preferred_element_type=f32)


def column(row):
    return jnp.transpose(jnp.broadcast_to(row, (LANES, LANES)))


def iota(shape, dim):
    return lax.broadcasted_iota(jnp.int32, shape, dim)


def onehot(mask):
    return jnp.where(mask, 1.0, 0.0).astype(bf16)


def two(value):
    high = value.astype(bf16)
    return high, (value - high.astype(f32)).astype(bf16)


def three(value):
    high = value.astype(bf16).astype(f32)
    mid = (value - high).astype(bf16).astype(f32)
    return high, mid, (value - high - mid).astype(bf16).astype(f32)


def lanes_of(blocks):
    return blocks[0] if len(blocks) == 1 else jnp.concatenate(blocks, 1)


def aligned(start, size, unit):
    return pl.ds(pl.multiple_of(start, unit), size)


def stack_two(value):
    high, low = two(value)
    return jnp.concatenate([high, low], 0)


def spread(perm, here, rank):
    lane = iota((LANES, LANES), 1).astype(f32)
    for c in range(perm.shape[1] // LANES):
        perm[here, c * LANES : (c + 1) * LANES] = onehot(lane + float(c * LANES) == rank)


def place_kernel(fine, slot_ref, points_ref, base_ref, flag_ref, place_ref, pos_ref, masked, low_hot):
    chunks = slot_ref.shape[0]
    slots = slot_ref[...]
    slot = slots.astype(f32)
    within = slots & (chunks * LANES - 1)
    high, low = (within >> 5).astype(f32), (within & 31).astype(f32)
    ranks = []
    for r in range(chunks):
        here = slice(r * LANES, (r + 1) * LANES)
        mine = column(slot[r : r + 1])
        before = jnp.zeros((LANES, LANES), f32)
        for c in range(chunks):
            before += jnp.where(slot[c : c + 1] < mine, 1.0, 0.0)
        rank = jnp.broadcast_to(jnp.sum(before, axis=1, keepdims=True), (LANES, LANES))
        ranks.append(jnp.transpose(rank)[0:1])
        pos_ref[r : r + 1, :] = ranks[-1]
        spread(low_hot, here, (rank.astype(jnp.int32) & (LOW - 1)).astype(f32))
    scaled = points_ref[...] * point_scale
    ph, plo = two(scaled)
    nh, nm, nl = three(-0.5 * jnp.sum(scaled * scaled, axis=0, keepdims=True))
    high, low = lanes_of([high[c : c + 1] for c in range(chunks)]), lanes_of([low[c : c + 1] for c in range(chunks)])
    sub = iota((16, chunks * LANES), 0)
    extra = jnp.where(sub == 0, high, jnp.where(sub == 1, low, 0.0))
    extra = jnp.where(sub == 2, nh, jnp.where(sub == 3, nm, jnp.where(sub == 4, nl, extra)))
    high_part = lanes_of(ranks).astype(jnp.int32) // LOW
    parts = place_ref.shape[1] // LOW
    first = (lax.axis_index("leaf") ^ lax.axis_index("rep")) * parts if fine else 0
    for h in range(parts):
        here = high_part == first + h
        masked[h * COORD : h * COORD + 64, :] = jnp.where(here, ph.astype(f32), 0.0).astype(bf16)
        masked[h * COORD + 64 : h * COORD + 128, :] = jnp.where(here, plo.astype(f32), 0.0).astype(bf16)
        masked[h * COORD + 128 : (h + 1) * COORD, :] = jnp.where(here, extra, 0.0).astype(bf16)
    placed = nn(masked[...], low_hot[...])
    tail = iota((PLACE_ROWS - TAIL, LOW), 0)
    for h in range(parts):
        at = slice(h * LOW, (h + 1) * LOW)
        moved = placed[h * COORD : (h + 1) * COORD]
        place_ref[0:TAIL, at] = moved[0:64] + moved[64:128]
        slot_row = moved[128:129] * 32.0 + moved[129:130]
        norm_row = moved[130:131] + moved[131:132] + moved[132:133]
        place_ref[TAIL:, at] = jnp.where(tail == SLOT, slot_row, jnp.where(tail == NORM, norm_row, 0.0))
    if fine:
        place_ref[TAIL + BASE : TAIL + BASE + 1, 0:SK] = base_ref[...].astype(f32)
        place_ref[TAIL + FLAGS : TAIL + FLAGS + flag_ref.shape[0], 0 : flag_ref.shape[1]] = flag_ref[...].astype(f32)


def light_kernel(blocks, pos_ref, weights_ref, *refs):
    light_refs, (masked, low_hot, placed) = refs[:-3], refs[-3:]
    chunks = pos_ref.shape[0]
    high_count = chunks * LANES // LOW
    low_part, high_part = parts_of(lanes_of([pos_ref[c : c + 1, :] for c in range(chunks)]))
    low_by_column(low_hot, low_part.astype(f32))
    for c in range(chunks):
        at = slice(c * LANES, (c + 1) * LANES)
        turned = jnp.transpose(weights_ref[at, :])
        for h in range(high_count):
            masked[h * LANES : (h + 1) * LANES, at] = jnp.where(high_part[:, at] == h, turned, 0.0).astype(bf16)
    moved = nn(masked[...], low_hot[...])
    for h in range(high_count):
        if not blocks:
            light_refs[0][:, h * LOW : (h + 1) * LOW] = moved[h * LANES : (h + 1) * LANES]
        placed[h] = moved[h * LANES : (h + 1) * LANES]
    if not blocks:
        return
    width, parts = LANES // blocks, high_count // 2
    for other, light_ref in enumerate(light_refs):
        first = (lax.axis_index("leaf") ^ lax.axis_index("rep") ^ other) * parts
        for step in range(blocks):
            columns = aligned((lax.axis_index("sub") ^ step) * width, width, width)
            for h in range(parts):
                light_ref[step, :, h * LOW : (h + 1) * LOW] = placed[first + h, columns, :]


def join_kernel(kept_ref, got_ref, *out_refs):
    half = kept_ref.shape[1]
    for step, out_ref in enumerate(out_refs):
        out_ref[0:half, :] = kept_ref[step]
        out_ref[half:, :] = got_ref[step]


class Layout:
    def __init__(self, blocks, trees, rows, fine):
        self.blocks, self.rows, self.fine = blocks, rows, fine
        self.count = blocks * trees if fine else 1
        self.per = rows // self.count
        self.halves = 2 if fine else 1
        self.span = LEAF // self.halves

    def core(self):
        return lax.axis_index("rep") if self.fine else 0

    def lanes(self, index):
        return slice(index * self.per, (index + 1) * self.per)

    def columns(self, group, half, each):
        if self.fine and group >= self.blocks:
            half = 1 - half
        return slice(half * each, (half + 1) * each)

    def gather(self, refs, index, part):
        return lanes_of([ref[part, self.lanes(index)] for ref in refs])

    def info(self, refs, small_ref, index):
        if not self.fine:
            return small_ref[index]
        core = lax.axis_index("rep")
        found = jnp.zeros((PLACE_ROWS - TAIL, SK), f32)
        for step in range(self.blocks):
            mine, theirs = refs[step][TAIL:, 0:SK], refs[self.blocks + step][TAIL:, 0:SK]
            here = jnp.where(core == 0, mine, theirs)
            found = jnp.where((lax.axis_index("sub") ^ step) == index, here, found)
        return found


def low_by_column(out, low):
    for c in range(out.shape[0] // LANES):
        at = slice(c * LANES, (c + 1) * LANES)
        spread(out, at, column(low[:, at]))


def parts_of(slots):
    slots = slots.astype(jnp.int32)
    return slots & (LOW - 1), slots // LOW


def feature_columns(out, at, tree):
    out[0:64, at] = tree[0:64].astype(bf16)
    out[64:128, at] = tree[0:64].astype(bf16)
    out[128:192, at] = tree[64:128].astype(bf16)
    out[192:208, at] = jnp.where(iota((16, tree.shape[1]), 0) < 8, tree[128:144].astype(f32), 0.0).astype(bf16)
    out[208:256, at] = jnp.zeros((48, tree.shape[1]), bf16)


def feature_rows(high, low, extra):
    first = jnp.transpose(jnp.concatenate([high, low], 0))
    second = jnp.transpose(jnp.concatenate([high, extra, jnp.zeros((56, high.shape[1]), f32)], 0))
    return first.astype(bf16), second.astype(bf16)


def target_columns(layout, out, tree_ref):
    span = layout.span
    for leaf in range(out.shape[1] // span):
        here = aligned(leaf * LEAF + layout.core() * span, span, span)
        feature_columns(out, slice(leaf * span, (leaf + 1) * span), tree_ref[:, here])


def tile_exponents(layout, tiles, tile, a_ref, bt_ref):
    source = aligned(tiles[1, tile] * LEAF, LEAF, LEAF)
    target = aligned(tiles[0, tile] * layout.span, layout.span, layout.span)
    return nn(a_ref[source, :], bt_ref[:, target])


def list_tiles(count_ref, list_ref, tiles, times):
    every = count_ref.shape[1]

    def tally(leaf, carry):
        for other in range(every):
            times[leaf * every + other] = (leaf == other).astype(jnp.int32)

        def add(slot, carry):
            at = leaf * every + list_ref[leaf, slot]
            times[at] = times[at] + 1
            return carry

        return lax.fori_loop(0, count_ref[0, leaf], add, carry)

    lax.fori_loop(0, every, tally, 0)

    def write(other, filled):
        for leaf in range(every):
            many = times[leaf * every + other]
            tiles[0, filled] = leaf
            tiles[1, filled] = other
            tiles[2, filled] = many
            filled = filled + (many > 0).astype(jnp.int32)
        return filled

    filled = lax.fori_loop(0, every, write, jnp.int32(0))

    def pad(more, carry):
        tiles[0, more] = 0
        tiles[1, more] = 0
        tiles[2, more] = 0
        return carry

    lax.fori_loop(filled, tiles.shape[1] - 1, pad, 0)
    tiles[0, tiles.shape[1] - 1] = filled


def points_kernel(layout, trees, count_ref, list_ref, upper_ref, *refs):
    if not layout.fine:
        small_ref, refs = refs[0], refs[1:]
    else:
        small_ref = None
    place_refs, refs = refs[: layout.count], refs[layout.count :]
    tree_ref, a_hbm, base_hbm, sk_ref, upper_tiles_ref, top_ref, slot_ref, info_ref, tiles = refs[:9]
    masked, low_hot, a_ref, base_ref, sk_t, sk_bt, sems, times = refs[9:]
    blocks, rows = layout.blocks, layout.rows

    def keep(node, found):
        at = slice(node * SK, (node + 1) * SK)
        sk_t[:, at] = found.astype(bf16)
        sk_ref[at, 0:128], sk_ref[at, 128:256] = feature_rows(found[0:64], found[64:128], found[136:144])
        feature_columns(sk_bt, at, found)

    high_parts = rows // LOW
    infos = []
    for index in range(blocks):
        tail = layout.gather(place_refs, index, slice(TAIL, PLACE_ROWS))
        slots = tail[SLOT : SLOT + 1]
        slot_ref[index : index + 1, :] = slots
        infos.append(layout.info(place_refs, small_ref, index))
        info_ref[index] = infos[-1]
        low_part, high_part = parts_of(slots)
        low_by_column(low_hot.at[index], low_part.astype(f32))
        points = layout.gather(place_refs, index, slice(0, TAIL))
        high, low = two(points)
        nh, nm, nl = three(tail[NORM : NORM + 1])
        sub = iota((16, rows), 0)
        norms = jnp.where((sub == 3) | (sub == 8), nh, jnp.where((sub == 4) | (sub == 9), nm, nl))
        is_norm = ((sub >= 3) & (sub < 6)) | ((sub >= 8) & (sub < 11))
        is_one = (sub < 3) | ((sub >= 11) & (sub < 14))
        extra = jnp.where(is_norm, norms, jnp.where(is_one, 1.0, 0.0))
        for h in range(high_parts):
            here = high_part == h
            at = h * COORD
            masked[index, at : at + 64, :] = jnp.where(here, high.astype(f32), 0.0).astype(bf16)
            masked[index, at + 64 : at + 128, :] = jnp.where(here, low.astype(f32), 0.0).astype(bf16)
            masked[index, at + 128 : at + COORD, :] = jnp.where(here, extra, 0.0).astype(bf16)
    copies = []
    for index in range(blocks):
        placed = nn(masked[index], low_hot[index])
        for h in range(high_parts):
            part = placed[h * COORD : (h + 1) * COORD]
            at = slice(index * rows + h * LOW, index * rows + (h + 1) * LOW)
            tree_ref[:, at] = part.astype(bf16)
            a_ref[at, 0:128], a_ref[at, 128:256] = feature_rows(part[0:64], part[64:128], part[136:144])
        mine = slice(index * rows, (index + 1) * rows)
        copies.append(pltpu.make_async_copy(a_ref.at[mine], a_hbm.at[mine], sems.at[0, index]))
        copies[-1].start()
    for index in range(blocks):
        mine = slice(index * rows, (index + 1) * rows)
        picked = onehot(iota((rows, SK), 0) == infos[index][BASE : BASE + 1].astype(jnp.int32))
        keep(index, nn(tree_ref[:, mine], picked))
    for index in range(blocks):
        mine = slice(index * rows, (index + 1) * rows)
        base_ref[index] = jnp.exp(nn(a_ref[mine, :], sk_bt[:, index * SK : (index + 1) * SK])).astype(bf16)
        copies.append(pltpu.make_async_copy(base_ref.at[index], base_hbm.at[index], sems.at[1, index]))
        copies[-1].start()
    start, count, offset, total = 0, blocks, 0, blocks * trees
    while count > 1:
        nodes = count // 2
        for j in range(nodes):
            pair = slice((start + 2 * j) * SK, (start + 2 * j + 2) * SK)
            row = offset + lax.axis_index("leaf") * nodes + j
            picked = onehot(iota((2 * SK, SK), 0) == upper_ref[pl.ds(row, 1), :])
            here = start + count + j
            keep(here, nn(sk_t[:, pair], picked))
            upper_tiles_ref[here - blocks] = jnp.exp(nn(sk_ref[pair, :], sk_bt[:, here * SK : (here + 1) * SK]))
        total = total // 2
        offset = offset + total
        start, count = start + count, nodes
    found = sk_t[:, start * SK : (start + 1) * SK].astype(f32)
    top_ref[0:64, :] = found[0:64] + found[64:128]
    top_ref[64:72, :] = found[128:136]
    list_tiles(count_ref, list_ref, tiles, times)
    for copy in copies:
        copy.wait()


def weights_kernel(layout, base_hbm, upper_tiles_ref, top_ref, slot_ref, *refs):
    light_refs, refs = refs[: layout.count], refs[layout.count :]
    if layout.fine:
        order = far_first(layout.blocks)
        order = order + [layout.blocks + step for step in order]
        light_refs = [light_refs[order.index(g)] for g in range(layout.count)]
    w_ref, coef_ref, pack_ref, masked, low_hot, base_ref, sems = refs
    blocks, rows = layout.blocks, layout.rows
    width = light_refs[0].shape[0]
    each = width // layout.halves
    pack_ref[0:PLACE_ROWS, :] = top_ref[...]
    for index in range(blocks):
        pltpu.make_async_copy(base_hbm.at[index], base_ref.at[index], sems.at[index]).start()

    def keep(node, coef):
        coef_ref[:, node * SK : (node + 1) * SK] = stack_two(coef)
        pack_ref[PLACE_ROWS:, :] = coef

    for index in range(blocks):
        low_part, high_part = parts_of(slot_ref[index : index + 1, :])
        low_by_column(low_hot.at[index], low_part.astype(f32))
        for half in range(layout.halves):
            light = [ref[layout.columns(g, half, each), layout.lanes(index)] for g, ref in enumerate(light_refs)]
            light = lanes_of(light)
            for h in range(rows // LOW):
                at = h * width + half * each
                masked[index, at : at + each, :] = jnp.where(high_part == h, light, 0.0).astype(bf16)
    for index in range(blocks):
        placed = nn(masked[index], low_hot[index])
        for h in range(rows // LOW):
            at = index * rows + h * LOW
            w_ref[:, at : at + LOW] = placed[h * width : (h + 1) * width].astype(bf16)
    for index in range(blocks):
        pltpu.make_async_copy(base_hbm.at[index], base_ref.at[index], sems.at[index]).wait()
        keep(index, nn(w_ref[:, index * rows : (index + 1) * rows], base_ref[index]))
    start, count = 0, blocks
    while count > 1:
        for j in range(count // 2):
            pair = slice((start + 2 * j) * SK, (start + 2 * j + 2) * SK)
            here = start + count + j
            high, low = two(upper_tiles_ref[here - blocks])
            coef = nn(coef_ref[:, pair], high)
            keep(here, coef[:width] + coef[width:] + nn(coef_ref[0:width, pair], low))
        start, count = start + count, count // 2


def near_kernel(layout, tiles, a_hbm, tree_ref, w_ref, acc, a_ref, bt_ref, sems, even, odd, even_tile, odd_tile):
    span = layout.span
    size = a_ref.shape[0] // 2
    copies = []
    for half in range(2):
        rows = slice(half * size, (half + 1) * size)
        copies.append(pltpu.make_async_copy(a_hbm.at[rows], a_ref.at[rows], sems.at[half]))
        copies[-1].start()
    filled = tiles[0, tiles.shape[1] - 1]
    acc[...] = jnp.zeros_like(acc)
    target_columns(layout, bt_ref, tree_ref)

    def exponents(unit, out):
        for k in range(2):
            out[k] = tile_exponents(layout, tiles, 2 * unit + k, a_ref, bt_ref)

    def add(tile, block):
        source = aligned(tiles[1, tile] * LEAF, LEAF, LEAF)
        target = aligned(tiles[0, tile] * span, span, span)
        acc[:, target] += tiles[2, tile].astype(f32) * nn(w_ref[:, source], block)

    copies[0].wait()
    exponents(0, even)
    for k in range(2):
        even_tile[k] = jnp.exp(even[k]).astype(bf16)
    exponents(1, odd)
    copies[1].wait()

    def phase(unit, upcoming, ready, finished, previous):
        for k in range(2):
            upcoming[k] = tile_exponents(layout, tiles, 2 * (unit + 1) + k, a_ref, bt_ref)
            finished[k] = jnp.exp(ready[k]).astype(bf16)
            add(2 * (unit - 1) + k, previous[k])

    def step(pair, carry):
        phase(2 * pair + 1, even, odd, odd_tile, even_tile)
        phase(2 * pair + 2, odd, even, even_tile, odd_tile)
        return carry

    units = (filled + 1) // 2
    pairs = (units - 1) // 2
    lax.fori_loop(0, pairs, step, 0)
    for k in range(2):
        add(4 * pairs + k, even_tile[k])

    @pl.when(2 * pairs + 1 < units)
    def _():
        for k in range(2):
            odd_tile[k] = jnp.exp(odd[k]).astype(bf16)
            add(4 * pairs + 2 + k, odd_tile[k])


def far_kernel(layout, low_levels, pack_ref, slot_ref, info_ref, tree_ref, sk_ref, coef_ref, near_ref, *refs):
    out_refs, refs = refs[: layout.halves], refs[layout.halves :]
    tops, coefs, scaled, low_hot, bt_ref, sums, masked = refs[:7]
    powers, tiles = refs[7:9], refs[9:11]
    blocks, rows = layout.blocks, layout.rows
    ups, width = pack_ref.shape[0], near_ref.shape[0]
    levels = low_levels + ups
    span, core = layout.span, layout.core()
    per_block = rows // LEAF
    lane = iota((1, SK), 1)
    for up in range(ups):
        pack = pack_ref[up]
        high, low = two(pack[0:64])
        sub = iota((8, SK), 0)
        extra = jnp.where(sub == 0, pack[67:68], jnp.where(sub == 1, pack[68:69], pack[69:70]))
        extra = jnp.where(sub < 3, extra, jnp.where(sub < 6, 1.0, 0.0))
        at = slice((low_levels + up) * SK, (low_levels + up + 1) * SK)
        rows_of = feature_rows(high.astype(f32), low.astype(f32), extra)
        coef = stack_two(pack[PLACE_ROWS:])
        for index in range(blocks):
            tops[index, at, 0:128], tops[index, at, 128:256] = rows_of
            coefs[index, :, at] = coef
    for index in range(blocks):
        node, start, count = index, 0, blocks
        for level in range(low_levels):
            at = slice(level * SK, (level + 1) * SK)
            other = slice((start + (node ^ 1)) * SK, (start + (node ^ 1) + 1) * SK)
            tops[index, at, :] = sk_ref[other, :]
            coefs[index, :, at] = coef_ref[:, other]
            node, start, count = node // 2, start + count, count // 2
        for leaf in range(per_block):
            flags = info_ref[index, FLAGS + leaf : FLAGS + leaf + 1, :]
            used = []
            for level in range(levels):
                flag = jnp.sum(jnp.where(lane == level, flags, 0.0), axis=1, keepdims=True)
                used.append(jnp.broadcast_to(flag, (1, SK)))
            used = jnp.concatenate(used, 1)
            scaled[index * per_block + leaf] = (coefs[index].astype(f32) * used).astype(bf16)

    target_columns(layout, bt_ref, tree_ref)

    def exponents(leaf):
        powers[leaf % 2][...] = nn(tops[leaf // per_block], bt_ref[:, leaf * span : (leaf + 1) * span])

    def product(leaf):
        here = slice(leaf * span, (leaf + 1) * span)
        far = nn(scaled[leaf], tiles[leaf % 2][...])
        sums[:, here] = near_ref[:, here] + far[:width] + far[width:]

    leaves = blocks * per_block
    exponents(0)
    for leaf in range(leaves):
        if leaf + 1 < leaves:
            exponents(leaf + 1)
        tiles[leaf % 2][...] = jnp.exp(powers[leaf % 2][...]).astype(bf16)
        if leaf:
            product(leaf - 1)
    product(leaves - 1)

    high_parts = []
    pieces = rows // LOW // layout.halves
    for index in range(blocks):
        low_part, high_part = parts_of(slot_ref[index : index + 1, :])
        high_parts.append(high_part)
        for c in range(rows // LANES):
            at = slice(c * LANES, (c + 1) * LANES)
            low_hot[index, :, at] = onehot(iota((LOW, LANES), 0) == low_part[:, at])
        for k in range(pieces):
            at = (index * pieces + k) * LOW
            masked[index, k * 2 * width : (k + 1) * 2 * width, :] = stack_two(sums[:, at : at + LOW])
    for index in range(blocks):
        moved = nn(masked[index], low_hot[index])
        result = jnp.zeros((2 * width, rows), f32)
        for k in range(pieces):
            here = high_parts[index] == k * layout.halves + core
            result = jnp.where(here, moved[k * 2 * width : (k + 1) * 2 * width], result)
        result = result[:width] + result[width:]
        if not layout.fine:
            out_refs[0][0, :, layout.lanes(index)] = result
            continue
        for g in range(layout.count):
            out_ref = out_refs[g // blocks]
            out_ref[g % blocks, :, layout.lanes(index)] = result[:, g * layout.per : (g + 1) * layout.per]


def add_kernel(kept_ref, got_ref, *out_refs):
    half = kept_ref.shape[1] // 2
    for step, out_ref in enumerate(out_refs):
        out_ref[0:half, :] = kept_ref[step, 0:half, :] + got_ref[step, half:, :]
        out_ref[half:, :] = kept_ref[step, half:, :] + got_ref[step, 0:half, :]


def far_first(blocks):
    return list(reversed(range(blocks)))


def final_kernel(blocks, pos_ref, *refs):
    back_refs, (weights_ref, out_ref, perm, vals) = refs[:-4], refs[-4:]
    chunks = pos_ref.shape[0]
    rows = chunks * LANES
    width, split = back_refs[0].shape
    width = LANES // blocks if blocks else width
    step = 512

    def make(first):
        for r in range(first // LANES, (first + step) // LANES):
            spread(perm, slice(r * LANES, (r + 1) * LANES), column(pos_ref[r : r + 1, :]))

    make(0)
    for g, back_ref in enumerate(back_refs):
        columns, at = 0, slice(0, rows)
        value = back_ref[...]
        if blocks:
            columns = (lax.axis_index("sub") ^ far_first(blocks)[g % blocks]) * width
            at = aligned((lax.axis_index("leaf") ^ lax.axis_index("rep") ^ (g // blocks)) * split, split, split)
            value = value[0:width] if g < blocks else value[width:]
        high, low = two(value)
        vals[aligned(columns, width, width), at] = high
        vals[aligned(columns + LANES, width, width), at] = low
    for s in range(rows // step):
        here = slice(s * step, (s + 1) * step)
        if (s + 1) * step < rows:
            make((s + 1) * step)
        moved = nt(perm[here, :], vals[...])
        out_ref[here, :] = ridge * weights_ref[here, :] + moved[:, :LANES] + moved[:, LANES:]


def upper_levels(pack, skeleton_upper, my_leaf, trees, blocks):
    devices = trees * blocks
    level = blocks.bit_length() - 1
    offset = sum(devices >> step for step in range(1, level + 1))
    line = jnp.arange(pack.shape[0])[:, None]
    is_point, is_norm = line < DIM, (line >= DIM + 3) & (line < DIM + 6)
    is_coef = line >= PLACE_ROWS
    packs, own, stride = [], pack, 1
    while stride < trees:
        other = lax.ppermute(own, "leaf", [(i, i ^ stride) for i in range(trees)])
        packs.append(other)
        stride *= 2
        if stride < trees:
            second = (my_leaf // (stride // 2)) % 2 == 1
            pair = jnp.where(second, jnp.concatenate([other, own], 1), jnp.concatenate([own, other], 1))
            chosen = pair[:, skeleton_upper[offset + my_leaf // stride]]
            level += 1
            offset += devices >> level
            norms = jnp.sum(jnp.where(is_norm, pair, 0.0), axis=0)
            chosen_norms = jnp.sum(jnp.where(is_norm, chosen, 0.0), axis=0)
            inner = jnp.dot(
                jnp.where(is_point, pair, 0.0).T, jnp.where(is_point, chosen, 0.0), precision=highest
            )
            tile = jnp.exp(inner + norms[:, None] + chosen_norms[None])
            own = jnp.where(is_coef, jnp.dot(pair, tile, precision=highest), chosen)
    return jnp.stack(packs)


def body(points, weights, tree_slot, near_count, near_list, skeleton_base, skeleton_upper, far_use):
    blocks, trees, reps = lax.axis_size("sub"), lax.axis_size("leaf"), lax.axis_size("rep")
    devices = blocks * trees
    rows, columns = weights.shape
    low_levels = blocks.bit_length() - 1
    ups = trees.bit_length() - 1
    width = columns // blocks
    part = rows // trees
    per = part // blocks
    total = blocks * rows
    leaves = total // LEAF
    my_leaf = lax.axis_index("leaf")
    fine = trees == 2 and reps == 2 and per % LANES == 0
    layout = Layout(blocks, trees, rows, fine)
    split = part if fine else rows
    cols = width * layout.halves

    place, pos = pl.pallas_call(
        functools.partial(place_kernel, fine),
        out_shape=(shaped((PLACE_ROWS, split), f32), shaped((rows // LANES, LANES), f32)),
        in_specs=[spec()] * 4,
        out_specs=(spec(),) * 2,
        scratch_shapes=[vm((split // LOW * COORD, rows), bf16), vm((rows, LOW), bf16)],
        compiler_params=params(),
        name="sort_points",
    )(tree_slot.reshape(rows // LANES, LANES), points.T, skeleton_base, far_use)
    axes = ("leaf", "sub", "rep")

    def swap(value, step, other=0):
        pairs = []
        for leaf in range(trees):
            for sub in range(blocks):
                for core in range(reps):
                    to = ((leaf ^ core ^ other) * blocks + (sub ^ step)) * reps + core
                    pairs.append(((leaf * blocks + sub) * reps + core, to))
        return lax.ppermute(value, axes, pairs)

    def other_core(value):
        return lax.ppermute(value, "rep", [(0, 1), (1, 0)])

    def sorted_light(pos):
        if fine:
            shapes = (shaped((blocks, width, part), f32),) * 2
        else:
            shapes = (shaped((columns, rows), f32),)
        return pl.pallas_call(
            functools.partial(light_kernel, blocks if fine else 0),
            out_shape=shapes,
            in_specs=[spec()] * 2,
            out_specs=(spec(),) * len(shapes),
            scratch_shapes=[
                vm((rows // LOW * LANES, rows), bf16),
                vm((rows, LOW), bf16),
                vm((rows // LOW, LANES, LOW), f32),
            ],
            compiler_params=params(40),
            name="sort_weights",
        )(in_hbm(pos), in_hbm(weights))

    if fine:
        place = {0: swap(place, 0)}
        stride = blocks // 2
        while stride:
            for step in sorted(place):
                place[step | stride] = lax.ppermute(place[step], "sub", [(i, i ^ stride) for i in range(blocks)])
            stride //= 2
        kept, sent = sorted_light(pos)
        place, kept, sent = lax.optimization_barrier((place, kept, sent))
        light = pl.pallas_call(
            join_kernel,
            out_shape=(shaped((cols, part), f32),) * blocks,
            in_specs=[spec()] * 2,
            out_specs=(spec(),) * blocks,
            compiler_params=params(40),
            name="join_cores",
        )(kept, other_core(sent))
        theirs = {step: other_core(one) for step, one in place.items()}
        place = [place[step] for step in range(blocks)] + [theirs[step] for step in range(blocks)]
        light = [swap(light[step], step) for step in far_first(blocks)]
        small = []
    else:
        info = jnp.pad(far_use.astype(f32), ((FLAGS, 5 - far_use.shape[0]), (0, SK - far_use.shape[1])))
        small = [lax.all_gather(info.at[BASE].set(skeleton_base[0].astype(f32)), "sub", axis=0, tiled=False)]
        place = place.reshape(PLACE_ROWS, trees, part).transpose(1, 0, 2)
        place = lax.all_to_all(place, "leaf", split_axis=0, concat_axis=0, tiled=True)
        place = lax.all_gather(place, "sub", axis=0, tiled=False)
        place = place.transpose(1, 0, 2, 3).reshape(devices, PLACE_ROWS, blocks, per)
        place = [place.transpose(1, 2, 0, 3).reshape(PLACE_ROWS, total)]
        light = sorted_light(pos)[0].reshape(columns, trees, part).transpose(1, 0, 2).reshape(devices, width, part)
        light = lax.all_to_all(light, ("leaf", "sub"), split_axis=0, concat_axis=0, tiled=True)
        light = light.reshape(devices, width, blocks, per)
        light = [light.transpose(1, 2, 0, 3).reshape(width, total)]

    nodes = 2 * blocks - 1
    tree, feat_a, base, sk, upper_tiles, top, slots, info, tiles = pl.pallas_call(
        functools.partial(points_kernel, layout, trees),
        out_shape=(
            vm((COORD, total), bf16),
            pltpu.MemorySpace.HBM((total, FEAT), bf16),
            pltpu.MemorySpace.HBM((blocks, rows, SK), bf16),
            vm((nodes * SK, FEAT), bf16),
            vm((blocks - 1, 2 * SK, SK), f32),
            vm((PLACE_ROWS, SK), f32),
            vm((blocks, rows), f32),
            vm((blocks, 8, SK), f32),
            pltpu.MemorySpace.HBM((3, leaves * leaves + 8), jnp.int32),
        ),
        in_specs=[spec(SMEM)] * 2 + [spec()] * (1 + len(small) + layout.count),
        out_specs=(spec(), spec(pl.ANY), spec(pl.ANY)) + (spec(),) * 5 + (spec(SMEM),),
        scratch_shapes=[
            vm((blocks, rows // LOW * COORD, rows), bf16),
            vm((blocks, rows, LOW), bf16),
            vm((total, FEAT), bf16),
            vm((blocks, rows, SK), bf16),
            vm((COORD, nodes * SK), bf16),
            vm((FEAT, nodes * SK), bf16),
            pltpu.SemaphoreType.DMA((2, blocks)),
            pltpu.SMEM((leaves * leaves,), jnp.int32),
        ],
        compiler_params=params(40),
        name="tree_points",
    )(in_hbm(near_count), in_hbm(near_list[0]), in_hbm(skeleton_upper), *small, *place)

    if fine:
        light, slots = lax.optimization_barrier((light, slots))
        light = light + [other_core(one) for one in light]
    tree_light, coefs, pack = pl.pallas_call(
        functools.partial(weights_kernel, layout),
        out_shape=(
            vm((cols, total), bf16),
            vm((2 * cols, nodes * SK), bf16),
            shaped((PLACE_ROWS + cols, SK), f32),
        ),
        in_specs=[spec(pl.ANY)] + [spec()] * (3 + layout.count),
        out_specs=(spec(),) * 3,
        scratch_shapes=[
            vm((blocks, rows // LOW * cols, rows), bf16),
            vm((blocks, rows, LOW), bf16),
            vm((blocks, rows, SK), bf16),
            pltpu.SemaphoreType.DMA((blocks,)),
        ],
        compiler_params=params(40),
        name="tree_weights",
    )(in_hbm(base), held(upper_tiles), held(top), held(slots), *light)

    packs = upper_levels(pack, skeleton_upper, my_leaf, trees, blocks)

    near = pl.pallas_call(
        functools.partial(near_kernel, layout),
        out_shape=vm((cols, total // layout.halves), f32),
        in_specs=[spec(SMEM), spec(pl.ANY)] + [spec()] * 2,
        out_specs=spec(),
        scratch_shapes=[
            vm((total, FEAT), bf16),
            vm((FEAT, total // layout.halves), bf16),
            pltpu.SemaphoreType.DMA((2,)),
        ]
        + [vm((2, LEAF, layout.span), f32)] * 2
        + [vm((2, LEAF, layout.span), bf16)] * 2,
        compiler_params=params(40),
        name="near",
    )(in_hbm(tiles), in_hbm(feat_a), held(tree), held(tree_light))

    levels = low_levels + ups
    back = pl.pallas_call(
        functools.partial(far_kernel, layout, low_levels),
        out_shape=(shaped((layout.count // layout.halves, cols, total // layout.count), f32),) * layout.halves,
        in_specs=[spec()] * 7,
        out_specs=(spec(),) * layout.halves,
        scratch_shapes=[
            vm((blocks, levels * SK, FEAT), bf16),
            vm((blocks, 2 * cols, levels * SK), bf16),
            vm((leaves, 2 * cols, levels * SK), bf16),
            vm((blocks, LOW, rows), bf16),
            vm((FEAT, total // layout.halves), bf16),
            vm((cols, total // layout.halves), f32),
            vm((blocks, rows // LOW // layout.halves * 2 * cols, LOW), bf16),
        ]
        + [vm((levels * SK, layout.span), f32)] * 2
        + [vm((levels * SK, layout.span), bf16)] * 2,
        compiler_params=params(40),
        name="far",
    )(packs, *[held(one) for one in (slots, info, tree, sk, coefs, near)])

    if fine:
        kept, sent = back
        sums = pl.pallas_call(
            add_kernel,
            out_shape=(shaped((cols, part), f32),) * blocks,
            in_specs=[spec()] * 2,
            out_specs=(spec(),) * blocks,
            compiler_params=params(40),
            name="add_cores",
        )(kept, other_core(sent))
        back = [swap(sums[step], step) for step in far_first(blocks)]
        back = back + [other_core(one) for one in back]
    else:
        back = back[0].reshape(cols, blocks, devices, per).transpose(2, 0, 1, 3).reshape(devices, width, part)
        back = lax.all_to_all(back, ("leaf", "sub"), split_axis=0, concat_axis=0, tiled=True)
        back = [back.reshape(trees, columns, part).transpose(1, 0, 2).reshape(columns, rows)]

    return pl.pallas_call(
        functools.partial(final_kernel, blocks if fine else 0),
        out_shape=shaped((rows, columns), f32),
        in_specs=[spec()] * (2 + layout.count),
        out_specs=spec(),
        scratch_shapes=[vm((rows, rows), bf16), vm((2 * LANES, rows), bf16)],
        compiler_params=params(40),
        name="to_input_order",
    )(pos, *back, weights)


def solution(mesh):
    in_specs = (
        P(("groups", "leaf", "sub"), None),
        P(("groups", "leaf", "sub"), "rep"),
        P(("groups", "leaf", "sub")),
        P(("groups", "leaf"), None),
        P(("groups", "leaf"), None, None),
        P(("groups", "leaf", "sub"), None),
        P("groups", None),
        P(("groups", "leaf", "sub"), None),
    )
    out_specs = P(("groups", "leaf", "sub"), "rep")
    return jax.shard_map(body, mesh=mesh, in_specs=in_specs, out_specs=out_specs, check_vma=False)
```
